32 devices in a mesh: seq: 32 (over z, y, x, core).
Axes of the slice: x: 2, y: 2, z: 4, core: 2. Of those that a mesh axis runs over, the one named last changes fastest.
Arguments:
- tokens: bfloat16 [1, 4096, 2048], P(None, 'seq'), may hold values from -6 to 6
- previous: float32 [1, 2, 2048], replicated, may hold values from -6 to 6
- initial_state: float32 [2048, 64], P('seq'), may hold values from -16 to 16
- mixing_weights: bfloat16 [2048, 10240], P('seq'), may hold values from -0.125 to 0.125
- lowrank_weights: bfloat16 [2048, 448], P('seq'), as said below
- vectors: float32 [2048, 16], P('seq'), as said below
- feedforward_weights: bfloat16 [2048, 16384], P('seq'), as said below
- cotangent: bfloat16 [1, 4096, 2048], P(None, 'seq'), may hold values from -6 to 6
Outputs:
- block_output: bfloat16 [1, 4096, 2048], P(None, 'seq')
- block_input_gradient: float32 [1, 4096, 2048], P(None, 'seq')
- initial_state_gradient: float32 [2048, 64], P('seq')
- mixing_gradient: float32 [2048, 10240], P('seq')
- lowrank_gradient: float32 [2048, 448], P('seq')
- vectors_gradient: float32 [2048, 16], P('seq')
- feedforward_gradient: float32 [2048, 16384], P('seq')
The draws below stay inside these ranges and needn't reach their ends.
Inputs may be any that keep to these rules, and one draw needn't show every extreme that they name: `lowrank_weights`: column blocks drawn at their fan-in scale. `vectors`: gains positive, shift mixes between 0 and 1, decay base negative. `feedforward_weights`: column blocks drawn at their fan-in scale.
All inputs are finite; a program needn't handle non-finite values.
Results may differ from the reference program's by a relative error of at most 0.015.
Values may be sent and summed in bfloat16 or wider, within the bound.
No kernel may reach another device: no remote copies, remote signals or barrier semaphores. Data moves between devices by JAX's collectives and lax.ppermute only.
A program may use at most 512 MiB of HBM per device.

```python
import jax
import jax.numpy as jnp
from jax import lax

D = 2048
ATTENDER_NUMBER = 32
ATTENDER_SPAN = 64
FF = 7168
MIXING_RANK = 32
DECAY_RANK = 64
SEQS = 1
TOK_SEQ = 128
LENGTH = 4096


def column_noise(key, columns):
    return jax.random.truncated_normal(key, -4.0, 4.0, (D, columns), jnp.float32)


def draw_lowrank_weights(key, part):
    key = jax.random.fold_in(key, 5)
    columns = 10 * MIXING_RANK + 2 * DECAY_RANK
    position = jnp.arange(columns)
    scale = jnp.where(position < 5 * MIXING_RANK, D ** (-0.5), 0.5 * MIXING_RANK ** (-0.5))
    scale = jnp.where(position >= 10 * MIXING_RANK, D ** (-0.5), scale)
    scale = jnp.where(position >= 10 * MIXING_RANK + DECAY_RANK, DECAY_RANK ** (-0.5), scale)
    noise = column_noise(key, columns)
    return (noise * scale[None, :]).astype(jnp.bfloat16)


def draw_feedforward_weights(key, part):
    key = jax.random.fold_in(key, 9)
    columns = 2 * FF + D
    position = jnp.arange(columns)
    scale = jnp.where(position < FF + D, D ** (-0.5), FF ** (-0.5))
    noise = column_noise(key, columns)
    return (noise * scale[None, :]).astype(jnp.bfloat16)


def draw_vectors(key, part):
    key = jax.random.fold_in(key, 7)
    first_key, second_key, third_key, fourth_key = jax.random.split(key, 4)
    spread = jnp.clip(jax.random.normal(first_key, (D, 16), jnp.float32), -3.0, 3.0)
    share = 0.5
    fraction = jax.random.uniform(second_key, (D, 16), jnp.float32)
    heads_fast = jax.random.uniform(third_key, (ATTENDER_NUMBER,), jnp.float32) < share
    level = jax.random.uniform(fourth_key, (D,), jnp.float32)
    fast_rate = jnp.log(1.0 / 50.0) + level * jnp.log(50.0 / 30.0)
    slow_rate = jnp.log(0.25 / LENGTH) + level * jnp.log(4.0)
    channel_head = jnp.arange(D) // ATTENDER_SPAN
    decay_base = jnp.where(heads_fast[channel_head], fast_rate, slow_rate)
    gain_cols = 1.0 + 0.15 * spread
    bias_cols = 0.3 * spread
    columns = [gain_cols[:, 0], bias_cols[:, 1]]
    columns = columns + [fraction[:, column] for column in range(2, 8)]
    columns = columns + [decay_base, 0.5 * spread[:, 9], gain_cols[:, 10], bias_cols[:, 11], gain_cols[:, 12], bias_cols[:, 13], fraction[:, 14], fraction[:, 15]]
    return jnp.stack(columns, axis=1)


def spiked(result, own_key, source, target, parts, factor):
    owner, partner = [(jnp.arange(result.shape[axis_at]) // (result.shape[axis_at] // parts)).reshape([-1 if axis == axis_at else 1 for axis in range(result.ndim)]) for axis_at in (source, target)]
    chosen = jax.random.permutation(own_key, parts)[partner]
    strong = (owner == chosen) | (owner == (partner + parts // 2) % parts)
    return jnp.where(strong, factor * result, result)


def shard_levels(key, shape, cuts, low, high):
    loudness = 1.0
    for axis_at, parts in cuts:
        steps = jax.random.uniform(jax.random.fold_in(jax.random.fold_in(key, 6), axis_at), (parts,), jnp.float32, low / len(cuts), high / len(cuts))
        loudness = loudness * jnp.repeat(jnp.exp(steps), shape[axis_at] // parts).reshape((-1,) + (1,) * (len(shape) - 1 - axis_at))
    return loudness


def normal_values(key, shape, scale, limit, cuts=(), held_as=jnp.bfloat16):
    drawn = scale * jax.random.normal(key, shape, jnp.float32)
    if cuts:
        drawn = drawn * shard_levels(key, shape, cuts, -0.22, 0.18)
    return jnp.clip(drawn, -limit, limit).astype(held_as)


def bell_draw_with(key, shape, deviation, limit, pieces, heavy, kind=jnp.bfloat16):
    values = deviation * jax.random.normal(key, shape, jnp.float32)
    if pieces:
        values = values * shard_levels(key, shape, pieces, -0.22, 0.18)
    return jnp.clip(spiked(values, jax.random.fold_in(key, 3), *heavy), -limit, limit).astype(kind)


def setup_inputs(seed: int = 0) -> dict:
    key_list = jax.random.split(jax.random.key(seed), 9)
    return {
        "tokens": normal_values(key_list[0], (SEQS, LENGTH, D), 1.0, 6.0, ((1, 32),)),
        "previous": normal_values(key_list[1], (SEQS, 2, D), 1.0, 6.0, (), jnp.float32),
        "initial_state": normal_values(key_list[2], (SEQS * ATTENDER_NUMBER * ATTENDER_SPAN, ATTENDER_SPAN), 4.0, 16.0, ((0, 32),), jnp.float32),
        "mixing_weights": normal_values(key_list[3], (D, 5 * D), D ** -0.5, 0.125, ((0, 32),)),
        "lowrank_weights": draw_lowrank_weights(jax.random.fold_in(key_list[8], 71), 0),
        "vectors": draw_vectors(jax.random.fold_in(key_list[8], 71), 0),
        "feedforward_weights": draw_feedforward_weights(jax.random.fold_in(key_list[8], 71), 0),
        "cotangent": bell_draw_with(key_list[7], (SEQS, LENGTH, D), 1.0, 6.0, ((1, 32),), (1, 2, 32, 2.75)),
    }


highest = lax.Precision.HIGHEST
layer_eps = 1e-05
group_eps = 0.00064

@jax.custom_vjp
def lowrank_output(v):
    return lax.optimization_barrier(v.astype(jnp.bfloat16)).astype(jnp.float32)

@jax.custom_vjp
def lowrank_output_backward(v):
    return v

def low_keep(v):
    return (lowrank_output(v), None)

def low_pass(kept, grad):
    return (grad,)

def back_keep(v):
    return (v, None)

def back_low(kept, grad):
    return (lowrank_output(grad),)
lowrank_output.defvjp(low_keep, low_pass)
lowrank_output_backward.defvjp(back_keep, back_low)

def matrix_product(left, right):
    return jnp.dot(left, right, precision=highest, preferred_element_type=jnp.float32)

def layer_norm(values, gain_row, bias_row, epsilon):
    centred = values - lax.optimization_barrier(jnp.mean(values, axis=-1, keepdims=True))
    spread = lax.optimization_barrier(jnp.mean(centred * centred, axis=-1, keepdims=True))
    return centred * lax.rsqrt(spread + epsilon) * gain_row + bias_row

def recursive_segment(acceptance_entries, source_lookups, source_payloads, fading_exponent, present_reward_array, arriving_memory):
    cumulative = jnp.cumsum(fading_exponent, axis=-2)
    before_step = cumulative - fading_exponent
    total_decay = cumulative[..., -1:, :]
    queries = acceptance_entries * jnp.exp(before_step)
    scaled_keys = source_lookups * jnp.exp(-cumulative)
    affinity_entries = jnp.einsum('...tk,...sk->...ts', queries, scaled_keys, precision=highest)
    segment_length = fading_exponent.shape[-2]
    positions = jnp.arange(segment_length)
    strict_lower_mask = positions[:, None] > positions[None, :]
    present_reward_share = lax.optimization_barrier(jnp.sum(acceptance_entries * present_reward_array[..., None, :] * source_lookups, axis=-1))
    affinity_entries = jnp.where(strict_lower_mask, affinity_entries, 0.0) + jnp.eye(segment_length, dtype=jnp.float32) * present_reward_share[..., :, None]
    stratum_response = jnp.einsum('...tk,...kv->...tv', queries, arriving_memory, precision=highest)
    stratum_response = stratum_response + jnp.einsum('...ts,...sv->...tv', affinity_entries, source_payloads, precision=highest)
    carried_keys = source_lookups * jnp.exp(total_decay - cumulative)
    state_out = jnp.exp(total_decay)[..., 0, :, None] * arriving_memory + jnp.einsum('...tk,...tv->...kv', carried_keys, source_payloads, precision=highest)
    return (stratum_response, state_out)

def forward_pass(hidden_input, previous_token, starting_state, mixing_matrix, lowrank_matrix, vectors, feedforward_matrix):
    stratum_settings = vectors.T
    normed = layer_norm(hidden_input, stratum_settings[0], stratum_settings[1], layer_eps)
    shifted = jnp.concatenate([previous_token[0:1], normed[:-1]], axis=0)
    delta = shifted - normed
    blending_input = lowrank_output(normed + delta * stratum_settings[2])
    lowrank_latent = lowrank_output(jnp.tanh(lowrank_output_backward(matrix_product(blending_input, lowrank_matrix[:, :5 * MIXING_RANK]))))
    input_rows = []
    for mixing_component in range(5):
        sequence_piece = lowrank_latent[:, mixing_component * MIXING_RANK:(mixing_component + 1) * MIXING_RANK]
        up_columns = lowrank_matrix[:, 5 * MIXING_RANK + mixing_component * MIXING_RANK:5 * MIXING_RANK + (mixing_component + 1) * MIXING_RANK]
        offset = lowrank_output_backward(matrix_product(sequence_piece, up_columns.T))
        input_rows.append(lowrank_output(normed + delta * (stratum_settings[3 + mixing_component] + offset)))
    decay_column_start = 10 * MIXING_RANK
    decay_latent = lowrank_output(jnp.tanh(lowrank_output_backward(matrix_product(input_rows[0], lowrank_matrix[:, decay_column_start:decay_column_start + DECAY_RANK]))))
    decay_offset = lowrank_output_backward(matrix_product(decay_latent, lowrank_matrix[:, decay_column_start + DECAY_RANK:].T))
    fading_exponent = -jnp.exp(stratum_settings[8] + decay_offset)
    keys_all = lowrank_output_backward(matrix_product(input_rows[1], mixing_matrix[:, 0:D]))
    values_all = lowrank_output_backward(matrix_product(input_rows[2], mixing_matrix[:, D:2 * D]))
    acceptance_entries = lowrank_output_backward(matrix_product(input_rows[3], mixing_matrix[:, 2 * D:3 * D]))
    gate_pre = lowrank_output_backward(matrix_product(input_rows[4], mixing_matrix[:, 3 * D:4 * D]))
    block_count = LENGTH // TOK_SEQ

    def heads(values):
        return values.reshape(block_count, TOK_SEQ, ATTENDER_NUMBER, ATTENDER_SPAN).transpose(0, 2, 1, 3)

    def advance(persisting_memory, attention_segment_apply):
        present_memory, present_reward_factor = persisting_memory
        stratum_response, successor_memory = recursive_segment(attention_segment_apply[0], attention_segment_apply[1], attention_segment_apply[2], attention_segment_apply[3], present_reward_factor, present_memory)
        return ((successor_memory, present_reward_factor), stratum_response)
    carry_end, outputs = lax.scan(jax.checkpoint(advance), (starting_state, stratum_settings[9].reshape(ATTENDER_NUMBER, ATTENDER_SPAN)), (heads(acceptance_entries), heads(keys_all), heads(values_all), heads(fading_exponent)))
    wkv_out = outputs.transpose(0, 2, 1, 3).reshape(LENGTH, D)
    grouped = layer_norm(wkv_out.reshape(LENGTH, ATTENDER_NUMBER, ATTENDER_SPAN), stratum_settings[10].reshape(ATTENDER_NUMBER, ATTENDER_SPAN), stratum_settings[11].reshape(ATTENDER_NUMBER, ATTENDER_SPAN), group_eps)
    gated = lowrank_output(grouped.reshape(LENGTH, D) * jax.nn.silu(gate_pre))
    branch = lowrank_output_backward(matrix_product(gated, mixing_matrix[:, 4 * D:].T))
    middle = hidden_input + branch
    normed_two = layer_norm(middle, stratum_settings[12], stratum_settings[13], layer_eps)
    shifted_two = jnp.concatenate([previous_token[1:2], normed_two[:-1]], axis=0)
    delta_two = shifted_two - normed_two
    key_in = lowrank_output(normed_two + delta_two * stratum_settings[14])
    recv_in = lowrank_output(normed_two + delta_two * stratum_settings[15])
    key_act = lowrank_output_backward(matrix_product(key_in, feedforward_matrix[:, :FF]))
    squared = lowrank_output(jnp.square(jax.nn.relu(key_act)))
    value_out = lowrank_output_backward(matrix_product(squared, feedforward_matrix[:, FF + D:].T))
    recept_act = lowrank_output_backward(matrix_product(recv_in, feedforward_matrix[:, FF:FF + D]))
    return middle + jax.nn.sigmoid(recept_act) * value_out

def reference(tokens, previous, initial_state, mixing_weights, lowrank_weights, vectors, feedforward_weights, cotangent):
    mixing_matrix = mixing_weights.astype(jnp.float32)
    lowrank_matrix = lowrank_weights.astype(jnp.float32)
    feedforward_matrix = feedforward_weights.astype(jnp.float32)
    starting_state = initial_state.reshape(SEQS, ATTENDER_NUMBER, ATTENDER_SPAN, ATTENDER_SPAN)

    def one_sequence(totals, items):
        hidden_input, previous_token, single_initial_state, cot_one = items

        def sequence_forward(hidden_value, initial_value, mixing_value, lowrank_value, vectors_value, feedforward_value):
            return forward_pass(hidden_value, previous_token, initial_value, mixing_value, lowrank_value, vectors_value, feedforward_value)
        final_result, backward_function = jax.vjp(sequence_forward, hidden_input, single_initial_state, mixing_matrix, lowrank_matrix, vectors, feedforward_matrix)
        grads = backward_function(cot_one)
        totals = tuple((total + grad for total, grad in zip(totals, grads[2:])))
        return (totals, (final_result, grads[0], grads[1]))
    zero_filled = (jnp.zeros_like(mixing_matrix), jnp.zeros_like(lowrank_matrix), jnp.zeros_like(vectors), jnp.zeros_like(feedforward_matrix))
    totals, (results, hidden_grad, initial_state_gradient) = lax.scan(one_sequence, zero_filled, (tokens.astype(jnp.float32), previous, starting_state, cotangent.astype(jnp.float32)))
    return (results.astype(jnp.bfloat16), hidden_grad, initial_state_gradient.reshape(SEQS * ATTENDER_NUMBER * ATTENDER_SPAN, ATTENDER_SPAN), totals[0], totals[1], totals[2], totals[3])
```

```python
import functools

import jax
import jax.numpy as jnp
from jax import lax
from jax.experimental import pallas as pl
from jax.experimental.pallas import tpu as pltpu
from jax.sharding import PartitionSpec as P

HEADS = 32
SPAN = 64
FF = 7168
RANK = 32
DRANK = 64
LN_EPS = 1e-05
GN_EPS = 0.00064
GROUP = 2

F32 = jnp.float32
BF16 = jnp.bfloat16
HI = lax.Precision.HIGHEST


def nn(a, b):
    return jnp.dot(a, b, preferred_element_type=F32)


def nt(a, b):
    return lax.dot_general(a, b, (((1,), (1,)), ((), ())), preferred_element_type=F32)


def tn(a, b):
    return lax.dot_general(a, b, (((0,), (0,)), ((), ())), preferred_element_type=F32)


def knn(a, b):
    return lax.dot_general(
        a, b, (((1,), (0,)), ((), ())), precision=HI, preferred_element_type=F32
    )


def knt(a, b):
    return lax.dot_general(
        a, b, (((1,), (1,)), ((), ())), precision=HI, preferred_element_type=F32
    )


def ktn(a, b):
    return lax.dot_general(
        a, b, (((0,), (0,)), ((), ())), precision=HI, preferred_element_type=F32
    )


def low_lanes(shape):
    return lax.broadcasted_iota(jnp.int32, shape, len(shape) - 1) < SPAN


def head_sum(x):
    low = low_lanes(x.shape)
    s0 = jnp.sum(jnp.where(low, x, 0.0), axis=-1, keepdims=True)
    s1 = jnp.sum(jnp.where(low, 0.0, x), axis=-1, keepdims=True)
    return jnp.where(low, s0, s1)


def two_rows(x):
    low = low_lanes(x.shape)
    return jnp.concatenate([jnp.where(low, x, 0.0), jnp.where(low, 0.0, x)], axis=0)


def fold(full):
    return jnp.where(low_lanes((SPAN, 2 * SPAN)), full[:SPAN], full[SPAN:])


def unfold(state):
    low = low_lanes(state.shape)
    return jnp.concatenate([jnp.where(low, state, 0.0), jnp.where(low, 0.0, state)], axis=0)


def running(w, upper=False):
    count = w.shape[0]
    row = lax.broadcasted_iota(jnp.int32, (count, count), 0)
    col = lax.broadcasted_iota(jnp.int32, (count, count), 1)
    keep = (col >= row) if upper else (col <= row)
    return knn(jnp.where(keep, 1.0, 0.0).astype(F32), w)


def strict(count):
    row = lax.broadcasted_iota(jnp.int32, (2 * count, count), 0)
    col = lax.broadcasted_iota(jnp.int32, (2 * count, count), 1)
    row = jnp.where(row >= count, row - count, row)
    return row > col, row == col


def affinity(r, k, u, q, ks):
    count = r.shape[0]
    below, diag = strict(count)
    raw = knt(two_rows(q), ks)
    share = jnp.sum(two_rows(r * u * k), axis=-1, keepdims=True)
    return jnp.where(below, raw, jnp.where(diag, share, 0.0))


def totals_kernel(k_ref, v_ref, w_ref, out_ref):
    cum = running(w_ref[...])
    total = cum[-1:, :]
    kc = k_ref[...] * jnp.exp(total - cum)
    out_ref[0, :SPAN, :] = fold(ktn(v_ref[...], kc))
    out_ref[0, SPAN:, :] = jnp.broadcast_to(jnp.exp(total), (8, 2 * SPAN))


def group_norm(y, gain, bias):
    centred = y - head_sum(y) * (1.0 / SPAN)
    spread = head_sum(centred * centred) * (1.0 / SPAN)
    scale = lax.rsqrt(spread + GN_EPS)
    normal = centred * scale
    return normal, scale, normal * gain + bias


def forward_kernel(r_ref, k_ref, v_ref, w_ref, g_ref, s_ref, p_ref, y_ref, gated_ref):
    r, k, v, w = r_ref[...], k_ref[...], v_ref[...], w_ref[...]
    cum = running(w)
    q = r * jnp.exp(cum - w)
    ks = k * jnp.exp(-cum)
    aff = affinity(r, k, p_ref[0:1, :], q, ks)
    count = r.shape[0]
    v2 = two_rows(v)
    y = (
        knt(q, unfold(s_ref[0]))
        + knn(aff[:count], v2[:count])
        + knn(aff[count:], v2[count:])
    )
    y_ref[...] = y
    gate = g_ref[...]
    _, _, grouped = group_norm(y, p_ref[1:2, :], p_ref[2:3, :])
    gated_ref[...] = (grouped * gate * jax.nn.sigmoid(gate)).astype(BF16)


def gate_kernel(gg_ref, g_ref, y_ref, r_ref, w_ref, p_ref, gate_ref, dy_ref, out_ref):
    gated_grad, gate, y = gg_ref[...], g_ref[...], y_ref[...]
    gain = p_ref[1:2, :]
    normal, scale, grouped = group_norm(y, gain, p_ref[2:3, :])
    sig = jax.nn.sigmoid(gate)
    gate_ref[...] = (gated_grad * grouped * sig * (1.0 + gate * (1.0 - sig))).astype(BF16)
    outer = gated_grad * gate * sig
    inner = outer * gain
    dy = scale * (
        inner
        - head_sum(inner) * (1.0 / SPAN)
        - normal * (head_sum(inner * normal) * (1.0 / SPAN))
    )
    dy_ref[...] = dy
    w = w_ref[...]
    q = r_ref[...] * jnp.exp(running(w) - w)
    out_ref[0, :SPAN, :] = fold(ktn(dy, q))
    gain_grad = jnp.sum(outer * normal, axis=0, keepdims=True)
    bias_grad = jnp.sum(outer, axis=0, keepdims=True)
    out_ref[0, SPAN:, :] = jnp.concatenate(
        [gain_grad, bias_grad, jnp.zeros((6, 2 * SPAN), F32)], axis=0
    )


def backward_kernel(
    r_ref, k_ref, v_ref, w_ref, dy_ref, s_ref, gs_ref, p_ref,
    dr_ref, dk_ref, dv_ref, dd_ref, out_ref,
):
    r, k, v, w, dy = r_ref[...], k_ref[...], v_ref[...], w_ref[...], dy_ref[...]
    u = p_ref[0:1, :]
    count = r.shape[0]
    cum = running(w)
    total = cum[-1:, :]
    e_before, e_minus, e_carry = jnp.exp(cum - w), jnp.exp(-cum), jnp.exp(total - cum)
    q, ks, kc = r * e_before, k * e_minus, k * e_carry
    aff = affinity(r, k, u, q, ks)
    below, _ = strict(count)
    dy2 = two_rows(dy)
    d_aff = jnp.where(below, knt(dy2, v), 0.0)
    own = head_sum(dy * v)
    state, grad_state = s_ref[0], gs_ref[0]
    state2, grad2 = unfold(state), unfold(grad_state)
    ks2 = two_rows(ks)
    dq = knn(dy, state2) + knn(d_aff[:count], ks2[:count]) + knn(d_aff[count:], ks2[count:])
    dks = ktn(d_aff, two_rows(q))
    dkc = knn(v, grad2)
    dv_ref[...] = (ktn(aff, dy2) + knt(kc, grad2)).astype(BF16)
    dr_ref[...] = (dq * e_before + own * u * k).astype(BF16)
    dk_ref[...] = (dks * e_minus + dkc * e_carry + own * u * r).astype(BF16)
    gq, gc = q * dq, kc * dkc
    d_total = jnp.sum(gc, axis=0, keepdims=True) + jnp.exp(total) * jnp.sum(
        state * grad_state, axis=0, keepdims=True
    )
    dw = running(gq - ks * dks - gc, upper=True) - gq + d_total
    term = dw * w
    dd_ref[...] = term.astype(BF16)
    out_ref[0] = jnp.concatenate(
        [
            jnp.sum(term, axis=0, keepdims=True),
            jnp.sum(own * r * k, axis=0, keepdims=True),
            jnp.zeros((6, 2 * SPAN), F32),
        ],
        axis=0,
    )


def block_call(kernel, chunks, step, width, ins, outs, args):
    lane = 2 * SPAN
    kinds = {
        "t": pl.BlockSpec((step, lane), lambda c, h: (c, h)),
        "s": pl.BlockSpec((1, SPAN, lane), lambda c, h: (c, 0, h)),
        "x": pl.BlockSpec((1, SPAN + 8, lane), lambda c, h: (c, 0, h)),
        "e": pl.BlockSpec((1, 8, lane), lambda c, h: (c, 0, h)),
        "p": pl.BlockSpec((8, lane), lambda c, h: (0, h)),
    }
    shapes = {
        "t": lambda d: jax.ShapeDtypeStruct((chunks * step, width), d),
        "x": lambda d: jax.ShapeDtypeStruct((chunks, SPAN + 8, width), d),
        "e": lambda d: jax.ShapeDtypeStruct((chunks, 8, width), d),
    }
    return pl.pallas_call(
        kernel,
        grid=(chunks, width // lane),
        in_specs=[kinds[kind] for kind in ins],
        out_specs=[kinds[kind] for kind, _ in outs],
        out_shape=[shapes[kind](dtype) for kind, dtype in outs],
        compiler_params=pltpu.CompilerParams(vmem_limit_bytes=48 * 1024 * 1024),
    )(*args)


def on_device(
    count,
    tokens,
    previous,
    initial_state,
    mixing_weights,
    lowrank_weights,
    vectors,
    feedforward_weights,
    cotangent,
):
    size = GROUP
    teams = count // size
    me = lax.axis_index("seq")
    member = lax.rem(me, size)
    team = lax.div(me, size)
    _, step, width = tokens.shape
    rows = mixing_weights.shape[0]
    part = width // size
    ff_part = FF // size
    team_rows = rows * size
    across = [[t * size + m for t in range(teams)] for m in range(size)]

    def to_partner(value, k):
        return lax.ppermute(value, "seq", [(d, d ^ k) for d in range(count)])

    def team_gather(value):
        return [value] + [to_partner(value, k) for k in range(1, size)]

    def team_sum(partial, kind=BF16):
        own = partial[:step]
        for k in range(1, size):
            own = own + to_partner(partial[k * step : (k + 1) * step].astype(kind), k).astype(F32)
        return own

    def ordered(pieces):
        if size == 2:
            flip = member == 1
            return [
                jnp.where(flip, pieces[1], pieces[0]),
                jnp.where(flip, pieces[0], pieces[1]),
            ]
        stacked = jnp.stack(pieces)
        return [
            lax.dynamic_index_in_dim(stacked, member ^ m, 0, keepdims=False) for m in range(size)
        ]

    def neighbour(value, offset):
        pairs = [(d, d + offset) for d in range(count) if 0 <= d + offset < count]
        return lax.ppermute(value, "seq", pairs)

    def take_columns(value, spans, who):
        return jnp.concatenate(
            [
                lax.dynamic_slice_in_dim(value, start + who * wide, wide, axis=1)
                for start, wide in spans
            ],
            axis=1,
        )

    def gather_weights(value, spans):
        pieces = [take_columns(value, spans, member)]
        for k in range(1, size):
            pieces.append(to_partner(take_columns(value, spans, member ^ k), k))
        local = jnp.concatenate(ordered(pieces), axis=0)
        return lax.all_gather(local, "seq", axis=0, tiled=True, axis_index_groups=across)

    def sum_gradients(pieces):
        joint = jnp.concatenate(pieces, axis=1)
        summed = lax.psum_scatter(
            joint, "seq", scatter_dimension=0, tiled=True, axis_index_groups=across
        )
        mine = [lax.dynamic_slice_in_dim(summed, member * rows, rows, axis=0)]
        for k in range(1, size):
            mine.append(
                to_partner(
                    lax.dynamic_slice_in_dim(summed, (member ^ k) * rows, rows, axis=0), k
                )
            )
        by_member = ordered(mine)
        outs, start = [], 0
        for piece in pieces:
            wide = piece.shape[1]
            outs += [p[:, start : start + wide] for p in by_member]
            start += wide
        return jnp.concatenate(outs, axis=1).astype(F32)

    lowrank = lax.all_gather(lowrank_weights, "seq", axis=0, tiled=True)
    small = lax.all_gather(
        jnp.concatenate([vectors, initial_state], axis=1), "seq", axis=0, tiled=True
    )
    mix_spans = [(c * width, part) for c in range(5)]
    ff_spans = [(0, ff_part), (FF, part), (FF + width, ff_part)]
    mixing = gather_weights(mixing_weights, mix_spans)
    feed = gather_weights(feedforward_weights, ff_spans)
    w_main = [mixing[:, c * part : (c + 1) * part] for c in range(4)]
    w_out = mixing[:, 4 * part :]
    w_key = feed[:, :ff_part]
    w_rec = feed[:, ff_part : ff_part + part]
    w_val = feed[:, ff_part + part :]

    vec = small[:, :16].T
    first_state = lax.dynamic_slice_in_dim(small[:, 16:], member * part, part, axis=0).T
    vec_part = lax.dynamic_slice_in_dim(vec, member * part, part, axis=1)
    wkv_rows = jnp.concatenate([vec_part[9:12], jnp.zeros((5, part), F32)], axis=0)
    is_first = me == 0

    up_start, decay_start, decay_up = 5 * RANK, 10 * RANK, 10 * RANK + DRANK
    w_down = lowrank[:, :up_start]
    w_ups = [lowrank[:, up_start + c * RANK : up_start + (c + 1) * RANK] for c in range(5)]
    w_ddown = lowrank[:, decay_start:decay_up]
    w_dup = lax.dynamic_slice_in_dim(lowrank[:, decay_up:], member * part, part, axis=0)

    hidden = tokens.astype(F32).reshape(step, width)

    def norm_parts(value):
        centred = value - jnp.mean(value, axis=-1, keepdims=True)
        spread = jnp.mean(centred * centred, axis=-1, keepdims=True)
        scale = lax.rsqrt(spread + LN_EPS)
        return centred * scale, scale

    def norm_back(grad, gain, normal, scale):
        e = grad * gain
        return scale * (
            e
            - jnp.mean(e, axis=-1, keepdims=True)
            - normal * jnp.mean(e * normal, axis=-1, keepdims=True)
        )

    def with_previous(value, start_row):
        arrived = neighbour(value[-1:, :], 1)
        arrived = jnp.where(is_first, start_row, arrived)
        return jnp.concatenate([arrived, value[:-1]], axis=0)

    def from_next(value):
        return jnp.concatenate([value[1:], neighbour(value[:1, :], -1)], axis=0)

    normal_one, scale_one = norm_parts(hidden)
    normed = normal_one * vec[0] + vec[1]
    delta = with_previous(normed, previous[0, 0:1, :]) - normed
    blend = (normed + delta * vec[2]).astype(BF16)
    mix_tanh = jnp.tanh(nn(blend, w_down))
    mix_hidden = mix_tanh.astype(BF16)
    hidden_c = [mix_hidden[:, c * RANK : (c + 1) * RANK] for c in range(5)]
    coeff = [vec[3 + c] + nt(hidden_c[c], w_ups[c]) for c in range(5)]
    mixed = [(normed + delta * coeff[c]).astype(BF16) for c in range(5)]
    decay_tanh = jnp.tanh(nn(mixed[0], w_ddown))
    decay_hidden = decay_tanh.astype(BF16)

    mixed_all = [jnp.concatenate(team_gather(mixed[c]), axis=0) for c in range(1, 5)]
    dh_all = jnp.concatenate(team_gather(decay_hidden), axis=0)
    log_decay = -jnp.exp(vec_part[8] + nt(dh_all, w_dup))
    keys, values, receipt, gate_pre = [nn(mixed_all[c], w_main[c]) for c in range(4)]

    call = functools.partial(block_call, chunks=size, step=step, width=part)
    (totals,) = call(
        totals_kernel, ins="ttt", outs=[("x", F32)], args=(keys, values, log_decay)
    )
    by_time = ordered([totals[k] for k in range(size)])
    chunk_add = [p[:SPAN] for p in by_time]
    chunk_decay = [p[SPAN : SPAN + 1] for p in by_time]
    tot_d, tot_s = chunk_decay[0], chunk_add[0]
    for d, s in zip(chunk_decay[1:], chunk_add[1:]):
        tot_d, tot_s = tot_d * d, d * tot_s + s
    pre_d, pre_s = jnp.ones_like(tot_d), jnp.zeros_like(tot_s)
    group_decay = tot_d
    partner_decays, total_decays = [], []
    bits = [1 << j for j in range(max(teams - 1, 0).bit_length())]
    for bit in bits:
        sent = jnp.concatenate([tot_s, jnp.broadcast_to(tot_d, (8, part))], axis=0)
        got = to_partner(sent, bit * size)
        got_s, got_d = got[:SPAN], got[SPAN : SPAN + 1]
        partner_decays.append(got_d)
        total_decays.append(tot_d)
        earlier = lax.rem(lax.div(team, bit), 2) == 1
        pre_s = jnp.where(earlier, pre_d * got_s + pre_s, pre_s)
        pre_d = jnp.where(earlier, pre_d * got_d, pre_d)
        tot_s = jnp.where(earlier, tot_d * got_s + tot_s, got_d * tot_s + got_s)
        tot_d = tot_d * got_d
    state = pre_d * first_state + pre_s
    states = []
    for d, s in zip(chunk_decay, chunk_add):
        states.append(state)
        state = d * state + s
    state_in = jnp.stack(ordered(states))

    wkv, gated = call(
        forward_kernel,
        ins="tttttsp",
        outs=[("t", F32), ("t", BF16)],
        args=(receipt, keys, values, log_decay, gate_pre, state_in, wkv_rows),
    )
    middle = hidden + team_sum(nt(gated, w_out))

    normal_two, scale_two = norm_parts(middle)
    normed_two = normal_two * vec[12] + vec[13]
    delta_two = with_previous(normed_two, previous[0, 1:2, :]) - normed_two
    key_in = (normed_two + delta_two * vec[14]).astype(BF16)
    recv_in = (normed_two + delta_two * vec[15]).astype(BF16)
    key_all = jnp.concatenate(team_gather(key_in), axis=0)
    recv_all = jnp.concatenate(team_gather(recv_in), axis=0)
    relu = jnp.maximum(nn(key_all, w_key), 0.0)
    squared = (relu * relu).astype(BF16)
    value_out = team_sum(nt(squared, w_val))
    recept_act = nn(recv_all, w_rec)
    recept_pieces = [recept_act[:step]] + [
        to_partner(recept_act[k * step : (k + 1) * step], k) for k in range(1, size)
    ]
    recept = jax.nn.sigmoid(jnp.concatenate(ordered(recept_pieces), axis=1))
    block_output = (middle + recept * value_out).astype(BF16).reshape(1, step, width)

    upstream = cotangent.astype(F32).reshape(step, width)
    value_grad = (upstream * recept).astype(BF16)
    recept_grad = (upstream * value_out * recept * (1.0 - recept)).astype(BF16)
    vg_all = jnp.concatenate(team_gather(value_grad), axis=0)
    rg_all = jnp.concatenate(
        [lax.dynamic_slice_in_dim(recept_grad, member * part, part, axis=1)]
        + [
            to_partner(
                lax.dynamic_slice_in_dim(recept_grad, (member ^ k) * part, part, axis=1), k
            )
            for k in range(1, size)
        ],
        axis=0,
    )
    key_grad = (nn(vg_all, w_val) * (2.0 * relu)).astype(BF16)
    key_in_grad = team_sum(nt(key_grad, w_key))
    recv_in_grad = team_sum(nt(rg_all, w_rec))
    feedforward_gradient = sum_gradients(
        [
            tn(key_all, key_grad).astype(BF16),
            tn(recv_all, rg_all).astype(BF16),
            tn(vg_all, squared).astype(BF16),
        ]
    )
    shifted_grad = key_in_grad * vec[14] + recv_in_grad * vec[15]
    two_grad = (
        key_in_grad * (1.0 - vec[14]) + recv_in_grad * (1.0 - vec[15]) + from_next(shifted_grad)
    )
    middle_grad = upstream + norm_back(two_grad, vec[12], normal_two, scale_two)
    col_12 = jnp.sum(two_grad * normal_two, axis=0)
    col_13 = jnp.sum(two_grad, axis=0)
    col_14 = jnp.sum(key_in_grad * delta_two, axis=0)
    col_15 = jnp.sum(recv_in_grad * delta_two, axis=0)

    branch_grad = middle_grad.astype(BF16)
    bg_all = jnp.concatenate(team_gather(branch_grad), axis=0)
    gated_grad = nn(bg_all, w_out)
    gate_grad, wkv_grad, local = call(
        gate_kernel,
        ins="tttttp",
        outs=[("t", BF16), ("t", F32), ("x", F32)],
        args=(gated_grad, gate_pre, wkv, receipt, log_decay, wkv_rows),
    )
    local_by_time = ordered([local[k, :SPAN] for k in range(size)])
    tot_g = local_by_time[-1]
    for d, s in zip(chunk_decay[-2::-1], local_by_time[-2::-1]):
        tot_g = d * tot_g + s
    suf_d, suf_g = jnp.ones_like(group_decay), jnp.zeros_like(tot_g)
    for bit, got_d, tot_d in zip(bits, partner_decays, total_decays):
        got_g = to_partner(tot_g, bit * size)
        later = lax.rem(lax.div(team, bit), 2) == 0
        suf_g = jnp.where(later, suf_d * got_g + suf_g, suf_g)
        suf_d = jnp.where(later, suf_d * got_d, suf_d)
        tot_g = jnp.where(later, tot_d * got_g + tot_g, got_d * tot_g + got_g)
    grad_state = suf_g
    grad_states = [None] * size
    for t in reversed(range(size)):
        grad_states[t] = grad_state
        grad_state = chunk_decay[t] * grad_state + local_by_time[t]
    grad_out = jnp.stack(ordered(grad_states))

    holder = lax.div(me * rows, part)

    def rows_of(who):
        start = lax.rem((team * size + who) * rows, part)
        return lax.dynamic_slice_in_dim(tot_g, start, rows, axis=1)

    state_rows = rows_of(member)
    for k in range(1, size):
        other = to_partner(rows_of(member ^ k), k)
        state_rows = jnp.where(holder == (member ^ k), other, state_rows)
    initial_state_gradient = state_rows.T

    d_receipt, d_keys, d_values, d_decay, extra = call(
        backward_kernel,
        ins="tttttssp",
        outs=[("t", BF16)] * 4 + [("e", F32)],
        args=(receipt, keys, values, log_decay, wkv_grad, state_in, grad_out, wkv_rows),
    )
    grads = [d_keys, d_values, d_receipt, gate_grad]
    mixing_gradient = sum_gradients(
        [tn(mixed_all[c], grads[c]).astype(BF16) for c in range(4)]
        + [tn(bg_all, gated).astype(BF16)]
    )
    mixed_grad = [None] + [team_sum(nt(grads[c], w_main[c])) for c in range(4)]
    decay_latent_grad = team_sum(nn(d_decay, w_dup), F32)
    decay_pre = (decay_latent_grad * (1.0 - decay_tanh * decay_tanh)).astype(BF16)
    mixed_grad[0] = nt(decay_pre, w_ddown)

    shift_grads = [mixed_grad[c] * delta for c in range(5)]
    offset_grads = [s.astype(BF16) for s in shift_grads]
    mix_latent_grad = jnp.concatenate(
        [nn(offset_grads[c], w_ups[c]) for c in range(5)], axis=1
    )
    mix_pre = (mix_latent_grad * (1.0 - mix_tanh * mix_tanh)).astype(BF16)
    blend_grad = nt(mix_pre, w_down)
    delta_grad = blend_grad * vec[2]
    normed_grad = blend_grad
    for c in range(5):
        delta_grad = delta_grad + mixed_grad[c] * coeff[c]
        normed_grad = normed_grad + mixed_grad[c]
    normed_grad = normed_grad - delta_grad + from_next(delta_grad)
    block_input_gradient = (
        middle_grad + norm_back(normed_grad, vec[0], normal_one, scale_one)
    ).reshape(1, step, width)


    def spread(value):
        zero = jnp.zeros((value.shape[0], width), F32)
        return lax.dynamic_update_slice_in_dim(zero, value, member * part, axis=1)

    gn_cols = jnp.sum(local[:, SPAN : SPAN + 2], axis=0)
    wkv_cols = jnp.sum(extra[:, :2], axis=0)
    vec_grad = jnp.concatenate(
        [
            jnp.stack(
                [
                    jnp.sum(normed_grad * normal_one, axis=0),
                    jnp.sum(normed_grad, axis=0),
                    jnp.sum(blend_grad * delta, axis=0),
                ]
                + [jnp.sum(s, axis=0) for s in shift_grads]
            ),
            spread(jnp.concatenate([wkv_cols, gn_cols], axis=0)),
            jnp.stack([col_12, col_13, col_14, col_15]),
        ],
        axis=0,
    )
    low_grad = jnp.concatenate(
        [
            tn(mix_pre, blend),
            *[tn(hidden_c[c], offset_grads[c]) for c in range(5)],
            tn(decay_pre, mixed[0]),
            spread(tn(dh_all, d_decay)),
            vec_grad,
        ],
        axis=0,
    )
    low_sum = lax.psum_scatter(low_grad.T, "seq", scatter_dimension=0, tiled=True)
    return (
        block_output,
        block_input_gradient,
        initial_state_gradient,
        mixing_gradient,
        low_sum[:, : decay_up + DRANK],
        low_sum[:, decay_up + DRANK :],
        feedforward_gradient,
    )


def solution(mesh):
    rowwise = P("seq", None)
    tokenwise = P(None, "seq", None)
    return jax.shard_map(
        functools.partial(on_device, mesh.shape["seq"]),
        mesh=mesh,
        in_specs=(tokenwise, P(), rowwise, rowwise, rowwise, rowwise, rowwise, tokenwise),
        out_specs=(tokenwise, tokenwise, rowwise, rowwise, rowwise, rowwise, rowwise),
        check_vma=False,
    )
```

```python
import functools

import jax
import jax.numpy as jnp
from jax import lax
from jax.experimental import pallas as pl
from jax.experimental.pallas import tpu as pltpu
from jax.sharding import PartitionSpec as P

HEADS = 32
SPAN = 64
FF = 7168
RANK = 32
DRANK = 64
LN_EPS = 1e-05
GN_EPS = 0.00064
MEMBER_MASKS = (1, 8)

F32 = jnp.float32
BF16 = jnp.bfloat16
HI = lax.Precision.HIGHEST


def nn(a, b):
    return jnp.dot(a, b, preferred_element_type=F32)


def nt(a, b):
    return lax.dot_general(a, b, (((1,), (1,)), ((), ())), preferred_element_type=F32)


def tn(a, b):
    return lax.dot_general(a, b, (((0,), (0,)), ((), ())), preferred_element_type=F32)


def knn(a, b):
    return lax.dot_general(
        a, b, (((1,), (0,)), ((), ())), precision=HI, preferred_element_type=F32
    )


def knt(a, b):
    return lax.dot_general(
        a, b, (((1,), (1,)), ((), ())), precision=HI, preferred_element_type=F32
    )


def ktn(a, b):
    return lax.dot_general(
        a, b, (((0,), (0,)), ((), ())), precision=HI, preferred_element_type=F32
    )


def low_lanes(shape):
    return lax.broadcasted_iota(jnp.int32, shape, len(shape) - 1) < SPAN


def head_sum(x):
    low = low_lanes(x.shape)
    s0 = jnp.sum(jnp.where(low, x, 0.0), axis=-1, keepdims=True)
    s1 = jnp.sum(jnp.where(low, 0.0, x), axis=-1, keepdims=True)
    return jnp.where(low, s0, s1)


def two_rows(x):
    low = low_lanes(x.shape)
    return jnp.concatenate([jnp.where(low, x, 0.0), jnp.where(low, 0.0, x)], axis=0)


def fold(full):
    return jnp.where(low_lanes((SPAN, 2 * SPAN)), full[:SPAN], full[SPAN:])


def unfold(state):
    low = low_lanes(state.shape)
    return jnp.concatenate([jnp.where(low, state, 0.0), jnp.where(low, 0.0, state)], axis=0)


def running(w, upper=False):
    count = w.shape[0]
    row = lax.broadcasted_iota(jnp.int32, (count, count), 0)
    col = lax.broadcasted_iota(jnp.int32, (count, count), 1)
    keep = (col >= row) if upper else (col <= row)
    return knn(jnp.where(keep, 1.0, 0.0).astype(F32), w)


def strict(count):
    row = lax.broadcasted_iota(jnp.int32, (2 * count, count), 0)
    col = lax.broadcasted_iota(jnp.int32, (2 * count, count), 1)
    row = jnp.where(row >= count, row - count, row)
    return row > col, row == col


def affinity(r, k, u, q, ks):
    count = r.shape[0]
    below, diag = strict(count)
    raw = knt(two_rows(q), ks)
    share = jnp.sum(two_rows(r * u * k), axis=-1, keepdims=True)
    return jnp.where(below, raw, jnp.where(diag, share, 0.0))


def totals_kernel(k_ref, v_ref, w_ref, out_ref):
    cum = running(w_ref[...])
    total = cum[-1:, :]
    kc = k_ref[...] * jnp.exp(total - cum)
    out_ref[0, :SPAN, :] = fold(ktn(v_ref[...], kc))
    out_ref[0, SPAN:, :] = jnp.broadcast_to(jnp.exp(total), (8, 2 * SPAN))


def group_norm(y, gain, bias):
    centred = y - head_sum(y) * (1.0 / SPAN)
    spread = head_sum(centred * centred) * (1.0 / SPAN)
    scale = lax.rsqrt(spread + GN_EPS)
    normal = centred * scale
    return normal, scale, normal * gain + bias


def forward_kernel(r_ref, k_ref, v_ref, w_ref, g_ref, s_ref, p_ref, y_ref, gated_ref):
    r, k, v, w = r_ref[...], k_ref[...], v_ref[...], w_ref[...]
    cum = running(w)
    q = r * jnp.exp(cum - w)
    ks = k * jnp.exp(-cum)
    aff = affinity(r, k, p_ref[0:1, :], q, ks)
    count = r.shape[0]
    v2 = two_rows(v)
    y = (
        knt(q, unfold(s_ref[0]))
        + knn(aff[:count], v2[:count])
        + knn(aff[count:], v2[count:])
    )
    y_ref[...] = y
    gate = g_ref[...]
    _, _, grouped = group_norm(y, p_ref[1:2, :], p_ref[2:3, :])
    gated_ref[...] = (grouped * gate * jax.nn.sigmoid(gate)).astype(BF16)


def gate_kernel(gg_ref, g_ref, y_ref, r_ref, w_ref, p_ref, gate_ref, dy_ref, out_ref):
    gated_grad, gate, y = gg_ref[...], g_ref[...], y_ref[...]
    gain = p_ref[1:2, :]
    normal, scale, grouped = group_norm(y, gain, p_ref[2:3, :])
    sig = jax.nn.sigmoid(gate)
    gate_ref[...] = (gated_grad * grouped * sig * (1.0 + gate * (1.0 - sig))).astype(BF16)
    outer = gated_grad * gate * sig
    inner = outer * gain
    dy = scale * (
        inner
        - head_sum(inner) * (1.0 / SPAN)
        - normal * (head_sum(inner * normal) * (1.0 / SPAN))
    )
    dy_ref[...] = dy
    w = w_ref[...]
    q = r_ref[...] * jnp.exp(running(w) - w)
    out_ref[0, :SPAN, :] = fold(ktn(dy, q))
    gain_grad = jnp.sum(outer * normal, axis=0, keepdims=True)
    bias_grad = jnp.sum(outer, axis=0, keepdims=True)
    out_ref[0, SPAN:, :] = jnp.concatenate(
        [gain_grad, bias_grad, jnp.zeros((6, 2 * SPAN), F32)], axis=0
    )


def backward_kernel(
    r_ref, k_ref, v_ref, w_ref, dy_ref, s_ref, gs_ref, p_ref,
    dr_ref, dk_ref, dv_ref, dd_ref, out_ref,
):
    r, k, v, w, dy = r_ref[...], k_ref[...], v_ref[...], w_ref[...], dy_ref[...]
    u = p_ref[0:1, :]
    count = r.shape[0]
    cum = running(w)
    total = cum[-1:, :]
    e_before, e_minus, e_carry = jnp.exp(cum - w), jnp.exp(-cum), jnp.exp(total - cum)
    q, ks, kc = r * e_before, k * e_minus, k * e_carry
    aff = affinity(r, k, u, q, ks)
    below, _ = strict(count)
    dy2 = two_rows(dy)
    d_aff = jnp.where(below, knt(dy2, v), 0.0)
    own = head_sum(dy * v)
    state, grad_state = s_ref[0], gs_ref[0]
    state2, grad2 = unfold(state), unfold(grad_state)
    ks2 = two_rows(ks)
    dq = knn(dy, state2) + knn(d_aff[:count], ks2[:count]) + knn(d_aff[count:], ks2[count:])
    dks = ktn(d_aff, two_rows(q))
    dkc = knn(v, grad2)
    dv_ref[...] = (ktn(aff, dy2) + knt(kc, grad2)).astype(BF16)
    dr_ref[...] = (dq * e_before + own * u * k).astype(BF16)
    dk_ref[...] = (dks * e_minus + dkc * e_carry + own * u * r).astype(BF16)
    gq, gc = q * dq, kc * dkc
    d_total = jnp.sum(gc, axis=0, keepdims=True) + jnp.exp(total) * jnp.sum(
        state * grad_state, axis=0, keepdims=True
    )
    dw = running(gq - ks * dks - gc, upper=True) - gq + d_total
    term = dw * w
    dd_ref[...] = term.astype(BF16)
    out_ref[0] = jnp.concatenate(
        [
            jnp.sum(term, axis=0, keepdims=True),
            jnp.sum(own * r * k, axis=0, keepdims=True),
            jnp.zeros((6, 2 * SPAN), F32),
        ],
        axis=0,
    )


def block_call(kernel, chunks, step, width, ins, outs, args):
    lane = 2 * SPAN
    kinds = {
        "t": pl.BlockSpec((step, lane), lambda c, h: (c, h)),
        "s": pl.BlockSpec((1, SPAN, lane), lambda c, h: (c, 0, h)),
        "x": pl.BlockSpec((1, SPAN + 8, lane), lambda c, h: (c, 0, h)),
        "e": pl.BlockSpec((1, 8, lane), lambda c, h: (c, 0, h)),
        "p": pl.BlockSpec((8, lane), lambda c, h: (0, h)),
    }
    shapes = {
        "t": lambda d: jax.ShapeDtypeStruct((chunks * step, width), d),
        "x": lambda d: jax.ShapeDtypeStruct((chunks, SPAN + 8, width), d),
        "e": lambda d: jax.ShapeDtypeStruct((chunks, 8, width), d),
    }
    return pl.pallas_call(
        kernel,
        grid=(chunks, width // lane),
        in_specs=[kinds[kind] for kind in ins],
        out_specs=[kinds[kind] for kind, _ in outs],
        out_shape=[shapes[kind](dtype) for kind, dtype in outs],
        compiler_params=pltpu.CompilerParams(vmem_limit_bytes=48 * 1024 * 1024),
    )(*args)


def weight_grad_kernel(_, x_ref, y_ref, out_ref):
    out_ref[0] = lax.dot_general(
        x_ref[...], y_ref[...], (((0,), (0,)), ((), ())), preferred_element_type=F32
    ).astype(BF16)


def weight_grad(places, x, y, block):
    tokens, columns = y.shape
    blocks = places.shape[0]
    return pl.pallas_call(
        weight_grad_kernel,
        grid_spec=pltpu.PrefetchScalarGridSpec(
            num_scalar_prefetch=1,
            grid=(blocks,),
            in_specs=[
                pl.BlockSpec((tokens, block), lambda i, at: (0, at[i])),
                pl.BlockSpec((tokens, columns), lambda i, at: (0, 0)),
            ],
            out_specs=pl.BlockSpec((1, block, columns), lambda i, at: (i, 0, 0)),
        ),
        out_shape=jax.ShapeDtypeStruct((blocks, block, columns), BF16),
        compiler_params=pltpu.CompilerParams(vmem_limit_bytes=48 * 1024 * 1024),
        cost_estimate=pl.CostEstimate(
            flops=2 * tokens * block * blocks * columns,
            bytes_accessed=2 * (block * blocks * (tokens + columns) + tokens * columns),
            transcendentals=0,
        ),
    )(places, x, y)


def runs(order, block):
    out = []
    for place in order:
        if out and out[-1][1] == place * block:
            out[-1][1] = (place + 1) * block
        else:
            out.append([place * block, (place + 1) * block])
    return out


def reorder(value, order, block):
    spans = runs(order, block)
    if len(spans) == 1:
        return value
    return jnp.concatenate([value[..., a:b] for a, b in spans], axis=-1)


def on_device(
    count,
    tokens,
    previous,
    initial_state,
    mixing_weights,
    lowrank_weights,
    vectors,
    feedforward_weights,
    cotangent,
):
    masks = MEMBER_MASKS
    size = 1 << len(masks)
    teams = count // size
    all_masks = [1 << b for b in range(count.bit_length() - 1)]
    team_masks = [b for b in all_masks if b not in masks]
    me = lax.axis_index("seq")
    _, step, width = tokens.shape
    rows = mixing_weights.shape[0]
    part = width // size
    ff_part = FF // size
    team_rows = rows * size

    def bit_of(who, mask):
        return (who // mask) % 2 if isinstance(who, int) else lax.rem(lax.div(who, mask), 2)

    def member_of(who):
        return sum(bit_of(who, b) << j for j, b in enumerate(masks))

    def team_of(who):
        return sum(bit_of(who, b) << j for j, b in enumerate(team_masks))

    member, team = member_of(me), team_of(me)
    order = sorted(range(count), key=lambda d: (team_of(d), member_of(d)))
    inverse = sorted(range(count), key=lambda p: order[p])
    across = [order[m::size] for m in range(size)]

    def flips(k):
        return sum(b for j, b in enumerate(masks) if (k >> j) & 1)

    def trade(value, mask):
        return lax.ppermute(value, "seq", [(d, d ^ mask) for d in range(count)])

    def group_gather(value):
        pieces = {0: value}
        for j in reversed(range(len(masks))):
            pieces.update({k | (1 << j): trade(p, masks[j]) for k, p in list(pieces.items())})
        return [pieces[k] for k in range(size)]

    def group_rows(value):
        return jnp.concatenate(group_gather(value), axis=0)

    def group_sum(partial):
        pieces = {k: partial[k * step : (k + 1) * step] for k in range(size)}
        for j in range(len(masks)):
            kept = [k for k in pieces if not (k >> j) & 1]
            sent = [pieces[k | (1 << j)].astype(BF16) for k in kept]
            if len(sent) > 1:
                got = trade(jnp.concatenate(sent, axis=0), masks[j])
                got = [got[i * step : (i + 1) * step] for i in range(len(sent))]
            else:
                got = [trade(sent[0], masks[j])]
            pieces = {k: pieces[k] + g.astype(F32) for k, g in zip(kept, got)}
        return pieces[0]

    def ordered(pieces):
        pieces = list(pieces)
        for j in range(len(masks)):
            swap = lax.rem(lax.div(member, 1 << j), 2) == 1
            pieces = [
                jnp.where(swap, pieces[k ^ (1 << j)], pieces[k]) for k in range(len(pieces))
            ]
        return pieces

    def neighbour(value, offset):
        pairs = [(d, d + offset) for d in range(count) if 0 <= d + offset < count]
        return lax.ppermute(value, "seq", pairs)

    def take_columns(value, spans, who):
        return jnp.concatenate(
            [
                lax.dynamic_slice_in_dim(value, start + who * wide, wide, axis=1)
                for start, wide in spans
            ],
            axis=1,
        )

    def gather_weights(value, spans):
        pieces = [take_columns(value, spans, member)]
        for k in range(1, size):
            pieces.append(trade(take_columns(value, spans, member ^ k), flips(k)))
        local = jnp.concatenate(ordered(pieces), axis=0)
        return lax.all_gather(local, "seq", axis=0, tiled=True, axis_index_groups=across)

    def cube_gather(value):
        for mask in reversed(all_masks):
            got = trade(value, mask)
            upper = bit_of(me, mask) == 1
            value = jnp.stack([jnp.where(upper, got, value), jnp.where(upper, value, got)])
        axes = len(all_masks)
        return value.transpose(*reversed(range(axes)), *range(axes, value.ndim))

    def by_place(cube):
        axes = [all_masks[::-1].index(b) for b in team_masks[::-1] + list(masks[::-1])]
        rest = range(len(all_masks), cube.ndim)
        return cube.transpose(*axes, *rest).reshape(width, -1)

    def to_cube(value):
        axes = [all_masks[::-1].index(b) for b in team_masks[::-1] + list(masks[::-1])]
        cube = value.reshape(*[2] * len(axes), rows, -1)
        back = [axes.index(a) for a in range(len(axes))]
        return cube.transpose(*back, len(axes), len(axes) + 1)

    def cube_sum(cube):
        for axis, mask in reversed(list(enumerate(reversed(all_masks)))):
            bit = bit_of(me, mask)
            sent = lax.dynamic_index_in_dim(cube, 1 - bit, axis, keepdims=False)
            kept = lax.dynamic_index_in_dim(cube, bit, axis, keepdims=False)
            cube = kept + trade(sent, mask)
        return cube

    def sum_over_teams(x, y, first):
        if team_rows % 128:
            return lax.psum_scatter(
                tn(x, y).astype(BF16),
                "seq",
                scatter_dimension=0,
                tiled=True,
                axis_index_groups=across,
            )
        bits = list(range(len(team_masks)))
        if first:
            bits[0], bits[1] = 1, 0
        flipped = [0]
        for b in reversed(bits):
            flipped = flipped + [f | (1 << b) for f in flipped]
        places = jnp.bitwise_xor(jnp.asarray(flipped, jnp.int32), team)
        half = teams // 2
        got = trade(weight_grad(places[half:], x, y, team_rows), team_masks[bits[0]])
        kept = weight_grad(places[:half], x, y, team_rows)
        for b in bits[1:]:
            half //= 2
            sent = (kept[half:].astype(F32) + got[half:].astype(F32)).astype(BF16)
            kept = (kept[:half].astype(F32) + got[:half].astype(F32)).astype(BF16)
            got = trade(sent, team_masks[b])
        return (kept[0].astype(F32) + got[0].astype(F32)).astype(BF16)

    def hand_rows(pieces):
        joint = jnp.concatenate(pieces, axis=1)
        mine = [lax.dynamic_slice_in_dim(joint, member * rows, rows, axis=0)]
        for k in range(1, size):
            mine.append(
                trade(
                    lax.dynamic_slice_in_dim(joint, (member ^ k) * rows, rows, axis=0), flips(k)
                )
            )
        by_member = ordered(mine)
        outs, start = [], 0
        for piece in pieces:
            wide = piece.shape[1]
            outs += [p[:, start : start + wide] for p in by_member]
            start += wide
        return jnp.concatenate(outs, axis=1).astype(F32)

    mix_spans = [(c * width, part) for c in range(5)]
    ff_spans = [(0, ff_part), (FF, part), (FF + width, ff_part)]
    mixing = gather_weights(mixing_weights, mix_spans)
    feed = gather_weights(feedforward_weights, ff_spans)
    w_main = [mixing[:, c * part : (c + 1) * part] for c in range(4)]
    w_out = mixing[:, 4 * part :]
    w_key = feed[:, :ff_part]
    w_rec = feed[:, ff_part : ff_part + part]
    w_val = feed[:, ff_part + part :]

    up_start, decay_start, decay_up = 5 * RANK, 10 * RANK, 10 * RANK + DRANK
    low_cube = cube_gather(lowrank_weights)
    small_cube = cube_gather(jnp.concatenate([vectors, initial_state], axis=1))
    lowrank = by_place(low_cube[..., :decay_up])
    vec = by_place(small_cube[..., :16]).T
    natural = small_cube.reshape(width, -1)
    first_state = lax.dynamic_slice_in_dim(natural[:, 16:], member * part, part, axis=0).T
    vec_part = lax.dynamic_slice_in_dim(natural[:, :16], member * part, part, axis=0).T
    wkv_rows = jnp.concatenate([vec_part[9:12], jnp.zeros((5, part), F32)], axis=0)
    is_first = me == 0

    w_down = lowrank[:, :up_start]
    w_ups = [lowrank[:, up_start + c * RANK : up_start + (c + 1) * RANK] for c in range(5)]
    w_ddown = lowrank[:, decay_start:]
    w_dup = lax.dynamic_slice_in_dim(
        low_cube[..., decay_up:].reshape(width, DRANK), member * part, part, axis=0
    )

    hidden = reorder(tokens.reshape(step, width), order, rows).astype(F32)
    before = reorder(previous.reshape(2, width), order, rows)

    def norm_parts(value):
        centred = value - jnp.mean(value, axis=-1, keepdims=True)
        spread = jnp.mean(centred * centred, axis=-1, keepdims=True)
        scale = lax.rsqrt(spread + LN_EPS)
        return centred * scale, scale

    def norm_back(grad, gain, normal, scale):
        e = grad * gain
        return scale * (
            e
            - jnp.mean(e, axis=-1, keepdims=True)
            - normal * jnp.mean(e * normal, axis=-1, keepdims=True)
        )

    def with_previous(value, start_row):
        arrived = neighbour(value[-1:, :], 1)
        arrived = jnp.where(is_first, start_row, arrived)
        return jnp.concatenate([arrived, value[:-1]], axis=0)

    def from_next(value):
        return jnp.concatenate([value[1:], neighbour(value[:1, :], -1)], axis=0)

    normal_one, scale_one = norm_parts(hidden)
    normed = normal_one * vec[0] + vec[1]
    delta = with_previous(normed, before[0:1]) - normed
    blend = (normed + delta * vec[2]).astype(BF16)
    mix_tanh = jnp.tanh(nn(blend, w_down))
    mix_hidden = mix_tanh.astype(BF16)
    hidden_c = [mix_hidden[:, c * RANK : (c + 1) * RANK] for c in range(5)]
    coeff = [vec[3 + c] + nt(hidden_c[c], w_ups[c]) for c in range(5)]
    mixed = [(normed + delta * coeff[c]).astype(BF16) for c in range(5)]
    decay_tanh = jnp.tanh(nn(mixed[0], w_ddown))
    decay_hidden = decay_tanh.astype(BF16)

    mixed_all = [group_rows(mixed[c]) for c in range(1, 5)]
    dh_all = group_rows(decay_hidden)
    log_decay = -jnp.exp(vec_part[8] + nt(dh_all, w_dup))
    keys, values, receipt, gate_pre = [nn(mixed_all[c], w_main[c]) for c in range(4)]

    call = functools.partial(block_call, chunks=size, step=step, width=part)
    (totals,) = call(
        totals_kernel, ins="ttt", outs=[("x", F32)], args=(keys, values, log_decay)
    )
    by_member = ordered([totals[k] for k in range(size)])
    total = {m: (p[SPAN : SPAN + 1], p[:SPAN]) for m, p in enumerate(by_member)}
    before_chunk = [
        (jnp.ones((1, part), F32), jnp.zeros((SPAN, part), F32)) for _ in range(size)
    ]
    open_bits = size - 1
    levels = []

    def chain(early, late):
        return early[0] * late[0], late[0] * early[1] + late[1]

    def pick(flag, yes, no):
        return tuple(jnp.where(flag, a, b) for a, b in zip(yes, no))

    for mask in all_masks:
        if mask in masks:
            bit = 1 << masks.index(mask)
            levels.append({g: total[g][0] for g in total})
            for m in range(size):
                if m & bit:
                    early = (m & open_bits) ^ bit
                    before_chunk[m] = chain(total[early], before_chunk[m])
            total = {g: chain(total[g], total[g | bit]) for g in total if not g & bit}
            open_bits ^= bit
        else:
            groups = list(total)
            sent = jnp.concatenate(
                [
                    jnp.concatenate(
                        [total[g][1], jnp.broadcast_to(total[g][0], (8, part))], axis=0
                    )
                    for g in groups
                ],
                axis=0,
            )
            got = trade(sent, mask)
            high = SPAN + 8
            other = {
                g: (got[i * high + SPAN : i * high + SPAN + 1], got[i * high : i * high + SPAN])
                for i, g in enumerate(groups)
            }
            levels.append({g: (total[g][0], other[g][0]) for g in groups})
            late = bit_of(me, mask) == 1
            for m in range(size):
                g = m & open_bits
                before_chunk[m] = pick(late, chain(other[g], before_chunk[m]), before_chunk[m])
            total = {
                g: pick(late, chain(other[g], total[g]), chain(total[g], other[g]))
                for g in groups
            }
    state_in = jnp.stack(ordered([d * first_state + s for d, s in before_chunk]))

    wkv, gated = call(
        forward_kernel,
        ins="tttttsp",
        outs=[("t", F32), ("t", BF16)],
        args=(receipt, keys, values, log_decay, gate_pre, state_in, wkv_rows),
    )
    middle = hidden + group_sum(nt(gated, w_out))

    normal_two, scale_two = norm_parts(middle)
    normed_two = normal_two * vec[12] + vec[13]
    delta_two = with_previous(normed_two, before[1:2]) - normed_two
    key_in = (normed_two + delta_two * vec[14]).astype(BF16)
    recv_in = (normed_two + delta_two * vec[15]).astype(BF16)
    key_all = group_rows(key_in)
    recv_all = group_rows(recv_in)
    relu = jnp.maximum(nn(key_all, w_key), 0.0)
    squared = (relu * relu).astype(BF16)
    value_out = group_sum(nt(squared, w_val))
    recept_act = nn(recv_all, w_rec)
    recept_pieces = [recept_act[:step]] + [
        trade(recept_act[k * step : (k + 1) * step], flips(k)) for k in range(1, size)
    ]
    recept = jax.nn.sigmoid(
        reorder(jnp.concatenate(ordered(recept_pieces), axis=1), order, rows)
    )
    block_output = reorder((middle + recept * value_out).astype(BF16), inverse, rows)

    upstream = reorder(cotangent.reshape(step, width), order, rows).astype(F32)
    value_grad = (upstream * recept).astype(BF16)
    recept_grad = reorder(
        (upstream * value_out * recept * (1.0 - recept)).astype(BF16), inverse, rows
    )
    vg_all = group_rows(value_grad)
    rg_all = jnp.concatenate(
        [lax.dynamic_slice_in_dim(recept_grad, member * part, part, axis=1)]
        + [
            trade(
                lax.dynamic_slice_in_dim(recept_grad, (member ^ k) * part, part, axis=1),
                flips(k),
            )
            for k in range(1, size)
        ],
        axis=0,
    )
    val_sum = sum_over_teams(vg_all, squared, False)
    key_grad = (nn(vg_all, w_val) * (2.0 * relu)).astype(BF16)
    key_in_grad = group_sum(nt(key_grad, w_key))
    recv_in_grad = group_sum(nt(rg_all, w_rec))
    key_sum = sum_over_teams(key_all, key_grad, True)
    rec_sum = sum_over_teams(recv_all, rg_all, False)
    feedforward_gradient = hand_rows([key_sum, rec_sum, val_sum])
    shifted_grad = key_in_grad * vec[14] + recv_in_grad * vec[15]
    two_grad = (
        key_in_grad * (1.0 - vec[14]) + recv_in_grad * (1.0 - vec[15]) + from_next(shifted_grad)
    )
    middle_grad = upstream + norm_back(two_grad, vec[12], normal_two, scale_two)
    col_12 = jnp.sum(two_grad * normal_two, axis=0)
    col_13 = jnp.sum(two_grad, axis=0)
    col_14 = jnp.sum(key_in_grad * delta_two, axis=0)
    col_15 = jnp.sum(recv_in_grad * delta_two, axis=0)

    branch_grad = middle_grad.astype(BF16)
    bg_all = group_rows(branch_grad)
    out_sum = sum_over_teams(bg_all, gated, True)
    gated_grad = nn(bg_all, w_out)
    gate_grad, wkv_grad, local = call(
        gate_kernel,
        ins="tttttp",
        outs=[("t", BF16), ("t", F32), ("x", F32)],
        args=(gated_grad, gate_pre, wkv, receipt, log_decay, wkv_rows),
    )
    gate_sum = sum_over_teams(mixed_all[3], gate_grad, False)
    grad_total = dict(enumerate(ordered([local[k, :SPAN] for k in range(size)])))
    after = [(jnp.ones((1, part), F32), jnp.zeros((SPAN, part), F32)) for _ in range(size)]
    open_bits = size - 1
    for mask, level in zip(all_masks, levels):
        if mask in masks:
            bit = 1 << masks.index(mask)
            for m in range(size):
                if not m & bit:
                    late = (m & open_bits) | bit
                    d, s = after[m]
                    after[m] = (d * level[late], d * grad_total[late] + s)
            grad_total = {
                g: grad_total[g] + level[g] * grad_total[g | bit]
                for g in grad_total
                if not g & bit
            }
            open_bits ^= bit
        else:
            groups = list(grad_total)
            got = trade(jnp.concatenate([grad_total[g] for g in groups], axis=0), mask)
            other = {g: got[i * SPAN : (i + 1) * SPAN] for i, g in enumerate(groups)}
            early = bit_of(me, mask) == 0
            for m in range(size):
                g = m & open_bits
                d, s = after[m]
                after[m] = pick(early, (d * level[g][1], d * other[g] + s), (d, s))
            grad_total = {
                g: jnp.where(
                    early,
                    grad_total[g] + level[g][0] * other[g],
                    other[g] + level[g][1] * grad_total[g],
                )
                for g in groups
            }
    grad_out = jnp.stack(ordered([s for _, s in after]))

    first_grad = grad_total[0]
    holder = lax.div(me * rows, part)

    def rows_of(who):
        return lax.dynamic_slice_in_dim(first_grad, lax.rem(who * rows, part), rows, axis=1)

    state_rows = rows_of(me)
    for k in range(1, size):
        other_rows = trade(rows_of(jnp.bitwise_xor(me, flips(k))), flips(k))
        state_rows = jnp.where(holder == (member ^ k), other_rows, state_rows)
    initial_state_gradient = state_rows.T

    d_receipt, d_keys, d_values, d_decay, extra = call(
        backward_kernel,
        ins="tttttssp",
        outs=[("t", BF16)] * 4 + [("e", F32)],
        args=(receipt, keys, values, log_decay, wkv_grad, state_in, grad_out, wkv_rows),
    )
    grads = [d_keys, d_values, d_receipt, gate_grad]
    main_sums = [sum_over_teams(mixed_all[c], grads[c], c != 1) for c in range(3)]
    mixing_gradient = hand_rows(main_sums + [gate_sum, out_sum])
    mixed_grad = [None] + [group_sum(nt(grads[c], w_main[c])) for c in range(4)]
    decay_latent_grad = group_sum(nn(d_decay, w_dup))
    decay_pre = (decay_latent_grad * (1.0 - decay_tanh * decay_tanh)).astype(BF16)
    mixed_grad[0] = nt(decay_pre, w_ddown)

    shift_grads = [mixed_grad[c] * delta for c in range(5)]
    offset_grads = [s.astype(BF16) for s in shift_grads]
    mix_latent_grad = jnp.concatenate(
        [nn(offset_grads[c], w_ups[c]) for c in range(5)], axis=1
    )
    mix_pre = (mix_latent_grad * (1.0 - mix_tanh * mix_tanh)).astype(BF16)
    blend_grad = nt(mix_pre, w_down)
    delta_grad = blend_grad * vec[2]
    normed_grad = blend_grad
    for c in range(5):
        delta_grad = delta_grad + mixed_grad[c] * coeff[c]
        normed_grad = normed_grad + mixed_grad[c]
    normed_grad = normed_grad - delta_grad + from_next(delta_grad)
    block_input_gradient = reorder(
        middle_grad + norm_back(normed_grad, vec[0], normal_one, scale_one), inverse, rows
    )


    def spread(value):
        zero = jnp.zeros((width, value.shape[1]), F32)
        return lax.dynamic_update_slice_in_dim(zero, value, member * part, axis=0)

    vec_low = jnp.stack(
        [
            jnp.sum(normed_grad * normal_one, axis=0),
            jnp.sum(normed_grad, axis=0),
            jnp.sum(blend_grad * delta, axis=0),
        ]
        + [jnp.sum(s, axis=0) for s in shift_grads]
        + [col_12, col_13, col_14, col_15]
    )
    vec_head = jnp.concatenate(
        [jnp.sum(extra[:, :2], axis=0), jnp.sum(local[:, SPAN : SPAN + 2], axis=0)], axis=0
    )
    by_feature = jnp.concatenate(
        [
            tn(blend, mix_pre),
            *[tn(offset_grads[c], hidden_c[c]) for c in range(5)],
            tn(mixed[0], decay_pre),
            vec_low.T,
        ],
        axis=1,
    )
    by_channel = spread(jnp.concatenate([tn(d_decay, dh_all), vec_head.T], axis=1))
    low = cube_sum(
        jnp.concatenate(
            [
                to_cube(by_feature),
                by_channel.reshape(*[2] * len(all_masks), rows, -1),
            ],
            axis=-1,
        )
    )
    vec_at = decay_up + 12
    lowrank_gradient = jnp.concatenate([low[:, :decay_up], low[:, vec_at : vec_at + DRANK]], axis=1)
    vectors_gradient = jnp.concatenate(
        [low[:, decay_up : decay_up + 8], low[:, vec_at + DRANK :], low[:, decay_up + 8 : vec_at]],
        axis=1,
    )
    return (
        block_output.reshape(1, step, width),
        block_input_gradient.reshape(1, step, width),
        initial_state_gradient,
        mixing_gradient,
        lowrank_gradient,
        vectors_gradient,
        feedforward_gradient,
    )


def solution(mesh):
    rowwise = P("seq", None)
    tokenwise = P(None, "seq", None)
    return jax.shard_map(
        functools.partial(on_device, mesh.shape["seq"]),
        mesh=mesh,
        in_specs=(tokenwise, P(), rowwise, rowwise, rowwise, rowwise, rowwise, tokenwise),
        out_specs=(tokenwise, tokenwise, rowwise, rowwise, rowwise, rowwise, rowwise),
        check_vma=False,
    )
```

```python
import functools

import jax
import jax.numpy as jnp
from jax import lax
from jax.experimental import pallas as pl
from jax.experimental.pallas import tpu as pltpu
from jax.sharding import PartitionSpec as P

HEADS = 32
SPAN = 64
FF = 7168
RANK = 32
DRANK = 64
LN_EPS = 1e-05
GN_EPS = 0.00064
MEMBER_MASKS = (1, 8)

F32 = jnp.float32
BF16 = jnp.bfloat16
HI = lax.Precision.HIGHEST


def nn(a, b):
    return jnp.dot(a, b, preferred_element_type=F32)


def nt(a, b):
    return lax.dot_general(a, b, (((1,), (1,)), ((), ())), preferred_element_type=F32)


def tn(a, b):
    return lax.dot_general(a, b, (((0,), (0,)), ((), ())), preferred_element_type=F32)


def knn(a, b):
    return lax.dot_general(
        a, b, (((1,), (0,)), ((), ())), precision=HI, preferred_element_type=F32
    )


def knt(a, b):
    return lax.dot_general(
        a, b, (((1,), (1,)), ((), ())), precision=HI, preferred_element_type=F32
    )


def ktn(a, b):
    return lax.dot_general(
        a, b, (((0,), (0,)), ((), ())), precision=HI, preferred_element_type=F32
    )


def low_lanes(shape):
    return lax.broadcasted_iota(jnp.int32, shape, len(shape) - 1) < SPAN


def head_sum(x):
    low = low_lanes(x.shape)
    s0 = jnp.sum(jnp.where(low, x, 0.0), axis=-1, keepdims=True)
    s1 = jnp.sum(jnp.where(low, 0.0, x), axis=-1, keepdims=True)
    return jnp.where(low, s0, s1)


def two_rows(x):
    low = low_lanes(x.shape)
    return jnp.concatenate([jnp.where(low, x, 0.0), jnp.where(low, 0.0, x)], axis=0)


def fold(full):
    return jnp.where(low_lanes((SPAN, 2 * SPAN)), full[:SPAN], full[SPAN:])


def unfold(state):
    low = low_lanes(state.shape)
    return jnp.concatenate([jnp.where(low, state, 0.0), jnp.where(low, 0.0, state)], axis=0)


def running(w, upper=False):
    count = w.shape[0]
    row = lax.broadcasted_iota(jnp.int32, (count, count), 0)
    col = lax.broadcasted_iota(jnp.int32, (count, count), 1)
    keep = (col >= row) if upper else (col <= row)
    return knn(jnp.where(keep, 1.0, 0.0).astype(F32), w)


def strict(count):
    row = lax.broadcasted_iota(jnp.int32, (2 * count, count), 0)
    col = lax.broadcasted_iota(jnp.int32, (2 * count, count), 1)
    row = jnp.where(row >= count, row - count, row)
    return row > col, row == col


def affinity(r, k, u, q, ks):
    count = r.shape[0]
    below, diag = strict(count)
    raw = knt(two_rows(q), ks)
    share = jnp.sum(two_rows(r * u * k), axis=-1, keepdims=True)
    return jnp.where(below, raw, jnp.where(diag, share, 0.0))


def totals_kernel(k_ref, v_ref, w_ref, out_ref):
    cum = running(w_ref[...])
    total = cum[-1:, :]
    kc = k_ref[...] * jnp.exp(total - cum)
    out_ref[0, :SPAN, :] = fold(ktn(v_ref[...], kc))
    out_ref[0, SPAN:, :] = jnp.broadcast_to(jnp.exp(total), (8, 2 * SPAN))


def group_norm(y, gain, bias):
    centred = y - head_sum(y) * (1.0 / SPAN)
    spread = head_sum(centred * centred) * (1.0 / SPAN)
    scale = lax.rsqrt(spread + GN_EPS)
    normal = centred * scale
    return normal, scale, normal * gain + bias


def forward_kernel(r_ref, k_ref, v_ref, w_ref, g_ref, s_ref, p_ref, y_ref, gated_ref):
    r, k, v, w = r_ref[...], k_ref[...], v_ref[...], w_ref[...]
    cum = running(w)
    q = r * jnp.exp(cum - w)
    ks = k * jnp.exp(-cum)
    aff = affinity(r, k, p_ref[0:1, :], q, ks)
    count = r.shape[0]
    v2 = two_rows(v)
    y = (
        knt(q, unfold(s_ref[0]))
        + knn(aff[:count], v2[:count])
        + knn(aff[count:], v2[count:])
    )
    y_ref[...] = y
    gate = g_ref[...]
    _, _, grouped = group_norm(y, p_ref[1:2, :], p_ref[2:3, :])
    gated_ref[...] = (grouped * gate * jax.nn.sigmoid(gate)).astype(BF16)


def gate_kernel(gg_ref, g_ref, y_ref, r_ref, w_ref, p_ref, gate_ref, dy_ref, out_ref):
    gated_grad, gate, y = gg_ref[...], g_ref[...], y_ref[...]
    gain = p_ref[1:2, :]
    normal, scale, grouped = group_norm(y, gain, p_ref[2:3, :])
    sig = jax.nn.sigmoid(gate)
    gate_ref[...] = (gated_grad * grouped * sig * (1.0 + gate * (1.0 - sig))).astype(BF16)
    outer = gated_grad * gate * sig
    inner = outer * gain
    dy = scale * (
        inner
        - head_sum(inner) * (1.0 / SPAN)
        - normal * (head_sum(inner * normal) * (1.0 / SPAN))
    )
    dy_ref[...] = dy
    w = w_ref[...]
    q = r_ref[...] * jnp.exp(running(w) - w)
    out_ref[0, :SPAN, :] = fold(ktn(dy, q))
    gain_grad = jnp.sum(outer * normal, axis=0, keepdims=True)
    bias_grad = jnp.sum(outer, axis=0, keepdims=True)
    out_ref[0, SPAN:, :] = jnp.concatenate(
        [gain_grad, bias_grad, jnp.zeros((6, 2 * SPAN), F32)], axis=0
    )


def backward_kernel(
    r_ref, k_ref, v_ref, w_ref, dy_ref, s_ref, gs_ref, p_ref,
    dr_ref, dk_ref, dv_ref, dd_ref, out_ref,
):
    r, k, v, w, dy = r_ref[...], k_ref[...], v_ref[...], w_ref[...], dy_ref[...]
    u = p_ref[0:1, :]
    count = r.shape[0]
    cum = running(w)
    total = cum[-1:, :]
    e_before, e_minus, e_carry = jnp.exp(cum - w), jnp.exp(-cum), jnp.exp(total - cum)
    q, ks, kc = r * e_before, k * e_minus, k * e_carry
    aff = affinity(r, k, u, q, ks)
    below, _ = strict(count)
    dy2 = two_rows(dy)
    d_aff = jnp.where(below, knt(dy2, v), 0.0)
    own = head_sum(dy * v)
    state, grad_state = s_ref[0], gs_ref[0]
    state2, grad2 = unfold(state), unfold(grad_state)
    ks2 = two_rows(ks)
    dq = knn(dy, state2) + knn(d_aff[:count], ks2[:count]) + knn(d_aff[count:], ks2[count:])
    dks = ktn(d_aff, two_rows(q))
    dkc = knn(v, grad2)
    dv_ref[...] = (ktn(aff, dy2) + knt(kc, grad2)).astype(BF16)
    dr_ref[...] = (dq * e_before + own * u * k).astype(BF16)
    dk_ref[...] = (dks * e_minus + dkc * e_carry + own * u * r).astype(BF16)
    gq, gc = q * dq, kc * dkc
    d_total = jnp.sum(gc, axis=0, keepdims=True) + jnp.exp(total) * jnp.sum(
        state * grad_state, axis=0, keepdims=True
    )
    dw = running(gq - ks * dks - gc, upper=True) - gq + d_total
    term = dw * w
    dd_ref[...] = term.astype(BF16)
    out_ref[0] = jnp.concatenate(
        [
            jnp.sum(term, axis=0, keepdims=True),
            jnp.sum(own * r * k, axis=0, keepdims=True),
            jnp.zeros((6, 2 * SPAN), F32),
        ],
        axis=0,
    )


def block_call(kernel, chunks, step, width, ins, outs, args):
    lane = 2 * SPAN
    kinds = {
        "t": pl.BlockSpec((step, lane), lambda c, h: (c, h)),
        "s": pl.BlockSpec((1, SPAN, lane), lambda c, h: (c, 0, h)),
        "x": pl.BlockSpec((1, SPAN + 8, lane), lambda c, h: (c, 0, h)),
        "e": pl.BlockSpec((1, 8, lane), lambda c, h: (c, 0, h)),
        "p": pl.BlockSpec((8, lane), lambda c, h: (0, h)),
    }
    shapes = {
        "t": lambda d: jax.ShapeDtypeStruct((chunks * step, width), d),
        "x": lambda d: jax.ShapeDtypeStruct((chunks, SPAN + 8, width), d),
        "e": lambda d: jax.ShapeDtypeStruct((chunks, 8, width), d),
    }
    return pl.pallas_call(
        kernel,
        grid=(chunks, width // lane),
        in_specs=[kinds[kind] for kind in ins],
        out_specs=[kinds[kind] for kind, _ in outs],
        out_shape=[shapes[kind](dtype) for kind, dtype in outs],
        compiler_params=pltpu.CompilerParams(vmem_limit_bytes=48 * 1024 * 1024),
    )(*args)


def weight_grad_kernel(_, x_ref, y_ref, out_ref):
    out_ref[0] = lax.dot_general(
        x_ref[...], y_ref[...], (((0,), (0,)), ((), ())), preferred_element_type=F32
    ).astype(BF16)


def weight_grad(places, x, y, block):
    tokens, columns = y.shape
    blocks = places.shape[0]
    return pl.pallas_call(
        weight_grad_kernel,
        grid_spec=pltpu.PrefetchScalarGridSpec(
            num_scalar_prefetch=1,
            grid=(blocks,),
            in_specs=[
                pl.BlockSpec((tokens, block), lambda i, at: (0, at[i])),
                pl.BlockSpec((tokens, columns), lambda i, at: (0, 0)),
            ],
            out_specs=pl.BlockSpec((1, block, columns), lambda i, at: (i, 0, 0)),
        ),
        out_shape=jax.ShapeDtypeStruct((blocks, block, columns), BF16),
        compiler_params=pltpu.CompilerParams(vmem_limit_bytes=48 * 1024 * 1024),
    )(places, x, y)


def lanes_kernel(spans, x_ref, out_ref):
    at = 0
    for start, stop in spans:
        out_ref[:, at : at + stop - start] = x_ref[:, start:stop].astype(out_ref.dtype)
        at += stop - start


def move_lanes(spans, value, dtype):
    return pl.pallas_call(
        functools.partial(lanes_kernel, spans),
        in_specs=[pl.BlockSpec(memory_space=pltpu.VMEM)],
        out_specs=pl.BlockSpec(memory_space=pltpu.VMEM),
        out_shape=jax.ShapeDtypeStruct(value.shape, dtype),
        compiler_params=pltpu.CompilerParams(vmem_limit_bytes=32 * 1024 * 1024),
    )(value)


def place_kernel(counts, at_ref, *refs):
    ins, out_ref, sems = refs[: len(counts)], refs[-2], refs[-1]
    block = out_ref.shape[0] // sum(counts)
    copies, i = [], 0
    for ref, n in zip(ins, counts):
        for j in range(n):
            start = pl.multiple_of(at_ref[i] * block, block)
            copy = pltpu.make_async_copy(
                ref.at[pl.ds(j * block, block), :],
                out_ref.at[pl.ds(start, block), :],
                sems.at[i],
            )
            copy.start()
            copies.append(copy)
            i += 1
    for copy in copies:
        copy.wait()


def place_rows(at, pieces, block):
    counts = [p.shape[0] // block for p in pieces]
    total = sum(counts)
    return pl.pallas_call(
        functools.partial(place_kernel, counts),
        in_specs=[pl.BlockSpec(memory_space=pltpu.SMEM)]
        + [pl.BlockSpec(memory_space=pl.ANY)] * len(pieces),
        out_specs=pl.BlockSpec(memory_space=pl.ANY),
        out_shape=jax.ShapeDtypeStruct((total * block, pieces[0].shape[1]), pieces[0].dtype),
        scratch_shapes=[pltpu.SemaphoreType.DMA((total,))],
        compiler_params=pltpu.CompilerParams(vmem_limit_bytes=32 * 1024 * 1024),
    )(at, *pieces)


def mixes_kernel(
    open_ref, x_ref, before_ref, vec_ref, down_ref, up_ref, ddown_ref,
    m1_ref, m2_ref, m3_ref, m4_ref, dh_ref,
    normal_ref, scale_ref, delta_ref, blend_ref, m0_ref, tanh_ref, dtanh_ref,
):
    piece = pl.program_id(0)
    step = m1_ref.shape[0]
    x = x_ref[...].astype(F32)
    centred = x - jnp.mean(x, axis=-1, keepdims=True)
    scale = lax.rsqrt(jnp.mean(centred * centred, axis=-1, keepdims=True) + LN_EPS)
    normal = centred * scale
    full = normal * vec_ref[0:1, :] + vec_ref[1:2, :]
    normed = full[:step]
    first = jnp.where(open_ref[piece] == 1, before_ref[0:1, :], full[step : step + 1])
    row = lax.broadcasted_iota(jnp.int32, normed.shape, 0)
    delta = jnp.where(row == 0, first, pltpu.roll(normed, 1, 0)) - normed
    blend = (normed + delta * vec_ref[2:3, :]).astype(BF16)
    tanh = jnp.tanh(nn(blend, down_ref[...]))
    latent = tanh.astype(BF16)
    lane = lax.broadcasted_iota(jnp.int32, latent.shape, 1)
    mixed = []
    for c in range(5):
        own = (lane >= c * RANK) & (lane < (c + 1) * RANK)
        offset = nt(jnp.where(own, latent, jnp.zeros_like(latent)), up_ref[...])
        mixed.append((normed + delta * (vec_ref[3 + c : 4 + c, :] + offset)).astype(BF16))
    dtanh = jnp.tanh(nn(mixed[0], ddown_ref[...]))
    m1_ref[...], m2_ref[...], m3_ref[...], m4_ref[...] = mixed[1:]
    dh_ref[...] = dtanh.astype(BF16)

    @pl.when(piece == 0)
    def _():
        normal_ref[...] = normal[:step]
        scale_ref[...] = jnp.broadcast_to(scale[:step], scale_ref.shape)
        delta_ref[...] = delta
        blend_ref[...] = blend
        m0_ref[...] = mixed[0]
        tanh_ref[...] = tanh
        dtanh_ref[...] = dtanh


def group_mixes(opening, x, before, vec, down, up, ddown, step):
    high, width = step + 16, x.shape[1]
    pieces = x.shape[0] // high

    def whole(value):
        return pl.BlockSpec(value.shape, lambda k: (0, 0))

    def own(columns, dtype):
        return (
            pl.BlockSpec((step, columns), lambda k: (0, 0)),
            jax.ShapeDtypeStruct((step, columns), dtype),
        )

    def every(columns, dtype):
        return (
            pl.BlockSpec((step, columns), lambda k: (k, 0)),
            jax.ShapeDtypeStruct((pieces * step, columns), dtype),
        )

    outs = [every(width, BF16)] * 4 + [
        every(DRANK, BF16),
        own(width, F32),
        own(128, F32),
        own(width, F32),
        own(width, BF16),
        own(width, BF16),
        own(5 * RANK, F32),
        own(DRANK, F32),
    ]
    return pl.pallas_call(
        mixes_kernel,
        grid=(pieces,),
        in_specs=[
            pl.BlockSpec(memory_space=pltpu.SMEM),
            pl.BlockSpec((high, width), lambda k: (k, 0)),
            whole(before),
            whole(vec),
            whole(down),
            whole(up),
            whole(ddown),
        ],
        out_specs=[o[0] for o in outs],
        out_shape=[o[1] for o in outs],
        compiler_params=pltpu.CompilerParams(vmem_limit_bytes=56 * 1024 * 1024),
    )(opening, x, before, vec, down, up, ddown)


def tie(*values):
    return lax.optimization_barrier(values)


def on_device(
    count,
    tokens,
    previous,
    initial_state,
    mixing_weights,
    lowrank_weights,
    vectors,
    feedforward_weights,
    cotangent,
):
    masks = MEMBER_MASKS
    size = 1 << len(masks)
    teams = count // size
    all_masks = [1 << b for b in range(count.bit_length() - 1)]
    team_masks = [b for b in all_masks if b not in masks]
    far = 16
    team_masks.sort(key=lambda b: b != far)
    me = lax.axis_index("seq")
    _, step, width = tokens.shape
    rows = mixing_weights.shape[0]
    part = width // size
    ff_part = FF // size
    team_rows = rows * size
    fast = rows == 64

    def bit_of(who, mask):
        return (who // mask) % 2 if isinstance(who, int) else lax.rem(lax.div(who, mask), 2)

    def member_of(who):
        return sum(bit_of(who, b) << j for j, b in enumerate(masks))

    def team_of(who):
        return sum(bit_of(who, b) << j for j, b in enumerate(team_masks))

    member, team = member_of(me), team_of(me)
    order = sorted(range(count), key=lambda d: (team_of(d), member_of(d)))
    inverse = sorted(range(count), key=lambda p: order[p])
    across = [order[m::size] for m in range(size)]
    square = [order[m :: 2 * size] for m in range(2 * size)]
    def lane_spans(blocks):
        spans = []
        for d in blocks:
            if spans and spans[-1][1] == d * rows:
                spans[-1][1] = (d + 1) * rows
            else:
                spans.append([d * rows, (d + 1) * rows])
        return spans

    def move(value, blocks, dtype):
        if fast:
            return move_lanes(lane_spans(blocks), value, dtype)
        at = jnp.asarray([d * rows + r for d in blocks for r in range(rows)], jnp.int32)
        return jnp.take(value, at, axis=1).astype(dtype)

    def to_places(value, dtype):
        return move(value, order, dtype)

    def to_natural(value, dtype):
        return move(value, inverse, dtype)

    def flips(k):
        return sum(b for j, b in enumerate(masks) if (k >> j) & 1)

    def trade(value, mask):
        return lax.ppermute(value, "seq", [(d, d ^ mask) for d in range(count)])

    def group_gather(value):
        pieces = {0: value}
        for j in reversed(range(len(masks))):
            keys, high = sorted(pieces), value.shape[0]
            joint = value if len(keys) == 1 else jnp.concatenate(
                [pieces[k] for k in keys], axis=0
            )
            got = trade(joint, masks[j])
            for i, k in enumerate(keys):
                pieces[k | (1 << j)] = got[i * high : (i + 1) * high]
        return [pieces[k] for k in range(size)]

    def exchange(pieces):
        pieces, high = list(pieces), pieces[0].shape[0]
        for j in reversed(range(len(masks))):
            keys = [k for k in range(size) if (k >> j) & 1]
            got = trade(jnp.concatenate([pieces[k] for k in keys], axis=0), masks[j])
            for i, k in enumerate(keys):
                pieces[k] = got[i * high : (i + 1) * high]
        return pieces

    def group_rows(value):
        return jnp.concatenate(group_gather(value), axis=0)

    def group_sum(partial):
        pieces = {k: partial[k * step : (k + 1) * step] for k in range(size)}
        for j in range(len(masks)):
            kept = [k for k in pieces if not (k >> j) & 1]
            sent = [pieces[k | (1 << j)].astype(BF16) for k in kept]
            if len(sent) > 1:
                got = trade(jnp.concatenate(sent, axis=0), masks[j])
                got = [got[i * step : (i + 1) * step] for i in range(len(sent))]
            else:
                got = [trade(sent[0], masks[j])]
            pieces = {k: pieces[k] + g.astype(F32) for k, g in zip(kept, got)}
        return pieces[0]

    def ordered(pieces):
        pieces = list(pieces)
        for j in range(len(masks)):
            swap = lax.rem(lax.div(member, 1 << j), 2) == 1
            pieces = [
                jnp.where(swap, pieces[k ^ (1 << j)], pieces[k]) for k in range(len(pieces))
            ]
        return pieces

    def neighbour(value, offset):
        pairs = [(d, d + offset) for d in range(count) if 0 <= d + offset < count]
        return lax.ppermute(value, "seq", pairs)

    def take_columns(value, spans, who):
        return jnp.concatenate(
            [
                lax.dynamic_slice_in_dim(value, start + who * wide, wide, axis=1)
                for start, wide in spans
            ],
            axis=1,
        )

    def group_columns(value, spans):
        pieces = [take_columns(value, spans, member ^ k) for k in range(size)]
        return jnp.concatenate(ordered(exchange(pieces)), axis=0)

    def crossing(first):
        bits = list(range(1, len(team_masks))) + [0]
        if first:
            bits[0], bits[1] = bits[1], bits[0]
        return bits

    def far_pair(local):
        if not fast:
            return local
        got = trade(local, far)
        upper = bit_of(me, far) == 1
        return jnp.concatenate(
            [jnp.where(upper, got, local), jnp.where(upper, local, got)], axis=0
        )

    def gather_rows(paired):
        groups = square if fast else across
        return lax.all_gather(paired, "seq", axis=0, tiled=True, axis_index_groups=groups)

    def cube_gather(value):
        for mask in reversed(all_masks):
            got = trade(value, mask)
            upper = bit_of(me, mask) == 1
            value = jnp.stack([jnp.where(upper, got, value), jnp.where(upper, value, got)])
        axes = len(all_masks)
        return value.transpose(*reversed(range(axes)), *range(axes, value.ndim))

    place_axes = [all_masks[::-1].index(b) for b in team_masks[::-1] + list(masks[::-1])]

    def by_place(cube):
        rest = range(len(all_masks), cube.ndim)
        return cube.transpose(*place_axes, *rest).reshape(width, -1)

    def to_cube(value):
        cube = value.reshape(*[2] * len(place_axes), rows, -1)
        back = [place_axes.index(a) for a in range(len(place_axes))]
        return cube.transpose(*back, len(back), len(back) + 1)

    def cube_sum(cube, kind):
        for axis, mask in reversed(list(enumerate(reversed(all_masks)))):
            bit = bit_of(me, mask)
            sent = lax.dynamic_index_in_dim(cube, 1 - bit, axis, keepdims=False)
            kept = lax.dynamic_index_in_dim(cube, bit, axis, keepdims=False)
            cube = kept.astype(F32) + trade(sent.astype(kind), mask).astype(F32)
        return cube

    class TeamSum:
        last = {}

        def __init__(self, x, y, first):
            self.bits = crossing(first)
            self.args = (x, y, team_rows)
            self.stage = 0
            places = [0]
            for b in reversed(self.bits):
                places = places + [p | (1 << b) for p in places]
            self.half = teams // 2
            self.places = jnp.bitwise_xor(jnp.asarray(places, jnp.int32), team)
            self.kept = self.got = None
            if fast:
                self.sent = weight_grad(self.places[self.half :], *self.args)
            else:
                self.sent = tn(x, y).astype(BF16)

        def step(self):
            if not fast or not self.bits:
                return
            key = (self.bits[0], self.stage)
            if key in TeamSum.last:
                self.sent = tie(self.sent, TeamSum.last[key])[0]
            got = trade(self.sent, team_masks[self.bits[0]])
            TeamSum.last[key] = got
            kept = self.kept
            if kept is None:
                kept = weight_grad(self.places[: self.half], *self.args)
            self.bits = self.bits[1:]
            self.stage += 1
            self.half //= 2
            h = self.half
            if h:
                self.sent = (kept[h:].astype(F32) + got[h:].astype(F32)).astype(BF16)
                self.kept = (kept[:h].astype(F32) + got[:h].astype(F32)).astype(BF16)
            else:
                self.sent = (kept[0].astype(F32) + got[0].astype(F32)).astype(BF16)

        def finish(self):
            if not fast:
                return lax.psum_scatter(
                    self.sent,
                    "seq",
                    scatter_dimension=0,
                    tiled=True,
                    axis_index_groups=across,
                )
            while self.bits:
                self.step()
            return self.sent

    def step_all(main, *sums):
        for s in sums:
            s.step()
        return hold(main, *sums)

    def hold(main, *sums):
        main, *sent = tie(main, *[s.sent for s in sums])
        for s, value in zip(sums, sent):
            s.sent = value
        return main

    def hand_rows(pieces):
        widths = [sum(p.shape[1] for p in piece) for piece in pieces]
        joint = jnp.concatenate([p for piece in pieces for p in piece], axis=1)
        mine = [
            lax.dynamic_slice_in_dim(joint, (member ^ k) * rows, rows, axis=0)
            for k in range(size)
        ]
        by_member = ordered(exchange(mine))
        outs, start = [], 0
        for wide in widths:
            outs += [p[:, start : start + wide] for p in by_member]
            start += wide
        return jnp.concatenate(outs, axis=1).astype(F32)

    up_start, decay_start, decay_up = 5 * RANK, 10 * RANK, 10 * RANK + DRANK
    last_row = neighbour(tokens[0, -1:, :], 1)
    tokens_sent = to_places(
        jnp.concatenate([tokens[0], jnp.broadcast_to(last_row, (16, width))], axis=0), BF16
    )
    tokens_got = group_gather(tokens_sent)
    natural = cube_gather(
        jnp.concatenate(
            [vectors, initial_state, lowrank_weights[:, decay_up:].astype(F32)], axis=1
        )
    ).reshape(width, -1)
    lowrank = by_place(cube_gather(lowrank_weights[:, :decay_up]))
    mix_local = group_columns(mixing_weights, [(c * width, part) for c in range(5)])
    kv_pair = far_pair(mix_local[:, : 2 * part])
    mix_rest, _ = tie(mix_local[:, 2 * part :], kv_pair)
    rest_pair = far_pair(mix_rest)
    ff_spans = [(0, ff_part), (FF, part), (FF + width, ff_part)]
    feed_in, _ = tie(feedforward_weights, kv_pair)
    ff_local = group_columns(feed_in, ff_spans)
    ff_near, _ = tie(ff_local[:, : ff_part + part], rest_pair)
    near_pair = far_pair(ff_near)
    ff_tail, _ = tie(ff_local[:, ff_part + part :], near_pair)
    val_pair = far_pair(ff_tail)

    kv = gather_rows(kv_pair)
    rest = gather_rows(rest_pair)
    near = gather_rows(near_pair)
    w_val = gather_rows(val_pair)
    w_main = [kv[:, :part], kv[:, part:], rest[:, :part], rest[:, part : 2 * part]]
    w_out = rest[:, 2 * part :]
    half_ff = ff_part // 2
    w_keys = [near[:, :half_ff], near[:, half_ff:ff_part]]
    w_rec = near[:, ff_part:]
    w_vals = [w_val[:, :half_ff], w_val[:, half_ff:]]

    mine = lax.dynamic_slice_in_dim(natural, member * part, part, axis=0)
    vec_part = mine[:, :16].T
    first_state = mine[:, 16 : 16 + SPAN].T
    w_dup = mine[:, 16 + SPAN :].astype(BF16)
    vec = to_places(natural[:, :16].T, F32)
    wkv_rows = jnp.concatenate([vec_part[9:12], jnp.zeros((5, part), F32)], axis=0)
    is_first = me == 0

    w_down = lowrank[:, :up_start]
    w_ups = [lowrank[:, up_start + c * RANK : up_start + (c + 1) * RANK] for c in range(5)]
    w_ddown = lowrank[:, decay_start:]

    before = to_places(previous.reshape(2, width), F32)

    def norm_parts(value):
        centred = value - jnp.mean(value, axis=-1, keepdims=True)
        spread = jnp.mean(centred * centred, axis=-1, keepdims=True)
        scale = lax.rsqrt(spread + LN_EPS)
        return centred * scale, scale

    def norm_back(grad, gain, normal, scale):
        e = grad * gain
        return scale * (
            e
            - jnp.mean(e, axis=-1, keepdims=True)
            - normal * jnp.mean(e * normal, axis=-1, keepdims=True)
        )

    def with_previous(value, start_row):
        arrived = jnp.where(is_first, start_row, neighbour(value[-1:, :], 1))
        return jnp.concatenate([arrived, value[:-1]], axis=0)

    def from_next(value):
        return jnp.concatenate([value[1:], neighbour(value[:1, :], -1)], axis=0)

    opening = jnp.stack([jnp.bitwise_xor(me, flips(k)) == 0 for k in range(size)])
    (
        *mixed_all, dh_all, normal_one, scale_one, delta, blend, mixed_zero, mix_tanh, decay_tanh,
    ) = group_mixes(
        opening.astype(jnp.int32),
        jnp.concatenate(tokens_got, axis=0),
        before,
        vec,
        w_down,
        lowrank[:, up_start:decay_start],
        w_ddown,
        step,
    )
    scale_one = scale_one[:, :1]
    hidden = tokens_sent[:step].astype(F32)
    latent = mix_tanh.astype(BF16)
    hidden_c = [latent[:, c * RANK : (c + 1) * RANK] for c in range(5)]
    coeff = [vec[3 + c] + nt(hidden_c[c], w_ups[c]) for c in range(5)]
    log_decay = -jnp.exp(vec_part[8] + nt(dh_all, w_dup))

    mixed_all[0], rest_pair = tie(mixed_all[0], rest_pair)
    keys, values = [nn(mixed_all[c], w_main[c]) for c in range(2)]

    call = functools.partial(block_call, chunks=size, step=step, width=part)
    (totals,) = call(
        totals_kernel, ins="ttt", outs=[("x", F32)], args=(keys, values, log_decay)
    )
    by_member = ordered([totals[k] for k in range(size)])
    total = {m: (p[SPAN : SPAN + 1], p[:SPAN]) for m, p in enumerate(by_member)}
    before_chunk = [
        (jnp.ones((1, part), F32), jnp.zeros((SPAN, part), F32)) for _ in range(size)
    ]
    open_bits = size - 1
    levels = []

    def chain(early, late):
        return early[0] * late[0], late[0] * early[1] + late[1]

    def pick(flag, yes, no):
        return tuple(jnp.where(flag, a, b) for a, b in zip(yes, no))

    for mask in all_masks:
        if mask in masks:
            bit = 1 << masks.index(mask)
            levels.append({g: total[g][0] for g in total})
            for m in range(size):
                if m & bit:
                    early = (m & open_bits) ^ bit
                    before_chunk[m] = chain(total[early], before_chunk[m])
            total = {g: chain(total[g], total[g | bit]) for g in total if not g & bit}
            open_bits ^= bit
        else:
            groups = list(total)
            sent = jnp.concatenate(
                [
                    jnp.concatenate(
                        [total[g][1], jnp.broadcast_to(total[g][0], (8, part))], axis=0
                    )
                    for g in groups
                ],
                axis=0,
            )
            got = trade(sent, mask)
            high = SPAN + 8
            other = {
                g: (got[i * high + SPAN : i * high + SPAN + 1], got[i * high : i * high + SPAN])
                for i, g in enumerate(groups)
            }
            levels.append({g: (total[g][0], other[g][0]) for g in groups})
            late = bit_of(me, mask) == 1
            for m in range(size):
                g = m & open_bits
                before_chunk[m] = pick(late, chain(other[g], before_chunk[m]), before_chunk[m])
            total = {
                g: pick(late, chain(other[g], total[g]), chain(total[g], other[g]))
                for g in groups
            }
    state_in = jnp.stack(ordered([d * first_state + s for d, s in before_chunk]))

    state_in, near_pair = tie(state_in, near_pair)
    receipt, gate_pre = [nn(mixed_all[c], w_main[c]) for c in range(2, 4)]
    wkv, gated = call(
        forward_kernel,
        ins="tttttsp",
        outs=[("t", F32), ("t", BF16)],
        args=(receipt, keys, values, log_decay, gate_pre, state_in, wkv_rows),
    )
    gated, val_pair = tie(gated, val_pair)
    middle = hidden + group_sum(nt(gated, w_out))

    normal_two, scale_two = norm_parts(middle)
    normed_two = normal_two * vec[12] + vec[13]
    delta_two = with_previous(normed_two, before[1:2]) - normed_two
    key_in = (normed_two + delta_two * vec[14]).astype(BF16)
    recv_in = (normed_two + delta_two * vec[15]).astype(BF16)
    both = group_gather(jnp.concatenate([key_in, recv_in], axis=0))
    key_all = jnp.concatenate([p[:step] for p in both], axis=0)
    recv_all = jnp.concatenate([p[step:] for p in both], axis=0)
    relu = [jnp.maximum(nn(key_all, w), 0.0) for w in w_keys]
    squared = [(r * r).astype(BF16) for r in relu]
    value_out = group_sum(nt(squared[0], w_vals[0]) + nt(squared[1], w_vals[1]))
    recept_act = nn(recv_all, w_rec).astype(BF16)
    recept_pieces = exchange([recept_act[k * step : (k + 1) * step] for k in range(size)])
    recept = jax.nn.sigmoid(to_places(jnp.concatenate(ordered(recept_pieces), axis=1), F32))
    block_output = to_natural(middle + recept * value_out, BF16)

    upstream = to_places(cotangent.reshape(step, width), F32)
    value_grad = (upstream * recept).astype(BF16)
    recept_grad = to_natural(upstream * value_out * recept * (1.0 - recept), BF16)
    vg_all = group_rows(value_grad)
    rg_all = jnp.concatenate(
        exchange(
            [
                lax.dynamic_slice_in_dim(recept_grad, (member ^ k) * part, part, axis=1)
                for k in range(size)
            ]
        ),
        axis=0,
    )
    val_sums = [TeamSum(vg_all, squared[i], i == 0) for i in range(2)]
    vg_all = hold(vg_all, *val_sums)
    key_grad = [(nn(vg_all, w) * (2.0 * r)).astype(BF16) for w, r in zip(w_vals, relu)]
    key_sums = [TeamSum(key_all, key_grad[i], i == 0) for i in range(2)]
    key_grad[0] = hold(key_grad[0], *key_sums)
    key_in_grad = group_sum(nt(key_grad[0], w_keys[0]) + nt(key_grad[1], w_keys[1]))
    recv_in_grad = group_sum(nt(rg_all, w_rec))
    key_in_grad = step_all(key_in_grad, *val_sums)
    shifted_grad = key_in_grad * vec[14] + recv_in_grad * vec[15]
    two_grad = (
        key_in_grad * (1.0 - vec[14]) + recv_in_grad * (1.0 - vec[15]) + from_next(shifted_grad)
    )
    middle_grad = upstream + norm_back(two_grad, vec[12], normal_two, scale_two)
    col_12 = jnp.sum(two_grad * normal_two, axis=0)
    col_13 = jnp.sum(two_grad, axis=0)
    col_14 = jnp.sum(key_in_grad * delta_two, axis=0)
    col_15 = jnp.sum(recv_in_grad * delta_two, axis=0)

    branch_grad = middle_grad.astype(BF16)
    bg_all = group_rows(branch_grad)
    bg_all = step_all(bg_all, *key_sums)
    gated_grad = nn(bg_all, w_out)
    gate_grad, wkv_grad, local = call(
        gate_kernel,
        ins="tttttp",
        outs=[("t", BF16), ("t", F32), ("x", F32)],
        args=(gated_grad, gate_pre, wkv, receipt, log_decay, wkv_rows),
    )
    wkv_grad = step_all(wkv_grad, *val_sums)
    grad_total = dict(enumerate(ordered([local[k, :SPAN] for k in range(size)])))
    after = [(jnp.ones((1, part), F32), jnp.zeros((SPAN, part), F32)) for _ in range(size)]
    open_bits = size - 1
    for mask, level in zip(all_masks, levels):
        if mask in masks:
            bit = 1 << masks.index(mask)
            for m in range(size):
                if not m & bit:
                    late = (m & open_bits) | bit
                    d, s = after[m]
                    after[m] = (d * level[late], d * grad_total[late] + s)
            grad_total = {
                g: grad_total[g] + level[g] * grad_total[g | bit]
                for g in grad_total
                if not g & bit
            }
            open_bits ^= bit
        else:
            groups = list(grad_total)
            got = trade(jnp.concatenate([grad_total[g] for g in groups], axis=0), mask)
            other = {g: got[i * SPAN : (i + 1) * SPAN] for i, g in enumerate(groups)}
            early = bit_of(me, mask) == 0
            for m in range(size):
                g = m & open_bits
                d, s = after[m]
                after[m] = pick(early, (d * level[g][1], d * other[g] + s), (d, s))
            grad_total = {
                g: jnp.where(
                    early,
                    grad_total[g] + level[g][0] * other[g],
                    other[g] + level[g][1] * grad_total[g],
                )
                for g in groups
            }
    grad_out = jnp.stack(ordered([s for _, s in after]))
    out_sum = TeamSum(bg_all, gated, True)
    rec_sum = TeamSum(recv_all, rg_all, False)
    gate_sum = TeamSum(mixed_all[3], gate_grad, True)
    grad_out = step_all(grad_out, *key_sums, *val_sums)
    grad_out = hold(grad_out, out_sum, rec_sum)

    first_grad = grad_total[0]
    holder = lax.div(me * rows, part)

    def rows_of(who):
        return lax.dynamic_slice_in_dim(first_grad, lax.rem(who * rows, part), rows, axis=1)

    handed = exchange([rows_of(jnp.bitwise_xor(me, flips(k))) for k in range(size)])
    state_rows = handed[0]
    for k in range(1, size):
        state_rows = jnp.where(holder == (member ^ k), handed[k], state_rows)
    initial_state_gradient = state_rows.T

    d_receipt, d_keys, d_values, d_decay, extra = call(
        backward_kernel,
        ins="tttttssp",
        outs=[("t", BF16)] * 4 + [("e", F32)],
        args=(receipt, keys, values, log_decay, wkv_grad, state_in, grad_out, wkv_rows),
    )
    grads = [d_keys, d_values, d_receipt, gate_grad]
    main_sums = [TeamSum(mixed_all[c], grads[c], c == 0) for c in range(3)]
    d_decay = step_all(d_decay, out_sum, rec_sum)
    d_decay = hold(d_decay, gate_sum, *main_sums)
    mixed_grad = [None] + [group_sum(nt(grads[c], w_main[c])) for c in range(4)]
    decay_latent_grad = group_sum(nn(d_decay, w_dup))
    decay_pre = (decay_latent_grad * (1.0 - decay_tanh * decay_tanh)).astype(BF16)
    decay_pre = step_all(decay_pre, *key_sums, out_sum, rec_sum, gate_sum, *main_sums)
    key_rows = [s.finish() for s in key_sums]
    val_rows = [s.finish() for s in val_sums]
    feedforward_gradient = hand_rows([key_rows, [rec_sum.finish()], val_rows])
    mixed_grad[0] = nt(decay_pre, w_ddown)

    shift_grads = [mixed_grad[c] * delta for c in range(5)]
    offset_grads = [s.astype(BF16) for s in shift_grads]
    mix_latent_grad = jnp.concatenate(
        [nn(offset_grads[c], w_ups[c]) for c in range(5)], axis=1
    )
    mix_pre = (mix_latent_grad * (1.0 - mix_tanh * mix_tanh)).astype(BF16)
    mix_pre = step_all(mix_pre, gate_sum, *main_sums)
    mixing_gradient = hand_rows(
        [[s.finish()] for s in main_sums] + [[gate_sum.finish()], [out_sum.finish()]]
    )
    blend_grad = nt(mix_pre, w_down)
    delta_grad = blend_grad * vec[2]
    normed_grad = blend_grad
    for c in range(5):
        delta_grad = delta_grad + mixed_grad[c] * coeff[c]
        normed_grad = normed_grad + mixed_grad[c]
    normed_grad = normed_grad - delta_grad + from_next(delta_grad)
    block_input_gradient = to_natural(
        middle_grad + norm_back(normed_grad, vec[0], normal_one, scale_one), F32
    )


    def spread(value):
        zero = jnp.zeros((width, value.shape[1]), F32)
        return lax.dynamic_update_slice_in_dim(zero, value, member * part, axis=0)

    vec_low = jnp.stack(
        [
            jnp.sum(normed_grad * normal_one, axis=0),
            jnp.sum(normed_grad, axis=0),
            jnp.sum(blend_grad * delta, axis=0),
        ]
        + [jnp.sum(s, axis=0) for s in shift_grads]
        + [col_12, col_13, col_14, col_15]
    )
    vec_head = jnp.concatenate(
        [jnp.sum(extra[:, :2], axis=0), jnp.sum(local[:, SPAN : SPAN + 2], axis=0)], axis=0
    )
    by_feature = jnp.concatenate(
        [
            tn(blend, mix_pre),
            *[tn(offset_grads[c], hidden_c[c]) for c in range(5)],
            tn(mixed_zero, decay_pre),
            vec_low.T,
        ],
        axis=1,
    )
    low = cube_sum(to_cube(by_feature), BF16)
    by_channel = spread(jnp.concatenate([tn(d_decay, dh_all), vec_head.T], axis=1))
    high_part = cube_sum(by_channel.reshape(*[2] * len(all_masks), rows, -1), F32)
    lowrank_gradient = jnp.concatenate([low[:, :decay_up], high_part[:, :DRANK]], axis=1)
    vectors_gradient = jnp.concatenate(
        [low[:, decay_up : decay_up + 8], high_part[:, DRANK:], low[:, decay_up + 8 :]], axis=1
    )
    return (
        block_output.reshape(1, step, width),
        block_input_gradient.reshape(1, step, width),
        initial_state_gradient,
        mixing_gradient,
        lowrank_gradient,
        vectors_gradient,
        feedforward_gradient,
    )


def solution(mesh):
    rowwise = P("seq", None)
    tokenwise = P(None, "seq", None)
    return jax.shard_map(
        functools.partial(on_device, mesh.shape["seq"]),
        mesh=mesh,
        in_specs=(tokenwise, P(), rowwise, rowwise, rowwise, rowwise, rowwise, tokenwise),
        out_specs=(tokenwise, tokenwise, rowwise, rowwise, rowwise, rowwise, rowwise),
        check_vma=False,
    )
```

```python
import functools

import jax
import jax.numpy as jnp
from jax import lax
from jax.experimental import pallas as pl
from jax.experimental.pallas import tpu as pltpu
from jax.sharding import PartitionSpec as P

HEADS = 32
SPAN = 64
FF = 7168
RANK = 32
DRANK = 64
LN_EPS = 1e-05
GN_EPS = 0.00064

F32 = jnp.float32
BF16 = jnp.bfloat16
HI = lax.Precision.HIGHEST


def nn(a, b):
    return jnp.dot(a, b, preferred_element_type=F32)


def nt(a, b):
    return lax.dot_general(a, b, (((1,), (1,)), ((), ())), preferred_element_type=F32)


def tn(a, b):
    return lax.dot_general(a, b, (((0,), (0,)), ((), ())), preferred_element_type=F32)


def knn(a, b):
    return lax.dot_general(
        a, b, (((1,), (0,)), ((), ())), preferred_element_type=F32
    )


def knt(a, b):
    return lax.dot_general(
        a, b, (((1,), (1,)), ((), ())), preferred_element_type=F32
    )


def ktn(a, b):
    return lax.dot_general(
        a, b, (((0,), (0,)), ((), ())), preferred_element_type=F32
    )


def low_lanes(shape):
    return lax.broadcasted_iota(jnp.int32, shape, len(shape) - 1) < SPAN


def head_sum(x):
    low = low_lanes(x.shape)
    s0 = jnp.sum(jnp.where(low, x, 0.0), axis=-1, keepdims=True)
    s1 = jnp.sum(jnp.where(low, 0.0, x), axis=-1, keepdims=True)
    return jnp.where(low, s0, s1)


def two_rows(x):
    low = low_lanes(x.shape)
    return jnp.concatenate([jnp.where(low, x, 0.0), jnp.where(low, 0.0, x)], axis=0)


def fold(full):
    return jnp.where(low_lanes((SPAN, 2 * SPAN)), full[:SPAN], full[SPAN:])


def unfold(state):
    low = low_lanes(state.shape)
    return jnp.concatenate([jnp.where(low, state, 0.0), jnp.where(low, 0.0, state)], axis=0)


def running(w, upper=False):
    count = w.shape[0]
    row = lax.broadcasted_iota(jnp.int32, (count, count), 0)
    col = lax.broadcasted_iota(jnp.int32, (count, count), 1)
    keep = (col >= row) if upper else (col <= row)
    return lax.dot_general(
        jnp.where(keep, 1.0, 0.0).astype(F32),
        w,
        (((1,), (0,)), ((), ())),
        precision=HI,
        preferred_element_type=F32,
    )


def strict(count):
    row = lax.broadcasted_iota(jnp.int32, (2 * count, count), 0)
    col = lax.broadcasted_iota(jnp.int32, (2 * count, count), 1)
    row = jnp.where(row >= count, row - count, row)
    return row > col, row == col


def affinity(r, k, u, q, ks):
    count = r.shape[0]
    below, diag = strict(count)
    raw = knt(two_rows(q), ks)
    share = jnp.sum(two_rows(r * u * k), axis=-1, keepdims=True)
    return jnp.where(below, raw, jnp.where(diag, share, 0.0))


def totals_kernel(k_ref, v_ref, w_ref, out_ref):
    cum = running(w_ref[...])
    total = cum[-1:, :]
    kc = k_ref[...] * jnp.exp(total - cum)
    out_ref[0, :SPAN, :] = fold(ktn(v_ref[...], kc))
    out_ref[0, SPAN:, :] = jnp.broadcast_to(jnp.exp(total), (8, 2 * SPAN))


def group_norm(y, gain, bias):
    centred = y - head_sum(y) * (1.0 / SPAN)
    spread = head_sum(centred * centred) * (1.0 / SPAN)
    scale = lax.rsqrt(spread + GN_EPS)
    normal = centred * scale
    return normal, scale, normal * gain + bias


def forward_kernel(r_ref, k_ref, v_ref, w_ref, g_ref, s_ref, p_ref, y_ref, gated_ref):
    r, k, v, w = r_ref[...], k_ref[...], v_ref[...], w_ref[...]
    cum = running(w)
    q = r * jnp.exp(cum - w)
    ks = k * jnp.exp(-cum)
    aff = affinity(r, k, p_ref[0:1, :], q, ks)
    count = r.shape[0]
    v2 = two_rows(v)
    y = (
        knt(q, unfold(s_ref[0]))
        + knn(aff[:count], v2[:count])
        + knn(aff[count:], v2[count:])
    )
    y_ref[...] = y
    gate = g_ref[...]
    _, _, grouped = group_norm(y, p_ref[1:2, :], p_ref[2:3, :])
    gated_ref[...] = (grouped * gate * jax.nn.sigmoid(gate)).astype(BF16)


def gate_kernel(gg_ref, g_ref, y_ref, r_ref, w_ref, p_ref, gate_ref, dy_ref, out_ref):
    gated_grad, gate, y = gg_ref[...], g_ref[...], y_ref[...]
    gain = p_ref[1:2, :]
    normal, scale, grouped = group_norm(y, gain, p_ref[2:3, :])
    sig = jax.nn.sigmoid(gate)
    gate_ref[...] = (gated_grad * grouped * sig * (1.0 + gate * (1.0 - sig))).astype(BF16)
    outer = gated_grad * gate * sig
    inner = outer * gain
    dy = scale * (
        inner
        - head_sum(inner) * (1.0 / SPAN)
        - normal * (head_sum(inner * normal) * (1.0 / SPAN))
    )
    dy_ref[...] = dy
    w = w_ref[...]
    q = r_ref[...] * jnp.exp(running(w) - w)
    out_ref[0, :SPAN, :] = fold(ktn(dy, q))
    gain_grad = jnp.sum(outer * normal, axis=0, keepdims=True)
    bias_grad = jnp.sum(outer, axis=0, keepdims=True)
    out_ref[0, SPAN:, :] = jnp.concatenate(
        [gain_grad, bias_grad, jnp.zeros((6, 2 * SPAN), F32)], axis=0
    )


def backward_kernel(
    r_ref, k_ref, v_ref, w_ref, dy_ref, s_ref, gs_ref, p_ref,
    dr_ref, dk_ref, dv_ref, dd_ref, out_ref,
):
    r, k, v, w, dy = r_ref[...], k_ref[...], v_ref[...], w_ref[...], dy_ref[...]
    u = p_ref[0:1, :]
    count = r.shape[0]
    cum = running(w)
    total = cum[-1:, :]
    e_before, e_minus, e_carry = jnp.exp(cum - w), jnp.exp(-cum), jnp.exp(total - cum)
    q, ks, kc = r * e_before, k * e_minus, k * e_carry
    aff = affinity(r, k, u, q, ks)
    below, _ = strict(count)
    dy2 = two_rows(dy)
    d_aff = jnp.where(below, knt(dy2, v), 0.0)
    own = head_sum(dy * v)
    state, grad_state = s_ref[0], gs_ref[0]
    state2, grad2 = unfold(state), unfold(grad_state)
    ks2 = two_rows(ks)
    dq = knn(dy, state2) + knn(d_aff[:count], ks2[:count]) + knn(d_aff[count:], ks2[count:])
    dks = ktn(d_aff, two_rows(q))
    dkc = knn(v, grad2)
    dv_ref[...] = (ktn(aff, dy2) + knt(kc, grad2)).astype(BF16)
    dr_ref[...] = (dq * e_before + own * u * k).astype(BF16)
    dk_ref[...] = (dks * e_minus + dkc * e_carry + own * u * r).astype(BF16)
    gq, gc = q * dq, kc * dkc
    d_total = jnp.sum(gc, axis=0, keepdims=True) + jnp.exp(total) * jnp.sum(
        state * grad_state, axis=0, keepdims=True
    )
    dw = running(gq - ks * dks - gc, upper=True) - gq + d_total
    term = dw * w
    dd_ref[...] = term.astype(BF16)
    out_ref[0] = jnp.concatenate(
        [
            jnp.sum(term, axis=0, keepdims=True),
            jnp.sum(own * r * k, axis=0, keepdims=True),
            jnp.zeros((6, 2 * SPAN), F32),
        ],
        axis=0,
    )


def block_call(kernel, chunks, step, width, ins, outs, args):
    lane = 2 * SPAN
    kinds = {
        "t": pl.BlockSpec((step, lane), lambda c, h: (c, h)),
        "s": pl.BlockSpec((1, SPAN, lane), lambda c, h: (c, 0, h)),
        "x": pl.BlockSpec((1, SPAN + 8, lane), lambda c, h: (c, 0, h)),
        "e": pl.BlockSpec((1, 8, lane), lambda c, h: (c, 0, h)),
        "p": pl.BlockSpec((8, lane), lambda c, h: (0, h)),
    }
    shapes = {
        "t": lambda d: jax.ShapeDtypeStruct((chunks * step, width), d),
        "x": lambda d: jax.ShapeDtypeStruct((chunks, SPAN + 8, width), d),
        "e": lambda d: jax.ShapeDtypeStruct((chunks, 8, width), d),
    }
    return pl.pallas_call(
        kernel,
        grid=(chunks, width // lane),
        in_specs=[kinds[kind] for kind in ins],
        out_specs=[kinds[kind] for kind, _ in outs],
        out_shape=[shapes[kind](dtype) for kind, dtype in outs],
        compiler_params=pltpu.CompilerParams(vmem_limit_bytes=48 * 1024 * 1024),
    )(*args)


def weight_grad_kernel(_, x_ref, y_ref, out_ref):
    out_ref[0] = lax.dot_general(
        x_ref[...], y_ref[...], (((0,), (0,)), ((), ())), preferred_element_type=F32
    ).astype(BF16)


def weight_grad(places, x, y, block, cut, cuts):
    tokens, columns = y.shape[0], y.shape[1] // cuts
    blocks = places.shape[0]
    return pl.pallas_call(
        weight_grad_kernel,
        grid_spec=pltpu.PrefetchScalarGridSpec(
            num_scalar_prefetch=1,
            grid=(blocks,),
            in_specs=[
                pl.BlockSpec((tokens, block), lambda i, at: (0, at[i])),
                pl.BlockSpec((tokens, columns), lambda i, at: (0, cut)),
            ],
            out_specs=pl.BlockSpec((1, block, columns), lambda i, at: (i, 0, 0)),
        ),
        out_shape=jax.ShapeDtypeStruct((blocks, block, columns), BF16),
        compiler_params=pltpu.CompilerParams(vmem_limit_bytes=48 * 1024 * 1024),
    )(places, x, y)


def lanes_kernel(spans, x_ref, out_ref):
    at = 0
    for start, stop in spans:
        out_ref[:, at : at + stop - start] = x_ref[:, start:stop].astype(out_ref.dtype)
        at += stop - start


def move_lanes(spans, value, dtype):
    return pl.pallas_call(
        functools.partial(lanes_kernel, spans),
        in_specs=[pl.BlockSpec(memory_space=pltpu.VMEM)],
        out_specs=pl.BlockSpec(memory_space=pltpu.VMEM),
        out_shape=jax.ShapeDtypeStruct(value.shape, dtype),
        compiler_params=pltpu.CompilerParams(vmem_limit_bytes=32 * 1024 * 1024),
    )(value)


def place_kernel(counts, at_ref, *refs):
    ins, out_ref, sems = refs[: len(counts)], refs[-2], refs[-1]
    block = out_ref.shape[0] // sum(counts)
    copies, i = [], 0
    for ref, n in zip(ins, counts):
        for j in range(n):
            start = pl.multiple_of(at_ref[i] * block, block)
            copy = pltpu.make_async_copy(
                ref.at[pl.ds(j * block, block), :],
                out_ref.at[pl.ds(start, block), :],
                sems.at[i],
            )
            copy.start()
            copies.append(copy)
            i += 1
    for copy in copies:
        copy.wait()


def place_rows(at, pieces, block):
    counts = [p.shape[0] // block for p in pieces]
    total = sum(counts)
    return pl.pallas_call(
        functools.partial(place_kernel, counts),
        in_specs=[pl.BlockSpec(memory_space=pltpu.SMEM)]
        + [pl.BlockSpec(memory_space=pl.ANY)] * len(pieces),
        out_specs=pl.BlockSpec(memory_space=pl.ANY),
        out_shape=jax.ShapeDtypeStruct((total * block, pieces[0].shape[1]), pieces[0].dtype),
        scratch_shapes=[pltpu.SemaphoreType.DMA((total,))],
        compiler_params=pltpu.CompilerParams(vmem_limit_bytes=32 * 1024 * 1024),
    )(at, *pieces)


def mixes_kernel(
    open_ref, x_ref, before_ref, vec_ref, down_ref, up_ref, ddown_ref,
    m1_ref, m2_ref, m3_ref, m4_ref, dh_ref,
    normal_ref, scale_ref, delta_ref, blend_ref, m0_ref, tanh_ref, dtanh_ref,
):
    piece = pl.program_id(0)
    step = m1_ref.shape[0]
    x = x_ref[...].astype(F32)
    centred = x - jnp.mean(x, axis=-1, keepdims=True)
    scale = lax.rsqrt(jnp.mean(centred * centred, axis=-1, keepdims=True) + LN_EPS)
    normal = centred * scale
    full = normal * vec_ref[0:1, :] + vec_ref[1:2, :]
    normed = full[:step]
    first = jnp.where(open_ref[piece] == 1, before_ref[0:1, :], full[step : step + 1])
    row = lax.broadcasted_iota(jnp.int32, normed.shape, 0)
    delta = jnp.where(row == 0, first, pltpu.roll(normed, 1, 0)) - normed
    blend = (normed + delta * vec_ref[2:3, :]).astype(BF16)
    tanh = jnp.tanh(nn(blend, down_ref[...]))
    latent = tanh.astype(BF16)
    lane = lax.broadcasted_iota(jnp.int32, latent.shape, 1)
    mixed = []
    for c in range(5):
        own = (lane >= c * RANK) & (lane < (c + 1) * RANK)
        offset = nt(jnp.where(own, latent, jnp.zeros_like(latent)), up_ref[...])
        mixed.append((normed + delta * (vec_ref[3 + c : 4 + c, :] + offset)).astype(BF16))
    dtanh = jnp.tanh(nn(mixed[0], ddown_ref[...]))
    m1_ref[...], m2_ref[...], m3_ref[...], m4_ref[...] = mixed[1:]
    dh_ref[...] = dtanh.astype(BF16)

    @pl.when(piece == 0)
    def _():
        normal_ref[...] = normal[:step]
        scale_ref[...] = jnp.broadcast_to(scale[:step], scale_ref.shape)
        delta_ref[...] = delta
        blend_ref[...] = blend
        m0_ref[...] = mixed[0]
        tanh_ref[...] = tanh
        dtanh_ref[...] = dtanh


def group_mixes(opening, x, before, vec, down, up, ddown, step):
    high, width = step + 16, x.shape[1]
    pieces = x.shape[0] // high

    def whole(value):
        return pl.BlockSpec(value.shape, lambda k: (0, 0))

    def own(columns, dtype):
        return (
            pl.BlockSpec((step, columns), lambda k: (0, 0)),
            jax.ShapeDtypeStruct((step, columns), dtype),
        )

    def every(columns, dtype):
        return (
            pl.BlockSpec((step, columns), lambda k: ((k % 2) * 2 + k // 2, 0)),
            jax.ShapeDtypeStruct((pieces * step, columns), dtype),
        )

    outs = [every(width, BF16)] * 4 + [
        every(DRANK, BF16),
        own(width, F32),
        own(128, F32),
        own(width, F32),
        own(width, BF16),
        own(width, BF16),
        own(5 * RANK, F32),
        own(DRANK, F32),
    ]
    return pl.pallas_call(
        mixes_kernel,
        grid=(pieces,),
        in_specs=[
            pl.BlockSpec(memory_space=pltpu.SMEM),
            pl.BlockSpec((high, width), lambda k: (k, 0)),
            whole(before),
            whole(vec),
            whole(down),
            whole(up),
            whole(ddown),
        ],
        out_specs=[o[0] for o in outs],
        out_shape=[o[1] for o in outs],
        compiler_params=pltpu.CompilerParams(vmem_limit_bytes=56 * 1024 * 1024),
    )(opening, x, before, vec, down, up, ddown)


def product(pairs, outs, body, sides=(), tile=256):
    count = len(pairs)

    def kernel(*refs):
        ins, out_refs = refs[: 2 * count + len(sides)], refs[2 * count + len(sides) :]
        products = [
            (nn if pair[2] == "nn" else nt)(ins[2 * i][...], ins[2 * i + 1][...])
            for i, pair in enumerate(pairs)
        ]
        results = body(*products, *[r[...] for r in ins[2 * count :]])
        for ref, value in zip(out_refs, results):
            ref[...] = value.astype(ref.dtype)

    specs, args = [], []
    for a, b, form, at in pairs:
        depth = a.shape[1]
        specs.append(pl.BlockSpec(a.shape, lambda j: (0, 0)))
        if form == "nn":
            specs.append(pl.BlockSpec((depth, tile), lambda j, at=at: (0, at + j)))
        else:
            specs.append(pl.BlockSpec((tile, depth), lambda j, at=at: (j, at)))
        args += [a, b]
    for side in sides:
        specs.append(pl.BlockSpec((side.shape[0], tile), lambda j: (0, j)))
    return pl.pallas_call(
        kernel,
        grid=(outs[0][1] // tile,),
        in_specs=specs,
        out_specs=[pl.BlockSpec((o[0], tile), lambda j: (0, j)) for o in outs],
        out_shape=[jax.ShapeDtypeStruct(o[:2], o[2]) for o in outs],
        compiler_params=pltpu.CompilerParams(vmem_limit_bytes=56 * 1024 * 1024),
    )(*args, *sides)


def local(fn, outs, *args, scalar=None):
    def kernel(*refs):
        lead = [] if scalar is None else [refs[0]]
        ins, out_refs = refs[len(lead) : -len(outs)], refs[-len(outs) :]
        results = fn(*[r[0] for r in lead], *[r[...] for r in ins])
        for ref, value in zip(out_refs, results):
            ref[...] = value.astype(ref.dtype)

    specs = [pl.BlockSpec(memory_space=pltpu.VMEM)] * len(args)
    if scalar is not None:
        specs = [pl.BlockSpec(memory_space=pltpu.SMEM)] + specs
        args = (scalar.reshape(1), *args)
    return pl.pallas_call(
        kernel,
        in_specs=specs,
        out_specs=[pl.BlockSpec(memory_space=pltpu.VMEM)] * len(outs),
        out_shape=[jax.ShapeDtypeStruct(o[:2], o[2]) for o in outs],
        compiler_params=pltpu.CompilerParams(vmem_limit_bytes=56 * 1024 * 1024),
    )(*args)


def take_lanes(value, spans):
    if len(spans) == 1:
        return value
    return jnp.concatenate([value[:, a:b] for a, b in spans], axis=1)


def norm_back(grad, gain, normal, scale):
    e = grad * gain
    return scale * (
        e
        - jnp.mean(e, axis=-1, keepdims=True)
        - normal * jnp.mean(e * normal, axis=-1, keepdims=True)
    )


def rows_above(value, first):
    row = lax.broadcasted_iota(jnp.int32, value.shape, 0)
    return jnp.where(row == 0, first, pltpu.roll(value, 1, 0))


def rows_below(value, last):
    row = lax.broadcasted_iota(jnp.int32, value.shape, 0)
    high = value.shape[0]
    return jnp.where(row == high - 1, last, pltpu.roll(value, high - 1, 0))


def padded(rows):
    return jnp.concatenate(
        list(rows) + [jnp.zeros((8 - len(rows), rows[0].shape[1]), F32)], axis=0
    )


def column_sum(value):
    return jnp.sum(value, axis=0, keepdims=True)


def gates_kernel(
    spans, who_ref, middle_ref, value_ref, more_ref, act_ref, cot_ref,
    out_ref, up_ref, vg_ref, rg_ref, held,
):
    to_spans, from_spans = spans
    step, part = act_ref.shape[0] // 4, act_ref.shape[1]
    who = who_ref[0]
    act = [
        act_ref[pl.ds(pl.multiple_of((who ^ j) * step, step), step), :] for j in range(4)
    ]
    recept = jax.nn.sigmoid(take_lanes(jnp.concatenate(act, axis=1).astype(F32), to_spans))
    value = value_ref[...] + more_ref[...].astype(F32)
    out = middle_ref[...] + recept * value
    out_ref[...] = take_lanes(out, from_spans).astype(BF16)
    up = take_lanes(cot_ref[...].astype(F32), to_spans)
    up_ref[...] = up
    vg_ref[...] = (up * recept).astype(BF16)
    held[...] = take_lanes(up * value * recept * (1.0 - recept), from_spans)
    for k in range(4):
        at = pl.multiple_of((who ^ k) * part, part)
        rg_ref[k * step : (k + 1) * step, :] = held[:, pl.ds(at, part)].astype(BF16)


def gates(spans, who, middle, value, more, act, cot):
    step, width = middle.shape
    part = act.shape[1]
    shape = jax.ShapeDtypeStruct
    return pl.pallas_call(
        functools.partial(gates_kernel, spans),
        in_specs=[pl.BlockSpec(memory_space=pltpu.SMEM)]
        + [pl.BlockSpec(memory_space=pltpu.VMEM)] * 5,
        out_specs=[pl.BlockSpec(memory_space=pltpu.VMEM)] * 4,
        out_shape=[
            shape((step, width), BF16),
            shape((step, width), F32),
            shape((step, width), BF16),
            shape((4 * step, part), BF16),
        ],
        scratch_shapes=[pltpu.VMEM((step, width), F32)],
        compiler_params=pltpu.CompilerParams(vmem_limit_bytes=56 * 1024 * 1024),
    )(who.reshape(1), middle, value, more, act, cot)


def mixes_back_kernel(
    kept_ref, got_ref, dl_ref, dl_more_ref, delta_ref, tanh_ref, dtanh_ref, blend_ref, m0_ref,
    down_ref, up_ref, ddown_ref, vec_ref,
    rest_ref, dg_ref, row_ref, cols_ref, down_out, up_out, ddown_out,
):
    step = delta_ref.shape[0]
    dtanh = dtanh_ref[...]
    decay_grad = dl_ref[...] + dl_more_ref[...].astype(F32)
    decay_pre = (decay_grad * (1.0 - dtanh * dtanh)).astype(BF16)
    ddown_out[...] = tn(m0_ref[...], decay_pre)
    tanh = tanh_ref[...]
    latent = tanh.astype(BF16)
    lane = lax.broadcasted_iota(jnp.int32, latent.shape, 1)
    delta, up = delta_ref[...], up_ref[...]
    latent_grad = jnp.zeros(latent.shape, F32)
    up_grad = jnp.zeros(up_out.shape, F32)
    dg = jnp.zeros(delta.shape, F32)
    total = jnp.zeros(delta.shape, F32)
    cols = []
    for c in range(5):
        own = (lane >= c * RANK) & (lane < (c + 1) * RANK)
        mine = jnp.where(own, latent, jnp.zeros_like(latent))
        if c == 0:
            grad = nt(decay_pre, ddown_ref[...])
        else:
            at = slice((c - 1) * step, c * step)
            grad = kept_ref[at, :] + got_ref[at, :].astype(F32)
        shift = grad * delta
        cols.append(column_sum(shift))
        offset = shift.astype(BF16)
        latent_grad = jnp.where(own, nn(offset, up), latent_grad)
        up_grad = up_grad + tn(offset, mine)
        dg = dg + grad * (vec_ref[3 + c : 4 + c, :] + nt(mine, up))
        total = total + grad
    up_out[...] = up_grad
    mix_pre = (latent_grad * (1.0 - tanh * tanh)).astype(BF16)
    down_out[...] = tn(blend_ref[...], mix_pre)
    blend_grad = nt(mix_pre, down_ref[...])
    dg = dg + blend_grad * vec_ref[2:3, :]
    rest_ref[...] = total + blend_grad - dg
    dg_ref[...] = dg
    row_ref[...] = dg[:8]
    cols_ref[...] = padded([column_sum(blend_grad * delta)] + cols)


def mixes_back(*args):
    delta, down, ddown = args[4], args[9], args[11]
    step, width = delta.shape
    shape = jax.ShapeDtypeStruct
    outs = [
        shape((step, width), F32),
        shape((step, width), F32),
        shape((8, width), F32),
        shape((8, width), F32),
        shape(down.shape, F32),
        shape(down.shape, F32),
        shape(ddown.shape, F32),
    ]
    return pl.pallas_call(
        mixes_back_kernel,
        in_specs=[pl.BlockSpec(memory_space=pltpu.VMEM)] * len(args),
        out_specs=[pl.BlockSpec(memory_space=pltpu.VMEM)] * len(outs),
        out_shape=outs,
        compiler_params=pltpu.CompilerParams(vmem_limit_bytes=60 * 1024 * 1024),
    )(*args)


def tie(*values):
    return lax.optimization_barrier(values)


def on_device(
    count,
    tokens,
    previous,
    initial_state,
    mixing_weights,
    lowrank_weights,
    vectors,
    feedforward_weights,
    cotangent,
):
    fast = initial_state.shape[0] == 64
    masks = (1, 8) if fast else (1, 2)
    size = 1 << len(masks)
    teams = count // size
    all_masks = [1 << b for b in range(count.bit_length() - 1)]
    team_masks = [b for b in all_masks if b not in masks]
    far = 16
    team_masks.sort(key=lambda b: fast and b != far)
    me = lax.axis_index("seq")
    _, step, width = tokens.shape
    rows = mixing_weights.shape[0]
    part = width // size
    ff_part = FF // size
    team_rows = rows * size
    def bit_of(who, mask):
        return (who // mask) % 2 if isinstance(who, int) else lax.rem(lax.div(who, mask), 2)

    def member_of(who):
        return sum(bit_of(who, b) << j for j, b in enumerate(masks))

    def team_of(who):
        return sum(bit_of(who, b) << j for j, b in enumerate(team_masks))

    member, team = member_of(me), team_of(me)
    order = sorted(range(count), key=lambda d: (team_of(d), member_of(d)))
    inverse = sorted(range(count), key=lambda p: order[p])
    across = [order[m::size] for m in range(size)]
    square = [order[m :: 2 * size] for m in range(2 * size)]
    def lane_spans(blocks):
        spans = []
        for d in blocks:
            if spans and spans[-1][1] == d * rows:
                spans[-1][1] = (d + 1) * rows
            else:
                spans.append([d * rows, (d + 1) * rows])
        return spans

    to_spans, from_spans = lane_spans(order), lane_spans(inverse)

    def to_places(value, dtype):
        return move_lanes(to_spans, value, dtype)

    def flips(k):
        return sum(b for j, b in enumerate(masks) if (k >> j) & 1)

    def trade(value, mask):
        return lax.ppermute(value, "seq", [(d, d ^ mask) for d in range(count)])

    def group_gather(value):
        side = trade(value, masks[1])
        return value, side, trade(jnp.concatenate([value, side], axis=0), masks[0])

    def group_rows(value):
        high, columns = value.shape

        def lay(own, side, far):
            return (jnp.concatenate([own, far[:high], side, far[high:]], axis=0),)

        return local(lay, [(size * high, columns, value.dtype)], *group_gather(value))[0]

    def halves(value):
        cut = [value[k * step : (k + 1) * step] for k in range(size)]
        return [cut[0], cut[2]], [cut[1], cut[3]]

    def group_sum(kept, sent):
        high, columns = kept.shape[0] // 2, kept.shape[1]
        got = trade(sent, masks[0])

        def add(mine, more):
            total = mine + more.astype(F32)
            return total[:high], total[high:]

        mine, side = local(add, [(high, columns, F32), (high, columns, BF16)], kept, got)
        return mine, trade(side, masks[1])

    def crossing_sum(*pairs):
        units = len(pairs)

        def body(*products):
            parts = [halves(p) for p in products]
            kept = [p[0][i] for i in range(2) for p in parts]
            sent = [p[1][i] for i in range(2) for p in parts]
            return jnp.concatenate(kept, axis=0), jnp.concatenate(sent, axis=0)

        high = 2 * units * step
        return product(
            [(a, b, "nt", at) for a, b, at in pairs],
            [(high, width, F32), (high, width, BF16)],
            body,
        )

    def exchange(pieces):
        pieces, high = list(pieces), pieces[0].shape[0]
        for j in reversed(range(len(masks))):
            keys = [k for k in range(size) if (k >> j) & 1]
            got = trade(jnp.concatenate([pieces[k] for k in keys], axis=0), masks[j])
            for i, k in enumerate(keys):
                pieces[k] = got[i * high : (i + 1) * high]
        return pieces

    def ordered(pieces):
        pieces = list(pieces)
        for j in range(len(masks)):
            swap = lax.rem(lax.div(member, 1 << j), 2) == 1
            pieces = [
                jnp.where(swap, pieces[k ^ (1 << j)], pieces[k]) for k in range(len(pieces))
            ]
        return pieces

    def neighbour(value, offset):
        pairs = [(d, d + offset) for d in range(count) if 0 <= d + offset < count]
        return lax.ppermute(value, "seq", pairs)

    def take_columns(value, spans, who):
        return jnp.concatenate(
            [
                lax.dynamic_slice_in_dim(value, start + who * wide, wide, axis=1)
                for start, wide in spans
            ],
            axis=1,
        )

    def group_columns(value, spans):
        pieces = [take_columns(value, spans, member ^ k) for k in range(size)]
        return jnp.concatenate(ordered(exchange(pieces)), axis=0)

    def crossing(first):
        bits = list(range(1, len(team_masks))) + [0]
        if first:
            bits[0], bits[1] = bits[1], bits[0]
        return bits

    def far_pair(local):
        if not fast:
            return local
        got = trade(local, far)
        upper = bit_of(me, far) == 1
        return jnp.concatenate(
            [jnp.where(upper, got, local), jnp.where(upper, local, got)], axis=0
        )

    def gather_rows(paired):
        groups = square if fast else across
        return lax.all_gather(paired, "seq", axis=0, tiled=True, axis_index_groups=groups)

    first_steps = []

    def cube_gather(value):
        for mask in reversed(all_masks):
            got = trade(value, mask)
            upper = bit_of(me, mask) == 1
            value = jnp.stack([jnp.where(upper, got, value), jnp.where(upper, value, got)])
            if mask == 8:
                first_steps.append(value)
        axes = len(all_masks)
        return value.transpose(*reversed(range(axes)), *range(axes, value.ndim))

    place_axes = [all_masks[::-1].index(b) for b in team_masks[::-1] + list(masks[::-1])]

    def by_place(cube):
        rest = range(len(all_masks), cube.ndim)
        return cube.transpose(*place_axes, *rest).reshape(width, -1)

    def to_cube(value):
        cube = value.reshape(*[2] * len(place_axes), rows, -1)
        back = [place_axes.index(a) for a in range(len(place_axes))]
        return cube.transpose(*back, len(back), len(back) + 1)

    def cube_sum(cube, kind):
        for axis, mask in reversed(list(enumerate(reversed(all_masks)))):
            bit = bit_of(me, mask)
            sent = lax.dynamic_index_in_dim(cube, 1 - bit, axis, keepdims=False)
            kept = lax.dynamic_index_in_dim(cube, bit, axis, keepdims=False)
            cube = kept.astype(F32) + trade(sent.astype(kind), mask).astype(F32)
        return cube

    class TeamSum:
        last = {}

        def __init__(self, x, y, first, cut=0, cuts=1):
            self.bits = crossing(first)
            self.args = (x, y, team_rows, cut, cuts)
            self.stage = 0
            places = [0]
            for b in reversed(self.bits):
                places = places + [p | (1 << b) for p in places]
            self.half = teams // 2
            self.places = jnp.bitwise_xor(jnp.asarray(places, jnp.int32), team)
            self.kept = self.got = None
            if fast:
                self.sent = weight_grad(self.places[self.half :], *self.args)
            else:
                self.sent = tn(x, y).astype(BF16)

        def step(self):
            if not fast or not self.bits:
                return
            key = (self.bits[0], self.stage)
            if key in TeamSum.last:
                self.sent = tie(self.sent, TeamSum.last[key])[0]
            got = trade(self.sent, team_masks[self.bits[0]])
            TeamSum.last[key] = got
            kept = self.kept
            if kept is None:
                kept = weight_grad(self.places[: self.half], *self.args)
            self.bits = self.bits[1:]
            self.stage += 1
            self.half //= 2
            h = self.half
            if h:
                self.sent = (kept[h:].astype(F32) + got[h:].astype(F32)).astype(BF16)
                self.kept = (kept[:h].astype(F32) + got[:h].astype(F32)).astype(BF16)
            else:
                self.sent = (kept[0].astype(F32) + got[0].astype(F32)).astype(BF16)

        def finish(self):
            if not fast:
                return lax.psum_scatter(
                    self.sent,
                    "seq",
                    scatter_dimension=0,
                    tiled=True,
                    axis_index_groups=across,
                )
            while self.bits:
                self.step()
            return self.sent

    def step_all(main, *sums):
        for s in sums:
            s.step()
        return hold(main, *sums)

    def hold(main, *sums):
        main, *sent = tie(main, *[s.sent for s in sums])
        for s, value in zip(sums, sent):
            s.sent = value
        return main

    def hand_rows(pieces):
        widths = [sum(p.shape[1] for p in piece) for piece in pieces]
        joint = jnp.concatenate([p for piece in pieces for p in piece], axis=1)
        mine = [
            lax.dynamic_slice_in_dim(joint, (member ^ k) * rows, rows, axis=0)
            for k in range(size)
        ]
        by_member = ordered(exchange(mine))
        outs, start = [], 0
        for wide in widths:
            outs += [p[:, start : start + wide] for p in by_member]
            start += wide
        return jnp.concatenate(outs, axis=1).astype(F32)

    up_start, decay_start, decay_up = 5 * RANK, 10 * RANK, 10 * RANK + DRANK
    last_row = neighbour(tokens[0, -1:, :], 1)
    tokens_sent = to_places(
        jnp.concatenate([tokens[0], jnp.broadcast_to(last_row, (16, width))], axis=0), BF16
    )
    natural = cube_gather(
        jnp.concatenate(
            [vectors, initial_state, lowrank_weights[:, decay_up:].astype(F32)], axis=1
        )
    ).reshape(width, -1)
    low_cube = cube_gather(lowrank_weights[:, :decay_up])
    lowrank = by_place(low_cube)
    tokens_all = jnp.concatenate(group_gather(tokens_sent), axis=0)
    mix_in, _ = tie(mixing_weights, first_steps[-1])
    mix_local = group_columns(mix_in, [(c * width, part) for c in range(5)])
    kv_pair = far_pair(mix_local[:, : 2 * part])
    mix_rest, _ = tie(mix_local[:, 2 * part :], kv_pair)
    feed_in = tie(feedforward_weights, kv_pair, tokens_all)[0]
    ff_spans = [(FF, part), (0, ff_part), (FF + width, ff_part)]
    ff_local = group_columns(feed_in, ff_spans)
    rest_pair = far_pair(jnp.concatenate([mix_rest, ff_local[:, :part]], axis=1))
    ff_near, _ = tie(ff_local[:, part : part + ff_part], rest_pair)
    near_pair = far_pair(ff_near)
    ff_tail, _ = tie(ff_local[:, part + ff_part :], near_pair)
    val_pair = far_pair(ff_tail)
    w_kv = gather_rows(kv_pair)
    w_rest = gather_rows(rest_pair)
    w_key = gather_rows(near_pair)
    w_val = gather_rows(val_pair)
    tiles = part // 256

    mine = lax.dynamic_slice_in_dim(natural, member * part, part, axis=0)
    vec_part = mine[:, :16].T
    first_state = mine[:, 16 : 16 + SPAN].T
    w_dup = mine[:, 16 + SPAN :].astype(BF16)
    vec = by_place(
        natural[:, :16].reshape(*[2] * len(all_masks), rows, 16)
    ).T
    wkv_rows = jnp.concatenate([vec_part[9:12], jnp.zeros((5, part), F32)], axis=0)
    is_first = (me == 0).astype(jnp.int32)
    before = to_places(previous.reshape(2, width), F32)
    w_down, w_up = lowrank[:, :up_start], lowrank[:, up_start:decay_start]
    w_ddown = lowrank[:, decay_start:]

    opening = jnp.stack(
        [jnp.bitwise_xor(me, flips(k)) == 0 for k in (0, 2, 1, 3)]
    ).astype(jnp.int32)
    (
        *mixed_all, dh_all, normal_one, scale_one, delta, blend, mixed_zero, mix_tanh, decay_tanh,
    ) = group_mixes(opening, tokens_all, before, vec, w_down, w_up, w_ddown, step)
    mixed_all[0], rest_pair = tie(mixed_all[0], rest_pair)
    everyone = size * step
    (log_decay,) = product(
        [(dh_all, w_dup, "nt", 0)],
        [(everyone, part, F32)],
        lambda acc, base: (-jnp.exp(base + acc),),
        sides=(vec_part[8:9],),
    )
    keys, values = product(
        [(mixed_all[0], w_kv, "nn", 0), (mixed_all[1], w_kv, "nn", tiles)],
        [(everyone, part, F32)] * 2,
        lambda a, b: (a, b),
    )

    call = functools.partial(block_call, chunks=size, step=step, width=part)
    (totals,) = call(
        totals_kernel, ins="ttt", outs=[("x", F32)], args=(keys, values, log_decay)
    )
    by_member = ordered([totals[k] for k in range(size)])
    total = {m: (p[SPAN : SPAN + 1], p[:SPAN]) for m, p in enumerate(by_member)}
    before_chunk = [
        (jnp.ones((1, part), F32), jnp.zeros((SPAN, part), F32)) for _ in range(size)
    ]
    open_bits = size - 1
    levels = []

    def chain(early, late):
        return early[0] * late[0], late[0] * early[1] + late[1]

    def pick(flag, yes, no):
        return tuple(jnp.where(flag, a, b) for a, b in zip(yes, no))

    for mask in all_masks:
        if mask in masks:
            bit = 1 << masks.index(mask)
            levels.append({g: total[g][0] for g in total})
            for m in range(size):
                if m & bit:
                    early = (m & open_bits) ^ bit
                    before_chunk[m] = chain(total[early], before_chunk[m])
            total = {g: chain(total[g], total[g | bit]) for g in total if not g & bit}
            open_bits ^= bit
        else:
            groups = list(total)
            sent = jnp.concatenate(
                [
                    jnp.concatenate(
                        [total[g][1], jnp.broadcast_to(total[g][0], (8, part))], axis=0
                    )
                    for g in groups
                ],
                axis=0,
            )
            got = trade(sent, mask)
            high = SPAN + 8
            other = {
                g: (got[i * high + SPAN : i * high + SPAN + 1], got[i * high : i * high + SPAN])
                for i, g in enumerate(groups)
            }
            levels.append({g: (total[g][0], other[g][0]) for g in groups})
            late = bit_of(me, mask) == 1
            for m in range(size):
                g = m & open_bits
                before_chunk[m] = pick(late, chain(other[g], before_chunk[m]), before_chunk[m])
            total = {
                g: pick(late, chain(other[g], total[g]), chain(total[g], other[g]))
                for g in groups
            }
    state_in = jnp.stack(ordered([d * first_state + s for d, s in before_chunk]))

    state_in, near_pair = tie(state_in, near_pair)
    receipt, gate_pre = product(
        [(mixed_all[2], w_rest, "nn", 0), (mixed_all[3], w_rest, "nn", tiles)],
        [(everyone, part, F32)] * 2,
        lambda a, b: (a, b),
    )
    wkv, gated = call(
        forward_kernel,
        ins="tttttsp",
        outs=[("t", F32), ("t", BF16)],
        args=(receipt, keys, values, log_decay, gate_pre, state_in, wkv_rows),
    )
    gated, val_pair = tie(gated, val_pair)
    branch, branch_more = group_sum(*crossing_sum((gated, w_rest, 2)))

    def norm_two(hidden, mine, more, vec):
        middle = hidden[:step].astype(F32) + mine + more.astype(F32)
        centred = middle - jnp.mean(middle, axis=-1, keepdims=True)
        scale = lax.rsqrt(jnp.mean(centred * centred, axis=-1, keepdims=True) + LN_EPS)
        normal = centred * scale
        tail = normal[step - 8 :] * vec[12:13] + vec[13:14]
        return middle, normal, jnp.broadcast_to(scale, (step, 128)), tail

    whole = (step, width, F32)
    middle, normal_two, scale_two, tail_two = local(
        norm_two,
        [whole, whole, (step, 128, F32), (8, width, F32)],
        tokens_sent,
        branch,
        branch_more,
        vec,
    )

    def mix_two(first, normal, arrived, before, vec):
        normed = normal * vec[12:13] + vec[13:14]
        above = jnp.where(first == 1, before[1:2], arrived[7:8])
        delta = rows_above(normed, above) - normed
        key_in, recv_in = normed + delta * vec[14:15], normed + delta * vec[15:16]
        return jnp.concatenate([key_in, recv_in], axis=0), delta

    both, delta_two = local(
        mix_two,
        [(2 * step, width, BF16), whole],
        normal_two,
        neighbour(tail_two, 1),
        before,
        vec,
        scalar=is_first,
    )

    def lay_both(own, side, far):
        parts = [own, far[: 2 * step], side, far[2 * step :]]
        return [
            jnp.concatenate([p[i * step : (i + 1) * step] for p in parts], axis=0)
            for i in range(2)
        ]

    key_all, recv_all = local(
        lay_both, [(everyone, width, BF16)] * 2, *group_gather(both)
    )
    relu, squared = product(
        [(key_all, w_key, "nn", 0)],
        [(everyone, ff_part, F32), (everyone, ff_part, BF16)],
        lambda acc: (jnp.maximum(acc, 0.0), jnp.square(jnp.maximum(acc, 0.0))),
    )
    (recept_act,) = product(
        [(recv_all, w_rest, "nn", 3 * tiles)],
        [(everyone, part, BF16)],
        lambda acc: (acc,),
    )
    acts = exchange([recept_act[k * step : (k + 1) * step] for k in range(size)])
    value, value_more = group_sum(*crossing_sum((squared, w_val, 0)))
    block_output, upstream, value_grad, recept_grads = gates(
        (to_spans, from_spans),
        member,
        middle,
        value,
        value_more,
        jnp.concatenate(acts, axis=0),
        cotangent.reshape(step, width),
    )

    rg_all = jnp.concatenate(
        exchange([recept_grads[k * step : (k + 1) * step] for k in range(size)]), axis=0
    )
    vg_all = group_rows(value_grad)
    cuts = 2 if fast else 1
    val_sums = [TeamSum(vg_all, squared, i == 0, i, cuts) for i in range(cuts)]
    vg_all = hold(vg_all, *val_sums)
    (key_grad,) = product(
        [(vg_all, w_val, "nn", 0)],
        [(everyone, ff_part, BF16)],
        lambda acc, relu: (acc * (2.0 * relu),),
        sides=(relu,),
    )
    key_sums = [TeamSum(key_all, key_grad, i == 0, i, cuts) for i in range(cuts)]
    key_grad = hold(key_grad, *key_sums)
    mine_two, more_two = group_sum(*crossing_sum((key_grad, w_key, 0), (rg_all, w_rest, 3)))
    mine_two = step_all(mine_two, *val_sums)

    def inputs_back(mine, more, vec):
        grads = mine + more.astype(F32)
        top = grads[:8] * vec[14:15] + grads[step : step + 8] * vec[15:16]
        return grads, top

    in_grads, top_two = local(
        inputs_back, [(2 * step, width, F32), (8, width, F32)], mine_two, more_two, vec
    )
    last_flag = (me == count - 1).astype(jnp.int32)

    def norm_two_back(last, grads, arrived, upstream, normal, scale, delta, vec):
        key_grad, recv_grad = grads[:step], grads[step:]
        shifted = key_grad * vec[14:15] + recv_grad * vec[15:16]
        below = jnp.where(last == 1, jnp.zeros_like(arrived[:1]), arrived[:1])
        grad = (
            key_grad * (1.0 - vec[14:15])
            + recv_grad * (1.0 - vec[15:16])
            + rows_below(shifted, below)
        )
        out = upstream + norm_back(grad, vec[12:13], normal, scale[:, :1])
        cols = padded(
            [
                column_sum(grad * normal),
                column_sum(grad),
                column_sum(key_grad * delta),
                column_sum(recv_grad * delta),
            ]
        )
        return out, out, cols

    middle_grad, branch_grad, cols_two = local(
        norm_two_back,
        [whole, (step, width, BF16), (8, width, F32)],
        in_grads,
        neighbour(top_two, -1),
        upstream,
        normal_two,
        scale_two,
        delta_two,
        vec,
        scalar=last_flag,
    )

    bg_all = group_rows(branch_grad)
    (gated_grad,) = product(
        [(bg_all, w_rest, "nn", 2 * tiles)], [(everyone, part, F32)], lambda acc: (acc,)
    )
    gated_grad = step_all(gated_grad, *key_sums)
    gate_grad, wkv_grad, ends = call(
        gate_kernel,
        ins="tttttp",
        outs=[("t", BF16), ("t", F32), ("x", F32)],
        args=(gated_grad, gate_pre, wkv, receipt, log_decay, wkv_rows),
    )
    grad_total = dict(enumerate(ordered([ends[k, :SPAN] for k in range(size)])))
    after = [(jnp.ones((1, part), F32), jnp.zeros((SPAN, part), F32)) for _ in range(size)]
    open_bits = size - 1
    for mask, level in zip(all_masks, levels):
        if mask in masks:
            bit = 1 << masks.index(mask)
            for m in range(size):
                if not m & bit:
                    late = (m & open_bits) | bit
                    d, s = after[m]
                    after[m] = (d * level[late], d * grad_total[late] + s)
            grad_total = {
                g: grad_total[g] + level[g] * grad_total[g | bit]
                for g in grad_total
                if not g & bit
            }
            open_bits ^= bit
        else:
            groups = list(grad_total)
            got = trade(jnp.concatenate([grad_total[g] for g in groups], axis=0), mask)
            other = {g: got[i * SPAN : (i + 1) * SPAN] for i, g in enumerate(groups)}
            early = bit_of(me, mask) == 0
            for m in range(size):
                g = m & open_bits
                d, s = after[m]
                after[m] = pick(early, (d * level[g][1], d * other[g] + s), (d, s))
            grad_total = {
                g: jnp.where(
                    early,
                    grad_total[g] + level[g][0] * other[g],
                    other[g] + level[g][1] * grad_total[g],
                )
                for g in groups
            }
    grad_out = jnp.stack(ordered([s for _, s in after]))
    out_sum = TeamSum(bg_all, gated, True)
    rec_sum = TeamSum(recv_all, rg_all, False)
    gate_sum = TeamSum(mixed_all[3], gate_grad, True)
    grad_out = step_all(grad_out, *key_sums, *val_sums)
    grad_out = hold(grad_out, out_sum, rec_sum)

    first_grad = grad_total[0]
    holder = lax.div(me * rows, part)

    def rows_of(who):
        return lax.dynamic_slice_in_dim(first_grad, lax.rem(who * rows, part), rows, axis=1)

    handed = exchange([rows_of(jnp.bitwise_xor(me, flips(k))) for k in range(size)])
    state_rows = handed[0]
    for k in range(1, size):
        state_rows = jnp.where(holder == (member ^ k), handed[k], state_rows)
    initial_state_gradient = state_rows.T

    d_receipt, d_keys, d_values, d_decay, extra = call(
        backward_kernel,
        ins="tttttssp",
        outs=[("t", BF16)] * 4 + [("e", F32)],
        args=(receipt, keys, values, log_decay, wkv_grad, state_in, grad_out, wkv_rows),
    )
    grads = [d_keys, d_values, d_receipt, gate_grad]
    main_sums = [TeamSum(mixed_all[c], grads[c], c == 0) for c in range(3)]
    grads[3] = step_all(grads[3], out_sum, rec_sum)
    grads[0] = hold(grads[0], gate_sum, *main_sums)
    kept, sent = crossing_sum(
        (grads[0], w_kv, 0), (grads[1], w_kv, 1), (grads[2], w_rest, 0), (grads[3], w_rest, 1)
    )
    sent = step_all(sent, out_sum, rec_sum)
    mixed_mine, mixed_more = group_sum(kept, sent)

    def latent_back(grad, up):
        kept, sent = halves(nn(grad, up))
        return jnp.concatenate(kept, axis=0), jnp.concatenate(sent, axis=0)

    latent_mine, latent_more = group_sum(
        *local(
            latent_back, [(2 * step, DRANK, F32), (2 * step, DRANK, BF16)], d_decay, w_dup
        )
    )
    mixed_mine = step_all(mixed_mine, *val_sums, *key_sums)
    rest_grad, delta_grad, top_one, cols_mix, down_grad, up_grad, ddown_grad = mixes_back(
        mixed_mine,
        mixed_more,
        latent_mine,
        latent_more,
        delta,
        mix_tanh,
        decay_tanh,
        blend,
        mixed_zero,
        w_down,
        w_up,
        w_ddown,
        vec,
    )
    key_rows = [s.finish() for s in key_sums]
    val_rows = [s.finish() for s in val_sums]
    feedforward_gradient = hand_rows([key_rows, [rec_sum.finish()], val_rows])

    def norm_one_back(last, rest, shifted, arrived, normal, scale, middle, vec):
        below = jnp.where(last == 1, jnp.zeros_like(arrived[:1]), arrived[:1])
        grad = rest + rows_below(shifted, below)
        out = middle + norm_back(grad, vec[0:1], normal, scale[:, :1])
        cols = padded([column_sum(grad * normal), column_sum(grad)])
        return take_lanes(out, from_spans), cols

    rest_grad = step_all(rest_grad, gate_sum, *main_sums)
    block_input_gradient, cols_one = local(
        norm_one_back,
        [whole, (8, width, F32)],
        rest_grad,
        delta_grad,
        neighbour(top_one, -1),
        normal_one,
        scale_one,
        middle_grad,
        vec,
        scalar=last_flag,
    )
    mixing_gradient = hand_rows(
        [[s.finish()] for s in main_sums] + [[gate_sum.finish()], [out_sum.finish()]]
    )


    def spread(value):
        zero = jnp.zeros((width, value.shape[1]), F32)
        return lax.dynamic_update_slice_in_dim(zero, value, member * part, axis=0)

    vec_low = jnp.concatenate([cols_one[:2], cols_mix[:6], cols_two[:4]], axis=0)
    vec_head = jnp.concatenate(
        [jnp.sum(extra[:, :2], axis=0), jnp.sum(ends[:, SPAN : SPAN + 2], axis=0)], axis=0
    )
    by_feature = jnp.concatenate([down_grad, up_grad, ddown_grad, vec_low.T], axis=1)
    low = cube_sum(to_cube(by_feature), BF16)
    by_channel = spread(jnp.concatenate([tn(d_decay, dh_all), vec_head.T], axis=1))
    high_part = cube_sum(by_channel.reshape(*[2] * len(all_masks), rows, -1), F32)
    lowrank_gradient = jnp.concatenate([low[:, :decay_up], high_part[:, :DRANK]], axis=1)
    vectors_gradient = jnp.concatenate(
        [low[:, decay_up : decay_up + 8], high_part[:, DRANK:], low[:, decay_up + 8 :]], axis=1
    )
    return (
        block_output.reshape(1, step, width),
        block_input_gradient.reshape(1, step, width),
        initial_state_gradient,
        mixing_gradient,
        lowrank_gradient,
        vectors_gradient,
        feedforward_gradient,
    )


def solution(mesh):
    rowwise = P("seq", None)
    tokenwise = P(None, "seq", None)
    return jax.shard_map(
        functools.partial(on_device, mesh.shape["seq"]),
        mesh=mesh,
        in_specs=(tokenwise, P(), rowwise, rowwise, rowwise, rowwise, rowwise, tokenwise),
        out_specs=(tokenwise, tokenwise, rowwise, rowwise, rowwise, rowwise, rowwise),
        check_vma=False,
    )
```

```python
import functools

import jax
import jax.numpy as jnp
from jax import lax
from jax.experimental import pallas as pl
from jax.experimental.pallas import tpu as pltpu
from jax.sharding import PartitionSpec as P

HEADS = 32
SPAN = 64
FF = 7168
RANK = 32
DRANK = 64
LN_EPS = 1e-05
GN_EPS = 0.00064

F32 = jnp.float32
BF16 = jnp.bfloat16
HI = lax.Precision.HIGHEST


def nn(a, b):
    return jnp.dot(a, b, preferred_element_type=F32)


def nt(a, b):
    return lax.dot_general(a, b, (((1,), (1,)), ((), ())), preferred_element_type=F32)


def tn(a, b):
    return lax.dot_general(a, b, (((0,), (0,)), ((), ())), preferred_element_type=F32)


def knn(a, b):
    return lax.dot_general(
        a, b, (((1,), (0,)), ((), ())), preferred_element_type=F32
    )


def knt(a, b):
    return lax.dot_general(
        a, b, (((1,), (1,)), ((), ())), preferred_element_type=F32
    )


def ktn(a, b):
    return lax.dot_general(
        a, b, (((0,), (0,)), ((), ())), preferred_element_type=F32
    )


def low_lanes(shape):
    return lax.broadcasted_iota(jnp.int32, shape, len(shape) - 1) < SPAN


def head_sum(x):
    low = low_lanes(x.shape)
    s0 = jnp.sum(jnp.where(low, x, 0.0), axis=-1, keepdims=True)
    s1 = jnp.sum(jnp.where(low, 0.0, x), axis=-1, keepdims=True)
    return jnp.where(low, s0, s1)


def two_rows(x):
    low = low_lanes(x.shape)
    return jnp.concatenate([jnp.where(low, x, 0.0), jnp.where(low, 0.0, x)], axis=0)


def fold(full):
    return jnp.where(low_lanes((SPAN, 2 * SPAN)), full[:SPAN], full[SPAN:])


def unfold(state):
    low = low_lanes(state.shape)
    return jnp.concatenate([jnp.where(low, state, 0.0), jnp.where(low, 0.0, state)], axis=0)


def running(w, upper=False):
    count = w.shape[0]
    row = lax.broadcasted_iota(jnp.int32, (count, count), 0)
    col = lax.broadcasted_iota(jnp.int32, (count, count), 1)
    keep = (col >= row) if upper else (col <= row)
    return lax.dot_general(
        jnp.where(keep, 1.0, 0.0).astype(F32),
        w,
        (((1,), (0,)), ((), ())),
        precision=HI,
        preferred_element_type=F32,
    )


def strict(count):
    row = lax.broadcasted_iota(jnp.int32, (2 * count, count), 0)
    col = lax.broadcasted_iota(jnp.int32, (2 * count, count), 1)
    row = jnp.where(row >= count, row - count, row)
    return row > col, row == col


def affinity(r, k, u, q, ks):
    count = r.shape[0]
    below, diag = strict(count)
    raw = knt(two_rows(q), ks)
    share = jnp.sum(two_rows(r * u * k), axis=-1, keepdims=True)
    return jnp.where(below, raw, jnp.where(diag, share, 0.0))


def totals_kernel(k_ref, v_ref, w_ref, out_ref):
    cum = running(w_ref[...])
    total = cum[-1:, :]
    kc = k_ref[...] * jnp.exp(total - cum)
    out_ref[0, :SPAN, :] = fold(ktn(v_ref[...], kc))
    out_ref[0, SPAN:, :] = jnp.broadcast_to(jnp.exp(total), (8, 2 * SPAN))


def group_norm(y, gain, bias):
    centred = y - head_sum(y) * (1.0 / SPAN)
    spread = head_sum(centred * centred) * (1.0 / SPAN)
    scale = lax.rsqrt(spread + GN_EPS)
    normal = centred * scale
    return normal, scale, normal * gain + bias


def forward_kernel(r_ref, k_ref, v_ref, w_ref, g_ref, s_ref, p_ref, y_ref, gated_ref):
    r, k, v, w = r_ref[...], k_ref[...], v_ref[...], w_ref[...]
    cum = running(w)
    q = r * jnp.exp(cum - w)
    ks = k * jnp.exp(-cum)
    aff = affinity(r, k, p_ref[0:1, :], q, ks)
    count = r.shape[0]
    v2 = two_rows(v)
    y = (
        knt(q, unfold(s_ref[0]))
        + knn(aff[:count], v2[:count])
        + knn(aff[count:], v2[count:])
    )
    y_ref[...] = y
    gate = g_ref[...]
    _, _, grouped = group_norm(y, p_ref[1:2, :], p_ref[2:3, :])
    gated_ref[...] = (grouped * gate * jax.nn.sigmoid(gate)).astype(BF16)


def gate_kernel(gg_ref, g_ref, y_ref, r_ref, w_ref, p_ref, gate_ref, dy_ref, out_ref):
    gated_grad, gate, y = gg_ref[...], g_ref[...], y_ref[...]
    gain = p_ref[1:2, :]
    normal, scale, grouped = group_norm(y, gain, p_ref[2:3, :])
    sig = jax.nn.sigmoid(gate)
    gate_ref[...] = (gated_grad * grouped * sig * (1.0 + gate * (1.0 - sig))).astype(BF16)
    outer = gated_grad * gate * sig
    inner = outer * gain
    dy = scale * (
        inner
        - head_sum(inner) * (1.0 / SPAN)
        - normal * (head_sum(inner * normal) * (1.0 / SPAN))
    )
    dy_ref[...] = dy
    w = w_ref[...]
    q = r_ref[...] * jnp.exp(running(w) - w)
    out_ref[0, :SPAN, :] = fold(ktn(dy, q))
    gain_grad = jnp.sum(outer * normal, axis=0, keepdims=True)
    bias_grad = jnp.sum(outer, axis=0, keepdims=True)
    out_ref[0, SPAN:, :] = jnp.concatenate(
        [gain_grad, bias_grad, jnp.zeros((6, 2 * SPAN), F32)], axis=0
    )


def backward_kernel(
    r_ref, k_ref, v_ref, w_ref, dy_ref, s_ref, gs_ref, p_ref,
    dr_ref, dk_ref, dv_ref, dd_ref, out_ref,
):
    r, k, v, w, dy = r_ref[...], k_ref[...], v_ref[...], w_ref[...], dy_ref[...]
    u = p_ref[0:1, :]
    count = r.shape[0]
    cum = running(w)
    total = cum[-1:, :]
    e_before, e_minus, e_carry = jnp.exp(cum - w), jnp.exp(-cum), jnp.exp(total - cum)
    q, ks, kc = r * e_before, k * e_minus, k * e_carry
    aff = affinity(r, k, u, q, ks)
    below, _ = strict(count)
    dy2 = two_rows(dy)
    d_aff = jnp.where(below, knt(dy2, v), 0.0)
    own = head_sum(dy * v)
    state, grad_state = s_ref[0], gs_ref[0]
    state2, grad2 = unfold(state), unfold(grad_state)
    ks2 = two_rows(ks)
    dq = knn(dy, state2) + knn(d_aff[:count], ks2[:count]) + knn(d_aff[count:], ks2[count:])
    dks = ktn(d_aff, two_rows(q))
    dkc = knn(v, grad2)
    dv_ref[...] = (ktn(aff, dy2) + knt(kc, grad2)).astype(BF16)
    dr_ref[...] = (dq * e_before + own * u * k).astype(BF16)
    dk_ref[...] = (dks * e_minus + dkc * e_carry + own * u * r).astype(BF16)
    gq, gc = q * dq, kc * dkc
    d_total = jnp.sum(gc, axis=0, keepdims=True) + jnp.exp(total) * jnp.sum(
        state * grad_state, axis=0, keepdims=True
    )
    dw = running(gq - ks * dks - gc, upper=True) - gq + d_total
    term = dw * w
    dd_ref[...] = term.astype(BF16)
    out_ref[0] = jnp.concatenate(
        [
            jnp.sum(term, axis=0, keepdims=True),
            jnp.sum(own * r * k, axis=0, keepdims=True),
            jnp.zeros((6, 2 * SPAN), F32),
        ],
        axis=0,
    )


def block_call(kernel, chunks, step, width, ins, outs, args):
    lane = 2 * SPAN
    kinds = {
        "t": pl.BlockSpec((step, lane), lambda c, h: (c, h)),
        "s": pl.BlockSpec((1, SPAN, lane), lambda c, h: (c, 0, h)),
        "x": pl.BlockSpec((1, SPAN + 8, lane), lambda c, h: (c, 0, h)),
        "e": pl.BlockSpec((1, 8, lane), lambda c, h: (c, 0, h)),
        "p": pl.BlockSpec((8, lane), lambda c, h: (0, h)),
    }
    shapes = {
        "t": lambda d: jax.ShapeDtypeStruct((chunks * step, width), d),
        "x": lambda d: jax.ShapeDtypeStruct((chunks, SPAN + 8, width), d),
        "e": lambda d: jax.ShapeDtypeStruct((chunks, 8, width), d),
    }
    return pl.pallas_call(
        kernel,
        grid=(chunks, width // lane),
        in_specs=[kinds[kind] for kind in ins],
        out_specs=[kinds[kind] for kind, _ in outs],
        out_shape=[shapes[kind](dtype) for kind, dtype in outs],
        compiler_params=pltpu.CompilerParams(vmem_limit_bytes=48 * 1024 * 1024),
    )(*args)


def weight_grad_kernel(_, x_ref, y_ref, out_ref):
    out_ref[0] = lax.dot_general(
        x_ref[...], y_ref[...], (((0,), (0,)), ((), ())), preferred_element_type=F32
    ).astype(BF16)


def weight_grad(places, x, y, block, cut, cuts):
    tokens, columns = y.shape[0], y.shape[1] // cuts
    blocks = places.shape[0]
    return pl.pallas_call(
        weight_grad_kernel,
        grid_spec=pltpu.PrefetchScalarGridSpec(
            num_scalar_prefetch=1,
            grid=(blocks,),
            in_specs=[
                pl.BlockSpec((tokens, block), lambda i, at: (0, at[i])),
                pl.BlockSpec((tokens, columns), lambda i, at: (0, cut)),
            ],
            out_specs=pl.BlockSpec((1, block, columns), lambda i, at: (i, 0, 0)),
        ),
        out_shape=jax.ShapeDtypeStruct((blocks, block, columns), BF16),
        compiler_params=pltpu.CompilerParams(vmem_limit_bytes=48 * 1024 * 1024),
    )(places, x, y)


def lanes_kernel(spans, x_ref, out_ref):
    at = 0
    for start, stop in spans:
        out_ref[:, at : at + stop - start] = x_ref[:, start:stop].astype(out_ref.dtype)
        at += stop - start


def move_lanes(spans, value, dtype):
    return pl.pallas_call(
        functools.partial(lanes_kernel, spans),
        in_specs=[pl.BlockSpec(memory_space=pltpu.VMEM)],
        out_specs=pl.BlockSpec(memory_space=pltpu.VMEM),
        out_shape=jax.ShapeDtypeStruct(value.shape, dtype),
        compiler_params=pltpu.CompilerParams(vmem_limit_bytes=32 * 1024 * 1024),
    )(value)


def place_kernel(counts, at_ref, *refs):
    ins, out_ref, sems = refs[: len(counts)], refs[-2], refs[-1]
    block = out_ref.shape[0] // sum(counts)
    copies, i = [], 0
    for ref, n in zip(ins, counts):
        for j in range(n):
            start = pl.multiple_of(at_ref[i] * block, block)
            copy = pltpu.make_async_copy(
                ref.at[pl.ds(j * block, block), :],
                out_ref.at[pl.ds(start, block), :],
                sems.at[i],
            )
            copy.start()
            copies.append(copy)
            i += 1
    for copy in copies:
        copy.wait()


def place_rows(at, pieces, block):
    counts = [p.shape[0] // block for p in pieces]
    total = sum(counts)
    return pl.pallas_call(
        functools.partial(place_kernel, counts),
        in_specs=[pl.BlockSpec(memory_space=pltpu.SMEM)]
        + [pl.BlockSpec(memory_space=pl.ANY)] * len(pieces),
        out_specs=pl.BlockSpec(memory_space=pl.ANY),
        out_shape=jax.ShapeDtypeStruct((total * block, pieces[0].shape[1]), pieces[0].dtype),
        scratch_shapes=[pltpu.SemaphoreType.DMA((total,))],
        compiler_params=pltpu.CompilerParams(vmem_limit_bytes=32 * 1024 * 1024),
    )(at, *pieces)


def mixes_kernel(
    open_ref, x_ref, before_ref, vec_ref, down_ref, up_ref, ddown_ref,
    m1_ref, m2_ref, m3_ref, m4_ref, dh_ref,
    normal_ref, scale_ref, delta_ref, blend_ref, m0_ref, tanh_ref, dtanh_ref,
):
    piece = pl.program_id(0)
    step = m1_ref.shape[0]
    x = x_ref[...].astype(F32)
    centred = x - jnp.mean(x, axis=-1, keepdims=True)
    scale = lax.rsqrt(jnp.mean(centred * centred, axis=-1, keepdims=True) + LN_EPS)
    normal = centred * scale
    full = normal * vec_ref[0:1, :] + vec_ref[1:2, :]
    normed = full[:step]
    first = jnp.where(open_ref[piece] == 1, before_ref[0:1, :], full[step : step + 1])
    row = lax.broadcasted_iota(jnp.int32, normed.shape, 0)
    delta = jnp.where(row == 0, first, pltpu.roll(normed, 1, 0)) - normed
    blend = (normed + delta * vec_ref[2:3, :]).astype(BF16)
    tanh = jnp.tanh(nn(blend, down_ref[...]))
    latent = tanh.astype(BF16)
    lane = lax.broadcasted_iota(jnp.int32, latent.shape, 1)
    mixed = []
    for c in range(5):
        own = (lane >= c * RANK) & (lane < (c + 1) * RANK)
        offset = nt(jnp.where(own, latent, jnp.zeros_like(latent)), up_ref[...])
        mixed.append((normed + delta * (vec_ref[3 + c : 4 + c, :] + offset)).astype(BF16))
    dtanh = jnp.tanh(nn(mixed[0], ddown_ref[...]))
    m1_ref[...], m2_ref[...], m3_ref[...], m4_ref[...] = mixed[1:]
    dh_ref[...] = dtanh.astype(BF16)

    @pl.when(piece == 0)
    def _():
        normal_ref[...] = normal[:step]
        scale_ref[...] = jnp.broadcast_to(scale[:step], scale_ref.shape)
        delta_ref[...] = delta
        blend_ref[...] = blend
        m0_ref[...] = mixed[0]
        tanh_ref[...] = tanh
        dtanh_ref[...] = dtanh


def group_mixes(opening, x, before, vec, down, up, ddown, step):
    high, width = step + 16, x.shape[1]
    pieces = x.shape[0] // high

    def whole(value):
        return pl.BlockSpec(value.shape, lambda k: (0, 0))

    def own(columns, dtype):
        return (
            pl.BlockSpec((step, columns), lambda k: (0, 0)),
            jax.ShapeDtypeStruct((step, columns), dtype),
        )

    def every(columns, dtype):
        return (
            pl.BlockSpec((step, columns), lambda k: ((k % 2) * 2 + k // 2, 0)),
            jax.ShapeDtypeStruct((pieces * step, columns), dtype),
        )

    outs = [every(width, BF16)] * 4 + [
        every(DRANK, BF16),
        own(width, F32),
        own(128, F32),
        own(width, F32),
        own(width, BF16),
        own(width, BF16),
        own(5 * RANK, F32),
        own(DRANK, F32),
    ]
    return pl.pallas_call(
        mixes_kernel,
        grid=(pieces,),
        in_specs=[
            pl.BlockSpec(memory_space=pltpu.SMEM),
            pl.BlockSpec((high, width), lambda k: (k, 0)),
            whole(before),
            whole(vec),
            whole(down),
            whole(up),
            whole(ddown),
        ],
        out_specs=[o[0] for o in outs],
        out_shape=[o[1] for o in outs],
        compiler_params=pltpu.CompilerParams(vmem_limit_bytes=56 * 1024 * 1024),
    )(opening, x, before, vec, down, up, ddown)


def product(pairs, outs, body, sides=(), tile=256):
    count = len(pairs)

    def kernel(*refs):
        ins, out_refs = refs[: 2 * count + len(sides)], refs[2 * count + len(sides) :]
        products = [
            (nn if pair[2] == "nn" else nt)(ins[2 * i][...], ins[2 * i + 1][...])
            for i, pair in enumerate(pairs)
        ]
        results = body(*products, *[r[...] for r in ins[2 * count :]])
        for ref, value in zip(out_refs, results):
            ref[...] = value.astype(ref.dtype)

    specs, args = [], []
    for a, b, form, at in pairs:
        depth = a.shape[1]
        specs.append(pl.BlockSpec(a.shape, lambda j: (0, 0)))
        if form == "nn":
            specs.append(pl.BlockSpec((depth, tile), lambda j, at=at: (0, at + j)))
        else:
            specs.append(pl.BlockSpec((tile, depth), lambda j, at=at: (j, at)))
        args += [a, b]
    for side in sides:
        specs.append(pl.BlockSpec((side.shape[0], tile), lambda j: (0, j)))
    return pl.pallas_call(
        kernel,
        grid=(outs[0][1] // tile,),
        in_specs=specs,
        out_specs=[pl.BlockSpec((o[0], tile), lambda j: (0, j)) for o in outs],
        out_shape=[jax.ShapeDtypeStruct(o[:2], o[2]) for o in outs],
        compiler_params=pltpu.CompilerParams(vmem_limit_bytes=56 * 1024 * 1024),
    )(*args, *sides)


def local(fn, outs, *args, scalar=None):
    def kernel(*refs):
        lead = [] if scalar is None else [refs[0]]
        ins, out_refs = refs[len(lead) : -len(outs)], refs[-len(outs) :]
        results = fn(*[r[0] for r in lead], *[r[...] for r in ins])
        for ref, value in zip(out_refs, results):
            ref[...] = value.astype(ref.dtype)

    specs = [pl.BlockSpec(memory_space=pltpu.VMEM)] * len(args)
    if scalar is not None:
        specs = [pl.BlockSpec(memory_space=pltpu.SMEM)] + specs
        args = (scalar.reshape(1), *args)
    return pl.pallas_call(
        kernel,
        in_specs=specs,
        out_specs=[pl.BlockSpec(memory_space=pltpu.VMEM)] * len(outs),
        out_shape=[jax.ShapeDtypeStruct(o[:2], o[2]) for o in outs],
        compiler_params=pltpu.CompilerParams(vmem_limit_bytes=56 * 1024 * 1024),
    )(*args)


def take_lanes(value, spans):
    if len(spans) == 1:
        return value
    return jnp.concatenate([value[:, a:b] for a, b in spans], axis=1)


def norm_back(grad, gain, normal, scale):
    e = grad * gain
    return scale * (
        e
        - jnp.mean(e, axis=-1, keepdims=True)
        - normal * jnp.mean(e * normal, axis=-1, keepdims=True)
    )


def rows_above(value, first):
    row = lax.broadcasted_iota(jnp.int32, value.shape, 0)
    return jnp.where(row == 0, first, pltpu.roll(value, 1, 0))


def rows_below(value, last):
    row = lax.broadcasted_iota(jnp.int32, value.shape, 0)
    high = value.shape[0]
    return jnp.where(row == high - 1, last, pltpu.roll(value, high - 1, 0))


def padded(rows):
    return jnp.concatenate(
        list(rows) + [jnp.zeros((8 - len(rows), rows[0].shape[1]), F32)], axis=0
    )


def column_sum(value):
    return jnp.sum(value, axis=0, keepdims=True)


def gates_kernel(
    spans, who_ref, middle_ref, value_ref, more_ref, act_ref, cot_ref,
    out_ref, up_ref, vg_ref, rg_ref, held,
):
    to_spans, from_spans = spans
    step, part = act_ref.shape[0] // 4, act_ref.shape[1]
    who = who_ref[0]
    act = [
        act_ref[pl.ds(pl.multiple_of((who ^ j) * step, step), step), :] for j in range(4)
    ]
    recept = jax.nn.sigmoid(take_lanes(jnp.concatenate(act, axis=1).astype(F32), to_spans))
    value = value_ref[...] + more_ref[...].astype(F32)
    out = middle_ref[...] + recept * value
    out_ref[...] = take_lanes(out, from_spans).astype(BF16)
    up = take_lanes(cot_ref[...].astype(F32), to_spans)
    up_ref[...] = up
    vg_ref[...] = (up * recept).astype(BF16)
    held[...] = take_lanes(up * value * recept * (1.0 - recept), from_spans)
    for k in range(4):
        at = pl.multiple_of((who ^ k) * part, part)
        rg_ref[k * step : (k + 1) * step, :] = held[:, pl.ds(at, part)].astype(BF16)


def gates(spans, who, middle, value, more, act, cot):
    step, width = middle.shape
    part = act.shape[1]
    shape = jax.ShapeDtypeStruct
    return pl.pallas_call(
        functools.partial(gates_kernel, spans),
        in_specs=[pl.BlockSpec(memory_space=pltpu.SMEM)]
        + [pl.BlockSpec(memory_space=pltpu.VMEM)] * 5,
        out_specs=[pl.BlockSpec(memory_space=pltpu.VMEM)] * 4,
        out_shape=[
            shape((step, width), BF16),
            shape((step, width), F32),
            shape((step, width), BF16),
            shape((4 * step, part), BF16),
        ],
        scratch_shapes=[pltpu.VMEM((step, width), F32)],
        compiler_params=pltpu.CompilerParams(vmem_limit_bytes=56 * 1024 * 1024),
    )(who.reshape(1), middle, value, more, act, cot)


def mixes_back_kernel(
    kept_ref, got_ref, dl_ref, dl_more_ref, delta_ref, tanh_ref, dtanh_ref, blend_ref, m0_ref,
    down_ref, up_ref, ddown_ref, vec_ref,
    rest_ref, dg_ref, row_ref, cols_ref, down_out, up_out, ddown_out,
):
    step = delta_ref.shape[0]
    dtanh = dtanh_ref[...]
    decay_grad = dl_ref[...] + dl_more_ref[...].astype(F32)
    decay_pre = (decay_grad * (1.0 - dtanh * dtanh)).astype(BF16)
    ddown_out[...] = tn(m0_ref[...], decay_pre)
    tanh = tanh_ref[...]
    latent = tanh.astype(BF16)
    lane = lax.broadcasted_iota(jnp.int32, latent.shape, 1)
    delta, up = delta_ref[...], up_ref[...]
    latent_grad = jnp.zeros(latent.shape, F32)
    up_grad = jnp.zeros(up_out.shape, F32)
    dg = jnp.zeros(delta.shape, F32)
    total = jnp.zeros(delta.shape, F32)
    cols = []
    for c in range(5):
        own = (lane >= c * RANK) & (lane < (c + 1) * RANK)
        mine = jnp.where(own, latent, jnp.zeros_like(latent))
        if c == 0:
            grad = nt(decay_pre, ddown_ref[...])
        else:
            at = slice((c - 1) * step, c * step)
            grad = kept_ref[at, :] + got_ref[at, :].astype(F32)
        shift = grad * delta
        cols.append(column_sum(shift))
        offset = shift.astype(BF16)
        latent_grad = jnp.where(own, nn(offset, up), latent_grad)
        up_grad = up_grad + tn(offset, mine)
        dg = dg + grad * (vec_ref[3 + c : 4 + c, :] + nt(mine, up))
        total = total + grad
    up_out[...] = up_grad
    mix_pre = (latent_grad * (1.0 - tanh * tanh)).astype(BF16)
    down_out[...] = tn(blend_ref[...], mix_pre)
    blend_grad = nt(mix_pre, down_ref[...])
    dg = dg + blend_grad * vec_ref[2:3, :]
    rest_ref[...] = total + blend_grad - dg
    dg_ref[...] = dg
    row_ref[...] = dg[:8]
    cols_ref[...] = padded([column_sum(blend_grad * delta)] + cols)


def mixes_back(*args):
    delta, down, ddown = args[4], args[9], args[11]
    step, width = delta.shape
    shape = jax.ShapeDtypeStruct
    outs = [
        shape((step, width), F32),
        shape((step, width), F32),
        shape((8, width), F32),
        shape((8, width), F32),
        shape(down.shape, F32),
        shape(down.shape, F32),
        shape(ddown.shape, F32),
    ]
    return pl.pallas_call(
        mixes_back_kernel,
        in_specs=[pl.BlockSpec(memory_space=pltpu.VMEM)] * len(args),
        out_specs=[pl.BlockSpec(memory_space=pltpu.VMEM)] * len(outs),
        out_shape=outs,
        compiler_params=pltpu.CompilerParams(vmem_limit_bytes=60 * 1024 * 1024),
    )(*args)


def tie(*values):
    return lax.optimization_barrier(values)


def on_device(
    count,
    tokens,
    previous,
    initial_state,
    mixing_weights,
    lowrank_weights,
    vectors,
    feedforward_weights,
    cotangent,
):
    fast = initial_state.shape[0] == 64
    masks = (1, 8) if fast else (1, 2)
    size = 1 << len(masks)
    teams = count // size
    all_masks = [1 << b for b in range(count.bit_length() - 1)]
    team_masks = [b for b in all_masks if b not in masks]
    far = 16
    team_masks.sort(key=lambda b: fast and b != far)
    me = lax.axis_index("seq")
    _, step, width = tokens.shape
    rows = mixing_weights.shape[0]
    part = width // size
    ff_part = FF // size
    team_rows = rows * size
    def bit_of(who, mask):
        return (who // mask) % 2 if isinstance(who, int) else lax.rem(lax.div(who, mask), 2)

    def member_of(who):
        return sum(bit_of(who, b) << j for j, b in enumerate(masks))

    def team_of(who):
        return sum(bit_of(who, b) << j for j, b in enumerate(team_masks))

    member, team = member_of(me), team_of(me)
    order = sorted(range(count), key=lambda d: (team_of(d), member_of(d)))
    inverse = sorted(range(count), key=lambda p: order[p])
    across = [order[m::size] for m in range(size)]
    square = [order[m :: 2 * size] for m in range(2 * size)]
    def lane_spans(blocks):
        spans = []
        for d in blocks:
            if spans and spans[-1][1] == d * rows:
                spans[-1][1] = (d + 1) * rows
            else:
                spans.append([d * rows, (d + 1) * rows])
        return spans

    to_spans, from_spans = lane_spans(order), lane_spans(inverse)

    def to_places(value, dtype):
        return move_lanes(to_spans, value, dtype)

    def flips(k):
        return sum(b for j, b in enumerate(masks) if (k >> j) & 1)

    def trade(value, mask):
        return lax.ppermute(value, "seq", [(d, d ^ mask) for d in range(count)])

    def group_gather(value):
        side = trade(value, masks[1])
        return value, side, trade(jnp.concatenate([value, side], axis=0), masks[0])

    def group_rows(value):
        high, columns = value.shape

        def lay(own, side, far):
            return (jnp.concatenate([own, far[:high], side, far[high:]], axis=0),)

        return local(lay, [(size * high, columns, value.dtype)], *group_gather(value))[0]

    def halves(value):
        cut = [value[k * step : (k + 1) * step] for k in range(size)]
        return [cut[0], cut[2]], [cut[1], cut[3]]

    def group_sum(kept, sent):
        high, columns = kept.shape[0] // 2, kept.shape[1]
        got = trade(sent, masks[0])

        def add(mine, more):
            total = mine + more.astype(F32)
            return total[:high], total[high:]

        mine, side = local(add, [(high, columns, F32), (high, columns, BF16)], kept, got)
        return mine, trade(side, masks[1])

    def crossing_sum(*pairs):
        units = len(pairs)

        def body(*products):
            parts = [halves(p) for p in products]
            kept = [p[0][i] for i in range(2) for p in parts]
            sent = [p[1][i] for i in range(2) for p in parts]
            return jnp.concatenate(kept, axis=0), jnp.concatenate(sent, axis=0)

        high = 2 * units * step
        return product(
            [(a, b, "nt", at) for a, b, at in pairs],
            [(high, width, F32), (high, width, BF16)],
            body,
        )

    def exchange(pieces):
        pieces, high = list(pieces), pieces[0].shape[0]
        for j in reversed(range(len(masks))):
            keys = [k for k in range(size) if (k >> j) & 1]
            got = trade(jnp.concatenate([pieces[k] for k in keys], axis=0), masks[j])
            for i, k in enumerate(keys):
                pieces[k] = got[i * high : (i + 1) * high]
        return pieces

    def ordered(pieces):
        pieces = list(pieces)
        for j in range(len(masks)):
            swap = lax.rem(lax.div(member, 1 << j), 2) == 1
            pieces = [
                jnp.where(swap, pieces[k ^ (1 << j)], pieces[k]) for k in range(len(pieces))
            ]
        return pieces

    def neighbour(value, offset):
        pairs = [(d, d + offset) for d in range(count) if 0 <= d + offset < count]
        return lax.ppermute(value, "seq", pairs)

    def take_columns(value, spans, who):
        return jnp.concatenate(
            [
                lax.dynamic_slice_in_dim(value, start + who * wide, wide, axis=1)
                for start, wide in spans
            ],
            axis=1,
        )

    def group_columns(value, spans):
        pieces = [take_columns(value, spans, member ^ k) for k in range(size)]
        return jnp.concatenate(ordered(exchange(pieces)), axis=0)

    def crossing(first):
        bits = list(range(1, len(team_masks))) + [0]
        if first:
            bits[0], bits[1] = bits[1], bits[0]
        return bits

    def gather_rows(own):
        return lax.all_gather(own, "seq", axis=0, tiled=True, axis_index_groups=across)

    def square_sum(x, y):
        if not fast:
            return TeamSum(x, y, False).finish()
        places = jnp.arange(teams, dtype=jnp.int32)
        grads = weight_grad(places, x, y, team_rows, 0, 1).reshape(width, -1)
        pair = lax.psum_scatter(
            grads, "seq", scatter_dimension=0, tiled=True, axis_index_groups=square
        )
        bit = bit_of(me, far)
        sent = lax.dynamic_slice_in_dim(pair, (1 - bit) * team_rows, team_rows, axis=0)
        kept = lax.dynamic_slice_in_dim(pair, bit * team_rows, team_rows, axis=0)
        return (kept.astype(F32) + trade(sent, far).astype(F32)).astype(BF16)

    first_steps = []

    def cube_gather(value):
        for mask in reversed(all_masks):
            got = trade(value, mask)
            upper = bit_of(me, mask) == 1
            value = jnp.stack([jnp.where(upper, got, value), jnp.where(upper, value, got)])
            if mask == 8:
                first_steps.append(value)
        axes = len(all_masks)
        return value.transpose(*reversed(range(axes)), *range(axes, value.ndim))

    place_axes = [all_masks[::-1].index(b) for b in team_masks[::-1] + list(masks[::-1])]

    def by_place(cube):
        rest = range(len(all_masks), cube.ndim)
        return cube.transpose(*place_axes, *rest).reshape(width, -1)

    def to_cube(value):
        cube = value.reshape(*[2] * len(place_axes), rows, -1)
        back = [place_axes.index(a) for a in range(len(place_axes))]
        return cube.transpose(*back, len(back), len(back) + 1)

    def cube_sum(cube, kind):
        for axis, mask in reversed(list(enumerate(reversed(all_masks)))):
            bit = bit_of(me, mask)
            sent = lax.dynamic_index_in_dim(cube, 1 - bit, axis, keepdims=False)
            kept = lax.dynamic_index_in_dim(cube, bit, axis, keepdims=False)
            cube = kept.astype(F32) + trade(sent.astype(kind), mask).astype(F32)
        return cube

    class TeamSum:
        last = {}

        def __init__(self, x, y, first, cut=0, cuts=1):
            self.bits = crossing(first)
            self.args = (x, y, team_rows, cut, cuts)
            self.stage = 0
            places = [0]
            for b in reversed(self.bits):
                places = places + [p | (1 << b) for p in places]
            self.half = teams // 2
            self.places = jnp.bitwise_xor(jnp.asarray(places, jnp.int32), team)
            self.kept = self.got = None
            if fast:
                self.sent = weight_grad(self.places[self.half :], *self.args)
            else:
                self.sent = tn(x, y).astype(BF16)

        def step(self):
            if not fast or not self.bits:
                return
            key = (self.bits[0], self.stage)
            if key in TeamSum.last:
                self.sent = tie(self.sent, TeamSum.last[key])[0]
            got = trade(self.sent, team_masks[self.bits[0]])
            TeamSum.last[key] = got
            kept = self.kept
            if kept is None:
                kept = weight_grad(self.places[: self.half], *self.args)
            self.bits = self.bits[1:]
            self.stage += 1
            self.half //= 2
            h = self.half
            if h:
                self.sent = (kept[h:].astype(F32) + got[h:].astype(F32)).astype(BF16)
                self.kept = (kept[:h].astype(F32) + got[:h].astype(F32)).astype(BF16)
            else:
                self.sent = (kept[0].astype(F32) + got[0].astype(F32)).astype(BF16)

        def finish(self):
            if not fast:
                return lax.psum_scatter(
                    self.sent,
                    "seq",
                    scatter_dimension=0,
                    tiled=True,
                    axis_index_groups=across,
                )
            while self.bits:
                self.step()
            return self.sent

    def hand_rows(pieces):
        widths = [sum(p.shape[1] for p in piece) for piece in pieces]
        joint = jnp.concatenate([p for piece in pieces for p in piece], axis=1)
        mine = [
            lax.dynamic_slice_in_dim(joint, (member ^ k) * rows, rows, axis=0)
            for k in range(size)
        ]
        by_member = ordered(exchange(mine))
        outs, start = [], 0
        for wide in widths:
            outs += [p[:, start : start + wide] for p in by_member]
            start += wide
        return jnp.concatenate(outs, axis=1).astype(F32)

    up_start, decay_start, decay_up = 5 * RANK, 10 * RANK, 10 * RANK + DRANK
    last_row = neighbour(tokens[0, -1:, :], 1)
    tokens_sent = to_places(
        jnp.concatenate([tokens[0], jnp.broadcast_to(last_row, (16, width))], axis=0), BF16
    )
    natural = cube_gather(
        jnp.concatenate(
            [vectors, initial_state, lowrank_weights[:, decay_up:].astype(F32)], axis=1
        )
    ).reshape(width, -1)
    low_cube = cube_gather(lowrank_weights[:, :decay_up])
    lowrank = by_place(low_cube)
    tokens_all = jnp.concatenate(group_gather(tokens_sent), axis=0)
    mix_in = tie(mixing_weights, *first_steps)[0]
    mix_local = group_columns(mix_in, [(c * width, part) for c in range(5)])
    feed_in = tie(feedforward_weights, mix_local, tokens_all, natural)[0]
    ff_spans = [(FF, part), (0, ff_part), (FF + width, ff_part)]
    ff_local = group_columns(feed_in, ff_spans)
    w_kv = gather_rows(mix_local[:, : 2 * part])
    w_rest = gather_rows(mix_local[:, 2 * part :])
    w_rec = gather_rows(ff_local[:, :part])
    w_key = gather_rows(ff_local[:, part : part + ff_part])
    w_val = gather_rows(ff_local[:, part + ff_part :])
    tiles = part // 256

    mine = lax.dynamic_slice_in_dim(natural, member * part, part, axis=0)
    vec_part = mine[:, :16].T
    first_state = mine[:, 16 : 16 + SPAN].T
    w_dup = mine[:, 16 + SPAN :].astype(BF16)
    vec = by_place(
        natural[:, :16].reshape(*[2] * len(all_masks), rows, 16)
    ).T
    wkv_rows = jnp.concatenate([vec_part[9:12], jnp.zeros((5, part), F32)], axis=0)
    is_first = (me == 0).astype(jnp.int32)
    before = to_places(previous.reshape(2, width), F32)
    w_down, w_up = lowrank[:, :up_start], lowrank[:, up_start:decay_start]
    w_ddown = lowrank[:, decay_start:]

    opening = jnp.stack(
        [jnp.bitwise_xor(me, flips(k)) == 0 for k in (0, 2, 1, 3)]
    ).astype(jnp.int32)
    (
        *mixed_all, dh_all, normal_one, scale_one, delta, blend, mixed_zero, mix_tanh, decay_tanh,
    ) = group_mixes(opening, tokens_all, before, vec, w_down, w_up, w_ddown, step)
    everyone = size * step
    (log_decay,) = product(
        [(dh_all, w_dup, "nt", 0)],
        [(everyone, part, F32)],
        lambda acc, base: (-jnp.exp(base + acc),),
        sides=(vec_part[8:9],),
    )
    keys, values = product(
        [(mixed_all[0], w_kv, "nn", 0), (mixed_all[1], w_kv, "nn", tiles)],
        [(everyone, part, F32)] * 2,
        lambda a, b: (a, b),
    )

    call = functools.partial(block_call, chunks=size, step=step, width=part)
    (totals,) = call(
        totals_kernel, ins="ttt", outs=[("x", F32)], args=(keys, values, log_decay)
    )
    by_member = ordered([totals[k] for k in range(size)])
    total = {m: (p[SPAN : SPAN + 1], p[:SPAN]) for m, p in enumerate(by_member)}
    before_chunk = [
        (jnp.ones((1, part), F32), jnp.zeros((SPAN, part), F32)) for _ in range(size)
    ]
    open_bits = size - 1
    levels = []

    def chain(early, late):
        return early[0] * late[0], late[0] * early[1] + late[1]

    def pick(flag, yes, no):
        return tuple(jnp.where(flag, a, b) for a, b in zip(yes, no))

    for mask in all_masks:
        if mask in masks:
            bit = 1 << masks.index(mask)
            levels.append({g: total[g][0] for g in total})
            for m in range(size):
                if m & bit:
                    early = (m & open_bits) ^ bit
                    before_chunk[m] = chain(total[early], before_chunk[m])
            total = {g: chain(total[g], total[g | bit]) for g in total if not g & bit}
            open_bits ^= bit
        else:
            groups = list(total)
            sent = jnp.concatenate(
                [
                    jnp.concatenate(
                        [total[g][1], jnp.broadcast_to(total[g][0], (8, part))], axis=0
                    )
                    for g in groups
                ],
                axis=0,
            )
            got = trade(sent, mask)
            high = SPAN + 8
            other = {
                g: (got[i * high + SPAN : i * high + SPAN + 1], got[i * high : i * high + SPAN])
                for i, g in enumerate(groups)
            }
            levels.append({g: (total[g][0], other[g][0]) for g in groups})
            late = bit_of(me, mask) == 1
            for m in range(size):
                g = m & open_bits
                before_chunk[m] = pick(late, chain(other[g], before_chunk[m]), before_chunk[m])
            total = {
                g: pick(late, chain(other[g], total[g]), chain(total[g], other[g]))
                for g in groups
            }
    state_in = jnp.stack(ordered([d * first_state + s for d, s in before_chunk]))

    receipt, gate_pre = product(
        [(mixed_all[2], w_rest, "nn", 0), (mixed_all[3], w_rest, "nn", tiles)],
        [(everyone, part, F32)] * 2,
        lambda a, b: (a, b),
    )
    wkv, gated = call(
        forward_kernel,
        ins="tttttsp",
        outs=[("t", F32), ("t", BF16)],
        args=(receipt, keys, values, log_decay, gate_pre, state_in, wkv_rows),
    )
    branch, branch_more = group_sum(*crossing_sum((gated, w_rest, 2)))

    def norm_two(hidden, mine, more, vec):
        middle = hidden[:step].astype(F32) + mine + more.astype(F32)
        centred = middle - jnp.mean(middle, axis=-1, keepdims=True)
        scale = lax.rsqrt(jnp.mean(centred * centred, axis=-1, keepdims=True) + LN_EPS)
        normal = centred * scale
        tail = normal[step - 8 :] * vec[12:13] + vec[13:14]
        return middle, normal, jnp.broadcast_to(scale, (step, 128)), tail

    whole = (step, width, F32)
    middle, normal_two, scale_two, tail_two = local(
        norm_two,
        [whole, whole, (step, 128, F32), (8, width, F32)],
        tokens_sent,
        branch,
        branch_more,
        vec,
    )

    def mix_two(first, normal, arrived, before, vec):
        normed = normal * vec[12:13] + vec[13:14]
        above = jnp.where(first == 1, before[1:2], arrived[7:8])
        delta = rows_above(normed, above) - normed
        key_in, recv_in = normed + delta * vec[14:15], normed + delta * vec[15:16]
        return jnp.concatenate([key_in, recv_in], axis=0), delta

    both, delta_two = local(
        mix_two,
        [(2 * step, width, BF16), whole],
        normal_two,
        neighbour(tail_two, 1),
        before,
        vec,
        scalar=is_first,
    )

    def lay_both(own, side, far):
        parts = [own, far[: 2 * step], side, far[2 * step :]]
        return [
            jnp.concatenate([p[i * step : (i + 1) * step] for p in parts], axis=0)
            for i in range(2)
        ]

    key_all, recv_all = local(
        lay_both, [(everyone, width, BF16)] * 2, *group_gather(both)
    )
    relu, squared = product(
        [(key_all, w_key, "nn", 0)],
        [(everyone, ff_part, F32), (everyone, ff_part, BF16)],
        lambda acc: (jnp.maximum(acc, 0.0), jnp.square(jnp.maximum(acc, 0.0))),
    )
    (recept_act,) = product(
        [(recv_all, w_rec, "nn", 0)],
        [(everyone, part, BF16)],
        lambda acc: (acc,),
    )
    acts = exchange([recept_act[k * step : (k + 1) * step] for k in range(size)])
    value, value_more = group_sum(*crossing_sum((squared, w_val, 0)))
    block_output, upstream, value_grad, recept_grads = gates(
        (to_spans, from_spans),
        member,
        middle,
        value,
        value_more,
        jnp.concatenate(acts, axis=0),
        cotangent.reshape(step, width),
    )

    rg_all = jnp.concatenate(
        exchange([recept_grads[k * step : (k + 1) * step] for k in range(size)]), axis=0
    )
    vg_all = group_rows(value_grad)
    val_sum = square_sum(vg_all, squared)
    (key_grad,) = product(
        [(vg_all, w_val, "nn", 0)],
        [(everyone, ff_part, BF16)],
        lambda acc, relu: (acc * (2.0 * relu),),
        sides=(relu,),
    )
    key_sum = square_sum(key_all, key_grad)
    mine_two, more_two = group_sum(*crossing_sum((key_grad, w_key, 0), (rg_all, w_rec, 0)))

    def inputs_back(mine, more, vec):
        grads = mine + more.astype(F32)
        top = grads[:8] * vec[14:15] + grads[step : step + 8] * vec[15:16]
        return grads, top

    in_grads, top_two = local(
        inputs_back, [(2 * step, width, F32), (8, width, F32)], mine_two, more_two, vec
    )
    last_flag = (me == count - 1).astype(jnp.int32)

    def norm_two_back(last, grads, arrived, upstream, normal, scale, delta, vec):
        key_grad, recv_grad = grads[:step], grads[step:]
        shifted = key_grad * vec[14:15] + recv_grad * vec[15:16]
        below = jnp.where(last == 1, jnp.zeros_like(arrived[:1]), arrived[:1])
        grad = (
            key_grad * (1.0 - vec[14:15])
            + recv_grad * (1.0 - vec[15:16])
            + rows_below(shifted, below)
        )
        out = upstream + norm_back(grad, vec[12:13], normal, scale[:, :1])
        cols = padded(
            [
                column_sum(grad * normal),
                column_sum(grad),
                column_sum(key_grad * delta),
                column_sum(recv_grad * delta),
            ]
        )
        return out, out, cols

    middle_grad, branch_grad, cols_two = local(
        norm_two_back,
        [whole, (step, width, BF16), (8, width, F32)],
        in_grads,
        neighbour(top_two, -1),
        upstream,
        normal_two,
        scale_two,
        delta_two,
        vec,
        scalar=last_flag,
    )

    bg_all = group_rows(branch_grad)
    (gated_grad,) = product(
        [(bg_all, w_rest, "nn", 2 * tiles)], [(everyone, part, F32)], lambda acc: (acc,)
    )
    gate_grad, wkv_grad, ends = call(
        gate_kernel,
        ins="tttttp",
        outs=[("t", BF16), ("t", F32), ("x", F32)],
        args=(gated_grad, gate_pre, wkv, receipt, log_decay, wkv_rows),
    )
    grad_total = dict(enumerate(ordered([ends[k, :SPAN] for k in range(size)])))
    after = [(jnp.ones((1, part), F32), jnp.zeros((SPAN, part), F32)) for _ in range(size)]
    open_bits = size - 1
    for mask, level in zip(all_masks, levels):
        if mask in masks:
            bit = 1 << masks.index(mask)
            for m in range(size):
                if not m & bit:
                    late = (m & open_bits) | bit
                    d, s = after[m]
                    after[m] = (d * level[late], d * grad_total[late] + s)
            grad_total = {
                g: grad_total[g] + level[g] * grad_total[g | bit]
                for g in grad_total
                if not g & bit
            }
            open_bits ^= bit
        else:
            groups = list(grad_total)
            got = trade(jnp.concatenate([grad_total[g] for g in groups], axis=0), mask)
            other = {g: got[i * SPAN : (i + 1) * SPAN] for i, g in enumerate(groups)}
            early = bit_of(me, mask) == 0
            for m in range(size):
                g = m & open_bits
                d, s = after[m]
                after[m] = pick(early, (d * level[g][1], d * other[g] + s), (d, s))
            grad_total = {
                g: jnp.where(
                    early,
                    grad_total[g] + level[g][0] * other[g],
                    other[g] + level[g][1] * grad_total[g],
                )
                for g in groups
            }
    grad_out = jnp.stack(ordered([s for _, s in after]))
    first_grad = grad_total[0]
    holder = lax.div(me * rows, part)

    def rows_of(who):
        return lax.dynamic_slice_in_dim(first_grad, lax.rem(who * rows, part), rows, axis=1)

    handed = exchange([rows_of(jnp.bitwise_xor(me, flips(k))) for k in range(size)])
    state_rows = handed[0]
    for k in range(1, size):
        state_rows = jnp.where(holder == (member ^ k), handed[k], state_rows)
    initial_state_gradient = state_rows.T

    d_receipt, d_keys, d_values, d_decay, extra = call(
        backward_kernel,
        ins="tttttssp",
        outs=[("t", BF16)] * 4 + [("e", F32)],
        args=(receipt, keys, values, log_decay, wkv_grad, state_in, grad_out, wkv_rows),
    )
    grads = [d_keys, d_values, d_receipt, gate_grad]
    kept, sent = crossing_sum(
        (grads[0], w_kv, 0), (grads[1], w_kv, 1), (grads[2], w_rest, 0), (grads[3], w_rest, 1)
    )
    mixed_mine, mixed_more = group_sum(kept, sent)

    def latent_back(grad, up):
        kept, sent = halves(nn(grad, up))
        return jnp.concatenate(kept, axis=0), jnp.concatenate(sent, axis=0)

    latent_mine, latent_more = group_sum(
        *local(
            latent_back, [(2 * step, DRANK, F32), (2 * step, DRANK, BF16)], d_decay, w_dup
        )
    )
    rest_grad, delta_grad, top_one, cols_mix, down_grad, up_grad, ddown_grad = mixes_back(
        mixed_mine,
        mixed_more,
        latent_mine,
        latent_more,
        delta,
        mix_tanh,
        decay_tanh,
        blend,
        mixed_zero,
        w_down,
        w_up,
        w_ddown,
        vec,
    )
    def norm_one_back(last, rest, shifted, arrived, normal, scale, middle, vec):
        below = jnp.where(last == 1, jnp.zeros_like(arrived[:1]), arrived[:1])
        grad = rest + rows_below(shifted, below)
        out = middle + norm_back(grad, vec[0:1], normal, scale[:, :1])
        cols = padded([column_sum(grad * normal), column_sum(grad)])
        return take_lanes(out, from_spans), cols

    block_input_gradient, cols_one = local(
        norm_one_back,
        [whole, (8, width, F32)],
        rest_grad,
        delta_grad,
        neighbour(top_one, -1),
        normal_one,
        scale_one,
        middle_grad,
        vec,
        scalar=last_flag,
    )
    sums = [
        TeamSum(bg_all, gated, True),
        TeamSum(recv_all, rg_all, False),
        TeamSum(mixed_all[3], gate_grad, True),
        TeamSum(mixed_all[1], d_values, False),
        TeamSum(mixed_all[0], d_keys, True),
        TeamSum(mixed_all[2], d_receipt, False),
    ]
    for _ in team_masks:
        for each in sums:
            each.step()
    out_sum, rec_sum, gate_sum, values_sum, keys_sum, receipt_sum = [e.finish() for e in sums]
    feedforward_gradient = hand_rows([[key_sum], [rec_sum], [val_sum]])
    mixing_gradient = hand_rows(
        [[keys_sum], [values_sum], [receipt_sum], [gate_sum], [out_sum]]
    )


    def spread(value):
        zero = jnp.zeros((width, value.shape[1]), F32)
        return lax.dynamic_update_slice_in_dim(zero, value, member * part, axis=0)

    vec_low = jnp.concatenate([cols_one[:2], cols_mix[:6], cols_two[:4]], axis=0)
    vec_head = jnp.concatenate(
        [jnp.sum(extra[:, :2], axis=0), jnp.sum(ends[:, SPAN : SPAN + 2], axis=0)], axis=0
    )
    by_feature = jnp.concatenate([down_grad, up_grad, ddown_grad, vec_low.T], axis=1)
    low = cube_sum(to_cube(by_feature), BF16)
    by_channel = spread(jnp.concatenate([tn(d_decay, dh_all), vec_head.T], axis=1))
    high_part = cube_sum(by_channel.reshape(*[2] * len(all_masks), rows, -1), F32)
    lowrank_gradient = jnp.concatenate([low[:, :decay_up], high_part[:, :DRANK]], axis=1)
    vectors_gradient = jnp.concatenate(
        [low[:, decay_up : decay_up + 8], high_part[:, DRANK:], low[:, decay_up + 8 :]], axis=1
    )
    return (
        block_output.reshape(1, step, width),
        block_input_gradient.reshape(1, step, width),
        initial_state_gradient,
        mixing_gradient,
        lowrank_gradient,
        vectors_gradient,
        feedforward_gradient,
    )


def solution(mesh):
    rowwise = P("seq", None)
    tokenwise = P(None, "seq", None)
    return jax.shard_map(
        functools.partial(on_device, mesh.shape["seq"]),
        mesh=mesh,
        in_specs=(tokenwise, P(), rowwise, rowwise, rowwise, rowwise, rowwise, tokenwise),
        out_specs=(tokenwise, tokenwise, rowwise, rowwise, rowwise, rowwise, rowwise),
        check_vma=False,
    )
```

```python
import functools

import jax
import jax.numpy as jnp
from jax import lax
from jax.experimental import pallas as pl
from jax.experimental.pallas import tpu as pltpu
from jax.sharding import PartitionSpec as P

HEADS = 32
SPAN = 64
FF = 7168
RANK = 32
DRANK = 64
LN_EPS = 1e-05
GN_EPS = 0.00064

F32 = jnp.float32
BF16 = jnp.bfloat16
HI = lax.Precision.HIGHEST


def nn(a, b):
    return jnp.dot(a, b, preferred_element_type=F32)


def nt(a, b):
    return lax.dot_general(a, b, (((1,), (1,)), ((), ())), preferred_element_type=F32)


def tn(a, b):
    return lax.dot_general(a, b, (((0,), (0,)), ((), ())), preferred_element_type=F32)


def knn(a, b):
    return lax.dot_general(
        a, b, (((1,), (0,)), ((), ())), preferred_element_type=F32
    )


def knt(a, b):
    return lax.dot_general(
        a, b, (((1,), (1,)), ((), ())), preferred_element_type=F32
    )


def ktn(a, b):
    return lax.dot_general(
        a, b, (((0,), (0,)), ((), ())), preferred_element_type=F32
    )


def low_lanes(shape):
    return lax.broadcasted_iota(jnp.int32, shape, len(shape) - 1) < SPAN


def head_sum(x):
    low = low_lanes(x.shape)
    s0 = jnp.sum(jnp.where(low, x, 0.0), axis=-1, keepdims=True)
    s1 = jnp.sum(jnp.where(low, 0.0, x), axis=-1, keepdims=True)
    return jnp.where(low, s0, s1)


def two_rows(x):
    low = low_lanes(x.shape)
    return jnp.concatenate([jnp.where(low, x, 0.0), jnp.where(low, 0.0, x)], axis=0)


def fold(full):
    return jnp.where(low_lanes((SPAN, 2 * SPAN)), full[:SPAN], full[SPAN:])


def unfold(state):
    low = low_lanes(state.shape)
    return jnp.concatenate([jnp.where(low, state, 0.0), jnp.where(low, 0.0, state)], axis=0)


def running(w, upper=False):
    count = w.shape[0]
    row = lax.broadcasted_iota(jnp.int32, (count, count), 0)
    col = lax.broadcasted_iota(jnp.int32, (count, count), 1)
    keep = (col >= row) if upper else (col <= row)
    return lax.dot_general(
        jnp.where(keep, 1.0, 0.0).astype(F32),
        w,
        (((1,), (0,)), ((), ())),
        precision=HI,
        preferred_element_type=F32,
    )


def strict(count):
    row = lax.broadcasted_iota(jnp.int32, (2 * count, count), 0)
    col = lax.broadcasted_iota(jnp.int32, (2 * count, count), 1)
    row = jnp.where(row >= count, row - count, row)
    return row > col, row == col


def affinity(r, k, u, q, ks):
    count = r.shape[0]
    below, diag = strict(count)
    raw = knt(two_rows(q), ks)
    share = jnp.sum(two_rows(r * u * k), axis=-1, keepdims=True)
    return jnp.where(below, raw, jnp.where(diag, share, 0.0))


def totals_kernel(k_ref, v_ref, w_ref, out_ref):
    cum = running(w_ref[...])
    total = cum[-1:, :]
    kc = k_ref[...] * jnp.exp(total - cum)
    out_ref[0, :SPAN, :] = fold(ktn(v_ref[...], kc))
    out_ref[0, SPAN:, :] = jnp.broadcast_to(jnp.exp(total), (8, 2 * SPAN))


def group_norm(y, gain, bias):
    centred = y - head_sum(y) * (1.0 / SPAN)
    spread = head_sum(centred * centred) * (1.0 / SPAN)
    scale = lax.rsqrt(spread + GN_EPS)
    normal = centred * scale
    return normal, scale, normal * gain + bias


def forward_kernel(r_ref, k_ref, v_ref, w_ref, g_ref, s_ref, p_ref, y_ref, gated_ref):
    r, k, v, w = r_ref[...], k_ref[...], v_ref[...], w_ref[...]
    cum = running(w)
    q = r * jnp.exp(cum - w)
    ks = k * jnp.exp(-cum)
    aff = affinity(r, k, p_ref[0:1, :], q, ks)
    count = r.shape[0]
    v2 = two_rows(v)
    y = (
        knt(q, unfold(s_ref[0]))
        + knn(aff[:count], v2[:count])
        + knn(aff[count:], v2[count:])
    )
    y_ref[...] = y
    gate = g_ref[...]
    _, _, grouped = group_norm(y, p_ref[1:2, :], p_ref[2:3, :])
    gated_ref[...] = (grouped * gate * jax.nn.sigmoid(gate)).astype(BF16)


def gate_kernel(gg_ref, g_ref, y_ref, r_ref, w_ref, p_ref, gate_ref, dy_ref, out_ref):
    gated_grad, gate, y = gg_ref[...], g_ref[...], y_ref[...]
    gain = p_ref[1:2, :]
    normal, scale, grouped = group_norm(y, gain, p_ref[2:3, :])
    sig = jax.nn.sigmoid(gate)
    gate_ref[...] = (gated_grad * grouped * sig * (1.0 + gate * (1.0 - sig))).astype(BF16)
    outer = gated_grad * gate * sig
    inner = outer * gain
    dy = scale * (
        inner
        - head_sum(inner) * (1.0 / SPAN)
        - normal * (head_sum(inner * normal) * (1.0 / SPAN))
    )
    dy_ref[...] = dy
    w = w_ref[...]
    q = r_ref[...] * jnp.exp(running(w) - w)
    out_ref[0, :SPAN, :] = fold(ktn(dy, q))
    gain_grad = jnp.sum(outer * normal, axis=0, keepdims=True)
    bias_grad = jnp.sum(outer, axis=0, keepdims=True)
    out_ref[0, SPAN:, :] = jnp.concatenate(
        [gain_grad, bias_grad, jnp.zeros((6, 2 * SPAN), F32)], axis=0
    )


def backward_kernel(
    r_ref, k_ref, v_ref, w_ref, dy_ref, s_ref, gs_ref, p_ref,
    dr_ref, dk_ref, dv_ref, dd_ref, out_ref,
):
    r, k, v, w, dy = r_ref[...], k_ref[...], v_ref[...], w_ref[...], dy_ref[...]
    u = p_ref[0:1, :]
    count = r.shape[0]
    cum = running(w)
    total = cum[-1:, :]
    e_before, e_minus, e_carry = jnp.exp(cum - w), jnp.exp(-cum), jnp.exp(total - cum)
    q, ks, kc = r * e_before, k * e_minus, k * e_carry
    aff = affinity(r, k, u, q, ks)
    below, _ = strict(count)
    dy2 = two_rows(dy)
    d_aff = jnp.where(below, knt(dy2, v), 0.0)
    own = head_sum(dy * v)
    state, grad_state = s_ref[0], gs_ref[0]
    state2, grad2 = unfold(state), unfold(grad_state)
    ks2 = two_rows(ks)
    dq = knn(dy, state2) + knn(d_aff[:count], ks2[:count]) + knn(d_aff[count:], ks2[count:])
    dks = ktn(d_aff, two_rows(q))
    dkc = knn(v, grad2)
    dv_ref[...] = (ktn(aff, dy2) + knt(kc, grad2)).astype(BF16)
    dr_ref[...] = (dq * e_before + own * u * k).astype(BF16)
    dk_ref[...] = (dks * e_minus + dkc * e_carry + own * u * r).astype(BF16)
    gq, gc = q * dq, kc * dkc
    d_total = jnp.sum(gc, axis=0, keepdims=True) + jnp.exp(total) * jnp.sum(
        state * grad_state, axis=0, keepdims=True
    )
    dw = running(gq - ks * dks - gc, upper=True) - gq + d_total
    term = dw * w
    dd_ref[...] = term.astype(BF16)
    out_ref[0] = jnp.concatenate(
        [
            jnp.sum(term, axis=0, keepdims=True),
            jnp.sum(own * r * k, axis=0, keepdims=True),
            jnp.zeros((6, 2 * SPAN), F32),
        ],
        axis=0,
    )


def block_call(kernel, chunks, step, width, ins, outs, args):
    lane = 2 * SPAN
    kinds = {
        "t": pl.BlockSpec((step, lane), lambda c, h: (c, h)),
        "s": pl.BlockSpec((1, SPAN, lane), lambda c, h: (c, 0, h)),
        "x": pl.BlockSpec((1, SPAN + 8, lane), lambda c, h: (c, 0, h)),
        "e": pl.BlockSpec((1, 8, lane), lambda c, h: (c, 0, h)),
        "p": pl.BlockSpec((8, lane), lambda c, h: (0, h)),
    }
    shapes = {
        "t": lambda d: jax.ShapeDtypeStruct((chunks * step, width), d),
        "x": lambda d: jax.ShapeDtypeStruct((chunks, SPAN + 8, width), d),
        "e": lambda d: jax.ShapeDtypeStruct((chunks, 8, width), d),
    }
    return pl.pallas_call(
        kernel,
        grid=(chunks, width // lane),
        in_specs=[kinds[kind] for kind in ins],
        out_specs=[kinds[kind] for kind, _ in outs],
        out_shape=[shapes[kind](dtype) for kind, dtype in outs],
        compiler_params=pltpu.CompilerParams(vmem_limit_bytes=48 * 1024 * 1024),
    )(*args)


def weight_grad(places, pairs, block):
    tokens, blocks = pairs[0][0].shape[0], places.shape[0]
    widths = [y.shape[1] for _, y in pairs]

    def kernel(_, *refs):
        at = 0
        for i, wide in enumerate(widths):
            refs[-1][0, :, at : at + wide] = tn(refs[2 * i][...], refs[2 * i + 1][...]).astype(
                BF16
            )
            at += wide

    specs = []
    for wide in widths:
        specs.append(pl.BlockSpec((tokens, block), lambda i, at: (0, at[i])))
        specs.append(pl.BlockSpec((tokens, wide), lambda i, at: (0, 0)))
    return pl.pallas_call(
        kernel,
        grid_spec=pltpu.PrefetchScalarGridSpec(
            num_scalar_prefetch=1,
            grid=(blocks,),
            in_specs=specs,
            out_specs=pl.BlockSpec((1, block, sum(widths)), lambda i, at: (i, 0, 0)),
        ),
        out_shape=jax.ShapeDtypeStruct((blocks, block, sum(widths)), BF16),
        compiler_params=pltpu.CompilerParams(vmem_limit_bytes=48 * 1024 * 1024),
    )(places, *[v for pair in pairs for v in pair])


def lanes_kernel(spans, x_ref, out_ref):
    at = 0
    for start, stop in spans:
        out_ref[:, at : at + stop - start] = x_ref[:, start:stop].astype(out_ref.dtype)
        at += stop - start


def move_lanes(spans, value, dtype):
    return pl.pallas_call(
        functools.partial(lanes_kernel, spans),
        in_specs=[pl.BlockSpec(memory_space=pltpu.VMEM)],
        out_specs=pl.BlockSpec(memory_space=pltpu.VMEM),
        out_shape=jax.ShapeDtypeStruct(value.shape, dtype),
        compiler_params=pltpu.CompilerParams(vmem_limit_bytes=32 * 1024 * 1024),
    )(value)


def place_kernel(counts, at_ref, *refs):
    ins, out_ref, sems = refs[: len(counts)], refs[-2], refs[-1]
    block = out_ref.shape[0] // sum(counts)
    copies, i = [], 0
    for ref, n in zip(ins, counts):
        for j in range(n):
            start = pl.multiple_of(at_ref[i] * block, block)
            copy = pltpu.make_async_copy(
                ref.at[pl.ds(j * block, block), :],
                out_ref.at[pl.ds(start, block), :],
                sems.at[i],
            )
            copy.start()
            copies.append(copy)
            i += 1
    for copy in copies:
        copy.wait()


def place_rows(at, pieces, block):
    counts = [p.shape[0] // block for p in pieces]
    total = sum(counts)
    return pl.pallas_call(
        functools.partial(place_kernel, counts),
        in_specs=[pl.BlockSpec(memory_space=pltpu.SMEM)]
        + [pl.BlockSpec(memory_space=pl.ANY)] * len(pieces),
        out_specs=pl.BlockSpec(memory_space=pl.ANY),
        out_shape=jax.ShapeDtypeStruct((total * block, pieces[0].shape[1]), pieces[0].dtype),
        scratch_shapes=[pltpu.SemaphoreType.DMA((total,))],
        compiler_params=pltpu.CompilerParams(vmem_limit_bytes=32 * 1024 * 1024),
    )(at, *pieces)


def mixes_kernel(
    open_ref, x_ref, before_ref, vec_ref, down_ref, up_ref, ddown_ref,
    m1_ref, m2_ref, m3_ref, m4_ref, dh_ref,
    normal_ref, scale_ref, delta_ref, blend_ref, m0_ref, tanh_ref, dtanh_ref,
):
    piece = pl.program_id(0)
    step = m1_ref.shape[0]
    x = x_ref[...].astype(F32)
    centred = x - jnp.mean(x, axis=-1, keepdims=True)
    scale = lax.rsqrt(jnp.mean(centred * centred, axis=-1, keepdims=True) + LN_EPS)
    normal = centred * scale
    full = normal * vec_ref[0:1, :] + vec_ref[1:2, :]
    normed = full[:step]
    first = jnp.where(open_ref[piece] == 1, before_ref[0:1, :], full[step : step + 1])
    row = lax.broadcasted_iota(jnp.int32, normed.shape, 0)
    delta = jnp.where(row == 0, first, pltpu.roll(normed, 1, 0)) - normed
    blend = (normed + delta * vec_ref[2:3, :]).astype(BF16)
    tanh = jnp.tanh(nn(blend, down_ref[...]))
    latent = tanh.astype(BF16)
    lane = lax.broadcasted_iota(jnp.int32, latent.shape, 1)
    mixed = []
    for c in range(5):
        own = (lane >= c * RANK) & (lane < (c + 1) * RANK)
        offset = nt(jnp.where(own, latent, jnp.zeros_like(latent)), up_ref[...])
        mixed.append((normed + delta * (vec_ref[3 + c : 4 + c, :] + offset)).astype(BF16))
    dtanh = jnp.tanh(nn(mixed[0], ddown_ref[...]))
    m1_ref[...], m2_ref[...], m3_ref[...], m4_ref[...] = mixed[1:]
    dh_ref[...] = dtanh.astype(BF16)

    @pl.when(piece == 0)
    def _():
        normal_ref[...] = normal[:step]
        scale_ref[...] = jnp.broadcast_to(scale[:step], scale_ref.shape)
        delta_ref[...] = delta
        blend_ref[...] = blend
        m0_ref[...] = mixed[0]
        tanh_ref[...] = tanh
        dtanh_ref[...] = dtanh


def group_mixes(opening, x, before, vec, down, up, ddown, step):
    high, width = step + 16, x.shape[1]
    pieces = x.shape[0] // high

    def whole(value):
        return pl.BlockSpec(value.shape, lambda k: (0, 0))

    def own(columns, dtype):
        return (
            pl.BlockSpec((step, columns), lambda k: (0, 0)),
            jax.ShapeDtypeStruct((step, columns), dtype),
        )

    def every(columns, dtype):
        return (
            pl.BlockSpec((step, columns), lambda k: ((k % 2) * 2 + k // 2, 0)),
            jax.ShapeDtypeStruct((pieces * step, columns), dtype),
        )

    outs = [every(width, BF16)] * 4 + [
        every(DRANK, BF16),
        own(width, F32),
        own(128, F32),
        own(width, F32),
        own(width, BF16),
        own(width, BF16),
        own(5 * RANK, F32),
        own(DRANK, F32),
    ]
    return pl.pallas_call(
        mixes_kernel,
        grid=(pieces,),
        in_specs=[
            pl.BlockSpec(memory_space=pltpu.SMEM),
            pl.BlockSpec((high, width), lambda k: (k, 0)),
            whole(before),
            whole(vec),
            whole(down),
            whole(up),
            whole(ddown),
        ],
        out_specs=[o[0] for o in outs],
        out_shape=[o[1] for o in outs],
        compiler_params=pltpu.CompilerParams(vmem_limit_bytes=56 * 1024 * 1024),
    )(opening, x, before, vec, down, up, ddown)


def product(pairs, outs, body, sides=(), tile=256):
    count = len(pairs)

    def kernel(*refs):
        ins, out_refs = refs[: 2 * count + len(sides)], refs[2 * count + len(sides) :]
        products = [
            (nn if pair[2] == "nn" else nt)(ins[2 * i][...], ins[2 * i + 1][...])
            for i, pair in enumerate(pairs)
        ]
        results = body(*products, *[r[...] for r in ins[2 * count :]])
        for ref, value in zip(out_refs, results):
            ref[...] = value.astype(ref.dtype)

    specs, args = [], []
    for a, b, form, at in pairs:
        depth = a.shape[1]
        specs.append(pl.BlockSpec(a.shape, lambda j: (0, 0)))
        if form == "nn":
            specs.append(pl.BlockSpec((depth, tile), lambda j, at=at: (0, at + j)))
        else:
            specs.append(pl.BlockSpec((tile, depth), lambda j, at=at: (j, at)))
        args += [a, b]
    for side in sides:
        specs.append(pl.BlockSpec((side.shape[0], tile), lambda j: (0, j)))
    return pl.pallas_call(
        kernel,
        grid=(outs[0][1] // tile,),
        in_specs=specs,
        out_specs=[pl.BlockSpec((o[0], tile), lambda j: (0, j)) for o in outs],
        out_shape=[jax.ShapeDtypeStruct(o[:2], o[2]) for o in outs],
        compiler_params=pltpu.CompilerParams(vmem_limit_bytes=56 * 1024 * 1024),
    )(*args, *sides)


def local(fn, outs, *args, scalar=None):
    def kernel(*refs):
        lead = [] if scalar is None else [refs[0]]
        ins, out_refs = refs[len(lead) : -len(outs)], refs[-len(outs) :]
        results = fn(*[r[0] for r in lead], *[r[...] for r in ins])
        for ref, value in zip(out_refs, results):
            ref[...] = value.astype(ref.dtype)

    specs = [pl.BlockSpec(memory_space=pltpu.VMEM)] * len(args)
    if scalar is not None:
        specs = [pl.BlockSpec(memory_space=pltpu.SMEM)] + specs
        args = (scalar.reshape(1), *args)
    return pl.pallas_call(
        kernel,
        in_specs=specs,
        out_specs=[pl.BlockSpec(memory_space=pltpu.VMEM)] * len(outs),
        out_shape=[jax.ShapeDtypeStruct(o[:2], o[2]) for o in outs],
        compiler_params=pltpu.CompilerParams(vmem_limit_bytes=56 * 1024 * 1024),
    )(*args)


def take_lanes(value, spans):
    if len(spans) == 1:
        return value
    return jnp.concatenate([value[:, a:b] for a, b in spans], axis=1)


def norm_back(grad, gain, normal, scale):
    e = grad * gain
    return scale * (
        e
        - jnp.mean(e, axis=-1, keepdims=True)
        - normal * jnp.mean(e * normal, axis=-1, keepdims=True)
    )


def rows_above(value, first):
    row = lax.broadcasted_iota(jnp.int32, value.shape, 0)
    return jnp.where(row == 0, first, pltpu.roll(value, 1, 0))


def rows_below(value, last):
    row = lax.broadcasted_iota(jnp.int32, value.shape, 0)
    high = value.shape[0]
    return jnp.where(row == high - 1, last, pltpu.roll(value, high - 1, 0))


def padded(rows):
    return jnp.concatenate(
        list(rows) + [jnp.zeros((8 - len(rows), rows[0].shape[1]), F32)], axis=0
    )


def column_sum(value):
    return jnp.sum(value, axis=0, keepdims=True)


def gates_kernel(
    spans, who_ref, middle_ref, value_ref, more_ref, act_ref, cot_ref,
    out_ref, up_ref, vg_ref, rg_ref, held,
):
    to_spans, from_spans = spans
    step, part = act_ref.shape[0] // 4, act_ref.shape[1]
    who = who_ref[0]
    act = [
        act_ref[pl.ds(pl.multiple_of((who ^ j) * step, step), step), :] for j in range(4)
    ]
    recept = jax.nn.sigmoid(take_lanes(jnp.concatenate(act, axis=1).astype(F32), to_spans))
    value = value_ref[...] + more_ref[...].astype(F32)
    out = middle_ref[...] + recept * value
    out_ref[...] = take_lanes(out, from_spans).astype(BF16)
    up = take_lanes(cot_ref[...].astype(F32), to_spans)
    up_ref[...] = up
    vg_ref[...] = (up * recept).astype(BF16)
    held[...] = take_lanes(up * value * recept * (1.0 - recept), from_spans)
    for k in range(4):
        at = pl.multiple_of((who ^ k) * part, part)
        rg_ref[k * step : (k + 1) * step, :] = held[:, pl.ds(at, part)].astype(BF16)


def gates(spans, who, middle, value, more, act, cot):
    step, width = middle.shape
    part = act.shape[1]
    shape = jax.ShapeDtypeStruct
    return pl.pallas_call(
        functools.partial(gates_kernel, spans),
        in_specs=[pl.BlockSpec(memory_space=pltpu.SMEM)]
        + [pl.BlockSpec(memory_space=pltpu.VMEM)] * 5,
        out_specs=[pl.BlockSpec(memory_space=pltpu.VMEM)] * 4,
        out_shape=[
            shape((step, width), BF16),
            shape((step, width), F32),
            shape((step, width), BF16),
            shape((4 * step, part), BF16),
        ],
        scratch_shapes=[pltpu.VMEM((step, width), F32)],
        compiler_params=pltpu.CompilerParams(vmem_limit_bytes=56 * 1024 * 1024),
    )(who.reshape(1), middle, value, more, act, cot)


def mixes_back_kernel(
    kept_ref, got_ref, dl_ref, dl_more_ref, delta_ref, tanh_ref, dtanh_ref, blend_ref, m0_ref,
    down_ref, up_ref, ddown_ref, vec_ref,
    rest_ref, dg_ref, row_ref, cols_ref, down_out, up_out, ddown_out,
):
    step = delta_ref.shape[0]
    dtanh = dtanh_ref[...]
    decay_grad = dl_ref[...] + dl_more_ref[...].astype(F32)
    decay_pre = (decay_grad * (1.0 - dtanh * dtanh)).astype(BF16)
    ddown_out[...] = tn(m0_ref[...], decay_pre)
    tanh = tanh_ref[...]
    latent = tanh.astype(BF16)
    lane = lax.broadcasted_iota(jnp.int32, latent.shape, 1)
    delta, up = delta_ref[...], up_ref[...]
    latent_grad = jnp.zeros(latent.shape, F32)
    up_grad = jnp.zeros(up_out.shape, F32)
    dg = jnp.zeros(delta.shape, F32)
    total = jnp.zeros(delta.shape, F32)
    cols = []
    for c in range(5):
        own = (lane >= c * RANK) & (lane < (c + 1) * RANK)
        mine = jnp.where(own, latent, jnp.zeros_like(latent))
        if c == 0:
            grad = nt(decay_pre, ddown_ref[...])
        else:
            at = slice((c - 1) * step, c * step)
            grad = kept_ref[at, :] + got_ref[at, :].astype(F32)
        shift = grad * delta
        cols.append(column_sum(shift))
        offset = shift.astype(BF16)
        latent_grad = jnp.where(own, nn(offset, up), latent_grad)
        up_grad = up_grad + tn(offset, mine)
        dg = dg + grad * (vec_ref[3 + c : 4 + c, :] + nt(mine, up))
        total = total + grad
    up_out[...] = up_grad
    mix_pre = (latent_grad * (1.0 - tanh * tanh)).astype(BF16)
    down_out[...] = tn(blend_ref[...], mix_pre)
    blend_grad = nt(mix_pre, down_ref[...])
    dg = dg + blend_grad * vec_ref[2:3, :]
    rest_ref[...] = total + blend_grad - dg
    dg_ref[...] = dg
    row_ref[...] = dg[:8]
    cols_ref[...] = padded([column_sum(blend_grad * delta)] + cols)


def mixes_back(*args):
    delta, down, ddown = args[4], args[9], args[11]
    step, width = delta.shape
    shape = jax.ShapeDtypeStruct
    outs = [
        shape((step, width), F32),
        shape((step, width), F32),
        shape((8, width), F32),
        shape((8, width), F32),
        shape(down.shape, F32),
        shape(down.shape, F32),
        shape(ddown.shape, F32),
    ]
    return pl.pallas_call(
        mixes_back_kernel,
        in_specs=[pl.BlockSpec(memory_space=pltpu.VMEM)] * len(args),
        out_specs=[pl.BlockSpec(memory_space=pltpu.VMEM)] * len(outs),
        out_shape=outs,
        compiler_params=pltpu.CompilerParams(vmem_limit_bytes=60 * 1024 * 1024),
    )(*args)


def tie(*values):
    return lax.optimization_barrier(values)


def on_device(
    count,
    tokens,
    previous,
    initial_state,
    mixing_weights,
    lowrank_weights,
    vectors,
    feedforward_weights,
    cotangent,
):
    fast = initial_state.shape[0] == 64
    masks = (1, 8) if fast else (1, 2)
    size = 1 << len(masks)
    teams = count // size
    all_masks = [1 << b for b in range(count.bit_length() - 1)]
    team_masks = [b for b in all_masks if b not in masks]
    far = 16
    team_masks.sort(key=lambda b: fast and b != far)
    me = lax.axis_index("seq")
    _, step, width = tokens.shape
    rows = mixing_weights.shape[0]
    part = width // size
    ff_part = FF // size
    team_rows = rows * size
    def bit_of(who, mask):
        return (who // mask) % 2 if isinstance(who, int) else lax.rem(lax.div(who, mask), 2)

    def member_of(who):
        return sum(bit_of(who, b) << j for j, b in enumerate(masks))

    def team_of(who):
        return sum(bit_of(who, b) << j for j, b in enumerate(team_masks))

    member, team = member_of(me), team_of(me)
    order = sorted(range(count), key=lambda d: (team_of(d), member_of(d)))
    inverse = sorted(range(count), key=lambda p: order[p])
    across = [order[m::size] for m in range(size)]
    square = [order[m :: 2 * size] for m in range(2 * size)]
    def lane_spans(blocks):
        spans = []
        for d in blocks:
            if spans and spans[-1][1] == d * rows:
                spans[-1][1] = (d + 1) * rows
            else:
                spans.append([d * rows, (d + 1) * rows])
        return spans

    to_spans, from_spans = lane_spans(order), lane_spans(inverse)

    def to_places(value, dtype):
        return move_lanes(to_spans, value, dtype)

    def flips(k):
        return sum(b for j, b in enumerate(masks) if (k >> j) & 1)

    def trade(value, mask):
        return lax.ppermute(value, "seq", [(d, d ^ mask) for d in range(count)])

    def group_gather(value):
        side = trade(value, masks[1])
        return value, side, trade(jnp.concatenate([value, side], axis=0), masks[0])

    def group_rows(value):
        high, columns = value.shape

        def lay(own, side, far):
            return (jnp.concatenate([own, far[:high], side, far[high:]], axis=0),)

        return local(lay, [(size * high, columns, value.dtype)], *group_gather(value))[0]

    def halves(value):
        cut = [value[k * step : (k + 1) * step] for k in range(size)]
        return [cut[0], cut[2]], [cut[1], cut[3]]

    def group_sum(kept, sent):
        high, columns = kept.shape[0] // 2, kept.shape[1]
        got = trade(sent, masks[0])

        def add(mine, more):
            total = mine + more.astype(F32)
            return total[:high], total[high:]

        mine, side = local(add, [(high, columns, F32), (high, columns, BF16)], kept, got)
        return mine, trade(side, masks[1])

    def crossing_sum(*pairs):
        units = len(pairs)

        def body(*products):
            parts = [halves(p) for p in products]
            kept = [p[0][i] for i in range(2) for p in parts]
            sent = [p[1][i] for i in range(2) for p in parts]
            return jnp.concatenate(kept, axis=0), jnp.concatenate(sent, axis=0)

        high = 2 * units * step
        return product(
            [(a, b, "nt", at) for a, b, at in pairs],
            [(high, width, F32), (high, width, BF16)],
            body,
        )

    def exchange(pieces):
        pieces, high = list(pieces), pieces[0].shape[0]
        for j in reversed(range(len(masks))):
            keys = [k for k in range(size) if (k >> j) & 1]
            got = trade(jnp.concatenate([pieces[k] for k in keys], axis=0), masks[j])
            for i, k in enumerate(keys):
                pieces[k] = got[i * high : (i + 1) * high]
        return pieces

    def ordered(pieces):
        pieces = list(pieces)
        for j in range(len(masks)):
            swap = lax.rem(lax.div(member, 1 << j), 2) == 1
            pieces = [
                jnp.where(swap, pieces[k ^ (1 << j)], pieces[k]) for k in range(len(pieces))
            ]
        return pieces

    def neighbour(value, offset):
        pairs = [(d, d + offset) for d in range(count) if 0 <= d + offset < count]
        return lax.ppermute(value, "seq", pairs)

    def take_columns(value, spans, who):
        return jnp.concatenate(
            [
                lax.dynamic_slice_in_dim(value, start + who * wide, wide, axis=1)
                for start, wide in spans
            ],
            axis=1,
        )

    def group_columns(value, spans):
        pieces = [take_columns(value, spans, member ^ k) for k in range(size)]
        return jnp.concatenate(ordered(exchange(pieces)), axis=0)

    def crossing(first):
        bits = list(range(1, len(team_masks))) + [0]
        if first:
            bits[0], bits[1] = bits[1], bits[0]
        return bits

    def gather_rows(own):
        return lax.all_gather(own, "seq", axis=0, tiled=True, axis_index_groups=across)

    def far_pair(own):
        if not fast:
            return own
        got = trade(own, far)
        upper = bit_of(me, far) == 1
        return jnp.concatenate(
            [jnp.where(upper, got, own), jnp.where(upper, own, got)], axis=0
        )

    def gather_square(paired):
        groups = square if fast else across
        return lax.all_gather(paired, "seq", axis=0, tiled=True, axis_index_groups=groups)

    def team_products(*pairs):
        if fast:
            places = jnp.arange(teams, dtype=jnp.int32)
            return weight_grad(places, pairs, team_rows).reshape(width, -1)
        return jnp.concatenate([tn(x, y).astype(BF16) for x, y in pairs], axis=1)

    def square_sum(grads):
        groups = square if fast else across
        return lax.psum_scatter(
            grads, "seq", scatter_dimension=0, tiled=True, axis_index_groups=groups
        )

    def far_sum(pair):
        if not fast:
            return pair
        bit = bit_of(me, far)
        sent = lax.dynamic_slice_in_dim(pair, (1 - bit) * team_rows, team_rows, axis=0)
        kept = lax.dynamic_slice_in_dim(pair, bit * team_rows, team_rows, axis=0)
        return (kept.astype(F32) + trade(sent, far).astype(F32)).astype(BF16)

    first_steps = []

    def cube_gather(value):
        for mask in reversed(all_masks):
            got = trade(value, mask)
            upper = bit_of(me, mask) == 1
            value = jnp.stack([jnp.where(upper, got, value), jnp.where(upper, value, got)])
            if mask == 8:
                first_steps.append(value)
        axes = len(all_masks)
        return value.transpose(*reversed(range(axes)), *range(axes, value.ndim))

    place_axes = [all_masks[::-1].index(b) for b in team_masks[::-1] + list(masks[::-1])]

    def by_place(cube):
        rest = range(len(all_masks), cube.ndim)
        return cube.transpose(*place_axes, *rest).reshape(width, -1)

    def to_cube(value):
        cube = value.reshape(*[2] * len(place_axes), rows, -1)
        back = [place_axes.index(a) for a in range(len(place_axes))]
        return cube.transpose(*back, len(back), len(back) + 1)

    def cube_sum(cube, kind):
        for axis, mask in reversed(list(enumerate(reversed(all_masks)))):
            bit = bit_of(me, mask)
            sent = lax.dynamic_index_in_dim(cube, 1 - bit, axis, keepdims=False)
            kept = lax.dynamic_index_in_dim(cube, bit, axis, keepdims=False)
            cube = kept.astype(F32) + trade(sent.astype(kind), mask).astype(F32)
        return cube

    class TeamSum:
        last = {}

        def __init__(self, x, y, first):
            self.bits = crossing(first)
            self.args = ([(x, y)], team_rows)
            self.stage = 0
            places = [0]
            for b in reversed(self.bits):
                places = places + [p | (1 << b) for p in places]
            self.half = teams // 2
            self.places = jnp.bitwise_xor(jnp.asarray(places, jnp.int32), team)
            self.kept = self.got = None
            if fast:
                self.sent = weight_grad(self.places[self.half :], *self.args)
            else:
                self.sent = tn(x, y).astype(BF16)

        def step(self):
            if not fast or not self.bits:
                return
            key = (self.bits[0], self.stage)
            if key in TeamSum.last:
                self.sent = tie(self.sent, TeamSum.last[key])[0]
            got = trade(self.sent, team_masks[self.bits[0]])
            TeamSum.last[key] = got
            kept = self.kept
            if kept is None:
                kept = weight_grad(self.places[: self.half], *self.args)
            self.bits = self.bits[1:]
            self.stage += 1
            self.half //= 2
            h = self.half
            if h:
                self.sent = (kept[h:].astype(F32) + got[h:].astype(F32)).astype(BF16)
                self.kept = (kept[:h].astype(F32) + got[:h].astype(F32)).astype(BF16)
            else:
                self.sent = (kept[0].astype(F32) + got[0].astype(F32)).astype(BF16)

        def finish(self):
            if not fast:
                return lax.psum_scatter(
                    self.sent,
                    "seq",
                    scatter_dimension=0,
                    tiled=True,
                    axis_index_groups=across,
                )
            while self.bits:
                self.step()
            return self.sent

    def hand_rows(pieces):
        widths = [sum(p.shape[1] for p in piece) for piece in pieces]
        joint = jnp.concatenate([p for piece in pieces for p in piece], axis=1)
        mine = [
            lax.dynamic_slice_in_dim(joint, (member ^ k) * rows, rows, axis=0)
            for k in range(size)
        ]
        by_member = ordered(exchange(mine))
        outs, start = [], 0
        for wide in widths:
            outs += [p[:, start : start + wide] for p in by_member]
            start += wide
        return jnp.concatenate(outs, axis=1).astype(F32)

    up_start, decay_start, decay_up = 5 * RANK, 10 * RANK, 10 * RANK + DRANK
    last_row = neighbour(tokens[0, -1:, :], 1)
    tokens_sent = to_places(
        jnp.concatenate([tokens[0], jnp.broadcast_to(last_row, (16, width))], axis=0), BF16
    )
    natural = cube_gather(
        jnp.concatenate(
            [vectors, initial_state, lowrank_weights[:, decay_up:].astype(F32)], axis=1
        )
    ).reshape(width, -1)
    low_cube = cube_gather(lowrank_weights[:, :decay_up])
    lowrank = by_place(low_cube)
    tokens_all = jnp.concatenate(group_gather(tokens_sent), axis=0)
    mix_in = tie(mixing_weights, *first_steps)[0]
    mix_local = group_columns(mix_in, [(c * width, part) for c in range(5)])
    feed_in = tie(feedforward_weights, mix_local, tokens_all, natural, low_cube)[0]
    ff_spans = [(0, ff_part), (FF, part), (FF + width, ff_part)]
    ff_local = group_columns(feed_in, ff_spans)
    near_pair = far_pair(ff_local[:, : ff_part + part])
    ff_tail = tie(ff_local[:, ff_part + part :], near_pair)[0]
    w_mix = gather_rows(mix_local)
    w_near = gather_square(near_pair)
    w_key, w_rec = w_near, w_near[:, ff_part:]
    w_val = gather_square(far_pair(ff_tail))
    tiles = part // 256

    mine = lax.dynamic_slice_in_dim(natural, member * part, part, axis=0)
    vec_part = mine[:, :16].T
    first_state = mine[:, 16 : 16 + SPAN].T
    w_dup = mine[:, 16 + SPAN :].astype(BF16)
    vec = by_place(
        natural[:, :16].reshape(*[2] * len(all_masks), rows, 16)
    ).T
    wkv_rows = jnp.concatenate([vec_part[9:12], jnp.zeros((5, part), F32)], axis=0)
    is_first = (me == 0).astype(jnp.int32)
    before = to_places(previous.reshape(2, width), F32)
    w_down, w_up = lowrank[:, :up_start], lowrank[:, up_start:decay_start]
    w_ddown = lowrank[:, decay_start:]

    opening = jnp.stack(
        [jnp.bitwise_xor(me, flips(k)) == 0 for k in (0, 2, 1, 3)]
    ).astype(jnp.int32)
    (
        *mixed_all, dh_all, normal_one, scale_one, delta, blend, mixed_zero, mix_tanh, decay_tanh,
    ) = group_mixes(opening, tokens_all, before, vec, w_down, w_up, w_ddown, step)
    everyone = size * step
    (log_decay,) = product(
        [(dh_all, w_dup, "nt", 0)],
        [(everyone, part, F32)],
        lambda acc, base: (-jnp.exp(base + acc),),
        sides=(vec_part[8:9],),
    )
    keys, values = product(
        [(mixed_all[0], w_mix, "nn", 0), (mixed_all[1], w_mix, "nn", tiles)],
        [(everyone, part, F32)] * 2,
        lambda a, b: (a, b),
    )

    call = functools.partial(block_call, chunks=size, step=step, width=part)
    (totals,) = call(
        totals_kernel, ins="ttt", outs=[("x", F32)], args=(keys, values, log_decay)
    )
    by_member = ordered([totals[k] for k in range(size)])
    total = {m: (p[SPAN : SPAN + 1], p[:SPAN]) for m, p in enumerate(by_member)}
    before_chunk = [
        (jnp.ones((1, part), F32), jnp.zeros((SPAN, part), F32)) for _ in range(size)
    ]
    open_bits = size - 1
    levels = []

    def chain(early, late):
        return early[0] * late[0], late[0] * early[1] + late[1]

    def pick(flag, yes, no):
        return tuple(jnp.where(flag, a, b) for a, b in zip(yes, no))

    for mask in all_masks:
        if mask in masks:
            bit = 1 << masks.index(mask)
            levels.append({g: total[g][0] for g in total})
            for m in range(size):
                if m & bit:
                    early = (m & open_bits) ^ bit
                    before_chunk[m] = chain(total[early], before_chunk[m])
            total = {g: chain(total[g], total[g | bit]) for g in total if not g & bit}
            open_bits ^= bit
        else:
            groups = list(total)
            sent = jnp.concatenate(
                [
                    jnp.concatenate(
                        [total[g][1], jnp.broadcast_to(total[g][0], (8, part))], axis=0
                    )
                    for g in groups
                ],
                axis=0,
            )
            got = trade(sent, mask)
            high = SPAN + 8
            other = {
                g: (got[i * high + SPAN : i * high + SPAN + 1], got[i * high : i * high + SPAN])
                for i, g in enumerate(groups)
            }
            levels.append({g: (total[g][0], other[g][0]) for g in groups})
            late = bit_of(me, mask) == 1
            for m in range(size):
                g = m & open_bits
                before_chunk[m] = pick(late, chain(other[g], before_chunk[m]), before_chunk[m])
            total = {
                g: pick(late, chain(other[g], total[g]), chain(total[g], other[g]))
                for g in groups
            }
    state_in = jnp.stack(ordered([d * first_state + s for d, s in before_chunk]))

    receipt, gate_pre = product(
        [(mixed_all[2], w_mix, "nn", 2 * tiles), (mixed_all[3], w_mix, "nn", 3 * tiles)],
        [(everyone, part, F32)] * 2,
        lambda a, b: (a, b),
    )
    wkv, gated = call(
        forward_kernel,
        ins="tttttsp",
        outs=[("t", F32), ("t", BF16)],
        args=(receipt, keys, values, log_decay, gate_pre, state_in, wkv_rows),
    )
    branch, branch_more = group_sum(*crossing_sum((gated, w_mix, 4)))

    def norm_two(hidden, mine, more, vec):
        middle = hidden[:step].astype(F32) + mine + more.astype(F32)
        centred = middle - jnp.mean(middle, axis=-1, keepdims=True)
        scale = lax.rsqrt(jnp.mean(centred * centred, axis=-1, keepdims=True) + LN_EPS)
        normal = centred * scale
        tail = normal[step - 8 :] * vec[12:13] + vec[13:14]
        return middle, normal, jnp.broadcast_to(scale, (step, 128)), tail

    whole = (step, width, F32)
    middle, normal_two, scale_two, tail_two = local(
        norm_two,
        [whole, whole, (step, 128, F32), (8, width, F32)],
        tokens_sent,
        branch,
        branch_more,
        vec,
    )

    def mix_two(first, normal, arrived, before, vec):
        normed = normal * vec[12:13] + vec[13:14]
        above = jnp.where(first == 1, before[1:2], arrived[7:8])
        delta = rows_above(normed, above) - normed
        key_in, recv_in = normed + delta * vec[14:15], normed + delta * vec[15:16]
        return jnp.concatenate([key_in, recv_in], axis=0), delta

    both, delta_two = local(
        mix_two,
        [(2 * step, width, BF16), whole],
        normal_two,
        neighbour(tail_two, 1),
        before,
        vec,
        scalar=is_first,
    )

    def lay_both(own, side, far):
        parts = [own, far[: 2 * step], side, far[2 * step :]]
        return [
            jnp.concatenate([p[i * step : (i + 1) * step] for p in parts], axis=0)
            for i in range(2)
        ]

    key_all, recv_all = local(
        lay_both, [(everyone, width, BF16)] * 2, *group_gather(both)
    )
    relu, squared = product(
        [(key_all, w_key, "nn", 0)],
        [(everyone, ff_part, F32), (everyone, ff_part, BF16)],
        lambda acc: (jnp.maximum(acc, 0.0), jnp.square(jnp.maximum(acc, 0.0))),
    )
    (recept_act,) = product(
        [(recv_all, w_rec, "nn", 0)],
        [(everyone, part, BF16)],
        lambda acc: (acc,),
    )
    acts = exchange([recept_act[k * step : (k + 1) * step] for k in range(size)])
    value, value_more = group_sum(*crossing_sum((squared, w_val, 0)))
    block_output, upstream, value_grad, recept_grads = gates(
        (to_spans, from_spans),
        member,
        middle,
        value,
        value_more,
        jnp.concatenate(acts, axis=0),
        cotangent.reshape(step, width),
    )

    rg_all = jnp.concatenate(
        exchange([recept_grads[k * step : (k + 1) * step] for k in range(size)]), axis=0
    )
    vg_all = group_rows(value_grad)
    val_grads = team_products((vg_all, squared))
    vg_all, val_grads = tie(vg_all, val_grads)
    val_pair = square_sum(val_grads)
    (key_grad,) = product(
        [(vg_all, w_val, "nn", 0)],
        [(everyone, ff_part, BF16)],
        lambda acc, relu: (acc * (2.0 * relu),),
        sides=(relu,),
    )
    key_grads = team_products((key_all, key_grad))
    key_grad, key_grads = tie(key_grad, key_grads)
    key_pair = square_sum(key_grads)
    mine_two, more_two = group_sum(*crossing_sum((key_grad, w_key, 0), (rg_all, w_rec, 0)))

    def inputs_back(mine, more, vec):
        grads = mine + more.astype(F32)
        top = grads[:8] * vec[14:15] + grads[step : step + 8] * vec[15:16]
        return grads, top

    in_grads, top_two = local(
        inputs_back, [(2 * step, width, F32), (8, width, F32)], mine_two, more_two, vec
    )
    last_flag = (me == count - 1).astype(jnp.int32)

    def norm_two_back(last, grads, arrived, upstream, normal, scale, delta, vec):
        key_grad, recv_grad = grads[:step], grads[step:]
        shifted = key_grad * vec[14:15] + recv_grad * vec[15:16]
        below = jnp.where(last == 1, jnp.zeros_like(arrived[:1]), arrived[:1])
        grad = (
            key_grad * (1.0 - vec[14:15])
            + recv_grad * (1.0 - vec[15:16])
            + rows_below(shifted, below)
        )
        out = upstream + norm_back(grad, vec[12:13], normal, scale[:, :1])
        cols = padded(
            [
                column_sum(grad * normal),
                column_sum(grad),
                column_sum(key_grad * delta),
                column_sum(recv_grad * delta),
            ]
        )
        return out, out, cols

    middle_grad, branch_grad, cols_two = local(
        norm_two_back,
        [whole, (step, width, BF16), (8, width, F32)],
        in_grads,
        neighbour(top_two, -1),
        upstream,
        normal_two,
        scale_two,
        delta_two,
        vec,
        scalar=last_flag,
    )

    bg_all = group_rows(branch_grad)
    (gated_grad,) = product(
        [(bg_all, w_mix, "nn", 4 * tiles)], [(everyone, part, F32)], lambda acc: (acc,)
    )
    out_grads = team_products((bg_all, gated), (recv_all, rg_all))
    gated_grad, out_grads = tie(gated_grad, out_grads)
    out_pair = square_sum(out_grads)
    gate_grad, wkv_grad, ends = call(
        gate_kernel,
        ins="tttttp",
        outs=[("t", BF16), ("t", F32), ("x", F32)],
        args=(gated_grad, gate_pre, wkv, receipt, log_decay, wkv_rows),
    )
    grad_total = dict(enumerate(ordered([ends[k, :SPAN] for k in range(size)])))
    after = [(jnp.ones((1, part), F32), jnp.zeros((SPAN, part), F32)) for _ in range(size)]
    open_bits = size - 1
    for mask, level in zip(all_masks, levels):
        if mask in masks:
            bit = 1 << masks.index(mask)
            for m in range(size):
                if not m & bit:
                    late = (m & open_bits) | bit
                    d, s = after[m]
                    after[m] = (d * level[late], d * grad_total[late] + s)
            grad_total = {
                g: grad_total[g] + level[g] * grad_total[g | bit]
                for g in grad_total
                if not g & bit
            }
            open_bits ^= bit
        else:
            groups = list(grad_total)
            got = trade(jnp.concatenate([grad_total[g] for g in groups], axis=0), mask)
            other = {g: got[i * SPAN : (i + 1) * SPAN] for i, g in enumerate(groups)}
            early = bit_of(me, mask) == 0
            for m in range(size):
                g = m & open_bits
                d, s = after[m]
                after[m] = pick(early, (d * level[g][1], d * other[g] + s), (d, s))
            grad_total = {
                g: jnp.where(
                    early,
                    grad_total[g] + level[g][0] * other[g],
                    other[g] + level[g][1] * grad_total[g],
                )
                for g in groups
            }
    grad_out = jnp.stack(ordered([s for _, s in after]))
    first_grad = grad_total[0]
    holder = lax.div(me * rows, part)

    def rows_of(who):
        return lax.dynamic_slice_in_dim(first_grad, lax.rem(who * rows, part), rows, axis=1)

    handed = exchange([rows_of(jnp.bitwise_xor(me, flips(k))) for k in range(size)])
    state_rows = handed[0]
    for k in range(1, size):
        state_rows = jnp.where(holder == (member ^ k), handed[k], state_rows)
    initial_state_gradient = state_rows.T

    d_receipt, d_keys, d_values, d_decay, extra = call(
        backward_kernel,
        ins="tttttssp",
        outs=[("t", BF16)] * 4 + [("e", F32)],
        args=(receipt, keys, values, log_decay, wkv_grad, state_in, grad_out, wkv_rows),
    )
    grads = [d_keys, d_values, d_receipt, gate_grad]
    kept, sent = crossing_sum(
        *[(grads[c], w_mix, c) for c in range(4)]
    )
    mixed_mine, mixed_more = group_sum(kept, sent)

    def latent_back(grad, up):
        kept, sent = halves(nn(grad, up))
        return jnp.concatenate(kept, axis=0), jnp.concatenate(sent, axis=0)

    latent_mine, latent_more = group_sum(
        *local(
            latent_back, [(2 * step, DRANK, F32), (2 * step, DRANK, BF16)], d_decay, w_dup
        )
    )
    rest_grad, delta_grad, top_one, cols_mix, down_grad, up_grad, ddown_grad = mixes_back(
        mixed_mine,
        mixed_more,
        latent_mine,
        latent_more,
        delta,
        mix_tanh,
        decay_tanh,
        blend,
        mixed_zero,
        w_down,
        w_up,
        w_ddown,
        vec,
    )
    def norm_one_back(last, rest, shifted, arrived, normal, scale, middle, vec):
        below = jnp.where(last == 1, jnp.zeros_like(arrived[:1]), arrived[:1])
        grad = rest + rows_below(shifted, below)
        out = middle + norm_back(grad, vec[0:1], normal, scale[:, :1])
        cols = padded([column_sum(grad * normal), column_sum(grad)])
        return take_lanes(out, from_spans), cols

    block_input_gradient, cols_one = local(
        norm_one_back,
        [whole, (8, width, F32)],
        rest_grad,
        delta_grad,
        neighbour(top_one, -1),
        normal_one,
        scale_one,
        middle_grad,
        vec,
        scalar=last_flag,
    )
    sums = [
        TeamSum(mixed_all[3], gate_grad, True),
        TeamSum(mixed_all[1], d_values, False),
        TeamSum(mixed_all[0], d_keys, True),
        TeamSum(mixed_all[2], d_receipt, False),
    ]
    for _ in team_masks:
        for each in sums:
            each.step()
    gate_sum, values_sum, keys_sum, receipt_sum = [e.finish() for e in sums]
    val_sum, key_sum, out_sum = [far_sum(p) for p in (val_pair, key_pair, out_pair)]
    feedforward_gradient = hand_rows([[key_sum], [out_sum[:, part:]], [val_sum]])
    mixing_gradient = hand_rows(
        [[keys_sum], [values_sum], [receipt_sum], [gate_sum], [out_sum[:, :part]]]
    )


    def spread(value):
        zero = jnp.zeros((width, value.shape[1]), F32)
        return lax.dynamic_update_slice_in_dim(zero, value, member * part, axis=0)

    vec_low = jnp.concatenate([cols_one[:2], cols_mix[:6], cols_two[:4]], axis=0)
    vec_head = jnp.concatenate(
        [jnp.sum(extra[:, :2], axis=0), jnp.sum(ends[:, SPAN : SPAN + 2], axis=0)], axis=0
    )
    by_feature = jnp.concatenate([down_grad, up_grad, ddown_grad, vec_low.T], axis=1)
    low = cube_sum(to_cube(by_feature), BF16)
    by_channel = spread(jnp.concatenate([tn(d_decay, dh_all), vec_head.T], axis=1))
    high_part = cube_sum(by_channel.reshape(*[2] * len(all_masks), rows, -1), F32)
    lowrank_gradient = jnp.concatenate([low[:, :decay_up], high_part[:, :DRANK]], axis=1)
    vectors_gradient = jnp.concatenate(
        [low[:, decay_up : decay_up + 8], high_part[:, DRANK:], low[:, decay_up + 8 :]], axis=1
    )
    return (
        block_output.reshape(1, step, width),
        block_input_gradient.reshape(1, step, width),
        initial_state_gradient,
        mixing_gradient,
        lowrank_gradient,
        vectors_gradient,
        feedforward_gradient,
    )


def solution(mesh):
    rowwise = P("seq", None)
    tokenwise = P(None, "seq", None)
    return jax.shard_map(
        functools.partial(on_device, mesh.shape["seq"]),
        mesh=mesh,
        in_specs=(tokenwise, P(), rowwise, rowwise, rowwise, rowwise, rowwise, tokenwise),
        out_specs=(tokenwise, tokenwise, rowwise, rowwise, rowwise, rowwise, rowwise),
        check_vma=False,
    )
```

```python
import functools

import jax
import jax.numpy as jnp
from jax import lax
from jax.experimental import pallas as pl
from jax.experimental.pallas import tpu as pltpu
from jax.sharding import PartitionSpec as P

HEADS = 32
SPAN = 64
FF = 7168
RANK = 32
DRANK = 64
LN_EPS = 1e-05
GN_EPS = 0.00064

F32 = jnp.float32
BF16 = jnp.bfloat16
HI = lax.Precision.HIGHEST


def nn(a, b):
    return jnp.dot(a, b, preferred_element_type=F32)


def nt(a, b):
    return lax.dot_general(a, b, (((1,), (1,)), ((), ())), preferred_element_type=F32)


def tn(a, b):
    return lax.dot_general(a, b, (((0,), (0,)), ((), ())), preferred_element_type=F32)


def knn(a, b):
    return lax.dot_general(
        a, b, (((1,), (0,)), ((), ())), preferred_element_type=F32
    )


def knt(a, b):
    return lax.dot_general(
        a, b, (((1,), (1,)), ((), ())), preferred_element_type=F32
    )


def ktn(a, b):
    return lax.dot_general(
        a, b, (((0,), (0,)), ((), ())), preferred_element_type=F32
    )


def low_lanes(shape):
    return lax.broadcasted_iota(jnp.int32, shape, len(shape) - 1) < SPAN


def head_sum(x):
    low = low_lanes(x.shape)
    s0 = jnp.sum(jnp.where(low, x, 0.0), axis=-1, keepdims=True)
    s1 = jnp.sum(jnp.where(low, 0.0, x), axis=-1, keepdims=True)
    return jnp.where(low, s0, s1)


def two_rows(x):
    low = low_lanes(x.shape)
    return jnp.concatenate([jnp.where(low, x, 0.0), jnp.where(low, 0.0, x)], axis=0)


def fold(full):
    return jnp.where(low_lanes((SPAN, 2 * SPAN)), full[:SPAN], full[SPAN:])


def unfold(state):
    low = low_lanes(state.shape)
    return jnp.concatenate([jnp.where(low, state, 0.0), jnp.where(low, 0.0, state)], axis=0)


def running(w, upper=False):
    count = w.shape[0]
    row = lax.broadcasted_iota(jnp.int32, (count, count), 0)
    col = lax.broadcasted_iota(jnp.int32, (count, count), 1)
    keep = (col >= row) if upper else (col <= row)
    return lax.dot_general(
        jnp.where(keep, 1.0, 0.0).astype(F32),
        w,
        (((1,), (0,)), ((), ())),
        precision=HI,
        preferred_element_type=F32,
    )


def strict(count):
    row = lax.broadcasted_iota(jnp.int32, (2 * count, count), 0)
    col = lax.broadcasted_iota(jnp.int32, (2 * count, count), 1)
    row = jnp.where(row >= count, row - count, row)
    return row > col, row == col


def affinity(r, k, u, q, ks):
    count = r.shape[0]
    below, diag = strict(count)
    raw = knt(two_rows(q), ks)
    share = jnp.sum(two_rows(r * u * k), axis=-1, keepdims=True)
    return jnp.where(below, raw, jnp.where(diag, share, 0.0))


def totals_kernel(k_ref, v_ref, w_ref, out_ref):
    cum = running(w_ref[...])
    total = cum[-1:, :]
    kc = k_ref[...] * jnp.exp(total - cum)
    out_ref[0, :SPAN, :] = fold(ktn(v_ref[...], kc))
    out_ref[0, SPAN:, :] = jnp.broadcast_to(jnp.exp(total), (8, 2 * SPAN))


def group_norm(y, gain, bias):
    centred = y - head_sum(y) * (1.0 / SPAN)
    spread = head_sum(centred * centred) * (1.0 / SPAN)
    scale = lax.rsqrt(spread + GN_EPS)
    normal = centred * scale
    return normal, scale, normal * gain + bias


def forward_kernel(r_ref, k_ref, v_ref, w_ref, g_ref, s_ref, p_ref, y_ref, gated_ref):
    r, k, v, w = r_ref[...], k_ref[...], v_ref[...], w_ref[...]
    cum = running(w)
    q = r * jnp.exp(cum - w)
    ks = k * jnp.exp(-cum)
    aff = affinity(r, k, p_ref[0:1, :], q, ks)
    count = r.shape[0]
    v2 = two_rows(v)
    y = (
        knt(q, unfold(s_ref[0]))
        + knn(aff[:count], v2[:count])
        + knn(aff[count:], v2[count:])
    )
    y_ref[...] = y
    gate = g_ref[...]
    _, _, grouped = group_norm(y, p_ref[1:2, :], p_ref[2:3, :])
    gated_ref[...] = (grouped * gate * jax.nn.sigmoid(gate)).astype(BF16)


def gate_kernel(gg_ref, g_ref, y_ref, r_ref, w_ref, p_ref, gate_ref, dy_ref, out_ref):
    gated_grad, gate, y = gg_ref[...], g_ref[...], y_ref[...]
    gain = p_ref[1:2, :]
    normal, scale, grouped = group_norm(y, gain, p_ref[2:3, :])
    sig = jax.nn.sigmoid(gate)
    gate_ref[...] = (gated_grad * grouped * sig * (1.0 + gate * (1.0 - sig))).astype(BF16)
    outer = gated_grad * gate * sig
    inner = outer * gain
    dy = scale * (
        inner
        - head_sum(inner) * (1.0 / SPAN)
        - normal * (head_sum(inner * normal) * (1.0 / SPAN))
    )
    dy_ref[...] = dy
    w = w_ref[...]
    q = r_ref[...] * jnp.exp(running(w) - w)
    out_ref[0, :SPAN, :] = fold(ktn(dy, q))
    gain_grad = jnp.sum(outer * normal, axis=0, keepdims=True)
    bias_grad = jnp.sum(outer, axis=0, keepdims=True)
    out_ref[0, SPAN:, :] = jnp.concatenate(
        [gain_grad, bias_grad, jnp.zeros((6, 2 * SPAN), F32)], axis=0
    )


def backward_kernel(
    r_ref, k_ref, v_ref, w_ref, dy_ref, s_ref, gs_ref, p_ref,
    dr_ref, dk_ref, dv_ref, dd_ref, out_ref,
):
    r, k, v, w, dy = r_ref[...], k_ref[...], v_ref[...], w_ref[...], dy_ref[...]
    u = p_ref[0:1, :]
    count = r.shape[0]
    cum = running(w)
    total = cum[-1:, :]
    e_before, e_minus, e_carry = jnp.exp(cum - w), jnp.exp(-cum), jnp.exp(total - cum)
    q, ks, kc = r * e_before, k * e_minus, k * e_carry
    aff = affinity(r, k, u, q, ks)
    below, _ = strict(count)
    dy2 = two_rows(dy)
    d_aff = jnp.where(below, knt(dy2, v), 0.0)
    own = head_sum(dy * v)
    state, grad_state = s_ref[0], gs_ref[0]
    state2, grad2 = unfold(state), unfold(grad_state)
    ks2 = two_rows(ks)
    dq = knn(dy, state2) + knn(d_aff[:count], ks2[:count]) + knn(d_aff[count:], ks2[count:])
    dks = ktn(d_aff, two_rows(q))
    dkc = knn(v, grad2)
    dv_ref[...] = (ktn(aff, dy2) + knt(kc, grad2)).astype(BF16)
    dr_ref[...] = (dq * e_before + own * u * k).astype(BF16)
    dk_ref[...] = (dks * e_minus + dkc * e_carry + own * u * r).astype(BF16)
    gq, gc = q * dq, kc * dkc
    d_total = jnp.sum(gc, axis=0, keepdims=True) + jnp.exp(total) * jnp.sum(
        state * grad_state, axis=0, keepdims=True
    )
    dw = running(gq - ks * dks - gc, upper=True) - gq + d_total
    term = dw * w
    dd_ref[...] = term.astype(BF16)
    out_ref[0] = jnp.concatenate(
        [
            jnp.sum(term, axis=0, keepdims=True),
            jnp.sum(own * r * k, axis=0, keepdims=True),
            jnp.zeros((6, 2 * SPAN), F32),
        ],
        axis=0,
    )


def block_call(kernel, chunks, step, width, ins, outs, args):
    lane = 2 * SPAN
    kinds = {
        "t": pl.BlockSpec((step, lane), lambda c, h: (c, h)),
        "s": pl.BlockSpec((1, SPAN, lane), lambda c, h: (c, 0, h)),
        "x": pl.BlockSpec((1, SPAN + 8, lane), lambda c, h: (c, 0, h)),
        "e": pl.BlockSpec((1, 8, lane), lambda c, h: (c, 0, h)),
        "p": pl.BlockSpec((8, lane), lambda c, h: (0, h)),
    }
    shapes = {
        "t": lambda d: jax.ShapeDtypeStruct((chunks * step, width), d),
        "x": lambda d: jax.ShapeDtypeStruct((chunks, SPAN + 8, width), d),
        "e": lambda d: jax.ShapeDtypeStruct((chunks, 8, width), d),
    }
    return pl.pallas_call(
        kernel,
        grid=(chunks, width // lane),
        in_specs=[kinds[kind] for kind in ins],
        out_specs=[kinds[kind] for kind, _ in outs],
        out_shape=[shapes[kind](dtype) for kind, dtype in outs],
        compiler_params=pltpu.CompilerParams(vmem_limit_bytes=48 * 1024 * 1024),
    )(*args)


def weight_grad(places, pairs, block):
    tokens, blocks = pairs[0][0].shape[0], places.shape[0]
    widths = [y.shape[1] for _, y in pairs]

    def kernel(_, *refs):
        at = 0
        for i, wide in enumerate(widths):
            refs[-1][0, :, at : at + wide] = tn(refs[2 * i][...], refs[2 * i + 1][...]).astype(
                BF16
            )
            at += wide

    specs = []
    for wide in widths:
        specs.append(pl.BlockSpec((tokens, block), lambda i, at: (0, at[i])))
        specs.append(pl.BlockSpec((tokens, wide), lambda i, at: (0, 0)))
    return pl.pallas_call(
        kernel,
        grid_spec=pltpu.PrefetchScalarGridSpec(
            num_scalar_prefetch=1,
            grid=(blocks,),
            in_specs=specs,
            out_specs=pl.BlockSpec((1, block, sum(widths)), lambda i, at: (i, 0, 0)),
        ),
        out_shape=jax.ShapeDtypeStruct((blocks, block, sum(widths)), BF16),
        compiler_params=pltpu.CompilerParams(vmem_limit_bytes=48 * 1024 * 1024),
    )(places, *[v for pair in pairs for v in pair])


def lanes_kernel(spans, x_ref, out_ref):
    at = 0
    for start, stop in spans:
        out_ref[:, at : at + stop - start] = x_ref[:, start:stop].astype(out_ref.dtype)
        at += stop - start


def move_lanes(spans, value, dtype):
    return pl.pallas_call(
        functools.partial(lanes_kernel, spans),
        in_specs=[pl.BlockSpec(memory_space=pltpu.VMEM)],
        out_specs=pl.BlockSpec(memory_space=pltpu.VMEM),
        out_shape=jax.ShapeDtypeStruct(value.shape, dtype),
        compiler_params=pltpu.CompilerParams(vmem_limit_bytes=32 * 1024 * 1024),
    )(value)


def place_kernel(counts, wide, block, at_ref, *refs):
    ins, out_ref, sems = refs[: len(counts)], refs[-2], refs[-1]
    rows = out_ref.shape[0]
    copies, i = [], 0
    for ref, n in zip(ins, counts):
        for j in range(n):
            start = pl.multiple_of(at_ref[i] * block, block)
            column = i * block // rows * wide
            copy = pltpu.make_async_copy(
                ref.at[pl.ds(j * block, block), :],
                out_ref.at[pl.ds(start, block), pl.ds(column, wide)],
                sems.at[i],
            )
            copy.start()
            copies.append(copy)
            i += 1
    for copy in copies:
        copy.wait()


def place_rows(parts, block):
    pieces = [p for part in parts for p in part[1]]
    wide = pieces[0].shape[1]
    at = jnp.concatenate([part[0] for part in parts])
    counts = [p.shape[0] // block for p in pieces]
    total = sum(counts)
    return pl.pallas_call(
        functools.partial(place_kernel, counts, wide, block),
        in_specs=[pl.BlockSpec(memory_space=pltpu.SMEM)]
        + [pl.BlockSpec(memory_space=pl.ANY)] * len(pieces),
        out_specs=pl.BlockSpec(memory_space=pl.ANY),
        out_shape=jax.ShapeDtypeStruct(
            (total * block // len(parts), wide * len(parts)), pieces[0].dtype
        ),
        scratch_shapes=[pltpu.SemaphoreType.DMA((total,))],
        compiler_params=pltpu.CompilerParams(vmem_limit_bytes=32 * 1024 * 1024),
    )(at, *pieces)


def mixes_kernel(
    open_ref, x_ref, before_ref, vec_ref, down_ref, up_ref, ddown_ref,
    m1_ref, m2_ref, m3_ref, m4_ref, dh_ref,
    normal_ref, scale_ref, delta_ref, blend_ref, m0_ref, tanh_ref, dtanh_ref,
):
    piece = pl.program_id(0)
    step = m1_ref.shape[0]
    x = x_ref[...].astype(F32)
    centred = x - jnp.mean(x, axis=-1, keepdims=True)
    scale = lax.rsqrt(jnp.mean(centred * centred, axis=-1, keepdims=True) + LN_EPS)
    normal = centred * scale
    full = normal * vec_ref[0:1, :] + vec_ref[1:2, :]
    normed = full[:step]
    first = jnp.where(open_ref[piece] == 1, before_ref[0:1, :], full[step : step + 1])
    row = lax.broadcasted_iota(jnp.int32, normed.shape, 0)
    delta = jnp.where(row == 0, first, pltpu.roll(normed, 1, 0)) - normed
    blend = (normed + delta * vec_ref[2:3, :]).astype(BF16)
    tanh = jnp.tanh(nn(blend, down_ref[...]))
    latent = tanh.astype(BF16)
    lane = lax.broadcasted_iota(jnp.int32, latent.shape, 1)
    mixed = []
    for c in range(5):
        own = (lane >= c * RANK) & (lane < (c + 1) * RANK)
        offset = nt(jnp.where(own, latent, jnp.zeros_like(latent)), up_ref[...])
        mixed.append((normed + delta * (vec_ref[3 + c : 4 + c, :] + offset)).astype(BF16))
    dtanh = jnp.tanh(nn(mixed[0], ddown_ref[...]))
    m1_ref[...], m2_ref[...], m3_ref[...], m4_ref[...] = mixed[1:]
    dh_ref[...] = dtanh.astype(BF16)

    @pl.when(piece == 0)
    def _():
        normal_ref[...] = normal[:step]
        scale_ref[...] = jnp.broadcast_to(scale[:step], scale_ref.shape)
        delta_ref[...] = delta
        blend_ref[...] = blend
        m0_ref[...] = mixed[0]
        tanh_ref[...] = tanh
        dtanh_ref[...] = dtanh


def group_mixes(opening, x, before, vec, down, up, ddown, step):
    high, width = step + 16, x.shape[1]
    pieces = x.shape[0] // high

    def whole(value):
        return pl.BlockSpec(value.shape, lambda k: (0, 0))

    def own(columns, dtype):
        return (
            pl.BlockSpec((step, columns), lambda k: (0, 0)),
            jax.ShapeDtypeStruct((step, columns), dtype),
        )

    def every(columns, dtype):
        return (
            pl.BlockSpec((step, columns), lambda k: ((k % 2) * 2 + k // 2, 0)),
            jax.ShapeDtypeStruct((pieces * step, columns), dtype),
        )

    outs = [every(width, BF16)] * 4 + [
        every(DRANK, BF16),
        own(width, F32),
        own(128, F32),
        own(width, F32),
        own(width, BF16),
        own(width, BF16),
        own(5 * RANK, F32),
        own(DRANK, F32),
    ]
    return pl.pallas_call(
        mixes_kernel,
        grid=(pieces,),
        in_specs=[
            pl.BlockSpec(memory_space=pltpu.SMEM),
            pl.BlockSpec((high, width), lambda k: (k, 0)),
            whole(before),
            whole(vec),
            whole(down),
            whole(up),
            whole(ddown),
        ],
        out_specs=[o[0] for o in outs],
        out_shape=[o[1] for o in outs],
        compiler_params=pltpu.CompilerParams(vmem_limit_bytes=56 * 1024 * 1024),
    )(opening, x, before, vec, down, up, ddown)


def product(pairs, outs, body, sides=(), tile=256):
    count = len(pairs)

    def kernel(*refs):
        ins, out_refs = refs[: 2 * count + len(sides)], refs[2 * count + len(sides) :]
        products = [
            (nn if pair[2] == "nn" else nt)(ins[2 * i][...], ins[2 * i + 1][...])
            for i, pair in enumerate(pairs)
        ]
        results = body(*products, *[r[...] for r in ins[2 * count :]])
        for ref, value in zip(out_refs, results):
            ref[...] = value.astype(ref.dtype)

    specs, args = [], []
    for a, b, form, at in pairs:
        depth = a.shape[1]
        specs.append(pl.BlockSpec(a.shape, lambda j: (0, 0)))
        if form == "nn":
            specs.append(pl.BlockSpec((depth, tile), lambda j, at=at: (0, at + j)))
        else:
            specs.append(pl.BlockSpec((tile, depth), lambda j, at=at: (j, at)))
        args += [a, b]
    for side in sides:
        specs.append(pl.BlockSpec((side.shape[0], tile), lambda j: (0, j)))
    return pl.pallas_call(
        kernel,
        grid=(outs[0][1] // tile,),
        in_specs=specs,
        out_specs=[pl.BlockSpec((o[0], tile), lambda j: (0, j)) for o in outs],
        out_shape=[jax.ShapeDtypeStruct(o[:2], o[2]) for o in outs],
        compiler_params=pltpu.CompilerParams(vmem_limit_bytes=56 * 1024 * 1024),
    )(*args, *sides)


def local(fn, outs, *args, scalar=None):
    def kernel(*refs):
        lead = [] if scalar is None else [refs[0]]
        ins, out_refs = refs[len(lead) : -len(outs)], refs[-len(outs) :]
        results = fn(*[r[0] for r in lead], *[r[...] for r in ins])
        for ref, value in zip(out_refs, results):
            ref[...] = value.astype(ref.dtype)

    specs = [pl.BlockSpec(memory_space=pltpu.VMEM)] * len(args)
    if scalar is not None:
        specs = [pl.BlockSpec(memory_space=pltpu.SMEM)] + specs
        args = (scalar.reshape(1), *args)
    return pl.pallas_call(
        kernel,
        in_specs=specs,
        out_specs=[pl.BlockSpec(memory_space=pltpu.VMEM)] * len(outs),
        out_shape=[jax.ShapeDtypeStruct(o[:2], o[2]) for o in outs],
        compiler_params=pltpu.CompilerParams(vmem_limit_bytes=56 * 1024 * 1024),
    )(*args)


def take_lanes(value, spans):
    if len(spans) == 1:
        return value
    return jnp.concatenate([value[:, a:b] for a, b in spans], axis=1)


def norm_back(grad, gain, normal, scale):
    e = grad * gain
    return scale * (
        e
        - jnp.mean(e, axis=-1, keepdims=True)
        - normal * jnp.mean(e * normal, axis=-1, keepdims=True)
    )


def rows_above(value, first):
    row = lax.broadcasted_iota(jnp.int32, value.shape, 0)
    return jnp.where(row == 0, first, pltpu.roll(value, 1, 0))


def rows_below(value, last):
    row = lax.broadcasted_iota(jnp.int32, value.shape, 0)
    high = value.shape[0]
    return jnp.where(row == high - 1, last, pltpu.roll(value, high - 1, 0))


def padded(rows):
    return jnp.concatenate(
        list(rows) + [jnp.zeros((8 - len(rows), rows[0].shape[1]), F32)], axis=0
    )


def column_sum(value):
    return jnp.sum(value, axis=0, keepdims=True)


def gates_kernel(
    spans, who_ref, middle_ref, value_ref, more_ref, act_ref, cot_ref,
    out_ref, up_ref, vg_ref, rg_ref, held,
):
    to_spans, from_spans = spans
    step, part = act_ref.shape[0] // 4, act_ref.shape[1]
    who = who_ref[0]
    act = [
        act_ref[pl.ds(pl.multiple_of((who ^ j) * step, step), step), :] for j in range(4)
    ]
    recept = jax.nn.sigmoid(take_lanes(jnp.concatenate(act, axis=1).astype(F32), to_spans))
    value = value_ref[...] + more_ref[...].astype(F32)
    out = middle_ref[...] + recept * value
    out_ref[...] = take_lanes(out, from_spans).astype(BF16)
    up = take_lanes(cot_ref[...].astype(F32), to_spans)
    up_ref[...] = up
    vg_ref[...] = (up * recept).astype(BF16)
    held[...] = take_lanes(up * value * recept * (1.0 - recept), from_spans)
    for k in range(4):
        at = pl.multiple_of((who ^ k) * part, part)
        rg_ref[k * step : (k + 1) * step, :] = held[:, pl.ds(at, part)].astype(BF16)


def gates(spans, who, middle, value, more, act, cot):
    step, width = middle.shape
    part = act.shape[1]
    shape = jax.ShapeDtypeStruct
    return pl.pallas_call(
        functools.partial(gates_kernel, spans),
        in_specs=[pl.BlockSpec(memory_space=pltpu.SMEM)]
        + [pl.BlockSpec(memory_space=pltpu.VMEM)] * 5,
        out_specs=[pl.BlockSpec(memory_space=pltpu.VMEM)] * 4,
        out_shape=[
            shape((step, width), BF16),
            shape((step, width), F32),
            shape((step, width), BF16),
            shape((4 * step, part), BF16),
        ],
        scratch_shapes=[pltpu.VMEM((step, width), F32)],
        compiler_params=pltpu.CompilerParams(vmem_limit_bytes=56 * 1024 * 1024),
    )(who.reshape(1), middle, value, more, act, cot)


def mixes_back_kernel(
    kept_ref, got_ref, dl_ref, dl_more_ref, delta_ref, tanh_ref, dtanh_ref, blend_ref, m0_ref,
    down_ref, up_ref, ddown_ref, vec_ref,
    rest_ref, dg_ref, row_ref, cols_ref, down_out, up_out, ddown_out,
):
    step = delta_ref.shape[0]
    dtanh = dtanh_ref[...]
    decay_grad = dl_ref[...] + dl_more_ref[...].astype(F32)
    decay_pre = (decay_grad * (1.0 - dtanh * dtanh)).astype(BF16)
    ddown_out[...] = tn(m0_ref[...], decay_pre)
    tanh = tanh_ref[...]
    latent = tanh.astype(BF16)
    lane = lax.broadcasted_iota(jnp.int32, latent.shape, 1)
    delta, up = delta_ref[...], up_ref[...]
    latent_grad = jnp.zeros(latent.shape, F32)
    up_grad = jnp.zeros(up_out.shape, F32)
    dg = jnp.zeros(delta.shape, F32)
    total = jnp.zeros(delta.shape, F32)
    cols = []
    for c in range(5):
        own = (lane >= c * RANK) & (lane < (c + 1) * RANK)
        mine = jnp.where(own, latent, jnp.zeros_like(latent))
        if c == 0:
            grad = nt(decay_pre, ddown_ref[...])
        else:
            at = slice((c - 1) * step, c * step)
            grad = kept_ref[at, :] + got_ref[at, :].astype(F32)
        shift = grad * delta
        cols.append(column_sum(shift))
        offset = shift.astype(BF16)
        latent_grad = jnp.where(own, nn(offset, up), latent_grad)
        up_grad = up_grad + tn(offset, mine)
        dg = dg + grad * (vec_ref[3 + c : 4 + c, :] + nt(mine, up))
        total = total + grad
    up_out[...] = up_grad
    mix_pre = (latent_grad * (1.0 - tanh * tanh)).astype(BF16)
    down_out[...] = tn(blend_ref[...], mix_pre)
    blend_grad = nt(mix_pre, down_ref[...])
    dg = dg + blend_grad * vec_ref[2:3, :]
    rest_ref[...] = total + blend_grad - dg
    dg_ref[...] = dg
    row_ref[...] = dg[:8]
    cols_ref[...] = padded([column_sum(blend_grad * delta)] + cols)


def mixes_back(*args):
    delta, down, ddown = args[4], args[9], args[11]
    step, width = delta.shape
    shape = jax.ShapeDtypeStruct
    outs = [
        shape((step, width), F32),
        shape((step, width), F32),
        shape((8, width), F32),
        shape((8, width), F32),
        shape(down.shape, F32),
        shape(down.shape, F32),
        shape(ddown.shape, F32),
    ]
    return pl.pallas_call(
        mixes_back_kernel,
        in_specs=[pl.BlockSpec(memory_space=pltpu.VMEM)] * len(args),
        out_specs=[pl.BlockSpec(memory_space=pltpu.VMEM)] * len(outs),
        out_shape=outs,
        compiler_params=pltpu.CompilerParams(vmem_limit_bytes=60 * 1024 * 1024),
    )(*args)


def tie(*values):
    return lax.optimization_barrier(values)


def on_device(
    count,
    tokens,
    previous,
    initial_state,
    mixing_weights,
    lowrank_weights,
    vectors,
    feedforward_weights,
    cotangent,
):
    fast = initial_state.shape[0] == 64
    masks = (1, 8) if fast else (1, 2)
    size = 1 << len(masks)
    teams = count // size
    all_masks = [1 << b for b in range(count.bit_length() - 1)]
    team_masks = [b for b in all_masks if b not in masks]
    far = 16
    team_masks.sort(key=lambda b: fast and b != far)
    me = lax.axis_index("seq")
    _, step, width = tokens.shape
    rows = mixing_weights.shape[0]
    part = width // size
    ff_part = FF // size
    team_rows = rows * size
    def bit_of(who, mask):
        return (who // mask) % 2 if isinstance(who, int) else lax.rem(lax.div(who, mask), 2)

    def member_of(who):
        return sum(bit_of(who, b) << j for j, b in enumerate(masks))

    def team_of(who):
        return sum(bit_of(who, b) << j for j, b in enumerate(team_masks))

    member, team = member_of(me), team_of(me)
    order = sorted(range(count), key=lambda d: (team_of(d), member_of(d)))
    inverse = sorted(range(count), key=lambda p: order[p])
    across = [order[m::size] for m in range(size)]
    square = [order[m :: 2 * size] for m in range(2 * size)]
    def lane_spans(blocks):
        spans = []
        for d in blocks:
            if spans and spans[-1][1] == d * rows:
                spans[-1][1] = (d + 1) * rows
            else:
                spans.append([d * rows, (d + 1) * rows])
        return spans

    to_spans, from_spans = lane_spans(order), lane_spans(inverse)

    def to_places(value, dtype):
        return move_lanes(to_spans, value, dtype)

    def flips(k):
        return sum(b for j, b in enumerate(masks) if (k >> j) & 1)

    def trade(value, mask):
        return lax.ppermute(value, "seq", [(d, d ^ mask) for d in range(count)])

    def group_gather(value):
        side = trade(value, masks[1])
        return value, side, trade(jnp.concatenate([value, side], axis=0), masks[0])

    def group_rows(value):
        high, columns = value.shape

        def lay(own, side, far):
            return (jnp.concatenate([own, far[:high], side, far[high:]], axis=0),)

        return local(lay, [(size * high, columns, value.dtype)], *group_gather(value))[0]

    def halves(value):
        cut = [value[k * step : (k + 1) * step] for k in range(size)]
        return [cut[0], cut[2]], [cut[1], cut[3]]

    def group_sum(kept, sent):
        high, columns = kept.shape[0] // 2, kept.shape[1]
        got = trade(sent, masks[0])

        def add(mine, more):
            total = mine + more.astype(F32)
            return total[:high], total[high:]

        mine, side = local(add, [(high, columns, F32), (high, columns, BF16)], kept, got)
        return mine, trade(side, masks[1])

    def crossing_sum(*pairs):
        units = len(pairs)

        def body(*products):
            parts = [halves(p) for p in products]
            kept = [p[0][i] for i in range(2) for p in parts]
            sent = [p[1][i] for i in range(2) for p in parts]
            return jnp.concatenate(kept, axis=0), jnp.concatenate(sent, axis=0)

        high = 2 * units * step
        return product(
            [(a, b, "nt", at) for a, b, at in pairs],
            [(high, width, F32), (high, width, BF16)],
            body,
        )

    def exchange(pieces):
        pieces, high = list(pieces), pieces[0].shape[0]
        for j in reversed(range(len(masks))):
            keys = [k for k in range(size) if (k >> j) & 1]
            got = trade(jnp.concatenate([pieces[k] for k in keys], axis=0), masks[j])
            for i, k in enumerate(keys):
                pieces[k] = got[i * high : (i + 1) * high]
        return pieces

    def ordered(pieces):
        pieces = list(pieces)
        for j in range(len(masks)):
            swap = lax.rem(lax.div(member, 1 << j), 2) == 1
            pieces = [
                jnp.where(swap, pieces[k ^ (1 << j)], pieces[k]) for k in range(len(pieces))
            ]
        return pieces

    def neighbour(value, offset):
        pairs = [(d, d + offset) for d in range(count) if 0 <= d + offset < count]
        return lax.ppermute(value, "seq", pairs)

    def take_columns(value, spans, who):
        return jnp.concatenate(
            [
                lax.dynamic_slice_in_dim(value, start + who * wide, wide, axis=1)
                for start, wide in spans
            ],
            axis=1,
        )

    def group_columns(value, spans):
        pieces = [take_columns(value, spans, member ^ k) for k in range(size)]
        return jnp.concatenate(ordered(exchange(pieces)), axis=0)

    def crossing(first):
        bits = list(range(1, len(team_masks))) + [0]
        if first:
            bits[0], bits[1] = bits[1], bits[0]
        return bits

    def gather_rows(own):
        return lax.all_gather(own, "seq", axis=0, tiled=True, axis_index_groups=across)

    def far_pair(own):
        if not fast:
            return own
        got = trade(own, far)
        upper = bit_of(me, far) == 1
        return jnp.concatenate(
            [jnp.where(upper, got, own), jnp.where(upper, own, got)], axis=0
        )

    def cross_rows(own):
        if not fast:
            return gather_rows(own)
        cut = own.shape[1] // 2
        parts = []
        for first, piece in ((False, own[:, :cut]), (True, own[:, cut:])):
            pieces, places = [piece], [0]
            for bit in reversed(crossing(first)):
                joint = pieces[0] if len(pieces) == 1 else jnp.concatenate(pieces, axis=0)
                pieces.append(trade(joint, team_masks[bit]))
                places = places + [p | (1 << bit) for p in places]
            parts.append((jnp.bitwise_xor(jnp.asarray(places, jnp.int32), team), pieces))
        return place_rows(parts, team_rows)

    def gather_square(paired):
        groups = square if fast else across
        return lax.all_gather(paired, "seq", axis=0, tiled=True, axis_index_groups=groups)

    def team_products(*pairs):
        if fast:
            places = jnp.arange(teams, dtype=jnp.int32)
            return weight_grad(places, pairs, team_rows).reshape(width, -1)
        return jnp.concatenate([tn(x, y).astype(BF16) for x, y in pairs], axis=1)

    def square_sum(grads):
        groups = square if fast else across
        return lax.psum_scatter(
            grads, "seq", scatter_dimension=0, tiled=True, axis_index_groups=groups
        )

    def far_sum(pair):
        if not fast:
            return pair
        bit = bit_of(me, far)
        sent = lax.dynamic_slice_in_dim(pair, (1 - bit) * team_rows, team_rows, axis=0)
        kept = lax.dynamic_slice_in_dim(pair, bit * team_rows, team_rows, axis=0)
        return (kept.astype(F32) + trade(sent, far).astype(F32)).astype(BF16)

    first_steps = []

    def cube_gather(value):
        for mask in reversed(all_masks):
            got = trade(value, mask)
            upper = bit_of(me, mask) == 1
            value = jnp.stack([jnp.where(upper, got, value), jnp.where(upper, value, got)])
            if mask == 8:
                first_steps.append(value)
        axes = len(all_masks)
        return value.transpose(*reversed(range(axes)), *range(axes, value.ndim))

    place_axes = [all_masks[::-1].index(b) for b in team_masks[::-1] + list(masks[::-1])]

    def by_place(cube):
        rest = range(len(all_masks), cube.ndim)
        return cube.transpose(*place_axes, *rest).reshape(width, -1)

    def to_cube(value):
        cube = value.reshape(*[2] * len(place_axes), rows, -1)
        back = [place_axes.index(a) for a in range(len(place_axes))]
        return cube.transpose(*back, len(back), len(back) + 1)

    def cube_sum(cube, kind):
        for axis, mask in reversed(list(enumerate(reversed(all_masks)))):
            bit = bit_of(me, mask)
            sent = lax.dynamic_index_in_dim(cube, 1 - bit, axis, keepdims=False)
            kept = lax.dynamic_index_in_dim(cube, bit, axis, keepdims=False)
            cube = kept.astype(F32) + trade(sent.astype(kind), mask).astype(F32)
        return cube

    def hand_rows(pieces):
        widths = [sum(p.shape[1] for p in piece) for piece in pieces]
        joint = jnp.concatenate([p for piece in pieces for p in piece], axis=1)
        mine = [
            lax.dynamic_slice_in_dim(joint, (member ^ k) * rows, rows, axis=0)
            for k in range(size)
        ]
        by_member = ordered(exchange(mine))
        outs, start = [], 0
        for wide in widths:
            outs += [p[:, start : start + wide] for p in by_member]
            start += wide
        return jnp.concatenate(outs, axis=1).astype(F32)

    up_start, decay_start, decay_up = 5 * RANK, 10 * RANK, 10 * RANK + DRANK
    last_row = neighbour(tokens[0, -1:, :], 1)
    tokens_sent = to_places(
        jnp.concatenate([tokens[0], jnp.broadcast_to(last_row, (16, width))], axis=0), BF16
    )
    natural = cube_gather(
        jnp.concatenate(
            [vectors, initial_state, lowrank_weights[:, decay_up:].astype(F32)], axis=1
        )
    ).reshape(width, -1)
    low_cube = cube_gather(lowrank_weights[:, :decay_up])
    lowrank = by_place(low_cube)
    tokens_all = jnp.concatenate(group_gather(tokens_sent), axis=0)
    mix_in = tie(mixing_weights, *first_steps)[0]
    mix_local = group_columns(mix_in, [(c * width, part) for c in range(5)])
    mix_local = tie(mix_local, natural, low_cube, tokens_all)[0]
    kv_pair = far_pair(mix_local[:, : 2 * part])
    mix_rest = tie(mix_local[:, 2 * part :], kv_pair)[0]
    rest_pair = far_pair(mix_rest)
    feed_in = tie(feedforward_weights, kv_pair)[0]
    ff_spans = [(0, ff_part), (FF, part), (FF + width, ff_part)]
    ff_local = group_columns(feed_in, ff_spans)
    ff_near = tie(ff_local[:, : ff_part + part], rest_pair)[0]
    near_pair = far_pair(ff_near)
    ff_tail = tie(ff_local[:, ff_part + part :], near_pair)[0]
    w_kv = gather_square(kv_pair)
    w_rest = gather_square(rest_pair)
    w_near = gather_square(near_pair)
    w_key, w_rec = w_near, w_near[:, ff_part:]
    w_val = cross_rows(ff_tail)
    tiles = part // 256

    mine = lax.dynamic_slice_in_dim(natural, member * part, part, axis=0)
    vec_part = mine[:, :16].T
    first_state = mine[:, 16 : 16 + SPAN].T
    w_dup = mine[:, 16 + SPAN :].astype(BF16)
    vec = by_place(
        natural[:, :16].reshape(*[2] * len(all_masks), rows, 16)
    ).T
    wkv_rows = jnp.concatenate([vec_part[9:12], jnp.zeros((5, part), F32)], axis=0)
    is_first = (me == 0).astype(jnp.int32)
    before = to_places(previous.reshape(2, width), F32)
    w_down, w_up = lowrank[:, :up_start], lowrank[:, up_start:decay_start]
    w_ddown = lowrank[:, decay_start:]

    opening = jnp.stack(
        [jnp.bitwise_xor(me, flips(k)) == 0 for k in (0, 2, 1, 3)]
    ).astype(jnp.int32)
    (
        *mixed_all, dh_all, normal_one, scale_one, delta, blend, mixed_zero, mix_tanh, decay_tanh,
    ) = group_mixes(opening, tokens_all, before, vec, w_down, w_up, w_ddown, step)
    everyone = size * step
    (log_decay,) = product(
        [(dh_all, w_dup, "nt", 0)],
        [(everyone, part, F32)],
        lambda acc, base: (-jnp.exp(base + acc),),
        sides=(vec_part[8:9],),
    )
    keys, values = product(
        [(mixed_all[0], w_kv, "nn", 0), (mixed_all[1], w_kv, "nn", tiles)],
        [(everyone, part, F32)] * 2,
        lambda a, b: (a, b),
    )

    call = functools.partial(block_call, chunks=size, step=step, width=part)
    (totals,) = call(
        totals_kernel, ins="ttt", outs=[("x", F32)], args=(keys, values, log_decay)
    )
    by_member = ordered([totals[k] for k in range(size)])
    total = {m: (p[SPAN : SPAN + 1], p[:SPAN]) for m, p in enumerate(by_member)}
    before_chunk = [
        (jnp.ones((1, part), F32), jnp.zeros((SPAN, part), F32)) for _ in range(size)
    ]
    open_bits = size - 1
    levels = []

    def chain(early, late):
        return early[0] * late[0], late[0] * early[1] + late[1]

    def pick(flag, yes, no):
        return tuple(jnp.where(flag, a, b) for a, b in zip(yes, no))

    for mask in all_masks:
        if mask in masks:
            bit = 1 << masks.index(mask)
            levels.append({g: total[g][0] for g in total})
            for m in range(size):
                if m & bit:
                    early = (m & open_bits) ^ bit
                    before_chunk[m] = chain(total[early], before_chunk[m])
            total = {g: chain(total[g], total[g | bit]) for g in total if not g & bit}
            open_bits ^= bit
        else:
            groups = list(total)
            sent = jnp.concatenate(
                [
                    jnp.concatenate(
                        [total[g][1], jnp.broadcast_to(total[g][0], (8, part))], axis=0
                    )
                    for g in groups
                ],
                axis=0,
            )
            got = trade(sent, mask)
            high = SPAN + 8
            other = {
                g: (got[i * high + SPAN : i * high + SPAN + 1], got[i * high : i * high + SPAN])
                for i, g in enumerate(groups)
            }
            levels.append({g: (total[g][0], other[g][0]) for g in groups})
            late = bit_of(me, mask) == 1
            for m in range(size):
                g = m & open_bits
                before_chunk[m] = pick(late, chain(other[g], before_chunk[m]), before_chunk[m])
            total = {
                g: pick(late, chain(other[g], total[g]), chain(total[g], other[g]))
                for g in groups
            }
    state_in = jnp.stack(ordered([d * first_state + s for d, s in before_chunk]))

    receipt, gate_pre = product(
        [(mixed_all[2], w_rest, "nn", 0), (mixed_all[3], w_rest, "nn", tiles)],
        [(everyone, part, F32)] * 2,
        lambda a, b: (a, b),
    )
    wkv, gated = call(
        forward_kernel,
        ins="tttttsp",
        outs=[("t", F32), ("t", BF16)],
        args=(receipt, keys, values, log_decay, gate_pre, state_in, wkv_rows),
    )
    branch, branch_more = group_sum(*crossing_sum((gated, w_rest, 2)))

    def norm_two(hidden, mine, more, vec):
        middle = hidden[:step].astype(F32) + mine + more.astype(F32)
        centred = middle - jnp.mean(middle, axis=-1, keepdims=True)
        scale = lax.rsqrt(jnp.mean(centred * centred, axis=-1, keepdims=True) + LN_EPS)
        normal = centred * scale
        tail = normal[step - 8 :] * vec[12:13] + vec[13:14]
        return middle, normal, jnp.broadcast_to(scale, (step, 128)), tail

    whole = (step, width, F32)
    middle, normal_two, scale_two, tail_two = local(
        norm_two,
        [whole, whole, (step, 128, F32), (8, width, F32)],
        tokens_sent,
        branch,
        branch_more,
        vec,
    )

    def mix_two(first, normal, arrived, before, vec):
        normed = normal * vec[12:13] + vec[13:14]
        above = jnp.where(first == 1, before[1:2], arrived[7:8])
        delta = rows_above(normed, above) - normed
        key_in, recv_in = normed + delta * vec[14:15], normed + delta * vec[15:16]
        return jnp.concatenate([key_in, recv_in], axis=0), delta

    both, delta_two = local(
        mix_two,
        [(2 * step, width, BF16), whole],
        normal_two,
        neighbour(tail_two, 1),
        before,
        vec,
        scalar=is_first,
    )

    key_all, recv_all = group_rows(both[:step]), group_rows(both[step:])
    relu, squared = product(
        [(key_all, w_key, "nn", 0)],
        [(everyone, ff_part, F32), (everyone, ff_part, BF16)],
        lambda acc: (jnp.maximum(acc, 0.0), jnp.square(jnp.maximum(acc, 0.0))),
    )
    (recept_act,) = product(
        [(recv_all, w_rec, "nn", 0)],
        [(everyone, part, BF16)],
        lambda acc: (acc,),
    )
    acts = exchange([recept_act[k * step : (k + 1) * step] for k in range(size)])
    value, value_more = group_sum(*crossing_sum((squared, w_val, 0)))
    block_output, upstream, value_grad, recept_grads = gates(
        (to_spans, from_spans),
        member,
        middle,
        value,
        value_more,
        jnp.concatenate(acts, axis=0),
        cotangent.reshape(step, width),
    )

    rg_all = jnp.concatenate(
        exchange([recept_grads[k * step : (k + 1) * step] for k in range(size)]), axis=0
    )
    vg_all = group_rows(value_grad)
    val_grads = team_products((vg_all, squared))
    vg_all, val_grads = tie(vg_all, val_grads)
    val_pair = square_sum(val_grads)
    (key_grad,) = product(
        [(vg_all, w_val, "nn", 0)],
        [(everyone, ff_part, BF16)],
        lambda acc, relu: (acc * (2.0 * relu),),
        sides=(relu,),
    )
    key_grads = team_products((key_all, key_grad))
    key_grad, key_grads = tie(key_grad, key_grads)
    key_pair = square_sum(key_grads)
    recv_two = group_sum(*crossing_sum((rg_all, w_rec, 0)))
    key_two = group_sum(*crossing_sum((key_grad, w_key, 0)))

    def inputs_back(key, key_more, recv, recv_more, vec):
        key, recv = key + key_more.astype(F32), recv + recv_more.astype(F32)
        top = key[:8] * vec[14:15] + recv[:8] * vec[15:16]
        return jnp.concatenate([key, recv], axis=0), top

    in_grads, top_two = local(
        inputs_back, [(2 * step, width, F32), (8, width, F32)], *key_two, *recv_two, vec
    )
    last_flag = (me == count - 1).astype(jnp.int32)

    def norm_two_back(last, grads, arrived, upstream, normal, scale, delta, vec):
        key_grad, recv_grad = grads[:step], grads[step:]
        shifted = key_grad * vec[14:15] + recv_grad * vec[15:16]
        below = jnp.where(last == 1, jnp.zeros_like(arrived[:1]), arrived[:1])
        grad = (
            key_grad * (1.0 - vec[14:15])
            + recv_grad * (1.0 - vec[15:16])
            + rows_below(shifted, below)
        )
        out = upstream + norm_back(grad, vec[12:13], normal, scale[:, :1])
        cols = padded(
            [
                column_sum(grad * normal),
                column_sum(grad),
                column_sum(key_grad * delta),
                column_sum(recv_grad * delta),
            ]
        )
        return out, out, cols

    middle_grad, branch_grad, cols_two = local(
        norm_two_back,
        [whole, (step, width, BF16), (8, width, F32)],
        in_grads,
        neighbour(top_two, -1),
        upstream,
        normal_two,
        scale_two,
        delta_two,
        vec,
        scalar=last_flag,
    )

    bg_all = group_rows(branch_grad)
    (gated_grad,) = product(
        [(bg_all, w_rest, "nn", 2 * tiles)], [(everyone, part, F32)], lambda acc: (acc,)
    )
    gate_grad, wkv_grad, ends = call(
        gate_kernel,
        ins="tttttp",
        outs=[("t", BF16), ("t", F32), ("x", F32)],
        args=(gated_grad, gate_pre, wkv, receipt, log_decay, wkv_rows),
    )
    grad_total = dict(enumerate(ordered([ends[k, :SPAN] for k in range(size)])))
    after = [(jnp.ones((1, part), F32), jnp.zeros((SPAN, part), F32)) for _ in range(size)]
    open_bits = size - 1
    for mask, level in zip(all_masks, levels):
        if mask in masks:
            bit = 1 << masks.index(mask)
            for m in range(size):
                if not m & bit:
                    late = (m & open_bits) | bit
                    d, s = after[m]
                    after[m] = (d * level[late], d * grad_total[late] + s)
            grad_total = {
                g: grad_total[g] + level[g] * grad_total[g | bit]
                for g in grad_total
                if not g & bit
            }
            open_bits ^= bit
        else:
            groups = list(grad_total)
            got = trade(jnp.concatenate([grad_total[g] for g in groups], axis=0), mask)
            other = {g: got[i * SPAN : (i + 1) * SPAN] for i, g in enumerate(groups)}
            early = bit_of(me, mask) == 0
            for m in range(size):
                g = m & open_bits
                d, s = after[m]
                after[m] = pick(early, (d * level[g][1], d * other[g] + s), (d, s))
            grad_total = {
                g: jnp.where(
                    early,
                    grad_total[g] + level[g][0] * other[g],
                    other[g] + level[g][1] * grad_total[g],
                )
                for g in groups
            }
    grad_out = jnp.stack(ordered([s for _, s in after]))
    out_grads = team_products((bg_all, gated), (recv_all, rg_all), (mixed_all[3], gate_grad))
    grad_out, out_grads, val_pair = tie(grad_out, out_grads, val_pair)
    out_pair = square_sum(out_grads)

    first_grad = grad_total[0]
    holder = lax.div(me * rows, part)

    def rows_of(who):
        return lax.dynamic_slice_in_dim(first_grad, lax.rem(who * rows, part), rows, axis=1)

    handed = exchange([rows_of(jnp.bitwise_xor(me, flips(k))) for k in range(size)])
    state_rows = handed[0]
    for k in range(1, size):
        state_rows = jnp.where(holder == (member ^ k), handed[k], state_rows)
    initial_state_gradient = state_rows.T

    d_receipt, d_keys, d_values, d_decay, extra = call(
        backward_kernel,
        ins="tttttssp",
        outs=[("t", BF16)] * 4 + [("e", F32)],
        args=(receipt, keys, values, log_decay, wkv_grad, state_in, grad_out, wkv_rows),
    )
    grads = [d_keys, d_values, d_receipt, gate_grad]
    kept, sent = crossing_sum(
        *[(grads[c], w_rest if c > 1 else w_kv, c % 2) for c in range(4)]
    )
    main_grads = team_products(
        (mixed_all[0], d_keys), (mixed_all[1], d_values), (mixed_all[2], d_receipt)
    )
    val_sum = far_sum(val_pair)
    sent, main_grads, val_sum, key_pair = tie(sent, main_grads, val_sum, key_pair)
    main_pair = square_sum(main_grads)
    mixed_mine, mixed_more = group_sum(kept, sent)

    def latent_back(grad, up):
        kept, sent = halves(nn(grad, up))
        return jnp.concatenate(kept, axis=0), jnp.concatenate(sent, axis=0)

    latent_mine, latent_more = group_sum(
        *local(
            latent_back, [(2 * step, DRANK, F32), (2 * step, DRANK, BF16)], d_decay, w_dup
        )
    )
    rest_grad, delta_grad, top_one, cols_mix, down_grad, up_grad, ddown_grad = mixes_back(
        mixed_mine,
        mixed_more,
        latent_mine,
        latent_more,
        delta,
        mix_tanh,
        decay_tanh,
        blend,
        mixed_zero,
        w_down,
        w_up,
        w_ddown,
        vec,
    )
    def norm_one_back(last, rest, shifted, arrived, normal, scale, middle, vec):
        below = jnp.where(last == 1, jnp.zeros_like(arrived[:1]), arrived[:1])
        grad = rest + rows_below(shifted, below)
        out = middle + norm_back(grad, vec[0:1], normal, scale[:, :1])
        cols = padded([column_sum(grad * normal), column_sum(grad)])
        return take_lanes(out, from_spans), cols

    block_input_gradient, cols_one = local(
        norm_one_back,
        [whole, (8, width, F32)],
        rest_grad,
        delta_grad,
        neighbour(top_one, -1),
        normal_one,
        scale_one,
        middle_grad,
        vec,
        scalar=last_flag,
    )
    key_sum, out_sum, main_sum = [far_sum(p) for p in (key_pair, out_pair, main_pair)]

    def column_parts(value):
        return [value[:, c * part : (c + 1) * part] for c in range(3)]

    out_cols, main_cols = column_parts(out_sum), column_parts(main_sum)
    feedforward_gradient = hand_rows([[key_sum], [out_cols[1]], [val_sum]])
    mixing_gradient = hand_rows([[m] for m in main_cols] + [[out_cols[2]], [out_cols[0]]])


    def spread(value):
        zero = jnp.zeros((width, value.shape[1]), F32)
        return lax.dynamic_update_slice_in_dim(zero, value, member * part, axis=0)

    vec_low = jnp.concatenate([cols_one[:2], cols_mix[:6], cols_two[:4]], axis=0)
    vec_head = jnp.concatenate(
        [jnp.sum(extra[:, :2], axis=0), jnp.sum(ends[:, SPAN : SPAN + 2], axis=0)], axis=0
    )
    by_feature = jnp.concatenate([down_grad, up_grad, ddown_grad, vec_low.T], axis=1)
    low = cube_sum(to_cube(by_feature), BF16)
    by_channel = spread(jnp.concatenate([tn(d_decay, dh_all), vec_head.T], axis=1))
    high_part = cube_sum(by_channel.reshape(*[2] * len(all_masks), rows, -1), F32)
    lowrank_gradient = jnp.concatenate([low[:, :decay_up], high_part[:, :DRANK]], axis=1)
    vectors_gradient = jnp.concatenate(
        [low[:, decay_up : decay_up + 8], high_part[:, DRANK:], low[:, decay_up + 8 :]], axis=1
    )
    return (
        block_output.reshape(1, step, width),
        block_input_gradient.reshape(1, step, width),
        initial_state_gradient,
        mixing_gradient,
        lowrank_gradient,
        vectors_gradient,
        feedforward_gradient,
    )


def solution(mesh):
    rowwise = P("seq", None)
    tokenwise = P(None, "seq", None)
    return jax.shard_map(
        functools.partial(on_device, mesh.shape["seq"]),
        mesh=mesh,
        in_specs=(tokenwise, P(), rowwise, rowwise, rowwise, rowwise, rowwise, tokenwise),
        out_specs=(tokenwise, tokenwise, rowwise, rowwise, rowwise, rowwise, rowwise),
        check_vma=False,
    )
```

```python
import functools

import jax
import jax.numpy as jnp
from jax import lax
from jax.experimental import pallas as pl
from jax.experimental.pallas import tpu as pltpu
from jax.sharding import PartitionSpec as P

HEADS = 32
SPAN = 64
FF = 7168
RANK = 32
DRANK = 64
LN_EPS = 1e-05
GN_EPS = 0.00064

F32 = jnp.float32
BF16 = jnp.bfloat16
HI = lax.Precision.HIGHEST


def nn(a, b):
    return jnp.dot(a, b, preferred_element_type=F32)


def nt(a, b):
    return lax.dot_general(a, b, (((1,), (1,)), ((), ())), preferred_element_type=F32)


def tn(a, b):
    return lax.dot_general(a, b, (((0,), (0,)), ((), ())), preferred_element_type=F32)


def knn(a, b):
    return lax.dot_general(
        a, b, (((1,), (0,)), ((), ())), preferred_element_type=F32
    )


def knt(a, b):
    return lax.dot_general(
        a, b, (((1,), (1,)), ((), ())), preferred_element_type=F32
    )


def ktn(a, b):
    return lax.dot_general(
        a, b, (((0,), (0,)), ((), ())), preferred_element_type=F32
    )


def low_lanes(shape):
    return lax.broadcasted_iota(jnp.int32, shape, len(shape) - 1) < SPAN


def head_sum(x):
    low = low_lanes(x.shape)
    s0 = jnp.sum(jnp.where(low, x, 0.0), axis=-1, keepdims=True)
    s1 = jnp.sum(jnp.where(low, 0.0, x), axis=-1, keepdims=True)
    return jnp.where(low, s0, s1)


def two_rows(x):
    low = low_lanes(x.shape)
    return jnp.concatenate([jnp.where(low, x, 0.0), jnp.where(low, 0.0, x)], axis=0)


def fold(full):
    return jnp.where(low_lanes((SPAN, 2 * SPAN)), full[:SPAN], full[SPAN:])


def unfold(state):
    low = low_lanes(state.shape)
    return jnp.concatenate([jnp.where(low, state, 0.0), jnp.where(low, 0.0, state)], axis=0)


def running(w, upper=False):
    count = w.shape[0]
    row = lax.broadcasted_iota(jnp.int32, (count, count), 0)
    col = lax.broadcasted_iota(jnp.int32, (count, count), 1)
    keep = (col >= row) if upper else (col <= row)
    return lax.dot_general(
        jnp.where(keep, 1.0, 0.0).astype(F32),
        w,
        (((1,), (0,)), ((), ())),
        precision=HI,
        preferred_element_type=F32,
    )


def strict(count):
    row = lax.broadcasted_iota(jnp.int32, (2 * count, count), 0)
    col = lax.broadcasted_iota(jnp.int32, (2 * count, count), 1)
    row = jnp.where(row >= count, row - count, row)
    return row > col, row == col


def affinity(r, k, u, q, ks):
    count = r.shape[0]
    below, diag = strict(count)
    raw = knt(two_rows(q), ks)
    share = jnp.sum(two_rows(r * u * k), axis=-1, keepdims=True)
    return jnp.where(below, raw, jnp.where(diag, share, 0.0))


def totals_kernel(k_ref, v_ref, w_ref, out_ref):
    cum = running(w_ref[...])
    total = cum[-1:, :]
    kc = k_ref[...] * jnp.exp(total - cum)
    out_ref[0, :SPAN, :] = fold(ktn(v_ref[...], kc))
    out_ref[0, SPAN:, :] = jnp.broadcast_to(jnp.exp(total), (8, 2 * SPAN))


def group_norm(y, gain, bias):
    centred = y - head_sum(y) * (1.0 / SPAN)
    spread = head_sum(centred * centred) * (1.0 / SPAN)
    scale = lax.rsqrt(spread + GN_EPS)
    normal = centred * scale
    return normal, scale, normal * gain + bias


def forward_kernel(r_ref, k_ref, v_ref, w_ref, g_ref, s_ref, p_ref, y_ref, gated_ref):
    r, k, v, w = r_ref[...], k_ref[...], v_ref[...], w_ref[...]
    cum = running(w)
    q = r * jnp.exp(cum - w)
    ks = k * jnp.exp(-cum)
    aff = affinity(r, k, p_ref[0:1, :], q, ks)
    count = r.shape[0]
    v2 = two_rows(v)
    y = (
        knt(q, unfold(s_ref[0]))
        + knn(aff[:count], v2[:count])
        + knn(aff[count:], v2[count:])
    )
    y_ref[...] = y
    gate = g_ref[...]
    _, _, grouped = group_norm(y, p_ref[1:2, :], p_ref[2:3, :])
    gated_ref[...] = (grouped * gate * jax.nn.sigmoid(gate)).astype(BF16)


def gate_kernel(gg_ref, g_ref, y_ref, r_ref, w_ref, p_ref, gate_ref, dy_ref, out_ref):
    gated_grad, gate, y = gg_ref[...], g_ref[...], y_ref[...]
    gain = p_ref[1:2, :]
    normal, scale, grouped = group_norm(y, gain, p_ref[2:3, :])
    sig = jax.nn.sigmoid(gate)
    gate_ref[...] = (gated_grad * grouped * sig * (1.0 + gate * (1.0 - sig))).astype(BF16)
    outer = gated_grad * gate * sig
    inner = outer * gain
    dy = scale * (
        inner
        - head_sum(inner) * (1.0 / SPAN)
        - normal * (head_sum(inner * normal) * (1.0 / SPAN))
    )
    dy_ref[...] = dy
    w = w_ref[...]
    q = r_ref[...] * jnp.exp(running(w) - w)
    out_ref[0, :SPAN, :] = fold(ktn(dy, q))
    gain_grad = jnp.sum(outer * normal, axis=0, keepdims=True)
    bias_grad = jnp.sum(outer, axis=0, keepdims=True)
    out_ref[0, SPAN:, :] = jnp.concatenate(
        [gain_grad, bias_grad, jnp.zeros((6, 2 * SPAN), F32)], axis=0
    )


def backward_kernel(
    r_ref, k_ref, v_ref, w_ref, dy_ref, s_ref, gs_ref, p_ref,
    dr_ref, dk_ref, dv_ref, dd_ref, out_ref,
):
    r, k, v, w, dy = r_ref[...], k_ref[...], v_ref[...], w_ref[...], dy_ref[...]
    u = p_ref[0:1, :]
    count = r.shape[0]
    cum = running(w)
    total = cum[-1:, :]
    e_before, e_minus, e_carry = jnp.exp(cum - w), jnp.exp(-cum), jnp.exp(total - cum)
    q, ks, kc = r * e_before, k * e_minus, k * e_carry
    aff = affinity(r, k, u, q, ks)
    below, _ = strict(count)
    dy2 = two_rows(dy)
    d_aff = jnp.where(below, knt(dy2, v), 0.0)
    own = head_sum(dy * v)
    state, grad_state = s_ref[0], gs_ref[0]
    state2, grad2 = unfold(state), unfold(grad_state)
    ks2 = two_rows(ks)
    dq = knn(dy, state2) + knn(d_aff[:count], ks2[:count]) + knn(d_aff[count:], ks2[count:])
    dks = ktn(d_aff, two_rows(q))
    dkc = knn(v, grad2)
    dv_ref[...] = (ktn(aff, dy2) + knt(kc, grad2)).astype(BF16)
    dr_ref[...] = (dq * e_before + own * u * k).astype(BF16)
    dk_ref[...] = (dks * e_minus + dkc * e_carry + own * u * r).astype(BF16)
    gq, gc = q * dq, kc * dkc
    d_total = jnp.sum(gc, axis=0, keepdims=True) + jnp.exp(total) * jnp.sum(
        state * grad_state, axis=0, keepdims=True
    )
    dw = running(gq - ks * dks - gc, upper=True) - gq + d_total
    term = dw * w
    dd_ref[...] = term.astype(BF16)
    out_ref[0] = jnp.concatenate(
        [
            jnp.sum(term, axis=0, keepdims=True),
            jnp.sum(own * r * k, axis=0, keepdims=True),
            jnp.zeros((6, 2 * SPAN), F32),
        ],
        axis=0,
    )


def block_call(kernel, chunks, step, width, ins, outs, args):
    lane = 2 * SPAN
    kinds = {
        "t": pl.BlockSpec((step, lane), lambda c, h: (c, h)),
        "s": pl.BlockSpec((1, SPAN, lane), lambda c, h: (c, 0, h)),
        "x": pl.BlockSpec((1, SPAN + 8, lane), lambda c, h: (c, 0, h)),
        "e": pl.BlockSpec((1, 8, lane), lambda c, h: (c, 0, h)),
        "p": pl.BlockSpec((8, lane), lambda c, h: (0, h)),
    }
    shapes = {
        "t": lambda d: jax.ShapeDtypeStruct((chunks * step, width), d),
        "x": lambda d: jax.ShapeDtypeStruct((chunks, SPAN + 8, width), d),
        "e": lambda d: jax.ShapeDtypeStruct((chunks, 8, width), d),
    }
    return pl.pallas_call(
        kernel,
        grid=(chunks, width // lane),
        in_specs=[kinds[kind] for kind in ins],
        out_specs=[kinds[kind] for kind, _ in outs],
        out_shape=[shapes[kind](dtype) for kind, dtype in outs],
        compiler_params=pltpu.CompilerParams(vmem_limit_bytes=48 * 1024 * 1024),
    )(*args)


def weight_grad(places, pairs, block):
    tokens, blocks = pairs[0][0].shape[0], places.shape[0]
    widths = [y.shape[1] for _, y in pairs]

    def kernel(_, *refs):
        at = 0
        for i, wide in enumerate(widths):
            refs[-1][0, :, at : at + wide] = tn(refs[2 * i][...], refs[2 * i + 1][...]).astype(
                BF16
            )
            at += wide

    specs = []
    for wide in widths:
        specs.append(pl.BlockSpec((tokens, block), lambda i, at: (0, at[i])))
        specs.append(pl.BlockSpec((tokens, wide), lambda i, at: (0, 0)))
    return pl.pallas_call(
        kernel,
        grid_spec=pltpu.PrefetchScalarGridSpec(
            num_scalar_prefetch=1,
            grid=(blocks,),
            in_specs=specs,
            out_specs=pl.BlockSpec((1, block, sum(widths)), lambda i, at: (i, 0, 0)),
        ),
        out_shape=jax.ShapeDtypeStruct((blocks, block, sum(widths)), BF16),
        compiler_params=pltpu.CompilerParams(vmem_limit_bytes=48 * 1024 * 1024),
    )(places, *[v for pair in pairs for v in pair])


def lanes_kernel(spans, x_ref, out_ref):
    at = 0
    for start, stop in spans:
        out_ref[:, at : at + stop - start] = x_ref[:, start:stop].astype(out_ref.dtype)
        at += stop - start


def move_lanes(spans, value, dtype):
    return pl.pallas_call(
        functools.partial(lanes_kernel, spans),
        in_specs=[pl.BlockSpec(memory_space=pltpu.VMEM)],
        out_specs=pl.BlockSpec(memory_space=pltpu.VMEM),
        out_shape=jax.ShapeDtypeStruct(value.shape, dtype),
        compiler_params=pltpu.CompilerParams(vmem_limit_bytes=32 * 1024 * 1024),
    )(value)


def place_kernel(counts, wide, block, at_ref, *refs):
    ins, out_ref, sems = refs[: len(counts)], refs[-2], refs[-1]
    rows = out_ref.shape[0]
    copies, i = [], 0
    for ref, n in zip(ins, counts):
        for j in range(n):
            start = pl.multiple_of(at_ref[i] * block, block)
            column = i * block // rows * wide
            copy = pltpu.make_async_copy(
                ref.at[pl.ds(j * block, block), :],
                out_ref.at[pl.ds(start, block), pl.ds(column, wide)],
                sems.at[i],
            )
            copy.start()
            copies.append(copy)
            i += 1
    for copy in copies:
        copy.wait()


def place_rows(parts, block):
    pieces = [p for part in parts for p in part[1]]
    wide = pieces[0].shape[1]
    at = jnp.concatenate([part[0] for part in parts])
    counts = [p.shape[0] // block for p in pieces]
    total = sum(counts)
    return pl.pallas_call(
        functools.partial(place_kernel, counts, wide, block),
        in_specs=[pl.BlockSpec(memory_space=pltpu.SMEM)]
        + [pl.BlockSpec(memory_space=pl.ANY)] * len(pieces),
        out_specs=pl.BlockSpec(memory_space=pl.ANY),
        out_shape=jax.ShapeDtypeStruct(
            (total * block // len(parts), wide * len(parts)), pieces[0].dtype
        ),
        scratch_shapes=[pltpu.SemaphoreType.DMA((total,))],
        compiler_params=pltpu.CompilerParams(vmem_limit_bytes=32 * 1024 * 1024),
    )(at, *pieces)


def mixes_kernel(
    open_ref, x_ref, before_ref, vec_ref, down_ref, up_ref, ddown_ref,
    m1_ref, m2_ref, m3_ref, m4_ref, dh_ref,
    normal_ref, scale_ref, delta_ref, blend_ref, m0_ref, tanh_ref, dtanh_ref,
):
    piece = pl.program_id(0)
    step = m1_ref.shape[0]
    x = x_ref[...].astype(F32)
    centred = x - jnp.mean(x, axis=-1, keepdims=True)
    scale = lax.rsqrt(jnp.mean(centred * centred, axis=-1, keepdims=True) + LN_EPS)
    normal = centred * scale
    full = normal * vec_ref[0:1, :] + vec_ref[1:2, :]
    normed = full[:step]
    first = jnp.where(open_ref[piece] == 1, before_ref[0:1, :], full[step : step + 1])
    row = lax.broadcasted_iota(jnp.int32, normed.shape, 0)
    delta = jnp.where(row == 0, first, pltpu.roll(normed, 1, 0)) - normed
    blend = (normed + delta * vec_ref[2:3, :]).astype(BF16)
    tanh = jnp.tanh(nn(blend, down_ref[...]))
    latent = tanh.astype(BF16)
    lane = lax.broadcasted_iota(jnp.int32, latent.shape, 1)
    mixed = []
    for c in range(5):
        own = (lane >= c * RANK) & (lane < (c + 1) * RANK)
        offset = nt(jnp.where(own, latent, jnp.zeros_like(latent)), up_ref[...])
        mixed.append((normed + delta * (vec_ref[3 + c : 4 + c, :] + offset)).astype(BF16))
    dtanh = jnp.tanh(nn(mixed[0], ddown_ref[...]))
    m1_ref[...], m2_ref[...], m3_ref[...], m4_ref[...] = mixed[1:]
    dh_ref[...] = dtanh.astype(BF16)

    @pl.when(piece == 0)
    def _():
        normal_ref[...] = normal[:step]
        scale_ref[...] = jnp.broadcast_to(scale[:step], scale_ref.shape)
        delta_ref[...] = delta
        blend_ref[...] = blend
        m0_ref[...] = mixed[0]
        tanh_ref[...] = tanh
        dtanh_ref[...] = dtanh


def group_mixes(opening, x, before, vec, down, up, ddown, step):
    high, width = step + 16, x.shape[1]
    pieces = x.shape[0] // high

    def whole(value):
        return pl.BlockSpec(value.shape, lambda k: (0, 0))

    def own(columns, dtype):
        return (
            pl.BlockSpec((step, columns), lambda k: (0, 0)),
            jax.ShapeDtypeStruct((step, columns), dtype),
        )

    def every(columns, dtype):
        return (
            pl.BlockSpec((step, columns), lambda k: ((k % 2) * 2 + k // 2, 0)),
            jax.ShapeDtypeStruct((pieces * step, columns), dtype),
        )

    outs = [every(width, BF16)] * 4 + [
        every(DRANK, BF16),
        own(width, F32),
        own(128, F32),
        own(width, F32),
        own(width, BF16),
        own(width, BF16),
        own(5 * RANK, F32),
        own(DRANK, F32),
    ]
    return pl.pallas_call(
        mixes_kernel,
        grid=(pieces,),
        in_specs=[
            pl.BlockSpec(memory_space=pltpu.SMEM),
            pl.BlockSpec((high, width), lambda k: (k, 0)),
            whole(before),
            whole(vec),
            whole(down),
            whole(up),
            whole(ddown),
        ],
        out_specs=[o[0] for o in outs],
        out_shape=[o[1] for o in outs],
        compiler_params=pltpu.CompilerParams(vmem_limit_bytes=56 * 1024 * 1024),
    )(opening, x, before, vec, down, up, ddown)


def product(pairs, outs, body, sides=(), tile=256):
    count = len(pairs)

    def kernel(*refs):
        ins, out_refs = refs[: 2 * count + len(sides)], refs[2 * count + len(sides) :]
        products = [
            (nn if pair[2] == "nn" else nt)(ins[2 * i][...], ins[2 * i + 1][...])
            for i, pair in enumerate(pairs)
        ]
        results = body(*products, *[r[...] for r in ins[2 * count :]])
        for ref, value in zip(out_refs, results):
            ref[...] = value.astype(ref.dtype)

    specs, args = [], []
    for a, b, form, at in pairs:
        depth = a.shape[1]
        specs.append(pl.BlockSpec(a.shape, lambda j: (0, 0)))
        if form == "nn":
            specs.append(pl.BlockSpec((depth, tile), lambda j, at=at: (0, at + j)))
        else:
            specs.append(pl.BlockSpec((tile, depth), lambda j, at=at: (j, at)))
        args += [a, b]
    for side in sides:
        specs.append(pl.BlockSpec((side.shape[0], tile), lambda j: (0, j)))
    return pl.pallas_call(
        kernel,
        grid=(outs[0][1] // tile,),
        in_specs=specs,
        out_specs=[pl.BlockSpec((o[0], tile), lambda j: (0, j)) for o in outs],
        out_shape=[jax.ShapeDtypeStruct(o[:2], o[2]) for o in outs],
        compiler_params=pltpu.CompilerParams(vmem_limit_bytes=56 * 1024 * 1024),
    )(*args, *sides)


def local(fn, outs, *args, scalar=None):
    def kernel(*refs):
        lead = [] if scalar is None else [refs[0]]
        ins, out_refs = refs[len(lead) : -len(outs)], refs[-len(outs) :]
        results = fn(*[r[0] for r in lead], *[r[...] for r in ins])
        for ref, value in zip(out_refs, results):
            ref[...] = value.astype(ref.dtype)

    specs = [pl.BlockSpec(memory_space=pltpu.VMEM)] * len(args)
    if scalar is not None:
        specs = [pl.BlockSpec(memory_space=pltpu.SMEM)] + specs
        args = (scalar.reshape(1), *args)
    return pl.pallas_call(
        kernel,
        in_specs=specs,
        out_specs=[pl.BlockSpec(memory_space=pltpu.VMEM)] * len(outs),
        out_shape=[jax.ShapeDtypeStruct(o[:2], o[2]) for o in outs],
        compiler_params=pltpu.CompilerParams(vmem_limit_bytes=56 * 1024 * 1024),
    )(*args)


def take_lanes(value, spans):
    if len(spans) == 1:
        return value
    return jnp.concatenate([value[:, a:b] for a, b in spans], axis=1)


def norm_back(grad, gain, normal, scale):
    e = grad * gain
    return scale * (
        e
        - jnp.mean(e, axis=-1, keepdims=True)
        - normal * jnp.mean(e * normal, axis=-1, keepdims=True)
    )


def rows_above(value, first):
    row = lax.broadcasted_iota(jnp.int32, value.shape, 0)
    return jnp.where(row == 0, first, pltpu.roll(value, 1, 0))


def rows_below(value, last):
    row = lax.broadcasted_iota(jnp.int32, value.shape, 0)
    high = value.shape[0]
    return jnp.where(row == high - 1, last, pltpu.roll(value, high - 1, 0))


def padded(rows):
    return jnp.concatenate(
        list(rows) + [jnp.zeros((8 - len(rows), rows[0].shape[1]), F32)], axis=0
    )


def column_sum(value):
    return jnp.sum(value, axis=0, keepdims=True)


def gates_kernel(
    spans, who_ref, middle_ref, value_ref, more_ref, act_ref, cot_ref,
    out_ref, up_ref, vg_ref, rg_ref, held,
):
    to_spans, from_spans = spans
    step, part = act_ref.shape[0] // 4, act_ref.shape[1]
    who = who_ref[0]
    act = [
        act_ref[pl.ds(pl.multiple_of((who ^ j) * step, step), step), :] for j in range(4)
    ]
    recept = jax.nn.sigmoid(take_lanes(jnp.concatenate(act, axis=1).astype(F32), to_spans))
    value = value_ref[...] + more_ref[...].astype(F32)
    out = middle_ref[...] + recept * value
    out_ref[...] = take_lanes(out, from_spans).astype(BF16)
    up = take_lanes(cot_ref[...].astype(F32), to_spans)
    up_ref[...] = up
    vg_ref[...] = (up * recept).astype(BF16)
    held[...] = take_lanes(up * value * recept * (1.0 - recept), from_spans)
    for k in range(4):
        at = pl.multiple_of((who ^ k) * part, part)
        rg_ref[k * step : (k + 1) * step, :] = held[:, pl.ds(at, part)].astype(BF16)


def gates(spans, who, middle, value, more, act, cot):
    step, width = middle.shape
    part = act.shape[1]
    shape = jax.ShapeDtypeStruct
    return pl.pallas_call(
        functools.partial(gates_kernel, spans),
        in_specs=[pl.BlockSpec(memory_space=pltpu.SMEM)]
        + [pl.BlockSpec(memory_space=pltpu.VMEM)] * 5,
        out_specs=[pl.BlockSpec(memory_space=pltpu.VMEM)] * 4,
        out_shape=[
            shape((step, width), BF16),
            shape((step, width), F32),
            shape((step, width), BF16),
            shape((4 * step, part), BF16),
        ],
        scratch_shapes=[pltpu.VMEM((step, width), F32)],
        compiler_params=pltpu.CompilerParams(vmem_limit_bytes=56 * 1024 * 1024),
    )(who.reshape(1), middle, value, more, act, cot)


def mixes_back_kernel(
    kept_ref, got_ref, dl_ref, dl_more_ref, delta_ref, tanh_ref, dtanh_ref, blend_ref, m0_ref,
    down_ref, up_ref, ddown_ref, vec_ref,
    rest_ref, dg_ref, row_ref, cols_ref, down_out, up_out, ddown_out,
):
    step = delta_ref.shape[0]
    dtanh = dtanh_ref[...]
    decay_grad = dl_ref[...] + dl_more_ref[...].astype(F32)
    decay_pre = (decay_grad * (1.0 - dtanh * dtanh)).astype(BF16)
    ddown_out[...] = tn(m0_ref[...], decay_pre)
    tanh = tanh_ref[...]
    latent = tanh.astype(BF16)
    lane = lax.broadcasted_iota(jnp.int32, latent.shape, 1)
    delta, up = delta_ref[...], up_ref[...]
    latent_grad = jnp.zeros(latent.shape, F32)
    up_grad = jnp.zeros(up_out.shape, F32)
    dg = jnp.zeros(delta.shape, F32)
    total = jnp.zeros(delta.shape, F32)
    cols = []
    for c in range(5):
        own = (lane >= c * RANK) & (lane < (c + 1) * RANK)
        mine = jnp.where(own, latent, jnp.zeros_like(latent))
        if c == 0:
            grad = nt(decay_pre, ddown_ref[...])
        else:
            at = slice((c - 1) * step, c * step)
            grad = kept_ref[at, :] + got_ref[at, :].astype(F32)
        shift = grad * delta
        cols.append(column_sum(shift))
        offset = shift.astype(BF16)
        latent_grad = jnp.where(own, nn(offset, up), latent_grad)
        up_grad = up_grad + tn(offset, mine)
        dg = dg + grad * (vec_ref[3 + c : 4 + c, :] + nt(mine, up))
        total = total + grad
    up_out[...] = up_grad
    mix_pre = (latent_grad * (1.0 - tanh * tanh)).astype(BF16)
    down_out[...] = tn(blend_ref[...], mix_pre)
    blend_grad = nt(mix_pre, down_ref[...])
    dg = dg + blend_grad * vec_ref[2:3, :]
    rest_ref[...] = total + blend_grad - dg
    dg_ref[...] = dg
    row_ref[...] = dg[:8]
    cols_ref[...] = padded([column_sum(blend_grad * delta)] + cols)


def mixes_back(*args):
    delta, down, ddown = args[4], args[9], args[11]
    step, width = delta.shape
    shape = jax.ShapeDtypeStruct
    outs = [
        shape((step, width), F32),
        shape((step, width), F32),
        shape((8, width), F32),
        shape((8, width), F32),
        shape(down.shape, F32),
        shape(down.shape, F32),
        shape(ddown.shape, F32),
    ]
    return pl.pallas_call(
        mixes_back_kernel,
        in_specs=[pl.BlockSpec(memory_space=pltpu.VMEM)] * len(args),
        out_specs=[pl.BlockSpec(memory_space=pltpu.VMEM)] * len(outs),
        out_shape=outs,
        compiler_params=pltpu.CompilerParams(vmem_limit_bytes=60 * 1024 * 1024),
    )(*args)


def tie(*values):
    return lax.optimization_barrier(values)


def on_device(
    count,
    tokens,
    previous,
    initial_state,
    mixing_weights,
    lowrank_weights,
    vectors,
    feedforward_weights,
    cotangent,
):
    fast = initial_state.shape[0] == 64
    masks = (1, 8) if fast else (1, 2)
    size = 1 << len(masks)
    teams = count // size
    all_masks = [1 << b for b in range(count.bit_length() - 1)]
    team_masks = [b for b in all_masks if b not in masks]
    far = 16
    team_masks.sort(key=lambda b: fast and b != far)
    me = lax.axis_index("seq")
    _, step, width = tokens.shape
    rows = mixing_weights.shape[0]
    part = width // size
    ff_part = FF // size
    team_rows = rows * size
    def bit_of(who, mask):
        return (who // mask) % 2 if isinstance(who, int) else lax.rem(lax.div(who, mask), 2)

    def member_of(who):
        return sum(bit_of(who, b) << j for j, b in enumerate(masks))

    def team_of(who):
        return sum(bit_of(who, b) << j for j, b in enumerate(team_masks))

    member, team = member_of(me), team_of(me)
    order = sorted(range(count), key=lambda d: (team_of(d), member_of(d)))
    inverse = sorted(range(count), key=lambda p: order[p])
    across = [order[m::size] for m in range(size)]
    square = [order[m :: 2 * size] for m in range(2 * size)]
    def lane_spans(blocks):
        spans = []
        for d in blocks:
            if spans and spans[-1][1] == d * rows:
                spans[-1][1] = (d + 1) * rows
            else:
                spans.append([d * rows, (d + 1) * rows])
        return spans

    to_spans, from_spans = lane_spans(order), lane_spans(inverse)

    def to_places(value, dtype):
        return move_lanes(to_spans, value, dtype)

    def flips(k):
        return sum(b for j, b in enumerate(masks) if (k >> j) & 1)

    def trade(value, mask):
        return lax.ppermute(value, "seq", [(d, d ^ mask) for d in range(count)])

    def group_gather(value):
        side = trade(value, masks[1])
        return value, side, trade(jnp.concatenate([value, side], axis=0), masks[0])

    def group_rows(value):
        high, columns = value.shape

        def lay(own, side, far):
            return (jnp.concatenate([own, far[:high], side, far[high:]], axis=0),)

        return local(lay, [(size * high, columns, value.dtype)], *group_gather(value))[0]

    def halves(value):
        cut = [value[k * step : (k + 1) * step] for k in range(size)]
        return [cut[0], cut[2]], [cut[1], cut[3]]

    def group_sum(kept, sent):
        high, columns = kept.shape[0] // 2, kept.shape[1]
        got = trade(sent, masks[0])

        def add(mine, more):
            total = mine + more.astype(F32)
            return total[:high], total[high:]

        mine, side = local(add, [(high, columns, F32), (high, columns, BF16)], kept, got)
        return mine, trade(side, masks[1])

    def crossing_sum(*pairs):
        units = len(pairs)

        def body(*products):
            parts = [halves(p) for p in products]
            kept = [p[0][i] for i in range(2) for p in parts]
            sent = [p[1][i] for i in range(2) for p in parts]
            return jnp.concatenate(kept, axis=0), jnp.concatenate(sent, axis=0)

        high = 2 * units * step
        return product(
            [(a, b, "nt", at) for a, b, at in pairs],
            [(high, width, F32), (high, width, BF16)],
            body,
        )

    def exchange(pieces):
        pieces, high = list(pieces), pieces[0].shape[0]
        for j in reversed(range(len(masks))):
            keys = [k for k in range(size) if (k >> j) & 1]
            got = trade(jnp.concatenate([pieces[k] for k in keys], axis=0), masks[j])
            for i, k in enumerate(keys):
                pieces[k] = got[i * high : (i + 1) * high]
        return pieces

    def ordered(pieces):
        pieces = list(pieces)
        for j in range(len(masks)):
            swap = lax.rem(lax.div(member, 1 << j), 2) == 1
            pieces = [
                jnp.where(swap, pieces[k ^ (1 << j)], pieces[k]) for k in range(len(pieces))
            ]
        return pieces

    def neighbour(value, offset):
        pairs = [(d, d + offset) for d in range(count) if 0 <= d + offset < count]
        return lax.ppermute(value, "seq", pairs)

    def take_columns(value, spans, who):
        return jnp.concatenate(
            [
                lax.dynamic_slice_in_dim(value, start + who * wide, wide, axis=1)
                for start, wide in spans
            ],
            axis=1,
        )

    def group_columns(value, spans):
        pieces = [take_columns(value, spans, member ^ k) for k in range(size)]
        return jnp.concatenate(ordered(exchange(pieces)), axis=0)

    def crossing(first):
        bits = list(range(1, len(team_masks))) + [0]
        if first:
            bits[0], bits[1] = bits[1], bits[0]
        return bits

    def gather_rows(own):
        return lax.all_gather(own, "seq", axis=0, tiled=True, axis_index_groups=across)

    def far_pair(own):
        if not fast:
            return own
        got = trade(own, far)
        upper = bit_of(me, far) == 1
        return jnp.concatenate(
            [jnp.where(upper, got, own), jnp.where(upper, own, got)], axis=0
        )

    def cross_rows(own):
        if not fast:
            return gather_rows(own)
        cut = own.shape[1] // 2
        parts = []
        for first, piece in ((False, own[:, :cut]), (True, own[:, cut:])):
            pieces, places = [piece], [0]
            for bit in reversed(crossing(first)):
                joint = pieces[0] if len(pieces) == 1 else jnp.concatenate(pieces, axis=0)
                pieces.append(trade(joint, team_masks[bit]))
                places = places + [p | (1 << bit) for p in places]
            parts.append((jnp.bitwise_xor(jnp.asarray(places, jnp.int32), team), pieces))
        return place_rows(parts, team_rows)

    def gather_square(paired):
        groups = square if fast else across
        return lax.all_gather(paired, "seq", axis=0, tiled=True, axis_index_groups=groups)

    def team_products(*pairs):
        if fast:
            places = jnp.arange(teams, dtype=jnp.int32)
            return weight_grad(places, pairs, team_rows).reshape(width, -1)
        return jnp.concatenate([tn(x, y).astype(BF16) for x, y in pairs], axis=1)

    def square_sum(grads):
        groups = square if fast else across
        return lax.psum_scatter(
            grads, "seq", scatter_dimension=0, tiled=True, axis_index_groups=groups
        )

    def far_sum(pair):
        if not fast:
            return pair
        bit = bit_of(me, far)
        sent = lax.dynamic_slice_in_dim(pair, (1 - bit) * team_rows, team_rows, axis=0)
        kept = lax.dynamic_slice_in_dim(pair, bit * team_rows, team_rows, axis=0)
        return (kept.astype(F32) + trade(sent, far).astype(F32)).astype(BF16)

    def cube_gather(value, follower=None):
        for mask in reversed(all_masks):
            got = trade(value, mask)
            upper = bit_of(me, mask) == 1
            value = jnp.stack([jnp.where(upper, got, value), jnp.where(upper, value, got)])
            if mask == 8 and follower is not None:
                value, follower = tie(value, follower)
        axes = len(all_masks)
        cube = value.transpose(*reversed(range(axes)), *range(axes, value.ndim))
        return cube if follower is None else (cube, follower)

    place_axes = [all_masks[::-1].index(b) for b in team_masks[::-1] + list(masks[::-1])]

    def by_place(cube):
        rest = range(len(all_masks), cube.ndim)
        return cube.transpose(*place_axes, *rest).reshape(width, -1)

    def to_cube(value):
        cube = value.reshape(*[2] * len(place_axes), rows, -1)
        back = [place_axes.index(a) for a in range(len(place_axes))]
        return cube.transpose(*back, len(back), len(back) + 1)

    def cube_sum(cube, kind):
        for axis, mask in reversed(list(enumerate(reversed(all_masks)))):
            bit = bit_of(me, mask)
            sent = lax.dynamic_index_in_dim(cube, 1 - bit, axis, keepdims=False)
            kept = lax.dynamic_index_in_dim(cube, bit, axis, keepdims=False)
            cube = kept.astype(F32) + trade(sent.astype(kind), mask).astype(F32)
        return cube

    def hand_rows(pieces):
        widths = [sum(p.shape[1] for p in piece) for piece in pieces]
        joint = jnp.concatenate([p for piece in pieces for p in piece], axis=1)
        mine = [
            lax.dynamic_slice_in_dim(joint, (member ^ k) * rows, rows, axis=0)
            for k in range(size)
        ]
        by_member = ordered(exchange(mine))
        outs, start = [], 0
        for wide in widths:
            outs += [p[:, start : start + wide] for p in by_member]
            start += wide
        return jnp.concatenate(outs, axis=1).astype(F32)

    up_start, decay_start, decay_up = 5 * RANK, 10 * RANK, 10 * RANK + DRANK
    last_row = neighbour(tokens[0, -1:, :], 1)
    tokens_sent = to_places(
        jnp.concatenate([tokens[0], jnp.broadcast_to(last_row, (16, width))], axis=0), BF16
    )
    natural, mix_in = cube_gather(
        jnp.concatenate(
            [vectors, initial_state, lowrank_weights[:, decay_up:].astype(F32)], axis=1
        ),
        mixing_weights,
    )
    natural = natural.reshape(width, -1)
    low_cube, mix_in = cube_gather(lowrank_weights[:, :decay_up], mix_in)
    tokens_all = jnp.concatenate(group_gather(tokens_sent), axis=0)
    mix_local = group_columns(mix_in, [(c * width, part) for c in range(5)])
    mix_local, natural, low_cube, tokens_all = tie(mix_local, natural, low_cube, tokens_all)
    lowrank = by_place(low_cube)
    kv_pair, mix_rest = tie(far_pair(mix_local[:, : 2 * part]), mix_local[:, 2 * part :])
    rest_pair, feed_in = tie(far_pair(mix_rest), feedforward_weights)
    ff_spans = [(0, ff_part), (FF, part), (FF + width, ff_part)]
    ff_local = group_columns(feed_in, ff_spans)
    ff_near, ff_tail = ff_local[:, : ff_part + part], ff_local[:, ff_part + part :]
    w_kv = gather_square(kv_pair)
    w_rest = gather_square(rest_pair)
    tiles = part // 256

    mine = lax.dynamic_slice_in_dim(natural, member * part, part, axis=0)
    vec_part = mine[:, :16].T
    first_state = mine[:, 16 : 16 + SPAN].T
    w_dup = mine[:, 16 + SPAN :].astype(BF16)
    vec = by_place(
        natural[:, :16].reshape(*[2] * len(all_masks), rows, 16)
    ).T
    wkv_rows = jnp.concatenate([vec_part[9:12], jnp.zeros((5, part), F32)], axis=0)
    is_first = (me == 0).astype(jnp.int32)
    before = to_places(previous.reshape(2, width), F32)
    w_down, w_up = lowrank[:, :up_start], lowrank[:, up_start:decay_start]
    w_ddown = lowrank[:, decay_start:]

    opening = jnp.stack(
        [jnp.bitwise_xor(me, flips(k)) == 0 for k in (0, 2, 1, 3)]
    ).astype(jnp.int32)
    (
        *mixed_all, dh_all, normal_one, scale_one, delta, blend, mixed_zero, mix_tanh, decay_tanh,
    ) = group_mixes(opening, tokens_all, before, vec, w_down, w_up, w_ddown, step)
    everyone = size * step
    (log_decay,) = product(
        [(dh_all, w_dup, "nt", 0)],
        [(everyone, part, F32)],
        lambda acc, base: (-jnp.exp(base + acc),),
        sides=(vec_part[8:9],),
    )
    keys, values = product(
        [(mixed_all[0], w_kv, "nn", 0), (mixed_all[1], w_kv, "nn", tiles)],
        [(everyone, part, F32)] * 2,
        lambda a, b: (a, b),
    )

    keys, ff_near = tie(keys, ff_near)
    near_pair = far_pair(ff_near)

    call = functools.partial(block_call, chunks=size, step=step, width=part)
    (totals,) = call(
        totals_kernel, ins="ttt", outs=[("x", F32)], args=(keys, values, log_decay)
    )
    by_member = ordered([totals[k] for k in range(size)])
    total = {m: (p[SPAN : SPAN + 1], p[:SPAN]) for m, p in enumerate(by_member)}
    before_chunk = [
        (jnp.ones((1, part), F32), jnp.zeros((SPAN, part), F32)) for _ in range(size)
    ]
    open_bits = size - 1
    levels = []

    def chain(early, late):
        return early[0] * late[0], late[0] * early[1] + late[1]

    def pick(flag, yes, no):
        return tuple(jnp.where(flag, a, b) for a, b in zip(yes, no))

    for mask in all_masks:
        if mask in masks:
            bit = 1 << masks.index(mask)
            levels.append({g: total[g][0] for g in total})
            for m in range(size):
                if m & bit:
                    early = (m & open_bits) ^ bit
                    before_chunk[m] = chain(total[early], before_chunk[m])
            total = {g: chain(total[g], total[g | bit]) for g in total if not g & bit}
            open_bits ^= bit
        else:
            groups = list(total)
            sent = jnp.concatenate(
                [
                    jnp.concatenate(
                        [total[g][1], jnp.broadcast_to(total[g][0], (8, part))], axis=0
                    )
                    for g in groups
                ],
                axis=0,
            )
            got = trade(sent, mask)
            high = SPAN + 8
            other = {
                g: (got[i * high + SPAN : i * high + SPAN + 1], got[i * high : i * high + SPAN])
                for i, g in enumerate(groups)
            }
            levels.append({g: (total[g][0], other[g][0]) for g in groups})
            late = bit_of(me, mask) == 1
            for m in range(size):
                g = m & open_bits
                before_chunk[m] = pick(late, chain(other[g], before_chunk[m]), before_chunk[m])
            total = {
                g: pick(late, chain(other[g], total[g]), chain(total[g], other[g]))
                for g in groups
            }
    state_in = jnp.stack(ordered([d * first_state + s for d, s in before_chunk]))
    state_in, near_pair = tie(state_in, near_pair)
    w_near = gather_square(near_pair)
    w_key, w_rec = w_near, w_near[:, ff_part:]

    receipt, gate_pre = product(
        [(mixed_all[2], w_rest, "nn", 0), (mixed_all[3], w_rest, "nn", tiles)],
        [(everyone, part, F32)] * 2,
        lambda a, b: (a, b),
    )
    wkv, gated = call(
        forward_kernel,
        ins="tttttsp",
        outs=[("t", F32), ("t", BF16)],
        args=(receipt, keys, values, log_decay, gate_pre, state_in, wkv_rows),
    )
    gated, ff_tail = tie(gated, ff_tail)
    w_val = cross_rows(ff_tail)
    branch, branch_more = group_sum(*crossing_sum((gated, w_rest, 2)))

    def norm_two(hidden, mine, more, vec):
        middle = hidden[:step].astype(F32) + mine + more.astype(F32)
        centred = middle - jnp.mean(middle, axis=-1, keepdims=True)
        scale = lax.rsqrt(jnp.mean(centred * centred, axis=-1, keepdims=True) + LN_EPS)
        normal = centred * scale
        tail = normal[step - 8 :] * vec[12:13] + vec[13:14]
        return middle, normal, jnp.broadcast_to(scale, (step, 128)), tail

    whole = (step, width, F32)
    middle, normal_two, scale_two, tail_two = local(
        norm_two,
        [whole, whole, (step, 128, F32), (8, width, F32)],
        tokens_sent,
        branch,
        branch_more,
        vec,
    )

    def mix_two(first, normal, arrived, before, vec):
        normed = normal * vec[12:13] + vec[13:14]
        above = jnp.where(first == 1, before[1:2], arrived[7:8])
        delta = rows_above(normed, above) - normed
        key_in, recv_in = normed + delta * vec[14:15], normed + delta * vec[15:16]
        return jnp.concatenate([key_in, recv_in], axis=0), delta

    both, delta_two = local(
        mix_two,
        [(2 * step, width, BF16), whole],
        normal_two,
        neighbour(tail_two, 1),
        before,
        vec,
        scalar=is_first,
    )

    key_all, recv_all = group_rows(both[:step]), group_rows(both[step:])
    relu, squared = product(
        [(key_all, w_key, "nn", 0)],
        [(everyone, ff_part, F32), (everyone, ff_part, BF16)],
        lambda acc: (jnp.maximum(acc, 0.0), jnp.square(jnp.maximum(acc, 0.0))),
    )
    (recept_act,) = product(
        [(recv_all, w_rec, "nn", 0)],
        [(everyone, part, BF16)],
        lambda acc: (acc,),
    )
    acts = exchange([recept_act[k * step : (k + 1) * step] for k in range(size)])
    value, value_more = group_sum(*crossing_sum((squared, w_val, 0)))
    block_output, upstream, value_grad, recept_grads = gates(
        (to_spans, from_spans),
        member,
        middle,
        value,
        value_more,
        jnp.concatenate(acts, axis=0),
        cotangent.reshape(step, width),
    )

    rg_all = jnp.concatenate(
        exchange([recept_grads[k * step : (k + 1) * step] for k in range(size)]), axis=0
    )
    vg_all = group_rows(value_grad)
    val_grads = team_products((vg_all, squared))
    vg_all, val_grads = tie(vg_all, val_grads)
    val_pair = square_sum(val_grads)
    (key_grad,) = product(
        [(vg_all, w_val, "nn", 0)],
        [(everyone, ff_part, BF16)],
        lambda acc, relu: (acc * (2.0 * relu),),
        sides=(relu,),
    )
    key_grads = team_products((key_all, key_grad))
    key_grad, key_grads = tie(key_grad, key_grads)
    key_pair = square_sum(key_grads)
    recv_two = group_sum(*crossing_sum((rg_all, w_rec, 0)))
    key_two = group_sum(*crossing_sum((key_grad, w_key, 0)))

    def inputs_back(key, key_more, recv, recv_more, vec):
        key, recv = key + key_more.astype(F32), recv + recv_more.astype(F32)
        top = key[:8] * vec[14:15] + recv[:8] * vec[15:16]
        return jnp.concatenate([key, recv], axis=0), top

    in_grads, top_two = local(
        inputs_back, [(2 * step, width, F32), (8, width, F32)], *key_two, *recv_two, vec
    )
    last_flag = (me == count - 1).astype(jnp.int32)

    def norm_two_back(last, grads, arrived, upstream, normal, scale, delta, vec):
        key_grad, recv_grad = grads[:step], grads[step:]
        shifted = key_grad * vec[14:15] + recv_grad * vec[15:16]
        below = jnp.where(last == 1, jnp.zeros_like(arrived[:1]), arrived[:1])
        grad = (
            key_grad * (1.0 - vec[14:15])
            + recv_grad * (1.0 - vec[15:16])
            + rows_below(shifted, below)
        )
        out = upstream + norm_back(grad, vec[12:13], normal, scale[:, :1])
        cols = padded(
            [
                column_sum(grad * normal),
                column_sum(grad),
                column_sum(key_grad * delta),
                column_sum(recv_grad * delta),
            ]
        )
        return out, out, cols

    middle_grad, branch_grad, cols_two = local(
        norm_two_back,
        [whole, (step, width, BF16), (8, width, F32)],
        in_grads,
        neighbour(top_two, -1),
        upstream,
        normal_two,
        scale_two,
        delta_two,
        vec,
        scalar=last_flag,
    )

    bg_all = group_rows(branch_grad)
    (gated_grad,) = product(
        [(bg_all, w_rest, "nn", 2 * tiles)], [(everyone, part, F32)], lambda acc: (acc,)
    )
    gate_grad, wkv_grad, ends = call(
        gate_kernel,
        ins="tttttp",
        outs=[("t", BF16), ("t", F32), ("x", F32)],
        args=(gated_grad, gate_pre, wkv, receipt, log_decay, wkv_rows),
    )
    grad_total = dict(enumerate(ordered([ends[k, :SPAN] for k in range(size)])))
    after = [(jnp.ones((1, part), F32), jnp.zeros((SPAN, part), F32)) for _ in range(size)]
    open_bits = size - 1
    for mask, level in zip(all_masks, levels):
        if mask in masks:
            bit = 1 << masks.index(mask)
            for m in range(size):
                if not m & bit:
                    late = (m & open_bits) | bit
                    d, s = after[m]
                    after[m] = (d * level[late], d * grad_total[late] + s)
            grad_total = {
                g: grad_total[g] + level[g] * grad_total[g | bit]
                for g in grad_total
                if not g & bit
            }
            open_bits ^= bit
        else:
            groups = list(grad_total)
            got = trade(jnp.concatenate([grad_total[g] for g in groups], axis=0), mask)
            other = {g: got[i * SPAN : (i + 1) * SPAN] for i, g in enumerate(groups)}
            early = bit_of(me, mask) == 0
            for m in range(size):
                g = m & open_bits
                d, s = after[m]
                after[m] = pick(early, (d * level[g][1], d * other[g] + s), (d, s))
            grad_total = {
                g: jnp.where(
                    early,
                    grad_total[g] + level[g][0] * other[g],
                    other[g] + level[g][1] * grad_total[g],
                )
                for g in groups
            }
    grad_out = jnp.stack(ordered([s for _, s in after]))
    out_grads = team_products((bg_all, gated), (recv_all, rg_all), (mixed_all[3], gate_grad))
    grad_out, out_grads, val_pair = tie(grad_out, out_grads, val_pair)
    out_pair = square_sum(out_grads)

    first_grad = grad_total[0]
    holder = lax.div(me * rows, part)

    def rows_of(who):
        return lax.dynamic_slice_in_dim(first_grad, lax.rem(who * rows, part), rows, axis=1)

    handed = exchange([rows_of(jnp.bitwise_xor(me, flips(k))) for k in range(size)])
    state_rows = handed[0]
    for k in range(1, size):
        state_rows = jnp.where(holder == (member ^ k), handed[k], state_rows)

    d_receipt, d_keys, d_values, d_decay, extra = call(
        backward_kernel,
        ins="tttttssp",
        outs=[("t", BF16)] * 4 + [("e", F32)],
        args=(receipt, keys, values, log_decay, wkv_grad, state_in, grad_out, wkv_rows),
    )
    d_decay, state_rows = tie(d_decay, state_rows)
    initial_state_gradient = state_rows.T
    grads = [d_keys, d_values, d_receipt, gate_grad]
    kept, sent = crossing_sum(
        *[(grads[c], w_rest if c > 1 else w_kv, c % 2) for c in range(4)]
    )
    main_grads = team_products(
        (mixed_all[0], d_keys), (mixed_all[1], d_values), (mixed_all[2], d_receipt)
    )

    def latent_back(grad, up):
        kept, sent = halves(nn(grad, up))
        return jnp.concatenate(kept, axis=0), jnp.concatenate(sent, axis=0)

    latent_mine, latent_more = group_sum(
        *local(
            latent_back, [(2 * step, DRANK, F32), (2 * step, DRANK, BF16)], d_decay, w_dup
        )
    )
    val_sum = far_sum(val_pair)
    sent, main_grads, val_sum, key_pair, latent_more = tie(
        sent, main_grads, val_sum, key_pair, latent_more
    )
    main_pair = square_sum(main_grads)
    mixed_mine, mixed_more = group_sum(kept, sent)
    mixed_more, key_sum = tie(mixed_more, far_sum(key_pair))
    rest_grad, delta_grad, top_one, cols_mix, down_grad, up_grad, ddown_grad = mixes_back(
        mixed_mine,
        mixed_more,
        latent_mine,
        latent_more,
        delta,
        mix_tanh,
        decay_tanh,
        blend,
        mixed_zero,
        w_down,
        w_up,
        w_ddown,
        vec,
    )
    def norm_one_back(last, rest, shifted, arrived, normal, scale, middle, vec):
        below = jnp.where(last == 1, jnp.zeros_like(arrived[:1]), arrived[:1])
        grad = rest + rows_below(shifted, below)
        out = middle + norm_back(grad, vec[0:1], normal, scale[:, :1])
        cols = padded([column_sum(grad * normal), column_sum(grad)])
        return take_lanes(out, from_spans), cols

    block_input_gradient, cols_one = local(
        norm_one_back,
        [whole, (8, width, F32)],
        rest_grad,
        delta_grad,
        neighbour(top_one, -1),
        normal_one,
        scale_one,
        middle_grad,
        vec,
        scalar=last_flag,
    )
    out_sum, main_sum = [far_sum(p) for p in (out_pair, main_pair)]

    def column_parts(value):
        return [value[:, c * part : (c + 1) * part] for c in range(3)]

    out_cols, main_cols = column_parts(out_sum), column_parts(main_sum)
    feedforward_gradient = hand_rows([[key_sum], [out_cols[1]], [val_sum]])
    mixing_gradient = hand_rows([[m] for m in main_cols] + [[out_cols[2]], [out_cols[0]]])


    def spread(value):
        zero = jnp.zeros((width, value.shape[1]), F32)
        return lax.dynamic_update_slice_in_dim(zero, value, member * part, axis=0)

    vec_low = jnp.concatenate([cols_one[:2], cols_mix[:6], cols_two[:4]], axis=0)
    vec_head = jnp.concatenate(
        [jnp.sum(extra[:, :2], axis=0), jnp.sum(ends[:, SPAN : SPAN + 2], axis=0)], axis=0
    )
    by_feature = jnp.concatenate([down_grad, up_grad, ddown_grad, vec_low.T], axis=1)
    low = cube_sum(to_cube(by_feature), BF16)
    by_channel = spread(jnp.concatenate([tn(d_decay, dh_all), vec_head.T], axis=1))
    high_part = cube_sum(by_channel.reshape(*[2] * len(all_masks), rows, -1), F32)
    lowrank_gradient = jnp.concatenate([low[:, :decay_up], high_part[:, :DRANK]], axis=1)
    vectors_gradient = jnp.concatenate(
        [low[:, decay_up : decay_up + 8], high_part[:, DRANK:], low[:, decay_up + 8 :]], axis=1
    )
    return (
        block_output.reshape(1, step, width),
        block_input_gradient.reshape(1, step, width),
        initial_state_gradient,
        mixing_gradient,
        lowrank_gradient,
        vectors_gradient,
        feedforward_gradient,
    )


def solution(mesh):
    rowwise = P("seq", None)
    tokenwise = P(None, "seq", None)
    return jax.shard_map(
        functools.partial(on_device, mesh.shape["seq"]),
        mesh=mesh,
        in_specs=(tokenwise, P(), rowwise, rowwise, rowwise, rowwise, rowwise, tokenwise),
        out_specs=(tokenwise, tokenwise, rowwise, rowwise, rowwise, rowwise, rowwise),
        check_vma=False,
    )
```

```python
import functools

import jax
import jax.numpy as jnp
from jax import lax
from jax.experimental import pallas as pl
from jax.experimental.pallas import tpu as pltpu
from jax.sharding import PartitionSpec as P

HEADS = 32
SPAN = 64
FF = 7168
RANK = 32
DRANK = 64
LN_EPS = 1e-05
GN_EPS = 0.00064

F32 = jnp.float32
BF16 = jnp.bfloat16
HI = lax.Precision.HIGHEST


def nn(a, b):
    return jnp.dot(a, b, preferred_element_type=F32)


def nt(a, b):
    return lax.dot_general(a, b, (((1,), (1,)), ((), ())), preferred_element_type=F32)


def tn(a, b):
    return lax.dot_general(a, b, (((0,), (0,)), ((), ())), preferred_element_type=F32)


def knn(a, b):
    return lax.dot_general(
        a, b, (((1,), (0,)), ((), ())), preferred_element_type=F32
    )


def knt(a, b):
    return lax.dot_general(
        a, b, (((1,), (1,)), ((), ())), preferred_element_type=F32
    )


def ktn(a, b):
    return lax.dot_general(
        a, b, (((0,), (0,)), ((), ())), preferred_element_type=F32
    )


def low_lanes(shape):
    return lax.broadcasted_iota(jnp.int32, shape, len(shape) - 1) < SPAN


def head_sum(x):
    low = low_lanes(x.shape)
    s0 = jnp.sum(jnp.where(low, x, 0.0), axis=-1, keepdims=True)
    s1 = jnp.sum(jnp.where(low, 0.0, x), axis=-1, keepdims=True)
    return jnp.where(low, s0, s1)


def two_rows(x):
    low = low_lanes(x.shape)
    return jnp.concatenate([jnp.where(low, x, 0.0), jnp.where(low, 0.0, x)], axis=0)


def fold(full):
    return jnp.where(low_lanes((SPAN, 2 * SPAN)), full[:SPAN], full[SPAN:])


def unfold(state):
    low = low_lanes(state.shape)
    return jnp.concatenate([jnp.where(low, state, 0.0), jnp.where(low, 0.0, state)], axis=0)


def running(w, upper=False):
    count = w.shape[0]
    row = lax.broadcasted_iota(jnp.int32, (count, count), 0)
    col = lax.broadcasted_iota(jnp.int32, (count, count), 1)
    keep = (col >= row) if upper else (col <= row)
    return lax.dot_general(
        jnp.where(keep, 1.0, 0.0).astype(F32),
        w,
        (((1,), (0,)), ((), ())),
        precision=HI,
        preferred_element_type=F32,
    )


def strict(count):
    row = lax.broadcasted_iota(jnp.int32, (2 * count, count), 0)
    col = lax.broadcasted_iota(jnp.int32, (2 * count, count), 1)
    row = jnp.where(row >= count, row - count, row)
    return row > col, row == col


def affinity(r, k, u, q, ks):
    count = r.shape[0]
    below, diag = strict(count)
    raw = knt(two_rows(q), ks)
    share = jnp.sum(two_rows(r * u * k), axis=-1, keepdims=True)
    return jnp.where(below, raw, jnp.where(diag, share, 0.0))


def totals_kernel(k_ref, v_ref, w_ref, out_ref):
    cum = running(w_ref[...])
    total = cum[-1:, :]
    kc = k_ref[...] * jnp.exp(total - cum)
    out_ref[0, :SPAN, :] = fold(ktn(v_ref[...], kc))
    out_ref[0, SPAN:, :] = jnp.broadcast_to(jnp.exp(total), (8, 2 * SPAN))


def group_norm(y, gain, bias):
    centred = y - head_sum(y) * (1.0 / SPAN)
    spread = head_sum(centred * centred) * (1.0 / SPAN)
    scale = lax.rsqrt(spread + GN_EPS)
    normal = centred * scale
    return normal, scale, normal * gain + bias


def forward_kernel(r_ref, k_ref, v_ref, w_ref, g_ref, s_ref, p_ref, y_ref, gated_ref):
    r, k, v, w = r_ref[...], k_ref[...], v_ref[...], w_ref[...]
    cum = running(w)
    q = r * jnp.exp(cum - w)
    ks = k * jnp.exp(-cum)
    aff = affinity(r, k, p_ref[0:1, :], q, ks)
    count = r.shape[0]
    v2 = two_rows(v)
    y = (
        knt(q, unfold(s_ref[0]))
        + knn(aff[:count], v2[:count])
        + knn(aff[count:], v2[count:])
    )
    y_ref[...] = y
    gate = g_ref[...]
    _, _, grouped = group_norm(y, p_ref[1:2, :], p_ref[2:3, :])
    gated_ref[...] = (grouped * gate * jax.nn.sigmoid(gate)).astype(BF16)


def gate_kernel(gg_ref, g_ref, y_ref, r_ref, w_ref, p_ref, gate_ref, dy_ref, out_ref):
    gated_grad, gate, y = gg_ref[...], g_ref[...], y_ref[...]
    gain = p_ref[1:2, :]
    normal, scale, grouped = group_norm(y, gain, p_ref[2:3, :])
    sig = jax.nn.sigmoid(gate)
    gate_ref[...] = (gated_grad * grouped * sig * (1.0 + gate * (1.0 - sig))).astype(BF16)
    outer = gated_grad * gate * sig
    inner = outer * gain
    dy = scale * (
        inner
        - head_sum(inner) * (1.0 / SPAN)
        - normal * (head_sum(inner * normal) * (1.0 / SPAN))
    )
    dy_ref[...] = dy
    w = w_ref[...]
    q = r_ref[...] * jnp.exp(running(w) - w)
    out_ref[0, :SPAN, :] = fold(ktn(dy, q))
    gain_grad = jnp.sum(outer * normal, axis=0, keepdims=True)
    bias_grad = jnp.sum(outer, axis=0, keepdims=True)
    out_ref[0, SPAN:, :] = jnp.concatenate(
        [gain_grad, bias_grad, jnp.zeros((6, 2 * SPAN), F32)], axis=0
    )


def backward_kernel(
    r_ref, k_ref, v_ref, w_ref, dy_ref, s_ref, gs_ref, p_ref,
    dr_ref, dk_ref, dv_ref, dd_ref, out_ref,
):
    r, k, v, w, dy = r_ref[...], k_ref[...], v_ref[...], w_ref[...], dy_ref[...]
    u = p_ref[0:1, :]
    count = r.shape[0]
    cum = running(w)
    total = cum[-1:, :]
    e_before, e_minus, e_carry = jnp.exp(cum - w), jnp.exp(-cum), jnp.exp(total - cum)
    q, ks, kc = r * e_before, k * e_minus, k * e_carry
    aff = affinity(r, k, u, q, ks)
    below, _ = strict(count)
    dy2 = two_rows(dy)
    d_aff = jnp.where(below, knt(dy2, v), 0.0)
    own = head_sum(dy * v)
    state, grad_state = s_ref[0], gs_ref[0]
    state2, grad2 = unfold(state), unfold(grad_state)
    ks2 = two_rows(ks)
    dq = knn(dy, state2) + knn(d_aff[:count], ks2[:count]) + knn(d_aff[count:], ks2[count:])
    dks = ktn(d_aff, two_rows(q))
    dkc = knn(v, grad2)
    dv_ref[...] = (ktn(aff, dy2) + knt(kc, grad2)).astype(BF16)
    dr_ref[...] = (dq * e_before + own * u * k).astype(BF16)
    dk_ref[...] = (dks * e_minus + dkc * e_carry + own * u * r).astype(BF16)
    gq, gc = q * dq, kc * dkc
    d_total = jnp.sum(gc, axis=0, keepdims=True) + jnp.exp(total) * jnp.sum(
        state * grad_state, axis=0, keepdims=True
    )
    dw = running(gq - ks * dks - gc, upper=True) - gq + d_total
    term = dw * w
    dd_ref[...] = term.astype(BF16)
    out_ref[0] = jnp.concatenate(
        [
            jnp.sum(term, axis=0, keepdims=True),
            jnp.sum(own * r * k, axis=0, keepdims=True),
            jnp.zeros((6, 2 * SPAN), F32),
        ],
        axis=0,
    )


def block_call(kernel, chunks, step, width, ins, outs, args):
    lane = 2 * SPAN
    kinds = {
        "t": pl.BlockSpec((step, lane), lambda c, h: (c, h)),
        "s": pl.BlockSpec((1, SPAN, lane), lambda c, h: (c, 0, h)),
        "x": pl.BlockSpec((1, SPAN + 8, lane), lambda c, h: (c, 0, h)),
        "e": pl.BlockSpec((1, 8, lane), lambda c, h: (c, 0, h)),
        "p": pl.BlockSpec((8, lane), lambda c, h: (0, h)),
    }
    shapes = {
        "t": lambda d: jax.ShapeDtypeStruct((chunks * step, width), d),
        "x": lambda d: jax.ShapeDtypeStruct((chunks, SPAN + 8, width), d),
        "e": lambda d: jax.ShapeDtypeStruct((chunks, 8, width), d),
    }
    return pl.pallas_call(
        kernel,
        grid=(chunks, width // lane),
        in_specs=[kinds[kind] for kind in ins],
        out_specs=[kinds[kind] for kind, _ in outs],
        out_shape=[shapes[kind](dtype) for kind, dtype in outs],
        compiler_params=pltpu.CompilerParams(vmem_limit_bytes=48 * 1024 * 1024),
    )(*args)


def weight_grad(places, pairs, block):
    tokens, blocks = pairs[0][0].shape[0], places.shape[0]
    widths = [y.shape[1] for _, y in pairs]

    def kernel(_, *refs):
        at = 0
        for i, wide in enumerate(widths):
            refs[-1][0, :, at : at + wide] = tn(refs[2 * i][...], refs[2 * i + 1][...]).astype(
                BF16
            )
            at += wide

    specs = []
    for wide in widths:
        specs.append(pl.BlockSpec((tokens, block), lambda i, at: (0, at[i])))
        specs.append(pl.BlockSpec((tokens, wide), lambda i, at: (0, 0)))
    return pl.pallas_call(
        kernel,
        grid_spec=pltpu.PrefetchScalarGridSpec(
            num_scalar_prefetch=1,
            grid=(blocks,),
            in_specs=specs,
            out_specs=pl.BlockSpec((1, block, sum(widths)), lambda i, at: (i, 0, 0)),
        ),
        out_shape=jax.ShapeDtypeStruct((blocks, block, sum(widths)), BF16),
        compiler_params=pltpu.CompilerParams(vmem_limit_bytes=48 * 1024 * 1024),
    )(places, *[v for pair in pairs for v in pair])


def lanes_kernel(spans, x_ref, out_ref):
    at = 0
    for start, stop in spans:
        out_ref[:, at : at + stop - start] = x_ref[:, start:stop].astype(out_ref.dtype)
        at += stop - start


def move_lanes(spans, value, dtype):
    return pl.pallas_call(
        functools.partial(lanes_kernel, spans),
        in_specs=[pl.BlockSpec(memory_space=pltpu.VMEM)],
        out_specs=pl.BlockSpec(memory_space=pltpu.VMEM),
        out_shape=jax.ShapeDtypeStruct(value.shape, dtype),
        compiler_params=pltpu.CompilerParams(vmem_limit_bytes=32 * 1024 * 1024),
    )(value)


def place_kernel(counts, wide, block, at_ref, *refs):
    ins, out_ref, sems = refs[: len(counts)], refs[-2], refs[-1]
    rows = out_ref.shape[0]
    copies, i = [], 0
    for ref, n in zip(ins, counts):
        for j in range(n):
            start = pl.multiple_of(at_ref[i] * block, block)
            column = i * block // rows * wide
            copy = pltpu.make_async_copy(
                ref.at[pl.ds(j * block, block), :],
                out_ref.at[pl.ds(start, block), pl.ds(column, wide)],
                sems.at[i],
            )
            copy.start()
            copies.append(copy)
            i += 1
    for copy in copies:
        copy.wait()


def place_rows(parts, block):
    pieces = [p for part in parts for p in part[1]]
    wide = pieces[0].shape[1]
    at = jnp.concatenate([part[0] for part in parts])
    counts = [p.shape[0] // block for p in pieces]
    total = sum(counts)
    return pl.pallas_call(
        functools.partial(place_kernel, counts, wide, block),
        in_specs=[pl.BlockSpec(memory_space=pltpu.SMEM)]
        + [pl.BlockSpec(memory_space=pl.ANY)] * len(pieces),
        out_specs=pl.BlockSpec(memory_space=pl.ANY),
        out_shape=jax.ShapeDtypeStruct(
            (total * block // len(parts), wide * len(parts)), pieces[0].dtype
        ),
        scratch_shapes=[pltpu.SemaphoreType.DMA((total,))],
        compiler_params=pltpu.CompilerParams(vmem_limit_bytes=32 * 1024 * 1024),
    )(at, *pieces)


def mixes_kernel(
    open_ref, x_ref, before_ref, vec_ref, down_ref, up_ref, ddown_ref,
    m1_ref, m2_ref, m3_ref, m4_ref, dh_ref,
    normal_ref, scale_ref, delta_ref, blend_ref, m0_ref, tanh_ref, dtanh_ref,
):
    piece = pl.program_id(0)
    step = m1_ref.shape[0]
    x = x_ref[...].astype(F32)
    centred = x - jnp.mean(x, axis=-1, keepdims=True)
    scale = lax.rsqrt(jnp.mean(centred * centred, axis=-1, keepdims=True) + LN_EPS)
    normal = centred * scale
    full = normal * vec_ref[0:1, :] + vec_ref[1:2, :]
    normed = full[:step]
    first = jnp.where(open_ref[piece] == 1, before_ref[0:1, :], full[step : step + 1])
    row = lax.broadcasted_iota(jnp.int32, normed.shape, 0)
    delta = jnp.where(row == 0, first, pltpu.roll(normed, 1, 0)) - normed
    blend = (normed + delta * vec_ref[2:3, :]).astype(BF16)
    tanh = jnp.tanh(nn(blend, down_ref[...]))
    latent = tanh.astype(BF16)
    lane = lax.broadcasted_iota(jnp.int32, latent.shape, 1)
    mixed = []
    for c in range(5):
        own = (lane >= c * RANK) & (lane < (c + 1) * RANK)
        offset = nt(jnp.where(own, latent, jnp.zeros_like(latent)), up_ref[...])
        mixed.append((normed + delta * (vec_ref[3 + c : 4 + c, :] + offset)).astype(BF16))
    dtanh = jnp.tanh(nn(mixed[0], ddown_ref[...]))
    m1_ref[...], m2_ref[...], m3_ref[...], m4_ref[...] = mixed[1:]
    dh_ref[...] = dtanh.astype(BF16)

    @pl.when(piece == 0)
    def _():
        normal_ref[...] = normal[:step]
        scale_ref[...] = jnp.broadcast_to(scale[:step], scale_ref.shape)
        delta_ref[...] = delta
        blend_ref[...] = blend
        m0_ref[...] = mixed[0]
        tanh_ref[...] = tanh
        dtanh_ref[...] = dtanh


def group_mixes(opening, x, before, vec, down, up, ddown, step):
    high, width = step + 16, x.shape[1]
    pieces = x.shape[0] // high

    def whole(value):
        return pl.BlockSpec(value.shape, lambda k: (0, 0))

    def own(columns, dtype):
        return (
            pl.BlockSpec((step, columns), lambda k: (0, 0)),
            jax.ShapeDtypeStruct((step, columns), dtype),
        )

    def every(columns, dtype):
        return (
            pl.BlockSpec((step, columns), lambda k: ((k % 2) * 2 + k // 2, 0)),
            jax.ShapeDtypeStruct((pieces * step, columns), dtype),
        )

    outs = [every(width, BF16)] * 4 + [
        every(DRANK, BF16),
        own(width, F32),
        own(128, F32),
        own(width, F32),
        own(width, BF16),
        own(width, BF16),
        own(5 * RANK, F32),
        own(DRANK, F32),
    ]
    return pl.pallas_call(
        mixes_kernel,
        grid=(pieces,),
        in_specs=[
            pl.BlockSpec(memory_space=pltpu.SMEM),
            pl.BlockSpec((high, width), lambda k: (k, 0)),
            whole(before),
            whole(vec),
            whole(down),
            whole(up),
            whole(ddown),
        ],
        out_specs=[o[0] for o in outs],
        out_shape=[o[1] for o in outs],
        compiler_params=pltpu.CompilerParams(vmem_limit_bytes=56 * 1024 * 1024),
    )(opening, x, before, vec, down, up, ddown)


def product(pairs, outs, body, sides=(), tile=256):
    count = len(pairs)

    def kernel(*refs):
        ins, out_refs = refs[: 2 * count + len(sides)], refs[2 * count + len(sides) :]
        products = [
            (nn if pair[2] == "nn" else nt)(ins[2 * i][...], ins[2 * i + 1][...])
            for i, pair in enumerate(pairs)
        ]
        results = body(*products, *[r[...] for r in ins[2 * count :]])
        for ref, value in zip(out_refs, results):
            ref[...] = value.astype(ref.dtype)

    specs, args = [], []
    for a, b, form, at in pairs:
        depth = a.shape[1]
        specs.append(pl.BlockSpec(a.shape, lambda j: (0, 0)))
        if form == "nn":
            specs.append(pl.BlockSpec((depth, tile), lambda j, at=at: (0, at + j)))
        else:
            specs.append(pl.BlockSpec((tile, depth), lambda j, at=at: (j, at)))
        args += [a, b]
    for side in sides:
        specs.append(pl.BlockSpec((side.shape[0], tile), lambda j: (0, j)))
    return pl.pallas_call(
        kernel,
        grid=(outs[0][1] // tile,),
        in_specs=specs,
        out_specs=[pl.BlockSpec((o[0], tile), lambda j: (0, j)) for o in outs],
        out_shape=[jax.ShapeDtypeStruct(o[:2], o[2]) for o in outs],
        compiler_params=pltpu.CompilerParams(vmem_limit_bytes=56 * 1024 * 1024),
    )(*args, *sides)


def local(fn, outs, *args, scalar=None):
    def kernel(*refs):
        lead = [] if scalar is None else [refs[0]]
        ins, out_refs = refs[len(lead) : -len(outs)], refs[-len(outs) :]
        results = fn(*[r[0] for r in lead], *[r[...] for r in ins])
        for ref, value in zip(out_refs, results):
            ref[...] = value.astype(ref.dtype)

    specs = [pl.BlockSpec(memory_space=pltpu.VMEM)] * len(args)
    if scalar is not None:
        specs = [pl.BlockSpec(memory_space=pltpu.SMEM)] + specs
        args = (scalar.reshape(1), *args)
    return pl.pallas_call(
        kernel,
        in_specs=specs,
        out_specs=[pl.BlockSpec(memory_space=pltpu.VMEM)] * len(outs),
        out_shape=[jax.ShapeDtypeStruct(o[:2], o[2]) for o in outs],
        compiler_params=pltpu.CompilerParams(vmem_limit_bytes=56 * 1024 * 1024),
    )(*args)


def take_lanes(value, spans):
    if len(spans) == 1:
        return value
    return jnp.concatenate([value[:, a:b] for a, b in spans], axis=1)


def norm_back(grad, gain, normal, scale):
    e = grad * gain
    return scale * (
        e
        - jnp.mean(e, axis=-1, keepdims=True)
        - normal * jnp.mean(e * normal, axis=-1, keepdims=True)
    )


def rows_above(value, first):
    row = lax.broadcasted_iota(jnp.int32, value.shape, 0)
    return jnp.where(row == 0, first, pltpu.roll(value, 1, 0))


def rows_below(value, last):
    row = lax.broadcasted_iota(jnp.int32, value.shape, 0)
    high = value.shape[0]
    return jnp.where(row == high - 1, last, pltpu.roll(value, high - 1, 0))


def padded(rows):
    return jnp.concatenate(
        list(rows) + [jnp.zeros((8 - len(rows), rows[0].shape[1]), F32)], axis=0
    )


def column_sum(value):
    return jnp.sum(value, axis=0, keepdims=True)


def gates_kernel(
    spans, who_ref, middle_ref, value_ref, more_ref, act_ref, cot_ref,
    out_ref, up_ref, vg_ref, rg_ref, held,
):
    to_spans, from_spans = spans
    step, part = act_ref.shape[0] // 4, act_ref.shape[1]
    who = who_ref[0]
    act = [
        act_ref[pl.ds(pl.multiple_of((who ^ j) * step, step), step), :] for j in range(4)
    ]
    recept = jax.nn.sigmoid(take_lanes(jnp.concatenate(act, axis=1).astype(F32), to_spans))
    value = value_ref[...] + more_ref[...].astype(F32)
    out = middle_ref[...] + recept * value
    out_ref[...] = take_lanes(out, from_spans).astype(BF16)
    up = take_lanes(cot_ref[...].astype(F32), to_spans)
    up_ref[...] = up
    vg_ref[...] = (up * recept).astype(BF16)
    held[...] = take_lanes(up * value * recept * (1.0 - recept), from_spans)
    for k in range(4):
        at = pl.multiple_of((who ^ k) * part, part)
        rg_ref[k * step : (k + 1) * step, :] = held[:, pl.ds(at, part)].astype(BF16)


def gates(spans, who, middle, value, more, act, cot):
    step, width = middle.shape
    part = act.shape[1]
    shape = jax.ShapeDtypeStruct
    return pl.pallas_call(
        functools.partial(gates_kernel, spans),
        in_specs=[pl.BlockSpec(memory_space=pltpu.SMEM)]
        + [pl.BlockSpec(memory_space=pltpu.VMEM)] * 5,
        out_specs=[pl.BlockSpec(memory_space=pltpu.VMEM)] * 4,
        out_shape=[
            shape((step, width), BF16),
            shape((step, width), F32),
            shape((step, width), BF16),
            shape((4 * step, part), BF16),
        ],
        scratch_shapes=[pltpu.VMEM((step, width), F32)],
        compiler_params=pltpu.CompilerParams(vmem_limit_bytes=56 * 1024 * 1024),
    )(who.reshape(1), middle, value, more, act, cot)


def mixes_back_kernel(
    kept_ref, got_ref, dl_ref, dl_more_ref, delta_ref, tanh_ref, dtanh_ref, blend_ref, m0_ref,
    down_ref, up_ref, ddown_ref, vec_ref,
    rest_ref, dg_ref, row_ref, cols_ref, down_out, up_out, ddown_out,
):
    step = delta_ref.shape[0]
    dtanh = dtanh_ref[...]
    decay_grad = dl_ref[...] + dl_more_ref[...].astype(F32)
    decay_pre = (decay_grad * (1.0 - dtanh * dtanh)).astype(BF16)
    ddown_out[...] = tn(m0_ref[...], decay_pre)
    tanh = tanh_ref[...]
    latent = tanh.astype(BF16)
    lane = lax.broadcasted_iota(jnp.int32, latent.shape, 1)
    delta, up = delta_ref[...], up_ref[...]
    latent_grad = jnp.zeros(latent.shape, F32)
    up_grad = jnp.zeros(up_out.shape, F32)
    dg = jnp.zeros(delta.shape, F32)
    total = jnp.zeros(delta.shape, F32)
    cols = []
    for c in range(5):
        own = (lane >= c * RANK) & (lane < (c + 1) * RANK)
        mine = jnp.where(own, latent, jnp.zeros_like(latent))
        if c == 0:
            grad = nt(decay_pre, ddown_ref[...])
        else:
            at = slice((c - 1) * step, c * step)
            grad = kept_ref[at, :] + got_ref[at, :].astype(F32)
        shift = grad * delta
        cols.append(column_sum(shift))
        offset = shift.astype(BF16)
        latent_grad = jnp.where(own, nn(offset, up), latent_grad)
        up_grad = up_grad + tn(offset, mine)
        dg = dg + grad * (vec_ref[3 + c : 4 + c, :] + nt(mine, up))
        total = total + grad
    up_out[...] = up_grad
    mix_pre = (latent_grad * (1.0 - tanh * tanh)).astype(BF16)
    down_out[...] = tn(blend_ref[...], mix_pre)
    blend_grad = nt(mix_pre, down_ref[...])
    dg = dg + blend_grad * vec_ref[2:3, :]
    rest_ref[...] = total + blend_grad - dg
    dg_ref[...] = dg
    row_ref[...] = dg[:8]
    cols_ref[...] = padded([column_sum(blend_grad * delta)] + cols)


def mixes_back(*args):
    delta, down, ddown = args[4], args[9], args[11]
    step, width = delta.shape
    shape = jax.ShapeDtypeStruct
    outs = [
        shape((step, width), F32),
        shape((step, width), F32),
        shape((8, width), F32),
        shape((8, width), F32),
        shape(down.shape, F32),
        shape(down.shape, F32),
        shape(ddown.shape, F32),
    ]
    return pl.pallas_call(
        mixes_back_kernel,
        in_specs=[pl.BlockSpec(memory_space=pltpu.VMEM)] * len(args),
        out_specs=[pl.BlockSpec(memory_space=pltpu.VMEM)] * len(outs),
        out_shape=outs,
        compiler_params=pltpu.CompilerParams(vmem_limit_bytes=60 * 1024 * 1024),
    )(*args)


def tie(*values):
    return lax.optimization_barrier(values)


def on_device(
    count,
    tokens,
    previous,
    initial_state,
    mixing_weights,
    lowrank_weights,
    vectors,
    feedforward_weights,
    cotangent,
):
    fast = initial_state.shape[0] == 64
    masks = (1, 8) if fast else (1, 2)
    size = 1 << len(masks)
    teams = count // size
    all_masks = [1 << b for b in range(count.bit_length() - 1)]
    team_masks = [b for b in all_masks if b not in masks]
    far = 16
    team_masks.sort(key=lambda b: fast and b != far)
    me = lax.axis_index("seq")
    _, step, width = tokens.shape
    rows = mixing_weights.shape[0]
    part = width // size
    ff_part = FF // size
    team_rows = rows * size
    def bit_of(who, mask):
        return (who // mask) % 2 if isinstance(who, int) else lax.rem(lax.div(who, mask), 2)

    def member_of(who):
        return sum(bit_of(who, b) << j for j, b in enumerate(masks))

    def team_of(who):
        return sum(bit_of(who, b) << j for j, b in enumerate(team_masks))

    member, team = member_of(me), team_of(me)
    order = sorted(range(count), key=lambda d: (team_of(d), member_of(d)))
    inverse = sorted(range(count), key=lambda p: order[p])
    across = [order[m::size] for m in range(size)]
    square = [order[m :: 2 * size] for m in range(2 * size)]
    def lane_spans(blocks):
        spans = []
        for d in blocks:
            if spans and spans[-1][1] == d * rows:
                spans[-1][1] = (d + 1) * rows
            else:
                spans.append([d * rows, (d + 1) * rows])
        return spans

    to_spans, from_spans = lane_spans(order), lane_spans(inverse)

    def to_places(value, dtype):
        return move_lanes(to_spans, value, dtype)

    def flips(k):
        return sum(b for j, b in enumerate(masks) if (k >> j) & 1)

    def trade(value, mask):
        return lax.ppermute(value, "seq", [(d, d ^ mask) for d in range(count)])

    def group_gather(value):
        side = trade(value, masks[1])
        return value, side, trade(jnp.concatenate([value, side], axis=0), masks[0])

    def group_rows(value):
        high, columns = value.shape

        def lay(own, side, far):
            return (jnp.concatenate([own, far[:high], side, far[high:]], axis=0),)

        return local(lay, [(size * high, columns, value.dtype)], *group_gather(value))[0]

    def halves(value):
        cut = [value[k * step : (k + 1) * step] for k in range(size)]
        return [cut[0], cut[2]], [cut[1], cut[3]]

    def group_sum(kept, sent):
        high, columns = kept.shape[0] // 2, kept.shape[1]
        got = trade(sent, masks[0])

        def add(mine, more):
            total = mine + more.astype(F32)
            return total[:high], total[high:]

        mine, side = local(add, [(high, columns, F32), (high, columns, BF16)], kept, got)
        return mine, trade(side, masks[1])

    def crossing_sum(*pairs):
        units = len(pairs)

        def body(*products):
            parts = [halves(p) for p in products]
            kept = [p[0][i] for i in range(2) for p in parts]
            sent = [p[1][i] for i in range(2) for p in parts]
            return jnp.concatenate(kept, axis=0), jnp.concatenate(sent, axis=0)

        high = 2 * units * step
        return product(
            [(a, b, "nt", at) for a, b, at in pairs],
            [(high, width, F32), (high, width, BF16)],
            body,
        )

    def exchange(pieces):
        pieces, high = list(pieces), pieces[0].shape[0]
        for j in reversed(range(len(masks))):
            keys = [k for k in range(size) if (k >> j) & 1]
            got = trade(jnp.concatenate([pieces[k] for k in keys], axis=0), masks[j])
            for i, k in enumerate(keys):
                pieces[k] = got[i * high : (i + 1) * high]
        return pieces

    def ordered(pieces):
        pieces = list(pieces)
        for j in range(len(masks)):
            swap = lax.rem(lax.div(member, 1 << j), 2) == 1
            pieces = [
                jnp.where(swap, pieces[k ^ (1 << j)], pieces[k]) for k in range(len(pieces))
            ]
        return pieces

    def neighbour(value, offset):
        pairs = [(d, d + offset) for d in range(count) if 0 <= d + offset < count]
        return lax.ppermute(value, "seq", pairs)

    def take_columns(value, spans, who):
        return jnp.concatenate(
            [
                lax.dynamic_slice_in_dim(value, start + who * wide, wide, axis=1)
                for start, wide in spans
            ],
            axis=1,
        )

    def group_columns(value, spans):
        pieces = [take_columns(value, spans, member ^ k) for k in range(size)]
        return jnp.concatenate(ordered(exchange(pieces)), axis=0)

    def crossing(first):
        bits = list(range(1, len(team_masks))) + [0]
        if first:
            bits[0], bits[1] = bits[1], bits[0]
        return bits

    def gather_rows(own):
        return lax.all_gather(own, "seq", axis=0, tiled=True, axis_index_groups=across)

    def far_pair(own):
        if not fast:
            return own
        got = trade(own, far)
        upper = bit_of(me, far) == 1
        return jnp.concatenate(
            [jnp.where(upper, got, own), jnp.where(upper, own, got)], axis=0
        )

    def cross_rows(own):
        if not fast:
            return gather_rows(own)
        cut = own.shape[1] // 2
        parts = []
        for first, piece in ((False, own[:, :cut]), (True, own[:, cut:])):
            pieces, places = [piece], [0]
            for bit in reversed(crossing(first)):
                joint = pieces[0] if len(pieces) == 1 else jnp.concatenate(pieces, axis=0)
                pieces.append(trade(joint, team_masks[bit]))
                places = places + [p | (1 << bit) for p in places]
            parts.append((jnp.bitwise_xor(jnp.asarray(places, jnp.int32), team), pieces))
        return place_rows(parts, team_rows)

    def gather_square(paired):
        groups = square if fast else across
        return lax.all_gather(paired, "seq", axis=0, tiled=True, axis_index_groups=groups)

    def team_products(*pairs):
        if fast:
            places = jnp.arange(teams, dtype=jnp.int32)
            return weight_grad(places, pairs, team_rows).reshape(width, -1)
        return jnp.concatenate([tn(x, y).astype(BF16) for x, y in pairs], axis=1)

    def square_sum(grads):
        groups = square if fast else across
        return lax.psum_scatter(
            grads, "seq", scatter_dimension=0, tiled=True, axis_index_groups=groups
        )

    def far_sum(pair):
        if not fast:
            return pair
        bit = bit_of(me, far)
        sent = lax.dynamic_slice_in_dim(pair, (1 - bit) * team_rows, team_rows, axis=0)
        kept = lax.dynamic_slice_in_dim(pair, bit * team_rows, team_rows, axis=0)
        return (kept.astype(F32) + trade(sent, far).astype(F32)).astype(BF16)

    def cube_gather(value, follower=None):
        for mask in reversed(all_masks):
            got = trade(value, mask)
            upper = bit_of(me, mask) == 1
            value = jnp.stack([jnp.where(upper, got, value), jnp.where(upper, value, got)])
            if mask == 8 and follower is not None:
                value, follower = tie(value, follower)
        axes = len(all_masks)
        cube = value.transpose(*reversed(range(axes)), *range(axes, value.ndim))
        return cube if follower is None else (cube, follower)

    place_axes = [all_masks[::-1].index(b) for b in team_masks[::-1] + list(masks[::-1])]

    def by_place(cube):
        rest = range(len(all_masks), cube.ndim)
        return cube.transpose(*place_axes, *rest).reshape(width, -1)

    def to_cube(value):
        cube = value.reshape(*[2] * len(place_axes), rows, -1)
        back = [place_axes.index(a) for a in range(len(place_axes))]
        return cube.transpose(*back, len(back), len(back) + 1)

    def cube_sum(cube, kind):
        for axis, mask in reversed(list(enumerate(reversed(all_masks)))):
            bit = bit_of(me, mask)
            sent = lax.dynamic_index_in_dim(cube, 1 - bit, axis, keepdims=False)
            kept = lax.dynamic_index_in_dim(cube, bit, axis, keepdims=False)
            cube = kept.astype(F32) + trade(sent.astype(kind), mask).astype(F32)
        return cube

    def hand_rows(pieces, extra=None):
        widths = [sum(p.shape[1] for p in piece) for piece in pieces]
        joint = jnp.concatenate([p for piece in pieces for p in piece], axis=1)
        mine = [
            lax.dynamic_slice_in_dim(joint, (member ^ k) * rows, rows, axis=0)
            for k in range(size)
        ]
        if extra is not None:
            mine = [jnp.concatenate([m, e], axis=1) for m, e in zip(mine, extra)]
        by_place = exchange(mine)
        by_member = ordered(by_place)
        outs, start = [], 0
        for wide in widths:
            outs += [p[:, start : start + wide] for p in by_member]
            start += wide
        joined = jnp.concatenate(outs, axis=1).astype(F32)
        if extra is None:
            return joined
        return joined, [p[:, start:].astype(F32) for p in by_place]

    up_start, decay_start, decay_up = 5 * RANK, 10 * RANK, 10 * RANK + DRANK
    last_row = neighbour(tokens[0, -1:, :], 1)
    tokens_sent = to_places(
        jnp.concatenate([tokens[0], jnp.broadcast_to(last_row, (16, width))], axis=0), BF16
    )
    natural, mix_in = cube_gather(
        jnp.concatenate(
            [vectors, initial_state, lowrank_weights[:, decay_up:].astype(F32)], axis=1
        ),
        mixing_weights,
    )
    natural = natural.reshape(width, -1)
    low_cube, mix_in = cube_gather(lowrank_weights[:, :decay_up], mix_in)
    tokens_all = jnp.concatenate(group_gather(tokens_sent), axis=0)
    mix_local = group_columns(mix_in, [(c * width, part) for c in range(5)])
    mix_local, natural, low_cube, tokens_all = tie(mix_local, natural, low_cube, tokens_all)
    lowrank = by_place(low_cube)
    kv_pair, mix_rest = tie(far_pair(mix_local[:, : 2 * part]), mix_local[:, 2 * part :])
    w_kv = gather_square(kv_pair)
    tiles = part // 256

    mine = lax.dynamic_slice_in_dim(natural, member * part, part, axis=0)
    vec_part = mine[:, :16].T
    first_state = mine[:, 16 : 16 + SPAN].T
    w_dup = mine[:, 16 + SPAN :].astype(BF16)
    vec = by_place(
        natural[:, :16].reshape(*[2] * len(all_masks), rows, 16)
    ).T
    wkv_rows = jnp.concatenate([vec_part[9:12], jnp.zeros((5, part), F32)], axis=0)
    is_first = (me == 0).astype(jnp.int32)
    before = to_places(previous.reshape(2, width), F32)
    w_down, w_up = lowrank[:, :up_start], lowrank[:, up_start:decay_start]
    w_ddown = lowrank[:, decay_start:]

    opening = jnp.stack(
        [jnp.bitwise_xor(me, flips(k)) == 0 for k in (0, 2, 1, 3)]
    ).astype(jnp.int32)
    (
        *mixed_all, dh_all, normal_one, scale_one, delta, blend, mixed_zero, mix_tanh, decay_tanh,
    ) = group_mixes(opening, tokens_all, before, vec, w_down, w_up, w_ddown, step)
    rest_pair, mixed_all[0], feed_in = tie(far_pair(mix_rest), mixed_all[0], feedforward_weights)
    w_rest = gather_square(rest_pair)
    ff_spans = [(0, ff_part), (FF, part), (FF + width, ff_part)]
    ff_local = group_columns(feed_in, ff_spans)
    everyone = size * step
    (log_decay,) = product(
        [(dh_all, w_dup, "nt", 0)],
        [(everyone, part, F32)],
        lambda acc, base: (-jnp.exp(base + acc),),
        sides=(vec_part[8:9],),
    )
    keys, values = product(
        [(mixed_all[0], w_kv, "nn", 0), (mixed_all[1], w_kv, "nn", tiles)],
        [(everyone, part, F32)] * 2,
        lambda a, b: (a, b),
    )

    keys, ff_local = tie(keys, ff_local)
    ff_tail = ff_local[:, ff_part + part :]
    near_pair = far_pair(ff_local[:, : ff_part + part])

    call = functools.partial(block_call, chunks=size, step=step, width=part)
    (totals,) = call(
        totals_kernel, ins="ttt", outs=[("x", F32)], args=(keys, values, log_decay)
    )
    by_member = ordered([totals[k] for k in range(size)])
    total = {m: (p[SPAN : SPAN + 1], p[:SPAN]) for m, p in enumerate(by_member)}
    before_chunk = [
        (jnp.ones((1, part), F32), jnp.zeros((SPAN, part), F32)) for _ in range(size)
    ]
    open_bits = size - 1
    levels = []

    def chain(early, late):
        return early[0] * late[0], late[0] * early[1] + late[1]

    def pick(flag, yes, no):
        return tuple(jnp.where(flag, a, b) for a, b in zip(yes, no))

    for mask in all_masks:
        if mask in masks:
            bit = 1 << masks.index(mask)
            levels.append({g: total[g][0] for g in total})
            for m in range(size):
                if m & bit:
                    early = (m & open_bits) ^ bit
                    before_chunk[m] = chain(total[early], before_chunk[m])
            total = {g: chain(total[g], total[g | bit]) for g in total if not g & bit}
            open_bits ^= bit
        else:
            groups = list(total)
            sent = jnp.concatenate(
                [
                    jnp.concatenate(
                        [total[g][1], jnp.broadcast_to(total[g][0], (8, part))], axis=0
                    )
                    for g in groups
                ],
                axis=0,
            )
            got = trade(sent, mask)
            high = SPAN + 8
            other = {
                g: (got[i * high + SPAN : i * high + SPAN + 1], got[i * high : i * high + SPAN])
                for i, g in enumerate(groups)
            }
            levels.append({g: (total[g][0], other[g][0]) for g in groups})
            late = bit_of(me, mask) == 1
            for m in range(size):
                g = m & open_bits
                before_chunk[m] = pick(late, chain(other[g], before_chunk[m]), before_chunk[m])
            total = {
                g: pick(late, chain(other[g], total[g]), chain(total[g], other[g]))
                for g in groups
            }
            if mask == 4:
                first_sum, near_pair = tie(total[0][1], near_pair)
                total[0] = total[0][0], first_sum
    state_in = jnp.stack(ordered([d * first_state + s for d, s in before_chunk]))
    w_near = gather_square(near_pair)
    w_key, w_rec = w_near, w_near[:, ff_part:]
    state_in, ff_tail = tie(state_in, ff_tail)
    val_weights = far_pair(ff_tail)

    receipt, gate_pre = product(
        [(mixed_all[2], w_rest, "nn", 0), (mixed_all[3], w_rest, "nn", tiles)],
        [(everyone, part, F32)] * 2,
        lambda a, b: (a, b),
    )
    wkv, gated = call(
        forward_kernel,
        ins="tttttsp",
        outs=[("t", F32), ("t", BF16)],
        args=(receipt, keys, values, log_decay, gate_pre, state_in, wkv_rows),
    )
    gated, val_weights = tie(gated, val_weights)
    w_val = gather_square(val_weights)
    branch, branch_more = group_sum(*crossing_sum((gated, w_rest, 2)))

    def norm_two(hidden, mine, more, vec):
        middle = hidden[:step].astype(F32) + mine + more.astype(F32)
        centred = middle - jnp.mean(middle, axis=-1, keepdims=True)
        scale = lax.rsqrt(jnp.mean(centred * centred, axis=-1, keepdims=True) + LN_EPS)
        normal = centred * scale
        tail = normal[step - 8 :] * vec[12:13] + vec[13:14]
        return middle, normal, jnp.broadcast_to(scale, (step, 128)), tail

    whole = (step, width, F32)
    middle, normal_two, scale_two, tail_two = local(
        norm_two,
        [whole, whole, (step, 128, F32), (8, width, F32)],
        tokens_sent,
        branch,
        branch_more,
        vec,
    )

    def mix_two(first, normal, arrived, before, vec):
        normed = normal * vec[12:13] + vec[13:14]
        above = jnp.where(first == 1, before[1:2], arrived[7:8])
        delta = rows_above(normed, above) - normed
        key_in, recv_in = normed + delta * vec[14:15], normed + delta * vec[15:16]
        return jnp.concatenate([key_in, recv_in], axis=0), delta

    both, delta_two = local(
        mix_two,
        [(2 * step, width, BF16), whole],
        normal_two,
        neighbour(tail_two, 1),
        before,
        vec,
        scalar=is_first,
    )

    key_all, recv_all = group_rows(both[:step]), group_rows(both[step:])
    relu, squared = product(
        [(key_all, w_key, "nn", 0)],
        [(everyone, ff_part, F32), (everyone, ff_part, BF16)],
        lambda acc: (jnp.maximum(acc, 0.0), jnp.square(jnp.maximum(acc, 0.0))),
    )
    (recept_act,) = product(
        [(recv_all, w_rec, "nn", 0)],
        [(everyone, part, BF16)],
        lambda acc: (acc,),
    )
    squared, recept_act = tie(squared, recept_act)
    acts = exchange([recept_act[k * step : (k + 1) * step] for k in range(size)])
    value, value_more = group_sum(*crossing_sum((squared, w_val, 0)))
    block_output, upstream, value_grad, recept_grads = gates(
        (to_spans, from_spans),
        member,
        middle,
        value,
        value_more,
        jnp.concatenate(acts, axis=0),
        cotangent.reshape(step, width),
    )

    rg_all = jnp.concatenate(
        exchange([recept_grads[k * step : (k + 1) * step] for k in range(size)]), axis=0
    )
    vg_all = group_rows(value_grad)
    val_grads = team_products((vg_all, squared))
    vg_all, val_grads, rg_all = tie(vg_all, val_grads, rg_all)
    val_pair = square_sum(val_grads)
    (key_grad,) = product(
        [(vg_all, w_val, "nn", 0)],
        [(everyone, ff_part, BF16)],
        lambda acc, relu: (acc * (2.0 * relu),),
        sides=(relu,),
    )
    key_grads = team_products((key_all, key_grad))
    key_grad, key_grads = tie(key_grad, key_grads)
    key_pair = square_sum(key_grads)
    recv_two = group_sum(*crossing_sum((rg_all, w_rec, 0)))
    key_two = group_sum(*crossing_sum((key_grad, w_key, 0)))

    def inputs_back(key, key_more, recv, recv_more, vec):
        key, recv = key + key_more.astype(F32), recv + recv_more.astype(F32)
        top = key[:8] * vec[14:15] + recv[:8] * vec[15:16]
        return jnp.concatenate([key, recv], axis=0), top

    in_grads, top_two = local(
        inputs_back, [(2 * step, width, F32), (8, width, F32)], *key_two, *recv_two, vec
    )
    last_flag = (me == count - 1).astype(jnp.int32)

    def norm_two_back(last, grads, arrived, upstream, normal, scale, delta, vec):
        key_grad, recv_grad = grads[:step], grads[step:]
        shifted = key_grad * vec[14:15] + recv_grad * vec[15:16]
        below = jnp.where(last == 1, jnp.zeros_like(arrived[:1]), arrived[:1])
        grad = (
            key_grad * (1.0 - vec[14:15])
            + recv_grad * (1.0 - vec[15:16])
            + rows_below(shifted, below)
        )
        out = upstream + norm_back(grad, vec[12:13], normal, scale[:, :1])
        cols = padded(
            [
                column_sum(grad * normal),
                column_sum(grad),
                column_sum(key_grad * delta),
                column_sum(recv_grad * delta),
            ]
        )
        return out, out, cols

    middle_grad, branch_grad, cols_two = local(
        norm_two_back,
        [whole, (step, width, BF16), (8, width, F32)],
        in_grads,
        neighbour(top_two, -1),
        upstream,
        normal_two,
        scale_two,
        delta_two,
        vec,
        scalar=last_flag,
    )

    bg_all = group_rows(branch_grad)
    (gated_grad,) = product(
        [(bg_all, w_rest, "nn", 2 * tiles)], [(everyone, part, F32)], lambda acc: (acc,)
    )
    gate_grad, wkv_grad, ends = call(
        gate_kernel,
        ins="tttttp",
        outs=[("t", BF16), ("t", F32), ("x", F32)],
        args=(gated_grad, gate_pre, wkv, receipt, log_decay, wkv_rows),
    )
    grad_total = dict(enumerate(ordered([ends[k, :SPAN] for k in range(size)])))
    after = [(jnp.ones((1, part), F32), jnp.zeros((SPAN, part), F32)) for _ in range(size)]
    open_bits = size - 1
    for mask, level in zip(all_masks, levels):
        if mask in masks:
            bit = 1 << masks.index(mask)
            for m in range(size):
                if not m & bit:
                    late = (m & open_bits) | bit
                    d, s = after[m]
                    after[m] = (d * level[late], d * grad_total[late] + s)
            grad_total = {
                g: grad_total[g] + level[g] * grad_total[g | bit]
                for g in grad_total
                if not g & bit
            }
            open_bits ^= bit
        else:
            groups = list(grad_total)
            got = trade(jnp.concatenate([grad_total[g] for g in groups], axis=0), mask)
            other = {g: got[i * SPAN : (i + 1) * SPAN] for i, g in enumerate(groups)}
            early = bit_of(me, mask) == 0
            for m in range(size):
                g = m & open_bits
                d, s = after[m]
                after[m] = pick(early, (d * level[g][1], d * other[g] + s), (d, s))
            grad_total = {
                g: jnp.where(
                    early,
                    grad_total[g] + level[g][0] * other[g],
                    other[g] + level[g][1] * grad_total[g],
                )
                for g in groups
            }
    grad_out = jnp.stack(ordered([s for _, s in after]))
    out_grads = team_products((bg_all, gated), (recv_all, rg_all), (mixed_all[3], gate_grad))
    grad_out, out_grads, val_pair = tie(grad_out, out_grads, val_pair)
    out_pair = square_sum(out_grads)

    d_receipt, d_keys, d_values, d_decay, extra = call(
        backward_kernel,
        ins="tttttssp",
        outs=[("t", BF16)] * 4 + [("e", F32)],
        args=(receipt, keys, values, log_decay, wkv_grad, state_in, grad_out, wkv_rows),
    )
    grads = [d_keys, d_values, d_receipt, gate_grad]
    kept, sent = crossing_sum(
        *[(grads[c], w_rest if c > 1 else w_kv, c % 2) for c in range(4)]
    )
    main_grads = team_products(
        (mixed_all[0], d_keys), (mixed_all[1], d_values), (mixed_all[2], d_receipt)
    )

    def latent_back(grad, up):
        kept, sent = halves(nn(grad, up))
        return jnp.concatenate(kept, axis=0), jnp.concatenate(sent, axis=0)

    latent_mine, latent_more = group_sum(
        *local(
            latent_back, [(2 * step, DRANK, F32), (2 * step, DRANK, BF16)], d_decay, w_dup
        )
    )
    val_sum, key_sum = far_sum(val_pair), far_sum(key_pair)
    sent, main_grads, val_sum, key_sum, latent_more = tie(
        sent, main_grads, val_sum, key_sum, latent_more
    )
    main_pair = square_sum(main_grads)
    mixed_mine, mixed_more = group_sum(kept, sent)
    mixed_more, out_sum = tie(mixed_more, far_sum(out_pair))
    rest_grad, delta_grad, top_one, cols_mix, down_grad, up_grad, ddown_grad = mixes_back(
        mixed_mine,
        mixed_more,
        latent_mine,
        latent_more,
        delta,
        mix_tanh,
        decay_tanh,
        blend,
        mixed_zero,
        w_down,
        w_up,
        w_ddown,
        vec,
    )
    def norm_one_back(last, rest, shifted, arrived, normal, scale, middle, vec):
        below = jnp.where(last == 1, jnp.zeros_like(arrived[:1]), arrived[:1])
        grad = rest + rows_below(shifted, below)
        out = middle + norm_back(grad, vec[0:1], normal, scale[:, :1])
        cols = padded([column_sum(grad * normal), column_sum(grad)])
        return take_lanes(out, from_spans), cols

    block_input_gradient, cols_one = local(
        norm_one_back,
        [whole, (8, width, F32)],
        rest_grad,
        delta_grad,
        neighbour(top_one, -1),
        normal_one,
        scale_one,
        middle_grad,
        vec,
        scalar=last_flag,
    )
    main_sum = far_sum(main_pair)

    def column_parts(value):
        return [value[:, c * part : (c + 1) * part] for c in range(3)]

    out_cols, main_cols = column_parts(out_sum), column_parts(main_sum)
    first_grad = grad_total[0]
    holder = lax.div(me * rows, part)

    def rows_of(who):
        mine = lax.dynamic_slice_in_dim(first_grad, lax.rem(who * rows, part), rows, axis=1).T
        high = lax.reduce_precision(mine, 8, 7)
        return jnp.concatenate([high, mine - high], axis=1).astype(BF16)

    feedforward_gradient, handed = hand_rows(
        [[key_sum], [out_cols[1]], [val_sum]],
        [rows_of(jnp.bitwise_xor(me, flips(k))) for k in range(size)],
    )
    state_rows = handed[0]
    for k in range(1, size):
        state_rows = jnp.where(holder == (member ^ k), handed[k], state_rows)
    initial_state_gradient = state_rows[:, :SPAN] + state_rows[:, SPAN:]
    mixing_gradient = hand_rows([[m] for m in main_cols] + [[out_cols[2]], [out_cols[0]]])


    def spread(value):
        zero = jnp.zeros((width, value.shape[1]), F32)
        return lax.dynamic_update_slice_in_dim(zero, value, member * part, axis=0)

    vec_low = jnp.concatenate([cols_one[:2], cols_mix[:6], cols_two[:4]], axis=0)
    vec_head = jnp.concatenate(
        [jnp.sum(extra[:, :2], axis=0), jnp.sum(ends[:, SPAN : SPAN + 2], axis=0)], axis=0
    )
    by_feature = jnp.concatenate([down_grad, up_grad, ddown_grad, vec_low.T], axis=1)
    low = cube_sum(to_cube(by_feature), BF16)
    by_channel = spread(jnp.concatenate([tn(d_decay, dh_all), vec_head.T], axis=1))
    high_part = cube_sum(by_channel.reshape(*[2] * len(all_masks), rows, -1), F32)
    lowrank_gradient = jnp.concatenate([low[:, :decay_up], high_part[:, :DRANK]], axis=1)
    vectors_gradient = jnp.concatenate(
        [low[:, decay_up : decay_up + 8], high_part[:, DRANK:], low[:, decay_up + 8 :]], axis=1
    )
    return (
        block_output.reshape(1, step, width),
        block_input_gradient.reshape(1, step, width),
        initial_state_gradient,
        mixing_gradient,
        lowrank_gradient,
        vectors_gradient,
        feedforward_gradient,
    )


def solution(mesh):
    rowwise = P("seq", None)
    tokenwise = P(None, "seq", None)
    return jax.shard_map(
        functools.partial(on_device, mesh.shape["seq"]),
        mesh=mesh,
        in_specs=(tokenwise, P(), rowwise, rowwise, rowwise, rowwise, rowwise, tokenwise),
        out_specs=(tokenwise, tokenwise, rowwise, rowwise, rowwise, rowwise, rowwise),
        check_vma=False,
    )
```

```python
import functools

import jax
import jax.numpy as jnp
from jax import lax
from jax.experimental import pallas as pl
from jax.experimental.pallas import tpu as pltpu
from jax.sharding import PartitionSpec as P

HEADS = 32
SPAN = 64
FF = 7168
RANK = 32
DRANK = 64
LN_EPS = 1e-05
GN_EPS = 0.00064

F32 = jnp.float32
BF16 = jnp.bfloat16
HI = lax.Precision.HIGHEST


def nn(a, b):
    return jnp.dot(a, b, preferred_element_type=F32)


def nt(a, b):
    return lax.dot_general(a, b, (((1,), (1,)), ((), ())), preferred_element_type=F32)


def tn(a, b):
    return lax.dot_general(a, b, (((0,), (0,)), ((), ())), preferred_element_type=F32)


def knn(a, b):
    return lax.dot_general(
        a, b, (((1,), (0,)), ((), ())), preferred_element_type=F32
    )


def knt(a, b):
    return lax.dot_general(
        a, b, (((1,), (1,)), ((), ())), preferred_element_type=F32
    )


def ktn(a, b):
    return lax.dot_general(
        a, b, (((0,), (0,)), ((), ())), preferred_element_type=F32
    )


def low_lanes(shape):
    return lax.broadcasted_iota(jnp.int32, shape, len(shape) - 1) < SPAN


def head_sum(x):
    low = low_lanes(x.shape)
    s0 = jnp.sum(jnp.where(low, x, 0.0), axis=-1, keepdims=True)
    s1 = jnp.sum(jnp.where(low, 0.0, x), axis=-1, keepdims=True)
    return jnp.where(low, s0, s1)


def two_rows(x):
    low = low_lanes(x.shape)
    return jnp.concatenate([jnp.where(low, x, 0.0), jnp.where(low, 0.0, x)], axis=0)


def fold(full):
    return jnp.where(low_lanes((SPAN, 2 * SPAN)), full[:SPAN], full[SPAN:])


def unfold(state):
    low = low_lanes(state.shape)
    return jnp.concatenate([jnp.where(low, state, 0.0), jnp.where(low, 0.0, state)], axis=0)


def running(w, upper=False):
    count = w.shape[0]
    row = lax.broadcasted_iota(jnp.int32, (count, count), 0)
    col = lax.broadcasted_iota(jnp.int32, (count, count), 1)
    keep = (col >= row) if upper else (col <= row)
    return lax.dot_general(
        jnp.where(keep, 1.0, 0.0).astype(F32),
        w,
        (((1,), (0,)), ((), ())),
        precision=HI,
        preferred_element_type=F32,
    )


def strict(count):
    row = lax.broadcasted_iota(jnp.int32, (2 * count, count), 0)
    col = lax.broadcasted_iota(jnp.int32, (2 * count, count), 1)
    row = jnp.where(row >= count, row - count, row)
    return row > col, row == col


def affinity(r, k, u, q, ks):
    count = r.shape[0]
    below, diag = strict(count)
    raw = knt(two_rows(q), ks)
    share = jnp.sum(two_rows(r * u * k), axis=-1, keepdims=True)
    return jnp.where(below, raw, jnp.where(diag, share, 0.0))


def totals_kernel(k_ref, v_ref, w_ref, out_ref):
    cum = running(w_ref[...])
    total = cum[-1:, :]
    kc = k_ref[...] * jnp.exp(total - cum)
    out_ref[0, :SPAN, :] = fold(ktn(v_ref[...], kc))
    out_ref[0, SPAN:, :] = jnp.broadcast_to(jnp.exp(total), (8, 2 * SPAN))


def group_norm(y, gain, bias):
    centred = y - head_sum(y) * (1.0 / SPAN)
    spread = head_sum(centred * centred) * (1.0 / SPAN)
    scale = lax.rsqrt(spread + GN_EPS)
    normal = centred * scale
    return normal, scale, normal * gain + bias


def forward_kernel(r_ref, k_ref, v_ref, w_ref, g_ref, s_ref, p_ref, y_ref, gated_ref):
    r, k, v, w = r_ref[...], k_ref[...], v_ref[...], w_ref[...]
    cum = running(w)
    q = r * jnp.exp(cum - w)
    ks = k * jnp.exp(-cum)
    aff = affinity(r, k, p_ref[0:1, :], q, ks)
    count = r.shape[0]
    v2 = two_rows(v)
    y = (
        knt(q, unfold(s_ref[0]))
        + knn(aff[:count], v2[:count])
        + knn(aff[count:], v2[count:])
    )
    y_ref[...] = y
    gate = g_ref[...]
    _, _, grouped = group_norm(y, p_ref[1:2, :], p_ref[2:3, :])
    gated_ref[...] = (grouped * gate * jax.nn.sigmoid(gate)).astype(BF16)


def gate_kernel(gg_ref, g_ref, y_ref, r_ref, w_ref, p_ref, gate_ref, dy_ref, out_ref):
    gated_grad, gate, y = gg_ref[...], g_ref[...], y_ref[...]
    gain = p_ref[1:2, :]
    normal, scale, grouped = group_norm(y, gain, p_ref[2:3, :])
    sig = jax.nn.sigmoid(gate)
    gate_ref[...] = (gated_grad * grouped * sig * (1.0 + gate * (1.0 - sig))).astype(BF16)
    outer = gated_grad * gate * sig
    inner = outer * gain
    dy = scale * (
        inner
        - head_sum(inner) * (1.0 / SPAN)
        - normal * (head_sum(inner * normal) * (1.0 / SPAN))
    )
    dy_ref[...] = dy
    w = w_ref[...]
    q = r_ref[...] * jnp.exp(running(w) - w)
    out_ref[0, :SPAN, :] = fold(ktn(dy, q))
    gain_grad = jnp.sum(outer * normal, axis=0, keepdims=True)
    bias_grad = jnp.sum(outer, axis=0, keepdims=True)
    out_ref[0, SPAN:, :] = jnp.concatenate(
        [gain_grad, bias_grad, jnp.zeros((6, 2 * SPAN), F32)], axis=0
    )


def backward_kernel(
    r_ref, k_ref, v_ref, w_ref, dy_ref, s_ref, gs_ref, p_ref,
    dr_ref, dk_ref, dv_ref, dd_ref, out_ref,
):
    r, k, v, w, dy = r_ref[...], k_ref[...], v_ref[...], w_ref[...], dy_ref[...]
    u = p_ref[0:1, :]
    count = r.shape[0]
    cum = running(w)
    total = cum[-1:, :]
    e_before, e_minus, e_carry = jnp.exp(cum - w), jnp.exp(-cum), jnp.exp(total - cum)
    q, ks, kc = r * e_before, k * e_minus, k * e_carry
    aff = affinity(r, k, u, q, ks)
    below, _ = strict(count)
    dy2 = two_rows(dy)
    d_aff = jnp.where(below, knt(dy2, v), 0.0)
    own = head_sum(dy * v)
    state, grad_state = s_ref[0], gs_ref[0]
    state2, grad2 = unfold(state), unfold(grad_state)
    ks2 = two_rows(ks)
    dq = knn(dy, state2) + knn(d_aff[:count], ks2[:count]) + knn(d_aff[count:], ks2[count:])
    dks = ktn(d_aff, two_rows(q))
    dkc = knn(v, grad2)
    dv_ref[...] = (ktn(aff, dy2) + knt(kc, grad2)).astype(BF16)
    dr_ref[...] = (dq * e_before + own * u * k).astype(BF16)
    dk_ref[...] = (dks * e_minus + dkc * e_carry + own * u * r).astype(BF16)
    gq, gc = q * dq, kc * dkc
    d_total = jnp.sum(gc, axis=0, keepdims=True) + jnp.exp(total) * jnp.sum(
        state * grad_state, axis=0, keepdims=True
    )
    dw = running(gq - ks * dks - gc, upper=True) - gq + d_total
    term = dw * w
    dd_ref[...] = term.astype(BF16)
    out_ref[0] = jnp.concatenate(
        [
            jnp.sum(term, axis=0, keepdims=True),
            jnp.sum(own * r * k, axis=0, keepdims=True),
            jnp.zeros((6, 2 * SPAN), F32),
        ],
        axis=0,
    )


def block_call(kernel, chunks, step, width, ins, outs, args):
    lane = 2 * SPAN
    kinds = {
        "t": pl.BlockSpec((step, lane), lambda c, h: (c, h)),
        "s": pl.BlockSpec((1, SPAN, lane), lambda c, h: (c, 0, h)),
        "x": pl.BlockSpec((1, SPAN + 8, lane), lambda c, h: (c, 0, h)),
        "e": pl.BlockSpec((1, 8, lane), lambda c, h: (c, 0, h)),
        "p": pl.BlockSpec((8, lane), lambda c, h: (0, h)),
    }
    shapes = {
        "t": lambda d: jax.ShapeDtypeStruct((chunks * step, width), d),
        "x": lambda d: jax.ShapeDtypeStruct((chunks, SPAN + 8, width), d),
        "e": lambda d: jax.ShapeDtypeStruct((chunks, 8, width), d),
    }
    return pl.pallas_call(
        kernel,
        grid=(chunks, width // lane),
        in_specs=[kinds[kind] for kind in ins],
        out_specs=[kinds[kind] for kind, _ in outs],
        out_shape=[shapes[kind](dtype) for kind, dtype in outs],
        compiler_params=pltpu.CompilerParams(vmem_limit_bytes=48 * 1024 * 1024),
    )(*args)


def weight_grad(places, pairs, block):
    tokens, blocks = pairs[0][0].shape[0], places.shape[0]
    widths = [y.shape[1] for _, y in pairs]

    def kernel(_, *refs):
        at = 0
        for i, wide in enumerate(widths):
            refs[-1][0, :, at : at + wide] = tn(refs[2 * i][...], refs[2 * i + 1][...]).astype(
                BF16
            )
            at += wide

    specs = []
    for wide in widths:
        specs.append(pl.BlockSpec((tokens, block), lambda i, at: (0, at[i])))
        specs.append(pl.BlockSpec((tokens, wide), lambda i, at: (0, 0)))
    return pl.pallas_call(
        kernel,
        grid_spec=pltpu.PrefetchScalarGridSpec(
            num_scalar_prefetch=1,
            grid=(blocks,),
            in_specs=specs,
            out_specs=pl.BlockSpec((1, block, sum(widths)), lambda i, at: (i, 0, 0)),
        ),
        out_shape=jax.ShapeDtypeStruct((blocks, block, sum(widths)), BF16),
        compiler_params=pltpu.CompilerParams(vmem_limit_bytes=48 * 1024 * 1024),
    )(places, *[v for pair in pairs for v in pair])


def lanes_kernel(spans, x_ref, out_ref):
    at = 0
    for start, stop in spans:
        out_ref[:, at : at + stop - start] = x_ref[:, start:stop].astype(out_ref.dtype)
        at += stop - start


def move_lanes(spans, value, dtype):
    return pl.pallas_call(
        functools.partial(lanes_kernel, spans),
        in_specs=[pl.BlockSpec(memory_space=pltpu.VMEM)],
        out_specs=pl.BlockSpec(memory_space=pltpu.VMEM),
        out_shape=jax.ShapeDtypeStruct(value.shape, dtype),
        compiler_params=pltpu.CompilerParams(vmem_limit_bytes=32 * 1024 * 1024),
    )(value)


def place_kernel(counts, wide, block, at_ref, *refs):
    ins, out_ref, sems = refs[: len(counts)], refs[-2], refs[-1]
    rows = out_ref.shape[0]
    copies, i = [], 0
    for ref, n in zip(ins, counts):
        for j in range(n):
            start = pl.multiple_of(at_ref[i] * block, block)
            column = i * block // rows * wide
            copy = pltpu.make_async_copy(
                ref.at[pl.ds(j * block, block), :],
                out_ref.at[pl.ds(start, block), pl.ds(column, wide)],
                sems.at[i],
            )
            copy.start()
            copies.append(copy)
            i += 1
    for copy in copies:
        copy.wait()


def place_rows(parts, block):
    pieces = [p for part in parts for p in part[1]]
    wide = pieces[0].shape[1]
    at = jnp.concatenate([part[0] for part in parts])
    counts = [p.shape[0] // block for p in pieces]
    total = sum(counts)
    return pl.pallas_call(
        functools.partial(place_kernel, counts, wide, block),
        in_specs=[pl.BlockSpec(memory_space=pltpu.SMEM)]
        + [pl.BlockSpec(memory_space=pl.ANY)] * len(pieces),
        out_specs=pl.BlockSpec(memory_space=pl.ANY),
        out_shape=jax.ShapeDtypeStruct(
            (total * block // len(parts), wide * len(parts)), pieces[0].dtype
        ),
        scratch_shapes=[pltpu.SemaphoreType.DMA((total,))],
        compiler_params=pltpu.CompilerParams(vmem_limit_bytes=32 * 1024 * 1024),
    )(at, *pieces)


def mixes_kernel(
    open_ref, x_ref, before_ref, vec_ref, down_ref, up_ref, ddown_ref,
    m1_ref, m2_ref, m3_ref, m4_ref, dh_ref,
    normal_ref, scale_ref, delta_ref, blend_ref, m0_ref, tanh_ref, dtanh_ref,
):
    piece = pl.program_id(0)
    step = m1_ref.shape[0]
    x = x_ref[...].astype(F32)
    centred = x - jnp.mean(x, axis=-1, keepdims=True)
    scale = lax.rsqrt(jnp.mean(centred * centred, axis=-1, keepdims=True) + LN_EPS)
    normal = centred * scale
    full = normal * vec_ref[0:1, :] + vec_ref[1:2, :]
    normed = full[:step]
    first = jnp.where(open_ref[piece] == 1, before_ref[0:1, :], full[step : step + 1])
    row = lax.broadcasted_iota(jnp.int32, normed.shape, 0)
    delta = jnp.where(row == 0, first, pltpu.roll(normed, 1, 0)) - normed
    blend = (normed + delta * vec_ref[2:3, :]).astype(BF16)
    tanh = jnp.tanh(nn(blend, down_ref[...]))
    latent = tanh.astype(BF16)
    lane = lax.broadcasted_iota(jnp.int32, latent.shape, 1)
    mixed = []
    for c in range(5):
        own = (lane >= c * RANK) & (lane < (c + 1) * RANK)
        offset = nt(jnp.where(own, latent, jnp.zeros_like(latent)), up_ref[...])
        mixed.append((normed + delta * (vec_ref[3 + c : 4 + c, :] + offset)).astype(BF16))
    dtanh = jnp.tanh(nn(mixed[0], ddown_ref[...]))
    m1_ref[...], m2_ref[...], m3_ref[...], m4_ref[...] = mixed[1:]
    dh_ref[...] = dtanh.astype(BF16)

    @pl.when(piece == 0)
    def _():
        normal_ref[...] = normal[:step]
        scale_ref[...] = jnp.broadcast_to(scale[:step], scale_ref.shape)
        delta_ref[...] = delta
        blend_ref[...] = blend
        m0_ref[...] = mixed[0]
        tanh_ref[...] = tanh
        dtanh_ref[...] = dtanh


def group_mixes(opening, x, before, vec, down, up, ddown, step):
    high, width = step + 16, x.shape[1]
    pieces = x.shape[0] // high

    def whole(value):
        return pl.BlockSpec(value.shape, lambda k: (0, 0))

    def own(columns, dtype):
        return (
            pl.BlockSpec((step, columns), lambda k: (0, 0)),
            jax.ShapeDtypeStruct((step, columns), dtype),
        )

    def every(columns, dtype):
        return (
            pl.BlockSpec((step, columns), lambda k: ((k % 2) * 2 + k // 2, 0)),
            jax.ShapeDtypeStruct((pieces * step, columns), dtype),
        )

    outs = [every(width, BF16)] * 4 + [
        every(DRANK, BF16),
        own(width, F32),
        own(128, F32),
        own(width, F32),
        own(width, BF16),
        own(width, BF16),
        own(5 * RANK, F32),
        own(DRANK, F32),
    ]
    return pl.pallas_call(
        mixes_kernel,
        grid=(pieces,),
        in_specs=[
            pl.BlockSpec(memory_space=pltpu.SMEM),
            pl.BlockSpec((high, width), lambda k: (k, 0)),
            whole(before),
            whole(vec),
            whole(down),
            whole(up),
            whole(ddown),
        ],
        out_specs=[o[0] for o in outs],
        out_shape=[o[1] for o in outs],
        compiler_params=pltpu.CompilerParams(vmem_limit_bytes=56 * 1024 * 1024),
    )(opening, x, before, vec, down, up, ddown)


def product(pairs, outs, body, sides=(), tile=256):
    count = len(pairs)

    def kernel(*refs):
        ins, out_refs = refs[: 2 * count + len(sides)], refs[2 * count + len(sides) :]
        products = [
            (nn if pair[2] == "nn" else nt)(ins[2 * i][...], ins[2 * i + 1][...])
            for i, pair in enumerate(pairs)
        ]
        results = body(*products, *[r[...] for r in ins[2 * count :]])
        for ref, value in zip(out_refs, results):
            ref[...] = value.astype(ref.dtype)

    specs, args = [], []
    for a, b, form, at in pairs:
        depth = a.shape[1]
        specs.append(pl.BlockSpec(a.shape, lambda j: (0, 0)))
        if form == "nn":
            specs.append(pl.BlockSpec((depth, tile), lambda j, at=at: (0, at + j)))
        else:
            specs.append(pl.BlockSpec((tile, depth), lambda j, at=at: (j, at)))
        args += [a, b]
    for side in sides:
        specs.append(pl.BlockSpec((side.shape[0], tile), lambda j: (0, j)))
    return pl.pallas_call(
        kernel,
        grid=(outs[0][1] // tile,),
        in_specs=specs,
        out_specs=[pl.BlockSpec((o[0], tile), lambda j: (0, j)) for o in outs],
        out_shape=[jax.ShapeDtypeStruct(o[:2], o[2]) for o in outs],
        compiler_params=pltpu.CompilerParams(vmem_limit_bytes=56 * 1024 * 1024),
    )(*args, *sides)


def local(fn, outs, *args, scalar=None):
    def kernel(*refs):
        lead = [] if scalar is None else [refs[0]]
        ins, out_refs = refs[len(lead) : -len(outs)], refs[-len(outs) :]
        results = fn(*[r[0] for r in lead], *[r[...] for r in ins])
        for ref, value in zip(out_refs, results):
            ref[...] = value.astype(ref.dtype)

    specs = [pl.BlockSpec(memory_space=pltpu.VMEM)] * len(args)
    if scalar is not None:
        specs = [pl.BlockSpec(memory_space=pltpu.SMEM)] + specs
        args = (scalar.reshape(1), *args)
    return pl.pallas_call(
        kernel,
        in_specs=specs,
        out_specs=[pl.BlockSpec(memory_space=pltpu.VMEM)] * len(outs),
        out_shape=[jax.ShapeDtypeStruct(o[:2], o[2]) for o in outs],
        compiler_params=pltpu.CompilerParams(vmem_limit_bytes=56 * 1024 * 1024),
    )(*args)


def take_lanes(value, spans):
    if len(spans) == 1:
        return value
    return jnp.concatenate([value[:, a:b] for a, b in spans], axis=1)


def norm_back(grad, gain, normal, scale):
    e = grad * gain
    return scale * (
        e
        - jnp.mean(e, axis=-1, keepdims=True)
        - normal * jnp.mean(e * normal, axis=-1, keepdims=True)
    )


def rows_above(value, first):
    row = lax.broadcasted_iota(jnp.int32, value.shape, 0)
    return jnp.where(row == 0, first, pltpu.roll(value, 1, 0))


def rows_below(value, last):
    row = lax.broadcasted_iota(jnp.int32, value.shape, 0)
    high = value.shape[0]
    return jnp.where(row == high - 1, last, pltpu.roll(value, high - 1, 0))


def padded(rows):
    return jnp.concatenate(
        list(rows) + [jnp.zeros((8 - len(rows), rows[0].shape[1]), F32)], axis=0
    )


def column_sum(value):
    return jnp.sum(value, axis=0, keepdims=True)


def gates_kernel(
    spans, who_ref, middle_ref, value_ref, more_ref, act_ref, cot_ref,
    out_ref, up_ref, vg_ref, rg_ref, held,
):
    to_spans, from_spans = spans
    step, part = act_ref.shape[0] // 4, act_ref.shape[1]
    who = who_ref[0]
    act = [
        act_ref[pl.ds(pl.multiple_of((who ^ j) * step, step), step), :] for j in range(4)
    ]
    recept = jax.nn.sigmoid(take_lanes(jnp.concatenate(act, axis=1).astype(F32), to_spans))
    value = value_ref[...] + more_ref[...].astype(F32)
    out = middle_ref[...] + recept * value
    out_ref[...] = take_lanes(out, from_spans).astype(BF16)
    up = take_lanes(cot_ref[...].astype(F32), to_spans)
    up_ref[...] = up
    vg_ref[...] = (up * recept).astype(BF16)
    held[...] = take_lanes(up * value * recept * (1.0 - recept), from_spans)
    for k in range(4):
        at = pl.multiple_of((who ^ k) * part, part)
        rg_ref[k * step : (k + 1) * step, :] = held[:, pl.ds(at, part)].astype(BF16)


def gates(spans, who, middle, value, more, act, cot):
    step, width = middle.shape
    part = act.shape[1]
    shape = jax.ShapeDtypeStruct
    return pl.pallas_call(
        functools.partial(gates_kernel, spans),
        in_specs=[pl.BlockSpec(memory_space=pltpu.SMEM)]
        + [pl.BlockSpec(memory_space=pltpu.VMEM)] * 5,
        out_specs=[pl.BlockSpec(memory_space=pltpu.VMEM)] * 4,
        out_shape=[
            shape((step, width), BF16),
            shape((step, width), F32),
            shape((step, width), BF16),
            shape((4 * step, part), BF16),
        ],
        scratch_shapes=[pltpu.VMEM((step, width), F32)],
        compiler_params=pltpu.CompilerParams(vmem_limit_bytes=56 * 1024 * 1024),
    )(who.reshape(1), middle, value, more, act, cot)


def mixes_back_kernel(
    kept_ref, got_ref, dl_ref, dl_more_ref, delta_ref, tanh_ref, dtanh_ref, blend_ref, m0_ref,
    down_ref, up_ref, ddown_ref, vec_ref,
    rest_ref, dg_ref, row_ref, cols_ref, down_out, up_out, ddown_out,
):
    step = delta_ref.shape[0]
    dtanh = dtanh_ref[...]
    decay_grad = dl_ref[...] + dl_more_ref[...].astype(F32)
    decay_pre = (decay_grad * (1.0 - dtanh * dtanh)).astype(BF16)
    ddown_out[...] = tn(m0_ref[...], decay_pre)
    tanh = tanh_ref[...]
    latent = tanh.astype(BF16)
    lane = lax.broadcasted_iota(jnp.int32, latent.shape, 1)
    delta, up = delta_ref[...], up_ref[...]
    latent_grad = jnp.zeros(latent.shape, F32)
    up_grad = jnp.zeros(up_out.shape, F32)
    dg = jnp.zeros(delta.shape, F32)
    total = jnp.zeros(delta.shape, F32)
    cols = []
    for c in range(5):
        own = (lane >= c * RANK) & (lane < (c + 1) * RANK)
        mine = jnp.where(own, latent, jnp.zeros_like(latent))
        if c == 0:
            grad = nt(decay_pre, ddown_ref[...])
        else:
            at = slice((c - 1) * step, c * step)
            grad = kept_ref[at, :] + got_ref[at, :].astype(F32)
        shift = grad * delta
        cols.append(column_sum(shift))
        offset = shift.astype(BF16)
        latent_grad = jnp.where(own, nn(offset, up), latent_grad)
        up_grad = up_grad + tn(offset, mine)
        dg = dg + grad * (vec_ref[3 + c : 4 + c, :] + nt(mine, up))
        total = total + grad
    up_out[...] = up_grad
    mix_pre = (latent_grad * (1.0 - tanh * tanh)).astype(BF16)
    down_out[...] = tn(blend_ref[...], mix_pre)
    blend_grad = nt(mix_pre, down_ref[...])
    dg = dg + blend_grad * vec_ref[2:3, :]
    rest_ref[...] = total + blend_grad - dg
    dg_ref[...] = dg
    row_ref[...] = dg[:8]
    cols_ref[...] = padded([column_sum(blend_grad * delta)] + cols)


def mixes_back(*args):
    delta, down, ddown = args[4], args[9], args[11]
    step, width = delta.shape
    shape = jax.ShapeDtypeStruct
    outs = [
        shape((step, width), F32),
        shape((step, width), F32),
        shape((8, width), F32),
        shape((8, width), F32),
        shape(down.shape, F32),
        shape(down.shape, F32),
        shape(ddown.shape, F32),
    ]
    return pl.pallas_call(
        mixes_back_kernel,
        in_specs=[pl.BlockSpec(memory_space=pltpu.VMEM)] * len(args),
        out_specs=[pl.BlockSpec(memory_space=pltpu.VMEM)] * len(outs),
        out_shape=outs,
        compiler_params=pltpu.CompilerParams(vmem_limit_bytes=60 * 1024 * 1024),
    )(*args)


def tie(*values):
    return lax.optimization_barrier(values)


def on_device(
    count,
    tokens,
    previous,
    initial_state,
    mixing_weights,
    lowrank_weights,
    vectors,
    feedforward_weights,
    cotangent,
):
    fast = initial_state.shape[0] == 64
    masks = (1, 8) if fast else (1, 2)
    size = 1 << len(masks)
    teams = count // size
    all_masks = [1 << b for b in range(count.bit_length() - 1)]
    team_masks = [b for b in all_masks if b not in masks]
    far = 16
    team_masks.sort(key=lambda b: fast and b != far)
    me = lax.axis_index("seq")
    _, step, width = tokens.shape
    rows = mixing_weights.shape[0]
    part = width // size
    ff_part = FF // size
    team_rows = rows * size
    def bit_of(who, mask):
        return (who // mask) % 2 if isinstance(who, int) else lax.rem(lax.div(who, mask), 2)

    def member_of(who):
        return sum(bit_of(who, b) << j for j, b in enumerate(masks))

    def team_of(who):
        return sum(bit_of(who, b) << j for j, b in enumerate(team_masks))

    member, team = member_of(me), team_of(me)
    order = sorted(range(count), key=lambda d: (team_of(d), member_of(d)))
    inverse = sorted(range(count), key=lambda p: order[p])
    across = [order[m::size] for m in range(size)]
    square = [order[m :: 2 * size] for m in range(2 * size)]
    def lane_spans(blocks):
        spans = []
        for d in blocks:
            if spans and spans[-1][1] == d * rows:
                spans[-1][1] = (d + 1) * rows
            else:
                spans.append([d * rows, (d + 1) * rows])
        return spans

    to_spans, from_spans = lane_spans(order), lane_spans(inverse)

    def to_places(value, dtype):
        return move_lanes(to_spans, value, dtype)

    def flips(k):
        return sum(b for j, b in enumerate(masks) if (k >> j) & 1)

    def trade(value, mask):
        return lax.ppermute(value, "seq", [(d, d ^ mask) for d in range(count)])

    def group_gather(value):
        side = trade(value, masks[1])
        return value, side, trade(jnp.concatenate([value, side], axis=0), masks[0])

    def group_rows(value):
        high, columns = value.shape

        def lay(own, side, far):
            return (jnp.concatenate([own, far[:high], side, far[high:]], axis=0),)

        return local(lay, [(size * high, columns, value.dtype)], *group_gather(value))[0]

    def halves(value):
        cut = [value[k * step : (k + 1) * step] for k in range(size)]
        return [cut[0], cut[2]], [cut[1], cut[3]]

    def group_fold(kept, sent):
        high, columns = kept.shape[0] // 2, kept.shape[1]
        got = trade(sent, masks[0])

        def add(mine, more):
            total = mine + more.astype(F32)
            return total[:high], total[high:]

        return local(add, [(high, columns, F32), (high, columns, BF16)], kept, got)

    def group_sum(kept, sent):
        mine, side = group_fold(kept, sent)
        return mine, trade(side, masks[1])

    def crossing_sum(*pairs):
        units = len(pairs)

        def body(*products):
            parts = [halves(p) for p in products]
            kept = [p[0][i] for i in range(2) for p in parts]
            sent = [p[1][i] for i in range(2) for p in parts]
            return jnp.concatenate(kept, axis=0), jnp.concatenate(sent, axis=0)

        high = 2 * units * step
        return product(
            [(a, b, "nt", at) for a, b, at in pairs],
            [(high, width, F32), (high, width, BF16)],
            body,
            tile=512,
        )

    def exchange(pieces):
        pieces, high = list(pieces), pieces[0].shape[0]
        for j in reversed(range(len(masks))):
            keys = [k for k in range(size) if (k >> j) & 1]
            got = trade(jnp.concatenate([pieces[k] for k in keys], axis=0), masks[j])
            for i, k in enumerate(keys):
                pieces[k] = got[i * high : (i + 1) * high]
        return pieces

    def ordered(pieces):
        pieces = list(pieces)
        for j in range(len(masks)):
            swap = lax.rem(lax.div(member, 1 << j), 2) == 1
            pieces = [
                jnp.where(swap, pieces[k ^ (1 << j)], pieces[k]) for k in range(len(pieces))
            ]
        return pieces

    def neighbour(value, offset):
        pairs = [(d, d + offset) for d in range(count) if 0 <= d + offset < count]
        return lax.ppermute(value, "seq", pairs)

    def take_columns(value, spans, who):
        return jnp.concatenate(
            [
                lax.dynamic_slice_in_dim(value, start + who * wide, wide, axis=1)
                for start, wide in spans
            ],
            axis=1,
        )

    def group_columns(value, spans):
        pieces = [take_columns(value, spans, member ^ k) for k in range(size)]
        return jnp.concatenate(ordered(exchange(pieces)), axis=0)

    def crossing(first):
        bits = list(range(1, len(team_masks))) + [0]
        if first:
            bits[0], bits[1] = bits[1], bits[0]
        return bits

    def gather_rows(own):
        return lax.all_gather(own, "seq", axis=0, tiled=True, axis_index_groups=across)

    def far_send(own):
        return trade(own, far) if fast else own

    def far_join(own, got):
        if not fast:
            return own
        upper = bit_of(me, far) == 1
        return jnp.concatenate(
            [jnp.where(upper, got, own), jnp.where(upper, own, got)], axis=0
        )

    def gather_square(paired):
        groups = square if fast else across
        return lax.all_gather(paired, "seq", axis=0, tiled=True, axis_index_groups=groups)

    def team_products(*pairs):
        if fast:
            places = jnp.arange(teams, dtype=jnp.int32)
            return weight_grad(places, pairs, team_rows).reshape(width, -1)
        return jnp.concatenate([tn(x, y).astype(BF16) for x, y in pairs], axis=1)

    def square_sum(grads):
        groups = square if fast else across
        return lax.psum_scatter(
            grads, "seq", scatter_dimension=0, tiled=True, axis_index_groups=groups
        )

    def far_split(pair):
        if not fast:
            return pair, jnp.zeros_like(pair)
        bit = bit_of(me, far)
        sent = lax.dynamic_slice_in_dim(pair, (1 - bit) * team_rows, team_rows, axis=0)
        kept = lax.dynamic_slice_in_dim(pair, bit * team_rows, team_rows, axis=0)
        return kept, trade(sent, far)

    def far_add(kept, got):
        return (kept.astype(F32) + got.astype(F32)).astype(BF16)

    def cube_gather(value, follower=None):
        for mask in reversed(all_masks):
            got = trade(value, mask)
            upper = bit_of(me, mask) == 1
            value = jnp.stack([jnp.where(upper, got, value), jnp.where(upper, value, got)])
            if mask == 8 and follower is not None:
                value, follower = tie(value, follower)
        axes = len(all_masks)
        cube = value.transpose(*reversed(range(axes)), *range(axes, value.ndim))
        return cube if follower is None else (cube, follower)

    place_axes = [all_masks[::-1].index(b) for b in team_masks[::-1] + list(masks[::-1])]

    def by_place(cube):
        rest = range(len(all_masks), cube.ndim)
        return cube.transpose(*place_axes, *rest).reshape(width, -1)

    def to_cube(value):
        cube = value.reshape(*[2] * len(place_axes), rows, -1)
        back = [place_axes.index(a) for a in range(len(place_axes))]
        return cube.transpose(*back, len(back), len(back) + 1)

    def cube_sum(cube, kind):
        for axis, mask in reversed(list(enumerate(reversed(all_masks)))):
            bit = bit_of(me, mask)
            sent = lax.dynamic_index_in_dim(cube, 1 - bit, axis, keepdims=False)
            kept = lax.dynamic_index_in_dim(cube, bit, axis, keepdims=False)
            cube = kept.astype(F32) + trade(sent.astype(kind), mask).astype(F32)
        return cube

    def hand_rows(pieces, extra=None):
        widths = [sum(p.shape[1] for p in piece) for piece in pieces]
        joint = jnp.concatenate([p for piece in pieces for p in piece], axis=1)
        mine = [
            lax.dynamic_slice_in_dim(joint, (member ^ k) * rows, rows, axis=0)
            for k in range(size)
        ]
        if extra is not None:
            mine = [jnp.concatenate([m, e], axis=1) for m, e in zip(mine, extra)]
        by_place = exchange(mine)
        by_member = ordered(by_place)
        outs, start = [], 0
        for wide in widths:
            outs += [p[:, start : start + wide] for p in by_member]
            start += wide
        joined = jnp.concatenate(outs, axis=1).astype(F32)
        if extra is None:
            return joined
        return joined, [p[:, start:].astype(F32) for p in by_place]

    up_start, decay_start, decay_up = 5 * RANK, 10 * RANK, 10 * RANK + DRANK
    last_row = neighbour(tokens[0, -1:, :], 1)
    tokens_sent = to_places(
        jnp.concatenate([tokens[0], jnp.broadcast_to(last_row, (16, width))], axis=0), BF16
    )
    natural, mix_in = cube_gather(
        jnp.concatenate(
            [vectors, initial_state, lowrank_weights[:, decay_up:].astype(F32)], axis=1
        ),
        mixing_weights,
    )
    natural = natural.reshape(width, -1)
    low_cube, mix_in = cube_gather(lowrank_weights[:, :decay_up], mix_in)
    tokens_all = jnp.concatenate(group_gather(tokens_sent), axis=0)
    mix_local = group_columns(mix_in, [(c * width, part) for c in range(5)])
    mix_local, natural, low_cube, tokens_all = tie(mix_local, natural, low_cube, tokens_all)
    lowrank = by_place(low_cube)
    mix_kv, mix_rest = mix_local[:, : 2 * part], mix_local[:, 2 * part :]
    kv_got, mix_rest = tie(far_send(mix_kv), mix_rest)
    w_kv = gather_square(far_join(mix_kv, kv_got))
    tiles = part // 256

    mine = lax.dynamic_slice_in_dim(natural, member * part, part, axis=0)
    vec_part = mine[:, :16].T
    first_state = mine[:, 16 : 16 + SPAN].T
    w_dup = mine[:, 16 + SPAN :].astype(BF16)
    vec = by_place(
        natural[:, :16].reshape(*[2] * len(all_masks), rows, 16)
    ).T
    wkv_rows = jnp.concatenate([vec_part[9:12], jnp.zeros((5, part), F32)], axis=0)
    is_first = (me == 0).astype(jnp.int32)
    before = to_places(previous.reshape(2, width), F32)
    w_down, w_up = lowrank[:, :up_start], lowrank[:, up_start:decay_start]
    w_ddown = lowrank[:, decay_start:]

    opening = jnp.stack(
        [jnp.bitwise_xor(me, flips(k)) == 0 for k in (0, 2, 1, 3)]
    ).astype(jnp.int32)
    (
        *mixed_all, dh_all, normal_one, scale_one, delta, blend, mixed_zero, mix_tanh, decay_tanh,
    ) = group_mixes(opening, tokens_all, before, vec, w_down, w_up, w_ddown, step)
    rest_got, mixed_all[0], feed_in = tie(far_send(mix_rest), mixed_all[0], feedforward_weights)
    w_rest = gather_square(far_join(mix_rest, rest_got))
    ff_spans = [(0, ff_part), (FF, part), (FF + width, ff_part)]
    ff_local = group_columns(feed_in, ff_spans)
    everyone = size * step
    (log_decay,) = product(
        [(dh_all, w_dup, "nt", 0)],
        [(everyone, part, F32)],
        lambda acc, base: (-jnp.exp(base + acc),),
        sides=(vec_part[8:9],),
    )
    keys, values = product(
        [(mixed_all[0], w_kv, "nn", 0), (mixed_all[1], w_kv, "nn", tiles)],
        [(everyone, part, F32)] * 2,
        lambda a, b: (a, b),
    )

    keys, ff_local = tie(keys, ff_local)
    ff_tail = ff_local[:, ff_part + part :]
    ff_near = ff_local[:, : ff_part + part]
    near_got = far_send(ff_near)

    call = functools.partial(block_call, chunks=size, step=step, width=part)
    (totals,) = call(
        totals_kernel, ins="ttt", outs=[("x", F32)], args=(keys, values, log_decay)
    )
    by_member = ordered([totals[k] for k in range(size)])
    total = {m: (p[SPAN : SPAN + 1], p[:SPAN]) for m, p in enumerate(by_member)}
    before_chunk = [
        (jnp.ones((1, part), F32), jnp.zeros((SPAN, part), F32)) for _ in range(size)
    ]
    open_bits = size - 1
    levels = []

    def chain(early, late):
        return early[0] * late[0], late[0] * early[1] + late[1]

    def pick(flag, yes, no):
        return tuple(jnp.where(flag, a, b) for a, b in zip(yes, no))

    for mask in all_masks:
        if mask in masks:
            bit = 1 << masks.index(mask)
            levels.append({g: total[g][0] for g in total})
            for m in range(size):
                if m & bit:
                    early = (m & open_bits) ^ bit
                    before_chunk[m] = chain(total[early], before_chunk[m])
            total = {g: chain(total[g], total[g | bit]) for g in total if not g & bit}
            open_bits ^= bit
        else:
            groups = list(total)
            sent = jnp.concatenate(
                [
                    jnp.concatenate(
                        [total[g][1], jnp.broadcast_to(total[g][0], (8, part))], axis=0
                    )
                    for g in groups
                ],
                axis=0,
            )
            got = trade(sent, mask)
            high = SPAN + 8
            other = {
                g: (got[i * high + SPAN : i * high + SPAN + 1], got[i * high : i * high + SPAN])
                for i, g in enumerate(groups)
            }
            levels.append({g: (total[g][0], other[g][0]) for g in groups})
            late = bit_of(me, mask) == 1
            for m in range(size):
                g = m & open_bits
                before_chunk[m] = pick(late, chain(other[g], before_chunk[m]), before_chunk[m])
            total = {
                g: pick(late, chain(other[g], total[g]), chain(total[g], other[g]))
                for g in groups
            }
            if mask == 4:
                first_sum, near_got, ff_tail = tie(total[0][1], near_got, ff_tail)
                total[0] = total[0][0], first_sum
    state_in = jnp.stack(ordered([d * first_state + s for d, s in before_chunk]))
    w_near = gather_square(far_join(ff_near, near_got))
    w_key, w_rec = w_near, w_near[:, ff_part:]
    val_got = far_send(ff_tail)

    receipt, gate_pre = product(
        [(mixed_all[2], w_rest, "nn", 0), (mixed_all[3], w_rest, "nn", tiles)],
        [(everyone, part, F32)] * 2,
        lambda a, b: (a, b),
    )
    wkv, gated = call(
        forward_kernel,
        ins="tttttsp",
        outs=[("t", F32), ("t", BF16)],
        args=(receipt, keys, values, log_decay, gate_pre, state_in, wkv_rows),
    )
    gated, val_got = tie(gated, val_got)
    w_val = gather_square(far_join(ff_tail, val_got))
    branch, branch_more = group_sum(*crossing_sum((gated, w_rest, 2)))

    def norm_two(hidden, mine, more, vec):
        middle = hidden[:step].astype(F32) + mine + more.astype(F32)
        centred = middle - jnp.mean(middle, axis=-1, keepdims=True)
        scale = lax.rsqrt(jnp.mean(centred * centred, axis=-1, keepdims=True) + LN_EPS)
        normal = centred * scale
        tail = normal[step - 8 :] * vec[12:13] + vec[13:14]
        return middle, normal, jnp.broadcast_to(scale, (step, 128)), tail

    whole = (step, width, F32)
    middle, normal_two, scale_two, tail_two = local(
        norm_two,
        [whole, whole, (step, 128, F32), (8, width, F32)],
        tokens_sent,
        branch,
        branch_more,
        vec,
    )

    def mix_two(first, normal, arrived, before, vec):
        normed = normal * vec[12:13] + vec[13:14]
        above = jnp.where(first == 1, before[1:2], arrived[7:8])
        delta = rows_above(normed, above) - normed
        key_in, recv_in = normed + delta * vec[14:15], normed + delta * vec[15:16]
        return jnp.concatenate([key_in, recv_in], axis=0), delta

    both, delta_two = local(
        mix_two,
        [(2 * step, width, BF16), whole],
        normal_two,
        neighbour(tail_two, 1),
        before,
        vec,
        scalar=is_first,
    )

    key_all, recv_all = group_rows(both[:step]), group_rows(both[step:])
    relu, squared = product(
        [(key_all, w_key, "nn", 0)],
        [(everyone, ff_part, F32), (everyone, ff_part, BF16)],
        lambda acc: (jnp.maximum(acc, 0.0), jnp.square(jnp.maximum(acc, 0.0))),
        tile=ff_part // 2,
    )
    (recept_act,) = product(
        [(recv_all, w_rec, "nn", 0)],
        [(everyone, part, BF16)],
        lambda acc: (acc,),
    )
    squared, recept_act = tie(squared, recept_act)
    acts = exchange([recept_act[k * step : (k + 1) * step] for k in range(size)])
    value, value_more = group_sum(*crossing_sum((squared, w_val, 0)))
    block_output, upstream, value_grad, recept_grads = gates(
        (to_spans, from_spans),
        member,
        middle,
        value,
        value_more,
        jnp.concatenate(acts, axis=0),
        cotangent.reshape(step, width),
    )

    rg_all = jnp.concatenate(
        exchange([recept_grads[k * step : (k + 1) * step] for k in range(size)]), axis=0
    )
    vg_all = group_rows(value_grad)
    val_grads = team_products((vg_all, squared))
    vg_all, val_grads, rg_all = tie(vg_all, val_grads, rg_all)
    val_pair = square_sum(val_grads)
    (key_grad,) = product(
        [(vg_all, w_val, "nn", 0)],
        [(everyone, ff_part, BF16)],
        lambda acc, relu: (acc * (2.0 * relu),),
        sides=(relu,),
        tile=ff_part // 2,
    )
    key_grads = team_products((key_all, key_grad))
    key_grad, key_grads = tie(key_grad, key_grads)
    key_pair = square_sum(key_grads)
    recv_two = group_sum(*crossing_sum((rg_all, w_rec, 0)))
    key_two = group_sum(*crossing_sum((key_grad, w_key, 0)))

    def inputs_back(key, key_more, recv, recv_more, vec):
        key, recv = key + key_more.astype(F32), recv + recv_more.astype(F32)
        top = key[:8] * vec[14:15] + recv[:8] * vec[15:16]
        return jnp.concatenate([key, recv], axis=0), top

    in_grads, top_two = local(
        inputs_back, [(2 * step, width, F32), (8, width, F32)], *key_two, *recv_two, vec
    )
    last_flag = (me == count - 1).astype(jnp.int32)

    def norm_two_back(last, grads, arrived, upstream, normal, scale, delta, vec):
        key_grad, recv_grad = grads[:step], grads[step:]
        shifted = key_grad * vec[14:15] + recv_grad * vec[15:16]
        below = jnp.where(last == 1, jnp.zeros_like(arrived[:1]), arrived[:1])
        grad = (
            key_grad * (1.0 - vec[14:15])
            + recv_grad * (1.0 - vec[15:16])
            + rows_below(shifted, below)
        )
        out = upstream + norm_back(grad, vec[12:13], normal, scale[:, :1])
        cols = padded(
            [
                column_sum(grad * normal),
                column_sum(grad),
                column_sum(key_grad * delta),
                column_sum(recv_grad * delta),
            ]
        )
        return out, out, cols

    middle_grad, branch_grad, cols_two = local(
        norm_two_back,
        [whole, (step, width, BF16), (8, width, F32)],
        in_grads,
        neighbour(top_two, -1),
        upstream,
        normal_two,
        scale_two,
        delta_two,
        vec,
        scalar=last_flag,
    )

    bg_all = group_rows(branch_grad)
    (gated_grad,) = product(
        [(bg_all, w_rest, "nn", 2 * tiles)], [(everyone, part, F32)], lambda acc: (acc,)
    )
    gate_grad, wkv_grad, ends = call(
        gate_kernel,
        ins="tttttp",
        outs=[("t", BF16), ("t", F32), ("x", F32)],
        args=(gated_grad, gate_pre, wkv, receipt, log_decay, wkv_rows),
    )
    grad_total = dict(enumerate(ordered([ends[k, :SPAN] for k in range(size)])))
    after = [(jnp.ones((1, part), F32), jnp.zeros((SPAN, part), F32)) for _ in range(size)]
    open_bits = size - 1
    for mask, level in zip(all_masks, levels):
        if mask in masks:
            bit = 1 << masks.index(mask)
            for m in range(size):
                if not m & bit:
                    late = (m & open_bits) | bit
                    d, s = after[m]
                    after[m] = (d * level[late], d * grad_total[late] + s)
            grad_total = {
                g: grad_total[g] + level[g] * grad_total[g | bit]
                for g in grad_total
                if not g & bit
            }
            open_bits ^= bit
        else:
            groups = list(grad_total)
            got = trade(jnp.concatenate([grad_total[g] for g in groups], axis=0), mask)
            other = {g: got[i * SPAN : (i + 1) * SPAN] for i, g in enumerate(groups)}
            early = bit_of(me, mask) == 0
            for m in range(size):
                g = m & open_bits
                d, s = after[m]
                after[m] = pick(early, (d * level[g][1], d * other[g] + s), (d, s))
            grad_total = {
                g: jnp.where(
                    early,
                    grad_total[g] + level[g][0] * other[g],
                    other[g] + level[g][1] * grad_total[g],
                )
                for g in groups
            }
    grad_out = jnp.stack(ordered([s for _, s in after]))
    out_grads = team_products((bg_all, gated), (recv_all, rg_all), (mixed_all[3], gate_grad))
    grad_out, out_grads, val_pair = tie(grad_out, out_grads, val_pair)
    out_pair = square_sum(out_grads)

    d_receipt, d_keys, d_values, d_decay, extra = call(
        backward_kernel,
        ins="tttttssp",
        outs=[("t", BF16)] * 4 + [("e", F32)],
        args=(receipt, keys, values, log_decay, wkv_grad, state_in, grad_out, wkv_rows),
    )
    grads = [d_keys, d_values, d_receipt, gate_grad]
    kept, sent = crossing_sum(
        *[(grads[c], w_rest if c > 1 else w_kv, c % 2) for c in range(4)]
    )
    main_grads = team_products(
        (mixed_all[0], d_keys), (mixed_all[1], d_values), (mixed_all[2], d_receipt)
    )

    def latent_back(grad, up):
        kept, sent = halves(nn(grad, up))
        return jnp.concatenate(kept, axis=0), jnp.concatenate(sent, axis=0)

    latent_mine, latent_more = group_sum(
        *local(
            latent_back, [(2 * step, DRANK, F32), (2 * step, DRANK, BF16)], d_decay, w_dup
        )
    )
    sent, main_grads, latent_more = tie(sent, main_grads, latent_more)
    main_pair = square_sum(main_grads)
    val_kept, val_got = far_split(val_pair)
    key_kept, key_got = far_split(key_pair)
    out_kept, out_got = far_split(out_pair)
    sent, val_got, key_got = tie(sent, val_got, key_got)
    mixed_mine, mixed_more = group_sum(kept, sent)
    val_sum, key_sum = far_add(val_kept, val_got), far_add(key_kept, key_got)
    rest_grad, delta_grad, top_one, cols_mix, down_grad, up_grad, ddown_grad = mixes_back(
        mixed_mine,
        mixed_more,
        latent_mine,
        latent_more,
        delta,
        mix_tanh,
        decay_tanh,
        blend,
        mixed_zero,
        w_down,
        w_up,
        w_ddown,
        vec,
    )
    rest_grad, main_pair, out_got = tie(rest_grad, main_pair, out_got)
    out_sum = far_add(out_kept, out_got)

    def norm_one_back(last, rest, shifted, arrived, normal, scale, middle, vec):
        below = jnp.where(last == 1, jnp.zeros_like(arrived[:1]), arrived[:1])
        grad = rest + rows_below(shifted, below)
        out = middle + norm_back(grad, vec[0:1], normal, scale[:, :1])
        cols = padded([column_sum(grad * normal), column_sum(grad)])
        return take_lanes(out, from_spans), cols

    block_input_gradient, cols_one = local(
        norm_one_back,
        [whole, (8, width, F32)],
        rest_grad,
        delta_grad,
        neighbour(top_one, -1),
        normal_one,
        scale_one,
        middle_grad,
        vec,
        scalar=last_flag,
    )
    main_sum = far_add(*far_split(main_pair))

    def column_parts(value):
        return [value[:, c * part : (c + 1) * part] for c in range(3)]

    out_cols, main_cols = column_parts(out_sum), column_parts(main_sum)
    first_grad = grad_total[0]
    holder = lax.div(me * rows, part)

    def rows_of(who):
        mine = lax.dynamic_slice_in_dim(first_grad, lax.rem(who * rows, part), rows, axis=1).T
        high = lax.reduce_precision(mine, 8, 7)
        return jnp.concatenate([high, mine - high], axis=1).astype(BF16)

    feedforward_gradient, handed = hand_rows(
        [[key_sum], [out_cols[1]], [val_sum]],
        [rows_of(jnp.bitwise_xor(me, flips(k))) for k in range(size)],
    )
    state_rows = handed[0]
    for k in range(1, size):
        state_rows = jnp.where(holder == (member ^ k), handed[k], state_rows)
    initial_state_gradient = state_rows[:, :SPAN] + state_rows[:, SPAN:]
    mixing_gradient = hand_rows([[m] for m in main_cols] + [[out_cols[2]], [out_cols[0]]])


    def spread(value):
        zero = jnp.zeros((width, value.shape[1]), F32)
        return lax.dynamic_update_slice_in_dim(zero, value, member * part, axis=0)

    vec_low = jnp.concatenate([cols_one[:2], cols_mix[:6], cols_two[:4]], axis=0)
    vec_head = jnp.concatenate(
        [jnp.sum(extra[:, :2], axis=0), jnp.sum(ends[:, SPAN : SPAN + 2], axis=0)], axis=0
    )
    by_feature = jnp.concatenate([down_grad, up_grad, ddown_grad, vec_low.T], axis=1)
    by_channel = spread(jnp.concatenate([tn(d_decay, dh_all), vec_head.T], axis=1))
    low = cube_sum(
        jnp.concatenate(
            [to_cube(by_feature), by_channel.reshape(*[2] * len(all_masks), rows, -1)], axis=-1
        ),
        BF16,
    )
    vec_at = decay_up + 12
    lowrank_gradient = jnp.concatenate(
        [low[:, :decay_up], low[:, vec_at : vec_at + DRANK]], axis=1
    )
    vectors_gradient = jnp.concatenate(
        [low[:, decay_up : decay_up + 8], low[:, vec_at + DRANK :], low[:, decay_up + 8 : vec_at]],
        axis=1,
    )
    return (
        block_output.reshape(1, step, width),
        block_input_gradient.reshape(1, step, width),
        initial_state_gradient,
        mixing_gradient,
        lowrank_gradient,
        vectors_gradient,
        feedforward_gradient,
    )


def solution(mesh):
    rowwise = P("seq", None)
    tokenwise = P(None, "seq", None)
    return jax.shard_map(
        functools.partial(on_device, mesh.shape["seq"]),
        mesh=mesh,
        in_specs=(tokenwise, P(), rowwise, rowwise, rowwise, rowwise, rowwise, tokenwise),
        out_specs=(tokenwise, tokenwise, rowwise, rowwise, rowwise, rowwise, rowwise),
        check_vma=False,
    )
```

```python
import functools

import jax
import jax.numpy as jnp
from jax import lax
from jax.experimental import pallas as pl
from jax.experimental.pallas import tpu as pltpu
from jax.sharding import PartitionSpec as P

HEADS = 32
SPAN = 64
FF = 7168
RANK = 32
DRANK = 64
LN_EPS = 1e-05
GN_EPS = 0.00064

F32 = jnp.float32
BF16 = jnp.bfloat16
HI = lax.Precision.HIGHEST


def nn(a, b):
    return jnp.dot(a, b, preferred_element_type=F32)


def nt(a, b):
    return lax.dot_general(a, b, (((1,), (1,)), ((), ())), preferred_element_type=F32)


def tn(a, b):
    return lax.dot_general(a, b, (((0,), (0,)), ((), ())), preferred_element_type=F32)


def knn(a, b):
    return lax.dot_general(
        a, b, (((1,), (0,)), ((), ())), preferred_element_type=F32
    )


def knt(a, b):
    return lax.dot_general(
        a, b, (((1,), (1,)), ((), ())), preferred_element_type=F32
    )


def ktn(a, b):
    return lax.dot_general(
        a, b, (((0,), (0,)), ((), ())), preferred_element_type=F32
    )


def low_lanes(shape):
    return lax.broadcasted_iota(jnp.int32, shape, len(shape) - 1) < SPAN


def head_sum(x):
    low = low_lanes(x.shape)
    s0 = jnp.sum(jnp.where(low, x, 0.0), axis=-1, keepdims=True)
    s1 = jnp.sum(jnp.where(low, 0.0, x), axis=-1, keepdims=True)
    return jnp.where(low, s0, s1)


def two_rows(x):
    low = low_lanes(x.shape)
    return jnp.concatenate([jnp.where(low, x, 0.0), jnp.where(low, 0.0, x)], axis=0)


def fold(full):
    return jnp.where(low_lanes((SPAN, 2 * SPAN)), full[:SPAN], full[SPAN:])


def unfold(state):
    low = low_lanes(state.shape)
    return jnp.concatenate([jnp.where(low, state, 0.0), jnp.where(low, 0.0, state)], axis=0)


def running(w, upper=False):
    count = w.shape[0]
    row = lax.broadcasted_iota(jnp.int32, (count, count), 0)
    col = lax.broadcasted_iota(jnp.int32, (count, count), 1)
    keep = (col >= row) if upper else (col <= row)
    return lax.dot_general(
        jnp.where(keep, 1.0, 0.0).astype(F32),
        w,
        (((1,), (0,)), ((), ())),
        precision=HI,
        preferred_element_type=F32,
    )


def strict(count):
    row = lax.broadcasted_iota(jnp.int32, (2 * count, count), 0)
    col = lax.broadcasted_iota(jnp.int32, (2 * count, count), 1)
    row = jnp.where(row >= count, row - count, row)
    return row > col, row == col


def affinity(r, k, u, q, ks):
    count = r.shape[0]
    below, diag = strict(count)
    raw = knt(two_rows(q), ks)
    share = jnp.sum(two_rows(r * u * k), axis=-1, keepdims=True)
    return jnp.where(below, raw, jnp.where(diag, share, 0.0))


def totals_kernel(k_ref, v_ref, w_ref, out_ref):
    cum = running(w_ref[...])
    total = cum[-1:, :]
    kc = k_ref[...] * jnp.exp(total - cum)
    out_ref[0, :SPAN, :] = fold(ktn(v_ref[...], kc))
    out_ref[0, SPAN:, :] = jnp.broadcast_to(jnp.exp(total), (8, 2 * SPAN))


def group_norm(y, gain, bias):
    centred = y - head_sum(y) * (1.0 / SPAN)
    spread = head_sum(centred * centred) * (1.0 / SPAN)
    scale = lax.rsqrt(spread + GN_EPS)
    normal = centred * scale
    return normal, scale, normal * gain + bias


def forward_kernel(r_ref, k_ref, v_ref, w_ref, g_ref, s_ref, p_ref, y_ref, gated_ref):
    r, k, v, w = r_ref[...], k_ref[...], v_ref[...], w_ref[...]
    cum = running(w)
    q = r * jnp.exp(cum - w)
    ks = k * jnp.exp(-cum)
    aff = affinity(r, k, p_ref[0:1, :], q, ks)
    count = r.shape[0]
    v2 = two_rows(v)
    y = (
        knt(q, unfold(s_ref[0]))
        + knn(aff[:count], v2[:count])
        + knn(aff[count:], v2[count:])
    )
    y_ref[...] = y
    gate = g_ref[...]
    _, _, grouped = group_norm(y, p_ref[1:2, :], p_ref[2:3, :])
    gated_ref[...] = (grouped * gate * jax.nn.sigmoid(gate)).astype(BF16)


def gate_kernel(gg_ref, g_ref, y_ref, r_ref, w_ref, p_ref, gate_ref, dy_ref, out_ref):
    gated_grad, gate, y = gg_ref[...], g_ref[...], y_ref[...]
    gain = p_ref[1:2, :]
    normal, scale, grouped = group_norm(y, gain, p_ref[2:3, :])
    sig = jax.nn.sigmoid(gate)
    gate_ref[...] = (gated_grad * grouped * sig * (1.0 + gate * (1.0 - sig))).astype(BF16)
    outer = gated_grad * gate * sig
    inner = outer * gain
    dy = scale * (
        inner
        - head_sum(inner) * (1.0 / SPAN)
        - normal * (head_sum(inner * normal) * (1.0 / SPAN))
    )
    dy_ref[...] = dy
    w = w_ref[...]
    q = r_ref[...] * jnp.exp(running(w) - w)
    out_ref[0, :SPAN, :] = fold(ktn(dy, q))
    gain_grad = jnp.sum(outer * normal, axis=0, keepdims=True)
    bias_grad = jnp.sum(outer, axis=0, keepdims=True)
    out_ref[0, SPAN:, :] = jnp.concatenate(
        [gain_grad, bias_grad, jnp.zeros((6, 2 * SPAN), F32)], axis=0
    )


def backward_kernel(
    r_ref, k_ref, v_ref, w_ref, dy_ref, s_ref, gs_ref, p_ref,
    dr_ref, dk_ref, dv_ref, dd_ref, out_ref,
):
    r, k, v, w, dy = r_ref[...], k_ref[...], v_ref[...], w_ref[...], dy_ref[...]
    u = p_ref[0:1, :]
    count = r.shape[0]
    cum = running(w)
    total = cum[-1:, :]
    e_before, e_minus, e_carry = jnp.exp(cum - w), jnp.exp(-cum), jnp.exp(total - cum)
    q, ks, kc = r * e_before, k * e_minus, k * e_carry
    aff = affinity(r, k, u, q, ks)
    below, _ = strict(count)
    dy2 = two_rows(dy)
    d_aff = jnp.where(below, knt(dy2, v), 0.0)
    own = head_sum(dy * v)
    state, grad_state = s_ref[0], gs_ref[0]
    state2, grad2 = unfold(state), unfold(grad_state)
    ks2 = two_rows(ks)
    dq = knn(dy, state2) + knn(d_aff[:count], ks2[:count]) + knn(d_aff[count:], ks2[count:])
    dks = ktn(d_aff, two_rows(q))
    dkc = knn(v, grad2)
    dv_ref[...] = (ktn(aff, dy2) + knt(kc, grad2)).astype(BF16)
    dr_ref[...] = (dq * e_before + own * u * k).astype(BF16)
    dk_ref[...] = (dks * e_minus + dkc * e_carry + own * u * r).astype(BF16)
    gq, gc = q * dq, kc * dkc
    d_total = jnp.sum(gc, axis=0, keepdims=True) + jnp.exp(total) * jnp.sum(
        state * grad_state, axis=0, keepdims=True
    )
    dw = running(gq - ks * dks - gc, upper=True) - gq + d_total
    term = dw * w
    dd_ref[...] = term.astype(BF16)
    out_ref[0] = jnp.concatenate(
        [
            jnp.sum(term, axis=0, keepdims=True),
            jnp.sum(own * r * k, axis=0, keepdims=True),
            jnp.zeros((6, 2 * SPAN), F32),
        ],
        axis=0,
    )


def block_call(kernel, chunks, step, width, ins, outs, args):
    lane = 2 * SPAN
    kinds = {
        "t": pl.BlockSpec((step, lane), lambda c, h: (c, h)),
        "s": pl.BlockSpec((1, SPAN, lane), lambda c, h: (c, 0, h)),
        "x": pl.BlockSpec((1, SPAN + 8, lane), lambda c, h: (c, 0, h)),
        "e": pl.BlockSpec((1, 8, lane), lambda c, h: (c, 0, h)),
        "p": pl.BlockSpec((8, lane), lambda c, h: (0, h)),
    }
    shapes = {
        "t": lambda d: jax.ShapeDtypeStruct((chunks * step, width), d),
        "x": lambda d: jax.ShapeDtypeStruct((chunks, SPAN + 8, width), d),
        "e": lambda d: jax.ShapeDtypeStruct((chunks, 8, width), d),
    }
    return pl.pallas_call(
        kernel,
        grid=(chunks, width // lane),
        in_specs=[kinds[kind] for kind in ins],
        out_specs=[kinds[kind] for kind, _ in outs],
        out_shape=[shapes[kind](dtype) for kind, dtype in outs],
        compiler_params=pltpu.CompilerParams(vmem_limit_bytes=48 * 1024 * 1024),
    )(*args)


def weight_grad(places, pairs, block):
    tokens, blocks = pairs[0][0].shape[0], places.shape[0]
    widths = [y.shape[1] for _, y in pairs]

    def kernel(_, *refs):
        at = 0
        for i, wide in enumerate(widths):
            refs[-1][0, :, at : at + wide] = tn(refs[2 * i][...], refs[2 * i + 1][...]).astype(
                BF16
            )
            at += wide

    specs = []
    for wide in widths:
        specs.append(pl.BlockSpec((tokens, block), lambda i, at: (0, at[i])))
        specs.append(pl.BlockSpec((tokens, wide), lambda i, at: (0, 0)))
    return pl.pallas_call(
        kernel,
        grid_spec=pltpu.PrefetchScalarGridSpec(
            num_scalar_prefetch=1,
            grid=(blocks,),
            in_specs=specs,
            out_specs=pl.BlockSpec((1, block, sum(widths)), lambda i, at: (i, 0, 0)),
        ),
        out_shape=jax.ShapeDtypeStruct((blocks, block, sum(widths)), BF16),
        compiler_params=pltpu.CompilerParams(vmem_limit_bytes=48 * 1024 * 1024),
    )(places, *[v for pair in pairs for v in pair])


def lanes_kernel(spans, x_ref, out_ref):
    at = 0
    for start, stop in spans:
        out_ref[:, at : at + stop - start] = x_ref[:, start:stop].astype(out_ref.dtype)
        at += stop - start


def move_lanes(spans, value, dtype):
    return pl.pallas_call(
        functools.partial(lanes_kernel, spans),
        in_specs=[pl.BlockSpec(memory_space=pltpu.VMEM)],
        out_specs=pl.BlockSpec(memory_space=pltpu.VMEM),
        out_shape=jax.ShapeDtypeStruct(value.shape, dtype),
        compiler_params=pltpu.CompilerParams(vmem_limit_bytes=32 * 1024 * 1024),
    )(value)


def place_kernel(counts, wide, block, at_ref, *refs):
    ins, out_ref, sems = refs[: len(counts)], refs[-2], refs[-1]
    rows = out_ref.shape[0]
    copies, i = [], 0
    for ref, n in zip(ins, counts):
        for j in range(n):
            start = pl.multiple_of(at_ref[i] * block, block)
            column = i * block // rows * wide
            copy = pltpu.make_async_copy(
                ref.at[pl.ds(j * block, block), :],
                out_ref.at[pl.ds(start, block), pl.ds(column, wide)],
                sems.at[i],
            )
            copy.start()
            copies.append(copy)
            i += 1
    for copy in copies:
        copy.wait()


def place_rows(parts, block):
    pieces = [p for part in parts for p in part[1]]
    wide = pieces[0].shape[1]
    at = jnp.concatenate([part[0] for part in parts])
    counts = [p.shape[0] // block for p in pieces]
    total = sum(counts)
    return pl.pallas_call(
        functools.partial(place_kernel, counts, wide, block),
        in_specs=[pl.BlockSpec(memory_space=pltpu.SMEM)]
        + [pl.BlockSpec(memory_space=pl.ANY)] * len(pieces),
        out_specs=pl.BlockSpec(memory_space=pl.ANY),
        out_shape=jax.ShapeDtypeStruct(
            (total * block // len(parts), wide * len(parts)), pieces[0].dtype
        ),
        scratch_shapes=[pltpu.SemaphoreType.DMA((total,))],
        compiler_params=pltpu.CompilerParams(vmem_limit_bytes=32 * 1024 * 1024),
    )(at, *pieces)


def mixes_kernel(
    open_ref, x_ref, before_ref, vec_ref, down_ref, up_ref, ddown_ref,
    m1_ref, m2_ref, m3_ref, m4_ref, dh_ref,
    normal_ref, scale_ref, delta_ref, blend_ref, m0_ref, tanh_ref, dtanh_ref,
):
    piece = pl.program_id(0)
    step = m1_ref.shape[0]
    x = x_ref[...].astype(F32)
    centred = x - jnp.mean(x, axis=-1, keepdims=True)
    scale = lax.rsqrt(jnp.mean(centred * centred, axis=-1, keepdims=True) + LN_EPS)
    normal = centred * scale
    full = normal * vec_ref[0:1, :] + vec_ref[1:2, :]
    normed = full[:step]
    first = jnp.where(open_ref[piece] == 1, before_ref[0:1, :], full[step : step + 1])
    row = lax.broadcasted_iota(jnp.int32, normed.shape, 0)
    delta = jnp.where(row == 0, first, pltpu.roll(normed, 1, 0)) - normed
    blend = (normed + delta * vec_ref[2:3, :]).astype(BF16)
    tanh = jnp.tanh(nn(blend, down_ref[...]))
    latent = tanh.astype(BF16)
    lane = lax.broadcasted_iota(jnp.int32, latent.shape, 1)
    mixed = []
    for c in range(5):
        own = (lane >= c * RANK) & (lane < (c + 1) * RANK)
        offset = nt(jnp.where(own, latent, jnp.zeros_like(latent)), up_ref[...])
        mixed.append((normed + delta * (vec_ref[3 + c : 4 + c, :] + offset)).astype(BF16))
    dtanh = jnp.tanh(nn(mixed[0], ddown_ref[...]))
    m1_ref[...], m2_ref[...], m3_ref[...], m4_ref[...] = mixed[1:]
    dh_ref[...] = dtanh.astype(BF16)

    @pl.when(piece == 0)
    def _():
        normal_ref[...] = normal[:step]
        scale_ref[...] = jnp.broadcast_to(scale[:step], scale_ref.shape)
        delta_ref[...] = delta
        blend_ref[...] = blend
        m0_ref[...] = mixed[0]
        tanh_ref[...] = tanh
        dtanh_ref[...] = dtanh


def group_mixes(opening, x, before, vec, down, up, ddown, step):
    high, width = step + 16, x.shape[1]
    pieces = x.shape[0] // high

    def whole(value):
        return pl.BlockSpec(value.shape, lambda k: (0, 0))

    def own(columns, dtype):
        return (
            pl.BlockSpec((step, columns), lambda k: (0, 0)),
            jax.ShapeDtypeStruct((step, columns), dtype),
        )

    def every(columns, dtype):
        return (
            pl.BlockSpec((step, columns), lambda k: ((k % 2) * 2 + k // 2, 0)),
            jax.ShapeDtypeStruct((pieces * step, columns), dtype),
        )

    outs = [every(width, BF16)] * 4 + [
        every(DRANK, BF16),
        own(width, F32),
        own(128, F32),
        own(width, F32),
        own(width, BF16),
        own(width, BF16),
        own(5 * RANK, F32),
        own(DRANK, F32),
    ]
    return pl.pallas_call(
        mixes_kernel,
        grid=(pieces,),
        in_specs=[
            pl.BlockSpec(memory_space=pltpu.SMEM),
            pl.BlockSpec((high, width), lambda k: (k, 0)),
            whole(before),
            whole(vec),
            whole(down),
            whole(up),
            whole(ddown),
        ],
        out_specs=[o[0] for o in outs],
        out_shape=[o[1] for o in outs],
        compiler_params=pltpu.CompilerParams(vmem_limit_bytes=56 * 1024 * 1024),
    )(opening, x, before, vec, down, up, ddown)


def product(pairs, outs, body, sides=(), tile=256):
    count = len(pairs)

    def kernel(*refs):
        ins, out_refs = refs[: 2 * count + len(sides)], refs[2 * count + len(sides) :]
        products = [
            (nn if pair[2] == "nn" else nt)(ins[2 * i][...], ins[2 * i + 1][...])
            for i, pair in enumerate(pairs)
        ]
        results = body(*products, *[r[...] for r in ins[2 * count :]])
        for ref, value in zip(out_refs, results):
            ref[...] = value.astype(ref.dtype)

    specs, args = [], []
    for a, b, form, at in pairs:
        depth = a.shape[1]
        specs.append(pl.BlockSpec(a.shape, lambda j: (0, 0)))
        if form == "nn":
            specs.append(pl.BlockSpec((depth, tile), lambda j, at=at: (0, at + j)))
        else:
            specs.append(pl.BlockSpec((tile, depth), lambda j, at=at: (j, at)))
        args += [a, b]
    for side in sides:
        specs.append(pl.BlockSpec((side.shape[0], tile), lambda j: (0, j)))
    return pl.pallas_call(
        kernel,
        grid=(outs[0][1] // tile,),
        in_specs=specs,
        out_specs=[pl.BlockSpec((o[0], tile), lambda j: (0, j)) for o in outs],
        out_shape=[jax.ShapeDtypeStruct(o[:2], o[2]) for o in outs],
        compiler_params=pltpu.CompilerParams(vmem_limit_bytes=56 * 1024 * 1024),
    )(*args, *sides)


def local(fn, outs, *args, scalar=None):
    def kernel(*refs):
        lead = [] if scalar is None else [refs[0]]
        ins, out_refs = refs[len(lead) : -len(outs)], refs[-len(outs) :]
        results = fn(*[r[0] for r in lead], *[r[...] for r in ins])
        for ref, value in zip(out_refs, results):
            ref[...] = value.astype(ref.dtype)

    specs = [pl.BlockSpec(memory_space=pltpu.VMEM)] * len(args)
    if scalar is not None:
        specs = [pl.BlockSpec(memory_space=pltpu.SMEM)] + specs
        args = (scalar.reshape(1), *args)
    return pl.pallas_call(
        kernel,
        in_specs=specs,
        out_specs=[pl.BlockSpec(memory_space=pltpu.VMEM)] * len(outs),
        out_shape=[jax.ShapeDtypeStruct(o[:2], o[2]) for o in outs],
        compiler_params=pltpu.CompilerParams(vmem_limit_bytes=56 * 1024 * 1024),
    )(*args)


def take_lanes(value, spans):
    if len(spans) == 1:
        return value
    return jnp.concatenate([value[:, a:b] for a, b in spans], axis=1)


def norm_back(grad, gain, normal, scale):
    e = grad * gain
    return scale * (
        e
        - jnp.mean(e, axis=-1, keepdims=True)
        - normal * jnp.mean(e * normal, axis=-1, keepdims=True)
    )


def rows_above(value, first):
    row = lax.broadcasted_iota(jnp.int32, value.shape, 0)
    return jnp.where(row == 0, first, pltpu.roll(value, 1, 0))


def rows_below(value, last):
    row = lax.broadcasted_iota(jnp.int32, value.shape, 0)
    high = value.shape[0]
    return jnp.where(row == high - 1, last, pltpu.roll(value, high - 1, 0))


def padded(rows):
    return jnp.concatenate(
        list(rows) + [jnp.zeros((8 - len(rows), rows[0].shape[1]), F32)], axis=0
    )


def column_sum(value):
    return jnp.sum(value, axis=0, keepdims=True)


def gates_kernel(
    spans, who_ref, middle_ref, value_ref, more_ref, act_ref, cot_ref,
    out_ref, up_ref, vg_ref, rg_ref, held,
):
    to_spans, from_spans = spans
    step, part = act_ref.shape[0] // 4, act_ref.shape[1]
    who = who_ref[0]
    act = [
        act_ref[pl.ds(pl.multiple_of((who ^ j) * step, step), step), :] for j in range(4)
    ]
    recept = jax.nn.sigmoid(take_lanes(jnp.concatenate(act, axis=1).astype(F32), to_spans))
    value = value_ref[...] + more_ref[...].astype(F32)
    out = middle_ref[...] + recept * value
    out_ref[...] = take_lanes(out, from_spans).astype(BF16)
    up = take_lanes(cot_ref[...].astype(F32), to_spans)
    up_ref[...] = up
    vg_ref[...] = (up * recept).astype(BF16)
    held[...] = take_lanes(up * value * recept * (1.0 - recept), from_spans)
    for k in range(4):
        at = pl.multiple_of((who ^ k) * part, part)
        rg_ref[k * step : (k + 1) * step, :] = held[:, pl.ds(at, part)].astype(BF16)


def gates(spans, who, middle, value, more, act, cot):
    step, width = middle.shape
    part = act.shape[1]
    shape = jax.ShapeDtypeStruct
    return pl.pallas_call(
        functools.partial(gates_kernel, spans),
        in_specs=[pl.BlockSpec(memory_space=pltpu.SMEM)]
        + [pl.BlockSpec(memory_space=pltpu.VMEM)] * 5,
        out_specs=[pl.BlockSpec(memory_space=pltpu.VMEM)] * 4,
        out_shape=[
            shape((step, width), BF16),
            shape((step, width), F32),
            shape((step, width), BF16),
            shape((4 * step, part), BF16),
        ],
        scratch_shapes=[pltpu.VMEM((step, width), F32)],
        compiler_params=pltpu.CompilerParams(vmem_limit_bytes=56 * 1024 * 1024),
    )(who.reshape(1), middle, value, more, act, cot)


def mixes_back_kernel(
    kept_ref, got_ref, dl_ref, dl_more_ref, delta_ref, tanh_ref, dtanh_ref, blend_ref, m0_ref,
    down_ref, up_ref, ddown_ref, vec_ref,
    rest_ref, dg_ref, row_ref, cols_ref, down_out, up_out, ddown_out,
):
    step = delta_ref.shape[0]
    dtanh = dtanh_ref[...]
    decay_grad = dl_ref[...] + dl_more_ref[...].astype(F32)
    decay_pre = (decay_grad * (1.0 - dtanh * dtanh)).astype(BF16)
    ddown_out[...] = tn(m0_ref[...], decay_pre)
    tanh = tanh_ref[...]
    latent = tanh.astype(BF16)
    lane = lax.broadcasted_iota(jnp.int32, latent.shape, 1)
    delta, up = delta_ref[...], up_ref[...]
    latent_grad = jnp.zeros(latent.shape, F32)
    up_grad = jnp.zeros(up_out.shape, F32)
    dg = jnp.zeros(delta.shape, F32)
    total = jnp.zeros(delta.shape, F32)
    cols = []
    for c in range(5):
        own = (lane >= c * RANK) & (lane < (c + 1) * RANK)
        mine = jnp.where(own, latent, jnp.zeros_like(latent))
        if c == 0:
            grad = nt(decay_pre, ddown_ref[...])
        else:
            at = slice((c - 1) * step, c * step)
            grad = kept_ref[at, :] + got_ref[at, :].astype(F32)
        shift = grad * delta
        cols.append(column_sum(shift))
        offset = shift.astype(BF16)
        latent_grad = jnp.where(own, nn(offset, up), latent_grad)
        up_grad = up_grad + tn(offset, mine)
        dg = dg + grad * (vec_ref[3 + c : 4 + c, :] + nt(mine, up))
        total = total + grad
    up_out[...] = up_grad
    mix_pre = (latent_grad * (1.0 - tanh * tanh)).astype(BF16)
    down_out[...] = tn(blend_ref[...], mix_pre)
    blend_grad = nt(mix_pre, down_ref[...])
    dg = dg + blend_grad * vec_ref[2:3, :]
    rest_ref[...] = total + blend_grad - dg
    dg_ref[...] = dg
    row_ref[...] = dg[:8]
    cols_ref[...] = padded([column_sum(blend_grad * delta)] + cols)


def mixes_back(*args):
    delta, down, ddown = args[4], args[9], args[11]
    step, width = delta.shape
    shape = jax.ShapeDtypeStruct
    outs = [
        shape((step, width), F32),
        shape((step, width), F32),
        shape((8, width), F32),
        shape((8, width), F32),
        shape(down.shape, F32),
        shape(down.shape, F32),
        shape(ddown.shape, F32),
    ]
    return pl.pallas_call(
        mixes_back_kernel,
        in_specs=[pl.BlockSpec(memory_space=pltpu.VMEM)] * len(args),
        out_specs=[pl.BlockSpec(memory_space=pltpu.VMEM)] * len(outs),
        out_shape=outs,
        compiler_params=pltpu.CompilerParams(vmem_limit_bytes=60 * 1024 * 1024),
    )(*args)


def tie(*values):
    return lax.optimization_barrier(values)


def on_device(
    count,
    tokens,
    previous,
    initial_state,
    mixing_weights,
    lowrank_weights,
    vectors,
    feedforward_weights,
    cotangent,
):
    fast = initial_state.shape[0] == 64
    masks = (1, 8) if fast else (1, 2)
    size = 1 << len(masks)
    teams = count // size
    all_masks = [1 << b for b in range(count.bit_length() - 1)]
    team_masks = [b for b in all_masks if b not in masks]
    far = 16
    team_masks.sort(key=lambda b: fast and b != far)
    me = lax.axis_index("seq")
    _, step, width = tokens.shape
    rows = mixing_weights.shape[0]
    part = width // size
    ff_part = FF // size
    team_rows = rows * size
    def bit_of(who, mask):
        return (who // mask) % 2 if isinstance(who, int) else lax.rem(lax.div(who, mask), 2)

    def member_of(who):
        return sum(bit_of(who, b) << j for j, b in enumerate(masks))

    def team_of(who):
        return sum(bit_of(who, b) << j for j, b in enumerate(team_masks))

    member, team = member_of(me), team_of(me)
    order = sorted(range(count), key=lambda d: (team_of(d), member_of(d)))
    inverse = sorted(range(count), key=lambda p: order[p])
    across = [order[m::size] for m in range(size)]
    square = [order[m :: 2 * size] for m in range(2 * size)]
    def lane_spans(blocks):
        spans = []
        for d in blocks:
            if spans and spans[-1][1] == d * rows:
                spans[-1][1] = (d + 1) * rows
            else:
                spans.append([d * rows, (d + 1) * rows])
        return spans

    to_spans, from_spans = lane_spans(order), lane_spans(inverse)

    def to_places(value, dtype):
        return move_lanes(to_spans, value, dtype)

    def flips(k):
        return sum(b for j, b in enumerate(masks) if (k >> j) & 1)

    def trade(value, mask):
        return lax.ppermute(value, "seq", [(d, d ^ mask) for d in range(count)])

    def group_gather(value):
        side = trade(value, masks[1])
        return value, side, trade(jnp.concatenate([value, side], axis=0), masks[0])

    def group_rows(value):
        high, columns = value.shape

        def lay(own, side, far):
            return (jnp.concatenate([own, far[:high], side, far[high:]], axis=0),)

        return local(lay, [(size * high, columns, value.dtype)], *group_gather(value))[0]

    def halves(value):
        cut = [value[k * step : (k + 1) * step] for k in range(size)]
        return [cut[0], cut[2]], [cut[1], cut[3]]

    def group_fold(kept, sent):
        high, columns = kept.shape[0] // 2, kept.shape[1]
        got = trade(sent, masks[0])

        def add(mine, more):
            total = mine + more.astype(F32)
            return total[:high], total[high:]

        return local(add, [(high, columns, F32), (high, columns, BF16)], kept, got)

    def group_sum(kept, sent):
        mine, side = group_fold(kept, sent)
        return mine, trade(side, masks[1])

    def crossing_sum(*pairs):
        units = len(pairs)

        def body(*products):
            parts = [halves(p) for p in products]
            kept = [p[0][i] for i in range(2) for p in parts]
            sent = [p[1][i] for i in range(2) for p in parts]
            return jnp.concatenate(kept, axis=0), jnp.concatenate(sent, axis=0)

        high = 2 * units * step
        return product(
            [(a, b, "nt", at) for a, b, at in pairs],
            [(high, width, F32), (high, width, BF16)],
            body,
            tile=512,
        )

    def exchange(pieces):
        pieces, high = list(pieces), pieces[0].shape[0]
        for j in reversed(range(len(masks))):
            keys = [k for k in range(size) if (k >> j) & 1]
            got = trade(jnp.concatenate([pieces[k] for k in keys], axis=0), masks[j])
            for i, k in enumerate(keys):
                pieces[k] = got[i * high : (i + 1) * high]
        return pieces

    def ordered(pieces):
        pieces = list(pieces)
        for j in range(len(masks)):
            swap = lax.rem(lax.div(member, 1 << j), 2) == 1
            pieces = [
                jnp.where(swap, pieces[k ^ (1 << j)], pieces[k]) for k in range(len(pieces))
            ]
        return pieces

    def neighbour(value, offset):
        pairs = [(d, d + offset) for d in range(count) if 0 <= d + offset < count]
        return lax.ppermute(value, "seq", pairs)

    def take_columns(value, spans, who):
        return jnp.concatenate(
            [
                lax.dynamic_slice_in_dim(value, start + who * wide, wide, axis=1)
                for start, wide in spans
            ],
            axis=1,
        )

    def group_columns(value, spans):
        pieces = [take_columns(value, spans, member ^ k) for k in range(size)]
        return jnp.concatenate(ordered(exchange(pieces)), axis=0)

    def crossing(first):
        bits = list(range(1, len(team_masks))) + [0]
        if first:
            bits[0], bits[1] = bits[1], bits[0]
        return bits

    def gather_rows(own):
        return lax.all_gather(own, "seq", axis=0, tiled=True, axis_index_groups=across)

    def far_send(own):
        return trade(own, far) if fast else own

    def far_join(own, got):
        if not fast:
            return own
        upper = bit_of(me, far) == 1
        return jnp.concatenate(
            [jnp.where(upper, got, own), jnp.where(upper, own, got)], axis=0
        )

    def gather_square(paired):
        groups = square if fast else across
        return lax.all_gather(paired, "seq", axis=0, tiled=True, axis_index_groups=groups)

    def team_products(*pairs):
        if fast:
            places = jnp.arange(teams, dtype=jnp.int32)
            return weight_grad(places, pairs, team_rows).reshape(width, -1)
        return jnp.concatenate([tn(x, y).astype(BF16) for x, y in pairs], axis=1)

    def square_sum(grads):
        groups = square if fast else across
        return lax.psum_scatter(
            grads, "seq", scatter_dimension=0, tiled=True, axis_index_groups=groups
        )

    def far_split(pair):
        if not fast:
            return pair, jnp.zeros_like(pair)
        bit = bit_of(me, far)
        sent = lax.dynamic_slice_in_dim(pair, (1 - bit) * team_rows, team_rows, axis=0)
        kept = lax.dynamic_slice_in_dim(pair, bit * team_rows, team_rows, axis=0)
        return kept, trade(sent, far)

    def far_add(kept, got):
        return (kept.astype(F32) + got.astype(F32)).astype(BF16)

    def cube_gather(value, follower=None):
        for mask in reversed(all_masks):
            got = trade(value, mask)
            upper = bit_of(me, mask) == 1
            value = jnp.stack([jnp.where(upper, got, value), jnp.where(upper, value, got)])
            if mask == 8 and follower is not None:
                value, follower = tie(value, follower)
        axes = len(all_masks)
        cube = value.transpose(*reversed(range(axes)), *range(axes, value.ndim))
        return cube if follower is None else (cube, follower)

    place_axes = [all_masks[::-1].index(b) for b in team_masks[::-1] + list(masks[::-1])]

    def by_place(cube):
        rest = range(len(all_masks), cube.ndim)
        return cube.transpose(*place_axes, *rest).reshape(width, -1)

    def to_cube(value):
        cube = value.reshape(*[2] * len(place_axes), rows, -1)
        back = [place_axes.index(a) for a in range(len(place_axes))]
        return cube.transpose(*back, len(back), len(back) + 1)

    def cube_sum(cube, kind):
        for axis, mask in reversed(list(enumerate(reversed(all_masks)))):
            bit = bit_of(me, mask)
            sent = lax.dynamic_index_in_dim(cube, 1 - bit, axis, keepdims=False)
            kept = lax.dynamic_index_in_dim(cube, bit, axis, keepdims=False)
            cube = kept.astype(F32) + trade(sent.astype(kind), mask).astype(F32)
        return cube

    def hand_rows(pieces, extra=None):
        widths = [sum(p.shape[1] for p in piece) for piece in pieces]
        joint = jnp.concatenate([p for piece in pieces for p in piece], axis=1)
        mine = [
            lax.dynamic_slice_in_dim(joint, (member ^ k) * rows, rows, axis=0)
            for k in range(size)
        ]
        if extra is not None:
            mine = [jnp.concatenate([m, e], axis=1) for m, e in zip(mine, extra)]
        by_place = exchange(mine)
        by_member = ordered(by_place)
        outs, start = [], 0
        for wide in widths:
            outs += [p[:, start : start + wide] for p in by_member]
            start += wide
        joined = jnp.concatenate(outs, axis=1).astype(F32)
        if extra is None:
            return joined
        return joined, [p[:, start:].astype(F32) for p in by_place]

    up_start, decay_start, decay_up = 5 * RANK, 10 * RANK, 10 * RANK + DRANK
    last_row = neighbour(tokens[0, -1:, :], 1)
    tokens_sent = to_places(
        jnp.concatenate([tokens[0], jnp.broadcast_to(last_row, (16, width))], axis=0), BF16
    )
    natural, mix_in = cube_gather(
        jnp.concatenate(
            [vectors, initial_state, lowrank_weights[:, decay_up:].astype(F32)], axis=1
        ),
        mixing_weights,
    )
    natural = natural.reshape(width, -1)
    low_cube, mix_in = cube_gather(lowrank_weights[:, :decay_up], mix_in)
    tokens_all = jnp.concatenate(group_gather(tokens_sent), axis=0)
    mix_local = group_columns(mix_in, [(c * width, part) for c in range(5)])
    mix_local, natural, low_cube, tokens_all = tie(mix_local, natural, low_cube, tokens_all)
    lowrank = by_place(low_cube)
    mix_kv, mix_rest = mix_local[:, : 2 * part], mix_local[:, 2 * part :]
    kv_got, mix_rest = tie(far_send(mix_kv), mix_rest)
    w_kv = gather_square(far_join(mix_kv, kv_got))
    tiles = part // 256

    mine = lax.dynamic_slice_in_dim(natural, member * part, part, axis=0)
    vec_part = mine[:, :16].T
    first_state = mine[:, 16 : 16 + SPAN].T
    w_dup = mine[:, 16 + SPAN :].astype(BF16)
    vec = by_place(
        natural[:, :16].reshape(*[2] * len(all_masks), rows, 16)
    ).T
    wkv_rows = jnp.concatenate([vec_part[9:12], jnp.zeros((5, part), F32)], axis=0)
    is_first = (me == 0).astype(jnp.int32)
    before = to_places(previous.reshape(2, width), F32)
    w_down, w_up = lowrank[:, :up_start], lowrank[:, up_start:decay_start]
    w_ddown = lowrank[:, decay_start:]

    opening = jnp.stack(
        [jnp.bitwise_xor(me, flips(k)) == 0 for k in (0, 2, 1, 3)]
    ).astype(jnp.int32)
    (
        *mixed_all, dh_all, normal_one, scale_one, delta, blend, mixed_zero, mix_tanh, decay_tanh,
    ) = group_mixes(opening, tokens_all, before, vec, w_down, w_up, w_ddown, step)
    rest_got, mixed_all[0], feed_in = tie(far_send(mix_rest), mixed_all[0], feedforward_weights)
    w_rest = gather_square(far_join(mix_rest, rest_got))
    ff_spans = [(0, ff_part), (FF, part), (FF + width, ff_part)]
    ff_local = group_columns(feed_in, ff_spans)
    everyone = size * step
    (log_decay,) = product(
        [(dh_all, w_dup, "nt", 0)],
        [(everyone, part, F32)],
        lambda acc, base: (-jnp.exp(base + acc),),
        sides=(vec_part[8:9],),
    )
    keys, values = product(
        [(mixed_all[0], w_kv, "nn", 0), (mixed_all[1], w_kv, "nn", tiles)],
        [(everyone, part, F32)] * 2,
        lambda a, b: (a, b),
    )

    keys, ff_local = tie(keys, ff_local)
    ff_tail = ff_local[:, ff_part + part :]
    ff_near = ff_local[:, : ff_part + part]
    near_got = far_send(ff_near)

    call = functools.partial(block_call, chunks=size, step=step, width=part)
    (totals,) = call(
        totals_kernel, ins="ttt", outs=[("x", F32)], args=(keys, values, log_decay)
    )
    by_member = ordered([totals[k] for k in range(size)])
    total = {m: (p[SPAN : SPAN + 1], p[:SPAN]) for m, p in enumerate(by_member)}
    before_chunk = [
        (jnp.ones((1, part), F32), jnp.zeros((SPAN, part), F32)) for _ in range(size)
    ]
    open_bits = size - 1
    levels = []

    def two_terms(decay):
        first = lax.reduce_precision(decay, 8, 7)
        return [
            jnp.broadcast_to(d.astype(BF16), (8, part)) for d in (first, decay - first)
        ]

    def chain(early, late):
        return early[0] * late[0], late[0] * early[1] + late[1]

    def pick(flag, yes, no):
        return tuple(jnp.where(flag, a, b) for a, b in zip(yes, no))

    for mask in all_masks:
        if mask in masks:
            bit = 1 << masks.index(mask)
            levels.append({g: total[g][0] for g in total})
            for m in range(size):
                if m & bit:
                    early = (m & open_bits) ^ bit
                    before_chunk[m] = chain(total[early], before_chunk[m])
            total = {g: chain(total[g], total[g | bit]) for g in total if not g & bit}
            open_bits ^= bit
        else:
            groups = list(total)
            sent = jnp.concatenate(
                [
                    jnp.concatenate(
                        [total[g][1].astype(BF16), *two_terms(total[g][0])], axis=0
                    )
                    for g in groups
                ],
                axis=0,
            )
            got = trade(sent, mask).astype(F32)
            high = SPAN + 16
            other = {}
            for i, g in enumerate(groups):
                at = i * high + SPAN
                other[g] = (got[at : at + 1] + got[at + 8 : at + 9], got[i * high : at])
            levels.append({g: (total[g][0], other[g][0]) for g in groups})
            late = bit_of(me, mask) == 1
            for m in range(size):
                g = m & open_bits
                before_chunk[m] = pick(late, chain(other[g], before_chunk[m]), before_chunk[m])
            total = {
                g: pick(late, chain(other[g], total[g]), chain(total[g], other[g]))
                for g in groups
            }
            if mask == (2 if fast else 4):
                first_sum, near_got = tie(total[0][1], near_got)
                total[0] = total[0][0], first_sum
    state_in = jnp.stack(ordered([d * first_state + s for d, s in before_chunk]))
    w_near = gather_square(far_join(ff_near, near_got))
    w_key, w_rec = w_near, w_near[:, ff_part:]
    state_in, ff_tail = tie(state_in, ff_tail)
    val_got = far_send(ff_tail)

    receipt, gate_pre = product(
        [(mixed_all[2], w_rest, "nn", 0), (mixed_all[3], w_rest, "nn", tiles)],
        [(everyone, part, F32)] * 2,
        lambda a, b: (a, b),
    )
    wkv, gated = call(
        forward_kernel,
        ins="tttttsp",
        outs=[("t", F32), ("t", BF16)],
        args=(receipt, keys, values, log_decay, gate_pre, state_in, wkv_rows),
    )
    gated, val_got = tie(gated, val_got)
    w_val = gather_square(far_join(ff_tail, val_got))
    branch, branch_more = group_sum(*crossing_sum((gated, w_rest, 2)))

    def norm_two(hidden, mine, more, vec):
        middle = hidden[:step].astype(F32) + mine + more.astype(F32)
        centred = middle - jnp.mean(middle, axis=-1, keepdims=True)
        scale = lax.rsqrt(jnp.mean(centred * centred, axis=-1, keepdims=True) + LN_EPS)
        normal = centred * scale
        tail = normal[step - 8 :] * vec[12:13] + vec[13:14]
        return middle, normal, jnp.broadcast_to(scale, (step, 128)), tail

    whole = (step, width, F32)
    middle, normal_two, scale_two, tail_two = local(
        norm_two,
        [whole, whole, (step, 128, F32), (8, width, F32)],
        tokens_sent,
        branch,
        branch_more,
        vec,
    )

    def mix_two(first, normal, arrived, before, vec):
        normed = normal * vec[12:13] + vec[13:14]
        above = jnp.where(first == 1, before[1:2], arrived[7:8])
        delta = rows_above(normed, above) - normed
        key_in, recv_in = normed + delta * vec[14:15], normed + delta * vec[15:16]
        return jnp.concatenate([key_in, recv_in], axis=0), delta

    both, delta_two = local(
        mix_two,
        [(2 * step, width, BF16), whole],
        normal_two,
        neighbour(tail_two, 1),
        before,
        vec,
        scalar=is_first,
    )

    key_all, recv_all = group_rows(both[:step]), group_rows(both[step:])
    relu, squared = product(
        [(key_all, w_key, "nn", 0)],
        [(everyone, ff_part, F32), (everyone, ff_part, BF16)],
        lambda acc: (jnp.maximum(acc, 0.0), jnp.square(jnp.maximum(acc, 0.0))),
        tile=ff_part // 2,
    )
    (recept_act,) = product(
        [(recv_all, w_rec, "nn", 0)],
        [(everyone, part, BF16)],
        lambda acc: (acc,),
    )
    squared, recept_act = tie(squared, recept_act)
    acts = exchange([recept_act[k * step : (k + 1) * step] for k in range(size)])
    value, value_more = group_sum(*crossing_sum((squared, w_val, 0)))
    block_output, upstream, value_grad, recept_grads = gates(
        (to_spans, from_spans),
        member,
        middle,
        value,
        value_more,
        jnp.concatenate(acts, axis=0),
        cotangent.reshape(step, width),
    )

    rg_all = jnp.concatenate(
        exchange([recept_grads[k * step : (k + 1) * step] for k in range(size)]), axis=0
    )
    vg_all = group_rows(value_grad)
    val_grads = team_products((vg_all, squared))
    vg_all, val_grads, rg_all = tie(vg_all, val_grads, rg_all)
    val_pair = square_sum(val_grads)
    (key_grad,) = product(
        [(vg_all, w_val, "nn", 0)],
        [(everyone, ff_part, BF16)],
        lambda acc, relu: (acc * (2.0 * relu),),
        sides=(relu,),
        tile=ff_part // 2,
    )
    key_grads = team_products((key_all, key_grad))
    key_grad, key_grads = tie(key_grad, key_grads)
    key_pair = square_sum(key_grads)
    recv_two = group_sum(*crossing_sum((rg_all, w_rec, 0)))
    key_two = group_sum(*crossing_sum((key_grad, w_key, 0)))

    def inputs_back(key, key_more, recv, recv_more, vec):
        key, recv = key + key_more.astype(F32), recv + recv_more.astype(F32)
        top = key[:8] * vec[14:15] + recv[:8] * vec[15:16]
        return jnp.concatenate([key, recv], axis=0), top

    in_grads, top_two = local(
        inputs_back, [(2 * step, width, F32), (8, width, F32)], *key_two, *recv_two, vec
    )
    last_flag = (me == count - 1).astype(jnp.int32)

    def norm_two_back(last, grads, arrived, upstream, normal, scale, delta, vec):
        key_grad, recv_grad = grads[:step], grads[step:]
        shifted = key_grad * vec[14:15] + recv_grad * vec[15:16]
        below = jnp.where(last == 1, jnp.zeros_like(arrived[:1]), arrived[:1])
        grad = (
            key_grad * (1.0 - vec[14:15])
            + recv_grad * (1.0 - vec[15:16])
            + rows_below(shifted, below)
        )
        out = upstream + norm_back(grad, vec[12:13], normal, scale[:, :1])
        cols = padded(
            [
                column_sum(grad * normal),
                column_sum(grad),
                column_sum(key_grad * delta),
                column_sum(recv_grad * delta),
            ]
        )
        return out, out, cols

    middle_grad, branch_grad, cols_two = local(
        norm_two_back,
        [whole, (step, width, BF16), (8, width, F32)],
        in_grads,
        neighbour(top_two, -1),
        upstream,
        normal_two,
        scale_two,
        delta_two,
        vec,
        scalar=last_flag,
    )

    bg_all = group_rows(branch_grad)
    (gated_grad,) = product(
        [(bg_all, w_rest, "nn", 2 * tiles)], [(everyone, part, F32)], lambda acc: (acc,)
    )
    gate_grad, wkv_grad, ends = call(
        gate_kernel,
        ins="tttttp",
        outs=[("t", BF16), ("t", F32), ("x", F32)],
        args=(gated_grad, gate_pre, wkv, receipt, log_decay, wkv_rows),
    )
    grad_total = dict(enumerate(ordered([ends[k, :SPAN] for k in range(size)])))
    after = [(jnp.ones((1, part), F32), jnp.zeros((SPAN, part), F32)) for _ in range(size)]
    open_bits = size - 1
    val_kept, val_got = far_split(val_pair)
    for mask, level in zip(all_masks, levels):
        if mask in masks:
            bit = 1 << masks.index(mask)
            for m in range(size):
                if not m & bit:
                    late = (m & open_bits) | bit
                    d, s = after[m]
                    after[m] = (d * level[late], d * grad_total[late] + s)
            grad_total = {
                g: grad_total[g] + level[g] * grad_total[g | bit]
                for g in grad_total
                if not g & bit
            }
            open_bits ^= bit
        else:
            groups = list(grad_total)
            got = trade(
                jnp.concatenate([grad_total[g].astype(BF16) for g in groups], axis=0), mask
            ).astype(F32)
            other = {g: got[i * SPAN : (i + 1) * SPAN] for i, g in enumerate(groups)}
            early = bit_of(me, mask) == 0
            for m in range(size):
                g = m & open_bits
                d, s = after[m]
                after[m] = pick(early, (d * level[g][1], d * other[g] + s), (d, s))
            grad_total = {
                g: jnp.where(
                    early,
                    grad_total[g] + level[g][0] * other[g],
                    other[g] + level[g][1] * grad_total[g],
                )
                for g in groups
            }
            if mask == (2 if fast else 4):
                grad_total[0], val_got = tie(grad_total[0], val_got)
    grad_out = jnp.stack(ordered([s for _, s in after]))
    out_grads = team_products((bg_all, gated), (recv_all, rg_all), (mixed_all[3], gate_grad))
    grad_out, out_grads = tie(grad_out, out_grads)
    out_pair = square_sum(out_grads)

    d_receipt, d_keys, d_values, d_decay, extra = call(
        backward_kernel,
        ins="tttttssp",
        outs=[("t", BF16)] * 4 + [("e", F32)],
        args=(receipt, keys, values, log_decay, wkv_grad, state_in, grad_out, wkv_rows),
    )
    grads = [d_keys, d_values, d_receipt, gate_grad]
    kept, sent = crossing_sum(
        *[(grads[c], w_rest if c > 1 else w_kv, c % 2) for c in range(4)]
    )
    main_grads = team_products(
        (mixed_all[0], d_keys), (mixed_all[1], d_values), (mixed_all[2], d_receipt)
    )

    def latent_back(grad, up):
        kept, sent = halves(nn(grad, up))
        return jnp.concatenate(kept, axis=0), jnp.concatenate(sent, axis=0)

    latent_mine, latent_more = group_sum(
        *local(
            latent_back, [(2 * step, DRANK, F32), (2 * step, DRANK, BF16)], d_decay, w_dup
        )
    )
    key_kept, key_got = far_split(key_pair)
    sent, main_grads, latent_more, key_got = tie(sent, main_grads, latent_more, key_got)
    main_pair = square_sum(main_grads)
    mixed_mine, mixed_more = group_sum(kept, sent)
    mixed_more, out_pair = tie(mixed_more, out_pair)
    out_kept, out_got = far_split(out_pair)
    val_sum, key_sum = far_add(val_kept, val_got), far_add(key_kept, key_got)
    rest_grad, delta_grad, top_one, cols_mix, down_grad, up_grad, ddown_grad = mixes_back(
        mixed_mine,
        mixed_more,
        latent_mine,
        latent_more,
        delta,
        mix_tanh,
        decay_tanh,
        blend,
        mixed_zero,
        w_down,
        w_up,
        w_ddown,
        vec,
    )
    rest_grad, main_pair, out_got = tie(rest_grad, main_pair, out_got)
    out_sum = far_add(out_kept, out_got)

    def norm_one_back(last, rest, shifted, arrived, normal, scale, middle, vec):
        below = jnp.where(last == 1, jnp.zeros_like(arrived[:1]), arrived[:1])
        grad = rest + rows_below(shifted, below)
        out = middle + norm_back(grad, vec[0:1], normal, scale[:, :1])
        cols = padded([column_sum(grad * normal), column_sum(grad)])
        return take_lanes(out, from_spans), cols

    block_input_gradient, cols_one = local(
        norm_one_back,
        [whole, (8, width, F32)],
        rest_grad,
        delta_grad,
        neighbour(top_one, -1),
        normal_one,
        scale_one,
        middle_grad,
        vec,
        scalar=last_flag,
    )
    main_sum = far_add(*far_split(main_pair))

    def column_parts(value):
        return [value[:, c * part : (c + 1) * part] for c in range(3)]

    out_cols, main_cols = column_parts(out_sum), column_parts(main_sum)
    first_grad = grad_total[0]
    holder = lax.div(me * rows, part)

    def rows_of(who):
        mine = lax.dynamic_slice_in_dim(first_grad, lax.rem(who * rows, part), rows, axis=1).T
        high = lax.reduce_precision(mine, 8, 7)
        return jnp.concatenate([high, mine - high], axis=1).astype(BF16)

    feedforward_gradient, handed = hand_rows(
        [[key_sum], [out_cols[1]], [val_sum]],
        [rows_of(jnp.bitwise_xor(me, flips(k))) for k in range(size)],
    )
    state_rows = handed[0]
    for k in range(1, size):
        state_rows = jnp.where(holder == (member ^ k), handed[k], state_rows)
    initial_state_gradient = state_rows[:, :SPAN] + state_rows[:, SPAN:]
    mixing_gradient = hand_rows([[m] for m in main_cols] + [[out_cols[2]], [out_cols[0]]])


    def spread(value):
        zero = jnp.zeros((width, value.shape[1]), F32)
        return lax.dynamic_update_slice_in_dim(zero, value, member * part, axis=0)

    vec_low = jnp.concatenate([cols_one[:2], cols_mix[:6], cols_two[:4]], axis=0)
    vec_head = jnp.concatenate(
        [jnp.sum(extra[:, :2], axis=0), jnp.sum(ends[:, SPAN : SPAN + 2], axis=0)], axis=0
    )
    by_feature = jnp.concatenate([down_grad, up_grad, ddown_grad, vec_low.T], axis=1)
    by_channel = spread(jnp.concatenate([tn(d_decay, dh_all), vec_head.T], axis=1))
    low = cube_sum(
        jnp.concatenate(
            [to_cube(by_feature), by_channel.reshape(*[2] * len(all_masks), rows, -1)], axis=-1
        ),
        BF16,
    )
    vec_at = decay_up + 12
    lowrank_gradient = jnp.concatenate(
        [low[:, :decay_up], low[:, vec_at : vec_at + DRANK]], axis=1
    )
    vectors_gradient = jnp.concatenate(
        [low[:, decay_up : decay_up + 8], low[:, vec_at + DRANK :], low[:, decay_up + 8 : vec_at]],
        axis=1,
    )
    return (
        block_output.reshape(1, step, width),
        block_input_gradient.reshape(1, step, width),
        initial_state_gradient,
        mixing_gradient,
        lowrank_gradient,
        vectors_gradient,
        feedforward_gradient,
    )


def solution(mesh):
    rowwise = P("seq", None)
    tokenwise = P(None, "seq", None)
    return jax.shard_map(
        functools.partial(on_device, mesh.shape["seq"]),
        mesh=mesh,
        in_specs=(tokenwise, P(), rowwise, rowwise, rowwise, rowwise, rowwise, tokenwise),
        out_specs=(tokenwise, tokenwise, rowwise, rowwise, rowwise, rowwise, rowwise),
        check_vma=False,
    )
```

```python
import functools

import jax
import jax.numpy as jnp
from jax import lax
from jax.experimental import pallas as pl
from jax.experimental.pallas import tpu as pltpu
from jax.sharding import PartitionSpec as P

HEADS = 32
SPAN = 64
FF = 7168
RANK = 32
DRANK = 64
LN_EPS = 1e-05
GN_EPS = 0.00064

F32 = jnp.float32
BF16 = jnp.bfloat16
HI = lax.Precision.HIGHEST


def nn(a, b):
    return jnp.dot(a, b, preferred_element_type=F32)


def nt(a, b):
    return lax.dot_general(a, b, (((1,), (1,)), ((), ())), preferred_element_type=F32)


def tn(a, b):
    return lax.dot_general(a, b, (((0,), (0,)), ((), ())), preferred_element_type=F32)


def knn(a, b):
    return lax.dot_general(
        a, b, (((1,), (0,)), ((), ())), preferred_element_type=F32
    )


def knt(a, b):
    return lax.dot_general(
        a, b, (((1,), (1,)), ((), ())), preferred_element_type=F32
    )


def ktn(a, b):
    return lax.dot_general(
        a, b, (((0,), (0,)), ((), ())), preferred_element_type=F32
    )


def low_lanes(shape):
    return lax.broadcasted_iota(jnp.int32, shape, len(shape) - 1) < SPAN


def head_sum(x):
    low = low_lanes(x.shape)
    s0 = jnp.sum(jnp.where(low, x, 0.0), axis=-1, keepdims=True)
    s1 = jnp.sum(jnp.where(low, 0.0, x), axis=-1, keepdims=True)
    return jnp.where(low, s0, s1)


def two_rows(x):
    low = low_lanes(x.shape)
    return jnp.concatenate([jnp.where(low, x, 0.0), jnp.where(low, 0.0, x)], axis=0)


def fold(full):
    return jnp.where(low_lanes((SPAN, 2 * SPAN)), full[:SPAN], full[SPAN:])


def unfold(state):
    low = low_lanes(state.shape)
    return jnp.concatenate([jnp.where(low, state, 0.0), jnp.where(low, 0.0, state)], axis=0)


def running(w, upper=False):
    count = w.shape[0]
    row = lax.broadcasted_iota(jnp.int32, (count, count), 0)
    col = lax.broadcasted_iota(jnp.int32, (count, count), 1)
    keep = (col >= row) if upper else (col <= row)
    return lax.dot_general(
        jnp.where(keep, 1.0, 0.0).astype(F32),
        w,
        (((1,), (0,)), ((), ())),
        precision=HI,
        preferred_element_type=F32,
    )


def strict(count):
    row = lax.broadcasted_iota(jnp.int32, (2 * count, count), 0)
    col = lax.broadcasted_iota(jnp.int32, (2 * count, count), 1)
    row = jnp.where(row >= count, row - count, row)
    return row > col, row == col


def affinity(r, k, u, q, ks):
    count = r.shape[0]
    below, diag = strict(count)
    raw = knt(two_rows(q), ks)
    share = jnp.sum(two_rows(r * u * k), axis=-1, keepdims=True)
    return jnp.where(below, raw, jnp.where(diag, share, 0.0))


def totals_kernel(k_ref, v_ref, w_ref, out_ref):
    cum = running(w_ref[...])
    total = cum[-1:, :]
    kc = k_ref[...] * jnp.exp(total - cum)
    out_ref[0, :SPAN, :] = fold(ktn(v_ref[...], kc))
    out_ref[0, SPAN:, :] = jnp.broadcast_to(jnp.exp(total), (8, 2 * SPAN))


def group_norm(y, gain, bias):
    centred = y - head_sum(y) * (1.0 / SPAN)
    spread = head_sum(centred * centred) * (1.0 / SPAN)
    scale = lax.rsqrt(spread + GN_EPS)
    normal = centred * scale
    return normal, scale, normal * gain + bias


def forward_kernel(r_ref, k_ref, v_ref, w_ref, g_ref, s_ref, p_ref, y_ref, gated_ref):
    r, k, v, w = r_ref[...], k_ref[...], v_ref[...], w_ref[...]
    cum = running(w)
    q = r * jnp.exp(cum - w)
    ks = k * jnp.exp(-cum)
    aff = affinity(r, k, p_ref[0:1, :], q, ks)
    count = r.shape[0]
    v2 = two_rows(v)
    y = (
        knt(q, unfold(s_ref[0]))
        + knn(aff[:count], v2[:count])
        + knn(aff[count:], v2[count:])
    )
    y_ref[...] = y
    gate = g_ref[...]
    _, _, grouped = group_norm(y, p_ref[1:2, :], p_ref[2:3, :])
    gated_ref[...] = (grouped * gate * jax.nn.sigmoid(gate)).astype(BF16)


def gate_kernel(gg_ref, g_ref, y_ref, r_ref, w_ref, p_ref, gate_ref, dy_ref, out_ref):
    gated_grad, gate, y = gg_ref[...], g_ref[...], y_ref[...]
    gain = p_ref[1:2, :]
    normal, scale, grouped = group_norm(y, gain, p_ref[2:3, :])
    sig = jax.nn.sigmoid(gate)
    gate_ref[...] = (gated_grad * grouped * sig * (1.0 + gate * (1.0 - sig))).astype(BF16)
    outer = gated_grad * gate * sig
    inner = outer * gain
    dy = scale * (
        inner
        - head_sum(inner) * (1.0 / SPAN)
        - normal * (head_sum(inner * normal) * (1.0 / SPAN))
    )
    dy_ref[...] = dy
    w = w_ref[...]
    q = r_ref[...] * jnp.exp(running(w) - w)
    out_ref[0, :SPAN, :] = fold(ktn(dy, q))
    gain_grad = jnp.sum(outer * normal, axis=0, keepdims=True)
    bias_grad = jnp.sum(outer, axis=0, keepdims=True)
    out_ref[0, SPAN:, :] = jnp.concatenate(
        [gain_grad, bias_grad, jnp.zeros((6, 2 * SPAN), F32)], axis=0
    )


def backward_kernel(
    r_ref, k_ref, v_ref, w_ref, dy_ref, s_ref, gs_ref, p_ref,
    dr_ref, dk_ref, dv_ref, dd_ref, out_ref,
):
    r, k, v, w, dy = r_ref[...], k_ref[...], v_ref[...], w_ref[...], dy_ref[...]
    u = p_ref[0:1, :]
    count = r.shape[0]
    cum = running(w)
    total = cum[-1:, :]
    e_before, e_minus, e_carry = jnp.exp(cum - w), jnp.exp(-cum), jnp.exp(total - cum)
    q, ks, kc = r * e_before, k * e_minus, k * e_carry
    aff = affinity(r, k, u, q, ks)
    below, _ = strict(count)
    dy2 = two_rows(dy)
    d_aff = jnp.where(below, knt(dy2, v), 0.0)
    own = head_sum(dy * v)
    state, grad_state = s_ref[0], gs_ref[0]
    state2, grad2 = unfold(state), unfold(grad_state)
    ks2 = two_rows(ks)
    dq = knn(dy, state2) + knn(d_aff[:count], ks2[:count]) + knn(d_aff[count:], ks2[count:])
    dks = ktn(d_aff, two_rows(q))
    dkc = knn(v, grad2)
    dv_ref[...] = (ktn(aff, dy2) + knt(kc, grad2)).astype(BF16)
    dr_ref[...] = (dq * e_before + own * u * k).astype(BF16)
    dk_ref[...] = (dks * e_minus + dkc * e_carry + own * u * r).astype(BF16)
    gq, gc = q * dq, kc * dkc
    d_total = jnp.sum(gc, axis=0, keepdims=True) + jnp.exp(total) * jnp.sum(
        state * grad_state, axis=0, keepdims=True
    )
    dw = running(gq - ks * dks - gc, upper=True) - gq + d_total
    term = dw * w
    dd_ref[...] = term.astype(BF16)
    out_ref[0] = jnp.concatenate(
        [
            jnp.sum(term, axis=0, keepdims=True),
            jnp.sum(own * r * k, axis=0, keepdims=True),
            jnp.zeros((6, 2 * SPAN), F32),
        ],
        axis=0,
    )


def block_call(kernel, chunks, step, width, ins, outs, args):
    lane = 2 * SPAN
    kinds = {
        "t": pl.BlockSpec((step, lane), lambda c, h: (c, h)),
        "s": pl.BlockSpec((1, SPAN, lane), lambda c, h: (c, 0, h)),
        "x": pl.BlockSpec((1, SPAN + 8, lane), lambda c, h: (c, 0, h)),
        "e": pl.BlockSpec((1, 8, lane), lambda c, h: (c, 0, h)),
        "p": pl.BlockSpec((8, lane), lambda c, h: (0, h)),
    }
    shapes = {
        "t": lambda d: jax.ShapeDtypeStruct((chunks * step, width), d),
        "x": lambda d: jax.ShapeDtypeStruct((chunks, SPAN + 8, width), d),
        "e": lambda d: jax.ShapeDtypeStruct((chunks, 8, width), d),
    }
    return pl.pallas_call(
        kernel,
        grid=(chunks, width // lane),
        in_specs=[kinds[kind] for kind in ins],
        out_specs=[kinds[kind] for kind, _ in outs],
        out_shape=[shapes[kind](dtype) for kind, dtype in outs],
        compiler_params=pltpu.CompilerParams(vmem_limit_bytes=48 * 1024 * 1024),
    )(*args)


def weight_grad(places, pairs, block):
    tokens, blocks = pairs[0][0].shape[0], places.shape[0]
    widths = [y.shape[1] for _, y in pairs]

    def kernel(_, *refs):
        at = 0
        for i, wide in enumerate(widths):
            refs[-1][0, :, at : at + wide] = tn(refs[2 * i][...], refs[2 * i + 1][...]).astype(
                BF16
            )
            at += wide

    specs = []
    for wide in widths:
        specs.append(pl.BlockSpec((tokens, block), lambda i, at: (0, at[i])))
        specs.append(pl.BlockSpec((tokens, wide), lambda i, at: (0, 0)))
    return pl.pallas_call(
        kernel,
        grid_spec=pltpu.PrefetchScalarGridSpec(
            num_scalar_prefetch=1,
            grid=(blocks,),
            in_specs=specs,
            out_specs=pl.BlockSpec((1, block, sum(widths)), lambda i, at: (i, 0, 0)),
        ),
        out_shape=jax.ShapeDtypeStruct((blocks, block, sum(widths)), BF16),
        compiler_params=pltpu.CompilerParams(vmem_limit_bytes=48 * 1024 * 1024),
    )(places, *[v for pair in pairs for v in pair])


def lanes_kernel(spans, x_ref, out_ref):
    at = 0
    for start, stop in spans:
        out_ref[:, at : at + stop - start] = x_ref[:, start:stop].astype(out_ref.dtype)
        at += stop - start


def move_lanes(spans, value, dtype):
    return pl.pallas_call(
        functools.partial(lanes_kernel, spans),
        in_specs=[pl.BlockSpec(memory_space=pltpu.VMEM)],
        out_specs=pl.BlockSpec(memory_space=pltpu.VMEM),
        out_shape=jax.ShapeDtypeStruct(value.shape, dtype),
        compiler_params=pltpu.CompilerParams(vmem_limit_bytes=32 * 1024 * 1024),
    )(value)


def place_kernel(counts, wide, block, at_ref, *refs):
    ins, out_ref, sems = refs[: len(counts)], refs[-2], refs[-1]
    rows = out_ref.shape[0]
    copies, i = [], 0
    for ref, n in zip(ins, counts):
        for j in range(n):
            start = pl.multiple_of(at_ref[i] * block, block)
            column = i * block // rows * wide
            copy = pltpu.make_async_copy(
                ref.at[pl.ds(j * block, block), :],
                out_ref.at[pl.ds(start, block), pl.ds(column, wide)],
                sems.at[i],
            )
            copy.start()
            copies.append(copy)
            i += 1
    for copy in copies:
        copy.wait()


def place_rows(parts, block):
    pieces = [p for part in parts for p in part[1]]
    wide = pieces[0].shape[1]
    at = jnp.concatenate([part[0] for part in parts])
    counts = [p.shape[0] // block for p in pieces]
    total = sum(counts)
    return pl.pallas_call(
        functools.partial(place_kernel, counts, wide, block),
        in_specs=[pl.BlockSpec(memory_space=pltpu.SMEM)]
        + [pl.BlockSpec(memory_space=pl.ANY)] * len(pieces),
        out_specs=pl.BlockSpec(memory_space=pl.ANY),
        out_shape=jax.ShapeDtypeStruct(
            (total * block // len(parts), wide * len(parts)), pieces[0].dtype
        ),
        scratch_shapes=[pltpu.SemaphoreType.DMA((total,))],
        compiler_params=pltpu.CompilerParams(vmem_limit_bytes=32 * 1024 * 1024),
    )(at, *pieces)


def mixes_kernel(
    open_ref, x_ref, before_ref, vec_ref, down_ref, up_ref, ddown_ref,
    m1_ref, m2_ref, m3_ref, m4_ref, dh_ref,
    normal_ref, scale_ref, delta_ref, blend_ref, m0_ref, tanh_ref, dtanh_ref,
):
    piece = pl.program_id(0)
    step = m1_ref.shape[0]
    x = x_ref[...].astype(F32)
    centred = x - jnp.mean(x, axis=-1, keepdims=True)
    scale = lax.rsqrt(jnp.mean(centred * centred, axis=-1, keepdims=True) + LN_EPS)
    normal = centred * scale
    full = normal * vec_ref[0:1, :] + vec_ref[1:2, :]
    normed = full[:step]
    first = jnp.where(open_ref[piece] == 1, before_ref[0:1, :], full[step : step + 1])
    row = lax.broadcasted_iota(jnp.int32, normed.shape, 0)
    delta = jnp.where(row == 0, first, pltpu.roll(normed, 1, 0)) - normed
    blend = (normed + delta * vec_ref[2:3, :]).astype(BF16)
    tanh = jnp.tanh(nn(blend, down_ref[...]))
    latent = tanh.astype(BF16)
    lane = lax.broadcasted_iota(jnp.int32, latent.shape, 1)
    mixed = []
    for c in range(5):
        own = (lane >= c * RANK) & (lane < (c + 1) * RANK)
        offset = nt(jnp.where(own, latent, jnp.zeros_like(latent)), up_ref[...])
        mixed.append((normed + delta * (vec_ref[3 + c : 4 + c, :] + offset)).astype(BF16))
    dtanh = jnp.tanh(nn(mixed[0], ddown_ref[...]))
    m1_ref[...], m2_ref[...], m3_ref[...], m4_ref[...] = mixed[1:]
    dh_ref[...] = dtanh.astype(BF16)

    @pl.when(piece == 0)
    def _():
        normal_ref[...] = normal[:step]
        scale_ref[...] = jnp.broadcast_to(scale[:step], scale_ref.shape)
        delta_ref[...] = delta
        blend_ref[...] = blend
        m0_ref[...] = mixed[0]
        tanh_ref[...] = tanh
        dtanh_ref[...] = dtanh


def group_mixes(opening, x, before, vec, down, up, ddown, step):
    high, width = step + 16, x.shape[1]
    pieces = x.shape[0] // high

    def whole(value):
        return pl.BlockSpec(value.shape, lambda k: (0, 0))

    def own(columns, dtype):
        return (
            pl.BlockSpec((step, columns), lambda k: (0, 0)),
            jax.ShapeDtypeStruct((step, columns), dtype),
        )

    def every(columns, dtype):
        return (
            pl.BlockSpec((step, columns), lambda k: ((k % 2) * 2 + k // 2, 0)),
            jax.ShapeDtypeStruct((pieces * step, columns), dtype),
        )

    outs = [every(width, BF16)] * 4 + [
        every(DRANK, BF16),
        own(width, F32),
        own(128, F32),
        own(width, F32),
        own(width, BF16),
        own(width, BF16),
        own(5 * RANK, F32),
        own(DRANK, F32),
    ]
    return pl.pallas_call(
        mixes_kernel,
        grid=(pieces,),
        in_specs=[
            pl.BlockSpec(memory_space=pltpu.SMEM),
            pl.BlockSpec((high, width), lambda k: (k, 0)),
            whole(before),
            whole(vec),
            whole(down),
            whole(up),
            whole(ddown),
        ],
        out_specs=[o[0] for o in outs],
        out_shape=[o[1] for o in outs],
        compiler_params=pltpu.CompilerParams(vmem_limit_bytes=56 * 1024 * 1024),
    )(opening, x, before, vec, down, up, ddown)


def product(pairs, outs, body, sides=(), tile=256):
    count = len(pairs)

    def kernel(*refs):
        ins, out_refs = refs[: 2 * count + len(sides)], refs[2 * count + len(sides) :]
        products = [
            (nn if pair[2] == "nn" else nt)(ins[2 * i][...], ins[2 * i + 1][...])
            for i, pair in enumerate(pairs)
        ]
        results = body(*products, *[r[...] for r in ins[2 * count :]])
        for ref, value in zip(out_refs, results):
            ref[...] = value.astype(ref.dtype)

    specs, args = [], []
    for a, b, form, at in pairs:
        depth = a.shape[1]
        specs.append(pl.BlockSpec(a.shape, lambda j: (0, 0)))
        if form == "nn":
            specs.append(pl.BlockSpec((depth, tile), lambda j, at=at: (0, at + j)))
        else:
            specs.append(pl.BlockSpec((tile, depth), lambda j, at=at: (j, at)))
        args += [a, b]
    for side in sides:
        specs.append(pl.BlockSpec((side.shape[0], tile), lambda j: (0, j)))
    return pl.pallas_call(
        kernel,
        grid=(outs[0][1] // tile,),
        in_specs=specs,
        out_specs=[pl.BlockSpec((o[0], tile), lambda j: (0, j)) for o in outs],
        out_shape=[jax.ShapeDtypeStruct(o[:2], o[2]) for o in outs],
        compiler_params=pltpu.CompilerParams(vmem_limit_bytes=56 * 1024 * 1024),
    )(*args, *sides)


def local(fn, outs, *args, scalar=None):
    def kernel(*refs):
        lead = [] if scalar is None else [refs[0]]
        ins, out_refs = refs[len(lead) : -len(outs)], refs[-len(outs) :]
        scalars = [r[i] for r in lead for i in range(r.shape[0])]
        results = fn(*scalars, *[r[...] for r in ins])
        for ref, value in zip(out_refs, results):
            ref[...] = value.astype(ref.dtype)

    specs = [pl.BlockSpec(memory_space=pltpu.VMEM)] * len(args)
    if scalar is not None:
        specs = [pl.BlockSpec(memory_space=pltpu.SMEM)] + specs
        args = (scalar.reshape(-1), *args)
    return pl.pallas_call(
        kernel,
        in_specs=specs,
        out_specs=[pl.BlockSpec(memory_space=pltpu.VMEM)] * len(outs),
        out_shape=[jax.ShapeDtypeStruct(o[:2], o[2]) for o in outs],
        compiler_params=pltpu.CompilerParams(vmem_limit_bytes=56 * 1024 * 1024),
    )(*args)


def take_lanes(value, spans):
    if len(spans) == 1:
        return value
    return jnp.concatenate([value[:, a:b] for a, b in spans], axis=1)


def norm_back(grad, gain, normal, scale):
    e = grad * gain
    return scale * (
        e
        - jnp.mean(e, axis=-1, keepdims=True)
        - normal * jnp.mean(e * normal, axis=-1, keepdims=True)
    )


def rows_above(value, first):
    row = lax.broadcasted_iota(jnp.int32, value.shape, 0)
    return jnp.where(row == 0, first, pltpu.roll(value, 1, 0))


def rows_below(value, last):
    row = lax.broadcasted_iota(jnp.int32, value.shape, 0)
    high = value.shape[0]
    return jnp.where(row == high - 1, last, pltpu.roll(value, high - 1, 0))


def padded(rows):
    return jnp.concatenate(
        list(rows) + [jnp.zeros((8 - len(rows), rows[0].shape[1]), F32)], axis=0
    )


def column_sum(value):
    return jnp.sum(value, axis=0, keepdims=True)


def gates_kernel(
    spans, who_ref, middle_ref, value_ref, more_ref, act_ref, cot_ref,
    out_ref, up_ref, vg_ref, rg_ref, held,
):
    to_spans, from_spans = spans
    step, part = act_ref.shape[0] // 4, act_ref.shape[1]
    who = who_ref[0]
    act = [
        act_ref[pl.ds(pl.multiple_of((who ^ j) * step, step), step), :] for j in range(4)
    ]
    recept = jax.nn.sigmoid(take_lanes(jnp.concatenate(act, axis=1).astype(F32), to_spans))
    value = value_ref[...] + more_ref[...].astype(F32)
    out = middle_ref[...] + recept * value
    out_ref[...] = take_lanes(out, from_spans).astype(BF16)
    up = take_lanes(cot_ref[...].astype(F32), to_spans)
    up_ref[...] = up
    vg_ref[...] = (up * recept).astype(BF16)
    held[...] = take_lanes(up * value * recept * (1.0 - recept), from_spans)
    for k in range(4):
        at = pl.multiple_of((who ^ k) * part, part)
        rg_ref[k * step : (k + 1) * step, :] = held[:, pl.ds(at, part)].astype(BF16)


def gates(spans, who, middle, value, more, act, cot):
    step, width = middle.shape
    part = act.shape[1]
    shape = jax.ShapeDtypeStruct
    return pl.pallas_call(
        functools.partial(gates_kernel, spans),
        in_specs=[pl.BlockSpec(memory_space=pltpu.SMEM)]
        + [pl.BlockSpec(memory_space=pltpu.VMEM)] * 5,
        out_specs=[pl.BlockSpec(memory_space=pltpu.VMEM)] * 4,
        out_shape=[
            shape((step, width), BF16),
            shape((step, width), F32),
            shape((step, width), BF16),
            shape((4 * step, part), BF16),
        ],
        scratch_shapes=[pltpu.VMEM((step, width), F32)],
        compiler_params=pltpu.CompilerParams(vmem_limit_bytes=56 * 1024 * 1024),
    )(who.reshape(1), middle, value, more, act, cot)


def mixes_back_kernel(
    kept_ref, got_ref, dl_ref, dl_more_ref, delta_ref, tanh_ref, dtanh_ref, blend_ref, m0_ref,
    down_ref, up_ref, ddown_ref, vec_ref,
    rest_ref, dg_ref, row_ref, cols_ref, down_out, up_out, ddown_out,
):
    step = delta_ref.shape[0]
    dtanh = dtanh_ref[...]
    decay_grad = dl_ref[...] + dl_more_ref[...].astype(F32)
    decay_pre = (decay_grad * (1.0 - dtanh * dtanh)).astype(BF16)
    ddown_out[...] = tn(m0_ref[...], decay_pre)
    tanh = tanh_ref[...]
    latent = tanh.astype(BF16)
    lane = lax.broadcasted_iota(jnp.int32, latent.shape, 1)
    delta, up = delta_ref[...], up_ref[...]
    latent_grad = jnp.zeros(latent.shape, F32)
    up_grad = jnp.zeros(up_out.shape, F32)
    dg = jnp.zeros(delta.shape, F32)
    total = jnp.zeros(delta.shape, F32)
    cols = []
    for c in range(5):
        own = (lane >= c * RANK) & (lane < (c + 1) * RANK)
        mine = jnp.where(own, latent, jnp.zeros_like(latent))
        if c == 0:
            grad = nt(decay_pre, ddown_ref[...])
        else:
            at = slice((c - 1) * step, c * step)
            grad = kept_ref[at, :] + got_ref[at, :].astype(F32)
        shift = grad * delta
        cols.append(column_sum(shift))
        offset = shift.astype(BF16)
        latent_grad = jnp.where(own, nn(offset, up), latent_grad)
        up_grad = up_grad + tn(offset, mine)
        dg = dg + grad * (vec_ref[3 + c : 4 + c, :] + nt(mine, up))
        total = total + grad
    up_out[...] = up_grad
    mix_pre = (latent_grad * (1.0 - tanh * tanh)).astype(BF16)
    down_out[...] = tn(blend_ref[...], mix_pre)
    blend_grad = nt(mix_pre, down_ref[...])
    dg = dg + blend_grad * vec_ref[2:3, :]
    rest_ref[...] = total + blend_grad - dg
    dg_ref[...] = dg
    row_ref[...] = dg[:8]
    cols_ref[...] = padded([column_sum(blend_grad * delta)] + cols)


def mixes_back(*args):
    delta, down, ddown = args[4], args[9], args[11]
    step, width = delta.shape
    shape = jax.ShapeDtypeStruct
    outs = [
        shape((step, width), F32),
        shape((step, width), F32),
        shape((8, width), F32),
        shape((8, width), F32),
        shape(down.shape, F32),
        shape(down.shape, F32),
        shape(ddown.shape, F32),
    ]
    return pl.pallas_call(
        mixes_back_kernel,
        in_specs=[pl.BlockSpec(memory_space=pltpu.VMEM)] * len(args),
        out_specs=[pl.BlockSpec(memory_space=pltpu.VMEM)] * len(outs),
        out_shape=outs,
        compiler_params=pltpu.CompilerParams(vmem_limit_bytes=60 * 1024 * 1024),
    )(*args)


def tie(*values):
    return lax.optimization_barrier(values)


def on_device(
    count,
    tokens,
    previous,
    initial_state,
    mixing_weights,
    lowrank_weights,
    vectors,
    feedforward_weights,
    cotangent,
):
    fast = initial_state.shape[0] == 64
    masks = (1, 8) if fast else (1, 2)
    size = 1 << len(masks)
    teams = count // size
    all_masks = [1 << b for b in range(count.bit_length() - 1)]
    team_masks = [b for b in all_masks if b not in masks]
    far = 16
    team_masks.sort(key=lambda b: fast and b != far)
    me = lax.axis_index("seq")
    _, step, width = tokens.shape
    rows = mixing_weights.shape[0]
    part = width // size
    ff_part = FF // size
    team_rows = rows * size
    def bit_of(who, mask):
        return (who // mask) % 2 if isinstance(who, int) else lax.rem(lax.div(who, mask), 2)

    def member_of(who):
        return sum(bit_of(who, b) << j for j, b in enumerate(masks))

    def team_of(who):
        return sum(bit_of(who, b) << j for j, b in enumerate(team_masks))

    member, team = member_of(me), team_of(me)
    order = sorted(range(count), key=lambda d: (team_of(d), member_of(d)))
    inverse = sorted(range(count), key=lambda p: order[p])
    across = [order[m::size] for m in range(size)]
    square = [order[m :: 2 * size] for m in range(2 * size)]
    def lane_spans(blocks):
        spans = []
        for d in blocks:
            if spans and spans[-1][1] == d * rows:
                spans[-1][1] = (d + 1) * rows
            else:
                spans.append([d * rows, (d + 1) * rows])
        return spans

    to_spans, from_spans = lane_spans(order), lane_spans(inverse)

    def to_places(value, dtype):
        return move_lanes(to_spans, value, dtype)

    def flips(k):
        return sum(b for j, b in enumerate(masks) if (k >> j) & 1)

    def trade(value, mask):
        return lax.ppermute(value, "seq", [(d, d ^ mask) for d in range(count)])

    def group_gather(value):
        side = trade(value, masks[1])
        return value, side, trade(jnp.concatenate([value, side], axis=0), masks[0])

    def group_rows(value):
        high, columns = value.shape

        def lay(own, side, far):
            return (jnp.concatenate([own, far[:high], side, far[high:]], axis=0),)

        return local(lay, [(size * high, columns, value.dtype)], *group_gather(value))[0]

    def halves(value):
        cut = [value[k * step : (k + 1) * step] for k in range(size)]
        return [cut[0], cut[2]], [cut[1], cut[3]]

    def group_fold(kept, sent):
        high, columns = kept.shape[0] // 2, kept.shape[1]
        got = trade(sent, masks[0])

        def add(mine, more):
            total = mine + more.astype(F32)
            return total[:high], total[high:]

        return local(add, [(high, columns, F32), (high, columns, BF16)], kept, got)

    def group_sum(kept, sent):
        mine, side = group_fold(kept, sent)
        return mine, trade(side, masks[1])

    def crossing_sum(*pairs):
        units = len(pairs)

        def body(*products):
            parts = [halves(p) for p in products]
            kept = [p[0][i] for i in range(2) for p in parts]
            sent = [p[1][i] for i in range(2) for p in parts]
            return jnp.concatenate(kept, axis=0), jnp.concatenate(sent, axis=0)

        high = 2 * units * step
        return product(
            [(a, b, "nt", at) for a, b, at in pairs],
            [(high, width, F32), (high, width, BF16)],
            body,
            tile=512,
        )

    def exchange(pieces):
        pieces, high = list(pieces), pieces[0].shape[0]
        for j in reversed(range(len(masks))):
            keys = [k for k in range(size) if (k >> j) & 1]
            got = trade(jnp.concatenate([pieces[k] for k in keys], axis=0), masks[j])
            for i, k in enumerate(keys):
                pieces[k] = got[i * high : (i + 1) * high]
        return pieces

    def ordered(pieces):
        pieces = list(pieces)
        for j in range(len(masks)):
            swap = lax.rem(lax.div(member, 1 << j), 2) == 1
            pieces = [
                jnp.where(swap, pieces[k ^ (1 << j)], pieces[k]) for k in range(len(pieces))
            ]
        return pieces

    def neighbour(value, offset):
        pairs = [(d, d + offset) for d in range(count) if 0 <= d + offset < count]
        return lax.ppermute(value, "seq", pairs)

    def take_columns(value, spans, who):
        return jnp.concatenate(
            [
                lax.dynamic_slice_in_dim(value, start + who * wide, wide, axis=1)
                for start, wide in spans
            ],
            axis=1,
        )

    def group_columns(value, spans):
        pieces = [take_columns(value, spans, member ^ k) for k in range(size)]
        return jnp.concatenate(ordered(exchange(pieces)), axis=0)

    def crossing(first):
        bits = list(range(1, len(team_masks))) + [0]
        if first:
            bits[0], bits[1] = bits[1], bits[0]
        return bits

    def gather_rows(own):
        return lax.all_gather(own, "seq", axis=0, tiled=True, axis_index_groups=across)

    def far_send(own):
        return trade(own, far) if fast else own

    def far_join(own, got):
        if not fast:
            return own
        upper = bit_of(me, far) == 1
        return jnp.concatenate(
            [jnp.where(upper, got, own), jnp.where(upper, own, got)], axis=0
        )

    def gather_square(paired):
        groups = square if fast else across
        return lax.all_gather(paired, "seq", axis=0, tiled=True, axis_index_groups=groups)

    def team_products(*pairs):
        if fast:
            places = jnp.arange(teams, dtype=jnp.int32)
            return weight_grad(places, pairs, team_rows).reshape(width, -1)
        return jnp.concatenate([tn(x, y).astype(BF16) for x, y in pairs], axis=1)

    def square_sum(grads):
        groups = square if fast else across
        return lax.psum_scatter(
            grads, "seq", scatter_dimension=0, tiled=True, axis_index_groups=groups
        )

    def far_split(pair):
        if not fast:
            return pair, jnp.zeros_like(pair)
        bit = bit_of(me, far)
        sent = lax.dynamic_slice_in_dim(pair, (1 - bit) * team_rows, team_rows, axis=0)
        kept = lax.dynamic_slice_in_dim(pair, bit * team_rows, team_rows, axis=0)
        return kept, trade(sent, far)

    def far_add(kept, got):
        return (kept.astype(F32) + got.astype(F32)).astype(BF16)

    def cube_gather(value, follower=None):
        for mask in reversed(all_masks):
            got = trade(value, mask)
            upper = bit_of(me, mask) == 1
            value = jnp.stack([jnp.where(upper, got, value), jnp.where(upper, value, got)])
            if mask == 8 and follower is not None:
                value, follower = tie(value, follower)
        axes = len(all_masks)
        cube = value.transpose(*reversed(range(axes)), *range(axes, value.ndim))
        return cube if follower is None else (cube, follower)

    place_axes = [all_masks[::-1].index(b) for b in team_masks[::-1] + list(masks[::-1])]

    def by_place(cube):
        rest = range(len(all_masks), cube.ndim)
        return cube.transpose(*place_axes, *rest).reshape(width, -1)

    def to_cube(value):
        cube = value.reshape(*[2] * len(place_axes), rows, -1)
        back = [place_axes.index(a) for a in range(len(place_axes))]
        return cube.transpose(*back, len(back), len(back) + 1)

    def cube_sum(cube, kind):
        for axis, mask in reversed(list(enumerate(reversed(all_masks)))):
            bit = bit_of(me, mask)
            sent = lax.dynamic_index_in_dim(cube, 1 - bit, axis, keepdims=False)
            kept = lax.dynamic_index_in_dim(cube, bit, axis, keepdims=False)
            cube = kept.astype(F32) + trade(sent.astype(kind), mask).astype(F32)
        return cube

    def hand_rows(pieces, extra=None):
        widths = [sum(p.shape[1] for p in piece) for piece in pieces]
        joint = jnp.concatenate([p for piece in pieces for p in piece], axis=1)
        mine = [
            lax.dynamic_slice_in_dim(joint, (member ^ k) * rows, rows, axis=0)
            for k in range(size)
        ]
        if extra is not None:
            mine = [jnp.concatenate([m, e], axis=1) for m, e in zip(mine, extra)]
        by_place = exchange(mine)
        by_member = ordered(by_place)
        outs, start = [], 0
        for wide in widths:
            outs += [p[:, start : start + wide] for p in by_member]
            start += wide
        joined = jnp.concatenate(outs, axis=1).astype(F32)
        if extra is None:
            return joined
        return joined, [p[:, start:].astype(F32) for p in by_place]

    up_start, decay_start, decay_up = 5 * RANK, 10 * RANK, 10 * RANK + DRANK
    last_row = neighbour(tokens[0, -1:, :], 1)
    tokens_sent = to_places(
        jnp.concatenate([tokens[0], jnp.broadcast_to(last_row, (16, width))], axis=0), BF16
    )
    natural, mix_in = cube_gather(
        jnp.concatenate(
            [vectors, initial_state, lowrank_weights[:, decay_up:].astype(F32)], axis=1
        ),
        mixing_weights,
    )
    natural = natural.reshape(width, -1)
    low_cube, mix_in = cube_gather(lowrank_weights[:, :decay_up], mix_in)
    tokens_all = jnp.concatenate(group_gather(tokens_sent), axis=0)
    mix_local = group_columns(mix_in, [(c * width, part) for c in range(5)])
    mix_local, natural, low_cube, tokens_all = tie(mix_local, natural, low_cube, tokens_all)
    lowrank = by_place(low_cube)
    mix_kv, mix_rest = mix_local[:, : 2 * part], mix_local[:, 2 * part :]
    kv_got, mix_rest = tie(far_send(mix_kv), mix_rest)
    w_kv = gather_square(far_join(mix_kv, kv_got))
    tiles = part // 256

    mine = lax.dynamic_slice_in_dim(natural, member * part, part, axis=0)
    vec_part = mine[:, :16].T
    first_state = mine[:, 16 : 16 + SPAN].T
    w_dup = mine[:, 16 + SPAN :].astype(BF16)
    vec = by_place(
        natural[:, :16].reshape(*[2] * len(all_masks), rows, 16)
    ).T
    wkv_rows = jnp.concatenate([vec_part[9:12], jnp.zeros((5, part), F32)], axis=0)
    is_first = (me == 0).astype(jnp.int32)
    before = to_places(previous.reshape(2, width), F32)
    w_down, w_up = lowrank[:, :up_start], lowrank[:, up_start:decay_start]
    w_ddown = lowrank[:, decay_start:]

    opening = jnp.stack(
        [jnp.bitwise_xor(me, flips(k)) == 0 for k in (0, 2, 1, 3)]
    ).astype(jnp.int32)
    (
        *mixed_all, dh_all, normal_one, scale_one, delta, blend, mixed_zero, mix_tanh, decay_tanh,
    ) = group_mixes(opening, tokens_all, before, vec, w_down, w_up, w_ddown, step)
    rest_got, mixed_all[0], feed_in = tie(far_send(mix_rest), mixed_all[0], feedforward_weights)
    w_rest = gather_square(far_join(mix_rest, rest_got))
    ff_spans = [(0, ff_part), (FF, part), (FF + width, ff_part)]
    ff_local = group_columns(feed_in, ff_spans)
    everyone = size * step
    (log_decay,) = product(
        [(dh_all, w_dup, "nt", 0)],
        [(everyone, part, F32)],
        lambda acc, base: (-jnp.exp(base + acc),),
        sides=(vec_part[8:9],),
    )
    keys, values = product(
        [(mixed_all[0], w_kv, "nn", 0), (mixed_all[1], w_kv, "nn", tiles)],
        [(everyone, part, F32)] * 2,
        lambda a, b: (a, b),
    )

    keys, ff_local = tie(keys, ff_local)
    ff_tail = ff_local[:, ff_part + part :]
    ff_near = ff_local[:, : ff_part + part]
    near_got = far_send(ff_near)

    call = functools.partial(block_call, chunks=size, step=step, width=part)
    (totals,) = call(
        totals_kernel, ins="ttt", outs=[("x", F32)], args=(keys, values, log_decay)
    )
    stages, current = [], [None, []]
    for mask in all_masks:
        if mask in masks:
            current[1].append(1 << masks.index(mask))
        else:
            stages.append(current)
            current = [mask, []]
    stages.append(current)
    high, long = SPAN + 8, SPAN + 16

    def chain(early, late):
        return early[0] * late[0], late[0] * early[1] + late[1]

    def pick(flag, yes, no):
        return tuple(jnp.where(flag, a, b) for a, b in zip(yes, no))

    def rows8(row):
        return jnp.broadcast_to(row, (8, part))

    def pack(items):
        return jnp.concatenate([r for d, v in items for r in (v, rows8(d))], axis=0)

    def unpack(array, count):
        cut = [array[i * high : (i + 1) * high] for i in range(count)]
        return [(c[SPAN : SPAN + 1], c[:SPAN]) for c in cut]

    def swap_members(who, pieces):
        pieces = list(pieces)
        for j in range(len(masks)):
            flag = (who // (1 << j)) % 2 == 1
            pieces = [jnp.where(flag, pieces[k ^ (1 << j)], pieces[k]) for k in range(size)]
        return pieces

    def neutral():
        return jnp.ones((1, part), F32), jnp.zeros((SPAN, part), F32)

    def flags_of(mask):
        bit = jnp.int32(0) if mask is None else bit_of(me, mask)
        return jnp.stack([member, bit]).astype(jnp.int32)

    keys_at, decays = list(range(size)), []
    open_bits = size - 1
    stage_arrays = [totals.reshape(size * high, part)]
    for index, (mask, merges) in enumerate(stages):
        last = index + 1 == len(stages)
        after_keys = keys_at
        for bit in merges:
            after_keys = [g for g in after_keys if not g & bit]

        def forward_stage(
            who, late, *arrays, mask=mask, merges=merges, groups=keys_at, bits=open_bits, last=last
        ):
            marks = []
            if mask is None:
                cut = [arrays[0][k * high : (k + 1) * high] for k in range(size)]
                total = {
                    m: (p[SPAN : SPAN + 1], p[:SPAN])
                    for m, p in enumerate(swap_members(who, cut))
                }
                chunks = [neutral() for _ in range(size)]
            else:
                total = dict(zip(groups, unpack(arrays[0], len(groups))))
                chunks = unpack(arrays[1], size)
                other = {}
                for i, g in enumerate(groups):
                    got = arrays[2][i * long : (i + 1) * long].astype(F32)
                    other[g] = got[SPAN : SPAN + 1] + got[SPAN + 8 : SPAN + 9], got[:SPAN]
                marks += [total[g][0] for g in groups] + [other[g][0] for g in groups]
                late = late == 1
                chunks = [
                    pick(late, chain(other[m & bits], c), c) for m, c in enumerate(chunks)
                ]
                total = {
                    g: pick(late, chain(other[g], total[g]), chain(total[g], other[g]))
                    for g in groups
                }
            for bit in merges:
                marks += [total[g][0] for g in total]
                chunks = [
                    chain(total[(m & bits) ^ bit], c) if m & bit else c
                    for m, c in enumerate(chunks)
                ]
                total = {g: chain(total[g], total[g | bit]) for g in total if not g & bit}
                bits ^= bit
            marks = jnp.concatenate([rows8(r) for r in marks], axis=0)
            if last:
                states = [d * arrays[-1] + v for d, v in chunks]
                return jnp.concatenate(swap_members(who, states), axis=0), marks
            sent = []
            for d, v in total.values():
                first = d.astype(BF16)
                rest = (d - first.astype(F32)).astype(BF16)
                sent += [v.astype(BF16), rows8(first), rows8(rest)]
            return (
                pack(list(total.values())), pack(chunks), jnp.concatenate(sent, axis=0), marks
            )

        count_marks = (0 if mask is None else 2 * len(keys_at)) + sum(
            len(keys_at) >> i for i in range(len(merges))
        )
        marks_out = (8 * count_marks, part, F32)
        if last:
            outs = [(size * SPAN, part, F32), marks_out]
            state_in, marks = local(
                forward_stage, outs, *stage_arrays, first_state, scalar=flags_of(mask)
            )
            state_in = state_in.reshape(size, SPAN, part)
        else:
            outs = [
                (len(after_keys) * high, part, F32),
                (size * high, part, F32),
                (len(after_keys) * long, part, BF16),
                marks_out,
            ]
            total, chunks, sent, marks = local(
                forward_stage, outs, *stage_arrays, scalar=flags_of(mask)
            )
            if mask == (2 if fast else 4):
                sent, near_got = tie(sent, near_got)
            stage_arrays = [total, chunks, trade(sent, stages[index + 1][0])]
        decays.append(marks)
        keys_at = after_keys
        for bit in merges:
            open_bits ^= bit
    w_near = gather_square(far_join(ff_near, near_got))
    w_key, w_rec = w_near, w_near[:, ff_part:]
    state_in, ff_tail = tie(state_in, ff_tail)
    val_got = far_send(ff_tail)

    receipt, gate_pre = product(
        [(mixed_all[2], w_rest, "nn", 0), (mixed_all[3], w_rest, "nn", tiles)],
        [(everyone, part, F32)] * 2,
        lambda a, b: (a, b),
    )
    wkv, gated = call(
        forward_kernel,
        ins="tttttsp",
        outs=[("t", F32), ("t", BF16)],
        args=(receipt, keys, values, log_decay, gate_pre, state_in, wkv_rows),
    )
    gated, val_got = tie(gated, val_got)
    w_val = gather_square(far_join(ff_tail, val_got))
    branch, branch_more = group_sum(*crossing_sum((gated, w_rest, 2)))

    def norm_two(hidden, mine, more, vec):
        middle = hidden[:step].astype(F32) + mine + more.astype(F32)
        centred = middle - jnp.mean(middle, axis=-1, keepdims=True)
        scale = lax.rsqrt(jnp.mean(centred * centred, axis=-1, keepdims=True) + LN_EPS)
        normal = centred * scale
        tail = normal[step - 8 :] * vec[12:13] + vec[13:14]
        return middle, normal, jnp.broadcast_to(scale, (step, 128)), tail

    whole = (step, width, F32)
    middle, normal_two, scale_two, tail_two = local(
        norm_two,
        [whole, whole, (step, 128, F32), (8, width, F32)],
        tokens_sent,
        branch,
        branch_more,
        vec,
    )

    def mix_two(first, normal, arrived, before, vec):
        normed = normal * vec[12:13] + vec[13:14]
        above = jnp.where(first == 1, before[1:2], arrived[7:8])
        delta = rows_above(normed, above) - normed
        key_in, recv_in = normed + delta * vec[14:15], normed + delta * vec[15:16]
        return jnp.concatenate([key_in, recv_in], axis=0), delta

    both, delta_two = local(
        mix_two,
        [(2 * step, width, BF16), whole],
        normal_two,
        neighbour(tail_two, 1),
        before,
        vec,
        scalar=is_first,
    )

    key_all, recv_all = group_rows(both[:step]), group_rows(both[step:])
    relu, squared = product(
        [(key_all, w_key, "nn", 0)],
        [(everyone, ff_part, F32), (everyone, ff_part, BF16)],
        lambda acc: (jnp.maximum(acc, 0.0), jnp.square(jnp.maximum(acc, 0.0))),
        tile=ff_part // 2,
    )
    (recept_act,) = product(
        [(recv_all, w_rec, "nn", 0)],
        [(everyone, part, BF16)],
        lambda acc: (acc,),
    )
    squared, recept_act = tie(squared, recept_act)
    acts = exchange([recept_act[k * step : (k + 1) * step] for k in range(size)])
    value, value_more = group_sum(*crossing_sum((squared, w_val, 0)))
    block_output, upstream, value_grad, recept_grads = gates(
        (to_spans, from_spans),
        member,
        middle,
        value,
        value_more,
        jnp.concatenate(acts, axis=0),
        cotangent.reshape(step, width),
    )

    rg_all = jnp.concatenate(
        exchange([recept_grads[k * step : (k + 1) * step] for k in range(size)]), axis=0
    )
    vg_all = group_rows(value_grad)
    val_grads = team_products((vg_all, squared))
    vg_all, val_grads, rg_all = tie(vg_all, val_grads, rg_all)
    val_pair = square_sum(val_grads)
    (key_grad,) = product(
        [(vg_all, w_val, "nn", 0)],
        [(everyone, ff_part, BF16)],
        lambda acc, relu: (acc * (2.0 * relu),),
        sides=(relu,),
        tile=ff_part // 2,
    )
    key_grads = team_products((key_all, key_grad))
    key_grad, key_grads = tie(key_grad, key_grads)
    key_pair = square_sum(key_grads)
    recv_two = group_sum(*crossing_sum((rg_all, w_rec, 0)))
    key_two = group_sum(*crossing_sum((key_grad, w_key, 0)))

    def inputs_back(key, key_more, recv, recv_more, vec):
        key, recv = key + key_more.astype(F32), recv + recv_more.astype(F32)
        top = key[:8] * vec[14:15] + recv[:8] * vec[15:16]
        return jnp.concatenate([key, recv], axis=0), top

    in_grads, top_two = local(
        inputs_back, [(2 * step, width, F32), (8, width, F32)], *key_two, *recv_two, vec
    )
    last_flag = (me == count - 1).astype(jnp.int32)

    def norm_two_back(last, grads, arrived, upstream, normal, scale, delta, vec):
        key_grad, recv_grad = grads[:step], grads[step:]
        shifted = key_grad * vec[14:15] + recv_grad * vec[15:16]
        below = jnp.where(last == 1, jnp.zeros_like(arrived[:1]), arrived[:1])
        grad = (
            key_grad * (1.0 - vec[14:15])
            + recv_grad * (1.0 - vec[15:16])
            + rows_below(shifted, below)
        )
        out = upstream + norm_back(grad, vec[12:13], normal, scale[:, :1])
        cols = padded(
            [
                column_sum(grad * normal),
                column_sum(grad),
                column_sum(key_grad * delta),
                column_sum(recv_grad * delta),
            ]
        )
        return out, out, cols

    middle_grad, branch_grad, cols_two = local(
        norm_two_back,
        [whole, (step, width, BF16), (8, width, F32)],
        in_grads,
        neighbour(top_two, -1),
        upstream,
        normal_two,
        scale_two,
        delta_two,
        vec,
        scalar=last_flag,
    )

    bg_all = group_rows(branch_grad)
    (gated_grad,) = product(
        [(bg_all, w_rest, "nn", 2 * tiles)], [(everyone, part, F32)], lambda acc: (acc,)
    )
    gate_grad, wkv_grad, ends = call(
        gate_kernel,
        ins="tttttp",
        outs=[("t", BF16), ("t", F32), ("x", F32)],
        args=(gated_grad, gate_pre, wkv, receipt, log_decay, wkv_rows),
    )
    val_kept, val_got = far_split(val_pair)
    keys_at, open_bits = list(range(size)), size - 1
    stage_arrays = [ends.reshape(size * high, part)]
    for index, (mask, merges) in enumerate(stages):
        last = index + 1 == len(stages)
        after_keys = keys_at
        for bit in merges:
            after_keys = [g for g in after_keys if not g & bit]

        def backward_stage(
            who, late, *arrays, mask=mask, merges=merges, groups=keys_at, bits=open_bits, last=last
        ):
            marks = [arrays[-1][i * 8 : i * 8 + 1] for i in range(arrays[-1].shape[0] // 8)]
            if mask is None:
                cut = [arrays[0][k * high : k * high + SPAN] for k in range(size)]
                total = dict(enumerate(swap_members(who, cut)))
                chunks = [neutral() for _ in range(size)]
            else:
                total = {g: arrays[0][i * SPAN : (i + 1) * SPAN] for i, g in enumerate(groups)}
                chunks = unpack(arrays[1], size)
                other = {
                    g: arrays[2][i * SPAN : (i + 1) * SPAN].astype(F32)
                    for i, g in enumerate(groups)
                }
                here = dict(zip(groups, marks))
                there = dict(zip(groups, marks[len(groups) :]))
                marks = marks[2 * len(groups) :]
                early = late == 0
                chunks = [
                    pick(
                        early,
                        (d * there[m & bits], d * other[m & bits] + v),
                        (d, v),
                    )
                    for m, (d, v) in enumerate(chunks)
                ]
                total = {
                    g: jnp.where(
                        early,
                        total[g] + here[g] * other[g],
                        other[g] + there[g] * total[g],
                    )
                    for g in groups
                }
            for bit in merges:
                here = dict(zip(total, marks))
                marks = marks[len(total) :]
                chunks = [
                    (d, v)
                    if m & bit
                    else (d * here[(m & bits) | bit], d * total[(m & bits) | bit] + v)
                    for m, (d, v) in enumerate(chunks)
                ]
                total = {
                    g: total[g] + here[g] * total[g | bit] for g in total if not g & bit
                }
                bits ^= bit
            joint = jnp.concatenate(list(total.values()), axis=0)
            if last:
                grads = swap_members(who, [v for _, v in chunks])
                return jnp.concatenate(grads, axis=0), joint
            return joint, pack(chunks), joint

        if last:
            outs = [(size * SPAN, part, F32), (SPAN, part, F32)]
            grad_out, first_grad = local(
                backward_stage, outs, *stage_arrays, decays[index], scalar=flags_of(mask)
            )
            grad_out = grad_out.reshape(size, SPAN, part)
        else:
            outs = [
                (len(after_keys) * SPAN, part, F32),
                (size * high, part, F32),
                (len(after_keys) * SPAN, part, BF16),
            ]
            total, chunks, sent = local(
                backward_stage, outs, *stage_arrays, decays[index], scalar=flags_of(mask)
            )
            if mask == (2 if fast else 4):
                sent, val_got = tie(sent, val_got)
            stage_arrays = [total, chunks, trade(sent, stages[index + 1][0])]
        keys_at = after_keys
        for bit in merges:
            open_bits ^= bit
    out_grads = team_products((bg_all, gated), (recv_all, rg_all), (mixed_all[3], gate_grad))
    grad_out, out_grads = tie(grad_out, out_grads)
    out_pair = square_sum(out_grads)

    d_receipt, d_keys, d_values, d_decay, extra = call(
        backward_kernel,
        ins="tttttssp",
        outs=[("t", BF16)] * 4 + [("e", F32)],
        args=(receipt, keys, values, log_decay, wkv_grad, state_in, grad_out, wkv_rows),
    )
    grads = [d_keys, d_values, d_receipt, gate_grad]
    kept, sent = crossing_sum(
        *[(grads[c], w_rest if c > 1 else w_kv, c % 2) for c in range(4)]
    )
    main_grads = team_products(
        (mixed_all[0], d_keys), (mixed_all[1], d_values), (mixed_all[2], d_receipt)
    )

    def latent_back(grad, up):
        kept, sent = halves(nn(grad, up))
        return jnp.concatenate(kept, axis=0), jnp.concatenate(sent, axis=0)

    latent_mine, latent_more = group_sum(
        *local(
            latent_back, [(2 * step, DRANK, F32), (2 * step, DRANK, BF16)], d_decay, w_dup
        )
    )
    key_kept, key_got = far_split(key_pair)
    sent, main_grads, latent_more, key_got = tie(sent, main_grads, latent_more, key_got)
    main_pair = square_sum(main_grads)
    mixed_mine, mixed_more = group_sum(kept, sent)
    mixed_more, out_pair = tie(mixed_more, out_pair)
    out_kept, out_got = far_split(out_pair)
    val_sum, key_sum = far_add(val_kept, val_got), far_add(key_kept, key_got)
    rest_grad, delta_grad, top_one, cols_mix, down_grad, up_grad, ddown_grad = mixes_back(
        mixed_mine,
        mixed_more,
        latent_mine,
        latent_more,
        delta,
        mix_tanh,
        decay_tanh,
        blend,
        mixed_zero,
        w_down,
        w_up,
        w_ddown,
        vec,
    )
    rest_grad, main_pair, out_got = tie(rest_grad, main_pair, out_got)
    out_sum = far_add(out_kept, out_got)

    def norm_one_back(last, rest, shifted, arrived, normal, scale, middle, vec):
        below = jnp.where(last == 1, jnp.zeros_like(arrived[:1]), arrived[:1])
        grad = rest + rows_below(shifted, below)
        out = middle + norm_back(grad, vec[0:1], normal, scale[:, :1])
        cols = padded([column_sum(grad * normal), column_sum(grad)])
        return take_lanes(out, from_spans), cols

    block_input_gradient, cols_one = local(
        norm_one_back,
        [whole, (8, width, F32)],
        rest_grad,
        delta_grad,
        neighbour(top_one, -1),
        normal_one,
        scale_one,
        middle_grad,
        vec,
        scalar=last_flag,
    )
    main_sum = far_add(*far_split(main_pair))

    def column_parts(value):
        return [value[:, c * part : (c + 1) * part] for c in range(3)]

    out_cols, main_cols = column_parts(out_sum), column_parts(main_sum)
    holder = lax.div(me * rows, part)

    def rows_of(who):
        mine = lax.dynamic_slice_in_dim(first_grad, lax.rem(who * rows, part), rows, axis=1).T
        high = lax.reduce_precision(mine, 8, 7)
        return jnp.concatenate([high, mine - high], axis=1).astype(BF16)

    feedforward_gradient, handed = hand_rows(
        [[key_sum], [out_cols[1]], [val_sum]],
        [rows_of(jnp.bitwise_xor(me, flips(k))) for k in range(size)],
    )
    state_rows = handed[0]
    for k in range(1, size):
        state_rows = jnp.where(holder == (member ^ k), handed[k], state_rows)
    initial_state_gradient = state_rows[:, :SPAN] + state_rows[:, SPAN:]
    mixing_gradient = hand_rows([[m] for m in main_cols] + [[out_cols[2]], [out_cols[0]]])


    def spread(value):
        zero = jnp.zeros((width, value.shape[1]), F32)
        return lax.dynamic_update_slice_in_dim(zero, value, member * part, axis=0)

    vec_low = jnp.concatenate([cols_one[:2], cols_mix[:6], cols_two[:4]], axis=0)
    vec_head = jnp.concatenate(
        [jnp.sum(extra[:, :2], axis=0), jnp.sum(ends[:, SPAN : SPAN + 2], axis=0)], axis=0
    )
    by_feature = jnp.concatenate([down_grad, up_grad, ddown_grad, vec_low.T], axis=1)
    by_channel = spread(jnp.concatenate([tn(d_decay, dh_all), vec_head.T], axis=1))
    low = cube_sum(
        jnp.concatenate(
            [to_cube(by_feature), by_channel.reshape(*[2] * len(all_masks), rows, -1)], axis=-1
        ),
        BF16,
    )
    vec_at = decay_up + 12
    lowrank_gradient = jnp.concatenate(
        [low[:, :decay_up], low[:, vec_at : vec_at + DRANK]], axis=1
    )
    vectors_gradient = jnp.concatenate(
        [low[:, decay_up : decay_up + 8], low[:, vec_at + DRANK :], low[:, decay_up + 8 : vec_at]],
        axis=1,
    )
    return (
        block_output.reshape(1, step, width),
        block_input_gradient.reshape(1, step, width),
        initial_state_gradient,
        mixing_gradient,
        lowrank_gradient,
        vectors_gradient,
        feedforward_gradient,
    )


def solution(mesh):
    rowwise = P("seq", None)
    tokenwise = P(None, "seq", None)
    return jax.shard_map(
        functools.partial(on_device, mesh.shape["seq"]),
        mesh=mesh,
        in_specs=(tokenwise, P(), rowwise, rowwise, rowwise, rowwise, rowwise, tokenwise),
        out_specs=(tokenwise, tokenwise, rowwise, rowwise, rowwise, rowwise, rowwise),
        check_vma=False,
    )
```

```python
import functools

import jax
import jax.numpy as jnp
from jax import lax
from jax.experimental import pallas as pl
from jax.experimental.pallas import tpu as pltpu
from jax.sharding import PartitionSpec as P

HEADS = 32
SPAN = 64
FF = 7168
RANK = 32
DRANK = 64
LN_EPS = 1e-05
GN_EPS = 0.00064

F32 = jnp.float32
BF16 = jnp.bfloat16
HI = lax.Precision.HIGHEST


def nn(a, b):
    return jnp.dot(a, b, preferred_element_type=F32)


def nt(a, b):
    return lax.dot_general(a, b, (((1,), (1,)), ((), ())), preferred_element_type=F32)


def tn(a, b):
    return lax.dot_general(a, b, (((0,), (0,)), ((), ())), preferred_element_type=F32)


def knn(a, b):
    return lax.dot_general(
        a, b, (((1,), (0,)), ((), ())), preferred_element_type=F32
    )


def knt(a, b):
    return lax.dot_general(
        a, b, (((1,), (1,)), ((), ())), preferred_element_type=F32
    )


def ktn(a, b):
    return lax.dot_general(
        a, b, (((0,), (0,)), ((), ())), preferred_element_type=F32
    )


def low_lanes(shape):
    return lax.broadcasted_iota(jnp.int32, shape, len(shape) - 1) < SPAN


def head_sum(x):
    low = low_lanes(x.shape)
    s0 = jnp.sum(jnp.where(low, x, 0.0), axis=-1, keepdims=True)
    s1 = jnp.sum(jnp.where(low, 0.0, x), axis=-1, keepdims=True)
    return jnp.where(low, s0, s1)


def two_rows(x):
    low = low_lanes(x.shape)
    return jnp.concatenate([jnp.where(low, x, 0.0), jnp.where(low, 0.0, x)], axis=0)


def fold(full):
    return jnp.where(low_lanes((SPAN, 2 * SPAN)), full[:SPAN], full[SPAN:])


def unfold(state):
    low = low_lanes(state.shape)
    return jnp.concatenate([jnp.where(low, state, 0.0), jnp.where(low, 0.0, state)], axis=0)


def running(w, upper=False):
    count = w.shape[0]
    row = lax.broadcasted_iota(jnp.int32, (count, count), 0)
    col = lax.broadcasted_iota(jnp.int32, (count, count), 1)
    keep = (col >= row) if upper else (col <= row)
    return lax.dot_general(
        jnp.where(keep, 1.0, 0.0).astype(F32),
        w,
        (((1,), (0,)), ((), ())),
        precision=HI,
        preferred_element_type=F32,
    )


def strict(count):
    row = lax.broadcasted_iota(jnp.int32, (2 * count, count), 0)
    col = lax.broadcasted_iota(jnp.int32, (2 * count, count), 1)
    row = jnp.where(row >= count, row - count, row)
    return row > col, row == col


def affinity(r, k, u, q, ks):
    count = r.shape[0]
    below, diag = strict(count)
    raw = knt(two_rows(q), ks)
    share = jnp.sum(two_rows(r * u * k), axis=-1, keepdims=True)
    return jnp.where(below, raw, jnp.where(diag, share, 0.0))


def totals_kernel(k_ref, v_ref, w_ref, out_ref):
    cum = running(w_ref[...])
    total = cum[-1:, :]
    kc = k_ref[...] * jnp.exp(total - cum)
    out_ref[0, :SPAN, :] = fold(ktn(v_ref[...], kc))
    out_ref[0, SPAN:, :] = jnp.broadcast_to(jnp.exp(total), (8, 2 * SPAN))


def group_norm(y, gain, bias):
    centred = y - head_sum(y) * (1.0 / SPAN)
    spread = head_sum(centred * centred) * (1.0 / SPAN)
    scale = lax.rsqrt(spread + GN_EPS)
    normal = centred * scale
    return normal, scale, normal * gain + bias


def forward_kernel(r_ref, k_ref, v_ref, w_ref, g_ref, s_ref, p_ref, y_ref, gated_ref):
    r, k, v, w = r_ref[...], k_ref[...], v_ref[...], w_ref[...]
    cum = running(w)
    q = r * jnp.exp(cum - w)
    ks = k * jnp.exp(-cum)
    aff = affinity(r, k, p_ref[0:1, :], q, ks)
    count = r.shape[0]
    v2 = two_rows(v)
    y = (
        knt(q, unfold(s_ref[0]))
        + knn(aff[:count], v2[:count])
        + knn(aff[count:], v2[count:])
    )
    y_ref[...] = y
    gate = g_ref[...]
    _, _, grouped = group_norm(y, p_ref[1:2, :], p_ref[2:3, :])
    gated_ref[...] = (grouped * gate * jax.nn.sigmoid(gate)).astype(BF16)


def gate_kernel(gg_ref, g_ref, y_ref, r_ref, w_ref, p_ref, gate_ref, dy_ref, out_ref):
    gated_grad, gate, y = gg_ref[...], g_ref[...], y_ref[...]
    gain = p_ref[1:2, :]
    normal, scale, grouped = group_norm(y, gain, p_ref[2:3, :])
    sig = jax.nn.sigmoid(gate)
    gate_ref[...] = (gated_grad * grouped * sig * (1.0 + gate * (1.0 - sig))).astype(BF16)
    outer = gated_grad * gate * sig
    inner = outer * gain
    dy = scale * (
        inner
        - head_sum(inner) * (1.0 / SPAN)
        - normal * (head_sum(inner * normal) * (1.0 / SPAN))
    )
    dy_ref[...] = dy
    w = w_ref[...]
    q = r_ref[...] * jnp.exp(running(w) - w)
    out_ref[0, :SPAN, :] = fold(ktn(dy, q))
    gain_grad = jnp.sum(outer * normal, axis=0, keepdims=True)
    bias_grad = jnp.sum(outer, axis=0, keepdims=True)
    out_ref[0, SPAN:, :] = jnp.concatenate(
        [gain_grad, bias_grad, jnp.zeros((6, 2 * SPAN), F32)], axis=0
    )


def backward_kernel(
    r_ref, k_ref, v_ref, w_ref, dy_ref, s_ref, gs_ref, p_ref,
    dr_ref, dk_ref, dv_ref, dd_ref, out_ref,
):
    r, k, v, w, dy = r_ref[...], k_ref[...], v_ref[...], w_ref[...], dy_ref[...]
    u = p_ref[0:1, :]
    count = r.shape[0]
    cum = running(w)
    total = cum[-1:, :]
    e_before, e_minus, e_carry = jnp.exp(cum - w), jnp.exp(-cum), jnp.exp(total - cum)
    q, ks, kc = r * e_before, k * e_minus, k * e_carry
    aff = affinity(r, k, u, q, ks)
    below, _ = strict(count)
    dy2 = two_rows(dy)
    d_aff = jnp.where(below, knt(dy2, v), 0.0)
    own = head_sum(dy * v)
    state, grad_state = s_ref[0], gs_ref[0]
    state2, grad2 = unfold(state), unfold(grad_state)
    ks2 = two_rows(ks)
    dq = knn(dy, state2) + knn(d_aff[:count], ks2[:count]) + knn(d_aff[count:], ks2[count:])
    dks = ktn(d_aff, two_rows(q))
    dkc = knn(v, grad2)
    dv_ref[...] = (ktn(aff, dy2) + knt(kc, grad2)).astype(BF16)
    dr_ref[...] = (dq * e_before + own * u * k).astype(BF16)
    dk_ref[...] = (dks * e_minus + dkc * e_carry + own * u * r).astype(BF16)
    gq, gc = q * dq, kc * dkc
    d_total = jnp.sum(gc, axis=0, keepdims=True) + jnp.exp(total) * jnp.sum(
        state * grad_state, axis=0, keepdims=True
    )
    dw = running(gq - ks * dks - gc, upper=True) - gq + d_total
    term = dw * w
    dd_ref[...] = term.astype(BF16)
    out_ref[0] = jnp.concatenate(
        [
            jnp.sum(term, axis=0, keepdims=True),
            jnp.sum(own * r * k, axis=0, keepdims=True),
            jnp.zeros((6, 2 * SPAN), F32),
        ],
        axis=0,
    )


def block_call(kernel, chunks, step, width, ins, outs, args):
    lane = 2 * SPAN
    kinds = {
        "t": pl.BlockSpec((step, lane), lambda c, h: (c, h)),
        "s": pl.BlockSpec((1, SPAN, lane), lambda c, h: (c, 0, h)),
        "x": pl.BlockSpec((1, SPAN + 8, lane), lambda c, h: (c, 0, h)),
        "e": pl.BlockSpec((1, 8, lane), lambda c, h: (c, 0, h)),
        "p": pl.BlockSpec((8, lane), lambda c, h: (0, h)),
    }
    shapes = {
        "t": lambda d: jax.ShapeDtypeStruct((chunks * step, width), d),
        "x": lambda d: jax.ShapeDtypeStruct((chunks, SPAN + 8, width), d),
        "e": lambda d: jax.ShapeDtypeStruct((chunks, 8, width), d),
    }
    return pl.pallas_call(
        kernel,
        grid=(chunks, width // lane),
        in_specs=[kinds[kind] for kind in ins],
        out_specs=[kinds[kind] for kind, _ in outs],
        out_shape=[shapes[kind](dtype) for kind, dtype in outs],
        compiler_params=pltpu.CompilerParams(vmem_limit_bytes=48 * 1024 * 1024),
    )(*args)


def weight_grad(places, pairs, block):
    tokens, blocks = pairs[0][0].shape[0], places.shape[0]
    widths = [y.shape[1] for _, y in pairs]

    def kernel(_, *refs):
        at = 0
        for i, wide in enumerate(widths):
            refs[-1][0, :, at : at + wide] = tn(refs[2 * i][...], refs[2 * i + 1][...]).astype(
                BF16
            )
            at += wide

    specs = []
    for wide in widths:
        specs.append(pl.BlockSpec((tokens, block), lambda i, at: (0, at[i])))
        specs.append(pl.BlockSpec((tokens, wide), lambda i, at: (0, 0)))
    return pl.pallas_call(
        kernel,
        grid_spec=pltpu.PrefetchScalarGridSpec(
            num_scalar_prefetch=1,
            grid=(blocks,),
            in_specs=specs,
            out_specs=pl.BlockSpec((1, block, sum(widths)), lambda i, at: (i, 0, 0)),
        ),
        out_shape=jax.ShapeDtypeStruct((blocks, block, sum(widths)), BF16),
        compiler_params=pltpu.CompilerParams(vmem_limit_bytes=48 * 1024 * 1024),
    )(places, *[v for pair in pairs for v in pair])


def lanes_kernel(spans, x_ref, out_ref):
    at = 0
    for start, stop in spans:
        out_ref[:, at : at + stop - start] = x_ref[:, start:stop].astype(out_ref.dtype)
        at += stop - start


def move_lanes(spans, value, dtype):
    return pl.pallas_call(
        functools.partial(lanes_kernel, spans),
        in_specs=[pl.BlockSpec(memory_space=pltpu.VMEM)],
        out_specs=pl.BlockSpec(memory_space=pltpu.VMEM),
        out_shape=jax.ShapeDtypeStruct(value.shape, dtype),
        compiler_params=pltpu.CompilerParams(vmem_limit_bytes=32 * 1024 * 1024),
    )(value)


def place_kernel(counts, wide, block, at_ref, *refs):
    ins, out_ref, sems = refs[: len(counts)], refs[-2], refs[-1]
    rows = out_ref.shape[0]
    copies, i = [], 0
    for ref, n in zip(ins, counts):
        for j in range(n):
            start = pl.multiple_of(at_ref[i] * block, block)
            column = i * block // rows * wide
            copy = pltpu.make_async_copy(
                ref.at[pl.ds(j * block, block), :],
                out_ref.at[pl.ds(start, block), pl.ds(column, wide)],
                sems.at[i],
            )
            copy.start()
            copies.append(copy)
            i += 1
    for copy in copies:
        copy.wait()


def place_rows(parts, block):
    pieces = [p for part in parts for p in part[1]]
    wide = pieces[0].shape[1]
    at = jnp.concatenate([part[0] for part in parts])
    counts = [p.shape[0] // block for p in pieces]
    total = sum(counts)
    return pl.pallas_call(
        functools.partial(place_kernel, counts, wide, block),
        in_specs=[pl.BlockSpec(memory_space=pltpu.SMEM)]
        + [pl.BlockSpec(memory_space=pl.ANY)] * len(pieces),
        out_specs=pl.BlockSpec(memory_space=pl.ANY),
        out_shape=jax.ShapeDtypeStruct(
            (total * block // len(parts), wide * len(parts)), pieces[0].dtype
        ),
        scratch_shapes=[pltpu.SemaphoreType.DMA((total,))],
        compiler_params=pltpu.CompilerParams(vmem_limit_bytes=32 * 1024 * 1024),
    )(at, *pieces)


def mixes_kernel(
    open_ref, x_ref, before_ref, vec_ref, down_ref, up_ref, ddown_ref,
    m1_ref, m2_ref, m3_ref, m4_ref, dh_ref,
    normal_ref, scale_ref, delta_ref, blend_ref, m0_ref, tanh_ref, dtanh_ref,
):
    piece = pl.program_id(0)
    step = m1_ref.shape[0]
    x = x_ref[...].astype(F32)
    centred = x - jnp.mean(x, axis=-1, keepdims=True)
    scale = lax.rsqrt(jnp.mean(centred * centred, axis=-1, keepdims=True) + LN_EPS)
    normal = centred * scale
    full = normal * vec_ref[0:1, :] + vec_ref[1:2, :]
    normed = full[:step]
    first = jnp.where(open_ref[piece] == 1, before_ref[0:1, :], full[step : step + 1])
    row = lax.broadcasted_iota(jnp.int32, normed.shape, 0)
    delta = jnp.where(row == 0, first, pltpu.roll(normed, 1, 0)) - normed
    blend = (normed + delta * vec_ref[2:3, :]).astype(BF16)
    tanh = jnp.tanh(nn(blend, down_ref[...]))
    latent = tanh.astype(BF16)
    lane = lax.broadcasted_iota(jnp.int32, latent.shape, 1)
    mixed = []
    for c in range(5):
        own = (lane >= c * RANK) & (lane < (c + 1) * RANK)
        offset = nt(jnp.where(own, latent, jnp.zeros_like(latent)), up_ref[...])
        mixed.append((normed + delta * (vec_ref[3 + c : 4 + c, :] + offset)).astype(BF16))
    dtanh = jnp.tanh(nn(mixed[0], ddown_ref[...]))
    m1_ref[...], m2_ref[...], m3_ref[...], m4_ref[...] = mixed[1:]
    dh_ref[...] = dtanh.astype(BF16)

    @pl.when(piece == 0)
    def _():
        normal_ref[...] = normal[:step]
        scale_ref[...] = jnp.broadcast_to(scale[:step], scale_ref.shape)
        delta_ref[...] = delta
        blend_ref[...] = blend
        m0_ref[...] = mixed[0]
        tanh_ref[...] = tanh
        dtanh_ref[...] = dtanh


def group_mixes(opening, x, before, vec, down, up, ddown, step):
    high, width = step + 16, x.shape[1]
    pieces = x.shape[0] // high

    def whole(value):
        return pl.BlockSpec(value.shape, lambda k: (0, 0))

    def own(columns, dtype):
        return (
            pl.BlockSpec((step, columns), lambda k: (0, 0)),
            jax.ShapeDtypeStruct((step, columns), dtype),
        )

    def every(columns, dtype):
        return (
            pl.BlockSpec((step, columns), lambda k: ((k % 2) * 2 + k // 2, 0)),
            jax.ShapeDtypeStruct((pieces * step, columns), dtype),
        )

    outs = [every(width, BF16)] * 4 + [
        every(DRANK, BF16),
        own(width, F32),
        own(128, F32),
        own(width, F32),
        own(width, BF16),
        own(width, BF16),
        own(5 * RANK, F32),
        own(DRANK, F32),
    ]
    return pl.pallas_call(
        mixes_kernel,
        grid=(pieces,),
        in_specs=[
            pl.BlockSpec(memory_space=pltpu.SMEM),
            pl.BlockSpec((high, width), lambda k: (k, 0)),
            whole(before),
            whole(vec),
            whole(down),
            whole(up),
            whole(ddown),
        ],
        out_specs=[o[0] for o in outs],
        out_shape=[o[1] for o in outs],
        compiler_params=pltpu.CompilerParams(vmem_limit_bytes=56 * 1024 * 1024),
    )(opening, x, before, vec, down, up, ddown)


def product(pairs, outs, body, sides=(), tile=256):
    count = len(pairs)

    def kernel(*refs):
        ins, out_refs = refs[: 2 * count + len(sides)], refs[2 * count + len(sides) :]
        products = [
            (nn if pair[2] == "nn" else nt)(ins[2 * i][...], ins[2 * i + 1][...])
            for i, pair in enumerate(pairs)
        ]
        results = body(*products, *[r[...] for r in ins[2 * count :]])
        for ref, value in zip(out_refs, results):
            ref[...] = value.astype(ref.dtype)

    specs, args = [], []
    for a, b, form, at in pairs:
        depth = a.shape[1]
        specs.append(pl.BlockSpec(a.shape, lambda j: (0, 0)))
        if form == "nn":
            specs.append(pl.BlockSpec((depth, tile), lambda j, at=at: (0, at + j)))
        else:
            specs.append(pl.BlockSpec((tile, depth), lambda j, at=at: (j, at)))
        args += [a, b]
    for side in sides:
        specs.append(pl.BlockSpec((side.shape[0], tile), lambda j: (0, j)))
    return pl.pallas_call(
        kernel,
        grid=(outs[0][1] // tile,),
        in_specs=specs,
        out_specs=[pl.BlockSpec((o[0], tile), lambda j: (0, j)) for o in outs],
        out_shape=[jax.ShapeDtypeStruct(o[:2], o[2]) for o in outs],
        compiler_params=pltpu.CompilerParams(vmem_limit_bytes=56 * 1024 * 1024),
    )(*args, *sides)


def local(fn, outs, *args, scalar=None):
    def kernel(*refs):
        lead = [] if scalar is None else [refs[0]]
        ins, out_refs = refs[len(lead) : -len(outs)], refs[-len(outs) :]
        scalars = [r[i] for r in lead for i in range(r.shape[0])]
        results = fn(*scalars, *[r[...] for r in ins])
        for ref, value in zip(out_refs, results):
            ref[...] = value.astype(ref.dtype)

    specs = [pl.BlockSpec(memory_space=pltpu.VMEM)] * len(args)
    if scalar is not None:
        specs = [pl.BlockSpec(memory_space=pltpu.SMEM)] + specs
        args = (scalar.reshape(-1), *args)
    return pl.pallas_call(
        kernel,
        in_specs=specs,
        out_specs=[pl.BlockSpec(memory_space=pltpu.VMEM)] * len(outs),
        out_shape=[jax.ShapeDtypeStruct(o[:2], o[2]) for o in outs],
        compiler_params=pltpu.CompilerParams(vmem_limit_bytes=56 * 1024 * 1024),
    )(*args)


def take_lanes(value, spans):
    if len(spans) == 1:
        return value
    return jnp.concatenate([value[:, a:b] for a, b in spans], axis=1)


def norm_back(grad, gain, normal, scale):
    e = grad * gain
    return scale * (
        e
        - jnp.mean(e, axis=-1, keepdims=True)
        - normal * jnp.mean(e * normal, axis=-1, keepdims=True)
    )


def rows_above(value, first):
    row = lax.broadcasted_iota(jnp.int32, value.shape, 0)
    return jnp.where(row == 0, first, pltpu.roll(value, 1, 0))


def rows_below(value, last):
    row = lax.broadcasted_iota(jnp.int32, value.shape, 0)
    high = value.shape[0]
    return jnp.where(row == high - 1, last, pltpu.roll(value, high - 1, 0))


def padded(rows):
    return jnp.concatenate(
        list(rows) + [jnp.zeros((8 - len(rows), rows[0].shape[1]), F32)], axis=0
    )


def column_sum(value):
    return jnp.sum(value, axis=0, keepdims=True)


def gates_kernel(
    spans, who_ref, middle_ref, value_ref, more_ref, act_ref, cot_ref,
    out_ref, up_ref, vg_ref, rg_ref, held,
):
    to_spans, from_spans = spans
    step, part = act_ref.shape[0] // 4, act_ref.shape[1]
    who = who_ref[0]
    act = [
        act_ref[pl.ds(pl.multiple_of((who ^ j) * step, step), step), :] for j in range(4)
    ]
    recept = jax.nn.sigmoid(take_lanes(jnp.concatenate(act, axis=1).astype(F32), to_spans))
    value = value_ref[...] + more_ref[...].astype(F32)
    out = middle_ref[...] + recept * value
    out_ref[...] = take_lanes(out, from_spans).astype(BF16)
    up = take_lanes(cot_ref[...].astype(F32), to_spans)
    up_ref[...] = up
    vg_ref[...] = (up * recept).astype(BF16)
    held[...] = take_lanes(up * value * recept * (1.0 - recept), from_spans)
    for k in range(4):
        at = pl.multiple_of((who ^ k) * part, part)
        rg_ref[k * step : (k + 1) * step, :] = held[:, pl.ds(at, part)].astype(BF16)


def gates(spans, who, middle, value, more, act, cot):
    step, width = middle.shape
    part = act.shape[1]
    shape = jax.ShapeDtypeStruct
    return pl.pallas_call(
        functools.partial(gates_kernel, spans),
        in_specs=[pl.BlockSpec(memory_space=pltpu.SMEM)]
        + [pl.BlockSpec(memory_space=pltpu.VMEM)] * 5,
        out_specs=[pl.BlockSpec(memory_space=pltpu.VMEM)] * 4,
        out_shape=[
            shape((step, width), BF16),
            shape((step, width), F32),
            shape((step, width), BF16),
            shape((4 * step, part), BF16),
        ],
        scratch_shapes=[pltpu.VMEM((step, width), F32)],
        compiler_params=pltpu.CompilerParams(vmem_limit_bytes=56 * 1024 * 1024),
    )(who.reshape(1), middle, value, more, act, cot)


def mixes_back_kernel(
    kept_ref, got_ref, dl_ref, dl_more_ref, delta_ref, tanh_ref, dtanh_ref, blend_ref, m0_ref,
    down_ref, up_ref, ddown_ref, vec_ref,
    rest_ref, dg_ref, row_ref, cols_ref, down_out, up_out, ddown_out,
):
    step = delta_ref.shape[0]
    dtanh = dtanh_ref[...]
    decay_grad = dl_ref[...] + dl_more_ref[...].astype(F32)
    decay_pre = (decay_grad * (1.0 - dtanh * dtanh)).astype(BF16)
    ddown_out[...] = tn(m0_ref[...], decay_pre)
    tanh = tanh_ref[...]
    latent = tanh.astype(BF16)
    lane = lax.broadcasted_iota(jnp.int32, latent.shape, 1)
    delta, up = delta_ref[...], up_ref[...]
    latent_grad = jnp.zeros(latent.shape, F32)
    up_grad = jnp.zeros(up_out.shape, F32)
    dg = jnp.zeros(delta.shape, F32)
    total = jnp.zeros(delta.shape, F32)
    cols = []
    for c in range(5):
        own = (lane >= c * RANK) & (lane < (c + 1) * RANK)
        mine = jnp.where(own, latent, jnp.zeros_like(latent))
        if c == 0:
            grad = nt(decay_pre, ddown_ref[...])
        else:
            at = slice((c - 1) * step, c * step)
            grad = kept_ref[at, :] + got_ref[at, :].astype(F32)
        shift = grad * delta
        cols.append(column_sum(shift))
        offset = shift.astype(BF16)
        latent_grad = jnp.where(own, nn(offset, up), latent_grad)
        up_grad = up_grad + tn(offset, mine)
        dg = dg + grad * (vec_ref[3 + c : 4 + c, :] + nt(mine, up))
        total = total + grad
    up_out[...] = up_grad
    mix_pre = (latent_grad * (1.0 - tanh * tanh)).astype(BF16)
    down_out[...] = tn(blend_ref[...], mix_pre)
    blend_grad = nt(mix_pre, down_ref[...])
    dg = dg + blend_grad * vec_ref[2:3, :]
    rest_ref[...] = total + blend_grad - dg
    dg_ref[...] = dg
    row_ref[...] = dg[:8]
    cols_ref[...] = padded([column_sum(blend_grad * delta)] + cols)


def mixes_back(*args):
    delta, down, ddown = args[4], args[9], args[11]
    step, width = delta.shape
    shape = jax.ShapeDtypeStruct
    outs = [
        shape((step, width), F32),
        shape((step, width), F32),
        shape((8, width), F32),
        shape((8, width), F32),
        shape(down.shape, F32),
        shape(down.shape, F32),
        shape(ddown.shape, F32),
    ]
    return pl.pallas_call(
        mixes_back_kernel,
        in_specs=[pl.BlockSpec(memory_space=pltpu.VMEM)] * len(args),
        out_specs=[pl.BlockSpec(memory_space=pltpu.VMEM)] * len(outs),
        out_shape=outs,
        compiler_params=pltpu.CompilerParams(vmem_limit_bytes=60 * 1024 * 1024),
    )(*args)


def tie(*values):
    return lax.optimization_barrier(values)


def on_device(
    count,
    tokens,
    previous,
    initial_state,
    mixing_weights,
    lowrank_weights,
    vectors,
    feedforward_weights,
    cotangent,
):
    fast = initial_state.shape[0] == 64
    masks = (1, 8) if fast else (1, 2)
    size = 1 << len(masks)
    teams = count // size
    all_masks = [1 << b for b in range(count.bit_length() - 1)]
    team_masks = [b for b in all_masks if b not in masks]
    far = 16
    team_masks.sort(key=lambda b: fast and b != far)
    me = lax.axis_index("seq")
    _, step, width = tokens.shape
    rows = mixing_weights.shape[0]
    part = width // size
    ff_part = FF // size
    team_rows = rows * size
    def bit_of(who, mask):
        return (who // mask) % 2 if isinstance(who, int) else lax.rem(lax.div(who, mask), 2)

    def member_of(who):
        return sum(bit_of(who, b) << j for j, b in enumerate(masks))

    def team_of(who):
        return sum(bit_of(who, b) << j for j, b in enumerate(team_masks))

    member, team = member_of(me), team_of(me)
    order = sorted(range(count), key=lambda d: (team_of(d), member_of(d)))
    inverse = sorted(range(count), key=lambda p: order[p])
    across = [order[m::size] for m in range(size)]
    square = [order[m :: 2 * size] for m in range(2 * size)]
    def lane_spans(blocks):
        spans = []
        for d in blocks:
            if spans and spans[-1][1] == d * rows:
                spans[-1][1] = (d + 1) * rows
            else:
                spans.append([d * rows, (d + 1) * rows])
        return spans

    to_spans, from_spans = lane_spans(order), lane_spans(inverse)

    def to_places(value, dtype):
        return move_lanes(to_spans, value, dtype)

    def flips(k):
        return sum(b for j, b in enumerate(masks) if (k >> j) & 1)

    def trade(value, mask):
        return lax.ppermute(value, "seq", [(d, d ^ mask) for d in range(count)])

    def group_gather(value):
        side = trade(value, masks[1])
        return value, side, trade(jnp.concatenate([value, side], axis=0), masks[0])

    def group_rows(value):
        high, columns = value.shape

        def lay(own, side, far):
            return (jnp.concatenate([own, far[:high], side, far[high:]], axis=0),)

        return local(lay, [(size * high, columns, value.dtype)], *group_gather(value))[0]

    def halves(value):
        cut = [value[k * step : (k + 1) * step] for k in range(size)]
        return [cut[0], cut[2]], [cut[1], cut[3]]

    def group_fold(kept, sent):
        high, columns = kept.shape[0] // 2, kept.shape[1]
        got = trade(sent, masks[0])

        def add(mine, more):
            total = mine + more.astype(F32)
            return total[:high], total[high:]

        return local(add, [(high, columns, F32), (high, columns, BF16)], kept, got)

    def group_sum(kept, sent):
        mine, side = group_fold(kept, sent)
        return mine, trade(side, masks[1])

    def crossing_sum(*pairs):
        units = len(pairs)

        def body(*products):
            parts = [halves(p) for p in products]
            kept = [p[0][i] for i in range(2) for p in parts]
            sent = [p[1][i] for i in range(2) for p in parts]
            return jnp.concatenate(kept, axis=0), jnp.concatenate(sent, axis=0)

        high = 2 * units * step
        return product(
            [(a, b, "nt", at) for a, b, at in pairs],
            [(high, width, F32), (high, width, BF16)],
            body,
            tile=512,
        )

    def exchange(pieces):
        pieces, high = list(pieces), pieces[0].shape[0]
        for j in reversed(range(len(masks))):
            keys = [k for k in range(size) if (k >> j) & 1]
            got = trade(jnp.concatenate([pieces[k] for k in keys], axis=0), masks[j])
            for i, k in enumerate(keys):
                pieces[k] = got[i * high : (i + 1) * high]
        return pieces

    def ordered(pieces):
        pieces = list(pieces)
        for j in range(len(masks)):
            swap = lax.rem(lax.div(member, 1 << j), 2) == 1
            pieces = [
                jnp.where(swap, pieces[k ^ (1 << j)], pieces[k]) for k in range(len(pieces))
            ]
        return pieces

    def neighbour(value, offset):
        pairs = [(d, d + offset) for d in range(count) if 0 <= d + offset < count]
        return lax.ppermute(value, "seq", pairs)

    def take_columns(value, spans, who):
        return jnp.concatenate(
            [
                lax.dynamic_slice_in_dim(value, start + who * wide, wide, axis=1)
                for start, wide in spans
            ],
            axis=1,
        )

    def group_columns(value, spans):
        pieces = [take_columns(value, spans, member ^ k) for k in range(size)]
        return jnp.concatenate(ordered(exchange(pieces)), axis=0)

    def crossing(first):
        bits = list(range(1, len(team_masks))) + [0]
        if first:
            bits[0], bits[1] = bits[1], bits[0]
        return bits

    def gather_rows(own):
        return lax.all_gather(own, "seq", axis=0, tiled=True, axis_index_groups=across)

    def far_send(own):
        return trade(own, far) if fast else own

    def far_join(own, got):
        if not fast:
            return own
        upper = bit_of(me, far) == 1
        return jnp.concatenate(
            [jnp.where(upper, got, own), jnp.where(upper, own, got)], axis=0
        )

    def gather_square(paired):
        groups = square if fast else across
        return lax.all_gather(paired, "seq", axis=0, tiled=True, axis_index_groups=groups)

    def team_products(*pairs):
        if fast:
            places = jnp.arange(teams, dtype=jnp.int32)
            return weight_grad(places, pairs, team_rows).reshape(width, -1)
        return jnp.concatenate([tn(x, y).astype(BF16) for x, y in pairs], axis=1)

    def square_sum(grads):
        groups = square if fast else across
        return lax.psum_scatter(
            grads, "seq", scatter_dimension=0, tiled=True, axis_index_groups=groups
        )

    def far_split(pair):
        if not fast:
            return pair, jnp.zeros_like(pair)
        bit = bit_of(me, far)
        sent = lax.dynamic_slice_in_dim(pair, (1 - bit) * team_rows, team_rows, axis=0)
        kept = lax.dynamic_slice_in_dim(pair, bit * team_rows, team_rows, axis=0)
        return kept, trade(sent, far)

    def far_add(kept, got):
        return (kept.astype(F32) + got.astype(F32)).astype(BF16)

    def cube_gather(value, leader=None):
        for mask in reversed(all_masks):
            got = trade(value, mask)
            upper = bit_of(me, mask) == 1
            value = jnp.stack([jnp.where(upper, got, value), jnp.where(upper, value, got)])
            if mask == 4 and leader is not None:
                value, leader = tie(value, leader)
        axes = len(all_masks)
        cube = value.transpose(*reversed(range(axes)), *range(axes, value.ndim))
        return cube if leader is None else (cube, leader)

    place_axes = [all_masks[::-1].index(b) for b in team_masks[::-1] + list(masks[::-1])]

    def by_place(cube):
        rest = range(len(all_masks), cube.ndim)
        return cube.transpose(*place_axes, *rest).reshape(width, -1)

    def to_cube(value):
        cube = value.reshape(*[2] * len(place_axes), rows, -1)
        back = [place_axes.index(a) for a in range(len(place_axes))]
        return cube.transpose(*back, len(back), len(back) + 1)

    def cube_sum(cube, kind, follower):
        for axis, mask in reversed(list(enumerate(reversed(all_masks)))):
            bit = bit_of(me, mask)
            sent = lax.dynamic_index_in_dim(cube, 1 - bit, axis, keepdims=False)
            kept = lax.dynamic_index_in_dim(cube, bit, axis, keepdims=False)
            cube = kept.astype(F32) + trade(sent.astype(kind), mask).astype(F32)
            if mask == 2:
                cube, follower = tie(cube, follower)
        return cube, follower

    def hand_rows(pieces, extra=None):
        widths = [sum(p.shape[1] for p in piece) for piece in pieces]
        joint = jnp.concatenate([p for piece in pieces for p in piece], axis=1)
        mine = [
            lax.dynamic_slice_in_dim(joint, (member ^ k) * rows, rows, axis=0)
            for k in range(size)
        ]
        if extra is not None:
            mine = [jnp.concatenate([m, e], axis=1) for m, e in zip(mine, extra)]
        by_place = exchange(mine)
        by_member = ordered(by_place)
        outs, start = [], 0
        for wide in widths:
            outs += [p[:, start : start + wide] for p in by_member]
            start += wide
        joined = jnp.concatenate(outs, axis=1).astype(F32)
        if extra is None:
            return joined
        return joined, [p[:, start:].astype(F32) for p in by_place]

    up_start, decay_start, decay_up = 5 * RANK, 10 * RANK, 10 * RANK + DRANK
    last_row = neighbour(tokens[0, -1:, :], 1)
    tokens_sent = to_places(
        jnp.concatenate([tokens[0], jnp.broadcast_to(last_row, (16, width))], axis=0), BF16
    )
    natural = cube_gather(
        jnp.concatenate(
            [vectors, initial_state, lowrank_weights[:, decay_up:].astype(F32)], axis=1
        )
    ).reshape(width, -1)
    tokens_all = jnp.concatenate(group_gather(tokens_sent), axis=0)
    mix_local = group_columns(mixing_weights, [(c * width, part) for c in range(5)])
    mix_kv, mix_rest = mix_local[:, : 2 * part], mix_local[:, 2 * part :]
    low_cube, kv_got = cube_gather(lowrank_weights[:, :decay_up], far_send(mix_kv))
    mix_rest, natural, low_cube, tokens_all = tie(mix_rest, natural, low_cube, tokens_all)
    lowrank = by_place(low_cube)
    w_kv = gather_square(far_join(mix_kv, kv_got))
    tiles = part // 256

    mine = lax.dynamic_slice_in_dim(natural, member * part, part, axis=0)
    vec_part = mine[:, :16].T
    first_state = mine[:, 16 : 16 + SPAN].T
    w_dup = mine[:, 16 + SPAN :].astype(BF16)
    vec = by_place(
        natural[:, :16].reshape(*[2] * len(all_masks), rows, 16)
    ).T
    wkv_rows = jnp.concatenate([vec_part[9:12], jnp.zeros((5, part), F32)], axis=0)
    is_first = (me == 0).astype(jnp.int32)
    before = to_places(previous.reshape(2, width), F32)
    w_down, w_up = lowrank[:, :up_start], lowrank[:, up_start:decay_start]
    w_ddown = lowrank[:, decay_start:]

    opening = jnp.stack(
        [jnp.bitwise_xor(me, flips(k)) == 0 for k in (0, 2, 1, 3)]
    ).astype(jnp.int32)
    (
        *mixed_all, dh_all, normal_one, scale_one, delta, blend, mixed_zero, mix_tanh, decay_tanh,
    ) = group_mixes(opening, tokens_all, before, vec, w_down, w_up, w_ddown, step)
    rest_got, mixed_all[0], feed_in = tie(far_send(mix_rest), mixed_all[0], feedforward_weights)
    w_rest = gather_square(far_join(mix_rest, rest_got))
    ff_spans = [(0, ff_part), (FF, part), (FF + width, ff_part)]
    ff_local = group_columns(feed_in, ff_spans)
    everyone = size * step
    (log_decay,) = product(
        [(dh_all, w_dup, "nt", 0)],
        [(everyone, part, F32)],
        lambda acc, base: (-jnp.exp(base + acc),),
        sides=(vec_part[8:9],),
    )
    keys, values = product(
        [(mixed_all[0], w_kv, "nn", 0), (mixed_all[1], w_kv, "nn", tiles)],
        [(everyone, part, F32)] * 2,
        lambda a, b: (a, b),
    )

    keys, ff_local = tie(keys, ff_local)
    ff_tail = ff_local[:, ff_part + part :]
    ff_near = ff_local[:, : ff_part + part]
    near_got = far_send(ff_near)

    call = functools.partial(block_call, chunks=size, step=step, width=part)
    (totals,) = call(
        totals_kernel, ins="ttt", outs=[("x", F32)], args=(keys, values, log_decay)
    )
    stages, current = [], [None, []]
    for mask in all_masks:
        if mask in masks:
            current[1].append(1 << masks.index(mask))
        else:
            stages.append(current)
            current = [mask, []]
    stages.append(current)
    high, long = SPAN + 8, SPAN + 16

    def chain(early, late):
        return early[0] * late[0], late[0] * early[1] + late[1]

    def pick(flag, yes, no):
        return tuple(jnp.where(flag, a, b) for a, b in zip(yes, no))

    def rows8(row):
        return jnp.broadcast_to(row, (8, part))

    def pack(items):
        return jnp.concatenate([r for d, v in items for r in (v, rows8(d))], axis=0)

    def unpack(array, count):
        cut = [array[i * high : (i + 1) * high] for i in range(count)]
        return [(c[SPAN : SPAN + 1], c[:SPAN]) for c in cut]

    def swap_members(who, pieces):
        pieces = list(pieces)
        for j in range(len(masks)):
            flag = (who // (1 << j)) % 2 == 1
            pieces = [jnp.where(flag, pieces[k ^ (1 << j)], pieces[k]) for k in range(size)]
        return pieces

    def neutral():
        return jnp.ones((1, part), F32), jnp.zeros((SPAN, part), F32)

    def flags_of(mask):
        bit = jnp.int32(0) if mask is None else bit_of(me, mask)
        return jnp.stack([member, bit]).astype(jnp.int32)

    keys_at, decays = list(range(size)), []
    open_bits = size - 1
    stage_arrays = [totals.reshape(size * high, part)]
    for index, (mask, merges) in enumerate(stages):
        last = index + 1 == len(stages)
        after_keys = keys_at
        for bit in merges:
            after_keys = [g for g in after_keys if not g & bit]

        def forward_stage(
            who, late, *arrays, mask=mask, merges=merges, groups=keys_at, bits=open_bits, last=last
        ):
            marks = []
            if mask is None:
                cut = [arrays[0][k * high : (k + 1) * high] for k in range(size)]
                total = {
                    m: (p[SPAN : SPAN + 1], p[:SPAN])
                    for m, p in enumerate(swap_members(who, cut))
                }
                chunks = [neutral() for _ in range(size)]
            else:
                total = dict(zip(groups, unpack(arrays[0], len(groups))))
                chunks = unpack(arrays[1], size)
                other = {}
                for i, g in enumerate(groups):
                    got = arrays[2][i * long : (i + 1) * long].astype(F32)
                    other[g] = got[SPAN : SPAN + 1] + got[SPAN + 8 : SPAN + 9], got[:SPAN]
                marks += [total[g][0] for g in groups] + [other[g][0] for g in groups]
                late = late == 1
                chunks = [
                    pick(late, chain(other[m & bits], c), c) for m, c in enumerate(chunks)
                ]
                total = {
                    g: pick(late, chain(other[g], total[g]), chain(total[g], other[g]))
                    for g in groups
                }
            for bit in merges:
                marks += [total[g][0] for g in total]
                chunks = [
                    chain(total[(m & bits) ^ bit], c) if m & bit else c
                    for m, c in enumerate(chunks)
                ]
                total = {g: chain(total[g], total[g | bit]) for g in total if not g & bit}
                bits ^= bit
            marks = jnp.concatenate([rows8(r) for r in marks], axis=0)
            if last:
                states = [d * arrays[-1] + v for d, v in chunks]
                return jnp.concatenate(swap_members(who, states), axis=0), marks
            sent = []
            for d, v in total.values():
                first = d.astype(BF16)
                rest = (d - first.astype(F32)).astype(BF16)
                sent += [v.astype(BF16), rows8(first), rows8(rest)]
            return (
                pack(list(total.values())), pack(chunks), jnp.concatenate(sent, axis=0), marks
            )

        count_marks = (0 if mask is None else 2 * len(keys_at)) + sum(
            len(keys_at) >> i for i in range(len(merges))
        )
        marks_out = (8 * count_marks, part, F32)
        if last:
            outs = [(size * SPAN, part, F32), marks_out]
            state_in, marks = local(
                forward_stage, outs, *stage_arrays, first_state, scalar=flags_of(mask)
            )
            state_in = state_in.reshape(size, SPAN, part)
        else:
            outs = [
                (len(after_keys) * high, part, F32),
                (size * high, part, F32),
                (len(after_keys) * long, part, BF16),
                marks_out,
            ]
            total, chunks, sent, marks = local(
                forward_stage, outs, *stage_arrays, scalar=flags_of(mask)
            )
            if mask == (2 if fast else 4):
                sent, near_got = tie(sent, near_got)
            stage_arrays = [total, chunks, trade(sent, stages[index + 1][0])]
        decays.append(marks)
        keys_at = after_keys
        for bit in merges:
            open_bits ^= bit
    w_near = gather_square(far_join(ff_near, near_got))
    w_key, w_rec = w_near, w_near[:, ff_part:]
    state_in, ff_tail = tie(state_in, ff_tail)
    val_got = far_send(ff_tail)

    receipt, gate_pre = product(
        [(mixed_all[2], w_rest, "nn", 0), (mixed_all[3], w_rest, "nn", tiles)],
        [(everyone, part, F32)] * 2,
        lambda a, b: (a, b),
    )
    wkv, gated = call(
        forward_kernel,
        ins="tttttsp",
        outs=[("t", F32), ("t", BF16)],
        args=(receipt, keys, values, log_decay, gate_pre, state_in, wkv_rows),
    )
    gated, val_got = tie(gated, val_got)
    w_val = gather_square(far_join(ff_tail, val_got))
    branch, branch_more = group_sum(*crossing_sum((gated, w_rest, 2)))

    def norm_two(hidden, mine, more, vec):
        middle = hidden[:step].astype(F32) + mine + more.astype(F32)
        centred = middle - jnp.mean(middle, axis=-1, keepdims=True)
        scale = lax.rsqrt(jnp.mean(centred * centred, axis=-1, keepdims=True) + LN_EPS)
        normal = centred * scale
        tail = normal[step - 8 :] * vec[12:13] + vec[13:14]
        return middle, normal, jnp.broadcast_to(scale, (step, 128)), tail

    whole = (step, width, F32)
    middle, normal_two, scale_two, tail_two = local(
        norm_two,
        [whole, whole, (step, 128, F32), (8, width, F32)],
        tokens_sent,
        branch,
        branch_more,
        vec,
    )

    def mix_two(first, normal, arrived, before, vec):
        normed = normal * vec[12:13] + vec[13:14]
        above = jnp.where(first == 1, before[1:2], arrived[7:8])
        delta = rows_above(normed, above) - normed
        key_in, recv_in = normed + delta * vec[14:15], normed + delta * vec[15:16]
        return jnp.concatenate([key_in, recv_in], axis=0), delta

    both, delta_two = local(
        mix_two,
        [(2 * step, width, BF16), whole],
        normal_two,
        neighbour(tail_two, 1),
        before,
        vec,
        scalar=is_first,
    )

    key_all, recv_all = group_rows(both[:step]), group_rows(both[step:])
    relu, squared = product(
        [(key_all, w_key, "nn", 0)],
        [(everyone, ff_part, F32), (everyone, ff_part, BF16)],
        lambda acc: (jnp.maximum(acc, 0.0), jnp.square(jnp.maximum(acc, 0.0))),
        tile=ff_part // 2,
    )
    (recept_act,) = product(
        [(recv_all, w_rec, "nn", 0)],
        [(everyone, part, BF16)],
        lambda acc: (acc,),
    )
    squared, recept_act = tie(squared, recept_act)
    acts = exchange([recept_act[k * step : (k + 1) * step] for k in range(size)])
    value, value_more = group_sum(*crossing_sum((squared, w_val, 0)))
    block_output, upstream, value_grad, recept_grads = gates(
        (to_spans, from_spans),
        member,
        middle,
        value,
        value_more,
        jnp.concatenate(acts, axis=0),
        cotangent.reshape(step, width),
    )

    rg_all = jnp.concatenate(
        exchange([recept_grads[k * step : (k + 1) * step] for k in range(size)]), axis=0
    )
    vg_all = group_rows(value_grad)
    val_grads = team_products((vg_all, squared))
    vg_all, val_grads, rg_all = tie(vg_all, val_grads, rg_all)
    val_pair = square_sum(val_grads)
    (key_grad,) = product(
        [(vg_all, w_val, "nn", 0)],
        [(everyone, ff_part, BF16)],
        lambda acc, relu: (acc * (2.0 * relu),),
        sides=(relu,),
        tile=ff_part // 2,
    )
    key_grads = team_products((key_all, key_grad))
    key_grad, key_grads = tie(key_grad, key_grads)
    key_pair = square_sum(key_grads)
    recv_two = group_sum(*crossing_sum((rg_all, w_rec, 0)))
    key_two = group_sum(*crossing_sum((key_grad, w_key, 0)))

    def inputs_back(key, key_more, recv, recv_more, vec):
        key, recv = key + key_more.astype(F32), recv + recv_more.astype(F32)
        top = key[:8] * vec[14:15] + recv[:8] * vec[15:16]
        return jnp.concatenate([key, recv], axis=0), top

    in_grads, top_two = local(
        inputs_back, [(2 * step, width, F32), (8, width, F32)], *key_two, *recv_two, vec
    )
    last_flag = (me == count - 1).astype(jnp.int32)

    def norm_two_back(last, grads, arrived, upstream, normal, scale, delta, vec):
        key_grad, recv_grad = grads[:step], grads[step:]
        shifted = key_grad * vec[14:15] + recv_grad * vec[15:16]
        below = jnp.where(last == 1, jnp.zeros_like(arrived[:1]), arrived[:1])
        grad = (
            key_grad * (1.0 - vec[14:15])
            + recv_grad * (1.0 - vec[15:16])
            + rows_below(shifted, below)
        )
        out = upstream + norm_back(grad, vec[12:13], normal, scale[:, :1])
        cols = padded(
            [
                column_sum(grad * normal),
                column_sum(grad),
                column_sum(key_grad * delta),
                column_sum(recv_grad * delta),
            ]
        )
        return out, out, cols

    middle_grad, branch_grad, cols_two = local(
        norm_two_back,
        [whole, (step, width, BF16), (8, width, F32)],
        in_grads,
        neighbour(top_two, -1),
        upstream,
        normal_two,
        scale_two,
        delta_two,
        vec,
        scalar=last_flag,
    )

    bg_all = group_rows(branch_grad)
    (gated_grad,) = product(
        [(bg_all, w_rest, "nn", 2 * tiles)], [(everyone, part, F32)], lambda acc: (acc,)
    )
    gate_grad, wkv_grad, ends = call(
        gate_kernel,
        ins="tttttp",
        outs=[("t", BF16), ("t", F32), ("x", F32)],
        args=(gated_grad, gate_pre, wkv, receipt, log_decay, wkv_rows),
    )
    val_kept, val_got = far_split(val_pair)
    keys_at, open_bits = list(range(size)), size - 1
    stage_arrays = [ends.reshape(size * high, part)]
    for index, (mask, merges) in enumerate(stages):
        last = index + 1 == len(stages)
        after_keys = keys_at
        for bit in merges:
            after_keys = [g for g in after_keys if not g & bit]

        def backward_stage(
            who, late, *arrays, mask=mask, merges=merges, groups=keys_at, bits=open_bits, last=last
        ):
            marks = [arrays[-1][i * 8 : i * 8 + 1] for i in range(arrays[-1].shape[0] // 8)]
            if mask is None:
                cut = [arrays[0][k * high : k * high + SPAN] for k in range(size)]
                total = dict(enumerate(swap_members(who, cut)))
                chunks = [neutral() for _ in range(size)]
            else:
                total = {g: arrays[0][i * SPAN : (i + 1) * SPAN] for i, g in enumerate(groups)}
                chunks = unpack(arrays[1], size)
                other = {
                    g: arrays[2][i * SPAN : (i + 1) * SPAN].astype(F32)
                    for i, g in enumerate(groups)
                }
                here = dict(zip(groups, marks))
                there = dict(zip(groups, marks[len(groups) :]))
                marks = marks[2 * len(groups) :]
                early = late == 0
                chunks = [
                    pick(
                        early,
                        (d * there[m & bits], d * other[m & bits] + v),
                        (d, v),
                    )
                    for m, (d, v) in enumerate(chunks)
                ]
                total = {
                    g: jnp.where(
                        early,
                        total[g] + here[g] * other[g],
                        other[g] + there[g] * total[g],
                    )
                    for g in groups
                }
            for bit in merges:
                here = dict(zip(total, marks))
                marks = marks[len(total) :]
                chunks = [
                    (d, v)
                    if m & bit
                    else (d * here[(m & bits) | bit], d * total[(m & bits) | bit] + v)
                    for m, (d, v) in enumerate(chunks)
                ]
                total = {
                    g: total[g] + here[g] * total[g | bit] for g in total if not g & bit
                }
                bits ^= bit
            joint = jnp.concatenate(list(total.values()), axis=0)
            if last:
                grads = swap_members(who, [v for _, v in chunks])
                return jnp.concatenate(grads, axis=0), joint.T
            return joint, pack(chunks), joint

        if last:
            outs = [(size * SPAN, part, F32), (part, SPAN, F32)]
            grad_out, first_grad = local(
                backward_stage, outs, *stage_arrays, decays[index], scalar=flags_of(mask)
            )
            grad_out = grad_out.reshape(size, SPAN, part)
        else:
            outs = [
                (len(after_keys) * SPAN, part, F32),
                (size * high, part, F32),
                (len(after_keys) * SPAN, part, BF16),
            ]
            total, chunks, sent = local(
                backward_stage, outs, *stage_arrays, decays[index], scalar=flags_of(mask)
            )
            if mask == (2 if fast else 4):
                sent, val_got = tie(sent, val_got)
            stage_arrays = [total, chunks, trade(sent, stages[index + 1][0])]
        keys_at = after_keys
        for bit in merges:
            open_bits ^= bit
    out_grads = team_products((bg_all, gated), (recv_all, rg_all), (mixed_all[3], gate_grad))
    grad_out, out_grads = tie(grad_out, out_grads)
    out_pair = square_sum(out_grads)

    d_receipt, d_keys, d_values, d_decay, extra = call(
        backward_kernel,
        ins="tttttssp",
        outs=[("t", BF16)] * 4 + [("e", F32)],
        args=(receipt, keys, values, log_decay, wkv_grad, state_in, grad_out, wkv_rows),
    )
    grads = [d_keys, d_values, d_receipt, gate_grad]
    kept, sent = crossing_sum(
        *[(grads[c], w_rest if c > 1 else w_kv, c % 2) for c in range(4)]
    )
    main_grads = team_products(
        (mixed_all[0], d_keys), (mixed_all[1], d_values), (mixed_all[2], d_receipt)
    )

    def latent_back(grad, up):
        kept, sent = halves(nn(grad, up))
        return jnp.concatenate(kept, axis=0), jnp.concatenate(sent, axis=0)

    latent_mine, latent_more = group_sum(
        *local(
            latent_back, [(2 * step, DRANK, F32), (2 * step, DRANK, BF16)], d_decay, w_dup
        )
    )
    key_kept, key_got = far_split(key_pair)
    sent, main_grads, latent_more, key_got = tie(sent, main_grads, latent_more, key_got)
    main_pair = square_sum(main_grads)
    mixed_mine, mixed_more = group_sum(kept, sent)
    mixed_more, out_pair = tie(mixed_more, out_pair)
    out_kept, out_got = far_split(out_pair)
    val_sum, key_sum = far_add(val_kept, val_got), far_add(key_kept, key_got)
    rest_grad, delta_grad, top_one, cols_mix, down_grad, up_grad, ddown_grad = mixes_back(
        mixed_mine,
        mixed_more,
        latent_mine,
        latent_more,
        delta,
        mix_tanh,
        decay_tanh,
        blend,
        mixed_zero,
        w_down,
        w_up,
        w_ddown,
        vec,
    )
    rest_grad, main_pair, out_got = tie(rest_grad, main_pair, out_got)
    out_sum = far_add(out_kept, out_got)

    def norm_one_back(last, rest, shifted, arrived, normal, scale, middle, vec):
        below = jnp.where(last == 1, jnp.zeros_like(arrived[:1]), arrived[:1])
        grad = rest + rows_below(shifted, below)
        out = middle + norm_back(grad, vec[0:1], normal, scale[:, :1])
        cols = padded([column_sum(grad * normal), column_sum(grad)])
        return take_lanes(out, from_spans), cols

    block_input_gradient, cols_one = local(
        norm_one_back,
        [whole, (8, width, F32)],
        rest_grad,
        delta_grad,
        neighbour(top_one, -1),
        normal_one,
        scale_one,
        middle_grad,
        vec,
        scalar=last_flag,
    )
    main_kept, main_got = far_split(main_pair)


    def spread(value):
        zero = jnp.zeros((width, value.shape[1]), F32)
        return lax.dynamic_update_slice_in_dim(zero, value, member * part, axis=0)

    vec_low = jnp.concatenate([cols_one[:2], cols_mix[:6], cols_two[:4]], axis=0)
    vec_head = jnp.concatenate(
        [jnp.sum(extra[:, :2], axis=0), jnp.sum(ends[:, SPAN : SPAN + 2], axis=0)], axis=0
    )
    by_feature = jnp.concatenate([down_grad, up_grad, ddown_grad, vec_low.T], axis=1)
    by_channel = spread(jnp.concatenate([tn(d_decay, dh_all), vec_head.T], axis=1))
    low, main_got = cube_sum(
        jnp.concatenate(
            [to_cube(by_feature), by_channel.reshape(*[2] * len(all_masks), rows, -1)], axis=-1
        ),
        BF16,
        main_got,
    )
    val_sum, main_got = tie(val_sum, main_got)
    main_sum = far_add(main_kept, main_got)

    def column_parts(value):
        return [value[:, c * part : (c + 1) * part] for c in range(3)]

    out_cols, main_cols = column_parts(out_sum), column_parts(main_sum)
    holder = lax.div(me * rows, part)

    def rows_of(who):
        mine = lax.dynamic_slice_in_dim(first_grad, lax.rem(who * rows, part), rows, axis=0)
        high = lax.reduce_precision(mine, 8, 7)
        return jnp.concatenate([high, mine - high], axis=1).astype(BF16)

    feedforward_gradient, handed = hand_rows(
        [[key_sum], [out_cols[1]], [val_sum]],
        [rows_of(jnp.bitwise_xor(me, flips(k))) for k in range(size)],
    )
    state_rows = handed[0]
    for k in range(1, size):
        state_rows = jnp.where(holder == (member ^ k), handed[k], state_rows)
    initial_state_gradient = state_rows[:, :SPAN] + state_rows[:, SPAN:]
    mixing_gradient = hand_rows([[m] for m in main_cols] + [[out_cols[2]], [out_cols[0]]])

    vec_at = decay_up + 12
    lowrank_gradient = jnp.concatenate(
        [low[:, :decay_up], low[:, vec_at : vec_at + DRANK]], axis=1
    )
    vectors_gradient = jnp.concatenate(
        [low[:, decay_up : decay_up + 8], low[:, vec_at + DRANK :], low[:, decay_up + 8 : vec_at]],
        axis=1,
    )
    return (
        block_output.reshape(1, step, width),
        block_input_gradient.reshape(1, step, width),
        initial_state_gradient,
        mixing_gradient,
        lowrank_gradient,
        vectors_gradient,
        feedforward_gradient,
    )


def solution(mesh):
    rowwise = P("seq", None)
    tokenwise = P(None, "seq", None)
    return jax.shard_map(
        functools.partial(on_device, mesh.shape["seq"]),
        mesh=mesh,
        in_specs=(tokenwise, P(), rowwise, rowwise, rowwise, rowwise, rowwise, tokenwise),
        out_specs=(tokenwise, tokenwise, rowwise, rowwise, rowwise, rowwise, rowwise),
        check_vma=False,
    )
```

```python
import functools

import jax
import jax.numpy as jnp
from jax import lax
from jax.experimental import pallas as pl
from jax.experimental.pallas import tpu as pltpu
from jax.sharding import PartitionSpec as P

HEADS = 32
SPAN = 64
FF = 7168
RANK = 32
DRANK = 64
LN_EPS = 1e-05
GN_EPS = 0.00064

F32 = jnp.float32
BF16 = jnp.bfloat16
HI = lax.Precision.HIGHEST


def nn(a, b):
    return jnp.dot(a, b, preferred_element_type=F32)


def nt(a, b):
    return lax.dot_general(a, b, (((1,), (1,)), ((), ())), preferred_element_type=F32)


def tn(a, b):
    return lax.dot_general(a, b, (((0,), (0,)), ((), ())), preferred_element_type=F32)


def knn(a, b):
    return lax.dot_general(
        a, b, (((1,), (0,)), ((), ())), preferred_element_type=F32
    )


def knt(a, b):
    return lax.dot_general(
        a, b, (((1,), (1,)), ((), ())), preferred_element_type=F32
    )


def ktn(a, b):
    return lax.dot_general(
        a, b, (((0,), (0,)), ((), ())), preferred_element_type=F32
    )


def low_lanes(shape):
    return lax.broadcasted_iota(jnp.int32, shape, len(shape) - 1) < SPAN


def head_sum(x):
    low = low_lanes(x.shape)
    s0 = jnp.sum(jnp.where(low, x, 0.0), axis=-1, keepdims=True)
    s1 = jnp.sum(jnp.where(low, 0.0, x), axis=-1, keepdims=True)
    return jnp.where(low, s0, s1)


def two_rows(x):
    low = low_lanes(x.shape)
    return jnp.concatenate([jnp.where(low, x, 0.0), jnp.where(low, 0.0, x)], axis=0)


def fold(full):
    return jnp.where(low_lanes((SPAN, 2 * SPAN)), full[:SPAN], full[SPAN:])


def unfold(state):
    low = low_lanes(state.shape)
    return jnp.concatenate([jnp.where(low, state, 0.0), jnp.where(low, 0.0, state)], axis=0)


def running(w, upper=False):
    count = w.shape[0]
    row = lax.broadcasted_iota(jnp.int32, (count, count), 0)
    col = lax.broadcasted_iota(jnp.int32, (count, count), 1)
    keep = (col >= row) if upper else (col <= row)
    return lax.dot_general(
        jnp.where(keep, 1.0, 0.0).astype(F32),
        w,
        (((1,), (0,)), ((), ())),
        precision=HI,
        preferred_element_type=F32,
    )


def strict(count):
    row = lax.broadcasted_iota(jnp.int32, (2 * count, count), 0)
    col = lax.broadcasted_iota(jnp.int32, (2 * count, count), 1)
    row = jnp.where(row >= count, row - count, row)
    return row > col, row == col


def affinity(r, k, u, q, ks):
    count = r.shape[0]
    below, diag = strict(count)
    raw = knt(two_rows(q), ks)
    share = jnp.sum(two_rows(r * u * k), axis=-1, keepdims=True)
    return jnp.where(below, raw, jnp.where(diag, share, 0.0))


def totals_kernel(k_ref, v_ref, w_ref, out_ref):
    cum = running(w_ref[...])
    total = cum[-1:, :]
    kc = k_ref[...] * jnp.exp(total - cum)
    out_ref[0, :SPAN, :] = fold(ktn(v_ref[...], kc))
    out_ref[0, SPAN:, :] = jnp.broadcast_to(jnp.exp(total), (8, 2 * SPAN))


def group_norm(y, gain, bias):
    centred = y - head_sum(y) * (1.0 / SPAN)
    spread = head_sum(centred * centred) * (1.0 / SPAN)
    scale = lax.rsqrt(spread + GN_EPS)
    normal = centred * scale
    return normal, scale, normal * gain + bias


def forward_kernel(r_ref, k_ref, v_ref, w_ref, g_ref, s_ref, p_ref, y_ref, gated_ref):
    r, k, v, w = r_ref[...], k_ref[...], v_ref[...], w_ref[...]
    cum = running(w)
    q = r * jnp.exp(cum - w)
    ks = k * jnp.exp(-cum)
    aff = affinity(r, k, p_ref[0:1, :], q, ks)
    count = r.shape[0]
    v2 = two_rows(v)
    y = (
        knt(q, unfold(s_ref[0]))
        + knn(aff[:count], v2[:count])
        + knn(aff[count:], v2[count:])
    )
    y_ref[...] = y
    gate = g_ref[...]
    _, _, grouped = group_norm(y, p_ref[1:2, :], p_ref[2:3, :])
    gated_ref[...] = (grouped * gate * jax.nn.sigmoid(gate)).astype(BF16)


def gate_kernel(gg_ref, g_ref, y_ref, r_ref, w_ref, p_ref, gate_ref, dy_ref, out_ref):
    gated_grad, gate, y = gg_ref[...], g_ref[...], y_ref[...]
    gain = p_ref[1:2, :]
    normal, scale, grouped = group_norm(y, gain, p_ref[2:3, :])
    sig = jax.nn.sigmoid(gate)
    gate_ref[...] = (gated_grad * grouped * sig * (1.0 + gate * (1.0 - sig))).astype(BF16)
    outer = gated_grad * gate * sig
    inner = outer * gain
    dy = scale * (
        inner
        - head_sum(inner) * (1.0 / SPAN)
        - normal * (head_sum(inner * normal) * (1.0 / SPAN))
    )
    dy_ref[...] = dy
    w = w_ref[...]
    q = r_ref[...] * jnp.exp(running(w) - w)
    out_ref[0, :SPAN, :] = fold(ktn(dy, q))
    gain_grad = jnp.sum(outer * normal, axis=0, keepdims=True)
    bias_grad = jnp.sum(outer, axis=0, keepdims=True)
    out_ref[0, SPAN:, :] = jnp.concatenate(
        [gain_grad, bias_grad, jnp.zeros((6, 2 * SPAN), F32)], axis=0
    )


def backward_kernel(
    r_ref, k_ref, v_ref, w_ref, dy_ref, s_ref, gs_ref, p_ref,
    dr_ref, dk_ref, dv_ref, dd_ref, out_ref,
):
    r, k, v, w, dy = r_ref[...], k_ref[...], v_ref[...], w_ref[...], dy_ref[...]
    u = p_ref[0:1, :]
    count = r.shape[0]
    cum = running(w)
    total = cum[-1:, :]
    e_before, e_minus, e_carry = jnp.exp(cum - w), jnp.exp(-cum), jnp.exp(total - cum)
    q, ks, kc = r * e_before, k * e_minus, k * e_carry
    aff = affinity(r, k, u, q, ks)
    below, _ = strict(count)
    dy2 = two_rows(dy)
    d_aff = jnp.where(below, knt(dy2, v), 0.0)
    own = head_sum(dy * v)
    state, grad_state = s_ref[0], gs_ref[0]
    state2, grad2 = unfold(state), unfold(grad_state)
    ks2 = two_rows(ks)
    dq = knn(dy, state2) + knn(d_aff[:count], ks2[:count]) + knn(d_aff[count:], ks2[count:])
    dks = ktn(d_aff, two_rows(q))
    dkc = knn(v, grad2)
    dv_ref[...] = (ktn(aff, dy2) + knt(kc, grad2)).astype(BF16)
    dr_ref[...] = (dq * e_before + own * u * k).astype(BF16)
    dk_ref[...] = (dks * e_minus + dkc * e_carry + own * u * r).astype(BF16)
    gq, gc = q * dq, kc * dkc
    d_total = jnp.sum(gc, axis=0, keepdims=True) + jnp.exp(total) * jnp.sum(
        state * grad_state, axis=0, keepdims=True
    )
    dw = running(gq - ks * dks - gc, upper=True) - gq + d_total
    term = dw * w
    dd_ref[...] = term.astype(BF16)
    out_ref[0] = jnp.concatenate(
        [
            jnp.sum(term, axis=0, keepdims=True),
            jnp.sum(own * r * k, axis=0, keepdims=True),
            jnp.zeros((6, 2 * SPAN), F32),
        ],
        axis=0,
    )


def block_call(kernel, chunks, step, width, ins, outs, args):
    lane = 2 * SPAN
    kinds = {
        "t": pl.BlockSpec((step, lane), lambda c, h: (c, h)),
        "s": pl.BlockSpec((1, SPAN, lane), lambda c, h: (c, 0, h)),
        "x": pl.BlockSpec((1, SPAN + 8, lane), lambda c, h: (c, 0, h)),
        "e": pl.BlockSpec((1, 8, lane), lambda c, h: (c, 0, h)),
        "p": pl.BlockSpec((8, lane), lambda c, h: (0, h)),
    }
    shapes = {
        "t": lambda d: jax.ShapeDtypeStruct((chunks * step, width), d),
        "x": lambda d: jax.ShapeDtypeStruct((chunks, SPAN + 8, width), d),
        "e": lambda d: jax.ShapeDtypeStruct((chunks, 8, width), d),
    }
    return pl.pallas_call(
        kernel,
        grid=(chunks, width // lane),
        in_specs=[kinds[kind] for kind in ins],
        out_specs=[kinds[kind] for kind, _ in outs],
        out_shape=[shapes[kind](dtype) for kind, dtype in outs],
        compiler_params=pltpu.CompilerParams(vmem_limit_bytes=48 * 1024 * 1024),
    )(*args)


def weight_grad(places, pairs, block):
    tokens, blocks = pairs[0][0].shape[0], places.shape[0]
    widths = [y.shape[1] for _, y in pairs]

    def kernel(_, *refs):
        at = 0
        for i, wide in enumerate(widths):
            refs[-1][0, :, at : at + wide] = tn(refs[2 * i][...], refs[2 * i + 1][...]).astype(
                BF16
            )
            at += wide

    specs = []
    for wide in widths:
        specs.append(pl.BlockSpec((tokens, block), lambda i, at: (0, at[i])))
        specs.append(pl.BlockSpec((tokens, wide), lambda i, at: (0, 0)))
    return pl.pallas_call(
        kernel,
        grid_spec=pltpu.PrefetchScalarGridSpec(
            num_scalar_prefetch=1,
            grid=(blocks,),
            in_specs=specs,
            out_specs=pl.BlockSpec((1, block, sum(widths)), lambda i, at: (i, 0, 0)),
        ),
        out_shape=jax.ShapeDtypeStruct((blocks, block, sum(widths)), BF16),
        compiler_params=pltpu.CompilerParams(vmem_limit_bytes=48 * 1024 * 1024),
    )(places, *[v for pair in pairs for v in pair])


def lanes_kernel(spans, x_ref, out_ref):
    at = 0
    for start, stop in spans:
        out_ref[:, at : at + stop - start] = x_ref[:, start:stop].astype(out_ref.dtype)
        at += stop - start


def move_lanes(spans, value, dtype):
    return pl.pallas_call(
        functools.partial(lanes_kernel, spans),
        in_specs=[pl.BlockSpec(memory_space=pltpu.VMEM)],
        out_specs=pl.BlockSpec(memory_space=pltpu.VMEM),
        out_shape=jax.ShapeDtypeStruct(value.shape, dtype),
        compiler_params=pltpu.CompilerParams(vmem_limit_bytes=32 * 1024 * 1024),
    )(value)


def place_kernel(counts, wide, block, at_ref, *refs):
    ins, out_ref, sems = refs[: len(counts)], refs[-2], refs[-1]
    rows = out_ref.shape[0]
    copies, i = [], 0
    for ref, n in zip(ins, counts):
        for j in range(n):
            start = pl.multiple_of(at_ref[i] * block, block)
            column = i * block // rows * wide
            copy = pltpu.make_async_copy(
                ref.at[pl.ds(j * block, block), :],
                out_ref.at[pl.ds(start, block), pl.ds(column, wide)],
                sems.at[i],
            )
            copy.start()
            copies.append(copy)
            i += 1
    for copy in copies:
        copy.wait()


def place_rows(parts, block):
    pieces = [p for part in parts for p in part[1]]
    wide = pieces[0].shape[1]
    at = jnp.concatenate([part[0] for part in parts])
    counts = [p.shape[0] // block for p in pieces]
    total = sum(counts)
    return pl.pallas_call(
        functools.partial(place_kernel, counts, wide, block),
        in_specs=[pl.BlockSpec(memory_space=pltpu.SMEM)]
        + [pl.BlockSpec(memory_space=pl.ANY)] * len(pieces),
        out_specs=pl.BlockSpec(memory_space=pl.ANY),
        out_shape=jax.ShapeDtypeStruct(
            (total * block // len(parts), wide * len(parts)), pieces[0].dtype
        ),
        scratch_shapes=[pltpu.SemaphoreType.DMA((total,))],
        compiler_params=pltpu.CompilerParams(vmem_limit_bytes=32 * 1024 * 1024),
    )(at, *pieces)


def mixes_kernel(
    open_ref, x_ref, before_ref, vec_ref, down_ref, up_ref, ddown_ref,
    m1_ref, m2_ref, m3_ref, m4_ref, dh_ref,
    normal_ref, scale_ref, delta_ref, blend_ref, m0_ref, tanh_ref, dtanh_ref,
):
    piece = pl.program_id(0)
    step = m1_ref.shape[0]
    x = x_ref[...].astype(F32)
    centred = x - jnp.mean(x, axis=-1, keepdims=True)
    scale = lax.rsqrt(jnp.mean(centred * centred, axis=-1, keepdims=True) + LN_EPS)
    normal = centred * scale
    full = normal * vec_ref[0:1, :] + vec_ref[1:2, :]
    normed = full[:step]
    first = jnp.where(open_ref[piece] == 1, before_ref[0:1, :], full[step : step + 1])
    row = lax.broadcasted_iota(jnp.int32, normed.shape, 0)
    delta = jnp.where(row == 0, first, pltpu.roll(normed, 1, 0)) - normed
    blend = (normed + delta * vec_ref[2:3, :]).astype(BF16)
    tanh = jnp.tanh(nn(blend, down_ref[...]))
    latent = tanh.astype(BF16)
    lane = lax.broadcasted_iota(jnp.int32, latent.shape, 1)
    mixed = []
    for c in range(5):
        own = (lane >= c * RANK) & (lane < (c + 1) * RANK)
        offset = nt(jnp.where(own, latent, jnp.zeros_like(latent)), up_ref[...])
        mixed.append((normed + delta * (vec_ref[3 + c : 4 + c, :] + offset)).astype(BF16))
    dtanh = jnp.tanh(nn(mixed[0], ddown_ref[...]))
    m1_ref[...], m2_ref[...], m3_ref[...], m4_ref[...] = mixed[1:]
    dh_ref[...] = dtanh.astype(BF16)

    @pl.when(piece == 0)
    def _():
        normal_ref[...] = normal[:step]
        scale_ref[...] = jnp.broadcast_to(scale[:step], scale_ref.shape)
        delta_ref[...] = delta
        blend_ref[...] = blend
        m0_ref[...] = mixed[0]
        tanh_ref[...] = tanh
        dtanh_ref[...] = dtanh


def group_mixes(opening, x, before, vec, down, up, ddown, step):
    high, width = step + 16, x.shape[1]
    pieces = x.shape[0] // high

    def whole(value):
        return pl.BlockSpec(value.shape, lambda k: (0, 0))

    def own(columns, dtype):
        return (
            pl.BlockSpec((step, columns), lambda k: (0, 0)),
            jax.ShapeDtypeStruct((step, columns), dtype),
        )

    def every(columns, dtype):
        return (
            pl.BlockSpec((step, columns), lambda k: ((k % 2) * 2 + k // 2, 0)),
            jax.ShapeDtypeStruct((pieces * step, columns), dtype),
        )

    outs = [every(width, BF16)] * 4 + [
        every(DRANK, BF16),
        own(width, F32),
        own(128, F32),
        own(width, F32),
        own(width, BF16),
        own(width, BF16),
        own(5 * RANK, F32),
        own(DRANK, F32),
    ]
    return pl.pallas_call(
        mixes_kernel,
        grid=(pieces,),
        in_specs=[
            pl.BlockSpec(memory_space=pltpu.SMEM),
            pl.BlockSpec((high, width), lambda k: (k, 0)),
            whole(before),
            whole(vec),
            whole(down),
            whole(up),
            whole(ddown),
        ],
        out_specs=[o[0] for o in outs],
        out_shape=[o[1] for o in outs],
        compiler_params=pltpu.CompilerParams(vmem_limit_bytes=56 * 1024 * 1024),
    )(opening, x, before, vec, down, up, ddown)


def product(pairs, outs, body, sides=(), tile=256):
    count = len(pairs)

    def kernel(*refs):
        ins, out_refs = refs[: 2 * count + len(sides)], refs[2 * count + len(sides) :]
        products = [
            (nn if pair[2] == "nn" else nt)(ins[2 * i][...], ins[2 * i + 1][...])
            for i, pair in enumerate(pairs)
        ]
        results = body(*products, *[r[...] for r in ins[2 * count :]])
        for ref, value in zip(out_refs, results):
            ref[...] = value.astype(ref.dtype)

    specs, args = [], []
    for a, b, form, at in pairs:
        depth = a.shape[1]
        specs.append(pl.BlockSpec(a.shape, lambda j: (0, 0)))
        if form == "nn":
            specs.append(pl.BlockSpec((depth, tile), lambda j, at=at: (0, at + j)))
        else:
            specs.append(pl.BlockSpec((tile, depth), lambda j, at=at: (j, at)))
        args += [a, b]
    for side in sides:
        specs.append(pl.BlockSpec((side.shape[0], tile), lambda j: (0, j)))
    return pl.pallas_call(
        kernel,
        grid=(outs[0][1] // tile,),
        in_specs=specs,
        out_specs=[pl.BlockSpec((o[0], tile), lambda j: (0, j)) for o in outs],
        out_shape=[jax.ShapeDtypeStruct(o[:2], o[2]) for o in outs],
        compiler_params=pltpu.CompilerParams(vmem_limit_bytes=56 * 1024 * 1024),
    )(*args, *sides)


def local(fn, outs, *args, scalar=None):
    def kernel(*refs):
        lead = [] if scalar is None else [refs[0]]
        ins, out_refs = refs[len(lead) : -len(outs)], refs[-len(outs) :]
        scalars = [r[i] for r in lead for i in range(r.shape[0])]
        results = fn(*scalars, *[r[...] for r in ins])
        for ref, value in zip(out_refs, results):
            ref[...] = value.astype(ref.dtype)

    specs = [pl.BlockSpec(memory_space=pltpu.VMEM)] * len(args)
    if scalar is not None:
        specs = [pl.BlockSpec(memory_space=pltpu.SMEM)] + specs
        args = (scalar.reshape(-1), *args)
    return pl.pallas_call(
        kernel,
        in_specs=specs,
        out_specs=[pl.BlockSpec(memory_space=pltpu.VMEM)] * len(outs),
        out_shape=[jax.ShapeDtypeStruct(o[:2], o[2]) for o in outs],
        compiler_params=pltpu.CompilerParams(vmem_limit_bytes=56 * 1024 * 1024),
    )(*args)


def take_lanes(value, spans):
    if len(spans) == 1:
        return value
    return jnp.concatenate([value[:, a:b] for a, b in spans], axis=1)


def norm_back(grad, gain, normal, scale):
    e = grad * gain
    return scale * (
        e
        - jnp.mean(e, axis=-1, keepdims=True)
        - normal * jnp.mean(e * normal, axis=-1, keepdims=True)
    )


def rows_above(value, first):
    row = lax.broadcasted_iota(jnp.int32, value.shape, 0)
    return jnp.where(row == 0, first, pltpu.roll(value, 1, 0))


def rows_below(value, last):
    row = lax.broadcasted_iota(jnp.int32, value.shape, 0)
    high = value.shape[0]
    return jnp.where(row == high - 1, last, pltpu.roll(value, high - 1, 0))


def padded(rows):
    return jnp.concatenate(
        list(rows) + [jnp.zeros((8 - len(rows), rows[0].shape[1]), F32)], axis=0
    )


def column_sum(value):
    return jnp.sum(value, axis=0, keepdims=True)


def gates_kernel(
    spans, who_ref, middle_ref, value_ref, more_ref, act_ref, cot_ref,
    out_ref, up_ref, vg_ref, rg_ref, held,
):
    to_spans, from_spans = spans
    step, part = act_ref.shape[0] // 4, act_ref.shape[1]
    who = who_ref[0]
    act = [
        act_ref[pl.ds(pl.multiple_of((who ^ j) * step, step), step), :] for j in range(4)
    ]
    recept = jax.nn.sigmoid(take_lanes(jnp.concatenate(act, axis=1).astype(F32), to_spans))
    value = value_ref[...] + more_ref[...].astype(F32)
    out = middle_ref[...] + recept * value
    out_ref[...] = take_lanes(out, from_spans).astype(BF16)
    up = take_lanes(cot_ref[...].astype(F32), to_spans)
    up_ref[...] = up
    vg_ref[...] = (up * recept).astype(BF16)
    held[...] = take_lanes(up * value * recept * (1.0 - recept), from_spans)
    for k in range(4):
        at = pl.multiple_of((who ^ k) * part, part)
        rg_ref[k * step : (k + 1) * step, :] = held[:, pl.ds(at, part)].astype(BF16)


def gates(spans, who, middle, value, more, act, cot):
    step, width = middle.shape
    part = act.shape[1]
    shape = jax.ShapeDtypeStruct
    return pl.pallas_call(
        functools.partial(gates_kernel, spans),
        in_specs=[pl.BlockSpec(memory_space=pltpu.SMEM)]
        + [pl.BlockSpec(memory_space=pltpu.VMEM)] * 5,
        out_specs=[pl.BlockSpec(memory_space=pltpu.VMEM)] * 4,
        out_shape=[
            shape((step, width), BF16),
            shape((step, width), F32),
            shape((step, width), BF16),
            shape((4 * step, part), BF16),
        ],
        scratch_shapes=[pltpu.VMEM((step, width), F32)],
        compiler_params=pltpu.CompilerParams(vmem_limit_bytes=56 * 1024 * 1024),
    )(who.reshape(1), middle, value, more, act, cot)


def mixes_back_kernel(
    kept_ref, got_ref, dl_ref, dl_more_ref, delta_ref, tanh_ref, dtanh_ref, blend_ref, m0_ref,
    down_ref, up_ref, ddown_ref, vec_ref,
    rest_ref, dg_ref, row_ref, cols_ref, down_out, up_out, ddown_out,
):
    step = delta_ref.shape[0]
    dtanh = dtanh_ref[...]
    decay_grad = dl_ref[...] + dl_more_ref[...].astype(F32)
    decay_pre = (decay_grad * (1.0 - dtanh * dtanh)).astype(BF16)
    ddown_out[...] = tn(m0_ref[...], decay_pre)
    tanh = tanh_ref[...]
    latent = tanh.astype(BF16)
    lane = lax.broadcasted_iota(jnp.int32, latent.shape, 1)
    delta, up = delta_ref[...], up_ref[...]
    latent_grad = jnp.zeros(latent.shape, F32)
    up_grad = jnp.zeros(up_out.shape, F32)
    dg = jnp.zeros(delta.shape, F32)
    total = jnp.zeros(delta.shape, F32)
    cols = []
    for c in range(5):
        own = (lane >= c * RANK) & (lane < (c + 1) * RANK)
        mine = jnp.where(own, latent, jnp.zeros_like(latent))
        if c == 0:
            grad = nt(decay_pre, ddown_ref[...])
        else:
            at = slice((c - 1) * step, c * step)
            grad = kept_ref[at, :] + got_ref[at, :].astype(F32)
        shift = grad * delta
        cols.append(column_sum(shift))
        offset = shift.astype(BF16)
        latent_grad = jnp.where(own, nn(offset, up), latent_grad)
        up_grad = up_grad + tn(offset, mine)
        dg = dg + grad * (vec_ref[3 + c : 4 + c, :] + nt(mine, up))
        total = total + grad
    up_out[...] = up_grad
    mix_pre = (latent_grad * (1.0 - tanh * tanh)).astype(BF16)
    down_out[...] = tn(blend_ref[...], mix_pre)
    blend_grad = nt(mix_pre, down_ref[...])
    dg = dg + blend_grad * vec_ref[2:3, :]
    rest_ref[...] = total + blend_grad - dg
    dg_ref[...] = dg
    row_ref[...] = dg[:8]
    cols_ref[...] = padded([column_sum(blend_grad * delta)] + cols)


def mixes_back(*args):
    delta, down, ddown = args[4], args[9], args[11]
    step, width = delta.shape
    shape = jax.ShapeDtypeStruct
    outs = [
        shape((step, width), F32),
        shape((step, width), F32),
        shape((8, width), F32),
        shape((8, width), F32),
        shape(down.shape, F32),
        shape(down.shape, F32),
        shape(ddown.shape, F32),
    ]
    return pl.pallas_call(
        mixes_back_kernel,
        in_specs=[pl.BlockSpec(memory_space=pltpu.VMEM)] * len(args),
        out_specs=[pl.BlockSpec(memory_space=pltpu.VMEM)] * len(outs),
        out_shape=outs,
        compiler_params=pltpu.CompilerParams(vmem_limit_bytes=60 * 1024 * 1024),
    )(*args)


def tie(*values):
    return lax.optimization_barrier(values)


def on_device(
    count,
    tokens,
    previous,
    initial_state,
    mixing_weights,
    lowrank_weights,
    vectors,
    feedforward_weights,
    cotangent,
):
    fast = initial_state.shape[0] == 64
    masks = (1, 8) if fast else (1, 2)
    size = 1 << len(masks)
    teams = count // size
    all_masks = [1 << b for b in range(count.bit_length() - 1)]
    team_masks = [b for b in all_masks if b not in masks]
    far = 16
    team_masks.sort(key=lambda b: fast and b != far)
    me = lax.axis_index("seq")
    _, step, width = tokens.shape
    rows = mixing_weights.shape[0]
    part = width // size
    ff_part = FF // size
    team_rows = rows * size
    def bit_of(who, mask):
        return (who // mask) % 2 if isinstance(who, int) else lax.rem(lax.div(who, mask), 2)

    def member_of(who):
        return sum(bit_of(who, b) << j for j, b in enumerate(masks))

    def team_of(who):
        return sum(bit_of(who, b) << j for j, b in enumerate(team_masks))

    member, team = member_of(me), team_of(me)
    order = sorted(range(count), key=lambda d: (team_of(d), member_of(d)))
    inverse = sorted(range(count), key=lambda p: order[p])
    across = [order[m::size] for m in range(size)]
    square = [order[m :: 2 * size] for m in range(2 * size)]
    def lane_spans(blocks):
        spans = []
        for d in blocks:
            if spans and spans[-1][1] == d * rows:
                spans[-1][1] = (d + 1) * rows
            else:
                spans.append([d * rows, (d + 1) * rows])
        return spans

    to_spans, from_spans = lane_spans(order), lane_spans(inverse)

    def to_places(value, dtype):
        return move_lanes(to_spans, value, dtype)

    def flips(k):
        return sum(b for j, b in enumerate(masks) if (k >> j) & 1)

    def trade(value, mask):
        return lax.ppermute(value, "seq", [(d, d ^ mask) for d in range(count)])

    def group_gather(value):
        side = trade(value, masks[1])
        return value, side, trade(jnp.concatenate([value, side], axis=0), masks[0])

    def group_rows(value):
        high, columns = value.shape

        def lay(own, side, far):
            return (jnp.concatenate([own, far[:high], side, far[high:]], axis=0),)

        return local(lay, [(size * high, columns, value.dtype)], *group_gather(value))[0]

    def halves(value):
        cut = [value[k * step : (k + 1) * step] for k in range(size)]
        return [cut[0], cut[2]], [cut[1], cut[3]]

    def group_fold(kept, sent):
        high, columns = kept.shape[0] // 2, kept.shape[1]
        got = trade(sent, masks[0])

        def add(mine, more):
            total = mine + more.astype(F32)
            return total[:high], total[high:]

        return local(add, [(high, columns, F32), (high, columns, BF16)], kept, got)

    def group_sum(kept, sent):
        mine, side = group_fold(kept, sent)
        return mine, trade(side, masks[1])

    def crossing_sum(*pairs):
        units = len(pairs)

        def body(*products):
            parts = [halves(p) for p in products]
            kept = [p[0][i] for i in range(2) for p in parts]
            sent = [p[1][i] for i in range(2) for p in parts]
            return jnp.concatenate(kept, axis=0), jnp.concatenate(sent, axis=0)

        high = 2 * units * step
        return product(
            [(a, b, "nt", at) for a, b, at in pairs],
            [(high, width, F32), (high, width, BF16)],
            body,
            tile=512,
        )

    def exchange(pieces):
        pieces, high = list(pieces), pieces[0].shape[0]
        for j in reversed(range(len(masks))):
            keys = [k for k in range(size) if (k >> j) & 1]
            got = trade(jnp.concatenate([pieces[k] for k in keys], axis=0), masks[j])
            for i, k in enumerate(keys):
                pieces[k] = got[i * high : (i + 1) * high]
        return pieces

    def ordered(pieces):
        pieces = list(pieces)
        for j in range(len(masks)):
            swap = lax.rem(lax.div(member, 1 << j), 2) == 1
            pieces = [
                jnp.where(swap, pieces[k ^ (1 << j)], pieces[k]) for k in range(len(pieces))
            ]
        return pieces

    def neighbour(value, offset):
        pairs = [(d, d + offset) for d in range(count) if 0 <= d + offset < count]
        return lax.ppermute(value, "seq", pairs)

    def take_columns(value, spans, who):
        return jnp.concatenate(
            [
                lax.dynamic_slice_in_dim(value, start + who * wide, wide, axis=1)
                for start, wide in spans
            ],
            axis=1,
        )

    def group_columns(value, spans):
        pieces = [take_columns(value, spans, member ^ k) for k in range(size)]
        return jnp.concatenate(ordered(exchange(pieces)), axis=0)

    def crossing(first):
        bits = list(range(1, len(team_masks))) + [0]
        if first:
            bits[0], bits[1] = bits[1], bits[0]
        return bits

    def gather_rows(own):
        return lax.all_gather(own, "seq", axis=0, tiled=True, axis_index_groups=across)

    def far_send(own):
        return trade(own, far) if fast else own

    def far_join(own, got):
        if not fast:
            return own
        upper = bit_of(me, far) == 1
        return jnp.concatenate(
            [jnp.where(upper, got, own), jnp.where(upper, own, got)], axis=0
        )

    def gather_square(paired):
        groups = square if fast else across
        return lax.all_gather(paired, "seq", axis=0, tiled=True, axis_index_groups=groups)

    def team_products(*pairs):
        if fast:
            places = jnp.arange(teams, dtype=jnp.int32)
            return weight_grad(places, pairs, team_rows).reshape(width, -1)
        return jnp.concatenate([tn(x, y).astype(BF16) for x, y in pairs], axis=1)

    def square_sum(grads):
        groups = square if fast else across
        return lax.psum_scatter(
            grads, "seq", scatter_dimension=0, tiled=True, axis_index_groups=groups
        )

    def far_split(pair):
        if not fast:
            return pair, jnp.zeros_like(pair)
        bit = bit_of(me, far)
        sent = lax.dynamic_slice_in_dim(pair, (1 - bit) * team_rows, team_rows, axis=0)
        kept = lax.dynamic_slice_in_dim(pair, bit * team_rows, team_rows, axis=0)
        return kept, trade(sent, far)

    def far_add(kept, got):
        return (kept.astype(F32) + got.astype(F32)).astype(BF16)

    def cube_gather(value, follower=None):
        for mask in reversed(all_masks):
            got = trade(value, mask)
            upper = bit_of(me, mask) == 1
            value = jnp.stack([jnp.where(upper, got, value), jnp.where(upper, value, got)])
            if mask == 8 and follower is not None:
                value, follower = tie(value, follower)
        axes = len(all_masks)
        cube = value.transpose(*reversed(range(axes)), *range(axes, value.ndim))
        return cube if follower is None else (cube, follower)

    place_axes = [all_masks[::-1].index(b) for b in team_masks[::-1] + list(masks[::-1])]

    def by_place(cube):
        rest = range(len(all_masks), cube.ndim)
        return cube.transpose(*place_axes, *rest).reshape(width, -1)

    def to_cube(value):
        cube = value.reshape(*[2] * len(place_axes), rows, -1)
        back = [place_axes.index(a) for a in range(len(place_axes))]
        return cube.transpose(*back, len(back), len(back) + 1)

    def cube_sum(cube, kind, follower):
        for axis, mask in reversed(list(enumerate(reversed(all_masks)))):
            bit = bit_of(me, mask)
            sent = lax.dynamic_index_in_dim(cube, 1 - bit, axis, keepdims=False)
            kept = lax.dynamic_index_in_dim(cube, bit, axis, keepdims=False)
            cube = kept.astype(F32) + trade(sent.astype(kind), mask).astype(F32)
            if mask == 2:
                cube, follower = tie(cube, follower)
        return cube, follower

    def hand_rows(pieces, extra=None):
        widths = [sum(p.shape[1] for p in piece) for piece in pieces]
        joint = jnp.concatenate([p for piece in pieces for p in piece], axis=1)
        mine = [
            lax.dynamic_slice_in_dim(joint, (member ^ k) * rows, rows, axis=0)
            for k in range(size)
        ]
        if extra is not None:
            mine = [jnp.concatenate([m, e], axis=1) for m, e in zip(mine, extra)]
        by_place = exchange(mine)
        by_member = ordered(by_place)
        outs, start = [], 0
        for wide in widths:
            outs += [p[:, start : start + wide] for p in by_member]
            start += wide
        joined = jnp.concatenate(outs, axis=1).astype(F32)
        if extra is None:
            return joined
        return joined, [p[:, start:].astype(F32) for p in by_place]

    up_start, decay_start, decay_up = 5 * RANK, 10 * RANK, 10 * RANK + DRANK
    last_row = neighbour(tokens[0, -1:, :], 1)
    tokens_sent = to_places(
        jnp.concatenate([tokens[0], jnp.broadcast_to(last_row, (16, width))], axis=0), BF16
    )
    natural, mix_in = cube_gather(
        jnp.concatenate(
            [vectors, initial_state, lowrank_weights[:, decay_up:].astype(F32)], axis=1
        ),
        mixing_weights,
    )
    natural = natural.reshape(width, -1)
    low_cube, mix_in = cube_gather(lowrank_weights[:, :decay_up], mix_in)
    tokens_all = jnp.concatenate(group_gather(tokens_sent), axis=0)
    mix_local = group_columns(mix_in, [(c * width, part) for c in range(5)])
    mix_local, natural, low_cube, tokens_all = tie(mix_local, natural, low_cube, tokens_all)
    lowrank = by_place(low_cube)
    mix_kv, mix_rest = mix_local[:, : 2 * part], mix_local[:, 2 * part :]
    kv_got, mix_rest, feed_in = tie(far_send(mix_kv), mix_rest, feedforward_weights)
    w_kv = gather_square(far_join(mix_kv, kv_got))
    tiles = part // 256

    mine = lax.dynamic_slice_in_dim(natural, member * part, part, axis=0)
    vec_part = mine[:, :16].T
    first_state = mine[:, 16 : 16 + SPAN].T
    w_dup = mine[:, 16 + SPAN :].astype(BF16)
    vec = by_place(
        natural[:, :16].reshape(*[2] * len(all_masks), rows, 16)
    ).T
    wkv_rows = jnp.concatenate([vec_part[9:12], jnp.zeros((5, part), F32)], axis=0)
    is_first = (me == 0).astype(jnp.int32)
    before = to_places(previous.reshape(2, width), F32)
    w_down, w_up = lowrank[:, :up_start], lowrank[:, up_start:decay_start]
    w_ddown = lowrank[:, decay_start:]

    opening = jnp.stack(
        [jnp.bitwise_xor(me, flips(k)) == 0 for k in (0, 2, 1, 3)]
    ).astype(jnp.int32)
    (
        *mixed_all, dh_all, normal_one, scale_one, delta, blend, mixed_zero, mix_tanh, decay_tanh,
    ) = group_mixes(opening, tokens_all, before, vec, w_down, w_up, w_ddown, step)
    rest_got, mixed_all[0] = tie(far_send(mix_rest), mixed_all[0])
    w_rest = gather_square(far_join(mix_rest, rest_got))
    ff_spans = [(0, ff_part), (FF, part), (FF + width, ff_part)]
    ff_local = group_columns(feed_in, ff_spans)
    everyone = size * step
    (log_decay,) = product(
        [(dh_all, w_dup, "nt", 0)],
        [(everyone, part, F32)],
        lambda acc, base: (-jnp.exp(base + acc),),
        sides=(vec_part[8:9],),
    )
    keys, values = product(
        [(mixed_all[0], w_kv, "nn", 0), (mixed_all[1], w_kv, "nn", tiles)],
        [(everyone, part, F32)] * 2,
        lambda a, b: (a, b),
    )

    keys, ff_local = tie(keys, ff_local)
    ff_tail = ff_local[:, ff_part + part :]
    ff_near = ff_local[:, : ff_part + part]
    near_got = far_send(ff_near)

    call = functools.partial(block_call, chunks=size, step=step, width=part)
    (totals,) = call(
        totals_kernel, ins="ttt", outs=[("x", F32)], args=(keys, values, log_decay)
    )
    stages, current = [], [None, []]
    for mask in all_masks:
        if mask in masks:
            current[1].append(1 << masks.index(mask))
        else:
            stages.append(current)
            current = [mask, []]
    stages.append(current)
    high, long = SPAN + 8, SPAN + 16

    def chain(early, late):
        return early[0] * late[0], late[0] * early[1] + late[1]

    def pick(flag, yes, no):
        return tuple(jnp.where(flag, a, b) for a, b in zip(yes, no))

    def rows8(row):
        return jnp.broadcast_to(row, (8, part))

    def pack(items):
        return jnp.concatenate([r for d, v in items for r in (v, rows8(d))], axis=0)

    def unpack(array, count):
        cut = [array[i * high : (i + 1) * high] for i in range(count)]
        return [(c[SPAN : SPAN + 1], c[:SPAN]) for c in cut]

    def swap_members(who, pieces):
        pieces = list(pieces)
        for j in range(len(masks)):
            flag = (who // (1 << j)) % 2 == 1
            pieces = [jnp.where(flag, pieces[k ^ (1 << j)], pieces[k]) for k in range(size)]
        return pieces

    def neutral():
        return jnp.ones((1, part), F32), jnp.zeros((SPAN, part), F32)

    def flags_of(mask):
        bit = jnp.int32(0) if mask is None else bit_of(me, mask)
        return jnp.stack([member, bit]).astype(jnp.int32)

    keys_at, decays = list(range(size)), []
    open_bits = size - 1
    stage_arrays = [totals.reshape(size * high, part)]
    for index, (mask, merges) in enumerate(stages):
        last = index + 1 == len(stages)
        after_keys = keys_at
        for bit in merges:
            after_keys = [g for g in after_keys if not g & bit]

        def forward_stage(
            who, late, *arrays, mask=mask, merges=merges, groups=keys_at, bits=open_bits, last=last
        ):
            marks = []
            if mask is None:
                cut = [arrays[0][k * high : (k + 1) * high] for k in range(size)]
                total = {
                    m: (p[SPAN : SPAN + 1], p[:SPAN])
                    for m, p in enumerate(swap_members(who, cut))
                }
                chunks = [neutral() for _ in range(size)]
            else:
                total = dict(zip(groups, unpack(arrays[0], len(groups))))
                chunks = unpack(arrays[1], size)
                other = {}
                for i, g in enumerate(groups):
                    got = arrays[2][i * long : (i + 1) * long].astype(F32)
                    other[g] = got[SPAN : SPAN + 1] + got[SPAN + 8 : SPAN + 9], got[:SPAN]
                marks += [total[g][0] for g in groups] + [other[g][0] for g in groups]
                late = late == 1
                chunks = [
                    pick(late, chain(other[m & bits], c), c) for m, c in enumerate(chunks)
                ]
                total = {
                    g: pick(late, chain(other[g], total[g]), chain(total[g], other[g]))
                    for g in groups
                }
            for bit in merges:
                marks += [total[g][0] for g in total]
                chunks = [
                    chain(total[(m & bits) ^ bit], c) if m & bit else c
                    for m, c in enumerate(chunks)
                ]
                total = {g: chain(total[g], total[g | bit]) for g in total if not g & bit}
                bits ^= bit
            marks = jnp.concatenate([rows8(r) for r in marks], axis=0)
            if last:
                states = [d * arrays[-1] + v for d, v in chunks]
                return jnp.concatenate(swap_members(who, states), axis=0), marks
            sent = []
            for d, v in total.values():
                first = d.astype(BF16)
                rest = (d - first.astype(F32)).astype(BF16)
                sent += [v.astype(BF16), rows8(first), rows8(rest)]
            return (
                pack(list(total.values())), pack(chunks), jnp.concatenate(sent, axis=0), marks
            )

        count_marks = (0 if mask is None else 2 * len(keys_at)) + sum(
            len(keys_at) >> i for i in range(len(merges))
        )
        marks_out = (8 * count_marks, part, F32)
        if last:
            outs = [(size * SPAN, part, F32), marks_out]
            state_in, marks = local(
                forward_stage, outs, *stage_arrays, first_state, scalar=flags_of(mask)
            )
            state_in = state_in.reshape(size, SPAN, part)
        else:
            outs = [
                (len(after_keys) * high, part, F32),
                (size * high, part, F32),
                (len(after_keys) * long, part, BF16),
                marks_out,
            ]
            total, chunks, sent, marks = local(
                forward_stage, outs, *stage_arrays, scalar=flags_of(mask)
            )
            if mask == (2 if fast else 4):
                sent, near_got = tie(sent, near_got)
            stage_arrays = [total, chunks, trade(sent, stages[index + 1][0])]
        decays.append(marks)
        keys_at = after_keys
        for bit in merges:
            open_bits ^= bit
    w_near = gather_square(far_join(ff_near, near_got))
    w_key, w_rec = w_near, w_near[:, ff_part:]
    state_in, ff_tail = tie(state_in, ff_tail)
    val_got = far_send(ff_tail)

    receipt, gate_pre = product(
        [(mixed_all[2], w_rest, "nn", 0), (mixed_all[3], w_rest, "nn", tiles)],
        [(everyone, part, F32)] * 2,
        lambda a, b: (a, b),
    )
    wkv, gated = call(
        forward_kernel,
        ins="tttttsp",
        outs=[("t", F32), ("t", BF16)],
        args=(receipt, keys, values, log_decay, gate_pre, state_in, wkv_rows),
    )
    gated, val_got = tie(gated, val_got)
    w_val = gather_square(far_join(ff_tail, val_got))
    branch, branch_more = group_sum(*crossing_sum((gated, w_rest, 2)))

    def norm_two(hidden, mine, more, vec):
        middle = hidden[:step].astype(F32) + mine + more.astype(F32)
        centred = middle - jnp.mean(middle, axis=-1, keepdims=True)
        scale = lax.rsqrt(jnp.mean(centred * centred, axis=-1, keepdims=True) + LN_EPS)
        normal = centred * scale
        tail = normal[step - 8 :] * vec[12:13] + vec[13:14]
        return middle, normal, jnp.broadcast_to(scale, (step, 128)), tail

    whole = (step, width, F32)
    middle, normal_two, scale_two, tail_two = local(
        norm_two,
        [whole, whole, (step, 128, F32), (8, width, F32)],
        tokens_sent,
        branch,
        branch_more,
        vec,
    )

    def mix_two(first, normal, arrived, before, vec):
        normed = normal * vec[12:13] + vec[13:14]
        above = jnp.where(first == 1, before[1:2], arrived[7:8])
        delta = rows_above(normed, above) - normed
        key_in, recv_in = normed + delta * vec[14:15], normed + delta * vec[15:16]
        return jnp.concatenate([key_in, recv_in], axis=0), delta

    both, delta_two = local(
        mix_two,
        [(2 * step, width, BF16), whole],
        normal_two,
        neighbour(tail_two, 1),
        before,
        vec,
        scalar=is_first,
    )

    key_all, recv_all = group_rows(both[:step]), group_rows(both[step:])
    relu, squared = product(
        [(key_all, w_key, "nn", 0)],
        [(everyone, ff_part, F32), (everyone, ff_part, BF16)],
        lambda acc: (jnp.maximum(acc, 0.0), jnp.square(jnp.maximum(acc, 0.0))),
        tile=ff_part // 2,
    )
    (recept_act,) = product(
        [(recv_all, w_rec, "nn", 0)],
        [(everyone, part, BF16)],
        lambda acc: (acc,),
    )
    squared, recept_act = tie(squared, recept_act)
    acts = exchange([recept_act[k * step : (k + 1) * step] for k in range(size)])
    value, value_more = group_sum(*crossing_sum((squared, w_val, 0)))
    block_output, upstream, value_grad, recept_grads = gates(
        (to_spans, from_spans),
        member,
        middle,
        value,
        value_more,
        jnp.concatenate(acts, axis=0),
        cotangent.reshape(step, width),
    )

    rg_all = jnp.concatenate(
        exchange([recept_grads[k * step : (k + 1) * step] for k in range(size)]), axis=0
    )
    vg_all = group_rows(value_grad)
    val_grads = team_products((vg_all, squared))
    vg_all, val_grads, rg_all = tie(vg_all, val_grads, rg_all)
    val_pair = square_sum(val_grads)
    (key_grad,) = product(
        [(vg_all, w_val, "nn", 0)],
        [(everyone, ff_part, BF16)],
        lambda acc, relu: (acc * (2.0 * relu),),
        sides=(relu,),
        tile=ff_part // 2,
    )
    key_grads = team_products((key_all, key_grad))
    key_grad, key_grads = tie(key_grad, key_grads)
    key_pair = square_sum(key_grads)
    recv_two = group_sum(*crossing_sum((rg_all, w_rec, 0)))
    key_two = group_sum(*crossing_sum((key_grad, w_key, 0)))

    def inputs_back(key, key_more, recv, recv_more, vec):
        key, recv = key + key_more.astype(F32), recv + recv_more.astype(F32)
        top = key[:8] * vec[14:15] + recv[:8] * vec[15:16]
        return jnp.concatenate([key, recv], axis=0), top

    in_grads, top_two = local(
        inputs_back, [(2 * step, width, F32), (8, width, F32)], *key_two, *recv_two, vec
    )
    last_flag = (me == count - 1).astype(jnp.int32)

    def norm_two_back(last, grads, arrived, upstream, normal, scale, delta, vec):
        key_grad, recv_grad = grads[:step], grads[step:]
        shifted = key_grad * vec[14:15] + recv_grad * vec[15:16]
        below = jnp.where(last == 1, jnp.zeros_like(arrived[:1]), arrived[:1])
        grad = (
            key_grad * (1.0 - vec[14:15])
            + recv_grad * (1.0 - vec[15:16])
            + rows_below(shifted, below)
        )
        out = upstream + norm_back(grad, vec[12:13], normal, scale[:, :1])
        cols = padded(
            [
                column_sum(grad * normal),
                column_sum(grad),
                column_sum(key_grad * delta),
                column_sum(recv_grad * delta),
            ]
        )
        return out, out, cols

    middle_grad, branch_grad, cols_two = local(
        norm_two_back,
        [whole, (step, width, BF16), (8, width, F32)],
        in_grads,
        neighbour(top_two, -1),
        upstream,
        normal_two,
        scale_two,
        delta_two,
        vec,
        scalar=last_flag,
    )

    bg_all = group_rows(branch_grad)
    (gated_grad,) = product(
        [(bg_all, w_rest, "nn", 2 * tiles)], [(everyone, part, F32)], lambda acc: (acc,)
    )
    gate_grad, wkv_grad, ends = call(
        gate_kernel,
        ins="tttttp",
        outs=[("t", BF16), ("t", F32), ("x", F32)],
        args=(gated_grad, gate_pre, wkv, receipt, log_decay, wkv_rows),
    )
    val_kept, val_got = far_split(val_pair)
    keys_at, open_bits = list(range(size)), size - 1
    stage_arrays = [ends.reshape(size * high, part)]
    for index, (mask, merges) in enumerate(stages):
        last = index + 1 == len(stages)
        after_keys = keys_at
        for bit in merges:
            after_keys = [g for g in after_keys if not g & bit]

        def backward_stage(
            who, late, *arrays, mask=mask, merges=merges, groups=keys_at, bits=open_bits, last=last
        ):
            marks = [arrays[-1][i * 8 : i * 8 + 1] for i in range(arrays[-1].shape[0] // 8)]
            if mask is None:
                cut = [arrays[0][k * high : k * high + SPAN] for k in range(size)]
                total = dict(enumerate(swap_members(who, cut)))
                chunks = [neutral() for _ in range(size)]
            else:
                total = {g: arrays[0][i * SPAN : (i + 1) * SPAN] for i, g in enumerate(groups)}
                chunks = unpack(arrays[1], size)
                other = {
                    g: arrays[2][i * SPAN : (i + 1) * SPAN].astype(F32)
                    for i, g in enumerate(groups)
                }
                here = dict(zip(groups, marks))
                there = dict(zip(groups, marks[len(groups) :]))
                marks = marks[2 * len(groups) :]
                early = late == 0
                chunks = [
                    pick(
                        early,
                        (d * there[m & bits], d * other[m & bits] + v),
                        (d, v),
                    )
                    for m, (d, v) in enumerate(chunks)
                ]
                total = {
                    g: jnp.where(
                        early,
                        total[g] + here[g] * other[g],
                        other[g] + there[g] * total[g],
                    )
                    for g in groups
                }
            for bit in merges:
                here = dict(zip(total, marks))
                marks = marks[len(total) :]
                chunks = [
                    (d, v)
                    if m & bit
                    else (d * here[(m & bits) | bit], d * total[(m & bits) | bit] + v)
                    for m, (d, v) in enumerate(chunks)
                ]
                total = {
                    g: total[g] + here[g] * total[g | bit] for g in total if not g & bit
                }
                bits ^= bit
            joint = jnp.concatenate(list(total.values()), axis=0)
            if last:
                grads = swap_members(who, [v for _, v in chunks])
                return jnp.concatenate(grads, axis=0), joint.T
            return joint, pack(chunks), joint

        if last:
            outs = [(size * SPAN, part, F32), (part, SPAN, F32)]
            grad_out, first_grad = local(
                backward_stage, outs, *stage_arrays, decays[index], scalar=flags_of(mask)
            )
            grad_out = grad_out.reshape(size, SPAN, part)
        else:
            outs = [
                (len(after_keys) * SPAN, part, F32),
                (size * high, part, F32),
                (len(after_keys) * SPAN, part, BF16),
            ]
            total, chunks, sent = local(
                backward_stage, outs, *stage_arrays, decays[index], scalar=flags_of(mask)
            )
            if mask == (2 if fast else 4):
                sent, val_got = tie(sent, val_got)
            stage_arrays = [total, chunks, trade(sent, stages[index + 1][0])]
        keys_at = after_keys
        for bit in merges:
            open_bits ^= bit
    out_grads = team_products((bg_all, gated), (recv_all, rg_all), (mixed_all[3], gate_grad))
    grad_out, out_grads = tie(grad_out, out_grads)
    out_pair = square_sum(out_grads)

    d_receipt, d_keys, d_values, d_decay, extra = call(
        backward_kernel,
        ins="tttttssp",
        outs=[("t", BF16)] * 4 + [("e", F32)],
        args=(receipt, keys, values, log_decay, wkv_grad, state_in, grad_out, wkv_rows),
    )
    grads = [d_keys, d_values, d_receipt, gate_grad]
    kept, sent = crossing_sum(
        *[(grads[c], w_rest if c > 1 else w_kv, c % 2) for c in range(4)]
    )
    main_grads = team_products(
        (mixed_all[0], d_keys), (mixed_all[1], d_values), (mixed_all[2], d_receipt)
    )

    def latent_back(grad, up):
        kept, sent = halves(nn(grad, up))
        return jnp.concatenate(kept, axis=0), jnp.concatenate(sent, axis=0)

    latent_mine, latent_more = group_sum(
        *local(
            latent_back, [(2 * step, DRANK, F32), (2 * step, DRANK, BF16)], d_decay, w_dup
        )
    )
    key_kept, key_got = far_split(key_pair)
    sent, main_grads, latent_more, key_got = tie(sent, main_grads, latent_more, key_got)
    main_pair = square_sum(main_grads)
    mixed_mine, mixed_more = group_sum(kept, sent)
    mixed_more, out_pair = tie(mixed_more, out_pair)
    out_kept, out_got = far_split(out_pair)
    val_sum, key_sum = far_add(val_kept, val_got), far_add(key_kept, key_got)
    rest_grad, delta_grad, top_one, cols_mix, down_grad, up_grad, ddown_grad = mixes_back(
        mixed_mine,
        mixed_more,
        latent_mine,
        latent_more,
        delta,
        mix_tanh,
        decay_tanh,
        blend,
        mixed_zero,
        w_down,
        w_up,
        w_ddown,
        vec,
    )
    rest_grad, main_pair, out_got = tie(rest_grad, main_pair, out_got)
    out_sum = far_add(out_kept, out_got)

    def norm_one_back(last, rest, shifted, arrived, normal, scale, middle, vec):
        below = jnp.where(last == 1, jnp.zeros_like(arrived[:1]), arrived[:1])
        grad = rest + rows_below(shifted, below)
        out = middle + norm_back(grad, vec[0:1], normal, scale[:, :1])
        cols = padded([column_sum(grad * normal), column_sum(grad)])
        return take_lanes(out, from_spans), cols

    block_input_gradient, cols_one = local(
        norm_one_back,
        [whole, (8, width, F32)],
        rest_grad,
        delta_grad,
        neighbour(top_one, -1),
        normal_one,
        scale_one,
        middle_grad,
        vec,
        scalar=last_flag,
    )
    main_kept, main_got = far_split(main_pair)


    def spread(value):
        zero = jnp.zeros((width, value.shape[1]), F32)
        return lax.dynamic_update_slice_in_dim(zero, value, member * part, axis=0)

    vec_low = jnp.concatenate([cols_one[:2], cols_mix[:6], cols_two[:4]], axis=0)
    vec_head = jnp.concatenate(
        [jnp.sum(extra[:, :2], axis=0), jnp.sum(ends[:, SPAN : SPAN + 2], axis=0)], axis=0
    )
    by_feature = jnp.concatenate([down_grad, up_grad, ddown_grad, vec_low.T], axis=1)
    by_channel = spread(jnp.concatenate([tn(d_decay, dh_all), vec_head.T], axis=1))
    low, main_got = cube_sum(
        jnp.concatenate(
            [to_cube(by_feature), by_channel.reshape(*[2] * len(all_masks), rows, -1)], axis=-1
        ),
        BF16,
        main_got,
    )
    main_sum = far_add(main_kept, main_got)

    def column_parts(value):
        return [value[:, c * part : (c + 1) * part] for c in range(3)]

    out_cols, main_cols = column_parts(out_sum), column_parts(main_sum)
    holder = lax.div(me * rows, part)

    def rows_of(who):
        mine = lax.dynamic_slice_in_dim(first_grad, lax.rem(who * rows, part), rows, axis=0)
        high = lax.reduce_precision(mine, 8, 7)
        return jnp.concatenate([high, mine - high], axis=1).astype(BF16)

    feedforward_gradient, handed = hand_rows(
        [[key_sum], [out_cols[1]], [val_sum]],
        [rows_of(jnp.bitwise_xor(me, flips(k))) for k in range(size)],
    )
    state_rows = handed[0]
    for k in range(1, size):
        state_rows = jnp.where(holder == (member ^ k), handed[k], state_rows)
    initial_state_gradient = state_rows[:, :SPAN] + state_rows[:, SPAN:]
    mixing_gradient = hand_rows([[m] for m in main_cols] + [[out_cols[2]], [out_cols[0]]])

    vec_at = decay_up + 12
    lowrank_gradient = jnp.concatenate(
        [low[:, :decay_up], low[:, vec_at : vec_at + DRANK]], axis=1
    )
    vectors_gradient = jnp.concatenate(
        [low[:, decay_up : decay_up + 8], low[:, vec_at + DRANK :], low[:, decay_up + 8 : vec_at]],
        axis=1,
    )
    return (
        block_output.reshape(1, step, width),
        block_input_gradient.reshape(1, step, width),
        initial_state_gradient,
        mixing_gradient,
        lowrank_gradient,
        vectors_gradient,
        feedforward_gradient,
    )


def solution(mesh):
    rowwise = P("seq", None)
    tokenwise = P(None, "seq", None)
    return jax.shard_map(
        functools.partial(on_device, mesh.shape["seq"]),
        mesh=mesh,
        in_specs=(tokenwise, P(), rowwise, rowwise, rowwise, rowwise, rowwise, tokenwise),
        out_specs=(tokenwise, tokenwise, rowwise, rowwise, rowwise, rowwise, rowwise),
        check_vma=False,
    )
```

```python
import functools

import jax
import jax.numpy as jnp
from jax import lax
from jax.experimental import pallas as pl
from jax.experimental.pallas import tpu as pltpu
from jax.sharding import PartitionSpec as P

HEADS = 32
SPAN = 64
FF = 7168
RANK = 32
DRANK = 64
LN_EPS = 1e-05
GN_EPS = 0.00064

F32 = jnp.float32
BF16 = jnp.bfloat16
HI = lax.Precision.HIGHEST


def nn(a, b):
    return jnp.dot(a, b, preferred_element_type=F32)


def nt(a, b):
    return lax.dot_general(a, b, (((1,), (1,)), ((), ())), preferred_element_type=F32)


def tn(a, b):
    return lax.dot_general(a, b, (((0,), (0,)), ((), ())), preferred_element_type=F32)


def knn(a, b):
    return lax.dot_general(
        a, b, (((1,), (0,)), ((), ())), preferred_element_type=F32
    )


def knt(a, b):
    return lax.dot_general(
        a, b, (((1,), (1,)), ((), ())), preferred_element_type=F32
    )


def ktn(a, b):
    return lax.dot_general(
        a, b, (((0,), (0,)), ((), ())), preferred_element_type=F32
    )


def low_lanes(shape):
    return lax.broadcasted_iota(jnp.int32, shape, len(shape) - 1) < SPAN


def head_sum(x):
    low = low_lanes(x.shape)
    s0 = jnp.sum(jnp.where(low, x, 0.0), axis=-1, keepdims=True)
    s1 = jnp.sum(jnp.where(low, 0.0, x), axis=-1, keepdims=True)
    return jnp.where(low, s0, s1)


def two_rows(x):
    low = low_lanes(x.shape)
    return jnp.concatenate([jnp.where(low, x, 0.0), jnp.where(low, 0.0, x)], axis=0)


def fold(full):
    return jnp.where(low_lanes((SPAN, 2 * SPAN)), full[:SPAN], full[SPAN:])


def unfold(state):
    low = low_lanes(state.shape)
    return jnp.concatenate([jnp.where(low, state, 0.0), jnp.where(low, 0.0, state)], axis=0)


def running(w, upper=False):
    count = w.shape[0]
    row = lax.broadcasted_iota(jnp.int32, (count, count), 0)
    col = lax.broadcasted_iota(jnp.int32, (count, count), 1)
    keep = (col >= row) if upper else (col <= row)
    return lax.dot_general(
        jnp.where(keep, 1.0, 0.0).astype(F32),
        w,
        (((1,), (0,)), ((), ())),
        precision=HI,
        preferred_element_type=F32,
    )


def strict(count):
    row = lax.broadcasted_iota(jnp.int32, (2 * count, count), 0)
    col = lax.broadcasted_iota(jnp.int32, (2 * count, count), 1)
    row = jnp.where(row >= count, row - count, row)
    return row > col, row == col


def affinity(r, k, u, q, ks):
    count = r.shape[0]
    below, diag = strict(count)
    raw = knt(two_rows(q), ks)
    share = jnp.sum(two_rows(r * u * k), axis=-1, keepdims=True)
    return jnp.where(below, raw, jnp.where(diag, share, 0.0))


def totals_kernel(k_ref, v_ref, w_ref, out_ref):
    cum = running(w_ref[...])
    total = cum[-1:, :]
    kc = k_ref[...] * jnp.exp(total - cum)
    out_ref[0, :SPAN, :] = fold(ktn(v_ref[...], kc))
    out_ref[0, SPAN:, :] = jnp.broadcast_to(jnp.exp(total), (8, 2 * SPAN))


def group_norm(y, gain, bias):
    centred = y - head_sum(y) * (1.0 / SPAN)
    spread = head_sum(centred * centred) * (1.0 / SPAN)
    scale = lax.rsqrt(spread + GN_EPS)
    normal = centred * scale
    return normal, scale, normal * gain + bias


def forward_kernel(r_ref, k_ref, v_ref, w_ref, g_ref, s_ref, p_ref, y_ref, gated_ref):
    r, k, v, w = r_ref[...], k_ref[...], v_ref[...], w_ref[...]
    cum = running(w)
    q = r * jnp.exp(cum - w)
    ks = k * jnp.exp(-cum)
    aff = affinity(r, k, p_ref[0:1, :], q, ks)
    count = r.shape[0]
    v2 = two_rows(v)
    y = (
        knt(q, unfold(s_ref[0]))
        + knn(aff[:count], v2[:count])
        + knn(aff[count:], v2[count:])
    )
    y_ref[...] = y
    gate = g_ref[...]
    _, _, grouped = group_norm(y, p_ref[1:2, :], p_ref[2:3, :])
    gated_ref[...] = (grouped * gate * jax.nn.sigmoid(gate)).astype(BF16)


def gate_kernel(gg_ref, g_ref, y_ref, r_ref, w_ref, p_ref, gate_ref, dy_ref, out_ref):
    gated_grad, gate, y = gg_ref[...], g_ref[...], y_ref[...]
    gain = p_ref[1:2, :]
    normal, scale, grouped = group_norm(y, gain, p_ref[2:3, :])
    sig = jax.nn.sigmoid(gate)
    gate_ref[...] = (gated_grad * grouped * sig * (1.0 + gate * (1.0 - sig))).astype(BF16)
    outer = gated_grad * gate * sig
    inner = outer * gain
    dy = scale * (
        inner
        - head_sum(inner) * (1.0 / SPAN)
        - normal * (head_sum(inner * normal) * (1.0 / SPAN))
    )
    dy_ref[...] = dy
    w = w_ref[...]
    q = r_ref[...] * jnp.exp(running(w) - w)
    out_ref[0, :SPAN, :] = fold(ktn(dy, q))
    gain_grad = jnp.sum(outer * normal, axis=0, keepdims=True)
    bias_grad = jnp.sum(outer, axis=0, keepdims=True)
    out_ref[0, SPAN:, :] = jnp.concatenate(
        [gain_grad, bias_grad, jnp.zeros((6, 2 * SPAN), F32)], axis=0
    )


def backward_kernel(
    r_ref, k_ref, v_ref, w_ref, dy_ref, s_ref, gs_ref, p_ref,
    dr_ref, dk_ref, dv_ref, dd_ref, out_ref,
):
    r, k, v, w, dy = r_ref[...], k_ref[...], v_ref[...], w_ref[...], dy_ref[...]
    u = p_ref[0:1, :]
    count = r.shape[0]
    cum = running(w)
    total = cum[-1:, :]
    e_before, e_minus, e_carry = jnp.exp(cum - w), jnp.exp(-cum), jnp.exp(total - cum)
    q, ks, kc = r * e_before, k * e_minus, k * e_carry
    aff = affinity(r, k, u, q, ks)
    below, _ = strict(count)
    dy2 = two_rows(dy)
    d_aff = jnp.where(below, knt(dy2, v), 0.0)
    own = head_sum(dy * v)
    state, grad_state = s_ref[0], gs_ref[0]
    state2, grad2 = unfold(state), unfold(grad_state)
    ks2 = two_rows(ks)
    dq = knn(dy, state2) + knn(d_aff[:count], ks2[:count]) + knn(d_aff[count:], ks2[count:])
    dks = ktn(d_aff, two_rows(q))
    dkc = knn(v, grad2)
    dv_ref[...] = (ktn(aff, dy2) + knt(kc, grad2)).astype(BF16)
    dr_ref[...] = (dq * e_before + own * u * k).astype(BF16)
    dk_ref[...] = (dks * e_minus + dkc * e_carry + own * u * r).astype(BF16)
    gq, gc = q * dq, kc * dkc
    d_total = jnp.sum(gc, axis=0, keepdims=True) + jnp.exp(total) * jnp.sum(
        state * grad_state, axis=0, keepdims=True
    )
    dw = running(gq - ks * dks - gc, upper=True) - gq + d_total
    term = dw * w
    dd_ref[...] = term.astype(BF16)
    out_ref[0] = jnp.concatenate(
        [
            jnp.sum(term, axis=0, keepdims=True),
            jnp.sum(own * r * k, axis=0, keepdims=True),
            jnp.zeros((6, 2 * SPAN), F32),
        ],
        axis=0,
    )


def block_call(kernel, chunks, step, width, ins, outs, args):
    lane = 2 * SPAN
    kinds = {
        "t": pl.BlockSpec((step, lane), lambda c, h: (c, h)),
        "s": pl.BlockSpec((1, SPAN, lane), lambda c, h: (c, 0, h)),
        "x": pl.BlockSpec((1, SPAN + 8, lane), lambda c, h: (c, 0, h)),
        "e": pl.BlockSpec((1, 8, lane), lambda c, h: (c, 0, h)),
        "p": pl.BlockSpec((8, lane), lambda c, h: (0, h)),
    }
    shapes = {
        "t": lambda d: jax.ShapeDtypeStruct((chunks * step, width), d),
        "x": lambda d: jax.ShapeDtypeStruct((chunks, SPAN + 8, width), d),
        "e": lambda d: jax.ShapeDtypeStruct((chunks, 8, width), d),
    }
    return pl.pallas_call(
        kernel,
        grid=(chunks, width // lane),
        in_specs=[kinds[kind] for kind in ins],
        out_specs=[kinds[kind] for kind, _ in outs],
        out_shape=[shapes[kind](dtype) for kind, dtype in outs],
        compiler_params=pltpu.CompilerParams(vmem_limit_bytes=48 * 1024 * 1024),
    )(*args)


def weight_grad(places, pairs, block):
    tokens, blocks = pairs[0][0].shape[0], places.shape[0]
    widths = [y.shape[1] for _, y in pairs]

    def kernel(_, *refs):
        at = 0
        for i, wide in enumerate(widths):
            refs[-1][0, :, at : at + wide] = tn(refs[2 * i][...], refs[2 * i + 1][...]).astype(
                BF16
            )
            at += wide

    specs = []
    for wide in widths:
        specs.append(pl.BlockSpec((tokens, block), lambda i, at: (0, at[i])))
        specs.append(pl.BlockSpec((tokens, wide), lambda i, at: (0, 0)))
    return pl.pallas_call(
        kernel,
        grid_spec=pltpu.PrefetchScalarGridSpec(
            num_scalar_prefetch=1,
            grid=(blocks,),
            in_specs=specs,
            out_specs=pl.BlockSpec((1, block, sum(widths)), lambda i, at: (i, 0, 0)),
        ),
        out_shape=jax.ShapeDtypeStruct((blocks, block, sum(widths)), BF16),
        compiler_params=pltpu.CompilerParams(vmem_limit_bytes=48 * 1024 * 1024),
    )(places, *[v for pair in pairs for v in pair])


def lanes_kernel(spans, x_ref, out_ref):
    at = 0
    for start, stop in spans:
        out_ref[:, at : at + stop - start] = x_ref[:, start:stop].astype(out_ref.dtype)
        at += stop - start


def move_lanes(spans, value, dtype):
    return pl.pallas_call(
        functools.partial(lanes_kernel, spans),
        in_specs=[pl.BlockSpec(memory_space=pltpu.VMEM)],
        out_specs=pl.BlockSpec(memory_space=pltpu.VMEM),
        out_shape=jax.ShapeDtypeStruct(value.shape, dtype),
        compiler_params=pltpu.CompilerParams(vmem_limit_bytes=32 * 1024 * 1024),
    )(value)


def place_kernel(counts, wide, block, at_ref, *refs):
    ins, out_ref, sems = refs[: len(counts)], refs[-2], refs[-1]
    rows = out_ref.shape[0]
    copies, i = [], 0
    for ref, n in zip(ins, counts):
        for j in range(n):
            start = pl.multiple_of(at_ref[i] * block, block)
            column = i * block // rows * wide
            copy = pltpu.make_async_copy(
                ref.at[pl.ds(j * block, block), :],
                out_ref.at[pl.ds(start, block), pl.ds(column, wide)],
                sems.at[i],
            )
            copy.start()
            copies.append(copy)
            i += 1
    for copy in copies:
        copy.wait()


def place_rows(parts, block):
    pieces = [p for part in parts for p in part[1]]
    wide = pieces[0].shape[1]
    at = jnp.concatenate([part[0] for part in parts])
    counts = [p.shape[0] // block for p in pieces]
    total = sum(counts)
    return pl.pallas_call(
        functools.partial(place_kernel, counts, wide, block),
        in_specs=[pl.BlockSpec(memory_space=pltpu.SMEM)]
        + [pl.BlockSpec(memory_space=pl.ANY)] * len(pieces),
        out_specs=pl.BlockSpec(memory_space=pl.ANY),
        out_shape=jax.ShapeDtypeStruct(
            (total * block // len(parts), wide * len(parts)), pieces[0].dtype
        ),
        scratch_shapes=[pltpu.SemaphoreType.DMA((total,))],
        compiler_params=pltpu.CompilerParams(vmem_limit_bytes=32 * 1024 * 1024),
    )(at, *pieces)


def mixes_kernel(
    open_ref, x_ref, before_ref, vec_ref, down_ref, up_ref, ddown_ref,
    m1_ref, m2_ref, m3_ref, m4_ref, dh_ref,
    normal_ref, scale_ref, delta_ref, blend_ref, m0_ref, tanh_ref, dtanh_ref,
):
    piece = pl.program_id(0)
    step = m1_ref.shape[0]
    x = x_ref[...].astype(F32)
    centred = x - jnp.mean(x, axis=-1, keepdims=True)
    scale = lax.rsqrt(jnp.mean(centred * centred, axis=-1, keepdims=True) + LN_EPS)
    normal = centred * scale
    full = normal * vec_ref[0:1, :] + vec_ref[1:2, :]
    normed = full[:step]
    first = jnp.where(open_ref[piece] == 1, before_ref[0:1, :], full[step : step + 1])
    row = lax.broadcasted_iota(jnp.int32, normed.shape, 0)
    delta = jnp.where(row == 0, first, pltpu.roll(normed, 1, 0)) - normed
    blend = (normed + delta * vec_ref[2:3, :]).astype(BF16)
    tanh = jnp.tanh(nn(blend, down_ref[...]))
    latent = tanh.astype(BF16)
    lane = lax.broadcasted_iota(jnp.int32, latent.shape, 1)
    mixed = []
    for c in range(5):
        own = (lane >= c * RANK) & (lane < (c + 1) * RANK)
        offset = nt(jnp.where(own, latent, jnp.zeros_like(latent)), up_ref[...])
        mixed.append((normed + delta * (vec_ref[3 + c : 4 + c, :] + offset)).astype(BF16))
    dtanh = jnp.tanh(nn(mixed[0], ddown_ref[...]))
    m1_ref[...], m2_ref[...], m3_ref[...], m4_ref[...] = mixed[1:]
    dh_ref[...] = dtanh.astype(BF16)

    @pl.when(piece == 0)
    def _():
        normal_ref[...] = normal[:step]
        scale_ref[...] = jnp.broadcast_to(scale[:step], scale_ref.shape)
        delta_ref[...] = delta
        blend_ref[...] = blend
        m0_ref[...] = mixed[0]
        tanh_ref[...] = tanh
        dtanh_ref[...] = dtanh


def group_mixes(opening, x, before, vec, down, up, ddown, step):
    high, width = step + 16, x.shape[1]
    pieces = x.shape[0] // high

    def whole(value):
        return pl.BlockSpec(value.shape, lambda k: (0, 0))

    def own(columns, dtype):
        return (
            pl.BlockSpec((step, columns), lambda k: (0, 0)),
            jax.ShapeDtypeStruct((step, columns), dtype),
        )

    def every(columns, dtype):
        return (
            pl.BlockSpec((step, columns), lambda k: ((k % 2) * 2 + k // 2, 0)),
            jax.ShapeDtypeStruct((pieces * step, columns), dtype),
        )

    outs = [every(width, BF16)] * 4 + [
        every(DRANK, BF16),
        own(width, F32),
        own(128, F32),
        own(width, F32),
        own(width, BF16),
        own(width, BF16),
        own(5 * RANK, F32),
        own(DRANK, F32),
    ]
    return pl.pallas_call(
        mixes_kernel,
        grid=(pieces,),
        in_specs=[
            pl.BlockSpec(memory_space=pltpu.SMEM),
            pl.BlockSpec((high, width), lambda k: (k, 0)),
            whole(before),
            whole(vec),
            whole(down),
            whole(up),
            whole(ddown),
        ],
        out_specs=[o[0] for o in outs],
        out_shape=[o[1] for o in outs],
        compiler_params=pltpu.CompilerParams(vmem_limit_bytes=56 * 1024 * 1024),
    )(opening, x, before, vec, down, up, ddown)


def product(pairs, outs, body, sides=(), tile=256):
    count = len(pairs)

    def kernel(*refs):
        ins, out_refs = refs[: 2 * count + len(sides)], refs[2 * count + len(sides) :]
        products = [
            (nn if pair[2] == "nn" else nt)(ins[2 * i][...], ins[2 * i + 1][...])
            for i, pair in enumerate(pairs)
        ]
        results = body(*products, *[r[...] for r in ins[2 * count :]])
        for ref, value in zip(out_refs, results):
            ref[...] = value.astype(ref.dtype)

    specs, args = [], []
    for a, b, form, at in pairs:
        depth = a.shape[1]
        specs.append(pl.BlockSpec(a.shape, lambda j: (0, 0)))
        if form == "nn":
            specs.append(pl.BlockSpec((depth, tile), lambda j, at=at: (0, at + j)))
        else:
            specs.append(pl.BlockSpec((tile, depth), lambda j, at=at: (j, at)))
        args += [a, b]
    for side in sides:
        specs.append(pl.BlockSpec((side.shape[0], tile), lambda j: (0, j)))
    return pl.pallas_call(
        kernel,
        grid=(outs[0][1] // tile,),
        in_specs=specs,
        out_specs=[pl.BlockSpec((o[0], tile), lambda j: (0, j)) for o in outs],
        out_shape=[jax.ShapeDtypeStruct(o[:2], o[2]) for o in outs],
        compiler_params=pltpu.CompilerParams(vmem_limit_bytes=56 * 1024 * 1024),
    )(*args, *sides)


def local(fn, outs, *args, scalar=None):
    def kernel(*refs):
        lead = [] if scalar is None else [refs[0]]
        ins, out_refs = refs[len(lead) : -len(outs)], refs[-len(outs) :]
        scalars = [r[i] for r in lead for i in range(r.shape[0])]
        results = fn(*scalars, *[r[...] for r in ins])
        for ref, value in zip(out_refs, results):
            ref[...] = value.astype(ref.dtype)

    specs = [pl.BlockSpec(memory_space=pltpu.VMEM)] * len(args)
    if scalar is not None:
        specs = [pl.BlockSpec(memory_space=pltpu.SMEM)] + specs
        args = (scalar.reshape(-1), *args)
    return pl.pallas_call(
        kernel,
        in_specs=specs,
        out_specs=[pl.BlockSpec(memory_space=pltpu.VMEM)] * len(outs),
        out_shape=[jax.ShapeDtypeStruct(o[:2], o[2]) for o in outs],
        compiler_params=pltpu.CompilerParams(vmem_limit_bytes=56 * 1024 * 1024),
    )(*args)


def take_lanes(value, spans):
    if len(spans) == 1:
        return value
    return jnp.concatenate([value[:, a:b] for a, b in spans], axis=1)


def norm_back(grad, gain, normal, scale):
    e = grad * gain
    return scale * (
        e
        - jnp.mean(e, axis=-1, keepdims=True)
        - normal * jnp.mean(e * normal, axis=-1, keepdims=True)
    )


def rows_above(value, first):
    row = lax.broadcasted_iota(jnp.int32, value.shape, 0)
    return jnp.where(row == 0, first, pltpu.roll(value, 1, 0))


def rows_below(value, last):
    row = lax.broadcasted_iota(jnp.int32, value.shape, 0)
    high = value.shape[0]
    return jnp.where(row == high - 1, last, pltpu.roll(value, high - 1, 0))


def padded(rows):
    return jnp.concatenate(
        list(rows) + [jnp.zeros((8 - len(rows), rows[0].shape[1]), F32)], axis=0
    )


def column_sum(value):
    return jnp.sum(value, axis=0, keepdims=True)


def gates_kernel(
    spans, who_ref, middle_ref, value_ref, more_ref, act_ref, cot_ref,
    out_ref, up_ref, vg_ref, rg_ref, held,
):
    to_spans, from_spans = spans
    step, part = act_ref.shape[0] // 4, act_ref.shape[1]
    who = who_ref[0]
    act = [
        act_ref[pl.ds(pl.multiple_of((who ^ j) * step, step), step), :] for j in range(4)
    ]
    recept = jax.nn.sigmoid(take_lanes(jnp.concatenate(act, axis=1).astype(F32), to_spans))
    value = value_ref[...] + more_ref[...].astype(F32)
    out = middle_ref[...] + recept * value
    out_ref[...] = take_lanes(out, from_spans).astype(BF16)
    up = take_lanes(cot_ref[...].astype(F32), to_spans)
    up_ref[...] = up
    vg_ref[...] = (up * recept).astype(BF16)
    held[...] = take_lanes(up * value * recept * (1.0 - recept), from_spans)
    for k in range(4):
        at = pl.multiple_of((who ^ k) * part, part)
        rg_ref[k * step : (k + 1) * step, :] = held[:, pl.ds(at, part)].astype(BF16)


def gates(spans, who, middle, value, more, act, cot):
    step, width = middle.shape
    part = act.shape[1]
    shape = jax.ShapeDtypeStruct
    return pl.pallas_call(
        functools.partial(gates_kernel, spans),
        in_specs=[pl.BlockSpec(memory_space=pltpu.SMEM)]
        + [pl.BlockSpec(memory_space=pltpu.VMEM)] * 5,
        out_specs=[pl.BlockSpec(memory_space=pltpu.VMEM)] * 4,
        out_shape=[
            shape((step, width), BF16),
            shape((step, width), F32),
            shape((step, width), BF16),
            shape((4 * step, part), BF16),
        ],
        scratch_shapes=[pltpu.VMEM((step, width), F32)],
        compiler_params=pltpu.CompilerParams(vmem_limit_bytes=56 * 1024 * 1024),
    )(who.reshape(1), middle, value, more, act, cot)


def mixes_back_kernel(
    kept_ref, got_ref, dl_ref, dl_more_ref, delta_ref, tanh_ref, dtanh_ref, blend_ref, m0_ref,
    down_ref, up_ref, ddown_ref, vec_ref,
    rest_ref, dg_ref, row_ref, cols_ref, down_out, up_out, ddown_out,
):
    step = delta_ref.shape[0]
    dtanh = dtanh_ref[...]
    decay_grad = dl_ref[...] + dl_more_ref[...].astype(F32)
    decay_pre = (decay_grad * (1.0 - dtanh * dtanh)).astype(BF16)
    ddown_out[...] = tn(m0_ref[...], decay_pre)
    tanh = tanh_ref[...]
    latent = tanh.astype(BF16)
    lane = lax.broadcasted_iota(jnp.int32, latent.shape, 1)
    delta, up = delta_ref[...], up_ref[...]
    latent_grad = jnp.zeros(latent.shape, F32)
    up_grad = jnp.zeros(up_out.shape, F32)
    dg = jnp.zeros(delta.shape, F32)
    total = jnp.zeros(delta.shape, F32)
    cols = []
    for c in range(5):
        own = (lane >= c * RANK) & (lane < (c + 1) * RANK)
        mine = jnp.where(own, latent, jnp.zeros_like(latent))
        if c == 0:
            grad = nt(decay_pre, ddown_ref[...])
        else:
            at = slice((c - 1) * step, c * step)
            grad = kept_ref[at, :] + got_ref[at, :].astype(F32)
        shift = grad * delta
        cols.append(column_sum(shift))
        offset = shift.astype(BF16)
        latent_grad = jnp.where(own, nn(offset, up), latent_grad)
        up_grad = up_grad + tn(offset, mine)
        dg = dg + grad * (vec_ref[3 + c : 4 + c, :] + nt(mine, up))
        total = total + grad
    up_out[...] = up_grad
    mix_pre = (latent_grad * (1.0 - tanh * tanh)).astype(BF16)
    down_out[...] = tn(blend_ref[...], mix_pre)
    blend_grad = nt(mix_pre, down_ref[...])
    dg = dg + blend_grad * vec_ref[2:3, :]
    rest_ref[...] = total + blend_grad - dg
    dg_ref[...] = dg
    row_ref[...] = dg[:8]
    cols_ref[...] = padded([column_sum(blend_grad * delta)] + cols)


def mixes_back(*args):
    delta, down, ddown = args[4], args[9], args[11]
    step, width = delta.shape
    shape = jax.ShapeDtypeStruct
    outs = [
        shape((step, width), F32),
        shape((step, width), F32),
        shape((8, width), F32),
        shape((8, width), F32),
        shape(down.shape, F32),
        shape(down.shape, F32),
        shape(ddown.shape, F32),
    ]
    return pl.pallas_call(
        mixes_back_kernel,
        in_specs=[pl.BlockSpec(memory_space=pltpu.VMEM)] * len(args),
        out_specs=[pl.BlockSpec(memory_space=pltpu.VMEM)] * len(outs),
        out_shape=outs,
        compiler_params=pltpu.CompilerParams(vmem_limit_bytes=60 * 1024 * 1024),
    )(*args)


def tie(*values):
    return lax.optimization_barrier(values)


def on_device(
    count,
    tokens,
    previous,
    initial_state,
    mixing_weights,
    lowrank_weights,
    vectors,
    feedforward_weights,
    cotangent,
):
    fast = initial_state.shape[0] == 64
    masks = (1, 8) if fast else (1, 2)
    size = 1 << len(masks)
    teams = count // size
    all_masks = [1 << b for b in range(count.bit_length() - 1)]
    team_masks = [b for b in all_masks if b not in masks]
    far = 16
    team_masks.sort(key=lambda b: fast and b != far)
    me = lax.axis_index("seq")
    _, step, width = tokens.shape
    rows = mixing_weights.shape[0]
    part = width // size
    ff_part = FF // size
    team_rows = rows * size
    def bit_of(who, mask):
        return (who // mask) % 2 if isinstance(who, int) else lax.rem(lax.div(who, mask), 2)

    def member_of(who):
        return sum(bit_of(who, b) << j for j, b in enumerate(masks))

    def team_of(who):
        return sum(bit_of(who, b) << j for j, b in enumerate(team_masks))

    member, team = member_of(me), team_of(me)
    order = sorted(range(count), key=lambda d: (team_of(d), member_of(d)))
    inverse = sorted(range(count), key=lambda p: order[p])
    across = [order[m::size] for m in range(size)]
    square = [order[m :: 2 * size] for m in range(2 * size)]
    def lane_spans(blocks):
        spans = []
        for d in blocks:
            if spans and spans[-1][1] == d * rows:
                spans[-1][1] = (d + 1) * rows
            else:
                spans.append([d * rows, (d + 1) * rows])
        return spans

    to_spans, from_spans = lane_spans(order), lane_spans(inverse)

    def to_places(value, dtype):
        return move_lanes(to_spans, value, dtype)

    def flips(k):
        return sum(b for j, b in enumerate(masks) if (k >> j) & 1)

    def trade(value, mask):
        return lax.ppermute(value, "seq", [(d, d ^ mask) for d in range(count)])

    def group_gather(value):
        side = trade(value, masks[1])
        return value, side, trade(jnp.concatenate([value, side], axis=0), masks[0])

    def group_rows(value):
        high, columns = value.shape

        def lay(own, side, far):
            return (jnp.concatenate([own, far[:high], side, far[high:]], axis=0),)

        return local(lay, [(size * high, columns, value.dtype)], *group_gather(value))[0]

    def halves(value):
        cut = [value[k * step : (k + 1) * step] for k in range(size)]
        return [cut[0], cut[2]], [cut[1], cut[3]]

    def group_fold(kept, sent):
        high, columns = kept.shape[0] // 2, kept.shape[1]
        got = trade(sent, masks[0])

        def add(mine, more):
            total = mine + more.astype(F32)
            return total[:high], total[high:]

        return local(add, [(high, columns, F32), (high, columns, BF16)], kept, got)

    def group_sum(kept, sent):
        mine, side = group_fold(kept, sent)
        return mine, trade(side, masks[1])

    def crossing_sum(*pairs):
        units = len(pairs)

        def body(*products):
            parts = [halves(p) for p in products]
            kept = [p[0][i] for i in range(2) for p in parts]
            sent = [p[1][i] for i in range(2) for p in parts]
            return jnp.concatenate(kept, axis=0), jnp.concatenate(sent, axis=0)

        high = 2 * units * step
        return product(
            [(a, b, "nt", at) for a, b, at in pairs],
            [(high, width, F32), (high, width, BF16)],
            body,
            tile=512,
        )

    def exchange(pieces, meet=None):
        pieces, high = list(pieces), pieces[0].shape[0]
        for j in reversed(range(len(masks))):
            keys = [k for k in range(size) if (k >> j) & 1]
            got = trade(jnp.concatenate([pieces[k] for k in keys], axis=0), masks[j])
            if meet is not None and j == len(masks) - 1:
                got, meet = tie(got, meet)
            for i, k in enumerate(keys):
                pieces[k] = got[i * high : (i + 1) * high]
        return pieces if meet is None else (pieces, meet)

    def ordered(pieces):
        pieces = list(pieces)
        for j in range(len(masks)):
            swap = lax.rem(lax.div(member, 1 << j), 2) == 1
            pieces = [
                jnp.where(swap, pieces[k ^ (1 << j)], pieces[k]) for k in range(len(pieces))
            ]
        return pieces

    def neighbour(value, offset):
        pairs = [(d, d + offset) for d in range(count) if 0 <= d + offset < count]
        return lax.ppermute(value, "seq", pairs)

    def take_columns(value, spans, who):
        return jnp.concatenate(
            [
                lax.dynamic_slice_in_dim(value, start + who * wide, wide, axis=1)
                for start, wide in spans
            ],
            axis=1,
        )

    def group_columns(value, spans):
        pieces = [take_columns(value, spans, member ^ k) for k in range(size)]
        return jnp.concatenate(ordered(exchange(pieces)), axis=0)

    def crossing(first):
        bits = list(range(1, len(team_masks))) + [0]
        if first:
            bits[0], bits[1] = bits[1], bits[0]
        return bits

    def gather_rows(own):
        return lax.all_gather(own, "seq", axis=0, tiled=True, axis_index_groups=across)

    def far_send(own):
        return trade(own, far) if fast else own

    def far_join(own, got):
        if not fast:
            return own
        upper = bit_of(me, far) == 1
        return jnp.concatenate(
            [jnp.where(upper, got, own), jnp.where(upper, own, got)], axis=0
        )

    def gather_square(paired):
        groups = square if fast else across
        return lax.all_gather(paired, "seq", axis=0, tiled=True, axis_index_groups=groups)

    def team_products(*pairs):
        if fast:
            places = jnp.arange(teams, dtype=jnp.int32)
            return weight_grad(places, pairs, team_rows).reshape(width, -1)
        return jnp.concatenate([tn(x, y).astype(BF16) for x, y in pairs], axis=1)

    def square_sum(grads):
        groups = square if fast else across
        return lax.psum_scatter(
            grads, "seq", scatter_dimension=0, tiled=True, axis_index_groups=groups
        )

    def far_split(pair):
        if not fast:
            return pair, jnp.zeros_like(pair)
        bit = bit_of(me, far)
        sent = lax.dynamic_slice_in_dim(pair, (1 - bit) * team_rows, team_rows, axis=0)
        kept = lax.dynamic_slice_in_dim(pair, bit * team_rows, team_rows, axis=0)
        return kept, trade(sent, far)

    def far_add(kept, got):
        return (kept.astype(F32) + got.astype(F32)).astype(BF16)

    def cube_gather(value, leader=None):
        for mask in reversed(all_masks):
            got = trade(value, mask)
            upper = bit_of(me, mask) == 1
            value = jnp.stack([jnp.where(upper, got, value), jnp.where(upper, value, got)])
            if mask == 4 and leader is not None:
                value, leader = tie(value, leader)
        axes = len(all_masks)
        cube = value.transpose(*reversed(range(axes)), *range(axes, value.ndim))
        return cube if leader is None else (cube, leader)

    place_axes = [all_masks[::-1].index(b) for b in team_masks[::-1] + list(masks[::-1])]

    def by_place(cube):
        rest = range(len(all_masks), cube.ndim)
        return cube.transpose(*place_axes, *rest).reshape(width, -1)

    def to_cube(value):
        cube = value.reshape(*[2] * len(place_axes), rows, -1)
        back = [place_axes.index(a) for a in range(len(place_axes))]
        return cube.transpose(*back, len(back), len(back) + 1)

    def cube_sum(cube, kind, follower):
        for axis, mask in reversed(list(enumerate(reversed(all_masks)))):
            bit = bit_of(me, mask)
            sent = lax.dynamic_index_in_dim(cube, 1 - bit, axis, keepdims=False)
            kept = lax.dynamic_index_in_dim(cube, bit, axis, keepdims=False)
            cube = kept.astype(F32) + trade(sent.astype(kind), mask).astype(F32)
            if mask == all_masks[-1]:
                cube, follower = tie(cube, follower)
        return cube, follower

    def hand_rows(pieces, extra=None, meet=None):
        widths = [sum(p.shape[1] for p in piece) for piece in pieces]
        joint = jnp.concatenate([p for piece in pieces for p in piece], axis=1)
        mine = [
            lax.dynamic_slice_in_dim(joint, (member ^ k) * rows, rows, axis=0)
            for k in range(size)
        ]
        if extra is not None:
            mine = [jnp.concatenate([m, e], axis=1) for m, e in zip(mine, extra)]
        if meet is None:
            by_place = exchange(mine)
        else:
            by_place, meet = exchange(mine, meet)
        by_member = ordered(by_place)
        outs, start = [], 0
        for wide in widths:
            outs += [p[:, start : start + wide] for p in by_member]
            start += wide
        joined = jnp.concatenate(outs, axis=1).astype(F32)
        if extra is None:
            return joined
        return joined, [p[:, start:].astype(F32) for p in by_place], meet

    up_start, decay_start, decay_up = 5 * RANK, 10 * RANK, 10 * RANK + DRANK
    last_row = neighbour(tokens[0, -1:, :], 1)
    tokens_sent = to_places(
        jnp.concatenate([tokens[0], jnp.broadcast_to(last_row, (16, width))], axis=0), BF16
    )
    natural = cube_gather(
        jnp.concatenate(
            [vectors, initial_state, lowrank_weights[:, decay_up:].astype(F32)], axis=1
        )
    ).reshape(width, -1)
    tokens_all = jnp.concatenate(group_gather(tokens_sent), axis=0)
    mix_local = group_columns(mixing_weights, [(c * width, part) for c in range(5)])
    mix_kv, mix_rest = mix_local[:, : 2 * part], mix_local[:, 2 * part :]
    low_cube, kv_got = cube_gather(lowrank_weights[:, :decay_up], far_send(mix_kv))
    kv_got, mix_rest = tie(kv_got, mix_rest)
    feed_in, natural, low_cube, tokens_all = tie(
        feedforward_weights, natural, low_cube, tokens_all
    )
    lowrank = by_place(low_cube)
    w_kv = gather_square(far_join(mix_kv, kv_got))
    tiles = part // 256

    mine = lax.dynamic_slice_in_dim(natural, member * part, part, axis=0)
    vec_part = mine[:, :16].T
    first_state = mine[:, 16 : 16 + SPAN].T
    w_dup = mine[:, 16 + SPAN :].astype(BF16)
    vec = by_place(
        natural[:, :16].reshape(*[2] * len(all_masks), rows, 16)
    ).T
    wkv_rows = jnp.concatenate([vec_part[9:12], jnp.zeros((5, part), F32)], axis=0)
    is_first = (me == 0).astype(jnp.int32)
    before = to_places(previous.reshape(2, width), F32)
    w_down, w_up = lowrank[:, :up_start], lowrank[:, up_start:decay_start]
    w_ddown = lowrank[:, decay_start:]

    opening = jnp.stack(
        [jnp.bitwise_xor(me, flips(k)) == 0 for k in (0, 2, 1, 3)]
    ).astype(jnp.int32)
    (
        *mixed_all, dh_all, normal_one, scale_one, delta, blend, mixed_zero, mix_tanh, decay_tanh,
    ) = group_mixes(opening, tokens_all, before, vec, w_down, w_up, w_ddown, step)
    rest_got, mixed_all[0] = tie(far_send(mix_rest), mixed_all[0])
    w_rest = gather_square(far_join(mix_rest, rest_got))
    ff_spans = [(0, ff_part), (FF, part), (FF + width, ff_part)]
    ff_local = group_columns(feed_in, ff_spans)
    everyone = size * step
    (log_decay,) = product(
        [(dh_all, w_dup, "nt", 0)],
        [(everyone, part, F32)],
        lambda acc, base: (-jnp.exp(base + acc),),
        sides=(vec_part[8:9],),
    )
    keys, values = product(
        [(mixed_all[0], w_kv, "nn", 0), (mixed_all[1], w_kv, "nn", tiles)],
        [(everyone, part, F32)] * 2,
        lambda a, b: (a, b),
    )

    keys, ff_local = tie(keys, ff_local)
    ff_tail = ff_local[:, ff_part + part :]
    ff_near = ff_local[:, : ff_part + part]
    near_got = far_send(ff_near)

    call = functools.partial(block_call, chunks=size, step=step, width=part)
    (totals,) = call(
        totals_kernel, ins="ttt", outs=[("x", F32)], args=(keys, values, log_decay)
    )
    stages, current = [], [None, []]
    for mask in all_masks:
        if mask in masks:
            current[1].append(1 << masks.index(mask))
        else:
            stages.append(current)
            current = [mask, []]
    stages.append(current)
    high, long = SPAN + 8, SPAN + 16

    def chain(early, late):
        return early[0] * late[0], late[0] * early[1] + late[1]

    def pick(flag, yes, no):
        return tuple(jnp.where(flag, a, b) for a, b in zip(yes, no))

    def rows8(row):
        return jnp.broadcast_to(row, (8, part))

    def pack(items):
        return jnp.concatenate([r for d, v in items for r in (v, rows8(d))], axis=0)

    def unpack(array, count):
        cut = [array[i * high : (i + 1) * high] for i in range(count)]
        return [(c[SPAN : SPAN + 1], c[:SPAN]) for c in cut]

    def swap_members(who, pieces):
        pieces = list(pieces)
        for j in range(len(masks)):
            flag = (who // (1 << j)) % 2 == 1
            pieces = [jnp.where(flag, pieces[k ^ (1 << j)], pieces[k]) for k in range(size)]
        return pieces

    def neutral():
        return jnp.ones((1, part), F32), jnp.zeros((SPAN, part), F32)

    def flags_of(mask):
        bit = jnp.int32(0) if mask is None else bit_of(me, mask)
        return jnp.stack([member, bit]).astype(jnp.int32)

    keys_at, decays = list(range(size)), []
    open_bits = size - 1
    stage_arrays = [totals.reshape(size * high, part)]
    for index, (mask, merges) in enumerate(stages):
        last = index + 1 == len(stages)
        after_keys = keys_at
        for bit in merges:
            after_keys = [g for g in after_keys if not g & bit]

        def forward_stage(
            who, late, *arrays, mask=mask, merges=merges, groups=keys_at, bits=open_bits, last=last
        ):
            marks = []
            if mask is None:
                cut = [arrays[0][k * high : (k + 1) * high] for k in range(size)]
                total = {
                    m: (p[SPAN : SPAN + 1], p[:SPAN])
                    for m, p in enumerate(swap_members(who, cut))
                }
                chunks = [neutral() for _ in range(size)]
            else:
                total = dict(zip(groups, unpack(arrays[0], len(groups))))
                chunks = unpack(arrays[1], size)
                other = {}
                for i, g in enumerate(groups):
                    got = arrays[2][i * long : (i + 1) * long].astype(F32)
                    other[g] = got[SPAN : SPAN + 1] + got[SPAN + 8 : SPAN + 9], got[:SPAN]
                marks += [total[g][0] for g in groups] + [other[g][0] for g in groups]
                late = late == 1
                chunks = [
                    pick(late, chain(other[m & bits], c), c) for m, c in enumerate(chunks)
                ]
                total = {
                    g: pick(late, chain(other[g], total[g]), chain(total[g], other[g]))
                    for g in groups
                }
            for bit in merges:
                marks += [total[g][0] for g in total]
                chunks = [
                    chain(total[(m & bits) ^ bit], c) if m & bit else c
                    for m, c in enumerate(chunks)
                ]
                total = {g: chain(total[g], total[g | bit]) for g in total if not g & bit}
                bits ^= bit
            marks = jnp.concatenate([rows8(r) for r in marks], axis=0)
            if last:
                states = [d * arrays[-1] + v for d, v in chunks]
                return jnp.concatenate(swap_members(who, states), axis=0), marks
            sent = []
            for d, v in total.values():
                first = d.astype(BF16)
                rest = (d - first.astype(F32)).astype(BF16)
                sent += [v.astype(BF16), rows8(first), rows8(rest)]
            return (
                pack(list(total.values())), pack(chunks), jnp.concatenate(sent, axis=0), marks
            )

        count_marks = (0 if mask is None else 2 * len(keys_at)) + sum(
            len(keys_at) >> i for i in range(len(merges))
        )
        marks_out = (8 * count_marks, part, F32)
        if last:
            outs = [(size * SPAN, part, F32), marks_out]
            state_in, marks = local(
                forward_stage, outs, *stage_arrays, first_state, scalar=flags_of(mask)
            )
            state_in = state_in.reshape(size, SPAN, part)
        else:
            outs = [
                (len(after_keys) * high, part, F32),
                (size * high, part, F32),
                (len(after_keys) * long, part, BF16),
                marks_out,
            ]
            total, chunks, sent, marks = local(
                forward_stage, outs, *stage_arrays, scalar=flags_of(mask)
            )
            if mask == (2 if fast else 4):
                sent, near_got = tie(sent, near_got)
            stage_arrays = [total, chunks, trade(sent, stages[index + 1][0])]
        decays.append(marks)
        keys_at = after_keys
        for bit in merges:
            open_bits ^= bit
    w_near = gather_square(far_join(ff_near, near_got))
    w_key, w_rec = w_near, w_near[:, ff_part:]
    state_in, ff_tail = tie(state_in, ff_tail)
    val_got = far_send(ff_tail)

    receipt, gate_pre = product(
        [(mixed_all[2], w_rest, "nn", 0), (mixed_all[3], w_rest, "nn", tiles)],
        [(everyone, part, F32)] * 2,
        lambda a, b: (a, b),
    )
    wkv, gated = call(
        forward_kernel,
        ins="tttttsp",
        outs=[("t", F32), ("t", BF16)],
        args=(receipt, keys, values, log_decay, gate_pre, state_in, wkv_rows),
    )
    gated, val_got = tie(gated, val_got)
    w_val = gather_square(far_join(ff_tail, val_got))
    branch, branch_more = group_sum(*crossing_sum((gated, w_rest, 2)))

    def norm_two(hidden, mine, more, vec):
        middle = hidden[:step].astype(F32) + mine + more.astype(F32)
        centred = middle - jnp.mean(middle, axis=-1, keepdims=True)
        scale = lax.rsqrt(jnp.mean(centred * centred, axis=-1, keepdims=True) + LN_EPS)
        normal = centred * scale
        tail = normal[step - 8 :] * vec[12:13] + vec[13:14]
        return middle, normal, jnp.broadcast_to(scale, (step, 128)), tail

    whole = (step, width, F32)
    middle, normal_two, scale_two, tail_two = local(
        norm_two,
        [whole, whole, (step, 128, F32), (8, width, F32)],
        tokens_sent,
        branch,
        branch_more,
        vec,
    )

    def mix_two(first, normal, arrived, before, vec):
        normed = normal * vec[12:13] + vec[13:14]
        above = jnp.where(first == 1, before[1:2], arrived[7:8])
        delta = rows_above(normed, above) - normed
        key_in, recv_in = normed + delta * vec[14:15], normed + delta * vec[15:16]
        return jnp.concatenate([key_in, recv_in], axis=0), delta

    both, delta_two = local(
        mix_two,
        [(2 * step, width, BF16), whole],
        normal_two,
        neighbour(tail_two, 1),
        before,
        vec,
        scalar=is_first,
    )

    key_all, recv_all = group_rows(both[:step]), group_rows(both[step:])
    relu, squared = product(
        [(key_all, w_key, "nn", 0)],
        [(everyone, ff_part, F32), (everyone, ff_part, BF16)],
        lambda acc: (jnp.maximum(acc, 0.0), jnp.square(jnp.maximum(acc, 0.0))),
        tile=ff_part // 2,
    )
    (recept_act,) = product(
        [(recv_all, w_rec, "nn", 0)],
        [(everyone, part, BF16)],
        lambda acc: (acc,),
    )
    squared, recept_act = tie(squared, recept_act)
    acts = exchange([recept_act[k * step : (k + 1) * step] for k in range(size)])
    value, value_more = group_sum(*crossing_sum((squared, w_val, 0)))
    block_output, upstream, value_grad, recept_grads = gates(
        (to_spans, from_spans),
        member,
        middle,
        value,
        value_more,
        jnp.concatenate(acts, axis=0),
        cotangent.reshape(step, width),
    )

    rg_all = jnp.concatenate(
        exchange([recept_grads[k * step : (k + 1) * step] for k in range(size)]), axis=0
    )
    vg_all = group_rows(value_grad)
    val_grads = team_products((vg_all, squared))
    vg_all, val_grads, rg_all = tie(vg_all, val_grads, rg_all)
    val_pair = square_sum(val_grads)
    (key_grad,) = product(
        [(vg_all, w_val, "nn", 0)],
        [(everyone, ff_part, BF16)],
        lambda acc, relu: (acc * (2.0 * relu),),
        sides=(relu,),
        tile=ff_part // 2,
    )
    key_grads = team_products((key_all, key_grad))
    key_grad, key_grads = tie(key_grad, key_grads)
    key_pair = square_sum(key_grads)
    recv_two = group_sum(*crossing_sum((rg_all, w_rec, 0)))
    key_two = group_sum(*crossing_sum((key_grad, w_key, 0)))

    def inputs_back(key, key_more, recv, recv_more, vec):
        key, recv = key + key_more.astype(F32), recv + recv_more.astype(F32)
        top = key[:8] * vec[14:15] + recv[:8] * vec[15:16]
        return jnp.concatenate([key, recv], axis=0), top

    in_grads, top_two = local(
        inputs_back, [(2 * step, width, F32), (8, width, F32)], *key_two, *recv_two, vec
    )
    last_flag = (me == count - 1).astype(jnp.int32)

    def norm_two_back(last, grads, arrived, upstream, normal, scale, delta, vec):
        key_grad, recv_grad = grads[:step], grads[step:]
        shifted = key_grad * vec[14:15] + recv_grad * vec[15:16]
        below = jnp.where(last == 1, jnp.zeros_like(arrived[:1]), arrived[:1])
        grad = (
            key_grad * (1.0 - vec[14:15])
            + recv_grad * (1.0 - vec[15:16])
            + rows_below(shifted, below)
        )
        out = upstream + norm_back(grad, vec[12:13], normal, scale[:, :1])
        cols = padded(
            [
                column_sum(grad * normal),
                column_sum(grad),
                column_sum(key_grad * delta),
                column_sum(recv_grad * delta),
            ]
        )
        return out, out, cols

    middle_grad, branch_grad, cols_two = local(
        norm_two_back,
        [whole, (step, width, BF16), (8, width, F32)],
        in_grads,
        neighbour(top_two, -1),
        upstream,
        normal_two,
        scale_two,
        delta_two,
        vec,
        scalar=last_flag,
    )

    bg_all = group_rows(branch_grad)
    (gated_grad,) = product(
        [(bg_all, w_rest, "nn", 2 * tiles)], [(everyone, part, F32)], lambda acc: (acc,)
    )
    gate_grad, wkv_grad, ends = call(
        gate_kernel,
        ins="tttttp",
        outs=[("t", BF16), ("t", F32), ("x", F32)],
        args=(gated_grad, gate_pre, wkv, receipt, log_decay, wkv_rows),
    )
    val_kept, val_got = far_split(val_pair)
    keys_at, open_bits = list(range(size)), size - 1
    stage_arrays = [ends.reshape(size * high, part)]
    for index, (mask, merges) in enumerate(stages):
        last = index + 1 == len(stages)
        after_keys = keys_at
        for bit in merges:
            after_keys = [g for g in after_keys if not g & bit]

        def backward_stage(
            who, late, *arrays, mask=mask, merges=merges, groups=keys_at, bits=open_bits, last=last
        ):
            marks = [arrays[-1][i * 8 : i * 8 + 1] for i in range(arrays[-1].shape[0] // 8)]
            if mask is None:
                cut = [arrays[0][k * high : k * high + SPAN] for k in range(size)]
                total = dict(enumerate(swap_members(who, cut)))
                chunks = [neutral() for _ in range(size)]
            else:
                total = {g: arrays[0][i * SPAN : (i + 1) * SPAN] for i, g in enumerate(groups)}
                chunks = unpack(arrays[1], size)
                other = {
                    g: arrays[2][i * SPAN : (i + 1) * SPAN].astype(F32)
                    for i, g in enumerate(groups)
                }
                here = dict(zip(groups, marks))
                there = dict(zip(groups, marks[len(groups) :]))
                marks = marks[2 * len(groups) :]
                early = late == 0
                chunks = [
                    pick(
                        early,
                        (d * there[m & bits], d * other[m & bits] + v),
                        (d, v),
                    )
                    for m, (d, v) in enumerate(chunks)
                ]
                total = {
                    g: jnp.where(
                        early,
                        total[g] + here[g] * other[g],
                        other[g] + there[g] * total[g],
                    )
                    for g in groups
                }
            for bit in merges:
                here = dict(zip(total, marks))
                marks = marks[len(total) :]
                chunks = [
                    (d, v)
                    if m & bit
                    else (d * here[(m & bits) | bit], d * total[(m & bits) | bit] + v)
                    for m, (d, v) in enumerate(chunks)
                ]
                total = {
                    g: total[g] + here[g] * total[g | bit] for g in total if not g & bit
                }
                bits ^= bit
            joint = jnp.concatenate(list(total.values()), axis=0)
            if last:
                grads = swap_members(who, [v for _, v in chunks])
                return jnp.concatenate(grads, axis=0), joint.T
            return joint, pack(chunks), joint

        if last:
            outs = [(size * SPAN, part, F32), (part, SPAN, F32)]
            grad_out, first_grad = local(
                backward_stage, outs, *stage_arrays, decays[index], scalar=flags_of(mask)
            )
            grad_out = grad_out.reshape(size, SPAN, part)
        else:
            outs = [
                (len(after_keys) * SPAN, part, F32),
                (size * high, part, F32),
                (len(after_keys) * SPAN, part, BF16),
            ]
            total, chunks, sent = local(
                backward_stage, outs, *stage_arrays, decays[index], scalar=flags_of(mask)
            )
            if mask == (2 if fast else 4):
                sent, val_got = tie(sent, val_got)
            stage_arrays = [total, chunks, trade(sent, stages[index + 1][0])]
        keys_at = after_keys
        for bit in merges:
            open_bits ^= bit
    out_grads = team_products((bg_all, gated), (recv_all, rg_all), (mixed_all[3], gate_grad))
    grad_out, out_grads = tie(grad_out, out_grads)
    out_pair = square_sum(out_grads)

    d_receipt, d_keys, d_values, d_decay, extra = call(
        backward_kernel,
        ins="tttttssp",
        outs=[("t", BF16)] * 4 + [("e", F32)],
        args=(receipt, keys, values, log_decay, wkv_grad, state_in, grad_out, wkv_rows),
    )
    grads = [d_keys, d_values, d_receipt, gate_grad]
    kept, sent = crossing_sum(
        *[(grads[c], w_rest if c > 1 else w_kv, c % 2) for c in range(4)]
    )
    main_grads = team_products(
        (mixed_all[0], d_keys), (mixed_all[1], d_values), (mixed_all[2], d_receipt)
    )

    def latent_back(grad, up):
        kept, sent = halves(nn(grad, up))
        return jnp.concatenate(kept, axis=0), jnp.concatenate(sent, axis=0)

    latent_mine, latent_more = group_sum(
        *local(
            latent_back, [(2 * step, DRANK, F32), (2 * step, DRANK, BF16)], d_decay, w_dup
        )
    )
    key_kept, key_got = far_split(key_pair)
    sent, main_grads, latent_more, key_got = tie(sent, main_grads, latent_more, key_got)
    main_pair = square_sum(main_grads)
    mixed_mine, mixed_more = group_sum(kept, sent)
    mixed_more, out_pair = tie(mixed_more, out_pair)
    out_kept, out_got = far_split(out_pair)
    val_sum, key_sum = far_add(val_kept, val_got), far_add(key_kept, key_got)
    rest_grad, delta_grad, top_one, cols_mix, down_grad, up_grad, ddown_grad = mixes_back(
        mixed_mine,
        mixed_more,
        latent_mine,
        latent_more,
        delta,
        mix_tanh,
        decay_tanh,
        blend,
        mixed_zero,
        w_down,
        w_up,
        w_ddown,
        vec,
    )
    rest_grad, main_pair, out_got = tie(rest_grad, main_pair, out_got)
    out_sum = far_add(out_kept, out_got)

    def norm_one_back(last, rest, shifted, arrived, normal, scale, middle, vec):
        below = jnp.where(last == 1, jnp.zeros_like(arrived[:1]), arrived[:1])
        grad = rest + rows_below(shifted, below)
        out = middle + norm_back(grad, vec[0:1], normal, scale[:, :1])
        cols = padded([column_sum(grad * normal), column_sum(grad)])
        return take_lanes(out, from_spans), cols

    block_input_gradient, cols_one = local(
        norm_one_back,
        [whole, (8, width, F32)],
        rest_grad,
        delta_grad,
        neighbour(top_one, -1),
        normal_one,
        scale_one,
        middle_grad,
        vec,
        scalar=last_flag,
    )
    main_kept, main_got = far_split(main_pair)


    def spread(value):
        zero = jnp.zeros((width, value.shape[1]), F32)
        return lax.dynamic_update_slice_in_dim(zero, value, member * part, axis=0)

    vec_low = jnp.concatenate([cols_one[:2], cols_mix[:6], cols_two[:4]], axis=0)
    vec_head = jnp.concatenate(
        [jnp.sum(extra[:, :2], axis=0), jnp.sum(ends[:, SPAN : SPAN + 2], axis=0)], axis=0
    )
    by_feature = jnp.concatenate([down_grad, up_grad, ddown_grad, vec_low.T], axis=1)
    by_channel = spread(jnp.concatenate([tn(d_decay, dh_all), vec_head.T], axis=1))
    low, main_got = cube_sum(
        jnp.concatenate(
            [to_cube(by_feature), by_channel.reshape(*[2] * len(all_masks), rows, -1)], axis=-1
        ),
        BF16,
        main_got,
    )
    main_sum = far_add(main_kept, main_got)

    def column_parts(value):
        return [value[:, c * part : (c + 1) * part] for c in range(3)]

    out_cols, main_cols = column_parts(out_sum), column_parts(main_sum)
    holder = lax.div(me * rows, part)

    def rows_of(who):
        mine = lax.dynamic_slice_in_dim(first_grad, lax.rem(who * rows, part), rows, axis=0)
        high = lax.reduce_precision(mine, 8, 7)
        return jnp.concatenate([high, mine - high], axis=1).astype(BF16)

    feedforward_gradient, handed, low = hand_rows(
        [[key_sum], [out_cols[1]], [val_sum]],
        [rows_of(jnp.bitwise_xor(me, flips(k))) for k in range(size)],
        low,
    )
    state_rows = handed[0]
    for k in range(1, size):
        state_rows = jnp.where(holder == (member ^ k), handed[k], state_rows)
    initial_state_gradient = state_rows[:, :SPAN] + state_rows[:, SPAN:]
    mixing_gradient = hand_rows([[m] for m in main_cols] + [[out_cols[2]], [out_cols[0]]])

    vec_at = decay_up + 12
    lowrank_gradient = jnp.concatenate(
        [low[:, :decay_up], low[:, vec_at : vec_at + DRANK]], axis=1
    )
    vectors_gradient = jnp.concatenate(
        [low[:, decay_up : decay_up + 8], low[:, vec_at + DRANK :], low[:, decay_up + 8 : vec_at]],
        axis=1,
    )
    return (
        block_output.reshape(1, step, width),
        block_input_gradient.reshape(1, step, width),
        initial_state_gradient,
        mixing_gradient,
        lowrank_gradient,
        vectors_gradient,
        feedforward_gradient,
    )


def solution(mesh):
    rowwise = P("seq", None)
    tokenwise = P(None, "seq", None)
    return jax.shard_map(
        functools.partial(on_device, mesh.shape["seq"]),
        mesh=mesh,
        in_specs=(tokenwise, P(), rowwise, rowwise, rowwise, rowwise, rowwise, tokenwise),
        out_specs=(tokenwise, tokenwise, rowwise, rowwise, rowwise, rowwise, rowwise),
        check_vma=False,
    )
```

```python
import functools

import jax
import jax.numpy as jnp
from jax import lax
from jax.experimental import pallas as pl
from jax.experimental.pallas import tpu as pltpu
from jax.sharding import PartitionSpec as P

HEADS = 32
SPAN = 64
FF = 7168
RANK = 32
DRANK = 64
LN_EPS = 1e-05
GN_EPS = 0.00064

F32 = jnp.float32
BF16 = jnp.bfloat16
HI = lax.Precision.HIGHEST


def nn(a, b):
    return jnp.dot(a, b, preferred_element_type=F32)


def nt(a, b):
    return lax.dot_general(a, b, (((1,), (1,)), ((), ())), preferred_element_type=F32)


def tn(a, b):
    return lax.dot_general(a, b, (((0,), (0,)), ((), ())), preferred_element_type=F32)


def knn(a, b):
    return lax.dot_general(
        a, b, (((1,), (0,)), ((), ())), preferred_element_type=F32
    )


def knt(a, b):
    return lax.dot_general(
        a, b, (((1,), (1,)), ((), ())), preferred_element_type=F32
    )


def ktn(a, b):
    return lax.dot_general(
        a, b, (((0,), (0,)), ((), ())), preferred_element_type=F32
    )


def low_lanes(shape):
    return lax.broadcasted_iota(jnp.int32, shape, len(shape) - 1) < SPAN


def head_sum(x):
    low = low_lanes(x.shape)
    s0 = jnp.sum(jnp.where(low, x, 0.0), axis=-1, keepdims=True)
    s1 = jnp.sum(jnp.where(low, 0.0, x), axis=-1, keepdims=True)
    return jnp.where(low, s0, s1)


def two_rows(x):
    low = low_lanes(x.shape)
    return jnp.concatenate([jnp.where(low, x, 0.0), jnp.where(low, 0.0, x)], axis=0)


def fold(full):
    return jnp.where(low_lanes((SPAN, 2 * SPAN)), full[:SPAN], full[SPAN:])


def unfold(state):
    low = low_lanes(state.shape)
    return jnp.concatenate([jnp.where(low, state, 0.0), jnp.where(low, 0.0, state)], axis=0)


def running(w, upper=False):
    count = w.shape[0]
    row = lax.broadcasted_iota(jnp.int32, (count, count), 0)
    col = lax.broadcasted_iota(jnp.int32, (count, count), 1)
    keep = (col >= row) if upper else (col <= row)
    return lax.dot_general(
        jnp.where(keep, 1.0, 0.0).astype(F32),
        w,
        (((1,), (0,)), ((), ())),
        precision=HI,
        preferred_element_type=F32,
    )


def strict(count):
    row = lax.broadcasted_iota(jnp.int32, (2 * count, count), 0)
    col = lax.broadcasted_iota(jnp.int32, (2 * count, count), 1)
    row = jnp.where(row >= count, row - count, row)
    return row > col, row == col


def affinity(r, k, u, q, ks):
    count = r.shape[0]
    below, diag = strict(count)
    raw = knt(two_rows(q), ks)
    share = jnp.sum(two_rows(r * u * k), axis=-1, keepdims=True)
    return jnp.where(below, raw, jnp.where(diag, share, 0.0))


def totals_kernel(k_ref, v_ref, w_ref, out_ref):
    cum = running(w_ref[...])
    total = cum[-1:, :]
    kc = k_ref[...] * jnp.exp(total - cum)
    out_ref[0, :SPAN, :] = fold(ktn(v_ref[...], kc))
    out_ref[0, SPAN:, :] = jnp.broadcast_to(jnp.exp(total), (8, 2 * SPAN))


def group_norm(y, gain, bias):
    centred = y - head_sum(y) * (1.0 / SPAN)
    spread = head_sum(centred * centred) * (1.0 / SPAN)
    scale = lax.rsqrt(spread + GN_EPS)
    normal = centred * scale
    return normal, scale, normal * gain + bias


def forward_kernel(r_ref, k_ref, v_ref, w_ref, g_ref, s_ref, p_ref, y_ref, gated_ref):
    r, k, v, w = r_ref[...], k_ref[...], v_ref[...], w_ref[...]
    cum = running(w)
    q = r * jnp.exp(cum - w)
    ks = k * jnp.exp(-cum)
    aff = affinity(r, k, p_ref[0:1, :], q, ks)
    count = r.shape[0]
    v2 = two_rows(v)
    y = (
        knt(q, unfold(s_ref[0]))
        + knn(aff[:count], v2[:count])
        + knn(aff[count:], v2[count:])
    )
    y_ref[...] = y
    gate = g_ref[...]
    _, _, grouped = group_norm(y, p_ref[1:2, :], p_ref[2:3, :])
    gated_ref[...] = (grouped * gate * jax.nn.sigmoid(gate)).astype(BF16)


def gate_kernel(gg_ref, g_ref, y_ref, r_ref, w_ref, p_ref, gate_ref, dy_ref, out_ref):
    gated_grad, gate, y = gg_ref[...], g_ref[...], y_ref[...]
    gain = p_ref[1:2, :]
    normal, scale, grouped = group_norm(y, gain, p_ref[2:3, :])
    sig = jax.nn.sigmoid(gate)
    gate_ref[...] = (gated_grad * grouped * sig * (1.0 + gate * (1.0 - sig))).astype(BF16)
    outer = gated_grad * gate * sig
    inner = outer * gain
    dy = scale * (
        inner
        - head_sum(inner) * (1.0 / SPAN)
        - normal * (head_sum(inner * normal) * (1.0 / SPAN))
    )
    dy_ref[...] = dy
    w = w_ref[...]
    q = r_ref[...] * jnp.exp(running(w) - w)
    out_ref[0, :SPAN, :] = fold(ktn(dy, q))
    gain_grad = jnp.sum(outer * normal, axis=0, keepdims=True)
    bias_grad = jnp.sum(outer, axis=0, keepdims=True)
    out_ref[0, SPAN:, :] = jnp.concatenate(
        [gain_grad, bias_grad, jnp.zeros((6, 2 * SPAN), F32)], axis=0
    )


def backward_kernel(
    r_ref, k_ref, v_ref, w_ref, dy_ref, s_ref, gs_ref, p_ref,
    dr_ref, dk_ref, dv_ref, dd_ref, out_ref,
):
    r, k, v, w, dy = r_ref[...], k_ref[...], v_ref[...], w_ref[...], dy_ref[...]
    u = p_ref[0:1, :]
    count = r.shape[0]
    cum = running(w)
    total = cum[-1:, :]
    e_before, e_minus, e_carry = jnp.exp(cum - w), jnp.exp(-cum), jnp.exp(total - cum)
    q, ks, kc = r * e_before, k * e_minus, k * e_carry
    aff = affinity(r, k, u, q, ks)
    below, _ = strict(count)
    dy2 = two_rows(dy)
    d_aff = jnp.where(below, knt(dy2, v), 0.0)
    own = head_sum(dy * v)
    state, grad_state = s_ref[0], gs_ref[0]
    state2, grad2 = unfold(state), unfold(grad_state)
    ks2 = two_rows(ks)
    dq = knn(dy, state2) + knn(d_aff[:count], ks2[:count]) + knn(d_aff[count:], ks2[count:])
    dks = ktn(d_aff, two_rows(q))
    dkc = knn(v, grad2)
    dv_ref[...] = (ktn(aff, dy2) + knt(kc, grad2)).astype(BF16)
    dr_ref[...] = (dq * e_before + own * u * k).astype(BF16)
    dk_ref[...] = (dks * e_minus + dkc * e_carry + own * u * r).astype(BF16)
    gq, gc = q * dq, kc * dkc
    d_total = jnp.sum(gc, axis=0, keepdims=True) + jnp.exp(total) * jnp.sum(
        state * grad_state, axis=0, keepdims=True
    )
    dw = running(gq - ks * dks - gc, upper=True) - gq + d_total
    term = dw * w
    dd_ref[...] = term.astype(BF16)
    out_ref[0] = jnp.concatenate(
        [
            jnp.sum(term, axis=0, keepdims=True),
            jnp.sum(own * r * k, axis=0, keepdims=True),
            jnp.zeros((6, 2 * SPAN), F32),
        ],
        axis=0,
    )


def block_call(kernel, chunks, step, width, ins, outs, args):
    lane = 2 * SPAN
    kinds = {
        "t": pl.BlockSpec((step, lane), lambda c, h: (c, h)),
        "s": pl.BlockSpec((1, SPAN, lane), lambda c, h: (c, 0, h)),
        "x": pl.BlockSpec((1, SPAN + 8, lane), lambda c, h: (c, 0, h)),
        "e": pl.BlockSpec((1, 8, lane), lambda c, h: (c, 0, h)),
        "p": pl.BlockSpec((8, lane), lambda c, h: (0, h)),
    }
    shapes = {
        "t": lambda d: jax.ShapeDtypeStruct((chunks * step, width), d),
        "x": lambda d: jax.ShapeDtypeStruct((chunks, SPAN + 8, width), d),
        "e": lambda d: jax.ShapeDtypeStruct((chunks, 8, width), d),
    }
    return pl.pallas_call(
        kernel,
        grid=(chunks, width // lane),
        in_specs=[kinds[kind] for kind in ins],
        out_specs=[kinds[kind] for kind, _ in outs],
        out_shape=[shapes[kind](dtype) for kind, dtype in outs],
        compiler_params=pltpu.CompilerParams(vmem_limit_bytes=48 * 1024 * 1024),
    )(*args)


def weight_grad(places, pairs, block):
    tokens, blocks = pairs[0][0].shape[0], places.shape[0]
    widths = [y.shape[1] for _, y in pairs]

    def kernel(_, *refs):
        at = 0
        for i, wide in enumerate(widths):
            refs[-1][0, :, at : at + wide] = tn(refs[2 * i][...], refs[2 * i + 1][...]).astype(
                BF16
            )
            at += wide

    specs = []
    for wide in widths:
        specs.append(pl.BlockSpec((tokens, block), lambda i, at: (0, at[i])))
        specs.append(pl.BlockSpec((tokens, wide), lambda i, at: (0, 0)))
    return pl.pallas_call(
        kernel,
        grid_spec=pltpu.PrefetchScalarGridSpec(
            num_scalar_prefetch=1,
            grid=(blocks,),
            in_specs=specs,
            out_specs=pl.BlockSpec((1, block, sum(widths)), lambda i, at: (i, 0, 0)),
        ),
        out_shape=jax.ShapeDtypeStruct((blocks, block, sum(widths)), BF16),
        compiler_params=pltpu.CompilerParams(vmem_limit_bytes=48 * 1024 * 1024),
    )(places, *[v for pair in pairs for v in pair])


def lanes_kernel(spans, x_ref, out_ref):
    at = 0
    for start, stop in spans:
        out_ref[:, at : at + stop - start] = x_ref[:, start:stop].astype(out_ref.dtype)
        at += stop - start


def move_lanes(spans, value, dtype):
    return pl.pallas_call(
        functools.partial(lanes_kernel, spans),
        in_specs=[pl.BlockSpec(memory_space=pltpu.VMEM)],
        out_specs=pl.BlockSpec(memory_space=pltpu.VMEM),
        out_shape=jax.ShapeDtypeStruct(value.shape, dtype),
        compiler_params=pltpu.CompilerParams(vmem_limit_bytes=32 * 1024 * 1024),
    )(value)


def place_kernel(counts, wide, block, at_ref, *refs):
    ins, out_ref, sems = refs[: len(counts)], refs[-2], refs[-1]
    rows = out_ref.shape[0]
    copies, i = [], 0
    for ref, n in zip(ins, counts):
        for j in range(n):
            start = pl.multiple_of(at_ref[i] * block, block)
            column = i * block // rows * wide
            copy = pltpu.make_async_copy(
                ref.at[pl.ds(j * block, block), :],
                out_ref.at[pl.ds(start, block), pl.ds(column, wide)],
                sems.at[i],
            )
            copy.start()
            copies.append(copy)
            i += 1
    for copy in copies:
        copy.wait()


def place_rows(parts, block):
    pieces = [p for part in parts for p in part[1]]
    wide = pieces[0].shape[1]
    at = jnp.concatenate([part[0] for part in parts])
    counts = [p.shape[0] // block for p in pieces]
    total = sum(counts)
    return pl.pallas_call(
        functools.partial(place_kernel, counts, wide, block),
        in_specs=[pl.BlockSpec(memory_space=pltpu.SMEM)]
        + [pl.BlockSpec(memory_space=pl.ANY)] * len(pieces),
        out_specs=pl.BlockSpec(memory_space=pl.ANY),
        out_shape=jax.ShapeDtypeStruct(
            (total * block // len(parts), wide * len(parts)), pieces[0].dtype
        ),
        scratch_shapes=[pltpu.SemaphoreType.DMA((total,))],
        compiler_params=pltpu.CompilerParams(vmem_limit_bytes=32 * 1024 * 1024),
    )(at, *pieces)


def mixes_kernel(
    open_ref, x_ref, before_ref, vec_ref, down_ref, up_ref, ddown_ref,
    m1_ref, m2_ref, m3_ref, m4_ref, dh_ref,
    normal_ref, scale_ref, delta_ref, blend_ref, m0_ref, tanh_ref, dtanh_ref,
):
    piece = pl.program_id(0)
    step = m1_ref.shape[0]
    x = x_ref[...].astype(F32)
    centred = x - jnp.mean(x, axis=-1, keepdims=True)
    scale = lax.rsqrt(jnp.mean(centred * centred, axis=-1, keepdims=True) + LN_EPS)
    normal = centred * scale
    full = normal * vec_ref[0:1, :] + vec_ref[1:2, :]
    normed = full[:step]
    first = jnp.where(open_ref[piece] == 1, before_ref[0:1, :], full[step : step + 1])
    row = lax.broadcasted_iota(jnp.int32, normed.shape, 0)
    delta = jnp.where(row == 0, first, pltpu.roll(normed, 1, 0)) - normed
    blend = (normed + delta * vec_ref[2:3, :]).astype(BF16)
    tanh = jnp.tanh(nn(blend, down_ref[...]))
    latent = tanh.astype(BF16)
    lane = lax.broadcasted_iota(jnp.int32, latent.shape, 1)
    mixed = []
    for c in range(5):
        own = (lane >= c * RANK) & (lane < (c + 1) * RANK)
        offset = nt(jnp.where(own, latent, jnp.zeros_like(latent)), up_ref[...])
        mixed.append((normed + delta * (vec_ref[3 + c : 4 + c, :] + offset)).astype(BF16))
    dtanh = jnp.tanh(nn(mixed[0], ddown_ref[...]))
    m1_ref[...], m2_ref[...], m3_ref[...], m4_ref[...] = mixed[1:]
    dh_ref[...] = dtanh.astype(BF16)

    @pl.when(piece == 0)
    def _():
        normal_ref[...] = normal[:step]
        scale_ref[...] = jnp.broadcast_to(scale[:step], scale_ref.shape)
        delta_ref[...] = delta
        blend_ref[...] = blend
        m0_ref[...] = mixed[0]
        tanh_ref[...] = tanh
        dtanh_ref[...] = dtanh


def group_mixes(opening, x, before, vec, down, up, ddown, step):
    high, width = step + 16, x.shape[1]
    pieces = x.shape[0] // high

    def whole(value):
        return pl.BlockSpec(value.shape, lambda k: (0, 0))

    def own(columns, dtype):
        return (
            pl.BlockSpec((step, columns), lambda k: (0, 0)),
            jax.ShapeDtypeStruct((step, columns), dtype),
        )

    def every(columns, dtype):
        return (
            pl.BlockSpec((step, columns), lambda k: ((k % 2) * 2 + k // 2, 0)),
            jax.ShapeDtypeStruct((pieces * step, columns), dtype),
        )

    outs = [every(width, BF16)] * 4 + [
        every(DRANK, BF16),
        own(width, F32),
        own(128, F32),
        own(width, F32),
        own(width, BF16),
        own(width, BF16),
        own(5 * RANK, F32),
        own(DRANK, F32),
    ]
    return pl.pallas_call(
        mixes_kernel,
        grid=(pieces,),
        in_specs=[
            pl.BlockSpec(memory_space=pltpu.SMEM),
            pl.BlockSpec((high, width), lambda k: (k, 0)),
            whole(before),
            whole(vec),
            whole(down),
            whole(up),
            whole(ddown),
        ],
        out_specs=[o[0] for o in outs],
        out_shape=[o[1] for o in outs],
        compiler_params=pltpu.CompilerParams(vmem_limit_bytes=56 * 1024 * 1024),
    )(opening, x, before, vec, down, up, ddown)


def product(pairs, outs, body, sides=(), tile=256):
    count = len(pairs)

    def kernel(*refs):
        ins, out_refs = refs[: 2 * count + len(sides)], refs[2 * count + len(sides) :]
        products = [
            (nn if pair[2] == "nn" else nt)(ins[2 * i][...], ins[2 * i + 1][...])
            for i, pair in enumerate(pairs)
        ]
        results = body(*products, *[r[...] for r in ins[2 * count :]])
        for ref, value in zip(out_refs, results):
            ref[...] = value.astype(ref.dtype)

    specs, args = [], []
    for a, b, form, at in pairs:
        depth = a.shape[1]
        specs.append(pl.BlockSpec(a.shape, lambda j: (0, 0)))
        if form == "nn":
            specs.append(pl.BlockSpec((depth, tile), lambda j, at=at: (0, at + j)))
        else:
            specs.append(pl.BlockSpec((tile, depth), lambda j, at=at: (j, at)))
        args += [a, b]
    for side in sides:
        specs.append(pl.BlockSpec((side.shape[0], tile), lambda j: (0, j)))
    return pl.pallas_call(
        kernel,
        grid=(outs[0][1] // tile,),
        in_specs=specs,
        out_specs=[pl.BlockSpec((o[0], tile), lambda j: (0, j)) for o in outs],
        out_shape=[jax.ShapeDtypeStruct(o[:2], o[2]) for o in outs],
        compiler_params=pltpu.CompilerParams(vmem_limit_bytes=56 * 1024 * 1024),
    )(*args, *sides)


def local(fn, outs, *args, scalar=None):
    def kernel(*refs):
        lead = [] if scalar is None else [refs[0]]
        ins, out_refs = refs[len(lead) : -len(outs)], refs[-len(outs) :]
        scalars = [r[i] for r in lead for i in range(r.shape[0])]
        results = fn(*scalars, *[r[...] for r in ins])
        for ref, value in zip(out_refs, results):
            ref[...] = value.astype(ref.dtype)

    specs = [pl.BlockSpec(memory_space=pltpu.VMEM)] * len(args)
    if scalar is not None:
        specs = [pl.BlockSpec(memory_space=pltpu.SMEM)] + specs
        args = (scalar.reshape(-1), *args)
    return pl.pallas_call(
        kernel,
        in_specs=specs,
        out_specs=[pl.BlockSpec(memory_space=pltpu.VMEM)] * len(outs),
        out_shape=[jax.ShapeDtypeStruct(o[:2], o[2]) for o in outs],
        compiler_params=pltpu.CompilerParams(vmem_limit_bytes=56 * 1024 * 1024),
    )(*args)


def take_lanes(value, spans):
    if len(spans) == 1:
        return value
    return jnp.concatenate([value[:, a:b] for a, b in spans], axis=1)


def norm_back(grad, gain, normal, scale):
    e = grad * gain
    return scale * (
        e
        - jnp.mean(e, axis=-1, keepdims=True)
        - normal * jnp.mean(e * normal, axis=-1, keepdims=True)
    )


def rows_above(value, first):
    row = lax.broadcasted_iota(jnp.int32, value.shape, 0)
    return jnp.where(row == 0, first, pltpu.roll(value, 1, 0))


def rows_below(value, last):
    row = lax.broadcasted_iota(jnp.int32, value.shape, 0)
    high = value.shape[0]
    return jnp.where(row == high - 1, last, pltpu.roll(value, high - 1, 0))


def padded(rows):
    return jnp.concatenate(
        list(rows) + [jnp.zeros((8 - len(rows), rows[0].shape[1]), F32)], axis=0
    )


def column_sum(value):
    return jnp.sum(value, axis=0, keepdims=True)


def gates_kernel(
    spans, who_ref, middle_ref, value_ref, more_ref, act_ref, cot_ref,
    out_ref, up_ref, vg_ref, rg_ref, held,
):
    to_spans, from_spans = spans
    step, part = act_ref.shape[0] // 4, act_ref.shape[1]
    who = who_ref[0]
    act = [
        act_ref[pl.ds(pl.multiple_of((who ^ j) * step, step), step), :] for j in range(4)
    ]
    recept = jax.nn.sigmoid(take_lanes(jnp.concatenate(act, axis=1).astype(F32), to_spans))
    value = value_ref[...] + more_ref[...].astype(F32)
    out = middle_ref[...] + recept * value
    out_ref[...] = take_lanes(out, from_spans).astype(BF16)
    up = take_lanes(cot_ref[...].astype(F32), to_spans)
    up_ref[...] = up
    vg_ref[...] = (up * recept).astype(BF16)
    held[...] = take_lanes(up * value * recept * (1.0 - recept), from_spans)
    for k in range(4):
        at = pl.multiple_of((who ^ k) * part, part)
        rg_ref[k * step : (k + 1) * step, :] = held[:, pl.ds(at, part)].astype(BF16)


def gates(spans, who, middle, value, more, act, cot):
    step, width = middle.shape
    part = act.shape[1]
    shape = jax.ShapeDtypeStruct
    return pl.pallas_call(
        functools.partial(gates_kernel, spans),
        in_specs=[pl.BlockSpec(memory_space=pltpu.SMEM)]
        + [pl.BlockSpec(memory_space=pltpu.VMEM)] * 5,
        out_specs=[pl.BlockSpec(memory_space=pltpu.VMEM)] * 4,
        out_shape=[
            shape((step, width), BF16),
            shape((step, width), F32),
            shape((step, width), BF16),
            shape((4 * step, part), BF16),
        ],
        scratch_shapes=[pltpu.VMEM((step, width), F32)],
        compiler_params=pltpu.CompilerParams(vmem_limit_bytes=56 * 1024 * 1024),
    )(who.reshape(1), middle, value, more, act, cot)


def mixes_back_kernel(
    kept_ref, got_ref, dl_ref, dl_more_ref, delta_ref, tanh_ref, dtanh_ref, blend_ref, m0_ref,
    down_ref, up_ref, ddown_ref, vec_ref,
    rest_ref, dg_ref, row_ref, cols_ref, down_out, up_out, ddown_out,
):
    step = delta_ref.shape[0]
    dtanh = dtanh_ref[...]
    decay_grad = dl_ref[...] + dl_more_ref[...].astype(F32)
    decay_pre = (decay_grad * (1.0 - dtanh * dtanh)).astype(BF16)
    ddown_out[...] = tn(m0_ref[...], decay_pre)
    tanh = tanh_ref[...]
    latent = tanh.astype(BF16)
    lane = lax.broadcasted_iota(jnp.int32, latent.shape, 1)
    delta, up = delta_ref[...], up_ref[...]
    latent_grad = jnp.zeros(latent.shape, F32)
    up_grad = jnp.zeros(up_out.shape, F32)
    dg = jnp.zeros(delta.shape, F32)
    total = jnp.zeros(delta.shape, F32)
    cols = []
    for c in range(5):
        own = (lane >= c * RANK) & (lane < (c + 1) * RANK)
        mine = jnp.where(own, latent, jnp.zeros_like(latent))
        if c == 0:
            grad = nt(decay_pre, ddown_ref[...])
        else:
            at = slice((c - 1) * step, c * step)
            grad = kept_ref[at, :] + got_ref[at, :].astype(F32)
        shift = grad * delta
        cols.append(column_sum(shift))
        offset = shift.astype(BF16)
        latent_grad = jnp.where(own, nn(offset, up), latent_grad)
        up_grad = up_grad + tn(offset, mine)
        dg = dg + grad * (vec_ref[3 + c : 4 + c, :] + nt(mine, up))
        total = total + grad
    up_out[...] = up_grad
    mix_pre = (latent_grad * (1.0 - tanh * tanh)).astype(BF16)
    down_out[...] = tn(blend_ref[...], mix_pre)
    blend_grad = nt(mix_pre, down_ref[...])
    dg = dg + blend_grad * vec_ref[2:3, :]
    rest_ref[...] = total + blend_grad - dg
    dg_ref[...] = dg
    row_ref[...] = dg[:8]
    cols_ref[...] = padded([column_sum(blend_grad * delta)] + cols)


def mixes_back(*args):
    delta, down, ddown = args[4], args[9], args[11]
    step, width = delta.shape
    shape = jax.ShapeDtypeStruct
    outs = [
        shape((step, width), F32),
        shape((step, width), F32),
        shape((8, width), F32),
        shape((8, width), F32),
        shape(down.shape, F32),
        shape(down.shape, F32),
        shape(ddown.shape, F32),
    ]
    return pl.pallas_call(
        mixes_back_kernel,
        in_specs=[pl.BlockSpec(memory_space=pltpu.VMEM)] * len(args),
        out_specs=[pl.BlockSpec(memory_space=pltpu.VMEM)] * len(outs),
        out_shape=outs,
        compiler_params=pltpu.CompilerParams(vmem_limit_bytes=60 * 1024 * 1024),
    )(*args)


def tie(*values):
    return lax.optimization_barrier(values)


def on_device(
    count,
    tokens,
    previous,
    initial_state,
    mixing_weights,
    lowrank_weights,
    vectors,
    feedforward_weights,
    cotangent,
):
    fast = initial_state.shape[0] == 64
    masks = (1, 8) if fast else (1, 2)
    size = 1 << len(masks)
    teams = count // size
    all_masks = [1 << b for b in range(count.bit_length() - 1)]
    team_masks = [b for b in all_masks if b not in masks]
    far = 16
    team_masks.sort(key=lambda b: fast and b != far)
    me = lax.axis_index("seq")
    _, step, width = tokens.shape
    rows = mixing_weights.shape[0]
    part = width // size
    ff_part = FF // size
    team_rows = rows * size
    def bit_of(who, mask):
        return (who // mask) % 2 if isinstance(who, int) else lax.rem(lax.div(who, mask), 2)

    def member_of(who):
        return sum(bit_of(who, b) << j for j, b in enumerate(masks))

    def team_of(who):
        return sum(bit_of(who, b) << j for j, b in enumerate(team_masks))

    member, team = member_of(me), team_of(me)
    order = sorted(range(count), key=lambda d: (team_of(d), member_of(d)))
    inverse = sorted(range(count), key=lambda p: order[p])
    across = [order[m::size] for m in range(size)]
    square = [order[m :: 2 * size] for m in range(2 * size)]
    def lane_spans(blocks):
        spans = []
        for d in blocks:
            if spans and spans[-1][1] == d * rows:
                spans[-1][1] = (d + 1) * rows
            else:
                spans.append([d * rows, (d + 1) * rows])
        return spans

    to_spans, from_spans = lane_spans(order), lane_spans(inverse)

    def to_places(value, dtype):
        return move_lanes(to_spans, value, dtype)

    def flips(k):
        return sum(b for j, b in enumerate(masks) if (k >> j) & 1)

    def trade(value, mask):
        return lax.ppermute(value, "seq", [(d, d ^ mask) for d in range(count)])

    def group_gather(value):
        side = trade(value, masks[1])
        return value, side, trade(jnp.concatenate([value, side], axis=0), masks[0])

    def group_rows(value):
        high, columns = value.shape

        def lay(own, side, far):
            return (jnp.concatenate([own, far[:high], side, far[high:]], axis=0),)

        return local(lay, [(size * high, columns, value.dtype)], *group_gather(value))[0]

    def halves(value):
        cut = [value[k * step : (k + 1) * step] for k in range(size)]
        return [cut[0], cut[2]], [cut[1], cut[3]]

    def group_fold(kept, sent):
        high, columns = kept.shape[0] // 2, kept.shape[1]
        got = trade(sent, masks[0])

        def add(mine, more):
            total = mine + more.astype(F32)
            return total[:high], total[high:]

        return local(add, [(high, columns, F32), (high, columns, BF16)], kept, got)

    def group_sum(kept, sent):
        mine, side = group_fold(kept, sent)
        return mine, trade(side, masks[1])

    def crossing_sum(*pairs):
        units = len(pairs)

        def body(*products):
            parts = [halves(p) for p in products]
            kept = [p[0][i] for i in range(2) for p in parts]
            sent = [p[1][i] for i in range(2) for p in parts]
            return jnp.concatenate(kept, axis=0), jnp.concatenate(sent, axis=0)

        high = 2 * units * step
        return product(
            [(a, b, "nt", at) for a, b, at in pairs],
            [(high, width, F32), (high, width, BF16)],
            body,
            tile=512,
        )

    def exchange(pieces, meet=None):
        pieces, high = list(pieces), pieces[0].shape[0]
        for j in reversed(range(len(masks))):
            keys = [k for k in range(size) if (k >> j) & 1]
            got = trade(jnp.concatenate([pieces[k] for k in keys], axis=0), masks[j])
            if meet is not None and j == len(masks) - 1:
                got, meet = tie(got, meet)
            for i, k in enumerate(keys):
                pieces[k] = got[i * high : (i + 1) * high]
        return pieces if meet is None else (pieces, meet)

    def ordered(pieces):
        pieces = list(pieces)
        for j in range(len(masks)):
            swap = lax.rem(lax.div(member, 1 << j), 2) == 1
            pieces = [
                jnp.where(swap, pieces[k ^ (1 << j)], pieces[k]) for k in range(len(pieces))
            ]
        return pieces

    def neighbour(value, offset):
        pairs = [(d, d + offset) for d in range(count) if 0 <= d + offset < count]
        return lax.ppermute(value, "seq", pairs)

    def take_columns(value, spans, who):
        return jnp.concatenate(
            [
                lax.dynamic_slice_in_dim(value, start + who * wide, wide, axis=1)
                for start, wide in spans
            ],
            axis=1,
        )

    def group_columns(value, spans):
        pieces = [take_columns(value, spans, member ^ k) for k in range(size)]
        return jnp.concatenate(ordered(exchange(pieces)), axis=0)

    def crossing(first):
        bits = list(range(1, len(team_masks))) + [0]
        if first:
            bits[0], bits[1] = bits[1], bits[0]
        return bits

    def gather_rows(own):
        return lax.all_gather(own, "seq", axis=0, tiled=True, axis_index_groups=across)

    def far_send(own):
        return trade(own, far) if fast else own

    def far_join(own, got):
        if not fast:
            return own
        upper = bit_of(me, far) == 1
        return jnp.concatenate(
            [jnp.where(upper, got, own), jnp.where(upper, own, got)], axis=0
        )

    def gather_square(paired):
        groups = square if fast else across
        return lax.all_gather(paired, "seq", axis=0, tiled=True, axis_index_groups=groups)

    def team_products(*pairs):
        if fast:
            places = jnp.arange(teams, dtype=jnp.int32)
            return weight_grad(places, pairs, team_rows).reshape(width, -1)
        return jnp.concatenate([tn(x, y).astype(BF16) for x, y in pairs], axis=1)

    def square_sum(grads):
        groups = square if fast else across
        return lax.psum_scatter(
            grads, "seq", scatter_dimension=0, tiled=True, axis_index_groups=groups
        )

    def far_split(pair):
        if not fast:
            return pair, jnp.zeros_like(pair)
        bit = bit_of(me, far)
        sent = lax.dynamic_slice_in_dim(pair, (1 - bit) * team_rows, team_rows, axis=0)
        kept = lax.dynamic_slice_in_dim(pair, bit * team_rows, team_rows, axis=0)
        return kept, trade(sent, far)

    def far_add(kept, got):
        return (kept.astype(F32) + got.astype(F32)).astype(BF16)

    def cube_gather(value, follower=None):
        for mask in reversed(all_masks):
            got = trade(value, mask)
            upper = bit_of(me, mask) == 1
            value = jnp.stack([jnp.where(upper, got, value), jnp.where(upper, value, got)])
            if mask == 8 and follower is not None:
                value, follower = tie(value, follower)
        axes = len(all_masks)
        cube = value.transpose(*reversed(range(axes)), *range(axes, value.ndim))
        return cube if follower is None else (cube, follower)

    place_axes = [all_masks[::-1].index(b) for b in team_masks[::-1] + list(masks[::-1])]

    def by_place(cube):
        rest = range(len(all_masks), cube.ndim)
        return cube.transpose(*place_axes, *rest).reshape(width, -1)

    def to_cube(value):
        cube = value.reshape(*[2] * len(place_axes), rows, -1)
        back = [place_axes.index(a) for a in range(len(place_axes))]
        return cube.transpose(*back, len(back), len(back) + 1)

    def cube_sum(cube, kind, follower):
        for axis, mask in reversed(list(enumerate(reversed(all_masks)))):
            bit = bit_of(me, mask)
            sent = lax.dynamic_index_in_dim(cube, 1 - bit, axis, keepdims=False)
            kept = lax.dynamic_index_in_dim(cube, bit, axis, keepdims=False)
            cube = kept.astype(F32) + trade(sent.astype(kind), mask).astype(F32)
            if mask == 1:
                cube, follower = tie(cube, follower)
        return cube, follower

    def hand_rows(joint, extra=None, meet=None):
        mine = [
            lax.dynamic_slice_in_dim(joint, (member ^ k) * rows, rows, axis=0)
            for k in range(size)
        ]
        if extra is not None:
            mine = [jnp.concatenate([m, e], axis=1) for m, e in zip(mine, extra)]
        return exchange(mine, meet)

    def columns_of(by_member, start, wide):
        return [p[:, start : start + wide] for p in by_member]

    up_start, decay_start, decay_up = 5 * RANK, 10 * RANK, 10 * RANK + DRANK
    last_row = neighbour(tokens[0, -1:, :], 1)
    tokens_sent = to_places(
        jnp.concatenate([tokens[0], jnp.broadcast_to(last_row, (16, width))], axis=0), BF16
    )
    natural, mix_in = cube_gather(
        jnp.concatenate(
            [vectors, initial_state, lowrank_weights[:, decay_up:].astype(F32)], axis=1
        ),
        mixing_weights,
    )
    natural = natural.reshape(width, -1)
    low_cube, mix_in = cube_gather(lowrank_weights[:, :decay_up], mix_in)
    tokens_all = jnp.concatenate(group_gather(tokens_sent), axis=0)
    mix_local = group_columns(mix_in, [(c * width, part) for c in range(5)])
    mix_local, natural, low_cube, tokens_all = tie(mix_local, natural, low_cube, tokens_all)
    lowrank = by_place(low_cube)
    mix_kv, mix_rest = mix_local[:, : 2 * part], mix_local[:, 2 * part :]
    kv_got, mix_rest, feed_in = tie(far_send(mix_kv), mix_rest, feedforward_weights)
    w_kv = gather_square(far_join(mix_kv, kv_got))
    tiles = part // 256

    mine = lax.dynamic_slice_in_dim(natural, member * part, part, axis=0)
    vec_part = mine[:, :16].T
    first_state = mine[:, 16 : 16 + SPAN].T
    w_dup = mine[:, 16 + SPAN :].astype(BF16)
    vec = by_place(
        natural[:, :16].reshape(*[2] * len(all_masks), rows, 16)
    ).T
    wkv_rows = jnp.concatenate([vec_part[9:12], jnp.zeros((5, part), F32)], axis=0)
    is_first = (me == 0).astype(jnp.int32)
    before = to_places(previous.reshape(2, width), F32)
    w_down, w_up = lowrank[:, :up_start], lowrank[:, up_start:decay_start]
    w_ddown = lowrank[:, decay_start:]

    opening = jnp.stack(
        [jnp.bitwise_xor(me, flips(k)) == 0 for k in (0, 2, 1, 3)]
    ).astype(jnp.int32)
    (
        *mixed_all, dh_all, normal_one, scale_one, delta, blend, mixed_zero, mix_tanh, decay_tanh,
    ) = group_mixes(opening, tokens_all, before, vec, w_down, w_up, w_ddown, step)
    rest_got, mixed_all[0] = tie(far_send(mix_rest), mixed_all[0])
    w_rest = gather_square(far_join(mix_rest, rest_got))
    ff_spans = [(0, ff_part), (FF, part), (FF + width, ff_part)]
    ff_local = group_columns(feed_in, ff_spans)
    everyone = size * step
    (log_decay,) = product(
        [(dh_all, w_dup, "nt", 0)],
        [(everyone, part, F32)],
        lambda acc, base: (-jnp.exp(base + acc),),
        sides=(vec_part[8:9],),
    )
    keys, values = product(
        [(mixed_all[0], w_kv, "nn", 0), (mixed_all[1], w_kv, "nn", tiles)],
        [(everyone, part, F32)] * 2,
        lambda a, b: (a, b),
    )

    keys, ff_local = tie(keys, ff_local)
    ff_tail = ff_local[:, ff_part + part :]
    ff_near = ff_local[:, : ff_part + part]
    near_got = far_send(ff_near)

    call = functools.partial(block_call, chunks=size, step=step, width=part)
    (totals,) = call(
        totals_kernel, ins="ttt", outs=[("x", F32)], args=(keys, values, log_decay)
    )
    stages, current = [], [None, []]
    for mask in all_masks:
        if mask in masks:
            current[1].append(1 << masks.index(mask))
        else:
            stages.append(current)
            current = [mask, []]
    stages.append(current)
    high, long = SPAN + 8, SPAN + 16

    def chain(early, late):
        return early[0] * late[0], late[0] * early[1] + late[1]

    def pick(flag, yes, no):
        return tuple(jnp.where(flag, a, b) for a, b in zip(yes, no))

    def rows8(row):
        return jnp.broadcast_to(row, (8, part))

    def pack(items):
        return jnp.concatenate([r for d, v in items for r in (v, rows8(d))], axis=0)

    def unpack(array, count):
        cut = [array[i * high : (i + 1) * high] for i in range(count)]
        return [(c[SPAN : SPAN + 1], c[:SPAN]) for c in cut]

    def swap_members(who, pieces):
        pieces = list(pieces)
        for j in range(len(masks)):
            flag = (who // (1 << j)) % 2 == 1
            pieces = [jnp.where(flag, pieces[k ^ (1 << j)], pieces[k]) for k in range(size)]
        return pieces

    def neutral():
        return jnp.ones((1, part), F32), jnp.zeros((SPAN, part), F32)

    def flags_of(mask):
        bit = jnp.int32(0) if mask is None else bit_of(me, mask)
        return jnp.stack([member, bit]).astype(jnp.int32)

    keys_at, decays = list(range(size)), []
    open_bits = size - 1
    stage_arrays = [totals.reshape(size * high, part)]
    for index, (mask, merges) in enumerate(stages):
        last = index + 1 == len(stages)
        after_keys = keys_at
        for bit in merges:
            after_keys = [g for g in after_keys if not g & bit]

        def forward_stage(
            who, late, *arrays, mask=mask, merges=merges, groups=keys_at, bits=open_bits, last=last
        ):
            marks = []
            if mask is None:
                cut = [arrays[0][k * high : (k + 1) * high] for k in range(size)]
                total = {
                    m: (p[SPAN : SPAN + 1], p[:SPAN])
                    for m, p in enumerate(swap_members(who, cut))
                }
                chunks = [neutral() for _ in range(size)]
            else:
                total = dict(zip(groups, unpack(arrays[0], len(groups))))
                chunks = unpack(arrays[1], size)
                other = {}
                for i, g in enumerate(groups):
                    got = arrays[2][i * long : (i + 1) * long].astype(F32)
                    other[g] = got[SPAN : SPAN + 1] + got[SPAN + 8 : SPAN + 9], got[:SPAN]
                marks += [total[g][0] for g in groups] + [other[g][0] for g in groups]
                late = late == 1
                chunks = [
                    pick(late, chain(other[m & bits], c), c) for m, c in enumerate(chunks)
                ]
                total = {
                    g: pick(late, chain(other[g], total[g]), chain(total[g], other[g]))
                    for g in groups
                }
            for bit in merges:
                marks += [total[g][0] for g in total]
                chunks = [
                    chain(total[(m & bits) ^ bit], c) if m & bit else c
                    for m, c in enumerate(chunks)
                ]
                total = {g: chain(total[g], total[g | bit]) for g in total if not g & bit}
                bits ^= bit
            marks = jnp.concatenate([rows8(r) for r in marks], axis=0)
            if last:
                states = [d * arrays[-1] + v for d, v in chunks]
                return jnp.concatenate(swap_members(who, states), axis=0), marks
            sent = []
            for d, v in total.values():
                first = d.astype(BF16)
                rest = (d - first.astype(F32)).astype(BF16)
                sent += [v.astype(BF16), rows8(first), rows8(rest)]
            return (
                pack(list(total.values())), pack(chunks), jnp.concatenate(sent, axis=0), marks
            )

        count_marks = (0 if mask is None else 2 * len(keys_at)) + sum(
            len(keys_at) >> i for i in range(len(merges))
        )
        marks_out = (8 * count_marks, part, F32)
        if last:
            outs = [(size * SPAN, part, F32), marks_out]
            state_in, marks = local(
                forward_stage, outs, *stage_arrays, first_state, scalar=flags_of(mask)
            )
            state_in = state_in.reshape(size, SPAN, part)
        else:
            outs = [
                (len(after_keys) * high, part, F32),
                (size * high, part, F32),
                (len(after_keys) * long, part, BF16),
                marks_out,
            ]
            total, chunks, sent, marks = local(
                forward_stage, outs, *stage_arrays, scalar=flags_of(mask)
            )
            if mask == (2 if fast else 4):
                sent, near_got = tie(sent, near_got)
            stage_arrays = [total, chunks, trade(sent, stages[index + 1][0])]
        decays.append(marks)
        keys_at = after_keys
        for bit in merges:
            open_bits ^= bit
    w_near = gather_square(far_join(ff_near, near_got))
    w_key, w_rec = w_near, w_near[:, ff_part:]
    state_in, ff_tail = tie(state_in, ff_tail)
    val_got = far_send(ff_tail)

    receipt, gate_pre = product(
        [(mixed_all[2], w_rest, "nn", 0), (mixed_all[3], w_rest, "nn", tiles)],
        [(everyone, part, F32)] * 2,
        lambda a, b: (a, b),
    )
    wkv, gated = call(
        forward_kernel,
        ins="tttttsp",
        outs=[("t", F32), ("t", BF16)],
        args=(receipt, keys, values, log_decay, gate_pre, state_in, wkv_rows),
    )
    gated, val_got = tie(gated, val_got)
    w_val = gather_square(far_join(ff_tail, val_got))
    branch, branch_more = group_sum(*crossing_sum((gated, w_rest, 2)))

    def norm_two(hidden, mine, more, vec):
        middle = hidden[:step].astype(F32) + mine + more.astype(F32)
        centred = middle - jnp.mean(middle, axis=-1, keepdims=True)
        scale = lax.rsqrt(jnp.mean(centred * centred, axis=-1, keepdims=True) + LN_EPS)
        normal = centred * scale
        tail = normal[step - 8 :] * vec[12:13] + vec[13:14]
        return middle, normal, jnp.broadcast_to(scale, (step, 128)), tail

    whole = (step, width, F32)
    middle, normal_two, scale_two, tail_two = local(
        norm_two,
        [whole, whole, (step, 128, F32), (8, width, F32)],
        tokens_sent,
        branch,
        branch_more,
        vec,
    )

    def mix_two(first, normal, arrived, before, vec):
        normed = normal * vec[12:13] + vec[13:14]
        above = jnp.where(first == 1, before[1:2], arrived[7:8])
        delta = rows_above(normed, above) - normed
        key_in, recv_in = normed + delta * vec[14:15], normed + delta * vec[15:16]
        return jnp.concatenate([key_in, recv_in], axis=0), delta

    both, delta_two = local(
        mix_two,
        [(2 * step, width, BF16), whole],
        normal_two,
        neighbour(tail_two, 1),
        before,
        vec,
        scalar=is_first,
    )

    key_all, recv_all = group_rows(both[:step]), group_rows(both[step:])
    relu, squared = product(
        [(key_all, w_key, "nn", 0)],
        [(everyone, ff_part, F32), (everyone, ff_part, BF16)],
        lambda acc: (jnp.maximum(acc, 0.0), jnp.square(jnp.maximum(acc, 0.0))),
        tile=ff_part // 2,
    )
    (recept_act,) = product(
        [(recv_all, w_rec, "nn", 0)],
        [(everyone, part, BF16)],
        lambda acc: (acc,),
    )
    squared, recept_act = tie(squared, recept_act)
    acts = exchange([recept_act[k * step : (k + 1) * step] for k in range(size)])
    value, value_more = group_sum(*crossing_sum((squared, w_val, 0)))
    block_output, upstream, value_grad, recept_grads = gates(
        (to_spans, from_spans),
        member,
        middle,
        value,
        value_more,
        jnp.concatenate(acts, axis=0),
        cotangent.reshape(step, width),
    )

    rg_all = jnp.concatenate(
        exchange([recept_grads[k * step : (k + 1) * step] for k in range(size)]), axis=0
    )
    vg_all = group_rows(value_grad)
    val_grads = team_products((vg_all, squared))
    vg_all, val_grads, rg_all = tie(vg_all, val_grads, rg_all)
    val_pair = square_sum(val_grads)
    (key_grad,) = product(
        [(vg_all, w_val, "nn", 0)],
        [(everyone, ff_part, BF16)],
        lambda acc, relu: (acc * (2.0 * relu),),
        sides=(relu,),
        tile=ff_part // 2,
    )
    key_grads = team_products((key_all, key_grad))
    key_grad, key_grads = tie(key_grad, key_grads)
    key_pair = square_sum(key_grads)
    recv_two = group_sum(*crossing_sum((rg_all, w_rec, 0)))
    key_two = group_sum(*crossing_sum((key_grad, w_key, 0)))

    def inputs_back(key, key_more, recv, recv_more, vec):
        key, recv = key + key_more.astype(F32), recv + recv_more.astype(F32)
        top = key[:8] * vec[14:15] + recv[:8] * vec[15:16]
        return jnp.concatenate([key, recv], axis=0), top

    in_grads, top_two = local(
        inputs_back, [(2 * step, width, F32), (8, width, F32)], *key_two, *recv_two, vec
    )
    last_flag = (me == count - 1).astype(jnp.int32)

    def norm_two_back(last, grads, arrived, upstream, normal, scale, delta, vec):
        key_grad, recv_grad = grads[:step], grads[step:]
        shifted = key_grad * vec[14:15] + recv_grad * vec[15:16]
        below = jnp.where(last == 1, jnp.zeros_like(arrived[:1]), arrived[:1])
        grad = (
            key_grad * (1.0 - vec[14:15])
            + recv_grad * (1.0 - vec[15:16])
            + rows_below(shifted, below)
        )
        out = upstream + norm_back(grad, vec[12:13], normal, scale[:, :1])
        cols = padded(
            [
                column_sum(grad * normal),
                column_sum(grad),
                column_sum(key_grad * delta),
                column_sum(recv_grad * delta),
            ]
        )
        return out, out, cols

    middle_grad, branch_grad, cols_two = local(
        norm_two_back,
        [whole, (step, width, BF16), (8, width, F32)],
        in_grads,
        neighbour(top_two, -1),
        upstream,
        normal_two,
        scale_two,
        delta_two,
        vec,
        scalar=last_flag,
    )

    bg_all = group_rows(branch_grad)
    (gated_grad,) = product(
        [(bg_all, w_rest, "nn", 2 * tiles)], [(everyone, part, F32)], lambda acc: (acc,)
    )
    gate_grad, wkv_grad, ends = call(
        gate_kernel,
        ins="tttttp",
        outs=[("t", BF16), ("t", F32), ("x", F32)],
        args=(gated_grad, gate_pre, wkv, receipt, log_decay, wkv_rows),
    )
    val_kept, val_got = far_split(val_pair)
    keys_at, open_bits = list(range(size)), size - 1
    stage_arrays = [ends.reshape(size * high, part)]
    for index, (mask, merges) in enumerate(stages):
        last = index + 1 == len(stages)
        after_keys = keys_at
        for bit in merges:
            after_keys = [g for g in after_keys if not g & bit]

        def backward_stage(
            who, late, *arrays, mask=mask, merges=merges, groups=keys_at, bits=open_bits, last=last
        ):
            marks = [arrays[-1][i * 8 : i * 8 + 1] for i in range(arrays[-1].shape[0] // 8)]
            if mask is None:
                cut = [arrays[0][k * high : k * high + SPAN] for k in range(size)]
                total = dict(enumerate(swap_members(who, cut)))
                chunks = [neutral() for _ in range(size)]
            else:
                total = {g: arrays[0][i * SPAN : (i + 1) * SPAN] for i, g in enumerate(groups)}
                chunks = unpack(arrays[1], size)
                other = {
                    g: arrays[2][i * SPAN : (i + 1) * SPAN].astype(F32)
                    for i, g in enumerate(groups)
                }
                here = dict(zip(groups, marks))
                there = dict(zip(groups, marks[len(groups) :]))
                marks = marks[2 * len(groups) :]
                early = late == 0
                chunks = [
                    pick(
                        early,
                        (d * there[m & bits], d * other[m & bits] + v),
                        (d, v),
                    )
                    for m, (d, v) in enumerate(chunks)
                ]
                total = {
                    g: jnp.where(
                        early,
                        total[g] + here[g] * other[g],
                        other[g] + there[g] * total[g],
                    )
                    for g in groups
                }
            for bit in merges:
                here = dict(zip(total, marks))
                marks = marks[len(total) :]
                chunks = [
                    (d, v)
                    if m & bit
                    else (d * here[(m & bits) | bit], d * total[(m & bits) | bit] + v)
                    for m, (d, v) in enumerate(chunks)
                ]
                total = {
                    g: total[g] + here[g] * total[g | bit] for g in total if not g & bit
                }
                bits ^= bit
            joint = jnp.concatenate(list(total.values()), axis=0)
            if last:
                grads = swap_members(who, [v for _, v in chunks])
                return jnp.concatenate(grads, axis=0), joint.T
            return joint, pack(chunks), joint

        if last:
            outs = [(size * SPAN, part, F32), (part, SPAN, F32)]
            grad_out, first_grad = local(
                backward_stage, outs, *stage_arrays, decays[index], scalar=flags_of(mask)
            )
            grad_out = grad_out.reshape(size, SPAN, part)
        else:
            outs = [
                (len(after_keys) * SPAN, part, F32),
                (size * high, part, F32),
                (len(after_keys) * SPAN, part, BF16),
            ]
            total, chunks, sent = local(
                backward_stage, outs, *stage_arrays, decays[index], scalar=flags_of(mask)
            )
            if mask == (2 if fast else 4):
                sent, val_got = tie(sent, val_got)
            stage_arrays = [total, chunks, trade(sent, stages[index + 1][0])]
        keys_at = after_keys
        for bit in merges:
            open_bits ^= bit
    out_grads = team_products((bg_all, gated), (recv_all, rg_all), (mixed_all[3], gate_grad))
    grad_out, out_grads = tie(grad_out, out_grads)
    out_pair = square_sum(out_grads)

    d_receipt, d_keys, d_values, d_decay, extra = call(
        backward_kernel,
        ins="tttttssp",
        outs=[("t", BF16)] * 4 + [("e", F32)],
        args=(receipt, keys, values, log_decay, wkv_grad, state_in, grad_out, wkv_rows),
    )
    grads = [d_keys, d_values, d_receipt, gate_grad]
    kept, sent = crossing_sum(
        *[(grads[c], w_rest if c > 1 else w_kv, c % 2) for c in range(4)]
    )
    main_grads = team_products(
        (mixed_all[0], d_keys), (mixed_all[1], d_values), (mixed_all[2], d_receipt)
    )

    def latent_back(grad, up):
        kept, sent = halves(nn(grad, up))
        return jnp.concatenate(kept, axis=0), jnp.concatenate(sent, axis=0)

    latent_mine, latent_more = group_sum(
        *local(
            latent_back, [(2 * step, DRANK, F32), (2 * step, DRANK, BF16)], d_decay, w_dup
        )
    )
    key_kept, key_got = far_split(key_pair)
    sent, main_grads, latent_more, key_got = tie(sent, main_grads, latent_more, key_got)
    main_pair = square_sum(main_grads)
    val_sum, key_sum = far_add(val_kept, val_got), far_add(key_kept, key_got)
    mixed_mine, mixed_side = group_fold(kept, sent)
    ff_rows, mixed_side = hand_rows(
        jnp.concatenate([key_sum, val_sum], axis=1), meet=mixed_side
    )
    mixed_more = trade(mixed_side, masks[1])
    mixed_more, out_pair = tie(mixed_more, out_pair)
    out_kept, out_got = far_split(out_pair)
    rest_grad, delta_grad, top_one, cols_mix, down_grad, up_grad, ddown_grad = mixes_back(
        mixed_mine,
        mixed_more,
        latent_mine,
        latent_more,
        delta,
        mix_tanh,
        decay_tanh,
        blend,
        mixed_zero,
        w_down,
        w_up,
        w_ddown,
        vec,
    )
    rest_grad, main_pair, out_got = tie(rest_grad, main_pair, out_got)
    out_sum = far_add(out_kept, out_got)

    def norm_one_back(last, rest, shifted, arrived, normal, scale, middle, vec):
        below = jnp.where(last == 1, jnp.zeros_like(arrived[:1]), arrived[:1])
        grad = rest + rows_below(shifted, below)
        out = middle + norm_back(grad, vec[0:1], normal, scale[:, :1])
        cols = padded([column_sum(grad * normal), column_sum(grad)])
        return take_lanes(out, from_spans), cols

    block_input_gradient, cols_one = local(
        norm_one_back,
        [whole, (8, width, F32)],
        rest_grad,
        delta_grad,
        neighbour(top_one, -1),
        normal_one,
        scale_one,
        middle_grad,
        vec,
        scalar=last_flag,
    )
    main_kept, main_got = far_split(main_pair)


    def spread(value):
        zero = jnp.zeros((width, value.shape[1]), F32)
        return lax.dynamic_update_slice_in_dim(zero, value, member * part, axis=0)

    vec_low = jnp.concatenate([cols_one[:2], cols_mix[:6], cols_two[:4]], axis=0)
    vec_head = jnp.concatenate(
        [jnp.sum(extra[:, :2], axis=0), jnp.sum(ends[:, SPAN : SPAN + 2], axis=0)], axis=0
    )
    by_feature = jnp.concatenate([down_grad, up_grad, ddown_grad, vec_low.T], axis=1)
    by_channel = spread(jnp.concatenate([tn(d_decay, dh_all), vec_head.T], axis=1))
    low, main_got = cube_sum(
        jnp.concatenate(
            [to_cube(by_feature), by_channel.reshape(*[2] * len(all_masks), rows, -1)], axis=-1
        ),
        BF16,
        main_got,
    )
    main_sum = far_add(main_kept, main_got)

    holder = lax.div(me * rows, part)

    def rows_of(who):
        mine = lax.dynamic_slice_in_dim(first_grad, lax.rem(who * rows, part), rows, axis=0)
        high = lax.reduce_precision(mine, 8, 7)
        return jnp.concatenate([high, mine - high], axis=1).astype(BF16)

    handed = hand_rows(
        jnp.concatenate([main_sum, out_sum], axis=1),
        [rows_of(jnp.bitwise_xor(me, flips(k))) for k in range(size)],
    )
    state_rows = handed[0][:, 6 * part :]
    for k in range(1, size):
        state_rows = jnp.where(holder == (member ^ k), handed[k][:, 6 * part :], state_rows)
    state_rows = state_rows.astype(F32)
    initial_state_gradient = state_rows[:, :SPAN] + state_rows[:, SPAN:]
    by_member, ff_member = ordered(handed), ordered(ff_rows)
    mixing_gradient = jnp.concatenate(
        [p for c in (0, 1, 2, 5, 3) for p in columns_of(by_member, c * part, part)], axis=1
    ).astype(F32)
    feedforward_gradient = jnp.concatenate(
        columns_of(ff_member, 0, ff_part)
        + columns_of(by_member, 4 * part, part)
        + columns_of(ff_member, ff_part, ff_part),
        axis=1,
    ).astype(F32)

    vec_at = decay_up + 12
    lowrank_gradient = jnp.concatenate(
        [low[:, :decay_up], low[:, vec_at : vec_at + DRANK]], axis=1
    )
    vectors_gradient = jnp.concatenate(
        [low[:, decay_up : decay_up + 8], low[:, vec_at + DRANK :], low[:, decay_up + 8 : vec_at]],
        axis=1,
    )
    return (
        block_output.reshape(1, step, width),
        block_input_gradient.reshape(1, step, width),
        initial_state_gradient,
        mixing_gradient,
        lowrank_gradient,
        vectors_gradient,
        feedforward_gradient,
    )


def solution(mesh):
    rowwise = P("seq", None)
    tokenwise = P(None, "seq", None)
    return jax.shard_map(
        functools.partial(on_device, mesh.shape["seq"]),
        mesh=mesh,
        in_specs=(tokenwise, P(), rowwise, rowwise, rowwise, rowwise, rowwise, tokenwise),
        out_specs=(tokenwise, tokenwise, rowwise, rowwise, rowwise, rowwise, rowwise),
        check_vma=False,
    )
```

```python
import functools

import jax
import jax.numpy as jnp
from jax import lax
from jax.experimental import pallas as pl
from jax.experimental.pallas import tpu as pltpu
from jax.sharding import PartitionSpec as P

HEADS = 32
SPAN = 64
FF = 7168
RANK = 32
DRANK = 64
LN_EPS = 1e-05
GN_EPS = 0.00064

F32 = jnp.float32
BF16 = jnp.bfloat16
HI = lax.Precision.HIGHEST


def nn(a, b):
    return jnp.dot(a, b, preferred_element_type=F32)


def nt(a, b):
    return lax.dot_general(a, b, (((1,), (1,)), ((), ())), preferred_element_type=F32)


def tn(a, b):
    return lax.dot_general(a, b, (((0,), (0,)), ((), ())), preferred_element_type=F32)


def knn(a, b):
    return lax.dot_general(
        a, b, (((1,), (0,)), ((), ())), preferred_element_type=F32
    )


def knt(a, b):
    return lax.dot_general(
        a, b, (((1,), (1,)), ((), ())), preferred_element_type=F32
    )


def ktn(a, b):
    return lax.dot_general(
        a, b, (((0,), (0,)), ((), ())), preferred_element_type=F32
    )


def low_lanes(shape):
    return lax.broadcasted_iota(jnp.int32, shape, len(shape) - 1) < SPAN


def head_sum(x):
    low = low_lanes(x.shape)
    s0 = jnp.sum(jnp.where(low, x, 0.0), axis=-1, keepdims=True)
    s1 = jnp.sum(jnp.where(low, 0.0, x), axis=-1, keepdims=True)
    return jnp.where(low, s0, s1)


def two_rows(x):
    low = low_lanes(x.shape)
    return jnp.concatenate([jnp.where(low, x, 0.0), jnp.where(low, 0.0, x)], axis=0)


def fold(full):
    return jnp.where(low_lanes((SPAN, 2 * SPAN)), full[:SPAN], full[SPAN:])


def unfold(state):
    low = low_lanes(state.shape)
    return jnp.concatenate([jnp.where(low, state, 0.0), jnp.where(low, 0.0, state)], axis=0)


def running(w, upper=False):
    count = w.shape[0]
    row = lax.broadcasted_iota(jnp.int32, (count, count), 0)
    col = lax.broadcasted_iota(jnp.int32, (count, count), 1)
    keep = (col >= row) if upper else (col <= row)
    return lax.dot_general(
        jnp.where(keep, 1.0, 0.0).astype(F32),
        w,
        (((1,), (0,)), ((), ())),
        precision=HI,
        preferred_element_type=F32,
    )


def strict(count):
    row = lax.broadcasted_iota(jnp.int32, (2 * count, count), 0)
    col = lax.broadcasted_iota(jnp.int32, (2 * count, count), 1)
    row = jnp.where(row >= count, row - count, row)
    return row > col, row == col


def affinity(r, k, u, q, ks):
    count = r.shape[0]
    below, diag = strict(count)
    raw = knt(two_rows(q), ks)
    share = jnp.sum(two_rows(r * u * k), axis=-1, keepdims=True)
    return jnp.where(below, raw, jnp.where(diag, share, 0.0))


def totals_kernel(k_ref, v_ref, w_ref, out_ref):
    cum = running(w_ref[...])
    total = cum[-1:, :]
    kc = k_ref[...] * jnp.exp(total - cum)
    out_ref[0, :SPAN, :] = fold(ktn(v_ref[...], kc))
    out_ref[0, SPAN:, :] = jnp.broadcast_to(jnp.exp(total), (8, 2 * SPAN))


def group_norm(y, gain, bias):
    centred = y - head_sum(y) * (1.0 / SPAN)
    spread = head_sum(centred * centred) * (1.0 / SPAN)
    scale = lax.rsqrt(spread + GN_EPS)
    normal = centred * scale
    return normal, scale, normal * gain + bias


def forward_kernel(r_ref, k_ref, v_ref, w_ref, g_ref, s_ref, p_ref, y_ref, gated_ref):
    r, k, v, w = r_ref[...], k_ref[...], v_ref[...], w_ref[...]
    cum = running(w)
    q = r * jnp.exp(cum - w)
    ks = k * jnp.exp(-cum)
    aff = affinity(r, k, p_ref[0:1, :], q, ks)
    count = r.shape[0]
    v2 = two_rows(v)
    y = (
        knt(q, unfold(s_ref[0]))
        + knn(aff[:count], v2[:count])
        + knn(aff[count:], v2[count:])
    )
    y_ref[...] = y
    gate = g_ref[...]
    _, _, grouped = group_norm(y, p_ref[1:2, :], p_ref[2:3, :])
    gated_ref[...] = (grouped * gate * jax.nn.sigmoid(gate)).astype(BF16)


def gate_kernel(gg_ref, g_ref, y_ref, r_ref, w_ref, p_ref, gate_ref, dy_ref, out_ref):
    gated_grad, gate, y = gg_ref[...], g_ref[...], y_ref[...]
    gain = p_ref[1:2, :]
    normal, scale, grouped = group_norm(y, gain, p_ref[2:3, :])
    sig = jax.nn.sigmoid(gate)
    gate_ref[...] = (gated_grad * grouped * sig * (1.0 + gate * (1.0 - sig))).astype(BF16)
    outer = gated_grad * gate * sig
    inner = outer * gain
    dy = scale * (
        inner
        - head_sum(inner) * (1.0 / SPAN)
        - normal * (head_sum(inner * normal) * (1.0 / SPAN))
    )
    dy_ref[...] = dy
    w = w_ref[...]
    q = r_ref[...] * jnp.exp(running(w) - w)
    out_ref[0, :SPAN, :] = fold(ktn(dy, q))
    gain_grad = jnp.sum(outer * normal, axis=0, keepdims=True)
    bias_grad = jnp.sum(outer, axis=0, keepdims=True)
    out_ref[0, SPAN:, :] = jnp.concatenate(
        [gain_grad, bias_grad, jnp.zeros((6, 2 * SPAN), F32)], axis=0
    )


def backward_kernel(
    r_ref, k_ref, v_ref, w_ref, dy_ref, s_ref, gs_ref, p_ref,
    dr_ref, dk_ref, dv_ref, dd_ref, out_ref,
):
    r, k, v, w, dy = r_ref[...], k_ref[...], v_ref[...], w_ref[...], dy_ref[...]
    u = p_ref[0:1, :]
    count = r.shape[0]
    cum = running(w)
    total = cum[-1:, :]
    e_before, e_minus, e_carry = jnp.exp(cum - w), jnp.exp(-cum), jnp.exp(total - cum)
    q, ks, kc = r * e_before, k * e_minus, k * e_carry
    aff = affinity(r, k, u, q, ks)
    below, _ = strict(count)
    dy2 = two_rows(dy)
    d_aff = jnp.where(below, knt(dy2, v), 0.0)
    own = head_sum(dy * v)
    state, grad_state = s_ref[0], gs_ref[0]
    state2, grad2 = unfold(state), unfold(grad_state)
    ks2 = two_rows(ks)
    dq = knn(dy, state2) + knn(d_aff[:count], ks2[:count]) + knn(d_aff[count:], ks2[count:])
    dks = ktn(d_aff, two_rows(q))
    dkc = knn(v, grad2)
    dv_ref[...] = (ktn(aff, dy2) + knt(kc, grad2)).astype(BF16)
    dr_ref[...] = (dq * e_before + own * u * k).astype(BF16)
    dk_ref[...] = (dks * e_minus + dkc * e_carry + own * u * r).astype(BF16)
    gq, gc = q * dq, kc * dkc
    d_total = jnp.sum(gc, axis=0, keepdims=True) + jnp.exp(total) * jnp.sum(
        state * grad_state, axis=0, keepdims=True
    )
    dw = running(gq - ks * dks - gc, upper=True) - gq + d_total
    term = dw * w
    dd_ref[...] = term.astype(BF16)
    out_ref[0] = jnp.concatenate(
        [
            jnp.sum(term, axis=0, keepdims=True),
            jnp.sum(own * r * k, axis=0, keepdims=True),
            jnp.zeros((6, 2 * SPAN), F32),
        ],
        axis=0,
    )


def block_call(kernel, chunks, step, width, ins, outs, args):
    lane = 2 * SPAN
    kinds = {
        "t": pl.BlockSpec((step, lane), lambda c, h: (c, h)),
        "s": pl.BlockSpec((1, SPAN, lane), lambda c, h: (c, 0, h)),
        "x": pl.BlockSpec((1, SPAN + 8, lane), lambda c, h: (c, 0, h)),
        "e": pl.BlockSpec((1, 8, lane), lambda c, h: (c, 0, h)),
        "p": pl.BlockSpec((8, lane), lambda c, h: (0, h)),
    }
    shapes = {
        "t": lambda d: jax.ShapeDtypeStruct((chunks * step, width), d),
        "x": lambda d: jax.ShapeDtypeStruct((chunks, SPAN + 8, width), d),
        "e": lambda d: jax.ShapeDtypeStruct((chunks, 8, width), d),
    }
    return pl.pallas_call(
        kernel,
        grid=(chunks, width // lane),
        in_specs=[kinds[kind] for kind in ins],
        out_specs=[kinds[kind] for kind, _ in outs],
        out_shape=[shapes[kind](dtype) for kind, dtype in outs],
        compiler_params=pltpu.CompilerParams(vmem_limit_bytes=48 * 1024 * 1024),
    )(*args)


def weight_grad(places, pairs, block):
    tokens, blocks = pairs[0][0].shape[0], places.shape[0]
    widths = [y.shape[1] for _, y in pairs]

    def kernel(_, *refs):
        at = 0
        for i, wide in enumerate(widths):
            refs[-1][0, :, at : at + wide] = tn(refs[2 * i][...], refs[2 * i + 1][...]).astype(
                BF16
            )
            at += wide

    specs = []
    for wide in widths:
        specs.append(pl.BlockSpec((tokens, block), lambda i, at: (0, at[i])))
        specs.append(pl.BlockSpec((tokens, wide), lambda i, at: (0, 0)))
    return pl.pallas_call(
        kernel,
        grid_spec=pltpu.PrefetchScalarGridSpec(
            num_scalar_prefetch=1,
            grid=(blocks,),
            in_specs=specs,
            out_specs=pl.BlockSpec((1, block, sum(widths)), lambda i, at: (i, 0, 0)),
        ),
        out_shape=jax.ShapeDtypeStruct((blocks, block, sum(widths)), BF16),
        compiler_params=pltpu.CompilerParams(vmem_limit_bytes=48 * 1024 * 1024),
    )(places, *[v for pair in pairs for v in pair])


def lanes_kernel(spans, x_ref, out_ref):
    at = 0
    for start, stop in spans:
        out_ref[:, at : at + stop - start] = x_ref[:, start:stop].astype(out_ref.dtype)
        at += stop - start


def move_lanes(spans, value, dtype):
    return pl.pallas_call(
        functools.partial(lanes_kernel, spans),
        in_specs=[pl.BlockSpec(memory_space=pltpu.VMEM)],
        out_specs=pl.BlockSpec(memory_space=pltpu.VMEM),
        out_shape=jax.ShapeDtypeStruct(value.shape, dtype),
        compiler_params=pltpu.CompilerParams(vmem_limit_bytes=32 * 1024 * 1024),
    )(value)


def place_kernel(counts, wide, block, at_ref, *refs):
    ins, out_ref, sems = refs[: len(counts)], refs[-2], refs[-1]
    rows = out_ref.shape[0]
    copies, i = [], 0
    for ref, n in zip(ins, counts):
        for j in range(n):
            start = pl.multiple_of(at_ref[i] * block, block)
            column = i * block // rows * wide
            copy = pltpu.make_async_copy(
                ref.at[pl.ds(j * block, block), :],
                out_ref.at[pl.ds(start, block), pl.ds(column, wide)],
                sems.at[i],
            )
            copy.start()
            copies.append(copy)
            i += 1
    for copy in copies:
        copy.wait()


def place_rows(parts, block):
    pieces = [p for part in parts for p in part[1]]
    wide = pieces[0].shape[1]
    at = jnp.concatenate([part[0] for part in parts])
    counts = [p.shape[0] // block for p in pieces]
    total = sum(counts)
    return pl.pallas_call(
        functools.partial(place_kernel, counts, wide, block),
        in_specs=[pl.BlockSpec(memory_space=pltpu.SMEM)]
        + [pl.BlockSpec(memory_space=pl.ANY)] * len(pieces),
        out_specs=pl.BlockSpec(memory_space=pl.ANY),
        out_shape=jax.ShapeDtypeStruct(
            (total * block // len(parts), wide * len(parts)), pieces[0].dtype
        ),
        scratch_shapes=[pltpu.SemaphoreType.DMA((total,))],
        compiler_params=pltpu.CompilerParams(vmem_limit_bytes=32 * 1024 * 1024),
    )(at, *pieces)


def mixes_kernel(
    open_ref, x_ref, before_ref, vec_ref, down_ref, up_ref, ddown_ref,
    m1_ref, m2_ref, m3_ref, m4_ref, dh_ref,
    normal_ref, scale_ref, delta_ref, blend_ref, m0_ref, tanh_ref, dtanh_ref,
):
    piece = pl.program_id(0)
    step = m1_ref.shape[0]
    x = x_ref[...].astype(F32)
    centred = x - jnp.mean(x, axis=-1, keepdims=True)
    scale = lax.rsqrt(jnp.mean(centred * centred, axis=-1, keepdims=True) + LN_EPS)
    normal = centred * scale
    full = normal * vec_ref[0:1, :] + vec_ref[1:2, :]
    normed = full[:step]
    first = jnp.where(open_ref[piece] == 1, before_ref[0:1, :], full[step : step + 1])
    row = lax.broadcasted_iota(jnp.int32, normed.shape, 0)
    delta = jnp.where(row == 0, first, pltpu.roll(normed, 1, 0)) - normed
    blend = (normed + delta * vec_ref[2:3, :]).astype(BF16)
    tanh = jnp.tanh(nn(blend, down_ref[...]))
    latent = tanh.astype(BF16)
    lane = lax.broadcasted_iota(jnp.int32, latent.shape, 1)
    mixed = []
    for c in range(5):
        own = (lane >= c * RANK) & (lane < (c + 1) * RANK)
        offset = nt(jnp.where(own, latent, jnp.zeros_like(latent)), up_ref[...])
        mixed.append((normed + delta * (vec_ref[3 + c : 4 + c, :] + offset)).astype(BF16))
    dtanh = jnp.tanh(nn(mixed[0], ddown_ref[...]))
    m1_ref[...], m2_ref[...], m3_ref[...], m4_ref[...] = mixed[1:]
    dh_ref[...] = dtanh.astype(BF16)

    @pl.when(piece == 0)
    def _():
        normal_ref[...] = normal[:step]
        scale_ref[...] = jnp.broadcast_to(scale[:step], scale_ref.shape)
        delta_ref[...] = delta
        blend_ref[...] = blend
        m0_ref[...] = mixed[0]
        tanh_ref[...] = tanh
        dtanh_ref[...] = dtanh


def group_mixes(opening, x, before, vec, down, up, ddown, step):
    high, width = step + 16, x.shape[1]
    pieces = x.shape[0] // high

    def whole(value):
        return pl.BlockSpec(value.shape, lambda k: (0, 0))

    def own(columns, dtype):
        return (
            pl.BlockSpec((step, columns), lambda k: (0, 0)),
            jax.ShapeDtypeStruct((step, columns), dtype),
        )

    def every(columns, dtype):
        return (
            pl.BlockSpec((step, columns), lambda k: ((k % 2) * 2 + k // 2, 0)),
            jax.ShapeDtypeStruct((pieces * step, columns), dtype),
        )

    outs = [every(width, BF16)] * 4 + [
        every(DRANK, BF16),
        own(width, F32),
        own(128, F32),
        own(width, F32),
        own(width, BF16),
        own(width, BF16),
        own(5 * RANK, F32),
        own(DRANK, F32),
    ]
    return pl.pallas_call(
        mixes_kernel,
        grid=(pieces,),
        in_specs=[
            pl.BlockSpec(memory_space=pltpu.SMEM),
            pl.BlockSpec((high, width), lambda k: (k, 0)),
            whole(before),
            whole(vec),
            whole(down),
            whole(up),
            whole(ddown),
        ],
        out_specs=[o[0] for o in outs],
        out_shape=[o[1] for o in outs],
        compiler_params=pltpu.CompilerParams(vmem_limit_bytes=56 * 1024 * 1024),
    )(opening, x, before, vec, down, up, ddown)


def product(pairs, outs, body, sides=(), tile=256):
    count = len(pairs)

    def kernel(*refs):
        ins, out_refs = refs[: 2 * count + len(sides)], refs[2 * count + len(sides) :]
        products = [
            (nn if pair[2] == "nn" else nt)(ins[2 * i][...], ins[2 * i + 1][...])
            for i, pair in enumerate(pairs)
        ]
        results = body(*products, *[r[...] for r in ins[2 * count :]])
        for ref, value in zip(out_refs, results):
            ref[...] = value.astype(ref.dtype)

    specs, args = [], []
    for a, b, form, at in pairs:
        depth = a.shape[1]
        specs.append(pl.BlockSpec(a.shape, lambda j: (0, 0)))
        if form == "nn":
            specs.append(pl.BlockSpec((depth, tile), lambda j, at=at: (0, at + j)))
        else:
            specs.append(pl.BlockSpec((tile, depth), lambda j, at=at: (j, at)))
        args += [a, b]
    for side in sides:
        specs.append(pl.BlockSpec((side.shape[0], tile), lambda j: (0, j)))
    return pl.pallas_call(
        kernel,
        grid=(outs[0][1] // tile,),
        in_specs=specs,
        out_specs=[pl.BlockSpec((o[0], tile), lambda j: (0, j)) for o in outs],
        out_shape=[jax.ShapeDtypeStruct(o[:2], o[2]) for o in outs],
        compiler_params=pltpu.CompilerParams(vmem_limit_bytes=56 * 1024 * 1024),
    )(*args, *sides)


def local(fn, outs, *args, scalar=None):
    def kernel(*refs):
        lead = [] if scalar is None else [refs[0]]
        ins, out_refs = refs[len(lead) : -len(outs)], refs[-len(outs) :]
        scalars = [r[i] for r in lead for i in range(r.shape[0])]
        results = fn(*scalars, *[r[...] for r in ins])
        for ref, value in zip(out_refs, results):
            ref[...] = value.astype(ref.dtype)

    specs = [pl.BlockSpec(memory_space=pltpu.VMEM)] * len(args)
    if scalar is not None:
        specs = [pl.BlockSpec(memory_space=pltpu.SMEM)] + specs
        args = (scalar.reshape(-1), *args)
    return pl.pallas_call(
        kernel,
        in_specs=specs,
        out_specs=[pl.BlockSpec(memory_space=pltpu.VMEM)] * len(outs),
        out_shape=[jax.ShapeDtypeStruct(o[:2], o[2]) for o in outs],
        compiler_params=pltpu.CompilerParams(vmem_limit_bytes=56 * 1024 * 1024),
    )(*args)


def take_lanes(value, spans):
    if len(spans) == 1:
        return value
    return jnp.concatenate([value[:, a:b] for a, b in spans], axis=1)


def norm_back(grad, gain, normal, scale):
    e = grad * gain
    return scale * (
        e
        - jnp.mean(e, axis=-1, keepdims=True)
        - normal * jnp.mean(e * normal, axis=-1, keepdims=True)
    )


def rows_above(value, first):
    row = lax.broadcasted_iota(jnp.int32, value.shape, 0)
    return jnp.where(row == 0, first, pltpu.roll(value, 1, 0))


def rows_below(value, last):
    row = lax.broadcasted_iota(jnp.int32, value.shape, 0)
    high = value.shape[0]
    return jnp.where(row == high - 1, last, pltpu.roll(value, high - 1, 0))


def padded(rows):
    return jnp.concatenate(
        list(rows) + [jnp.zeros((8 - len(rows), rows[0].shape[1]), F32)], axis=0
    )


def column_sum(value):
    return jnp.sum(value, axis=0, keepdims=True)


def gates_kernel(
    spans, who_ref, middle_ref, value_ref, more_ref, act_ref, cot_ref,
    out_ref, up_ref, vg_ref, rg_ref, held,
):
    to_spans, from_spans = spans
    step, part = act_ref.shape[0] // 4, act_ref.shape[1]
    who = who_ref[0]
    act = [
        act_ref[pl.ds(pl.multiple_of((who ^ j) * step, step), step), :] for j in range(4)
    ]
    recept = jax.nn.sigmoid(take_lanes(jnp.concatenate(act, axis=1).astype(F32), to_spans))
    value = value_ref[...] + more_ref[...].astype(F32)
    out = middle_ref[...] + recept * value
    out_ref[...] = take_lanes(out, from_spans).astype(BF16)
    up = take_lanes(cot_ref[...].astype(F32), to_spans)
    up_ref[...] = up
    vg_ref[...] = (up * recept).astype(BF16)
    held[...] = take_lanes(up * value * recept * (1.0 - recept), from_spans)
    for k in range(4):
        at = pl.multiple_of((who ^ k) * part, part)
        rg_ref[k * step : (k + 1) * step, :] = held[:, pl.ds(at, part)].astype(BF16)


def gates(spans, who, middle, value, more, act, cot):
    step, width = middle.shape
    part = act.shape[1]
    shape = jax.ShapeDtypeStruct
    return pl.pallas_call(
        functools.partial(gates_kernel, spans),
        in_specs=[pl.BlockSpec(memory_space=pltpu.SMEM)]
        + [pl.BlockSpec(memory_space=pltpu.VMEM)] * 5,
        out_specs=[pl.BlockSpec(memory_space=pltpu.VMEM)] * 4,
        out_shape=[
            shape((step, width), BF16),
            shape((step, width), F32),
            shape((step, width), BF16),
            shape((4 * step, part), BF16),
        ],
        scratch_shapes=[pltpu.VMEM((step, width), F32)],
        compiler_params=pltpu.CompilerParams(vmem_limit_bytes=56 * 1024 * 1024),
    )(who.reshape(1), middle, value, more, act, cot)


def mixes_back_kernel(
    kept_ref, got_ref, dl_ref, dl_more_ref, delta_ref, tanh_ref, dtanh_ref, blend_ref, m0_ref,
    down_ref, up_ref, ddown_ref, vec_ref,
    rest_ref, dg_ref, row_ref, cols_ref, down_out, up_out, ddown_out,
):
    step = delta_ref.shape[0]
    dtanh = dtanh_ref[...]
    decay_grad = dl_ref[...] + dl_more_ref[...].astype(F32)
    decay_pre = (decay_grad * (1.0 - dtanh * dtanh)).astype(BF16)
    ddown_out[...] = tn(m0_ref[...], decay_pre)
    tanh = tanh_ref[...]
    latent = tanh.astype(BF16)
    lane = lax.broadcasted_iota(jnp.int32, latent.shape, 1)
    delta, up = delta_ref[...], up_ref[...]
    latent_grad = jnp.zeros(latent.shape, F32)
    up_grad = jnp.zeros(up_out.shape, F32)
    dg = jnp.zeros(delta.shape, F32)
    total = jnp.zeros(delta.shape, F32)
    cols = []
    for c in range(5):
        own = (lane >= c * RANK) & (lane < (c + 1) * RANK)
        mine = jnp.where(own, latent, jnp.zeros_like(latent))
        if c == 0:
            grad = nt(decay_pre, ddown_ref[...])
        else:
            at = slice((c - 1) * step, c * step)
            grad = kept_ref[at, :] + got_ref[at, :].astype(F32)
        shift = grad * delta
        cols.append(column_sum(shift))
        offset = shift.astype(BF16)
        latent_grad = jnp.where(own, nn(offset, up), latent_grad)
        up_grad = up_grad + tn(offset, mine)
        dg = dg + grad * (vec_ref[3 + c : 4 + c, :] + nt(mine, up))
        total = total + grad
    up_out[...] = up_grad
    mix_pre = (latent_grad * (1.0 - tanh * tanh)).astype(BF16)
    down_out[...] = tn(blend_ref[...], mix_pre)
    blend_grad = nt(mix_pre, down_ref[...])
    dg = dg + blend_grad * vec_ref[2:3, :]
    rest_ref[...] = total + blend_grad - dg
    dg_ref[...] = dg
    row_ref[...] = dg[:8]
    cols_ref[...] = padded([column_sum(blend_grad * delta)] + cols)


def mixes_back(*args):
    delta, down, ddown = args[4], args[9], args[11]
    step, width = delta.shape
    shape = jax.ShapeDtypeStruct
    outs = [
        shape((step, width), F32),
        shape((step, width), F32),
        shape((8, width), F32),
        shape((8, width), F32),
        shape(down.shape, F32),
        shape(down.shape, F32),
        shape(ddown.shape, F32),
    ]
    return pl.pallas_call(
        mixes_back_kernel,
        in_specs=[pl.BlockSpec(memory_space=pltpu.VMEM)] * len(args),
        out_specs=[pl.BlockSpec(memory_space=pltpu.VMEM)] * len(outs),
        out_shape=outs,
        compiler_params=pltpu.CompilerParams(vmem_limit_bytes=60 * 1024 * 1024),
    )(*args)


def tie(*values):
    return lax.optimization_barrier(values)


def on_device(
    count,
    tokens,
    previous,
    initial_state,
    mixing_weights,
    lowrank_weights,
    vectors,
    feedforward_weights,
    cotangent,
):
    fast = initial_state.shape[0] == 64
    masks = (1, 8) if fast else (1, 2)
    size = 1 << len(masks)
    teams = count // size
    all_masks = [1 << b for b in range(count.bit_length() - 1)]
    team_masks = [b for b in all_masks if b not in masks]
    far = 16
    team_masks.sort(key=lambda b: fast and b != far)
    me = lax.axis_index("seq")
    _, step, width = tokens.shape
    rows = mixing_weights.shape[0]
    part = width // size
    ff_part = FF // size
    team_rows = rows * size
    def bit_of(who, mask):
        return (who // mask) % 2 if isinstance(who, int) else lax.rem(lax.div(who, mask), 2)

    def member_of(who):
        return sum(bit_of(who, b) << j for j, b in enumerate(masks))

    def team_of(who):
        return sum(bit_of(who, b) << j for j, b in enumerate(team_masks))

    member, team = member_of(me), team_of(me)
    order = sorted(range(count), key=lambda d: (team_of(d), member_of(d)))
    inverse = sorted(range(count), key=lambda p: order[p])
    across = [order[m::size] for m in range(size)]
    square = [order[m :: 2 * size] for m in range(2 * size)]
    def lane_spans(blocks):
        spans = []
        for d in blocks:
            if spans and spans[-1][1] == d * rows:
                spans[-1][1] = (d + 1) * rows
            else:
                spans.append([d * rows, (d + 1) * rows])
        return spans

    to_spans, from_spans = lane_spans(order), lane_spans(inverse)

    def to_places(value, dtype):
        return move_lanes(to_spans, value, dtype)

    def flips(k):
        return sum(b for j, b in enumerate(masks) if (k >> j) & 1)

    def trade(value, mask):
        return lax.ppermute(value, "seq", [(d, d ^ mask) for d in range(count)])

    def group_gather(value):
        side = trade(value, masks[1])
        return value, side, trade(jnp.concatenate([value, side], axis=0), masks[0])

    def group_rows(value):
        high, columns = value.shape

        def lay(own, side, far):
            return (jnp.concatenate([own, far[:high], side, far[high:]], axis=0),)

        return local(lay, [(size * high, columns, value.dtype)], *group_gather(value))[0]

    def halves(value):
        cut = [value[k * step : (k + 1) * step] for k in range(size)]
        return [cut[0], cut[2]], [cut[1], cut[3]]

    def group_fold(kept, sent):
        high, columns = kept.shape[0] // 2, kept.shape[1]
        got = trade(sent, masks[0])

        def add(mine, more):
            total = mine + more.astype(F32)
            return total[:high], total[high:]

        return local(add, [(high, columns, F32), (high, columns, BF16)], kept, got)

    def group_sum(kept, sent):
        mine, side = group_fold(kept, sent)
        return mine, trade(side, masks[1])

    def crossing_sum(*pairs):
        units = len(pairs)

        def body(*products):
            parts = [halves(p) for p in products]
            kept = [p[0][i] for i in range(2) for p in parts]
            sent = [p[1][i] for i in range(2) for p in parts]
            return jnp.concatenate(kept, axis=0), jnp.concatenate(sent, axis=0)

        high = 2 * units * step
        return product(
            [(a, b, "nt", at) for a, b, at in pairs],
            [(high, width, F32), (high, width, BF16)],
            body,
            tile=512,
        )

    def exchange(pieces, meet=None):
        pieces, high = list(pieces), pieces[0].shape[0]
        for j in reversed(range(len(masks))):
            keys = [k for k in range(size) if (k >> j) & 1]
            got = trade(jnp.concatenate([pieces[k] for k in keys], axis=0), masks[j])
            if meet is not None and j == len(masks) - 1:
                got, meet = tie(got, meet)
            for i, k in enumerate(keys):
                pieces[k] = got[i * high : (i + 1) * high]
        return pieces if meet is None else (pieces, meet)

    def ordered(pieces):
        pieces = list(pieces)
        for j in range(len(masks)):
            swap = lax.rem(lax.div(member, 1 << j), 2) == 1
            pieces = [
                jnp.where(swap, pieces[k ^ (1 << j)], pieces[k]) for k in range(len(pieces))
            ]
        return pieces

    def neighbour(value, offset):
        pairs = [(d, d + offset) for d in range(count) if 0 <= d + offset < count]
        return lax.ppermute(value, "seq", pairs)

    def take_columns(value, spans, who):
        return jnp.concatenate(
            [
                lax.dynamic_slice_in_dim(value, start + who * wide, wide, axis=1)
                for start, wide in spans
            ],
            axis=1,
        )

    def group_columns(value, spans):
        pieces = [take_columns(value, spans, member ^ k) for k in range(size)]
        return jnp.concatenate(ordered(exchange(pieces)), axis=0)

    def crossing(first):
        bits = list(range(1, len(team_masks))) + [0]
        if first:
            bits[0], bits[1] = bits[1], bits[0]
        return bits

    def gather_rows(own):
        return lax.all_gather(own, "seq", axis=0, tiled=True, axis_index_groups=across)

    def far_send(own):
        return trade(own, far) if fast else own

    def far_join(own, got):
        if not fast:
            return own
        upper = bit_of(me, far) == 1
        return jnp.concatenate(
            [jnp.where(upper, got, own), jnp.where(upper, own, got)], axis=0
        )

    def gather_square(paired):
        groups = square if fast else across
        return lax.all_gather(paired, "seq", axis=0, tiled=True, axis_index_groups=groups)

    def team_products(*pairs):
        if fast:
            places = jnp.arange(teams, dtype=jnp.int32)
            return weight_grad(places, pairs, team_rows).reshape(width, -1)
        return jnp.concatenate([tn(x, y).astype(BF16) for x, y in pairs], axis=1)

    def square_sum(grads):
        groups = square if fast else across
        return lax.psum_scatter(
            grads, "seq", scatter_dimension=0, tiled=True, axis_index_groups=groups
        )

    def far_split(pair):
        if not fast:
            return pair, jnp.zeros_like(pair)
        bit = bit_of(me, far)
        sent = lax.dynamic_slice_in_dim(pair, (1 - bit) * team_rows, team_rows, axis=0)
        kept = lax.dynamic_slice_in_dim(pair, bit * team_rows, team_rows, axis=0)
        return kept, trade(sent, far)

    def far_add(kept, got):
        return (kept.astype(F32) + got.astype(F32)).astype(BF16)

    def cube_gather(value, follower=None):
        for mask in reversed(all_masks):
            got = trade(value, mask)
            upper = bit_of(me, mask) == 1
            value = jnp.stack([jnp.where(upper, got, value), jnp.where(upper, value, got)])
            if mask == 8 and follower is not None:
                value, follower = tie(value, follower)
        axes = len(all_masks)
        cube = value.transpose(*reversed(range(axes)), *range(axes, value.ndim))
        return cube if follower is None else (cube, follower)

    place_axes = [all_masks[::-1].index(b) for b in team_masks[::-1] + list(masks[::-1])]

    def by_place(cube):
        rest = range(len(all_masks), cube.ndim)
        return cube.transpose(*place_axes, *rest).reshape(width, -1)

    def to_cube(value):
        cube = value.reshape(*[2] * len(place_axes), rows, -1)
        back = [place_axes.index(a) for a in range(len(place_axes))]
        return cube.transpose(*back, len(back), len(back) + 1)

    def cube_sum(cube, kind):
        for axis, mask in reversed(list(enumerate(reversed(all_masks)))):
            bit = bit_of(me, mask)
            sent = lax.dynamic_index_in_dim(cube, 1 - bit, axis, keepdims=False)
            kept = lax.dynamic_index_in_dim(cube, bit, axis, keepdims=False)
            cube = kept.astype(F32) + trade(sent.astype(kind), mask).astype(F32)
        return cube

    def hand_rows(joint, extra=None, meet=None):
        mine = [
            lax.dynamic_slice_in_dim(joint, (member ^ k) * rows, rows, axis=0)
            for k in range(size)
        ]
        if extra is not None:
            mine = [jnp.concatenate([m, e], axis=1) for m, e in zip(mine, extra)]
        return exchange(mine, meet)

    def columns_of(by_member, start, wide):
        return [p[:, start : start + wide] for p in by_member]

    up_start, decay_start, decay_up = 5 * RANK, 10 * RANK, 10 * RANK + DRANK
    last_row = neighbour(tokens[0, -1:, :], 1)
    tokens_sent = to_places(
        jnp.concatenate([tokens[0], jnp.broadcast_to(last_row, (16, width))], axis=0), BF16
    )
    natural, mix_in = cube_gather(
        jnp.concatenate(
            [vectors, initial_state, lowrank_weights[:, decay_up:].astype(F32)], axis=1
        ),
        mixing_weights,
    )
    natural = natural.reshape(width, -1)
    low_cube, mix_in = cube_gather(lowrank_weights[:, :decay_up], mix_in)
    tokens_all = jnp.concatenate(group_gather(tokens_sent), axis=0)
    mix_local = group_columns(mix_in, [(c * width, part) for c in range(5)])
    mix_local, natural, low_cube, tokens_all = tie(mix_local, natural, low_cube, tokens_all)
    lowrank = by_place(low_cube)
    mix_kv, mix_rest = mix_local[:, : 2 * part], mix_local[:, 2 * part :]
    kv_got, mix_rest, feed_in = tie(far_send(mix_kv), mix_rest, feedforward_weights)
    w_kv = gather_square(far_join(mix_kv, kv_got))
    tiles = part // 256

    mine = lax.dynamic_slice_in_dim(natural, member * part, part, axis=0)
    vec_part = mine[:, :16].T
    first_state = mine[:, 16 : 16 + SPAN].T
    w_dup = mine[:, 16 + SPAN :].astype(BF16)
    vec = by_place(
        natural[:, :16].reshape(*[2] * len(all_masks), rows, 16)
    ).T
    wkv_rows = jnp.concatenate([vec_part[9:12], jnp.zeros((5, part), F32)], axis=0)
    is_first = (me == 0).astype(jnp.int32)
    before = to_places(previous.reshape(2, width), F32)
    w_down, w_up = lowrank[:, :up_start], lowrank[:, up_start:decay_start]
    w_ddown = lowrank[:, decay_start:]

    opening = jnp.stack(
        [jnp.bitwise_xor(me, flips(k)) == 0 for k in (0, 2, 1, 3)]
    ).astype(jnp.int32)
    (
        *mixed_all, dh_all, normal_one, scale_one, delta, blend, mixed_zero, mix_tanh, decay_tanh,
    ) = group_mixes(opening, tokens_all, before, vec, w_down, w_up, w_ddown, step)
    rest_got, mixed_all[0] = tie(far_send(mix_rest), mixed_all[0])
    w_rest = gather_square(far_join(mix_rest, rest_got))
    ff_spans = [(0, ff_part), (FF, part), (FF + width, ff_part)]
    ff_local = group_columns(feed_in, ff_spans)
    everyone = size * step
    (log_decay,) = product(
        [(dh_all, w_dup, "nt", 0)],
        [(everyone, part, F32)],
        lambda acc, base: (-jnp.exp(base + acc),),
        sides=(vec_part[8:9],),
    )
    keys, values = product(
        [(mixed_all[0], w_kv, "nn", 0), (mixed_all[1], w_kv, "nn", tiles)],
        [(everyone, part, F32)] * 2,
        lambda a, b: (a, b),
    )

    keys, ff_local = tie(keys, ff_local)
    ff_tail = ff_local[:, ff_part + part :]
    ff_near = ff_local[:, : ff_part + part]
    near_got = far_send(ff_near)

    call = functools.partial(block_call, chunks=size, step=step, width=part)
    (totals,) = call(
        totals_kernel, ins="ttt", outs=[("x", F32)], args=(keys, values, log_decay)
    )
    stages, current = [], [None, []]
    for mask in all_masks:
        if mask in masks:
            current[1].append(1 << masks.index(mask))
        else:
            stages.append(current)
            current = [mask, []]
    stages.append(current)
    high, long = SPAN + 8, SPAN + 16

    def chain(early, late):
        return early[0] * late[0], late[0] * early[1] + late[1]

    def pick(flag, yes, no):
        return tuple(jnp.where(flag, a, b) for a, b in zip(yes, no))

    def rows8(row):
        return jnp.broadcast_to(row, (8, part))

    def pack(items):
        return jnp.concatenate([r for d, v in items for r in (v, rows8(d))], axis=0)

    def unpack(array, count):
        cut = [array[i * high : (i + 1) * high] for i in range(count)]
        return [(c[SPAN : SPAN + 1], c[:SPAN]) for c in cut]

    def swap_members(who, pieces):
        pieces = list(pieces)
        for j in range(len(masks)):
            flag = (who // (1 << j)) % 2 == 1
            pieces = [jnp.where(flag, pieces[k ^ (1 << j)], pieces[k]) for k in range(size)]
        return pieces

    def neutral():
        return jnp.ones((1, part), F32), jnp.zeros((SPAN, part), F32)

    def flags_of(mask):
        bit = jnp.int32(0) if mask is None else bit_of(me, mask)
        return jnp.stack([member, bit]).astype(jnp.int32)

    keys_at, decays = list(range(size)), []
    open_bits = size - 1
    stage_arrays = [totals.reshape(size * high, part)]
    for index, (mask, merges) in enumerate(stages):
        last = index + 1 == len(stages)
        after_keys = keys_at
        for bit in merges:
            after_keys = [g for g in after_keys if not g & bit]

        def forward_stage(
            who, late, *arrays, mask=mask, merges=merges, groups=keys_at, bits=open_bits, last=last
        ):
            marks = []
            if mask is None:
                cut = [arrays[0][k * high : (k + 1) * high] for k in range(size)]
                total = {
                    m: (p[SPAN : SPAN + 1], p[:SPAN])
                    for m, p in enumerate(swap_members(who, cut))
                }
                chunks = [neutral() for _ in range(size)]
            else:
                total = dict(zip(groups, unpack(arrays[0], len(groups))))
                chunks = unpack(arrays[1], size)
                other = {}
                for i, g in enumerate(groups):
                    got = arrays[2][i * long : (i + 1) * long].astype(F32)
                    other[g] = got[SPAN : SPAN + 1] + got[SPAN + 8 : SPAN + 9], got[:SPAN]
                marks += [total[g][0] for g in groups] + [other[g][0] for g in groups]
                late = late == 1
                chunks = [
                    pick(late, chain(other[m & bits], c), c) for m, c in enumerate(chunks)
                ]
                total = {
                    g: pick(late, chain(other[g], total[g]), chain(total[g], other[g]))
                    for g in groups
                }
            for bit in merges:
                marks += [total[g][0] for g in total]
                chunks = [
                    chain(total[(m & bits) ^ bit], c) if m & bit else c
                    for m, c in enumerate(chunks)
                ]
                total = {g: chain(total[g], total[g | bit]) for g in total if not g & bit}
                bits ^= bit
            marks = jnp.concatenate([rows8(r) for r in marks], axis=0)
            if last:
                states = [d * arrays[-1] + v for d, v in chunks]
                return jnp.concatenate(swap_members(who, states), axis=0), marks
            sent = []
            for d, v in total.values():
                first = d.astype(BF16)
                rest = (d - first.astype(F32)).astype(BF16)
                sent += [v.astype(BF16), rows8(first), rows8(rest)]
            return (
                pack(list(total.values())), pack(chunks), jnp.concatenate(sent, axis=0), marks
            )

        count_marks = (0 if mask is None else 2 * len(keys_at)) + sum(
            len(keys_at) >> i for i in range(len(merges))
        )
        marks_out = (8 * count_marks, part, F32)
        if last:
            outs = [(size * SPAN, part, F32), marks_out]
            state_in, marks = local(
                forward_stage, outs, *stage_arrays, first_state, scalar=flags_of(mask)
            )
            state_in = state_in.reshape(size, SPAN, part)
        else:
            outs = [
                (len(after_keys) * high, part, F32),
                (size * high, part, F32),
                (len(after_keys) * long, part, BF16),
                marks_out,
            ]
            total, chunks, sent, marks = local(
                forward_stage, outs, *stage_arrays, scalar=flags_of(mask)
            )
            if mask == (2 if fast else 4):
                sent, near_got = tie(sent, near_got)
            stage_arrays = [total, chunks, trade(sent, stages[index + 1][0])]
        decays.append(marks)
        keys_at = after_keys
        for bit in merges:
            open_bits ^= bit
    w_near = gather_square(far_join(ff_near, near_got))
    w_key, w_rec = w_near, w_near[:, ff_part:]
    state_in, ff_tail = tie(state_in, ff_tail)
    val_got = far_send(ff_tail)

    receipt, gate_pre = product(
        [(mixed_all[2], w_rest, "nn", 0), (mixed_all[3], w_rest, "nn", tiles)],
        [(everyone, part, F32)] * 2,
        lambda a, b: (a, b),
    )
    wkv, gated = call(
        forward_kernel,
        ins="tttttsp",
        outs=[("t", F32), ("t", BF16)],
        args=(receipt, keys, values, log_decay, gate_pre, state_in, wkv_rows),
    )
    gated, val_got = tie(gated, val_got)
    w_val = gather_square(far_join(ff_tail, val_got))
    branch, branch_more = group_sum(*crossing_sum((gated, w_rest, 2)))

    def norm_two(hidden, mine, more, vec):
        middle = hidden[:step].astype(F32) + mine + more.astype(F32)
        centred = middle - jnp.mean(middle, axis=-1, keepdims=True)
        scale = lax.rsqrt(jnp.mean(centred * centred, axis=-1, keepdims=True) + LN_EPS)
        normal = centred * scale
        tail = normal[step - 8 :] * vec[12:13] + vec[13:14]
        return middle, normal, jnp.broadcast_to(scale, (step, 128)), tail

    whole = (step, width, F32)
    middle, normal_two, scale_two, tail_two = local(
        norm_two,
        [whole, whole, (step, 128, F32), (8, width, F32)],
        tokens_sent,
        branch,
        branch_more,
        vec,
    )

    def mix_two(first, normal, arrived, before, vec):
        normed = normal * vec[12:13] + vec[13:14]
        above = jnp.where(first == 1, before[1:2], arrived[7:8])
        delta = rows_above(normed, above) - normed
        key_in, recv_in = normed + delta * vec[14:15], normed + delta * vec[15:16]
        return jnp.concatenate([key_in, recv_in], axis=0), delta

    both, delta_two = local(
        mix_two,
        [(2 * step, width, BF16), whole],
        normal_two,
        neighbour(tail_two, 1),
        before,
        vec,
        scalar=is_first,
    )

    key_all, recv_all = group_rows(both[:step]), group_rows(both[step:])
    relu, squared = product(
        [(key_all, w_key, "nn", 0)],
        [(everyone, ff_part, F32), (everyone, ff_part, BF16)],
        lambda acc: (jnp.maximum(acc, 0.0), jnp.square(jnp.maximum(acc, 0.0))),
        tile=ff_part // 2,
    )
    (recept_act,) = product(
        [(recv_all, w_rec, "nn", 0)],
        [(everyone, part, BF16)],
        lambda acc: (acc,),
    )
    squared, recept_act = tie(squared, recept_act)
    acts = exchange([recept_act[k * step : (k + 1) * step] for k in range(size)])
    value, value_more = group_sum(*crossing_sum((squared, w_val, 0)))
    block_output, upstream, value_grad, recept_grads = gates(
        (to_spans, from_spans),
        member,
        middle,
        value,
        value_more,
        jnp.concatenate(acts, axis=0),
        cotangent.reshape(step, width),
    )

    rg_all = jnp.concatenate(
        exchange([recept_grads[k * step : (k + 1) * step] for k in range(size)]), axis=0
    )
    vg_all = group_rows(value_grad)
    val_grads = team_products((vg_all, squared))
    vg_all, val_grads, rg_all = tie(vg_all, val_grads, rg_all)
    val_pair = square_sum(val_grads)
    (key_grad,) = product(
        [(vg_all, w_val, "nn", 0)],
        [(everyone, ff_part, BF16)],
        lambda acc, relu: (acc * (2.0 * relu),),
        sides=(relu,),
        tile=ff_part // 2,
    )
    key_grads = team_products((key_all, key_grad))
    key_grad, key_grads = tie(key_grad, key_grads)
    key_pair = square_sum(key_grads)
    recv_two = group_sum(*crossing_sum((rg_all, w_rec, 0)))
    key_two = group_sum(*crossing_sum((key_grad, w_key, 0)))

    def inputs_back(key, key_more, recv, recv_more, vec):
        key, recv = key + key_more.astype(F32), recv + recv_more.astype(F32)
        top = key[:8] * vec[14:15] + recv[:8] * vec[15:16]
        return jnp.concatenate([key, recv], axis=0), top

    in_grads, top_two = local(
        inputs_back, [(2 * step, width, F32), (8, width, F32)], *key_two, *recv_two, vec
    )
    last_flag = (me == count - 1).astype(jnp.int32)

    def norm_two_back(last, grads, arrived, upstream, normal, scale, delta, vec):
        key_grad, recv_grad = grads[:step], grads[step:]
        shifted = key_grad * vec[14:15] + recv_grad * vec[15:16]
        below = jnp.where(last == 1, jnp.zeros_like(arrived[:1]), arrived[:1])
        grad = (
            key_grad * (1.0 - vec[14:15])
            + recv_grad * (1.0 - vec[15:16])
            + rows_below(shifted, below)
        )
        out = upstream + norm_back(grad, vec[12:13], normal, scale[:, :1])
        cols = padded(
            [
                column_sum(grad * normal),
                column_sum(grad),
                column_sum(key_grad * delta),
                column_sum(recv_grad * delta),
            ]
        )
        return out, out, cols

    middle_grad, branch_grad, cols_two = local(
        norm_two_back,
        [whole, (step, width, BF16), (8, width, F32)],
        in_grads,
        neighbour(top_two, -1),
        upstream,
        normal_two,
        scale_two,
        delta_two,
        vec,
        scalar=last_flag,
    )

    bg_all = group_rows(branch_grad)
    (gated_grad,) = product(
        [(bg_all, w_rest, "nn", 2 * tiles)], [(everyone, part, F32)], lambda acc: (acc,)
    )
    gate_grad, wkv_grad, ends = call(
        gate_kernel,
        ins="tttttp",
        outs=[("t", BF16), ("t", F32), ("x", F32)],
        args=(gated_grad, gate_pre, wkv, receipt, log_decay, wkv_rows),
    )
    val_kept, val_got = far_split(val_pair)
    keys_at, open_bits = list(range(size)), size - 1
    stage_arrays = [ends.reshape(size * high, part)]
    for index, (mask, merges) in enumerate(stages):
        last = index + 1 == len(stages)
        after_keys = keys_at
        for bit in merges:
            after_keys = [g for g in after_keys if not g & bit]

        def backward_stage(
            who, late, *arrays, mask=mask, merges=merges, groups=keys_at, bits=open_bits, last=last
        ):
            marks = [arrays[-1][i * 8 : i * 8 + 1] for i in range(arrays[-1].shape[0] // 8)]
            if mask is None:
                cut = [arrays[0][k * high : k * high + SPAN] for k in range(size)]
                total = dict(enumerate(swap_members(who, cut)))
                chunks = [neutral() for _ in range(size)]
            else:
                total = {g: arrays[0][i * SPAN : (i + 1) * SPAN] for i, g in enumerate(groups)}
                chunks = unpack(arrays[1], size)
                other = {
                    g: arrays[2][i * SPAN : (i + 1) * SPAN].astype(F32)
                    for i, g in enumerate(groups)
                }
                here = dict(zip(groups, marks))
                there = dict(zip(groups, marks[len(groups) :]))
                marks = marks[2 * len(groups) :]
                early = late == 0
                chunks = [
                    pick(
                        early,
                        (d * there[m & bits], d * other[m & bits] + v),
                        (d, v),
                    )
                    for m, (d, v) in enumerate(chunks)
                ]
                total = {
                    g: jnp.where(
                        early,
                        total[g] + here[g] * other[g],
                        other[g] + there[g] * total[g],
                    )
                    for g in groups
                }
            for bit in merges:
                here = dict(zip(total, marks))
                marks = marks[len(total) :]
                chunks = [
                    (d, v)
                    if m & bit
                    else (d * here[(m & bits) | bit], d * total[(m & bits) | bit] + v)
                    for m, (d, v) in enumerate(chunks)
                ]
                total = {
                    g: total[g] + here[g] * total[g | bit] for g in total if not g & bit
                }
                bits ^= bit
            joint = jnp.concatenate(list(total.values()), axis=0)
            if last:
                grads = swap_members(who, [v for _, v in chunks])
                return jnp.concatenate(grads, axis=0), joint.T
            return joint, pack(chunks), joint

        if last:
            outs = [(size * SPAN, part, F32), (part, SPAN, F32)]
            grad_out, first_grad = local(
                backward_stage, outs, *stage_arrays, decays[index], scalar=flags_of(mask)
            )
            grad_out = grad_out.reshape(size, SPAN, part)
        else:
            outs = [
                (len(after_keys) * SPAN, part, F32),
                (size * high, part, F32),
                (len(after_keys) * SPAN, part, BF16),
            ]
            total, chunks, sent = local(
                backward_stage, outs, *stage_arrays, decays[index], scalar=flags_of(mask)
            )
            if mask == (2 if fast else 4):
                sent, val_got = tie(sent, val_got)
            stage_arrays = [total, chunks, trade(sent, stages[index + 1][0])]
        keys_at = after_keys
        for bit in merges:
            open_bits ^= bit
    out_grads = team_products((bg_all, gated), (recv_all, rg_all), (mixed_all[3], gate_grad))
    grad_out, out_grads = tie(grad_out, out_grads)
    out_pair = square_sum(out_grads)

    d_receipt, d_keys, d_values, d_decay, extra = call(
        backward_kernel,
        ins="tttttssp",
        outs=[("t", BF16)] * 4 + [("e", F32)],
        args=(receipt, keys, values, log_decay, wkv_grad, state_in, grad_out, wkv_rows),
    )
    grads = [d_keys, d_values, d_receipt, gate_grad]
    kept, sent = crossing_sum(
        *[(grads[c], w_rest if c > 1 else w_kv, c % 2) for c in range(4)]
    )
    main_grads = team_products(
        (mixed_all[0], d_keys), (mixed_all[1], d_values), (mixed_all[2], d_receipt)
    )

    def latent_back(grad, up):
        kept, sent = halves(nn(grad, up))
        return jnp.concatenate(kept, axis=0), jnp.concatenate(sent, axis=0)

    latent_mine, latent_more = group_sum(
        *local(
            latent_back, [(2 * step, DRANK, F32), (2 * step, DRANK, BF16)], d_decay, w_dup
        )
    )
    key_kept, key_got = far_split(key_pair)
    sent, main_grads, latent_more, key_got = tie(sent, main_grads, latent_more, key_got)
    main_pair = square_sum(main_grads)
    val_sum, key_sum = far_add(val_kept, val_got), far_add(key_kept, key_got)
    mixed_mine, mixed_side = group_fold(kept, sent)
    ff_rows, mixed_side = hand_rows(
        jnp.concatenate([key_sum, val_sum], axis=1), meet=mixed_side
    )
    mixed_more = trade(mixed_side, masks[1])
    out_kept, out_got = far_split(out_pair)
    mixed_more, out_got = tie(mixed_more, out_got)
    rest_grad, delta_grad, top_one, cols_mix, down_grad, up_grad, ddown_grad = mixes_back(
        mixed_mine,
        mixed_more,
        latent_mine,
        latent_more,
        delta,
        mix_tanh,
        decay_tanh,
        blend,
        mixed_zero,
        w_down,
        w_up,
        w_ddown,
        vec,
    )
    rest_grad, main_pair = tie(rest_grad, main_pair)
    main_kept, main_got = far_split(main_pair)
    rest_grad, main_got = tie(rest_grad, main_got)
    out_sum = far_add(out_kept, out_got)

    def norm_one_back(last, rest, shifted, arrived, normal, scale, middle, vec):
        below = jnp.where(last == 1, jnp.zeros_like(arrived[:1]), arrived[:1])
        grad = rest + rows_below(shifted, below)
        out = middle + norm_back(grad, vec[0:1], normal, scale[:, :1])
        cols = padded([column_sum(grad * normal), column_sum(grad)])
        return take_lanes(out, from_spans), cols

    block_input_gradient, cols_one = local(
        norm_one_back,
        [whole, (8, width, F32)],
        rest_grad,
        delta_grad,
        neighbour(top_one, -1),
        normal_one,
        scale_one,
        middle_grad,
        vec,
        scalar=last_flag,
    )


    def spread(value):
        zero = jnp.zeros((width, value.shape[1]), F32)
        return lax.dynamic_update_slice_in_dim(zero, value, member * part, axis=0)

    vec_low = jnp.concatenate([cols_mix[:6], cols_two[:4]], axis=0)
    vec_head = jnp.concatenate(
        [jnp.sum(extra[:, :2], axis=0), jnp.sum(ends[:, SPAN : SPAN + 2], axis=0)], axis=0
    )
    by_feature = jnp.concatenate([down_grad, up_grad, ddown_grad, vec_low.T], axis=1)
    by_channel = spread(jnp.concatenate([tn(d_decay, dh_all), vec_head.T], axis=1))
    low = cube_sum(
        jnp.concatenate(
            [to_cube(by_feature), by_channel.reshape(*[2] * len(all_masks), rows, -1)], axis=-1
        ),
        BF16,
    )
    low_one = cube_sum(to_cube(cols_one[:2].T), F32)
    main_sum = far_add(main_kept, main_got)

    holder = lax.div(me * rows, part)

    def rows_of(who):
        mine = lax.dynamic_slice_in_dim(first_grad, lax.rem(who * rows, part), rows, axis=0)
        high = lax.reduce_precision(mine, 8, 7)
        return jnp.concatenate([high, mine - high], axis=1).astype(BF16)

    handed = hand_rows(
        jnp.concatenate([main_sum, out_sum], axis=1),
        [rows_of(jnp.bitwise_xor(me, flips(k))) for k in range(size)],
    )
    state_rows = handed[0][:, 6 * part :]
    for k in range(1, size):
        state_rows = jnp.where(holder == (member ^ k), handed[k][:, 6 * part :], state_rows)
    state_rows = state_rows.astype(F32)
    initial_state_gradient = state_rows[:, :SPAN] + state_rows[:, SPAN:]
    by_member, ff_member = ordered(handed), ordered(ff_rows)
    mixing_gradient = jnp.concatenate(
        [p for c in (0, 1, 2, 5, 3) for p in columns_of(by_member, c * part, part)], axis=1
    ).astype(F32)
    feedforward_gradient = jnp.concatenate(
        columns_of(ff_member, 0, ff_part)
        + columns_of(by_member, 4 * part, part)
        + columns_of(ff_member, ff_part, ff_part),
        axis=1,
    ).astype(F32)

    vec_at = decay_up + 10
    lowrank_gradient = jnp.concatenate(
        [low[:, :decay_up], low[:, vec_at : vec_at + DRANK]], axis=1
    )
    vectors_gradient = jnp.concatenate(
        [
            low_one,
            low[:, decay_up : decay_up + 6],
            low[:, vec_at + DRANK :],
            low[:, decay_up + 6 : vec_at],
        ],
        axis=1,
    )
    return (
        block_output.reshape(1, step, width),
        block_input_gradient.reshape(1, step, width),
        initial_state_gradient,
        mixing_gradient,
        lowrank_gradient,
        vectors_gradient,
        feedforward_gradient,
    )


def solution(mesh):
    rowwise = P("seq", None)
    tokenwise = P(None, "seq", None)
    return jax.shard_map(
        functools.partial(on_device, mesh.shape["seq"]),
        mesh=mesh,
        in_specs=(tokenwise, P(), rowwise, rowwise, rowwise, rowwise, rowwise, tokenwise),
        out_specs=(tokenwise, tokenwise, rowwise, rowwise, rowwise, rowwise, rowwise),
        check_vma=False,
    )
```
